32 devices in a mesh: dp: 4 (over y, x), ctx: 2 (over core), tensor: 4 (over z).
Axes of the slice: x: 2, y: 2, z: 4, core: 2. Of those that a mesh axis runs over, the one named last changes fastest.
Arguments:
- token_ids: int32 [4, 2048], P('dp', 'ctx'), may hold values from 0 to 31999
- targets: int32 [4, 2048, 2], P('dp', 'ctx'), may hold values from 0 to 31999
- counted: int32 [4, 2048, 2], P('dp', 'ctx'), may hold values from 0 to 1, as said below
- routes: int32 [4, 2048, 2], P('dp', 'ctx'), may hold values from 0 to 7, all different within a row
- priority: int32 [8, 1024], P(('dp', 'ctx')), may hold values from 0 to 1023, each once within a row
- owner_of: int32 [137, 1], replicated, may hold values from 0 to 7, as said below
- master: float32 [4, 8, 21, 64, 768], P('tensor', ('dp', 'ctx')), as said below
- master_first: float32 [4, 8, 21, 64, 768], P('tensor', ('dp', 'ctx')), as said below
- master_second: float32 [4, 8, 21, 64, 768], P('tensor', ('dp', 'ctx')), as said below
- expert_in: float32 [8, 768, 3072], P(('dp', 'ctx'), None, 'tensor'), may hold values from -0.21875 to 0.21875
- expert_in_first: float32 [8, 768, 3072], P(('dp', 'ctx'), None, 'tensor'), may hold values from -0.00012207031 to 0.00012207031
- expert_in_second: float32 [8, 768, 3072], P(('dp', 'ctx'), None, 'tensor'), may hold values from 1.6052246e-10 to 2.5683593e-09
- expert_out: float32 [8, 3072, 768], P(('dp', 'ctx'), 'tensor'), may hold values from -0.109375 to 0.109375
- expert_out_first: float32 [8, 3072, 768], P(('dp', 'ctx'), 'tensor'), may hold values from -0.00024414062 to 0.00024414062
- expert_out_second: float32 [8, 3072, 768], P(('dp', 'ctx'), 'tensor'), may hold values from 6.420898e-10 to 1.0273437e-08
- norm_gains: float32 [3, 768], replicated, may hold values from 0.5 to 1.5
- norm_gains_first: float32 [3, 768], replicated, may hold values from -0.00390625 to 0.00390625
- norm_gains_second: float32 [3, 768], replicated, may hold values from 1.2841797e-07 to 2.0546875e-06
- router: float32 [768, 8], replicated, may hold values from -0.21875 to 0.21875
- router_first: float32 [768, 8], replicated, may hold values from -0.001953125 to 0.001953125
- router_second: float32 [768, 8], replicated, may hold values from 3.210449e-08 to 5.1367186e-07
- rel_bias: float32 [12, 8], P('tensor'), may hold values from -3 to 3
- rel_bias_first: float32 [12, 8], P('tensor'), may hold values from -0.015625 to 0.015625
- rel_bias_second: float32 [12, 8], P('tensor'), may hold values from 2.0546875e-06 to 3.2875e-05
Outputs:
- loss_totals: float32 [2], replicated
- master_new: float32 [4, 8, 21, 64, 768], P('tensor', ('dp', 'ctx'))
- master_first_new: float32 [4, 8, 21, 64, 768], P('tensor', ('dp', 'ctx'))
- master_second_new: float32 [4, 8, 21, 64, 768], P('tensor', ('dp', 'ctx'))
- expert_in_new: float32 [8, 768, 3072], P(('dp', 'ctx'), None, 'tensor')
- expert_in_first_new: float32 [8, 768, 3072], P(('dp', 'ctx'), None, 'tensor')
- expert_in_second_new: float32 [8, 768, 3072], P(('dp', 'ctx'), None, 'tensor')
- expert_out_new: float32 [8, 3072, 768], P(('dp', 'ctx'), 'tensor')
- expert_out_first_new: float32 [8, 3072, 768], P(('dp', 'ctx'), 'tensor')
- expert_out_second_new: float32 [8, 3072, 768], P(('dp', 'ctx'), 'tensor')
- norm_gains_new: float32 [3, 768], replicated
- norm_gains_first_new: float32 [3, 768], replicated
- norm_gains_second_new: float32 [3, 768], replicated
- router_new: float32 [768, 8], replicated
- router_first_new: float32 [768, 8], replicated
- router_second_new: float32 [768, 8], replicated
- rel_bias_new: float32 [12, 8], P('tensor')
- rel_bias_first_new: float32 [12, 8], P('tensor')
- rel_bias_second_new: float32 [12, 8], P('tensor')
The draws below stay inside these ranges and needn't reach their ends.
Inputs may be any that keep to these rules, and one draw needn't show every extreme that they name: `owner_of`: no owner holds more than 21 units, and one holds exactly 21. `counted`: position 0 of every sequence counts for both targets; the last position never counts for the first target and the last two never for the second. `master`: slots that hold no unit are zero. `master_first`: slots that hold no unit are zero. `master_second`: slots that hold no unit are zero. `routes`: the two experts of a token differ. `priority`: each row holds each of 0 to 1023 once.
All inputs are finite; a program needn't handle non-finite values.
Results may differ from the reference program's by a relative error of at most 0.0055.
The reference program's roundings to bfloat16 on the way count: a program that leaves them out, or rounds other values in their place, can miss the bound.
Values may be sent and summed in bfloat16 or wider, within the bound.
A program may use at most 320 MiB of HBM per device.

```python
import math
import jax
import jax.numpy as jnp
import numpy as np
from jax import lax

MODEL_DIMENSION = 768
H = 12
HD = 64
F = 3072
VOCAB = 32000
TOP = 2
BLOCK = 256
SEQUENCE_TOKENS = 2048
SEQ = 1
STEP = 10
UR = 64
RANKS = 4
OWNERS = 8
EXPERTS = 8
SEQUENCE_COUNT = 4
HALF = 1024
TOK_DEV = 1024
TOKENS = 8192
VS = 8000
HS = 192
NB = 8
UNITS = 137
MOST = 21
CAP = 288
N_DP = 4
N_CTX = 2


def owner_table(key):
    unit_order = jax.random.permutation(jax.random.fold_in(key, 101), UNITS)
    owner_order = jax.random.permutation(jax.random.fold_in(key, 102), OWNERS).astype(jnp.int32)
    position = jnp.arange(UNITS, dtype=jnp.int32)
    others = owner_order[1 + jnp.maximum(position - MOST, 0) % (OWNERS - 1)]
    assigned = jnp.where(position < MOST, owner_order[0], others).astype(jnp.int32)
    return jnp.zeros((UNITS,), jnp.int32).at[unit_order].set(assigned)


def slot_layout(owner_ids):
    unit_index = jnp.arange(UNITS, dtype=jnp.int32)
    earlier = (owner_ids[None, :] == owner_ids[:, None]) & (unit_index[None, :] < unit_index[:, None])
    unit_rank = jnp.sum(earlier.astype(jnp.int32), 1)
    placed = (owner_ids[None, None, :] == jnp.arange(OWNERS, dtype=jnp.int32)[:, None, None]) & (unit_rank[None, None, :] == jnp.arange(MOST, dtype=jnp.int32)[None, :, None])
    slot_filled = jnp.any(placed, 2).astype(jnp.float32)
    slot_unit = jnp.sum(jnp.where(placed, unit_index[None, None, :], 0), 2).astype(jnp.int32)
    return (slot_unit[None, :, :, None, None], slot_filled[None, :, :, None, None])


def gradient_size(unit_ids):
    tokens_all = 1.0 * TOKENS
    table_size = 3.0 * (VOCAB * tokens_all) ** (-0.5)
    query_size = 0.1 * tokens_all ** (-0.5)
    value_size = 2.0 * tokens_all ** (-0.5)
    project_size = 0.005 * tokens_all ** (-0.5)
    return jnp.where(unit_ids < VS // UR, table_size, jnp.where(unit_ids < (VS + 2 * HS) // UR, query_size, jnp.where(unit_ids < (VS + 3 * HS) // UR, value_size, project_size)))


def draw_owner_of(key, part):
    return owner_table(key)[:, None]


def draw_master(key, part):
    slot_unit, slot_filled = slot_layout(owner_table(key))
    key = jax.random.fold_in(key, 11)
    shape = (RANKS, OWNERS, MOST, UR, MODEL_DIMENSION)
    rank_index = jnp.arange(RANKS, dtype=jnp.int32)[:, None, None, None, None]
    row_index = jnp.arange(UR, dtype=jnp.int32)[None, None, None, :, None]
    vocab_row = (rank_index * VS + slot_unit * UR + row_index).astype(jnp.float32)
    rising = 1.0 + 2.0 * vocab_row / (VOCAB - 1)
    noise = jax.random.normal(key, shape, jnp.float32)
    table_scale = rising * MODEL_DIMENSION ** (-0.5)
    scale = jnp.where(slot_unit < VS // UR, table_scale, jnp.where(slot_unit < (VS + 3 * HS) // UR, MODEL_DIMENSION ** (-0.5), (SEQUENCE_TOKENS / (4.0 * MODEL_DIMENSION)) ** 0.5))
    return noise * scale * slot_filled


def draw_master_first(key, part):
    slot_unit, slot_filled = slot_layout(owner_table(key))
    key = jax.random.fold_in(key, 12)
    noise = jax.random.normal(key, (RANKS, OWNERS, MOST, UR, MODEL_DIMENSION), jnp.float32)
    return noise * 0.111 * gradient_size(slot_unit) * slot_filled


def draw_master_second(key, part):
    slot_unit, slot_filled = slot_layout(owner_table(key))
    key = jax.random.fold_in(key, 13)
    factor = jnp.exp(jax.random.uniform(key, (RANKS, OWNERS, MOST, UR, MODEL_DIMENSION), jnp.float32, jnp.log(0.5), jnp.log(8.0)))
    size = gradient_size(slot_unit)
    return factor * 0.0526 * size * size * slot_filled


def draw_counted(key, part):
    key = jax.random.fold_in(key, 21)
    sequence = jnp.arange(SEQUENCE_COUNT, dtype=jnp.int32)[:, None, None]
    position = jnp.arange(SEQUENCE_TOKENS, dtype=jnp.int32)[None, :, None]
    ahead = jnp.arange(2, dtype=jnp.int32)[None, None, :]
    chance = (SEQUENCE_COUNT - 1 + 2 * sequence) * (SEQUENCE_TOKENS - 1 + 2 * position)
    rolled = jax.random.randint(key, (SEQUENCE_COUNT, SEQUENCE_TOKENS, 2), 0, 9 * (SEQUENCE_COUNT - 1) * (SEQUENCE_TOKENS - 1))
    picked = (rolled < chance) & (position + ahead + 1 < SEQUENCE_TOKENS) | (position == 0)
    return picked.astype(jnp.int32)


def place_ends(entries, key, low, high):
    longest = entries.shape.index(max(entries.shape))
    spots = []
    for shift in (0, 1):
        where = [jax.random.randint(jax.random.fold_in(key, axis), (), 0, length) for axis, length in enumerate(entries.shape)]
        where[longest] = (where[longest] + shift) % entries.shape[longest]
        spots.append(tuple(where))
    return entries.at[spots[0]].set(low).at[spots[1]].set(high)


def level_of(stream_key, dims, cuts, least, largest):
    def one(dim, blocks):
        steps = jax.random.uniform(jax.random.fold_in(jax.random.fold_in(stream_key, 6), dim), (blocks,), jnp.float32, least / len(cuts), largest / len(cuts))
        return jnp.repeat(jnp.exp(steps), dims[dim] // blocks).reshape((-1,) + (1,) * (len(dims) - dim - 1))

    factor_of = one(*cuts[0])
    for cut in cuts[1:]:
        factor_of = factor_of * one(*cut)
    return factor_of


def rank_table(count, lean):
    portions = [(1 << 20) // math.isqrt(grade ** lean) + 1 for grade in range(1, count + 1)]
    deviation = 1 + sum(portions) // (1 << 30)
    return np.cumsum(np.array([max(1, weight // deviation) for weight in portions]))


def ranked(stream_key, extent, count, lean):
    table = rank_table(count, lean)
    lot = jax.random.randint(jax.random.fold_in(stream_key, 1), extent, 0, int(table[count - 1]))
    rank = jnp.searchsorted(jnp.asarray(table, jnp.int32), lot, side="right")
    return jax.random.permutation(jax.random.fold_in(stream_key, 2), count)[rank].astype(jnp.int32)


def different_ones(rng, rows, count, top, lift):
    ranking = jax.random.permutation(jax.random.fold_in(rng, 1), count)
    pull = ranking
    for power in range(3):
        pull = pull * pull // count
    pull = pull * lift // count
    tickets = jax.random.randint(jax.random.fold_in(rng, 2), (rows, count), 0, 4096) + pull
    fixed_rows = jax.random.permutation(jax.random.fold_in(rng, 3), rows)[jnp.arange(count) % rows]
    tickets = jnp.where(jnp.arange(rows)[:, None] == fixed_rows[None, :], 1 << 14, tickets)
    score = tickets * count + jnp.arange(count)
    return lax.top_k(score.astype(jnp.int32), top)[1].astype(jnp.int32)


def gaussian(rng, extent, spread, most, pieces=(), kind=jnp.bfloat16):
    gain = level_of(rng, extent, pieces, -0.22, 0.18) if pieces else 1.0
    values = jax.random.normal(rng, extent, jnp.float32) * spread * gain
    return jnp.minimum(jnp.maximum(values, -most), most).astype(kind)


def setup_inputs(seed: int = 0) -> dict:
    splits = jax.random.split(jax.random.key(seed), 25)
    return {
        "token_ids": place_ends(ranked(splits[0], (SEQUENCE_COUNT, SEQUENCE_TOKENS), VOCAB, 2), jax.random.fold_in(splits[0], 3), 0, VOCAB - 1).astype(jnp.int32),
        "targets": place_ends(ranked(splits[1], (SEQUENCE_COUNT, SEQUENCE_TOKENS, TOP), VOCAB, 2), jax.random.fold_in(splits[1], 3), 0, VOCAB - 1).astype(jnp.int32),
        "counted": draw_counted(jax.random.fold_in(splits[24], 71), 0),
        "routes": different_ones(splits[3], SEQUENCE_COUNT * SEQUENCE_TOKENS, EXPERTS, 2, 2048).reshape((SEQUENCE_COUNT, SEQUENCE_TOKENS, TOP)),
        "priority": jax.vmap(lambda own: jax.random.permutation(own, TOK_DEV))(jax.random.split(splits[4], OWNERS)).reshape((OWNERS, TOK_DEV)).astype(jnp.int32),
        "owner_of": draw_owner_of(jax.random.fold_in(splits[24], 71), 0),
        "master": draw_master(jax.random.fold_in(splits[24], 71), 0),
        "master_first": draw_master_first(jax.random.fold_in(splits[24], 71), 0),
        "master_second": draw_master_second(jax.random.fold_in(splits[24], 71), 0),
        "expert_in": gaussian(splits[9], (EXPERTS, MODEL_DIMENSION, F), MODEL_DIMENSION ** -0.5, 0.21875, ((0, 8), (2, 4)), jnp.float32),
        "expert_in_first": gaussian(splits[10], (EXPERTS, MODEL_DIMENSION, F), (0.111 * 0.02 * (TOKENS * EXPERTS) ** -0.5), 0.00012207031, ((0, 8), (2, 4)), jnp.float32),
        "expert_in_second": jnp.clip(jnp.exp(math.log(2.5683593030123575e-09) - 2.7725887 * jax.random.uniform(splits[11], (EXPERTS, MODEL_DIMENSION, F), jnp.float32) ** level_of(splits[11], (EXPERTS, MODEL_DIMENSION, F), ((0, 8), (2, 4)), -0.2, 0.2)), 1.6052245643827234e-10, 2.5683593030123575e-09),
        "expert_out": gaussian(splits[12], (EXPERTS, F, MODEL_DIMENSION), F ** -0.5, 0.109375, ((0, 8), (1, 4)), jnp.float32),
        "expert_out_first": gaussian(splits[13], (EXPERTS, F, MODEL_DIMENSION), (0.111 * 0.04 * (TOKENS * EXPERTS) ** -0.5), 0.00024414062, ((0, 8), (1, 4)), jnp.float32),
        "expert_out_second": jnp.clip(jnp.exp(math.log(1.027343721204943e-08) - 2.7725887 * jax.random.uniform(splits[14], (EXPERTS, F, MODEL_DIMENSION), jnp.float32) ** level_of(splits[14], (EXPERTS, F, MODEL_DIMENSION), ((0, 8), (1, 4)), -0.2, 0.2)), 6.420898257530894e-10, 1.027343721204943e-08),
        "norm_gains": jnp.clip(1.0 + 0.1 * jax.random.normal(splits[15], (3, MODEL_DIMENSION), jnp.float32), 0.5, 1.5),
        "norm_gains_first": gaussian(splits[16], (3, MODEL_DIMENSION), (0.111 * 0.2 * TOKENS ** -0.5), 0.00390625, (), jnp.float32),
        "norm_gains_second": jnp.clip(jnp.exp(jax.random.uniform(splits[17], (3, MODEL_DIMENSION), jnp.float32, math.log(1.284179660387963e-07), math.log(2.0546874566207407e-06))), 1.284179660387963e-07, 2.0546874566207407e-06),
        "router": gaussian(splits[18], (MODEL_DIMENSION, EXPERTS), MODEL_DIMENSION ** -0.5, 0.21875, (), jnp.float32),
        "router_first": gaussian(splits[19], (MODEL_DIMENSION, EXPERTS), (0.111 * 0.1 * TOKENS ** -0.5), 0.001953125, (), jnp.float32),
        "router_second": jnp.clip(jnp.exp(jax.random.uniform(splits[20], (MODEL_DIMENSION, EXPERTS), jnp.float32, math.log(3.2104491509699074e-08), math.log(5.136718641551852e-07))), 3.2104491509699074e-08, 5.136718641551852e-07),
        "rel_bias": gaussian(splits[21], (H, NB), 0.5, 3.0, ((0, 4),), jnp.float32),
        "rel_bias_first": gaussian(splits[22], (H, NB), (0.111 * 0.05 * BLOCK * (SEQUENCE_COUNT * NB) ** 0.5 * TOKENS ** -1), 0.015625, ((0, 4),), jnp.float32),
        "rel_bias_second": jnp.clip(jnp.exp(math.log(3.287499930593185e-05) - 2.7725887 * jax.random.uniform(splits[23], (H, NB), jnp.float32) ** level_of(splits[23], (H, NB), ((0, 4),), -0.2, 0.2)), 2.0546874566207407e-06, 3.287499930593185e-05),
    }


highest_precision = lax.Precision.HIGHEST
beta_first = 0.9
beta_second = 0.95
adam_epsilon = 1e-08
norm_epsilon = 1e-06
ahead_weight = 0.3
masked_score = -1e+30
rate_table = 0.1
rate_query = 0.05
rate_values = 0.05
rate_project = 0.5
rate_inner = 0.05
rate_outer = 0.03
rate_gains = 0.5
rate_router = 0.05
rate_biases = 0.5
decay_rate = 0.1

@jax.custom_vjp
def reduced_precision(v):
    return lax.optimization_barrier(v.astype(jnp.bfloat16)).astype(jnp.float32)

@jax.custom_vjp
def reduced_backward(v):
    return v

def low_keep(v):
    return (reduced_precision(v), None)

def low_pass(kept, grad):
    return (grad,)

def back_keep(v):
    return (v, None)

def back_low(kept, grad):
    return (reduced_precision(grad),)
reduced_precision.defvjp(low_keep, low_pass)
reduced_backward.defvjp(back_keep, back_low)

def rms_norm(values, gain_row):
    return values * lax.rsqrt(lax.optimization_barrier(jnp.mean(values * values, -1, keepdims=True)) + norm_epsilon) * gain_row

def adam_update(weight, moment_one, moment_two, gradient, step_rate, decay_factor):
    moment_new = beta_first * moment_one + (1.0 - beta_first) * gradient
    square_new = beta_second * moment_two + (1.0 - beta_second) * gradient * gradient
    moment_hat = moment_new / (1.0 - beta_first ** STEP)
    square_hat = square_new / (1.0 - beta_second ** STEP)
    weight_new = weight - step_rate * (moment_hat / (jnp.sqrt(square_hat) + adam_epsilon) + decay_factor * weight)
    return (weight_new, moment_new, square_new)

def slot_tables(owner_ids, owners, most_units):
    unit_count = owner_ids.shape[0]
    unit_index = jnp.arange(unit_count, dtype=jnp.int32)
    earlier = (owner_ids[None, :] == owner_ids[:, None]) & (unit_index[None, :] < unit_index[:, None])
    unit_rank = lax.optimization_barrier(jnp.sum(earlier.astype(jnp.int32), 1)).astype(jnp.int32)
    placed = (owner_ids[None, None, :] == jnp.arange(owners, dtype=jnp.int32)[:, None, None]) & (unit_rank[None, None, :] == jnp.arange(most_units, dtype=jnp.int32)[None, :, None])
    slot_filled = jnp.any(placed, 2)
    slot_unit = lax.optimization_barrier(jnp.sum(jnp.where(placed, unit_index[None, None, :], 0), 2)).astype(jnp.int32)
    return (unit_rank, slot_unit, slot_filled)

def unit_rates(unit_ids, table_units, query_units, value_units):
    return jnp.where(unit_ids < table_units, rate_table, jnp.where(unit_ids < query_units, rate_query, jnp.where(unit_ids < value_units, rate_values, rate_project)))

def pair_slots(route_pairs, priorities, experts, capacity):
    tokens_here = priorities.shape[0]
    pair_expert = route_pairs.T.reshape(-1).astype(jnp.int32)
    pair_key = (jnp.arange(2, dtype=jnp.int32)[:, None] * tokens_here + priorities[None, :].astype(jnp.int32)).reshape(-1)
    before = (pair_expert[None, :] == pair_expert[:, None]) & (pair_key[None, :] < pair_key[:, None])
    pair_rank = lax.optimization_barrier(jnp.sum(before.astype(jnp.int32), 1)).astype(jnp.int32)
    pair_kept = pair_rank < capacity
    pair_dest = (pair_expert * capacity + jnp.minimum(pair_rank, capacity - 1)).astype(jnp.int32)
    target_slot = jnp.where(pair_kept, pair_dest, experts * capacity).astype(jnp.int32)
    slot_source = jnp.full((experts * capacity,), 2 * tokens_here, jnp.int32).at[target_slot].set(jnp.arange(2 * tokens_here, dtype=jnp.int32), mode='drop')
    return (pair_kept, pair_dest, slot_source)

def to_devices(values):
    rest = values.shape[2:]
    shaped = values.reshape((N_DP, SEQ, N_CTX, HALF) + rest)
    return jnp.swapaxes(shaped, 1, 2).reshape((OWNERS, TOK_DEV) + rest)

def from_devices(values):
    rest = values.shape[2:]
    shaped = values.reshape((N_DP, N_CTX, SEQ, HALF) + rest)
    return jnp.swapaxes(shaped, 1, 2).reshape((SEQUENCE_COUNT, SEQUENCE_TOKENS) + rest)

def sequence_attention(seq_items, bias_table):
    queries, keys, values = seq_items
    outputs = []
    for context in range(N_CTX):
        query_part = queries[context * HALF:(context + 1) * HALF]
        key_parts = [keys[context * HALF:(context + 1) * HALF]]
        value_parts = [values[context * HALF:(context + 1) * HALF]]
        if context > 0:
            key_parts = [reduced_backward(keys[:context * HALF])] + key_parts
            value_parts = [reduced_backward(values[:context * HALF])] + value_parts
        key_all = jnp.concatenate(key_parts, 0)
        value_all = jnp.concatenate(value_parts, 0)
        query_blocks = (context * HALF + jnp.arange(HALF, dtype=jnp.int32)) // BLOCK
        key_blocks = jnp.arange((context + 1) * HALF, dtype=jnp.int32) // BLOCK
        distance = (query_blocks[:, None] - key_blocks[None, :]).astype(jnp.int32)
        bias_full = bias_table[:, jnp.clip(distance, 0, NB - 1)]
        scores = jnp.einsum('qhd,khd->hqk', query_part, key_all, precision=highest_precision) * HD ** (-0.5) + bias_full
        scores = jnp.where(distance[None] >= 0, reduced_backward(scores), masked_score)
        peak_value = lax.optimization_barrier(jnp.max(scores, -1, keepdims=True))
        exp_scores = jnp.exp(scores - peak_value)
        softmax_probs = exp_scores / lax.optimization_barrier(jnp.sum(exp_scores, -1, keepdims=True))
        attention_output = jnp.einsum('hqk,khd->qhd', reduced_precision(softmax_probs), value_all, precision=highest_precision)
        outputs.append(reduced_precision(reduced_backward(attention_output)))
    return jnp.concatenate(outputs, 0)

def sequence_loss(seq_items, table_low):
    normed, wanted, weights = seq_items
    logits = reduced_backward(jnp.einsum('ld,vd->lv', normed, table_low, precision=highest_precision))
    peak_value = lax.optimization_barrier(jnp.max(logits, -1, keepdims=True))
    logsum = peak_value[:, 0] + jnp.log(lax.optimization_barrier(jnp.sum(jnp.exp(logits - peak_value), -1)))
    target_logits = jnp.take_along_axis(logits, wanted, 1)
    return jnp.sum(weights * (logsum[:, None] - target_logits))

def reference(token_ids, targets, counted, routes, priority, owner_of, master, master_first, master_second, expert_in, expert_in_first, expert_in_second, expert_out, expert_out_first, expert_out_second, norm_gains, norm_gains_first, norm_gains_second, router, router_first, router_second, rel_bias, rel_bias_first, rel_bias_second):
    owner_ids = owner_of[:, 0].astype(jnp.int32)
    unit_rank, slot_unit, slot_filled = slot_tables(owner_ids, OWNERS, MOST)
    units = master[:, owner_ids, unit_rank].reshape(RANKS, UNITS * UR, MODEL_DIMENSION)
    joint = units[:, VS:VS + 3 * HS].reshape(RANKS, 3, HS, MODEL_DIMENSION)
    model_parameters = {'table': units[:, :VS].reshape(VOCAB, MODEL_DIMENSION), 'query': joint[:, 0].reshape(MODEL_DIMENSION, MODEL_DIMENSION), 'keys': joint[:, 1].reshape(MODEL_DIMENSION, MODEL_DIMENSION), 'values': joint[:, 2].reshape(MODEL_DIMENSION, MODEL_DIMENSION), 'project': units[:, VS + 3 * HS:].reshape(MODEL_DIMENSION, MODEL_DIMENSION), 'gains': norm_gains, 'router': router, 'biases': rel_bias, 'inner': expert_in, 'outer': expert_out}
    pair_kept, pair_dest, slot_source = jax.vmap(lambda route_pairs, priorities: pair_slots(route_pairs, priorities, EXPERTS, CAP))(to_devices(routes), priority)
    slot_full = (slot_source < 2 * TOK_DEV).astype(jnp.float32)
    slot_token = (slot_source % TOK_DEV).astype(jnp.int32)
    kept_rows = pair_kept.astype(jnp.float32)
    loss_weights = counted.astype(jnp.float32) * jnp.array([1.0, ahead_weight], jnp.float32)
    loss_weight = jnp.sum(loss_weights)
    shard_width = F // RANKS

    def forward(model_parameters):
        table_low = reduced_precision(model_parameters['table'])
        stream_zero = math.sqrt(MODEL_DIMENSION) * jnp.take(table_low, token_ids, axis=0)
        first_normalized = reduced_precision(rms_norm(stream_zero, model_parameters['gains'][0]))
        projected = []
        for weight_label in ('query', 'keys', 'values'):
            created_result = jnp.einsum('qif,gf->qig', first_normalized, reduced_precision(model_parameters[weight_label]), precision=highest_precision)
            projected.append(reduced_precision(reduced_backward(created_result)).reshape(SEQUENCE_COUNT, SEQUENCE_TOKENS, H, HD))
        attention_output = lax.map(jax.checkpoint(lambda seq_items: sequence_attention(seq_items, model_parameters['biases'])), tuple(projected))
        residual_branch = reduced_backward(jnp.einsum('myu,uo->myo', attention_output.reshape(SEQUENCE_COUNT, SEQUENCE_TOKENS, MODEL_DIMENSION), reduced_precision(model_parameters['project']), precision=highest_precision))
        stream_one = stream_zero + residual_branch
        second_normalized = reduced_precision(rms_norm(stream_one, model_parameters['gains'][1]))
        router_scores_raw = reduced_backward(jnp.einsum('ifo,oz->ifz', second_normalized, reduced_precision(model_parameters['router']), precision=highest_precision))
        gate_values = jax.nn.softmax(jnp.take_along_axis(router_scores_raw, routes, 2), -1)
        token_rows = to_devices(second_normalized)
        dispatch = (jnp.take_along_axis(token_rows, slot_token[..., None], 1) * slot_full[..., None]).reshape(OWNERS, EXPERTS, CAP, MODEL_DIMENSION)
        gate_rows = to_devices(gate_values)
        inner_low = reduced_precision(model_parameters['inner'])
        outer_low = reduced_precision(model_parameters['outer'])
        mixture = jnp.zeros((OWNERS, TOK_DEV, MODEL_DIMENSION), jnp.float32)
        for shard_index in range(RANKS):
            column_range = slice(shard_index * shard_width, (shard_index + 1) * shard_width)
            sent = reduced_backward(dispatch)
            hidden_pre = reduced_backward(jnp.einsum('oecd,edf->oecf', sent, inner_low[:, :, column_range], precision=highest_precision))
            active = reduced_precision(jax.nn.gelu(hidden_pre, approximate=True))
            partial_out = reduced_precision(reduced_backward(jnp.einsum('oecf,efd->oecd', active, outer_low[:, column_range], precision=highest_precision))).reshape(OWNERS, EXPERTS * CAP, MODEL_DIMENSION)
            picked = (jnp.take_along_axis(partial_out, pair_dest[..., None], 1) * kept_rows[..., None]).reshape(OWNERS, 2, TOK_DEV, MODEL_DIMENSION)
            mixture = mixture + gate_rows[..., 0:1] * picked[:, 0] + gate_rows[..., 1:2] * picked[:, 1]
        stream_two = stream_one + from_devices(mixture)
        normed_three = reduced_precision(rms_norm(stream_two, model_parameters['gains'][2]))
        losses = lax.map(jax.checkpoint(lambda seq_items: sequence_loss(seq_items, table_low)), (normed_three, targets, loss_weights))
        loss_sum = jnp.sum(losses)
        return (loss_sum / loss_weight, loss_sum)
    loss_mean, backward, loss_sum = jax.vjp(forward, model_parameters, has_aux=True)
    grads = backward(jnp.ones((), jnp.float32))[0]
    joint_grads = jnp.stack([grads['query'].reshape(RANKS, HS, MODEL_DIMENSION), grads['keys'].reshape(RANKS, HS, MODEL_DIMENSION), grads['values'].reshape(RANKS, HS, MODEL_DIMENSION)], 1).reshape(RANKS, 3 * HS, MODEL_DIMENSION)
    unit_grads = jnp.concatenate([grads['table'].reshape(RANKS, VS, MODEL_DIMENSION), joint_grads, grads['project'].reshape(RANKS, HS, MODEL_DIMENSION)], 1).reshape(RANKS, UNITS, UR, MODEL_DIMENSION)
    slot_grads = unit_grads[:, slot_unit] * slot_filled[None, :, :, None, None].astype(jnp.float32)
    slot_rates = unit_rates(slot_unit, VS // UR, (VS + 2 * HS) // UR, (VS + 3 * HS) // UR)[None, :, :, None, None]
    master_new, master_first_new, master_second_new = adam_update(master, master_first, master_second, slot_grads, slot_rates, decay_rate)
    inner_new, inner_first_new, inner_second_new = adam_update(expert_in, expert_in_first, expert_in_second, grads['inner'], rate_inner, decay_rate)
    outer_new, outer_first_new, outer_second_new = adam_update(expert_out, expert_out_first, expert_out_second, grads['outer'], rate_outer, decay_rate)
    gains_new, gains_first_new, gains_second_new = adam_update(norm_gains, norm_gains_first, norm_gains_second, grads['gains'], rate_gains, 0.0)
    router_new, router_first_new, router_second_new = adam_update(router, router_first, router_second, grads['router'], rate_router, decay_rate)
    biases_new, biases_first_new, biases_second_new = adam_update(rel_bias, rel_bias_first, rel_bias_second, grads['biases'], rate_biases, 0.0)
    loss_totals = jnp.stack([loss_sum, loss_weight])
    return (loss_totals, master_new, master_first_new, master_second_new, inner_new, inner_first_new, inner_second_new, outer_new, outer_first_new, outer_second_new, gains_new, gains_first_new, gains_second_new, router_new, router_first_new, router_second_new, biases_new, biases_first_new, biases_second_new)
```

```python
import functools
import math

import jax
import jax.numpy as jnp
from jax import lax
from jax.experimental import pallas as pl
from jax.experimental.pallas import tpu as pltpu
from jax.sharding import PartitionSpec as P

VOCAB = 32000
BLOCK = 256
STEP = 10


highest_precision = lax.Precision.HIGHEST
beta_first = 0.9
beta_second = 0.95
adam_epsilon = 1e-08
norm_epsilon = 1e-06
ahead_weight = 0.3
masked_score = -1e30
rate_table = 0.1
rate_query = 0.05
rate_values = 0.05
rate_project = 0.5
rate_inner = 0.05
rate_outer = 0.03
rate_gains = 0.5
rate_router = 0.05
rate_biases = 0.5
decay_rate = 0.1


def passed_along(value, axis, steps):
    count = lax.axis_size(axis)
    initial, last = (max(0, -steps), min(count, count - steps))
    return lax.ppermute(value, axis, [(source, source + steps) for source in range(initial, last)])

MESH_ID = pl.DeviceIdType.MESH
whole_vmem = pl.BlockSpec(memory_space=pltpu.VMEM)
whole_any = pl.BlockSpec(memory_space=pl.ANY)
line_rows = 128
line_lag = 3


def sum_line_kernel(
    count, meets_all, prologue, epilogue, n_extra, n_aux, n_scratch, part_ref, *refs
):
    extras = refs[:n_extra]
    out_ref = refs[n_extra]
    aux = refs[n_extra + 1 : n_extra + 1 + n_aux]
    rest = refs[n_extra + 1 + n_aux :]
    scratch = rest[:n_scratch]
    stage, from_end, from_mid, send_sem, end_sem, mid_sem, back_sem, back_recv = rest[n_scratch:]
    rank = lax.axis_index("tensor")
    inner = (rank == 1) | (rank == 2)
    end_peer = jnp.where(rank < 2, 1 - rank, 5 - rank)
    mid_peer = 3 - rank
    barrier = pltpu.get_barrier_semaphore()
    if not meets_all:
        pl.semaphore_signal(barrier, inc=1, device_id={"tensor": end_peer}, device_id_type=MESH_ID)

        @pl.when(inner)
        def _():
            pl.semaphore_signal(
                barrier, inc=1, device_id={"tensor": mid_peer}, device_id_type=MESH_ID
            )
            pl.semaphore_wait(barrier, 2)

        @pl.when(jnp.logical_not(inner))
        def _():
            pl.semaphore_wait(barrier, 1)
    else:
        for step in (1, 2, 3):
            other = lax.rem(rank + step, 4)
            pl.semaphore_signal(barrier, inc=1, device_id={"tensor": other}, device_id_type=MESH_ID)
        pl.semaphore_wait(barrier, 3)

    rows = line_rows

    def span(i):
        return pl.ds(pl.multiple_of(i * rows, rows), rows)

    def to_inner(i):
        return pltpu.make_async_remote_copy(
            src_ref=stage.at[i],
            dst_ref=from_end.at[i],
            send_sem=send_sem.at[i],
            recv_sem=end_sem.at[i],
            device_id={"tensor": end_peer},
            device_id_type=MESH_ID,
        )

    def to_middle(i):
        return pltpu.make_async_remote_copy(
            src_ref=stage.at[i],
            dst_ref=from_mid.at[i],
            send_sem=send_sem.at[i],
            recv_sem=mid_sem.at[i],
            device_id={"tensor": mid_peer},
            device_id_type=MESH_ID,
        )

    def to_end(i):
        return pltpu.make_async_remote_copy(
            src_ref=out_ref.at[span(i)],
            dst_ref=out_ref.at[span(i)],
            send_sem=back_sem.at[i],
            recv_sem=back_recv.at[i],
            device_id={"tensor": end_peer},
            device_id_type=MESH_ID,
        )

    @pl.when(jnp.logical_not(inner))
    def _():
        def push(i, carry):
            stage[i] = part_ref[span(i)].astype(jnp.bfloat16)
            to_inner(i).start()
            return carry

        lax.fori_loop(0, count, push, 0)

    if prologue is not None:
        prologue(rank, extras, aux, scratch)

    @pl.when(inner)
    def _():
        def step(i, carry):
            @pl.when(i < count)
            def _():
                to_inner(i).wait_recv()
                mine = part_ref[span(i)].astype(jnp.float32) + from_end[i].astype(jnp.float32)
                stage[i] = mine.astype(jnp.bfloat16)
                to_middle(i).start()

            @pl.when(i >= line_lag)
            def _():
                j = i - line_lag
                to_middle(j).wait_recv()
                total = stage[j].astype(jnp.float32) + from_mid[j].astype(jnp.float32)
                out_ref[span(j)] = epilogue(total, span(j), rank, extras, aux, scratch)
                to_end(j).start()

            return carry

        lax.fori_loop(0, count + line_lag, step, 0)

        def drain(i, carry):
            to_middle(i).wait_send()
            to_end(i).wait_send()
            return carry

        lax.fori_loop(0, count, drain, 0)

    @pl.when(jnp.logical_not(inner))
    def _():
        def finish(i, carry):
            to_end(i).wait_recv()
            to_inner(i).wait_send()
            return carry

        lax.fori_loop(0, count, finish, 0)


def sum_line(
    part, extras, aux_shapes, epilogue, collective_id, prologue=None, scratch=(), meets_all=False
):
    tokens, width = part.shape
    count = tokens // line_rows
    chunks = pltpu.VMEM((count, line_rows, width), jnp.bfloat16)
    return pl.pallas_call(
        functools.partial(
            sum_line_kernel,
            count,
            meets_all,
            prologue,
            epilogue,
            len(extras),
            len(aux_shapes),
            len(scratch),
        ),
        out_shape=[jax.ShapeDtypeStruct((tokens, width), jnp.bfloat16)] + list(aux_shapes),
        in_specs=[whole_vmem] * (1 + len(extras)),
        out_specs=[whole_vmem] * (1 + len(aux_shapes)),
        scratch_shapes=list(scratch)
        + [chunks, chunks, chunks]
        + [pltpu.SemaphoreType.DMA((count,))] * 5,
        compiler_params=pltpu.CompilerParams(
            collective_id=collective_id, has_side_effects=True, vmem_limit_bytes=48 << 20
        ),
    )(part, *extras)


def keep_total(total, span, rank, extras, aux, scratch):
    return total.astype(jnp.bfloat16)


def inverse_rms(values):
    return lax.rsqrt(jnp.mean(values * values, -1, keepdims=True) + norm_epsilon)


def finish_mixture(total, span, rank, extras, aux, scratch):
    stream_one, gain = extras
    stream_two = stream_one[span] + total
    aux[0][span] = stream_two
    return (stream_two * inverse_rms(stream_two) * gain[...]).astype(jnp.bfloat16)


def norm_back_rows(values, gain, upstream):
    inverse = inverse_rms(values)
    normed = values * inverse
    scaled = upstream * gain
    gain_grad = jnp.sum(upstream * normed, 0, keepdims=True)
    inputs_grad = inverse * (scaled - normed * jnp.mean(scaled * normed, -1, keepdims=True))
    return (inputs_grad, gain_grad)


def clear_gain(rank, extras, aux, scratch):
    aux[-1][...] = jnp.zeros_like(aux[-1])


def add_gain(rank, ref, gain_grad):
    ref[...] += jnp.where(rank == 1, gain_grad, 0.0)


def finish_head_grad(total, span, rank, extras, aux, scratch):
    stream_two, gain = extras
    grad_two, gain_grad = norm_back_rows(stream_two[span], gain[...], total)
    aux[0][span] = grad_two
    add_gain(rank, aux[1], gain_grad)
    return grad_two.astype(jnp.bfloat16)


def start_router_grad(rank, extras, aux, scratch):
    stream_one, gain, grad_two, gate_part, gates, routes, router_low = extras
    grad_one, logit_grad, gain_grad = aux
    landed, gate_send, gate_recv = scratch
    gain_grad[...] = jnp.zeros_like(gain_grad)
    copies = []
    for step in (1, 2, 3):
        copy = pltpu.make_async_remote_copy(
            src_ref=gate_part,
            dst_ref=landed.at[step - 1],
            send_sem=gate_send.at[step - 1],
            recv_sem=gate_recv.at[step - 1],
            device_id={"tensor": lax.rem(rank + step, 4)},
            device_id_type=MESH_ID,
        )
        copy.start()
        copies.append(copy)
    for copy in copies:
        copy.wait()
    gate_grad = jnp.zeros(gate_part.shape, jnp.float32)
    for source in range(4):
        piece = jnp.zeros(gate_part.shape, jnp.float32)
        for step in (1, 2, 3):
            piece = jnp.where(lax.rem(source + step, 4) == rank, landed[step - 1], piece)
        gate_grad = gate_grad + jnp.where(rank == source, gate_part[...], piece)
    weighted = gates[...] * gate_grad
    chosen = gates[...] * (gate_grad - (weighted[0:1] + weighted[1:2]))
    experts, tokens = logit_grad.shape
    row = lax.broadcasted_iota(jnp.int32, (experts, tokens), 0)
    placed = jnp.where(row == routes[0:1], chosen[0:1], 0.0) + jnp.where(
        row == routes[1:2], chosen[1:2], 0.0
    )
    logit_grad[...] = placed.astype(jnp.bfloat16)


def finish_expert_grad(total, span, rank, extras, aux, scratch):
    stream_one, gain, grad_two, gate_part, gates, routes, router_low = extras
    grad_one, logit_grad, gain_grad = aux
    upstream = total + lax.dot_general(
        logit_grad[:, span],
        router_low[...],
        (((0,), (1,)), ((), ())),
        preferred_element_type=jnp.float32,
    )
    part, gain_part = norm_back_rows(stream_one[span], gain[...], upstream)
    result = grad_two[span] + part
    grad_one[span] = result
    add_gain(rank, gain_grad, gain_part)
    return result.astype(jnp.bfloat16)


def finish_input_grad(scale, total, span, rank, extras, aux, scratch):
    embedded, gain, grad_one = extras
    stream_zero = embedded[span].astype(jnp.float32) * scale
    part, gain_part = norm_back_rows(stream_zero, gain[...], total)
    add_gain(rank, aux[0], gain_part)
    return ((grad_one[span] + part) * scale).astype(jnp.bfloat16)


def gather_line_kernel(count, *refs):
    ins = refs[:count]
    outs = refs[count : 2 * count]
    local_sem, send_sem, recv_sem = refs[2 * count :]
    rank = lax.axis_index("tensor")
    barrier = pltpu.get_barrier_semaphore()
    for step in (1, 2, 3):
        other = lax.rem(rank + step, 4)
        pl.semaphore_signal(barrier, inc=1, device_id={"tensor": other}, device_id_type=MESH_ID)
    pl.semaphore_wait(barrier, 3)
    copies = []
    for k in range(count):
        for step in (1, 2, 3):
            copy = pltpu.make_async_remote_copy(
                src_ref=ins[k],
                dst_ref=outs[k].at[rank],
                send_sem=send_sem.at[k, step - 1],
                recv_sem=recv_sem.at[k, step - 1],
                device_id={"tensor": lax.rem(rank + step, 4)},
                device_id_type=MESH_ID,
            )
            copy.start()
            copies.append(copy)
        own = pltpu.make_async_copy(ins[k], outs[k].at[rank], local_sem.at[k])
        own.start()
        own.wait()
    for copy in copies:
        copy.wait()


def gather_line(arrays, collective_id):
    count = len(arrays)
    return pl.pallas_call(
        functools.partial(gather_line_kernel, count),
        out_shape=[jax.ShapeDtypeStruct((4,) + x.shape, x.dtype) for x in arrays],
        in_specs=[whole_vmem] * count,
        out_specs=[whole_vmem] * count,
        scratch_shapes=[
            pltpu.SemaphoreType.DMA((count,)),
            pltpu.SemaphoreType.DMA((count, 3)),
            pltpu.SemaphoreType.DMA((count, 3)),
        ],
        compiler_params=pltpu.CompilerParams(
            collective_id=collective_id, has_side_effects=True, vmem_limit_bytes=40 << 20
        ),
    )(*arrays)


def pull_units_kernel(group, slots_ref, source_ref, out_ref, sem):
    start = pl.program_id(0) * group

    def push(u, carry):
        pltpu.make_async_copy(source_ref.at[slots_ref[start + u]], out_ref.at[u], sem).start()
        return carry

    lax.fori_loop(0, group, push, 0)
    pltpu.make_async_copy(out_ref, out_ref, sem).wait()


def pull_units(source, slots):
    count = slots.shape[0]
    unit_bytes = math.prod(source.shape[1:]) * source.dtype.itemsize
    group = max(k for k in range(1, count + 1) if count % k == 0 and (k <= 32 or k * unit_bytes < 15 << 20))
    return pl.pallas_call(
        functools.partial(pull_units_kernel, group),
        grid=(count // group,),
        out_shape=jax.ShapeDtypeStruct((count,) + source.shape[1:], source.dtype),
        in_specs=[pl.BlockSpec(memory_space=pltpu.SMEM), whole_any],
        out_specs=pl.BlockSpec((group,) + source.shape[1:], lambda k: (k,) + (0,) * (source.ndim - 1)),
        scratch_shapes=[pltpu.SemaphoreType.DMA],
        compiler_params=pltpu.CompilerParams(vmem_limit_bytes=40 << 20),
    )(slots, source)


def combined_all(x, axis, combine):
    everything = jax.tree.map(lambda part: lax.all_gather(part, axis), x)
    initial = jax.tree.map(lambda part: part[0], everything)

    def lap(k, so_far):
        return combine(so_far, jax.tree.map(lambda part: part[k], everything))

    return lax.fori_loop(1, lax.axis_size(axis), lap, initial)


def adam_update(weight, moment_one, moment_two, gradient, step_rate, decay_factor):
    moment_new = beta_first * moment_one + (1.0 - beta_first) * gradient
    square_new = beta_second * moment_two + (1.0 - beta_second) * gradient * gradient
    moment_hat = moment_new / (1.0 - beta_first**STEP)
    square_hat = square_new / (1.0 - beta_second**STEP)
    weight_new = weight - step_rate * (
        moment_hat / (jnp.sqrt(square_hat) + adam_epsilon) + decay_factor * weight
    )
    return (weight_new, moment_new, square_new)


def norm_forward(values, gain_row):
    return values * inverse_rms(values) * gain_row


def slot_tables(owner_ids, owners, most_units):
    unit_count = owner_ids.shape[0]
    unit_index = jnp.arange(unit_count, dtype=jnp.int32)
    earlier = (owner_ids[None, :] == owner_ids[:, None]) & (
        unit_index[None, :] < unit_index[:, None]
    )
    unit_rank = jnp.sum(earlier.astype(jnp.int32), 1)
    placed = (owner_ids[None, None, :] == jnp.arange(owners, dtype=jnp.int32)[:, None, None]) & (
        unit_rank[None, None, :] == jnp.arange(most_units, dtype=jnp.int32)[None, :, None]
    )
    slot_filled = jnp.any(placed, 2)
    slot_unit = jnp.sum(jnp.where(placed, unit_index[None, None, :], 0), 2)
    return (unit_rank, slot_unit, slot_filled)


def unit_rates(unit_ids, table_units, query_units, value_units):
    return jnp.where(
        unit_ids < table_units,
        rate_table,
        jnp.where(
            unit_ids < query_units,
            rate_query,
            jnp.where(unit_ids < value_units, rate_values, rate_project),
        ),
    )


def pair_slots(route_pairs, priorities, experts, capacity):
    tokens_here = priorities.shape[0]
    pair_expert = route_pairs.T.reshape(-1)
    pair_key = (
        jnp.arange(2, dtype=jnp.int32)[:, None] * tokens_here + priorities[None, :]
    ).reshape(-1)
    before = (pair_expert[None, :] == pair_expert[:, None]) & (
        pair_key[None, :] < pair_key[:, None]
    )
    pair_rank = jnp.sum(before.astype(jnp.int32), 1)
    pair_kept = pair_rank < capacity
    pair_dest = pair_expert * capacity + jnp.minimum(pair_rank, capacity - 1)
    return (pair_kept, pair_dest)


def gelu_tanh(values):
    return jax.nn.gelu(values, approximate=True)


def to_experts(buffer):
    return lax.all_to_all(buffer, ("dp", "ctx"), split_axis=0, concat_axis=0, tiled=True)


def from_experts(buffer):
    return lax.all_to_all(buffer, ("dp", "ctx"), split_axis=0, concat_axis=0, tiled=True)


def block_bias(bias_table, query_blocks, key_blocks, key_allowed):
    distance = query_blocks[:, None] - key_blocks[None, :]
    allowed = (distance >= 0) & key_allowed[None, :]
    buckets = bias_table.shape[1]
    onehot = (
        jnp.clip(distance, 0, buckets - 1)[:, :, None] == jnp.arange(buckets, dtype=jnp.int32)
    ).astype(jnp.float32)
    bias_block = jnp.einsum("qkr,hr->hqk", onehot, bias_table, precision=highest_precision)
    return (bias_block, allowed, onehot)


def tile_scores(query_tile, keys, bias_block, allowed):
    scores = jnp.einsum(
        "qhd,khd->hqk", query_tile, keys, preferred_element_type=jnp.float32
    ) * query_tile.shape[-1] ** (-0.5)
    head_count, row_count, column_count = scores.shape
    shaped = (
        scores.reshape(head_count, row_count // BLOCK, BLOCK, column_count // BLOCK, BLOCK)
        + bias_block[:, :, None, :, None]
    )
    return jnp.where(allowed[None, :, None, :, None], shaped, masked_score)


def tile_forward(query_tile, keys, values, bias_block, allowed):
    shaped = tile_scores(query_tile, keys, bias_block, allowed)
    peak_value = jnp.max(shaped, axis=(3, 4), keepdims=True)
    exp_scores = jnp.exp(shaped - peak_value)
    exp_total = jnp.sum(exp_scores, axis=(3, 4), keepdims=True)
    head_count = shaped.shape[0]
    softmax_low = (
        (exp_scores / exp_total)
        .astype(jnp.bfloat16)
        .reshape(head_count, query_tile.shape[0], keys.shape[0])
    )
    output = jnp.einsum("hqk,khd->qhd", softmax_low, values, preferred_element_type=jnp.float32)
    return (output.astype(jnp.bfloat16), peak_value + jnp.log(exp_total))


def tile_backward(query_tile, keys, values, grad_out, logsum, bias_block, allowed, onehot):
    shaped = tile_scores(query_tile, keys, bias_block, allowed)
    softmax_full = jnp.exp(shaped - logsum)
    head_count = shaped.shape[0]
    flat_shape = (head_count, query_tile.shape[0], keys.shape[0])
    softmax_low = softmax_full.reshape(flat_shape).astype(jnp.bfloat16)
    grad_softmax = jnp.einsum(
        "qhd,khd->hqk", grad_out, values, preferred_element_type=jnp.float32
    ).reshape(shaped.shape)
    row_inner = jnp.sum(softmax_full * grad_softmax, axis=(3, 4), keepdims=True)
    grad_scores = (softmax_full * (grad_softmax - row_inner)).astype(jnp.bfloat16)
    score_scale = query_tile.shape[-1] ** (-0.5)
    flat_scores = grad_scores.reshape(flat_shape)
    grad_query = (
        jnp.einsum("hqk,khd->qhd", flat_scores, keys, preferred_element_type=jnp.float32)
        * score_scale
    )
    grad_keys = (
        jnp.einsum("hqk,qhd->khd", flat_scores, query_tile, preferred_element_type=jnp.float32)
        * score_scale
    )
    grad_values = jnp.einsum(
        "hqk,qhd->khd", softmax_low, grad_out, preferred_element_type=jnp.float32
    )
    block_sums = jnp.sum(grad_scores.astype(jnp.float32), axis=(2, 4))
    grad_bias = jnp.einsum("hqk,qkr->hr", block_sums, onehot, precision=highest_precision)
    return (grad_query, grad_keys, grad_values, grad_bias)


def on_device(
    token_ids,
    targets,
    counted,
    routes,
    priority,
    owner_of,
    master,
    master_first,
    master_second,
    expert_in,
    expert_in_first,
    expert_in_second,
    expert_out,
    expert_out_first,
    expert_out_second,
    norm_gains,
    norm_gains_first,
    norm_gains_second,
    router,
    router_first,
    router_second,
    rel_bias,
    rel_bias_first,
    rel_bias_second,
):
    owners = lax.axis_size(("dp", "ctx"))
    tensor_ranks = lax.axis_size("tensor")
    my_owner = lax.axis_index(("dp", "ctx"))
    my_rank = lax.axis_index("tensor")
    my_context = lax.axis_index("ctx")
    sequences, half_length = token_ids.shape
    tokens_here = sequences * half_length
    most_units = master.shape[2]
    unit_rows = master.shape[3]
    model_width = master.shape[4]
    vocab_here = VOCAB // tensor_ranks
    heads_here = rel_bias.shape[0]
    head_size = model_width // (heads_here * tensor_ranks)
    hidden_here = heads_here * head_size
    experts = router.shape[1]
    experts_here = expert_in.shape[0]
    capacity = (18 * tokens_here + 8 * experts - 1) // (8 * experts)
    tile_rows = min(half_length, 512)
    head_rows_count = min(tokens_here, 512)
    table_units = vocab_here // unit_rows
    query_units = table_units + 2 * hidden_here // unit_rows
    value_units = table_units + 3 * hidden_here // unit_rows
    embed_scale = math.sqrt(model_width)
    owner_ids = owner_of[:, 0]
    unit_rank, slot_unit, slot_filled = slot_tables(owner_ids, owners, most_units)
    gathered = lax.all_gather(master[0, 0].astype(jnp.bfloat16), ("dp", "ctx"), axis=0, tiled=True)
    weights_low = pull_units(gathered, owner_ids * most_units + unit_rank).reshape(-1, model_width)
    table_low = weights_low[:vocab_here]
    joint_low = weights_low[vocab_here : vocab_here + 3 * hidden_here]
    project_low = weights_low[vocab_here + 3 * hidden_here :]
    rolled = [project_low] + [
        lax.ppermute(project_low, "tensor", [(source, (source + step) % 4) for source in range(4)])
        for step in (1, 2, 3)
    ]
    project_full = lax.dynamic_slice_in_dim(
        jnp.concatenate(rolled[::-1] + rolled[::-1], 0), (3 - my_rank) * hidden_here, model_width, 0
    )
    local_ids = token_ids.reshape(-1) - my_rank * vocab_here
    inside = (local_ids >= 0) & (local_ids < vocab_here)
    clipped_ids = jnp.clip(local_ids, 0, vocab_here - 1)
    looked = jnp.where(inside[:, None], jnp.take(table_low, clipped_ids, axis=0), 0)
    gain_rows = [norm_gains[k : k + 1] for k in range(3)]
    stream_shape = jax.ShapeDtypeStruct((tokens_here, model_width), jnp.float32)
    gain_shape = jax.ShapeDtypeStruct((1, model_width), jnp.float32)
    (embedded,) = sum_line(looked, [], [], keep_total, 1)
    stream_zero = embedded.astype(jnp.float32) * embed_scale
    first_normalized = norm_forward(stream_zero, norm_gains[0])
    normed_one_low = first_normalized.astype(jnp.bfloat16)
    joint = lax.dot_general(
        normed_one_low, joint_low, (((1,), (1,)), ((), ())), preferred_element_type=jnp.float32
    ).astype(jnp.bfloat16)
    queries = joint[:, :hidden_here].reshape(sequences, half_length, heads_here, head_size)
    pairs_here = joint[:, hidden_here:].reshape(sequences, half_length, 2 * hidden_here)
    pairs_before = passed_along(pairs_here, "ctx", 1)
    keyvals = jnp.concatenate([pairs_before, pairs_here], 1).reshape(
        sequences, 2 * half_length, 2, heads_here, head_size
    )
    keys_all = keyvals[:, :, 0]
    values_all = keyvals[:, :, 1]
    blocks_half = half_length // BLOCK
    tile_blocks = tile_rows // BLOCK
    tiles_sequence = half_length // tile_rows
    key_blocks = jnp.arange(2 * blocks_half, dtype=jnp.int32) + (my_context - 1) * blocks_half
    key_allowed = (jnp.arange(2 * blocks_half) >= blocks_half) | (my_context > 0)
    frames = [
        block_bias(
            rel_bias,
            my_context * blocks_half
            + tile_index * tile_blocks
            + jnp.arange(tile_blocks, dtype=jnp.int32),
            key_blocks,
            key_allowed,
        )
        for tile_index in range(tiles_sequence)
    ]

    def attend_forward(seq_items):
        seq_queries, seq_keys, seq_values = seq_items
        outputs = []
        logsums = []
        for tile_index in range(tiles_sequence):
            bias_block, allowed, onehot = frames[tile_index]
            output, logsum = tile_forward(
                seq_queries[tile_index * tile_rows : (tile_index + 1) * tile_rows],
                seq_keys,
                seq_values,
                bias_block,
                allowed,
            )
            outputs.append(output)
            logsums.append(logsum)
        return (jnp.concatenate(outputs, 0), jnp.concatenate(logsums, 1))

    attention_output, logsum_all = lax.map(attend_forward, (queries, keys_all, values_all))
    attended_flat = attention_output.reshape(tokens_here, hidden_here)
    (attended_all,) = gather_line([attended_flat.T], 2)
    stream_one = stream_zero + lax.dot_general(
        attended_all.reshape(model_width, tokens_here),
        project_full,
        (((0,), (0,)), ((), ())),
        preferred_element_type=jnp.float32,
    )
    second_normalized = norm_forward(stream_one, norm_gains[1])
    normed_two_low = second_normalized.astype(jnp.bfloat16)
    router_low = router.astype(jnp.bfloat16)
    router_scores_raw = jnp.dot(normed_two_low, router_low, preferred_element_type=jnp.float32)
    route_pairs = routes.reshape(tokens_here, 2)
    route_onehot = (route_pairs[:, :, None] == jnp.arange(experts, dtype=jnp.int32)).astype(
        jnp.float32
    )
    chosen = jnp.einsum("tke,te->tk", route_onehot, router_scores_raw, precision=highest_precision)
    gate_values = jax.nn.softmax(chosen, -1)
    pair_kept, pair_dest = pair_slots(route_pairs, priority[0], experts, capacity)
    slots = lax.broadcasted_iota(jnp.int32, (experts * capacity, tokens_here), 0)
    hits = [
        (slots == pair_dest[k * tokens_here : (k + 1) * tokens_here][None, :])
        & pair_kept[k * tokens_here : (k + 1) * tokens_here][None, :]
        for k in range(2)
    ]
    hit_low = [hit.astype(jnp.bfloat16) for hit in hits]
    both_low = (hits[0] | hits[1]).astype(jnp.bfloat16)
    dispatch_rows = jnp.dot(
        both_low, normed_two_low, preferred_element_type=jnp.float32
    ).astype(jnp.bfloat16).reshape(owners, experts_here * capacity, model_width)
    arrived = to_experts(dispatch_rows).reshape(owners, experts_here, capacity, model_width)
    inner_low = expert_in.astype(jnp.bfloat16)
    outer_low = expert_out.astype(jnp.bfloat16)
    hidden_pre = jnp.einsum(
        "oecd,edf->oecf", arrived, inner_low, preferred_element_type=jnp.float32
    )
    active_low = gelu_tanh(hidden_pre).astype(jnp.bfloat16)
    expert_part = jnp.einsum(
        "oecf,efd->oecd", active_low, outer_low, preferred_element_type=jnp.float32
    ).astype(jnp.bfloat16)
    returned = from_experts(
        expert_part.reshape(owners, experts_here * capacity, model_width)
    ).reshape(experts * capacity, model_width)
    pair_rows = [
        lax.dot_general(
            hit_low[k], returned, (((0,), (0,)), ((), ())), preferred_element_type=jnp.float32
        )
        for k in range(2)
    ]
    moe_partial = gate_values[:, 0:1] * pair_rows[0] + gate_values[:, 1:2] * pair_rows[1]
    head_low, stream_two = sum_line(
        moe_partial, [stream_one, gain_rows[2]], [stream_shape], finish_mixture, 3
    )
    head_tiles = tokens_here // head_rows_count
    head_rows = head_low.reshape(head_tiles, head_rows_count, model_width)
    local_targets = (targets.reshape(tokens_here, 2) - my_rank * vocab_here).reshape(
        head_tiles, head_rows_count, 2
    )
    columns = jnp.arange(vocab_here, dtype=jnp.int32)

    def head_forward(tile_items):
        rows_low, wanted = tile_items
        logits = lax.dot_general(
            rows_low, table_low, (((1,), (1,)), ((), ())), preferred_element_type=jnp.float32
        )
        peak_value = jnp.max(logits, 1)
        exp_total = jnp.sum(jnp.exp(logits - peak_value[:, None]), 1)
        picked = jnp.stack(
            [
                jnp.sum(jnp.where(columns[None, :] == wanted[:, which : which + 1], logits, 0.0), 1)
                for which in range(2)
            ],
            1,
        )
        return (peak_value, exp_total, picked)

    peaks, totals, picked = lax.map(head_forward, (head_rows, local_targets))

    def merge_totals(left_part, right_part):
        top_value = jnp.maximum(left_part[0], right_part[0])
        summed = left_part[1] * jnp.exp(left_part[0] - top_value) + right_part[1] * jnp.exp(
            right_part[0] - top_value
        )
        return (top_value, summed, left_part[2] + right_part[2])

    top_value, exp_total, target_logits = combined_all(
        (peaks.reshape(-1), totals.reshape(-1), picked.reshape(tokens_here, 2)),
        "tensor",
        merge_totals,
    )
    logsum_vocab = top_value + jnp.log(exp_total)
    loss_weights = counted.reshape(tokens_here, 2).astype(jnp.float32) * jnp.array(
        [1.0, ahead_weight], jnp.float32
    )
    loss_local = jnp.sum(loss_weights * (logsum_vocab[:, None] - target_logits))
    loss_totals = lax.psum(jnp.stack([loss_local, jnp.sum(loss_weights)]), ("dp", "ctx"))
    inverse_weight = 1.0 / loss_totals[1]

    def head_backward(running, tile_items):
        rows_low, wanted, logsum_rows, weight_rows = tile_items
        logits = lax.dot_general(
            rows_low, table_low, (((1,), (1,)), ((), ())), preferred_element_type=jnp.float32
        )
        softmax_full = jnp.exp(logits - logsum_rows[:, None])
        target_hits = jnp.where(
            columns[None, :] == wanted[:, 0:1], weight_rows[:, 0:1], 0.0
        ) + jnp.where(columns[None, :] == wanted[:, 1:2], weight_rows[:, 1:2], 0.0)
        grad_logits = (
            (jnp.sum(weight_rows, 1, keepdims=True) * softmax_full - target_hits) * inverse_weight
        ).astype(jnp.bfloat16)
        grad_rows = jnp.dot(grad_logits, table_low, preferred_element_type=jnp.float32)
        running = running + lax.dot_general(
            grad_logits, rows_low, (((0,), (0,)), ((), ())), preferred_element_type=jnp.float32
        )
        return (running, grad_rows)

    table_grad, grad_head = lax.scan(
        head_backward,
        jnp.zeros((vocab_here, model_width), jnp.float32),
        (
            head_rows,
            local_targets,
            logsum_vocab.reshape(head_tiles, head_rows_count),
            loss_weights.reshape(head_tiles, head_rows_count, 2),
        ),
    )
    grad_two_low, grad_two, gain_grad_three = sum_line(
        grad_head.reshape(tokens_here, model_width),
        [stream_two, gain_rows[2]],
        [stream_shape, gain_shape],
        finish_head_grad,
        4,
        prologue=clear_gain,
    )
    slot_scale = jnp.sum(
        jnp.where(hits[0], gate_values[:, 0][None, :], 0.0)
        + jnp.where(hits[1], gate_values[:, 1][None, :], 0.0),
        1,
    )
    slot_grads = jnp.dot(both_low, grad_two_low, preferred_element_type=jnp.float32)
    grad_dispatch = (
        (slot_grads * slot_scale[:, None])
        .astype(jnp.bfloat16)
        .reshape(owners, experts_here * capacity, model_width)
    )
    slot_dots = jnp.sum(slot_grads * returned.astype(jnp.float32), 1)
    gate_part = jnp.stack([jnp.sum(jnp.where(hit, slot_dots[:, None], 0.0), 0) for hit in hits])
    grad_arrived = to_experts(grad_dispatch).reshape(owners, experts_here, capacity, model_width)
    grad_active = jnp.einsum(
        "oecd,efd->oecf", grad_arrived, outer_low, preferred_element_type=jnp.float32
    )
    outer_grad = jnp.einsum(
        "oecf,oecd->efd", active_low, grad_arrived, preferred_element_type=jnp.float32
    )
    gelu_values, gelu_back = jax.vjp(gelu_tanh, hidden_pre)
    grad_hidden = gelu_back(grad_active)[0].astype(jnp.bfloat16)
    inner_grad = jnp.einsum(
        "oecd,oecf->edf", arrived, grad_hidden, preferred_element_type=jnp.float32
    )
    grad_back = jnp.einsum(
        "oecf,edf->oecd", grad_hidden, inner_low, preferred_element_type=jnp.float32
    ).astype(jnp.bfloat16)
    grad_returned = from_experts(
        grad_back.reshape(owners, experts_here * capacity, model_width)
    ).reshape(experts * capacity, model_width)
    moe_grad_part = lax.dot_general(
        both_low, grad_returned, (((0,), (0,)), ((), ())), preferred_element_type=jnp.float32
    )
    gate_block = pltpu.VMEM((3, 2, tokens_here), jnp.float32)
    grad_one_low, grad_one, logit_grad, gain_grad_two = sum_line(
        moe_grad_part,
        [
            stream_one,
            gain_rows[1],
            grad_two,
            gate_part,
            gate_values.T,
            route_pairs.T,
            router_low,
        ],
        [
            stream_shape,
            jax.ShapeDtypeStruct((experts, tokens_here), jnp.bfloat16),
            gain_shape,
        ],
        finish_expert_grad,
        5,
        prologue=start_router_grad,
        scratch=(gate_block, pltpu.SemaphoreType.DMA((3,)), pltpu.SemaphoreType.DMA((3,))),
        meets_all=True,
    )
    router_grad = lax.dot_general(
        normed_two_low, logit_grad, (((0,), (1,)), ((), ())), preferred_element_type=jnp.float32
    )
    project_grad = lax.dot_general(
        attended_flat, grad_one_low, (((0,), (0,)), ((), ())), preferred_element_type=jnp.float32
    )
    grad_attended = lax.dot_general(
        grad_one_low, project_low, (((1,), (1,)), ((), ())), preferred_element_type=jnp.float32
    ).astype(jnp.bfloat16)

    def attend_backward(seq_items):
        seq_queries, seq_keys, seq_values, seq_grad, seq_logsum = seq_items
        query_grads = []
        key_grad = jnp.zeros(seq_keys.shape, jnp.float32)
        value_grad = jnp.zeros(seq_values.shape, jnp.float32)
        bias_grad = jnp.zeros(rel_bias.shape, jnp.float32)
        for tile_index in range(tiles_sequence):
            bias_block, allowed, onehot = frames[tile_index]
            row_range = slice(tile_index * tile_rows, (tile_index + 1) * tile_rows)
            tile_logsum = seq_logsum[:, tile_index * tile_blocks : (tile_index + 1) * tile_blocks]
            grad_query, grad_keys, grad_values, grad_bias = tile_backward(
                seq_queries[row_range],
                seq_keys,
                seq_values,
                seq_grad[row_range],
                tile_logsum,
                bias_block,
                allowed,
                onehot,
            )
            query_grads.append(grad_query)
            key_grad = key_grad + grad_keys
            value_grad = value_grad + grad_values
            bias_grad = bias_grad + grad_bias
        return (jnp.concatenate(query_grads, 0), key_grad, value_grad, bias_grad)

    query_grad, key_grad, value_grad, bias_grads = lax.map(
        attend_backward,
        (
            queries,
            keys_all,
            values_all,
            grad_attended.reshape(sequences, half_length, heads_here, head_size),
            logsum_all,
        ),
    )
    bias_grad = jnp.sum(bias_grads, 0)
    pair_grad = jnp.stack([key_grad, value_grad], 2).reshape(
        sequences, 2 * half_length, 2 * hidden_here
    )
    grad_before = passed_along(pair_grad[:, :half_length].astype(jnp.bfloat16), "ctx", -1)
    pair_grad_here = pair_grad[:, half_length:] + grad_before.astype(jnp.float32)
    joint_grad = jnp.concatenate(
        [
            query_grad.reshape(tokens_here, hidden_here),
            pair_grad_here.reshape(tokens_here, 2 * hidden_here),
        ],
        1,
    ).astype(jnp.bfloat16)
    joint_weight_grad = lax.dot_general(
        joint_grad, normed_one_low, (((0,), (0,)), ((), ())), preferred_element_type=jnp.float32
    )
    zero_grad_low, gain_grad_one = sum_line(
        jnp.dot(joint_grad, joint_low, preferred_element_type=jnp.float32),
        [embedded, gain_rows[0], grad_one],
        [gain_shape],
        functools.partial(finish_input_grad, embed_scale),
        6,
        prologue=clear_gain,
    )
    onehot_ids = (
        (lax.broadcasted_iota(jnp.int32, (vocab_here, tokens_here), 0) == local_ids[None, :])
    ).astype(jnp.bfloat16)
    table_grad = table_grad + jnp.dot(
        onehot_ids, zero_grad_low, preferred_element_type=jnp.float32
    )
    unit_grads = jnp.concatenate(
        [
            table_grad,
            joint_weight_grad,
            project_grad,
        ],
        0,
    ).reshape(-1, unit_rows, model_width)
    my_units = jnp.take(slot_unit, my_owner, axis=0)
    my_filled = jnp.take(slot_filled, my_owner, axis=0)[:, None, None]
    outgoing = pull_units(unit_grads, slot_unit.reshape(-1))
    summed = lax.psum_scatter(outgoing, ("dp", "ctx"), scatter_dimension=0, tiled=True)
    mine = jnp.where(my_filled, summed, 0.0)
    gains_grad = lax.psum(
        jnp.concatenate([gain_grad_one, gain_grad_two, gain_grad_three], 0),
        ("dp", "ctx", "tensor"),
    )
    router_grad, bias_grad = lax.psum((router_grad, bias_grad), ("dp", "ctx"))
    slot_rates = unit_rates(my_units, table_units, query_units, value_units)[:, None, None]
    master_new, master_first_new, master_second_new = adam_update(
        master[0, 0], master_first[0, 0], master_second[0, 0], mine, slot_rates, decay_rate
    )
    inner_new, inner_first_new, inner_second_new = adam_update(
        expert_in, expert_in_first, expert_in_second, inner_grad, rate_inner, decay_rate
    )
    outer_new, outer_first_new, outer_second_new = adam_update(
        expert_out, expert_out_first, expert_out_second, outer_grad, rate_outer, decay_rate
    )
    gains_new, gains_first_new, gains_second_new = adam_update(
        norm_gains, norm_gains_first, norm_gains_second, gains_grad, rate_gains, 0.0
    )
    router_new, router_first_new, router_second_new = adam_update(
        router, router_first, router_second, router_grad, rate_router, decay_rate
    )
    biases_new, biases_first_new, biases_second_new = adam_update(
        rel_bias, rel_bias_first, rel_bias_second, bias_grad, rate_biases, 0.0
    )
    return (
        loss_totals,
        master_new[None, None],
        master_first_new[None, None],
        master_second_new[None, None],
        inner_new,
        inner_first_new,
        inner_second_new,
        outer_new,
        outer_first_new,
        outer_second_new,
        gains_new,
        gains_first_new,
        gains_second_new,
        router_new,
        router_first_new,
        router_second_new,
        biases_new,
        biases_first_new,
        biases_second_new,
    )


def solution(mesh):
    in_specs = (
        P("dp", "ctx"),
        P("dp", "ctx", None),
        P("dp", "ctx", None),
        P("dp", "ctx", None),
        P(("dp", "ctx"), None),
        P(),
        P("tensor", ("dp", "ctx"), None, None, None),
        P("tensor", ("dp", "ctx"), None, None, None),
        P("tensor", ("dp", "ctx"), None, None, None),
        P(("dp", "ctx"), None, "tensor"),
        P(("dp", "ctx"), None, "tensor"),
        P(("dp", "ctx"), None, "tensor"),
        P(("dp", "ctx"), "tensor", None),
        P(("dp", "ctx"), "tensor", None),
        P(("dp", "ctx"), "tensor", None),
        P(),
        P(),
        P(),
        P(),
        P(),
        P(),
        P("tensor", None),
        P("tensor", None),
        P("tensor", None),
    )
    out_specs = (
        P(),
        P("tensor", ("dp", "ctx"), None, None, None),
        P("tensor", ("dp", "ctx"), None, None, None),
        P("tensor", ("dp", "ctx"), None, None, None),
        P(("dp", "ctx"), None, "tensor"),
        P(("dp", "ctx"), None, "tensor"),
        P(("dp", "ctx"), None, "tensor"),
        P(("dp", "ctx"), "tensor", None),
        P(("dp", "ctx"), "tensor", None),
        P(("dp", "ctx"), "tensor", None),
        P(),
        P(),
        P(),
        P(),
        P(),
        P(),
        P("tensor", None),
        P("tensor", None),
        P("tensor", None),
    )
    return jax.shard_map(
        on_device, mesh=mesh, in_specs=in_specs, out_specs=out_specs, check_vma=False
    )
```

```python
import functools
import math

import jax
import jax.numpy as jnp
from jax import lax
from jax.experimental import pallas as pl
from jax.experimental.pallas import tpu as pltpu
from jax.sharding import PartitionSpec as P

VOCAB = 32000
BLOCK = 256
STEP = 10


highest_precision = lax.Precision.HIGHEST
beta_first = 0.9
beta_second = 0.95
adam_epsilon = 1e-08
norm_epsilon = 1e-06
ahead_weight = 0.3
masked_score = -1e30
rate_table = 0.1
rate_query = 0.05
rate_values = 0.05
rate_project = 0.5
rate_inner = 0.05
rate_outer = 0.03
rate_gains = 0.5
rate_router = 0.05
rate_biases = 0.5
decay_rate = 0.1


def passed_along(value, axis, steps):
    count = lax.axis_size(axis)
    initial, last = (max(0, -steps), min(count, count - steps))
    return lax.ppermute(value, axis, [(source, source + steps) for source in range(initial, last)])

MESH_ID = pl.DeviceIdType.MESH
whole_vmem = pl.BlockSpec(memory_space=pltpu.VMEM)
whole_any = pl.BlockSpec(memory_space=pl.ANY)
line_rows = 128
line_lag = 3


def sum_line_kernel(
    count, meets_all, prologue, epilogue, n_extra, n_aux, n_scratch, part_ref, *refs
):
    extras = refs[:n_extra]
    out_ref = refs[n_extra]
    aux = refs[n_extra + 1 : n_extra + 1 + n_aux]
    rest = refs[n_extra + 1 + n_aux :]
    scratch = rest[:n_scratch]
    stage, from_end, from_mid, send_sem, end_sem, mid_sem, back_sem, back_recv = rest[n_scratch:]
    rank = lax.axis_index("tensor")
    inner = (rank == 1) | (rank == 2)
    end_peer = jnp.where(rank < 2, 1 - rank, 5 - rank)
    mid_peer = 3 - rank
    barrier = pltpu.get_barrier_semaphore()
    if not meets_all:
        pl.semaphore_signal(barrier, inc=1, device_id={"tensor": end_peer}, device_id_type=MESH_ID)

        @pl.when(inner)
        def _():
            pl.semaphore_signal(
                barrier, inc=1, device_id={"tensor": mid_peer}, device_id_type=MESH_ID
            )
            pl.semaphore_wait(barrier, 2)

        @pl.when(jnp.logical_not(inner))
        def _():
            pl.semaphore_wait(barrier, 1)
    else:
        for step in (1, 2, 3):
            other = lax.rem(rank + step, 4)
            pl.semaphore_signal(barrier, inc=1, device_id={"tensor": other}, device_id_type=MESH_ID)
        pl.semaphore_wait(barrier, 3)

    rows = line_rows

    def span(i):
        return pl.ds(pl.multiple_of(i * rows, rows), rows)

    def to_inner(i):
        return pltpu.make_async_remote_copy(
            src_ref=stage.at[i],
            dst_ref=from_end.at[i],
            send_sem=send_sem.at[i],
            recv_sem=end_sem.at[i],
            device_id={"tensor": end_peer},
            device_id_type=MESH_ID,
        )

    def to_middle(i):
        return pltpu.make_async_remote_copy(
            src_ref=stage.at[i],
            dst_ref=from_mid.at[i],
            send_sem=send_sem.at[i],
            recv_sem=mid_sem.at[i],
            device_id={"tensor": mid_peer},
            device_id_type=MESH_ID,
        )

    def to_end(i):
        return pltpu.make_async_remote_copy(
            src_ref=out_ref.at[span(i)],
            dst_ref=out_ref.at[span(i)],
            send_sem=back_sem.at[i],
            recv_sem=back_recv.at[i],
            device_id={"tensor": end_peer},
            device_id_type=MESH_ID,
        )

    @pl.when(jnp.logical_not(inner))
    def _():
        def push(i, carry):
            stage[i] = part_ref[span(i)].astype(jnp.bfloat16)
            to_inner(i).start()
            return carry

        lax.fori_loop(0, count, push, 0)

    if prologue is not None:
        prologue(rank, extras, aux, scratch)

    @pl.when(inner)
    def _():
        def step(i, carry):
            @pl.when(i < count)
            def _():
                to_inner(i).wait_recv()
                mine = part_ref[span(i)].astype(jnp.float32) + from_end[i].astype(jnp.float32)
                stage[i] = mine.astype(jnp.bfloat16)
                to_middle(i).start()

            @pl.when(i >= line_lag)
            def _():
                j = i - line_lag
                to_middle(j).wait_recv()
                total = stage[j].astype(jnp.float32) + from_mid[j].astype(jnp.float32)
                out_ref[span(j)] = epilogue(total, span(j), rank, extras, aux, scratch)
                to_end(j).start()

            return carry

        lax.fori_loop(0, count + line_lag, step, 0)

        def drain(i, carry):
            to_middle(i).wait_send()
            to_end(i).wait_send()
            return carry

        lax.fori_loop(0, count, drain, 0)

    @pl.when(jnp.logical_not(inner))
    def _():
        def finish(i, carry):
            to_end(i).wait_recv()
            to_inner(i).wait_send()
            return carry

        lax.fori_loop(0, count, finish, 0)


def sum_line(
    part, extras, aux_shapes, epilogue, collective_id, prologue=None, scratch=(), meets_all=False
):
    tokens, width = part.shape
    count = tokens // line_rows
    chunks = pltpu.VMEM((count, line_rows, width), jnp.bfloat16)
    return pl.pallas_call(
        functools.partial(
            sum_line_kernel,
            count,
            meets_all,
            prologue,
            epilogue,
            len(extras),
            len(aux_shapes),
            len(scratch),
        ),
        out_shape=[jax.ShapeDtypeStruct((tokens, width), jnp.bfloat16)] + list(aux_shapes),
        in_specs=[whole_vmem] * (1 + len(extras)),
        out_specs=[whole_vmem] * (1 + len(aux_shapes)),
        scratch_shapes=list(scratch)
        + [chunks, chunks, chunks]
        + [pltpu.SemaphoreType.DMA((count,))] * 5,
        compiler_params=pltpu.CompilerParams(
            collective_id=collective_id, has_side_effects=True, vmem_limit_bytes=48 << 20
        ),
    )(part, *extras)


def keep_total(total, span, rank, extras, aux, scratch):
    return total.astype(jnp.bfloat16)


def inverse_rms(values):
    return lax.rsqrt(jnp.mean(values * values, -1, keepdims=True) + norm_epsilon)


def finish_mixture(total, span, rank, extras, aux, scratch):
    stream_one, gain = extras
    stream_two = stream_one[span] + total
    aux[0][span] = stream_two
    return (stream_two * inverse_rms(stream_two) * gain[...]).astype(jnp.bfloat16)


def norm_back_rows(values, gain, upstream):
    inverse = inverse_rms(values)
    normed = values * inverse
    scaled = upstream * gain
    gain_grad = jnp.sum(upstream * normed, 0, keepdims=True)
    inputs_grad = inverse * (scaled - normed * jnp.mean(scaled * normed, -1, keepdims=True))
    return (inputs_grad, gain_grad)


def clear_gain(rank, extras, aux, scratch):
    aux[-1][...] = jnp.zeros_like(aux[-1])


def add_gain(rank, ref, gain_grad):
    ref[...] += jnp.where(rank == 1, gain_grad, 0.0)


def finish_head_grad(total, span, rank, extras, aux, scratch):
    stream_two, gain = extras
    grad_two, gain_grad = norm_back_rows(stream_two[span], gain[...], total)
    aux[0][span] = grad_two
    add_gain(rank, aux[1], gain_grad)
    return grad_two.astype(jnp.bfloat16)


def start_router_grad(rank, extras, aux, scratch):
    stream_one, gain, grad_two, gate_part, gates, routes, router_low = extras
    grad_one, logit_grad, gain_grad = aux
    landed, gate_send, gate_recv = scratch
    gain_grad[...] = jnp.zeros_like(gain_grad)
    copies = []
    for step in (1, 2, 3):
        copy = pltpu.make_async_remote_copy(
            src_ref=gate_part,
            dst_ref=landed.at[step - 1],
            send_sem=gate_send.at[step - 1],
            recv_sem=gate_recv.at[step - 1],
            device_id={"tensor": lax.rem(rank + step, 4)},
            device_id_type=MESH_ID,
        )
        copy.start()
        copies.append(copy)
    for copy in copies:
        copy.wait()
    gate_grad = jnp.zeros(gate_part.shape, jnp.float32)
    for source in range(4):
        piece = jnp.zeros(gate_part.shape, jnp.float32)
        for step in (1, 2, 3):
            piece = jnp.where(lax.rem(source + step, 4) == rank, landed[step - 1], piece)
        gate_grad = gate_grad + jnp.where(rank == source, gate_part[...], piece)
    weighted = gates[...] * gate_grad
    chosen = gates[...] * (gate_grad - (weighted[0:1] + weighted[1:2]))
    experts, tokens = logit_grad.shape
    row = lax.broadcasted_iota(jnp.int32, (experts, tokens), 0)
    placed = jnp.where(row == routes[0:1], chosen[0:1], 0.0) + jnp.where(
        row == routes[1:2], chosen[1:2], 0.0
    )
    logit_grad[...] = placed.astype(jnp.bfloat16)


def finish_expert_grad(total, span, rank, extras, aux, scratch):
    stream_one, gain, grad_two, gate_part, gates, routes, router_low = extras
    grad_one, logit_grad, gain_grad = aux
    upstream = total + lax.dot_general(
        logit_grad[:, span],
        router_low[...],
        (((0,), (1,)), ((), ())),
        preferred_element_type=jnp.float32,
    )
    part, gain_part = norm_back_rows(stream_one[span], gain[...], upstream)
    result = grad_two[span] + part
    grad_one[span] = result
    add_gain(rank, gain_grad, gain_part)
    return result.astype(jnp.bfloat16)


def finish_input_grad(scale, total, span, rank, extras, aux, scratch):
    embedded, gain, grad_one = extras
    stream_zero = embedded[span].astype(jnp.float32) * scale
    part, gain_part = norm_back_rows(stream_zero, gain[...], total)
    add_gain(rank, aux[0], gain_part)
    return ((grad_one[span] + part) * scale).astype(jnp.bfloat16)


def gather_line_kernel(count, *refs):
    ins = refs[:count]
    outs = refs[count : 2 * count]
    local_sem, send_sem, recv_sem = refs[2 * count :]
    rank = lax.axis_index("tensor")
    barrier = pltpu.get_barrier_semaphore()
    for step in (1, 2, 3):
        other = lax.rem(rank + step, 4)
        pl.semaphore_signal(barrier, inc=1, device_id={"tensor": other}, device_id_type=MESH_ID)
    pl.semaphore_wait(barrier, 3)
    copies = []
    for k in range(count):
        for step in (1, 2, 3):
            copy = pltpu.make_async_remote_copy(
                src_ref=ins[k],
                dst_ref=outs[k].at[rank],
                send_sem=send_sem.at[k, step - 1],
                recv_sem=recv_sem.at[k, step - 1],
                device_id={"tensor": lax.rem(rank + step, 4)},
                device_id_type=MESH_ID,
            )
            copy.start()
            copies.append(copy)
        own = pltpu.make_async_copy(ins[k], outs[k].at[rank], local_sem.at[k])
        own.start()
        own.wait()
    for copy in copies:
        copy.wait()


def gather_line(arrays, collective_id):
    count = len(arrays)
    return pl.pallas_call(
        functools.partial(gather_line_kernel, count),
        out_shape=[jax.ShapeDtypeStruct((4,) + x.shape, x.dtype) for x in arrays],
        in_specs=[whole_vmem] * count,
        out_specs=[whole_vmem] * count,
        scratch_shapes=[
            pltpu.SemaphoreType.DMA((count,)),
            pltpu.SemaphoreType.DMA((count, 3)),
            pltpu.SemaphoreType.DMA((count, 3)),
        ],
        compiler_params=pltpu.CompilerParams(
            collective_id=collective_id, has_side_effects=True, vmem_limit_bytes=40 << 20
        ),
    )(*arrays)


def pull_units_kernel(group, slots_ref, source_ref, out_ref, sem):
    start = pl.program_id(0) * group

    def push(u, carry):
        pltpu.make_async_copy(source_ref.at[slots_ref[start + u]], out_ref.at[u], sem).start()
        return carry

    lax.fori_loop(0, group, push, 0)
    pltpu.make_async_copy(out_ref, out_ref, sem).wait()


def pull_units(source, slots):
    count = slots.shape[0]
    unit_bytes = math.prod(source.shape[1:]) * source.dtype.itemsize
    group = max(k for k in range(1, count + 1) if count % k == 0 and (k <= 32 or k * unit_bytes < 15 << 20))
    return pl.pallas_call(
        functools.partial(pull_units_kernel, group),
        grid=(count // group,),
        out_shape=jax.ShapeDtypeStruct((count,) + source.shape[1:], source.dtype),
        in_specs=[pl.BlockSpec(memory_space=pltpu.SMEM), whole_any],
        out_specs=pl.BlockSpec((group,) + source.shape[1:], lambda k: (k,) + (0,) * (source.ndim - 1)),
        scratch_shapes=[pltpu.SemaphoreType.DMA],
        compiler_params=pltpu.CompilerParams(vmem_limit_bytes=40 << 20),
    )(slots, source)


def attention_kernel(heads, size, bias_ref, own_ref, before_ref, out_ref, logsum_ref, scores, peak, total):
    tokens = own_ref.shape[1]
    blocks = tokens // BLOCK
    hidden = heads * size
    later = lax.axis_index("ctx") > 0

    for head in range(heads):
        query = own_ref[head * size : (head + 1) * size, :].astype(jnp.float32).T * size**-0.5
        query = query.astype(jnp.bfloat16)
        own_keys = own_ref[hidden + head * size : hidden + (head + 1) * size, :]
        old_keys = before_ref[head * size : (head + 1) * size, :]
        own_values = own_ref[2 * hidden + head * size : 2 * hidden + (head + 1) * size, :]
        own_values = own_values.astype(jnp.float32).T.astype(jnp.bfloat16)
        old_values = before_ref[hidden + head * size : hidden + (head + 1) * size, :]
        old_values = old_values.astype(jnp.float32).T.astype(jnp.bfloat16)
        for block in range(blocks):
            rows = query[block * BLOCK : (block + 1) * BLOCK]
            width = (block + 1) * BLOCK
            mine = jnp.dot(rows, own_keys[:, :width], preferred_element_type=jnp.float32)
            top = None
            parts = []
            for k in range(block + 1):
                part = mine[:, k * BLOCK : (k + 1) * BLOCK] + bias_ref[head, block - k]
                parts.append(part)
                high = jnp.max(part, 1, keepdims=True)
                top = high if top is None else jnp.maximum(top, high)
            peak[...] = top

            @pl.when(later)
            def _():
                old = jnp.dot(rows, old_keys, preferred_element_type=jnp.float32)
                top_old = None
                for k in range(blocks):
                    part = old[:, k * BLOCK : (k + 1) * BLOCK] + bias_ref[head, block + blocks - k]
                    scores[:, k * BLOCK : (k + 1) * BLOCK] = part
                    high = jnp.max(part, 1, keepdims=True)
                    top_old = high if top_old is None else jnp.maximum(top_old, high)
                peak[...] = jnp.maximum(peak[...], top_old)

            top = peak[...]
            parts = [jnp.exp(part - top) for part in parts]
            own_sum = None
            for part in parts:
                part_sum = jnp.sum(part, 1, keepdims=True)
                own_sum = part_sum if own_sum is None else own_sum + part_sum
            total[...] = own_sum

            @pl.when(later)
            def _():
                old_exp = jnp.exp(scores[...] - top)
                scores[...] = old_exp
                total[...] += jnp.sum(old_exp, 1, keepdims=True)

            full = total[...]
            inverse = 1.0 / full
            low = jnp.concatenate([(part * inverse).astype(jnp.bfloat16) for part in parts], 1)
            result = jnp.dot(low, own_values[:width], preferred_element_type=jnp.float32)
            peak[...] = top + jnp.log(full)
            logsum_ref[head, block * BLOCK : (block + 1) * BLOCK, :] = peak[...]
            place = (slice(head * size, (head + 1) * size), slice(block * BLOCK, (block + 1) * BLOCK))

            @pl.when(later)
            def _():
                low_old = (scores[...] * inverse).astype(jnp.bfloat16)
                both = result + jnp.dot(low_old, old_values, preferred_element_type=jnp.float32)
                out_ref[place] = both.T.astype(jnp.bfloat16)

            @pl.when(jnp.logical_not(later))
            def _():
                out_ref[place] = result.T.astype(jnp.bfloat16)


def attention(biases, own, before, heads, size):
    tokens = own.shape[1]
    return pl.pallas_call(
        functools.partial(attention_kernel, heads, size),
        out_shape=[
            jax.ShapeDtypeStruct((heads * size, tokens), jnp.bfloat16),
            jax.ShapeDtypeStruct((heads, tokens, 1), jnp.float32),
        ],
        in_specs=[pl.BlockSpec(memory_space=pltpu.SMEM), whole_vmem, whole_vmem],
        out_specs=[whole_vmem, whole_vmem],
        scratch_shapes=[
            pltpu.VMEM((BLOCK, tokens), jnp.float32),
            pltpu.VMEM((BLOCK, 1), jnp.float32),
            pltpu.VMEM((BLOCK, 1), jnp.float32),
        ],
        compiler_params=pltpu.CompilerParams(vmem_limit_bytes=40 << 20),
    )(biases, own, before)


def attention_back_kernel(
    heads, size, bias_ref, own_ref, before_ref, logsum_ref, grad_ref, project_ref,
    query_out, own_out, before_out, bias_out, probs, slopes, inner, query_sum, own_sum, before_sum,
):
    tokens = own_ref.shape[1]
    blocks = tokens // BLOCK
    hidden = heads * size
    later = lax.axis_index("ctx") > 0
    bias_out[...] = jnp.zeros_like(bias_out)

    def flipped(rows):
        return rows.astype(jnp.float32).T.astype(jnp.bfloat16)

    for head in range(heads):
        span = slice(head * size, (head + 1) * size)
        value_span = slice(hidden + head * size, hidden + (head + 1) * size)
        query_rows = own_ref[span, :]
        query = flipped(query_rows) * jnp.bfloat16(size**-0.5)
        own_keys = own_ref[hidden + head * size : hidden + (head + 1) * size, :]
        own_values = own_ref[2 * hidden + head * size : 2 * hidden + (head + 1) * size, :]
        old_keys = before_ref[span, :]
        old_values = before_ref[value_span, :]
        own_keys_flip = flipped(own_keys)
        grad = lax.dot_general(
            grad_ref[...], project_ref[span, :], (((1,), (1,)), ((), ())), preferred_element_type=jnp.float32
        )
        grad_rows = grad.T.astype(jnp.bfloat16)
        grad = grad.astype(jnp.bfloat16)
        own_sum[...] = jnp.zeros_like(own_sum)

        @pl.when(later)
        def _():
            before_sum[...] = jnp.zeros_like(before_sum)

        for block in range(blocks):
            at = slice(block * BLOCK, (block + 1) * BLOCK)
            width = (block + 1) * BLOCK
            rows, up = query[at], grad[at]
            lse = logsum_ref[head, at, :]
            score = jnp.dot(rows, own_keys[:, :width], preferred_element_type=jnp.float32)
            prob = jnp.concatenate(
                [
                    jnp.exp(score[:, k * BLOCK : (k + 1) * BLOCK] + (bias_ref[head, block - k] - lse))
                    for k in range(block + 1)
                ],
                1,
            )
            slope = jnp.dot(up, own_values[:, :width], preferred_element_type=jnp.float32)
            inner[...] = jnp.sum(prob * slope, 1, keepdims=True)

            @pl.when(later)
            def _():
                score = jnp.dot(rows, old_keys, preferred_element_type=jnp.float32)
                old_slope = jnp.dot(up, old_values, preferred_element_type=jnp.float32)
                old_prob = jnp.concatenate(
                    [
                        jnp.exp(
                            score[:, k * BLOCK : (k + 1) * BLOCK]
                            + (bias_ref[head, block + blocks - k] - lse)
                        )
                        for k in range(blocks)
                    ],
                    1,
                )
                probs[...] = old_prob
                slopes[...] = old_slope
                inner[...] += jnp.sum(old_prob * old_slope, 1, keepdims=True)

            row_inner = inner[...]
            low_grad = (prob * (slope - row_inner)).astype(jnp.bfloat16)
            query_sum[...] = jnp.dot(
                low_grad, own_keys_flip[:width], preferred_element_type=jnp.float32
            )
            own_sum[:size, :width] += jnp.dot(
                query_rows[:, at], low_grad, preferred_element_type=jnp.float32
            )
            own_sum[size:, :width] += jnp.dot(
                grad_rows[:, at], prob.astype(jnp.bfloat16), preferred_element_type=jnp.float32
            )
            for k in range(block + 1):
                line = head * 2 * blocks + block - k
                bias_out[line : line + 1, :] += jnp.sum(
                    low_grad[:, k * BLOCK : (k + 1) * BLOCK].astype(jnp.float32), 0, keepdims=True
                )

            @pl.when(later)
            def _():
                old_prob = probs[...]
                low_old = (old_prob * (slopes[...] - row_inner)).astype(jnp.bfloat16)
                query_sum[...] += jnp.dot(
                    low_old, flipped(old_keys), preferred_element_type=jnp.float32
                )
                before_sum[:size, :] += jnp.dot(
                    query_rows[:, at], low_old, preferred_element_type=jnp.float32
                )
                before_sum[size:, :] += jnp.dot(
                    grad_rows[:, at], old_prob.astype(jnp.bfloat16), preferred_element_type=jnp.float32
                )
                for k in range(blocks):
                    line = head * 2 * blocks + block + blocks - k
                    bias_out[line : line + 1, :] += jnp.sum(
                        low_old[:, k * BLOCK : (k + 1) * BLOCK].astype(jnp.float32), 0, keepdims=True
                    )

            query_out[span, at] = (query_sum[...].T * size**-0.5).astype(jnp.bfloat16)

        own_out[span, :] = own_sum[:size, :] * size**-0.5
        own_out[value_span, :] = own_sum[size:, :]

        @pl.when(later)
        def _():
            before_out[span, :] = (before_sum[:size, :] * size**-0.5).astype(jnp.bfloat16)
            before_out[value_span, :] = before_sum[size:, :].astype(jnp.bfloat16)

    @pl.when(jnp.logical_not(later))
    def _():
        before_out[...] = jnp.zeros_like(before_out)


def attention_back(biases, own, before, logsum, grad, project, heads, size):
    tokens = own.shape[1]
    hidden = heads * size
    return pl.pallas_call(
        functools.partial(attention_back_kernel, heads, size),
        out_shape=[
            jax.ShapeDtypeStruct((hidden, tokens), jnp.bfloat16),
            jax.ShapeDtypeStruct((2 * hidden, tokens), jnp.float32),
            jax.ShapeDtypeStruct((2 * hidden, tokens), jnp.bfloat16),
            jax.ShapeDtypeStruct((heads * 2 * (tokens // BLOCK), BLOCK), jnp.float32),
        ],
        in_specs=[pl.BlockSpec(memory_space=pltpu.SMEM)] + [whole_vmem] * 5,
        out_specs=[whole_vmem] * 4,
        scratch_shapes=[
            pltpu.VMEM((BLOCK, tokens), jnp.float32),
            pltpu.VMEM((BLOCK, tokens), jnp.float32),
            pltpu.VMEM((BLOCK, 1), jnp.float32),
            pltpu.VMEM((BLOCK, size), jnp.float32),
            pltpu.VMEM((2 * size, tokens), jnp.float32),
            pltpu.VMEM((2 * size, tokens), jnp.float32),
        ],
        compiler_params=pltpu.CompilerParams(vmem_limit_bytes=48 << 20),
    )(biases, own, before, logsum, grad, project)


def head_sums_kernel(table_ref, rows_ref, stats_ref, turned):
    @pl.when(pl.program_id(0) == 0)
    def _():
        turned[...] = rows_ref[...].astype(jnp.float32).T.astype(jnp.bfloat16)
        stats_ref[0:1, :] = jnp.full_like(stats_ref[0:1, :], masked_score)
        stats_ref[1:2, :] = jnp.zeros_like(stats_ref[1:2, :])

    logits = jnp.dot(table_ref[...], turned[...], preferred_element_type=jnp.float32)
    before = stats_ref[0:1, :]
    top = jnp.maximum(before, jnp.max(logits, 0, keepdims=True))
    stats_ref[1:2, :] = stats_ref[1:2, :] * jnp.exp(before - top) + jnp.sum(
        jnp.exp(logits - top), 0, keepdims=True
    )
    stats_ref[0:1, :] = top


def vocab_tile(vocab):
    return max(k for k in range(16, 1601, 16) if vocab % k == 0)


def head_sums(weights, rows, vocab):
    tokens, width = rows.shape
    tile = vocab_tile(vocab)
    return pl.pallas_call(
        head_sums_kernel,
        grid=(vocab // tile,),
        out_shape=jax.ShapeDtypeStruct((2, tokens), jnp.float32),
        in_specs=[pl.BlockSpec((tile, width), lambda k: (k, 0)), pl.BlockSpec((tokens, width), lambda k: (0, 0))],
        out_specs=pl.BlockSpec((2, tokens), lambda k: (0, 0)),
        scratch_shapes=[pltpu.VMEM((width, tokens), jnp.bfloat16)],
        compiler_params=pltpu.CompilerParams(vmem_limit_bytes=56 << 20),
    )(weights, rows)


def join_sums_kernel(stats_ref, logsum_ref, landed, send_sem, recv_sem):
    rank = lax.axis_index("tensor")
    barrier = pltpu.get_barrier_semaphore()
    for step in (1, 2, 3):
        other = lax.rem(rank + step, 4)
        pl.semaphore_signal(barrier, inc=1, device_id={"tensor": other}, device_id_type=MESH_ID)
    pl.semaphore_wait(barrier, 3)
    copies = []
    for step in (1, 2, 3):
        copy = pltpu.make_async_remote_copy(
            src_ref=stats_ref,
            dst_ref=landed.at[step - 1],
            send_sem=send_sem.at[step - 1],
            recv_sem=recv_sem.at[step - 1],
            device_id={"tensor": lax.rem(rank + step, 4)},
            device_id_type=MESH_ID,
        )
        copy.start()
        copies.append(copy)
    for copy in copies:
        copy.wait()
    tops, sums = [], []
    for source in range(4):
        piece = stats_ref[...]
        for step in (1, 2, 3):
            piece = jnp.where(lax.rem(source + step, 4) == rank, landed[step - 1], piece)
        tops.append(piece[0:1])
        sums.append(piece[1:2])
    top = jnp.maximum(jnp.maximum(tops[0], tops[1]), jnp.maximum(tops[2], tops[3]))
    total = sums[0] * jnp.exp(tops[0] - top)
    for source in (1, 2, 3):
        total = total + sums[source] * jnp.exp(tops[source] - top)
    logsum_ref[...] = top + jnp.log(total)


def join_sums(stats, collective_id):
    tokens = stats.shape[1]
    return pl.pallas_call(
        join_sums_kernel,
        out_shape=jax.ShapeDtypeStruct((1, tokens), jnp.float32),
        in_specs=[whole_vmem],
        out_specs=whole_vmem,
        scratch_shapes=[
            pltpu.VMEM((3, 2, tokens), jnp.float32),
            pltpu.SemaphoreType.DMA((3,)),
            pltpu.SemaphoreType.DMA((3,)),
        ],
        compiler_params=pltpu.CompilerParams(collective_id=collective_id, has_side_effects=True),
    )(stats)


def head_back_kernel(
    tile, table_ref, rows_ref, logsum_ref, wanted_ref, weight_ref, slope_ref, grad_ref, picked_ref, turned
):
    step = pl.program_id(0)

    @pl.when(step == 0)
    def _():
        turned[...] = rows_ref[...].astype(jnp.float32).T.astype(jnp.bfloat16)
        picked_ref[...] = jnp.zeros_like(picked_ref)
        grad_ref[...] = jnp.zeros_like(grad_ref)

    logits = jnp.dot(table_ref[...], turned[...], preferred_element_type=jnp.float32)
    row = lax.broadcasted_iota(jnp.int32, logits.shape, 0)
    base = step * tile
    hits = jnp.where(row == wanted_ref[0:1, :] - base, weight_ref[0:1, :], 0.0) + jnp.where(
        row == wanted_ref[1:2, :] - base, weight_ref[1:2, :], 0.0
    )
    picked_ref[...] += jnp.sum(hits * logits, 0, keepdims=True)
    softmax = jnp.exp(logits - logsum_ref[...])
    slope = ((weight_ref[2:3, :] * softmax - hits) * weight_ref[3:4, :]).astype(jnp.bfloat16)
    slope_ref[...] = slope
    grad_ref[...] += lax.dot_general(
        slope, table_ref[...], (((0,), (0,)), ((), ())), preferred_element_type=jnp.float32
    )


def head_back(weights, rows, logsum, wanted, weight_rows, vocab):
    tokens, width = rows.shape
    tile = vocab_tile(vocab)
    fixed = lambda k: (0, 0)
    return pl.pallas_call(
        functools.partial(head_back_kernel, tile),
        grid=(vocab // tile,),
        out_shape=[
            jax.ShapeDtypeStruct((vocab, tokens), jnp.bfloat16),
            jax.ShapeDtypeStruct((tokens, width), jnp.float32),
            jax.ShapeDtypeStruct((1, tokens), jnp.float32),
        ],
        in_specs=[
            pl.BlockSpec((tile, width), lambda k: (k, 0)),
            pl.BlockSpec((tokens, width), fixed),
            pl.BlockSpec((1, tokens), fixed),
            pl.BlockSpec((2, tokens), fixed),
            pl.BlockSpec((4, tokens), fixed),
        ],
        out_specs=[
            pl.BlockSpec((tile, tokens), lambda k: (k, 0)),
            pl.BlockSpec((tokens, width), fixed),
            pl.BlockSpec((1, tokens), fixed),
        ],
        scratch_shapes=[pltpu.VMEM((width, tokens), jnp.bfloat16)],
        compiler_params=pltpu.CompilerParams(vmem_limit_bytes=60 << 20),
    )(weights, rows, logsum, wanted, weight_rows)


def weight_grads_kernel(
    tile_units, tiles, place_ref, slope_ref, rows_ref, ids_ref, zero_ref, joint_ref, normed_ref,
    attended_ref, grad_ref, out_ref, made, sem,
):
    step = pl.program_id(0)
    unit_rows = out_ref.shape[1]
    buffer = lax.rem(step, 2)
    last_units = joint_ref.shape[0] // unit_rows + attended_ref.shape[0] // unit_rows

    def settle(which, count):
        pltpu.make_async_copy(
            made.at[which, pl.ds(0, count)], made.at[which, pl.ds(0, count)], sem.at[which]
        ).wait()

    def send(first, count):
        def push(u, carry):
            pltpu.make_async_copy(
                made.at[buffer, u], out_ref.at[place_ref[first + u]], sem.at[buffer]
            ).start()
            return carry

        lax.fori_loop(0, count, push, 0)

    @pl.when(step >= 2)
    def _():
        settle(buffer, tile_units)

    @pl.when(step < tiles)
    def _():
        row = lax.broadcasted_iota(jnp.int32, slope_ref.shape, 0)
        seen = jnp.where(row == ids_ref[...] - step * slope_ref.shape[0], 1.0, 0.0).astype(jnp.bfloat16)
        made[buffer] = (
            jnp.dot(slope_ref[...], rows_ref[...], preferred_element_type=jnp.float32)
            + jnp.dot(seen, zero_ref[...], preferred_element_type=jnp.float32)
        ).reshape(tile_units, unit_rows, -1)
        send(step * tile_units, tile_units)

    @pl.when(step == tiles)
    def _():
        joint_units = joint_ref.shape[0] // unit_rows
        made[buffer, pl.ds(0, joint_units)] = jnp.dot(
            joint_ref[...], normed_ref[...], preferred_element_type=jnp.float32
        ).reshape(joint_units, unit_rows, -1)
        made[buffer, pl.ds(joint_units, last_units - joint_units)] = jnp.dot(
            attended_ref[...], grad_ref[...], preferred_element_type=jnp.float32
        ).reshape(last_units - joint_units, unit_rows, -1)
        send(tiles * tile_units, last_units)
        settle(1 - buffer, tile_units)
        settle(buffer, last_units)


def weight_grads(place, slots, unit_rows, slope, rows, ids, zero, joint, normed, attended, grad):
    vocab, tokens = slope.shape
    width = rows.shape[1]
    tile = vocab_tile(vocab)
    tiles = vocab // tile
    fixed = lambda k: (0, 0)
    whole = lambda x: pl.BlockSpec(x.shape, fixed)
    return pl.pallas_call(
        functools.partial(weight_grads_kernel, tile // unit_rows, tiles),
        grid=(tiles + 1,),
        out_shape=jax.ShapeDtypeStruct((slots, unit_rows, width), jnp.float32),
        in_specs=[
            pl.BlockSpec(memory_space=pltpu.SMEM),
            pl.BlockSpec((tile, tokens), lambda k: (jnp.minimum(k, tiles - 1), 0)),
        ]
        + [whole(x) for x in (rows, ids, zero, joint, normed, attended, grad)],
        out_specs=whole_any,
        scratch_shapes=[
            pltpu.VMEM((2, tile // unit_rows, unit_rows, width), jnp.float32),
            pltpu.SemaphoreType.DMA((2,)),
        ],
        compiler_params=pltpu.CompilerParams(vmem_limit_bytes=60 << 20),
    )(place, slope, rows, ids, zero, joint, normed, attended, grad)


def adam_update(weight, moment_one, moment_two, gradient, step_rate, decay_factor):
    moment_new = beta_first * moment_one + (1.0 - beta_first) * gradient
    square_new = beta_second * moment_two + (1.0 - beta_second) * gradient * gradient
    moment_hat = moment_new / (1.0 - beta_first**STEP)
    square_hat = square_new / (1.0 - beta_second**STEP)
    weight_new = weight - step_rate * (
        moment_hat / (jnp.sqrt(square_hat) + adam_epsilon) + decay_factor * weight
    )
    return (weight_new, moment_new, square_new)


def norm_forward(values, gain_row):
    return values * inverse_rms(values) * gain_row


def slot_tables(owner_ids, owners, most_units):
    unit_count = owner_ids.shape[0]
    unit_index = jnp.arange(unit_count, dtype=jnp.int32)
    earlier = (owner_ids[None, :] == owner_ids[:, None]) & (
        unit_index[None, :] < unit_index[:, None]
    )
    unit_rank = jnp.sum(earlier.astype(jnp.int32), 1)
    placed = (owner_ids[None, None, :] == jnp.arange(owners, dtype=jnp.int32)[:, None, None]) & (
        unit_rank[None, None, :] == jnp.arange(most_units, dtype=jnp.int32)[None, :, None]
    )
    slot_filled = jnp.any(placed, 2)
    slot_unit = jnp.sum(jnp.where(placed, unit_index[None, None, :], 0), 2)
    return (unit_rank, slot_unit, slot_filled)


def unit_rates(unit_ids, table_units, query_units, value_units):
    return jnp.where(
        unit_ids < table_units,
        rate_table,
        jnp.where(
            unit_ids < query_units,
            rate_query,
            jnp.where(unit_ids < value_units, rate_values, rate_project),
        ),
    )


def pair_slots(route_pairs, priorities, experts, capacity):
    tokens_here = priorities.shape[0]
    pair_expert = route_pairs.T.reshape(-1)
    pair_key = (
        jnp.arange(2, dtype=jnp.int32)[:, None] * tokens_here + priorities[None, :]
    ).reshape(-1)
    before = (pair_expert[None, :] == pair_expert[:, None]) & (
        pair_key[None, :] < pair_key[:, None]
    )
    pair_rank = jnp.sum(before.astype(jnp.int32), 1)
    pair_kept = pair_rank < capacity
    pair_dest = pair_expert * capacity + jnp.minimum(pair_rank, capacity - 1)
    return (pair_kept, pair_dest)


def gelu_tanh(values):
    return jax.nn.gelu(values, approximate=True)


def to_experts(buffer):
    return lax.all_to_all(buffer, ("dp", "ctx"), split_axis=0, concat_axis=0, tiled=True)


def from_experts(buffer):
    return lax.all_to_all(buffer, ("dp", "ctx"), split_axis=0, concat_axis=0, tiled=True)


def on_device(
    token_ids,
    targets,
    counted,
    routes,
    priority,
    owner_of,
    master,
    master_first,
    master_second,
    expert_in,
    expert_in_first,
    expert_in_second,
    expert_out,
    expert_out_first,
    expert_out_second,
    norm_gains,
    norm_gains_first,
    norm_gains_second,
    router,
    router_first,
    router_second,
    rel_bias,
    rel_bias_first,
    rel_bias_second,
):
    owners = lax.axis_size(("dp", "ctx"))
    tensor_ranks = lax.axis_size("tensor")
    my_owner = lax.axis_index(("dp", "ctx"))
    my_rank = lax.axis_index("tensor")
    my_context = lax.axis_index("ctx")
    sequences, half_length = token_ids.shape
    tokens_here = sequences * half_length
    most_units = master.shape[2]
    unit_rows = master.shape[3]
    model_width = master.shape[4]
    vocab_here = VOCAB // tensor_ranks
    heads_here = rel_bias.shape[0]
    head_size = model_width // (heads_here * tensor_ranks)
    hidden_here = heads_here * head_size
    experts = router.shape[1]
    experts_here = expert_in.shape[0]
    capacity = (18 * tokens_here + 8 * experts - 1) // (8 * experts)
    table_units = vocab_here // unit_rows
    query_units = table_units + 2 * hidden_here // unit_rows
    value_units = table_units + 3 * hidden_here // unit_rows
    embed_scale = math.sqrt(model_width)
    owner_ids = owner_of[:, 0]
    unit_rank, slot_unit, slot_filled = slot_tables(owner_ids, owners, most_units)
    loss_weights = counted.reshape(tokens_here, 2).T.astype(jnp.float32) * jnp.array(
        [[1.0], [ahead_weight]], jnp.float32
    )
    weight_total = lax.psum(jnp.sum(loss_weights), ("dp", "ctx"))
    gathered = lax.all_gather(master[0, 0].astype(jnp.bfloat16), ("dp", "ctx"), axis=0, tiled=True)
    unit_slots = owner_ids * most_units + unit_rank
    weights_low = pull_units(gathered, unit_slots).reshape(-1, model_width)
    joint_low = weights_low[vocab_here : vocab_here + 3 * hidden_here]
    project_low = weights_low[vocab_here + 3 * hidden_here :]
    rolled = [project_low] + [
        lax.ppermute(project_low, "tensor", [(source, (source + step) % 4) for source in range(4)])
        for step in (1, 2, 3)
    ]
    project_full = lax.dynamic_slice_in_dim(
        jnp.concatenate(rolled[::-1] + rolled[::-1], 0), (3 - my_rank) * hidden_here, model_width, 0
    )
    local_ids = token_ids.reshape(-1) - my_rank * vocab_here
    inside = (local_ids >= 0) & (local_ids < vocab_here)
    clipped_ids = jnp.clip(local_ids, 0, vocab_here - 1)
    looked = jnp.where(inside[:, None], jnp.take(weights_low, clipped_ids, axis=0), 0)
    gain_rows = [norm_gains[k : k + 1] for k in range(3)]
    stream_shape = jax.ShapeDtypeStruct((tokens_here, model_width), jnp.float32)
    gain_shape = jax.ShapeDtypeStruct((1, model_width), jnp.float32)
    (embedded,) = sum_line(looked, [], [], keep_total, 1)
    stream_zero = embedded.astype(jnp.float32) * embed_scale
    first_normalized = norm_forward(stream_zero, norm_gains[0])
    normed_one_low = first_normalized.astype(jnp.bfloat16)
    joint = lax.dot_general(
        joint_low, normed_one_low, (((1,), (1,)), ((), ())), preferred_element_type=jnp.float32
    ).astype(jnp.bfloat16)
    pairs_before = passed_along(joint[hidden_here:], "ctx", 1)
    attended, logsum_rows = attention(rel_bias, joint, pairs_before, heads_here, head_size)
    (attended_all,) = gather_line([attended], 2)
    stream_one = stream_zero + lax.dot_general(
        attended_all.reshape(model_width, tokens_here),
        project_full,
        (((0,), (0,)), ((), ())),
        preferred_element_type=jnp.float32,
    )
    second_normalized = norm_forward(stream_one, norm_gains[1])
    normed_two_low = second_normalized.astype(jnp.bfloat16)
    router_low = router.astype(jnp.bfloat16)
    router_scores_raw = jnp.dot(normed_two_low, router_low, preferred_element_type=jnp.float32)
    route_pairs = routes.reshape(tokens_here, 2)
    route_onehot = (route_pairs[:, :, None] == jnp.arange(experts, dtype=jnp.int32)).astype(
        jnp.float32
    )
    chosen = jnp.einsum("tke,te->tk", route_onehot, router_scores_raw, precision=highest_precision)
    gate_values = jax.nn.softmax(chosen, -1)
    pair_kept, pair_dest = pair_slots(route_pairs, priority[0], experts, capacity)
    slots = lax.broadcasted_iota(jnp.int32, (experts * capacity, tokens_here), 0)
    hits = [
        (slots == pair_dest[k * tokens_here : (k + 1) * tokens_here][None, :])
        & pair_kept[k * tokens_here : (k + 1) * tokens_here][None, :]
        for k in range(2)
    ]
    hit_low = [hit.astype(jnp.bfloat16) for hit in hits]
    both_low = (hits[0] | hits[1]).astype(jnp.bfloat16)
    dispatch_rows = jnp.dot(
        both_low, normed_two_low, preferred_element_type=jnp.float32
    ).astype(jnp.bfloat16).reshape(owners, experts_here * capacity, model_width)
    arrived = to_experts(dispatch_rows).reshape(owners, experts_here, capacity, model_width)
    inner_low = expert_in.astype(jnp.bfloat16)
    outer_low = expert_out.astype(jnp.bfloat16)
    hidden_pre = jnp.einsum(
        "oecd,edf->oecf", arrived, inner_low, preferred_element_type=jnp.float32
    )
    active_low = gelu_tanh(hidden_pre).astype(jnp.bfloat16)
    expert_part = jnp.einsum(
        "oecf,efd->oecd", active_low, outer_low, preferred_element_type=jnp.float32
    ).astype(jnp.bfloat16)
    returned = from_experts(
        expert_part.reshape(owners, experts_here * capacity, model_width)
    ).reshape(experts * capacity, model_width)
    pair_rows = [
        lax.dot_general(
            hit_low[k], returned, (((0,), (0,)), ((), ())), preferred_element_type=jnp.float32
        )
        for k in range(2)
    ]
    moe_partial = gate_values[:, 0:1] * pair_rows[0] + gate_values[:, 1:2] * pair_rows[1]
    head_low, stream_two = sum_line(
        moe_partial, [stream_one, gain_rows[2]], [stream_shape], finish_mixture, 3
    )
    stats = head_sums(weights_low, head_low, vocab_here)
    logsum_vocab = join_sums(stats, 7)
    local_targets = targets.reshape(tokens_here, 2).T - my_rank * vocab_here
    weight_rows = jnp.concatenate(
        [
            loss_weights,
            loss_weights[0:1] + loss_weights[1:2],
            jnp.broadcast_to(1.0 / weight_total, (1, tokens_here)),
        ],
        0,
    )
    slopes, grad_head, target_sums = head_back(
        weights_low, head_low, logsum_vocab, local_targets, weight_rows, vocab_here
    )
    loss_local = (
        jnp.sum(weight_rows[2] * logsum_vocab[0]) * (my_rank == 0) - jnp.sum(target_sums)
    )
    grad_two_low, grad_two, gain_grad_three = sum_line(
        grad_head,
        [stream_two, gain_rows[2]],
        [stream_shape, gain_shape],
        finish_head_grad,
        4,
        prologue=clear_gain,
    )
    slot_scale = jnp.sum(
        jnp.where(hits[0], gate_values[:, 0][None, :], 0.0)
        + jnp.where(hits[1], gate_values[:, 1][None, :], 0.0),
        1,
    )
    slot_grads = jnp.dot(both_low, grad_two_low, preferred_element_type=jnp.float32)
    grad_dispatch = (
        (slot_grads * slot_scale[:, None])
        .astype(jnp.bfloat16)
        .reshape(owners, experts_here * capacity, model_width)
    )
    slot_dots = jnp.sum(slot_grads * returned.astype(jnp.float32), 1)
    gate_part = jnp.stack([jnp.sum(jnp.where(hit, slot_dots[:, None], 0.0), 0) for hit in hits])
    grad_arrived = to_experts(grad_dispatch).reshape(owners, experts_here, capacity, model_width)
    grad_active = jnp.einsum(
        "oecd,efd->oecf", grad_arrived, outer_low, preferred_element_type=jnp.float32
    )
    outer_grad = jnp.einsum(
        "oecf,oecd->efd", active_low, grad_arrived, preferred_element_type=jnp.float32
    )
    gelu_values, gelu_back = jax.vjp(gelu_tanh, hidden_pre)
    grad_hidden = gelu_back(grad_active)[0].astype(jnp.bfloat16)
    inner_grad = jnp.einsum(
        "oecd,oecf->edf", arrived, grad_hidden, preferred_element_type=jnp.float32
    )
    grad_back = jnp.einsum(
        "oecf,edf->oecd", grad_hidden, inner_low, preferred_element_type=jnp.float32
    ).astype(jnp.bfloat16)
    grad_returned = from_experts(
        grad_back.reshape(owners, experts_here * capacity, model_width)
    ).reshape(experts * capacity, model_width)
    moe_grad_part = lax.dot_general(
        both_low, grad_returned, (((0,), (0,)), ((), ())), preferred_element_type=jnp.float32
    )
    gate_block = pltpu.VMEM((3, 2, tokens_here), jnp.float32)
    grad_one_low, grad_one, logit_grad, gain_grad_two = sum_line(
        moe_grad_part,
        [
            stream_one,
            gain_rows[1],
            grad_two,
            gate_part,
            gate_values.T,
            route_pairs.T,
            router_low,
        ],
        [
            stream_shape,
            jax.ShapeDtypeStruct((experts, tokens_here), jnp.bfloat16),
            gain_shape,
        ],
        finish_expert_grad,
        5,
        prologue=start_router_grad,
        scratch=(gate_block, pltpu.SemaphoreType.DMA((3,)), pltpu.SemaphoreType.DMA((3,))),
        meets_all=True,
    )
    router_grad = lax.dot_general(
        normed_two_low, logit_grad, (((0,), (1,)), ((), ())), preferred_element_type=jnp.float32
    )
    query_grad, pair_grad, before_grad, bias_lines = attention_back(
        rel_bias,
        joint,
        pairs_before,
        logsum_rows,
        grad_one_low,
        project_low,
        heads_here,
        head_size,
    )
    grad_after = passed_along(before_grad, "ctx", -1)
    pair_grad_low = (pair_grad + grad_after.astype(jnp.float32)).astype(jnp.bfloat16)
    joint_grad = jnp.concatenate([query_grad, pair_grad_low], 0)
    distances = 2 * (half_length // BLOCK)
    bias_grad = jnp.sum(bias_lines, 1).reshape(heads_here, distances)
    zero_grad_low, gain_grad_one = sum_line(
        lax.dot_general(
            joint_grad, joint_low, (((0,), (0,)), ((), ())), preferred_element_type=jnp.float32
        ),
        [embedded, gain_rows[0], grad_one],
        [gain_shape],
        functools.partial(finish_input_grad, embed_scale),
        6,
        prologue=clear_gain,
    )
    my_units = jnp.take(slot_unit, my_owner, axis=0)
    my_filled = jnp.take(slot_filled, my_owner, axis=0)[:, None, None]
    outgoing = weight_grads(
        unit_slots,
        owners * most_units,
        unit_rows,
        slopes,
        head_low,
        local_ids[None, :],
        zero_grad_low,
        joint_grad,
        normed_one_low,
        attended,
        grad_one_low,
    )
    summed = lax.psum_scatter(outgoing, ("dp", "ctx"), scatter_dimension=0, tiled=True)
    mine = jnp.where(my_filled, summed, 0.0)
    gains_grad, loss_total = lax.psum(
        (jnp.concatenate([gain_grad_one, gain_grad_two, gain_grad_three], 0), loss_local),
        ("dp", "ctx", "tensor"),
    )
    router_grad, bias_grad = lax.psum((router_grad, bias_grad), ("dp", "ctx"))
    loss_totals = jnp.stack([loss_total, weight_total])
    slot_rates = unit_rates(my_units, table_units, query_units, value_units)[:, None, None]
    master_new, master_first_new, master_second_new = adam_update(
        master[0, 0], master_first[0, 0], master_second[0, 0], mine, slot_rates, decay_rate
    )
    inner_new, inner_first_new, inner_second_new = adam_update(
        expert_in, expert_in_first, expert_in_second, inner_grad, rate_inner, decay_rate
    )
    outer_new, outer_first_new, outer_second_new = adam_update(
        expert_out, expert_out_first, expert_out_second, outer_grad, rate_outer, decay_rate
    )
    gains_new, gains_first_new, gains_second_new = adam_update(
        norm_gains, norm_gains_first, norm_gains_second, gains_grad, rate_gains, 0.0
    )
    router_new, router_first_new, router_second_new = adam_update(
        router, router_first, router_second, router_grad, rate_router, decay_rate
    )
    biases_new, biases_first_new, biases_second_new = adam_update(
        rel_bias, rel_bias_first, rel_bias_second, bias_grad, rate_biases, 0.0
    )
    return (
        loss_totals,
        master_new[None, None],
        master_first_new[None, None],
        master_second_new[None, None],
        inner_new,
        inner_first_new,
        inner_second_new,
        outer_new,
        outer_first_new,
        outer_second_new,
        gains_new,
        gains_first_new,
        gains_second_new,
        router_new,
        router_first_new,
        router_second_new,
        biases_new,
        biases_first_new,
        biases_second_new,
    )


def solution(mesh):
    in_specs = (
        P("dp", "ctx"),
        P("dp", "ctx", None),
        P("dp", "ctx", None),
        P("dp", "ctx", None),
        P(("dp", "ctx"), None),
        P(),
        P("tensor", ("dp", "ctx"), None, None, None),
        P("tensor", ("dp", "ctx"), None, None, None),
        P("tensor", ("dp", "ctx"), None, None, None),
        P(("dp", "ctx"), None, "tensor"),
        P(("dp", "ctx"), None, "tensor"),
        P(("dp", "ctx"), None, "tensor"),
        P(("dp", "ctx"), "tensor", None),
        P(("dp", "ctx"), "tensor", None),
        P(("dp", "ctx"), "tensor", None),
        P(),
        P(),
        P(),
        P(),
        P(),
        P(),
        P("tensor", None),
        P("tensor", None),
        P("tensor", None),
    )
    out_specs = (
        P(),
        P("tensor", ("dp", "ctx"), None, None, None),
        P("tensor", ("dp", "ctx"), None, None, None),
        P("tensor", ("dp", "ctx"), None, None, None),
        P(("dp", "ctx"), None, "tensor"),
        P(("dp", "ctx"), None, "tensor"),
        P(("dp", "ctx"), None, "tensor"),
        P(("dp", "ctx"), "tensor", None),
        P(("dp", "ctx"), "tensor", None),
        P(("dp", "ctx"), "tensor", None),
        P(),
        P(),
        P(),
        P(),
        P(),
        P(),
        P("tensor", None),
        P("tensor", None),
        P("tensor", None),
    )
    return jax.shard_map(
        on_device, mesh=mesh, in_specs=in_specs, out_specs=out_specs, check_vma=False
    )
```

```python
import functools
import math

import jax
import jax.numpy as jnp
from jax import lax
from jax.experimental import pallas as pl
from jax.experimental.pallas import tpu as pltpu
from jax.sharding import PartitionSpec as P

VOCAB = 32000
BLOCK = 256
STEP = 10


highest_precision = lax.Precision.HIGHEST
beta_first = 0.9
beta_second = 0.95
adam_epsilon = 1e-08
norm_epsilon = 1e-06
ahead_weight = 0.3
masked_score = -1e30
rate_table = 0.1
rate_query = 0.05
rate_values = 0.05
rate_project = 0.5
rate_inner = 0.05
rate_outer = 0.03
rate_gains = 0.5
rate_router = 0.05
rate_biases = 0.5
decay_rate = 0.1


def passed_along(value, axis, steps):
    count = lax.axis_size(axis)
    initial, last = (max(0, -steps), min(count, count - steps))
    return lax.ppermute(value, axis, [(source, source + steps) for source in range(initial, last)])

MESH_ID = pl.DeviceIdType.MESH
whole_vmem = pl.BlockSpec(memory_space=pltpu.VMEM)
whole_any = pl.BlockSpec(memory_space=pl.ANY)
line_rows = 64
line_lag = 2


def sum_line_kernel(
    count, meets_all, prologue, epilogue, ending, n_extra, n_aux, n_scratch, part_ref, *refs
):
    extras = refs[:n_extra]
    out_ref = refs[n_extra]
    aux = refs[n_extra + 1 : n_extra + 1 + n_aux]
    rest = refs[n_extra + 1 + n_aux :]
    scratch = rest[:n_scratch]
    stage, from_end, from_mid, send_sem, end_sem, mid_sem, back_sem, back_recv = rest[n_scratch:]
    rank = lax.axis_index("tensor")
    inner = (rank == 1) | (rank == 2)
    end_peer = jnp.where(rank < 2, 1 - rank, 5 - rank)
    mid_peer = 3 - rank
    barrier = pltpu.get_barrier_semaphore()
    if not meets_all:
        pl.semaphore_signal(barrier, inc=1, device_id={"tensor": end_peer}, device_id_type=MESH_ID)

        @pl.when(inner)
        def _():
            pl.semaphore_signal(
                barrier, inc=1, device_id={"tensor": mid_peer}, device_id_type=MESH_ID
            )
            pl.semaphore_wait(barrier, 2)

        @pl.when(jnp.logical_not(inner))
        def _():
            pl.semaphore_wait(barrier, 1)
    else:
        for step in (1, 2, 3):
            other = lax.rem(rank + step, 4)
            pl.semaphore_signal(barrier, inc=1, device_id={"tensor": other}, device_id_type=MESH_ID)
        pl.semaphore_wait(barrier, 3)

    rows = line_rows

    def span(i):
        return pl.ds(pl.multiple_of(i * rows, rows), rows)

    def to_inner(i):
        return pltpu.make_async_remote_copy(
            src_ref=stage.at[i],
            dst_ref=from_end.at[i],
            send_sem=send_sem.at[i],
            recv_sem=end_sem.at[i],
            device_id={"tensor": end_peer},
            device_id_type=MESH_ID,
        )

    def to_middle(i):
        return pltpu.make_async_remote_copy(
            src_ref=stage.at[i],
            dst_ref=from_mid.at[i],
            send_sem=send_sem.at[i],
            recv_sem=mid_sem.at[i],
            device_id={"tensor": mid_peer},
            device_id_type=MESH_ID,
        )

    def to_end(i):
        return pltpu.make_async_remote_copy(
            src_ref=out_ref.at[span(i)],
            dst_ref=out_ref.at[span(i)],
            send_sem=back_sem.at[i],
            recv_sem=back_recv.at[i],
            device_id={"tensor": end_peer},
            device_id_type=MESH_ID,
        )

    @pl.when(jnp.logical_not(inner))
    def _():
        def push(i, carry):
            stage[i] = part_ref[span(i)].astype(jnp.bfloat16)
            to_inner(i).start()
            return carry

        lax.fori_loop(0, count, push, 0)

    if prologue is not None:
        prologue(rank, inner, extras, aux, scratch)

    @pl.when(inner)
    def _():
        def step(i, carry):
            @pl.when(i < count)
            def _():
                to_inner(i).wait_recv()
                mine = part_ref[span(i)].astype(jnp.float32) + from_end[i].astype(jnp.float32)
                stage[i] = mine.astype(jnp.bfloat16)
                to_middle(i).start()

            @pl.when(i >= line_lag)
            def _():
                j = i - line_lag
                to_middle(j).wait_recv()
                total = stage[j].astype(jnp.float32) + from_mid[j].astype(jnp.float32)
                out_ref[span(j)] = epilogue(total, span(j), rank, extras, aux, scratch)
                to_end(j).start()

            return carry

        lax.fori_loop(0, count + line_lag, step, 0)

        def drain(i, carry):
            to_middle(i).wait_send()
            to_end(i).wait_send()
            return carry

        lax.fori_loop(0, count, drain, 0)

    @pl.when(jnp.logical_not(inner))
    def _():
        def finish(i, carry):
            to_end(i).wait_recv()
            to_inner(i).wait_send()
            return carry

        lax.fori_loop(0, count, finish, 0)

    if ending is not None:
        ending(inner, end_peer, extras, aux, scratch)


def sum_line(
    part,
    extras,
    aux_shapes,
    epilogue,
    collective_id,
    prologue=None,
    scratch=(),
    meets_all=False,
    ending=None,
):
    tokens, width = part.shape
    count = tokens // line_rows
    chunks = pltpu.VMEM((count, line_rows, width), jnp.bfloat16)
    return pl.pallas_call(
        functools.partial(
            sum_line_kernel,
            count,
            meets_all,
            prologue,
            epilogue,
            ending,
            len(extras),
            len(aux_shapes),
            len(scratch),
        ),
        out_shape=[jax.ShapeDtypeStruct((tokens, width), jnp.bfloat16)] + list(aux_shapes),
        in_specs=[whole_vmem] * (1 + len(extras)),
        out_specs=[whole_vmem] * (1 + len(aux_shapes)),
        scratch_shapes=list(scratch)
        + [chunks, chunks, chunks]
        + [pltpu.SemaphoreType.DMA((count,))] * 5,
        compiler_params=pltpu.CompilerParams(
            collective_id=collective_id, has_side_effects=True, vmem_limit_bytes=48 << 20
        ),
    )(part, *extras)


def keep_total(total, span, rank, extras, aux, scratch):
    return total.astype(jnp.bfloat16)


def inverse_rms(values):
    return lax.rsqrt(jnp.mean(values * values, -1, keepdims=True) + norm_epsilon)


def finish_mixture(total, span, rank, extras, aux, scratch):
    stream_one, gain = extras
    stream_two = stream_one[span] + total
    aux[0][span] = stream_two
    return (stream_two * inverse_rms(stream_two) * gain[...]).astype(jnp.bfloat16)


def norm_back_rows(values, gain, upstream):
    inverse = inverse_rms(values)
    normed = values * inverse
    scaled = upstream * gain
    gain_grad = jnp.sum(upstream * normed, 0, keepdims=True)
    inputs_grad = inverse * (scaled - normed * jnp.mean(scaled * normed, -1, keepdims=True))
    return (inputs_grad, gain_grad)


def clear_gain(rank, inner, extras, aux, scratch):
    @pl.when(inner)
    def _():
        aux[-1][...] = jnp.zeros_like(aux[-1])


def share_gains(inner, end_peer, extras, aux, scratch):
    gains = aux[0]
    copy = pltpu.make_async_remote_copy(
        src_ref=gains,
        dst_ref=gains,
        send_sem=scratch[0],
        recv_sem=scratch[1],
        device_id={"tensor": end_peer},
        device_id_type=MESH_ID,
    )

    @pl.when(inner)
    def _():
        gains[1:2, :] = extras[3][...]
        gains[2:3, :] = extras[4][...]
        copy.start()
        copy.wait_send()

    @pl.when(jnp.logical_not(inner))
    def _():
        copy.wait_recv()


def finish_head_grad(total, span, rank, extras, aux, scratch):
    stream_two, gain = extras
    grad_two, gain_grad = norm_back_rows(stream_two[span], gain[...], total)
    aux[0][span] = grad_two
    aux[1][...] += gain_grad
    return grad_two.astype(jnp.bfloat16)


def start_router_grad(rank, inner, extras, aux, scratch):
    stream_one, gain, grad_two, gate_part, gates, routes, router_low = extras
    grad_one, logit_grad, target_total, gain_grad = aux
    landed, gate_send, gate_recv = scratch
    clear_gain(rank, inner, extras, aux, scratch)
    copies = []
    for step in (1, 2, 3):
        copy = pltpu.make_async_remote_copy(
            src_ref=gate_part,
            dst_ref=landed.at[step - 1],
            send_sem=gate_send.at[step - 1],
            recv_sem=gate_recv.at[step - 1],
            device_id={"tensor": lax.rem(rank + step, 4)},
            device_id_type=MESH_ID,
        )
        copy.start()
        copies.append(copy)
    for copy in copies:
        copy.wait()
    gate_grad = jnp.zeros(gate_part.shape, jnp.float32)
    for source in range(4):
        piece = jnp.zeros(gate_part.shape, jnp.float32)
        for step in (1, 2, 3):
            piece = jnp.where(lax.rem(source + step, 4) == rank, landed[step - 1], piece)
        gate_grad = gate_grad + jnp.where(rank == source, gate_part[...], piece)
    target_total[...] = gate_grad[2:3]
    gate_grad = gate_grad[0:2]
    weighted = gates[...] * gate_grad
    chosen = gates[...] * (gate_grad - (weighted[0:1] + weighted[1:2]))
    experts, tokens = logit_grad.shape
    row = lax.broadcasted_iota(jnp.int32, (experts, tokens), 0)
    placed = jnp.where(row == routes[0:1], chosen[0:1], 0.0) + jnp.where(
        row == routes[1:2], chosen[1:2], 0.0
    )
    logit_grad[...] = placed.astype(jnp.bfloat16)

    @pl.when(inner)
    def _():
        grad_one[...] = lax.dot_general(
            logit_grad[...],
            router_low[...],
            (((0,), (1,)), ((), ())),
            preferred_element_type=jnp.float32,
        )


def finish_expert_grad(total, span, rank, extras, aux, scratch):
    stream_one, gain, grad_two, gate_part, gates, routes, router_low = extras
    grad_one, logit_grad, target_total, gain_grad = aux
    part, gain_part = norm_back_rows(
        stream_one[span], gain[...], total + grad_one[span]
    )
    result = grad_two[span] + part
    grad_one[span] = result
    gain_grad[...] += gain_part
    return result.astype(jnp.bfloat16)


def finish_input_grad(scale, total, span, rank, extras, aux, scratch):
    embedded, gain, grad_one = extras[:3]
    stream_zero = embedded[span].astype(jnp.float32) * scale
    part, gain_part = norm_back_rows(stream_zero, gain[...], total)
    aux[0][0:1, :] += gain_part
    return ((grad_one[span] + part) * scale).astype(jnp.bfloat16)


def gather_line_kernel(count, *refs):
    ins = refs[:count]
    outs = refs[count : 2 * count]
    local_sem, send_sem, recv_sem = refs[2 * count :]
    rank = lax.axis_index("tensor")
    barrier = pltpu.get_barrier_semaphore()
    for step in (1, 2, 3):
        other = lax.rem(rank + step, 4)
        pl.semaphore_signal(barrier, inc=1, device_id={"tensor": other}, device_id_type=MESH_ID)
    pl.semaphore_wait(barrier, 3)
    copies = []
    for k in range(count):
        for step in (1, 2, 3):
            copy = pltpu.make_async_remote_copy(
                src_ref=ins[k],
                dst_ref=outs[k].at[rank],
                send_sem=send_sem.at[k, step - 1],
                recv_sem=recv_sem.at[k, step - 1],
                device_id={"tensor": lax.rem(rank + step, 4)},
                device_id_type=MESH_ID,
            )
            copy.start()
            copies.append(copy)
        own = pltpu.make_async_copy(ins[k], outs[k].at[rank], local_sem.at[k])
        own.start()
        own.wait()
    for copy in copies:
        copy.wait()


def gather_line(arrays, collective_id):
    count = len(arrays)
    return pl.pallas_call(
        functools.partial(gather_line_kernel, count),
        out_shape=[jax.ShapeDtypeStruct((4,) + x.shape, x.dtype) for x in arrays],
        in_specs=[whole_vmem] * count,
        out_specs=[whole_vmem] * count,
        scratch_shapes=[
            pltpu.SemaphoreType.DMA((count,)),
            pltpu.SemaphoreType.DMA((count, 3)),
            pltpu.SemaphoreType.DMA((count, 3)),
        ],
        compiler_params=pltpu.CompilerParams(
            collective_id=collective_id, has_side_effects=True, vmem_limit_bytes=40 << 20
        ),
    )(*arrays)


def pull_units_kernel(group, slots_ref, source_ref, out_ref, sem):
    start = pl.program_id(0) * group

    def push(u, carry):
        pltpu.make_async_copy(source_ref.at[slots_ref[start + u]], out_ref.at[u], sem).start()
        return carry

    lax.fori_loop(0, group, push, 0)
    pltpu.make_async_copy(out_ref, out_ref, sem).wait()


def pull_units(source, slots):
    count = slots.shape[0]
    unit_bytes = math.prod(source.shape[1:]) * source.dtype.itemsize
    group = max(k for k in range(1, count + 1) if count % k == 0 and (k <= 32 or k * unit_bytes < 15 << 20))
    return pl.pallas_call(
        functools.partial(pull_units_kernel, group),
        grid=(count // group,),
        out_shape=jax.ShapeDtypeStruct((count,) + source.shape[1:], source.dtype),
        in_specs=[pl.BlockSpec(memory_space=pltpu.SMEM), whole_any],
        out_specs=pl.BlockSpec((group,) + source.shape[1:], lambda k: (k,) + (0,) * (source.ndim - 1)),
        scratch_shapes=[pltpu.SemaphoreType.DMA],
        compiler_params=pltpu.CompilerParams(vmem_limit_bytes=40 << 20),
    )(slots, source)


def attention_kernel(heads, size, bias_ref, own_ref, before_ref, out_ref, logsum_ref, scores, peak, total):
    tokens = own_ref.shape[1]
    blocks = tokens // BLOCK
    hidden = heads * size
    later = lax.axis_index("ctx") > 0

    for head in range(heads):
        query = own_ref[head * size : (head + 1) * size, :].astype(jnp.float32).T * size**-0.5
        query = query.astype(jnp.bfloat16)
        own_keys = own_ref[hidden + head * size : hidden + (head + 1) * size, :]
        old_keys = before_ref[head * size : (head + 1) * size, :]
        own_values = own_ref[2 * hidden + head * size : 2 * hidden + (head + 1) * size, :]
        own_values = own_values.astype(jnp.float32).T.astype(jnp.bfloat16)
        old_values = before_ref[hidden + head * size : hidden + (head + 1) * size, :]
        old_values = old_values.astype(jnp.float32).T.astype(jnp.bfloat16)
        for block in range(blocks):
            rows = query[block * BLOCK : (block + 1) * BLOCK]
            width = (block + 1) * BLOCK
            mine = jnp.dot(rows, own_keys[:, :width], preferred_element_type=jnp.float32)
            top = None
            parts = []
            for k in range(block + 1):
                part = mine[:, k * BLOCK : (k + 1) * BLOCK] + bias_ref[head, block - k]
                parts.append(part)
                high = jnp.max(part, 1, keepdims=True)
                top = high if top is None else jnp.maximum(top, high)
            peak[...] = top

            @pl.when(later)
            def _():
                old = jnp.dot(rows, old_keys, preferred_element_type=jnp.float32)
                top_old = None
                for k in range(blocks):
                    part = old[:, k * BLOCK : (k + 1) * BLOCK] + bias_ref[head, block + blocks - k]
                    scores[:, k * BLOCK : (k + 1) * BLOCK] = part
                    high = jnp.max(part, 1, keepdims=True)
                    top_old = high if top_old is None else jnp.maximum(top_old, high)
                peak[...] = jnp.maximum(peak[...], top_old)

            top = peak[...]
            parts = [jnp.exp(part - top) for part in parts]
            own_sum = None
            for part in parts:
                part_sum = jnp.sum(part, 1, keepdims=True)
                own_sum = part_sum if own_sum is None else own_sum + part_sum
            total[...] = own_sum

            @pl.when(later)
            def _():
                old_exp = jnp.exp(scores[...] - top)
                scores[...] = old_exp
                total[...] += jnp.sum(old_exp, 1, keepdims=True)

            full = total[...]
            inverse = 1.0 / full
            low = jnp.concatenate([(part * inverse).astype(jnp.bfloat16) for part in parts], 1)
            result = jnp.dot(low, own_values[:width], preferred_element_type=jnp.float32)
            peak[...] = top + jnp.log(full)
            logsum_ref[head, block * BLOCK : (block + 1) * BLOCK, :] = peak[...]
            place = (slice(head * size, (head + 1) * size), slice(block * BLOCK, (block + 1) * BLOCK))

            @pl.when(later)
            def _():
                low_old = (scores[...] * inverse).astype(jnp.bfloat16)
                both = result + jnp.dot(low_old, old_values, preferred_element_type=jnp.float32)
                out_ref[place] = both.T.astype(jnp.bfloat16)

            @pl.when(jnp.logical_not(later))
            def _():
                out_ref[place] = result.T.astype(jnp.bfloat16)


def attention(biases, own, before, heads, size):
    tokens = own.shape[1]
    return pl.pallas_call(
        functools.partial(attention_kernel, heads, size),
        out_shape=[
            jax.ShapeDtypeStruct((heads * size, tokens), jnp.bfloat16),
            jax.ShapeDtypeStruct((heads, tokens, 1), jnp.float32),
        ],
        in_specs=[pl.BlockSpec(memory_space=pltpu.SMEM), whole_vmem, whole_vmem],
        out_specs=[whole_vmem, whole_vmem],
        scratch_shapes=[
            pltpu.VMEM((BLOCK, tokens), jnp.float32),
            pltpu.VMEM((BLOCK, 1), jnp.float32),
            pltpu.VMEM((BLOCK, 1), jnp.float32),
        ],
        compiler_params=pltpu.CompilerParams(vmem_limit_bytes=40 << 20),
    )(biases, own, before)


def attention_back_kernel(
    heads, size, bias_ref, own_ref, before_ref, logsum_ref, grad_ref, project_ref,
    query_out, own_out, before_out, bias_out, probs, slopes, inner, query_sum, own_sum, before_sum,
):
    tokens = own_ref.shape[1]
    blocks = tokens // BLOCK
    hidden = heads * size
    later = lax.axis_index("ctx") > 0
    bias_out[...] = jnp.zeros_like(bias_out)

    def flipped(rows):
        return rows.astype(jnp.float32).T.astype(jnp.bfloat16)

    for head in range(heads):
        span = slice(head * size, (head + 1) * size)
        value_span = slice(hidden + head * size, hidden + (head + 1) * size)
        query_rows = own_ref[span, :]
        query = flipped(query_rows) * jnp.bfloat16(size**-0.5)
        own_keys = own_ref[hidden + head * size : hidden + (head + 1) * size, :]
        own_values = own_ref[2 * hidden + head * size : 2 * hidden + (head + 1) * size, :]
        old_keys = before_ref[span, :]
        old_values = before_ref[value_span, :]
        own_keys_flip = flipped(own_keys)
        grad = lax.dot_general(
            grad_ref[...], project_ref[span, :], (((1,), (1,)), ((), ())), preferred_element_type=jnp.float32
        )
        grad_rows = grad.T.astype(jnp.bfloat16)
        grad = grad.astype(jnp.bfloat16)
        own_sum[...] = jnp.zeros_like(own_sum)

        @pl.when(later)
        def _():
            before_sum[...] = jnp.zeros_like(before_sum)

        for block in range(blocks):
            at = slice(block * BLOCK, (block + 1) * BLOCK)
            width = (block + 1) * BLOCK
            rows, up = query[at], grad[at]
            lse = logsum_ref[head, at, :]
            score = jnp.dot(rows, own_keys[:, :width], preferred_element_type=jnp.float32)
            prob = jnp.concatenate(
                [
                    jnp.exp(score[:, k * BLOCK : (k + 1) * BLOCK] + (bias_ref[head, block - k] - lse))
                    for k in range(block + 1)
                ],
                1,
            )
            slope = jnp.dot(up, own_values[:, :width], preferred_element_type=jnp.float32)
            inner[...] = jnp.sum(prob * slope, 1, keepdims=True)

            @pl.when(later)
            def _():
                score = jnp.dot(rows, old_keys, preferred_element_type=jnp.float32)
                old_slope = jnp.dot(up, old_values, preferred_element_type=jnp.float32)
                old_prob = jnp.concatenate(
                    [
                        jnp.exp(
                            score[:, k * BLOCK : (k + 1) * BLOCK]
                            + (bias_ref[head, block + blocks - k] - lse)
                        )
                        for k in range(blocks)
                    ],
                    1,
                )
                probs[...] = old_prob
                slopes[...] = old_slope
                inner[...] += jnp.sum(old_prob * old_slope, 1, keepdims=True)

            row_inner = inner[...]
            low_grad = (prob * (slope - row_inner)).astype(jnp.bfloat16)
            query_sum[...] = jnp.dot(
                low_grad, own_keys_flip[:width], preferred_element_type=jnp.float32
            )
            own_sum[:size, :width] += jnp.dot(
                query_rows[:, at], low_grad, preferred_element_type=jnp.float32
            )
            own_sum[size:, :width] += jnp.dot(
                grad_rows[:, at], prob.astype(jnp.bfloat16), preferred_element_type=jnp.float32
            )
            for k in range(block + 1):
                line = head * 2 * blocks + block - k
                bias_out[line : line + 1, :] += jnp.sum(
                    low_grad[:, k * BLOCK : (k + 1) * BLOCK].astype(jnp.float32), 0, keepdims=True
                )

            @pl.when(later)
            def _():
                old_prob = probs[...]
                low_old = (old_prob * (slopes[...] - row_inner)).astype(jnp.bfloat16)
                query_sum[...] += jnp.dot(
                    low_old, flipped(old_keys), preferred_element_type=jnp.float32
                )
                before_sum[:size, :] += jnp.dot(
                    query_rows[:, at], low_old, preferred_element_type=jnp.float32
                )
                before_sum[size:, :] += jnp.dot(
                    grad_rows[:, at], old_prob.astype(jnp.bfloat16), preferred_element_type=jnp.float32
                )
                for k in range(blocks):
                    line = head * 2 * blocks + block + blocks - k
                    bias_out[line : line + 1, :] += jnp.sum(
                        low_old[:, k * BLOCK : (k + 1) * BLOCK].astype(jnp.float32), 0, keepdims=True
                    )

            query_out[span, at] = (query_sum[...].T * size**-0.5).astype(jnp.bfloat16)

        own_out[span, :] = own_sum[:size, :] * size**-0.5
        own_out[value_span, :] = own_sum[size:, :]

        @pl.when(later)
        def _():
            before_out[span, :] = (before_sum[:size, :] * size**-0.5).astype(jnp.bfloat16)
            before_out[value_span, :] = before_sum[size:, :].astype(jnp.bfloat16)

    @pl.when(jnp.logical_not(later))
    def _():
        before_out[...] = jnp.zeros_like(before_out)


def attention_back(biases, own, before, logsum, grad, project, heads, size):
    tokens = own.shape[1]
    hidden = heads * size
    return pl.pallas_call(
        functools.partial(attention_back_kernel, heads, size),
        out_shape=[
            jax.ShapeDtypeStruct((hidden, tokens), jnp.bfloat16),
            jax.ShapeDtypeStruct((2 * hidden, tokens), jnp.float32),
            jax.ShapeDtypeStruct((2 * hidden, tokens), jnp.bfloat16),
            jax.ShapeDtypeStruct((heads * 2 * (tokens // BLOCK), BLOCK), jnp.float32),
        ],
        in_specs=[pl.BlockSpec(memory_space=pltpu.SMEM)] + [whole_vmem] * 5,
        out_specs=[whole_vmem] * 4,
        scratch_shapes=[
            pltpu.VMEM((BLOCK, tokens), jnp.float32),
            pltpu.VMEM((BLOCK, tokens), jnp.float32),
            pltpu.VMEM((BLOCK, 1), jnp.float32),
            pltpu.VMEM((BLOCK, size), jnp.float32),
            pltpu.VMEM((2 * size, tokens), jnp.float32),
            pltpu.VMEM((2 * size, tokens), jnp.float32),
        ],
        compiler_params=pltpu.CompilerParams(vmem_limit_bytes=48 << 20),
    )(biases, own, before, logsum, grad, project)


def head_sums_kernel(table_ref, rows_ref, stats_ref, turned):
    @pl.when(pl.program_id(0) == 0)
    def _():
        turned[...] = rows_ref[...].astype(jnp.float32).T.astype(jnp.bfloat16)
        stats_ref[0:1, :] = jnp.full_like(stats_ref[0:1, :], masked_score)
        stats_ref[1:2, :] = jnp.zeros_like(stats_ref[1:2, :])

    logits = jnp.dot(table_ref[...], turned[...], preferred_element_type=jnp.float32)
    before = stats_ref[0:1, :]
    top = jnp.maximum(before, jnp.max(logits, 0, keepdims=True))
    stats_ref[1:2, :] = stats_ref[1:2, :] * jnp.exp(before - top) + jnp.sum(
        jnp.exp(logits - top), 0, keepdims=True
    )
    stats_ref[0:1, :] = top


def vocab_tile(vocab):
    return max(k for k in range(16, 1601, 16) if vocab % k == 0)


def head_sums(weights, rows, vocab):
    tokens, width = rows.shape
    tile = vocab_tile(vocab)
    return pl.pallas_call(
        head_sums_kernel,
        grid=(vocab // tile,),
        out_shape=jax.ShapeDtypeStruct((2, tokens), jnp.float32),
        in_specs=[pl.BlockSpec((tile, width), lambda k: (k, 0)), pl.BlockSpec((tokens, width), lambda k: (0, 0))],
        out_specs=pl.BlockSpec((2, tokens), lambda k: (0, 0)),
        scratch_shapes=[pltpu.VMEM((width, tokens), jnp.bfloat16)],
        compiler_params=pltpu.CompilerParams(vmem_limit_bytes=56 << 20),
    )(weights, rows)


def join_sums_kernel(stats_ref, logsum_ref, landed, send_sem, recv_sem):
    rank = lax.axis_index("tensor")
    barrier = pltpu.get_barrier_semaphore()
    for step in (1, 2, 3):
        other = lax.rem(rank + step, 4)
        pl.semaphore_signal(barrier, inc=1, device_id={"tensor": other}, device_id_type=MESH_ID)
    pl.semaphore_wait(barrier, 3)
    copies = []
    for step in (1, 2, 3):
        copy = pltpu.make_async_remote_copy(
            src_ref=stats_ref,
            dst_ref=landed.at[step - 1],
            send_sem=send_sem.at[step - 1],
            recv_sem=recv_sem.at[step - 1],
            device_id={"tensor": lax.rem(rank + step, 4)},
            device_id_type=MESH_ID,
        )
        copy.start()
        copies.append(copy)
    for copy in copies:
        copy.wait()
    tops, sums = [], []
    for source in range(4):
        piece = stats_ref[...]
        for step in (1, 2, 3):
            piece = jnp.where(lax.rem(source + step, 4) == rank, landed[step - 1], piece)
        tops.append(piece[0:1])
        sums.append(piece[1:2])
    top = jnp.maximum(jnp.maximum(tops[0], tops[1]), jnp.maximum(tops[2], tops[3]))
    total = sums[0] * jnp.exp(tops[0] - top)
    for source in (1, 2, 3):
        total = total + sums[source] * jnp.exp(tops[source] - top)
    logsum_ref[...] = top + jnp.log(total)


def join_sums(stats, collective_id):
    tokens = stats.shape[1]
    return pl.pallas_call(
        join_sums_kernel,
        out_shape=jax.ShapeDtypeStruct((1, tokens), jnp.float32),
        in_specs=[whole_vmem],
        out_specs=whole_vmem,
        scratch_shapes=[
            pltpu.VMEM((3, 2, tokens), jnp.float32),
            pltpu.SemaphoreType.DMA((3,)),
            pltpu.SemaphoreType.DMA((3,)),
        ],
        compiler_params=pltpu.CompilerParams(collective_id=collective_id, has_side_effects=True),
    )(stats)


def head_back_kernel(
    tile, table_ref, rows_ref, logsum_ref, wanted_ref, weight_ref, slope_ref, grad_ref, picked_ref, turned
):
    step = pl.program_id(0)

    @pl.when(step == 0)
    def _():
        turned[...] = rows_ref[...].astype(jnp.float32).T.astype(jnp.bfloat16)
        picked_ref[...] = jnp.zeros_like(picked_ref)
        grad_ref[...] = jnp.zeros_like(grad_ref)

    logits = jnp.dot(table_ref[...], turned[...], preferred_element_type=jnp.float32)
    row = lax.broadcasted_iota(jnp.int32, logits.shape, 0)
    base = step * tile
    hits = jnp.where(row == wanted_ref[0:1, :] - base, weight_ref[0:1, :], 0.0) + jnp.where(
        row == wanted_ref[1:2, :] - base, weight_ref[1:2, :], 0.0
    )
    picked_ref[...] += jnp.sum(hits * logits, 0, keepdims=True)
    softmax = jnp.exp(logits - logsum_ref[...])
    slope = ((weight_ref[2:3, :] * softmax - hits) * weight_ref[3:4, :]).astype(jnp.bfloat16)
    slope_ref[...] = slope
    grad_ref[...] += lax.dot_general(
        slope, table_ref[...], (((0,), (0,)), ((), ())), preferred_element_type=jnp.float32
    )


def head_back(weights, rows, logsum, wanted, weight_rows, vocab):
    tokens, width = rows.shape
    tile = vocab_tile(vocab)
    fixed = lambda k: (0, 0)
    return pl.pallas_call(
        functools.partial(head_back_kernel, tile),
        grid=(vocab // tile,),
        out_shape=[
            jax.ShapeDtypeStruct((vocab, tokens), jnp.bfloat16),
            jax.ShapeDtypeStruct((tokens, width), jnp.float32),
            jax.ShapeDtypeStruct((1, tokens), jnp.float32),
        ],
        in_specs=[
            pl.BlockSpec((tile, width), lambda k: (k, 0)),
            pl.BlockSpec((tokens, width), fixed),
            pl.BlockSpec((1, tokens), fixed),
            pl.BlockSpec((2, tokens), fixed),
            pl.BlockSpec((4, tokens), fixed),
        ],
        out_specs=[
            pl.BlockSpec((tile, tokens), lambda k: (k, 0)),
            pl.BlockSpec((tokens, width), fixed),
            pl.BlockSpec((1, tokens), fixed),
        ],
        scratch_shapes=[pltpu.VMEM((width, tokens), jnp.bfloat16)],
        compiler_params=pltpu.CompilerParams(vmem_limit_bytes=60 << 20),
    )(weights, rows, logsum, wanted, weight_rows)


def weight_grads_kernel(
    tile_units, tiles, place_ref, slope_ref, rows_ref, ids_ref, zero_ref, joint_ref, normed_ref,
    attended_ref, grad_ref, out_ref, made, sem,
):
    step = pl.program_id(0)
    unit_rows = out_ref.shape[1]
    buffer = lax.rem(step, 2)
    last_units = joint_ref.shape[0] // unit_rows + attended_ref.shape[0] // unit_rows

    def settle(which, count):
        pltpu.make_async_copy(
            made.at[which, pl.ds(0, count)], made.at[which, pl.ds(0, count)], sem.at[which]
        ).wait()

    def send(first, count):
        def push(u, carry):
            pltpu.make_async_copy(
                made.at[buffer, u], out_ref.at[place_ref[first + u]], sem.at[buffer]
            ).start()
            return carry

        lax.fori_loop(0, count, push, 0)

    @pl.when(step >= 2)
    def _():
        settle(buffer, tile_units)

    @pl.when(step < tiles)
    def _():
        row = lax.broadcasted_iota(jnp.int32, slope_ref.shape, 0)
        seen = jnp.where(row == ids_ref[...] - step * slope_ref.shape[0], 1.0, 0.0).astype(jnp.bfloat16)
        made[buffer] = (
            jnp.dot(slope_ref[...], rows_ref[...], preferred_element_type=jnp.float32)
            + jnp.dot(seen, zero_ref[...], preferred_element_type=jnp.float32)
        ).astype(jnp.bfloat16).reshape(tile_units, unit_rows, -1)
        send(step * tile_units, tile_units)

    @pl.when(step == tiles)
    def _():
        joint_units = joint_ref.shape[0] // unit_rows
        made[buffer, pl.ds(0, joint_units)] = jnp.dot(
            joint_ref[...], normed_ref[...], preferred_element_type=jnp.float32
        ).astype(jnp.bfloat16).reshape(joint_units, unit_rows, -1)
        made[buffer, pl.ds(joint_units, last_units - joint_units)] = jnp.dot(
            attended_ref[...], grad_ref[...], preferred_element_type=jnp.float32
        ).astype(jnp.bfloat16).reshape(last_units - joint_units, unit_rows, -1)
        send(tiles * tile_units, last_units)
        settle(1 - buffer, tile_units)
        settle(buffer, last_units)


def weight_grads(place, slots, unit_rows, slope, rows, ids, zero, joint, normed, attended, grad):
    vocab, tokens = slope.shape
    width = rows.shape[1]
    tile = vocab_tile(vocab)
    tiles = vocab // tile
    fixed = lambda k: (0, 0)
    whole = lambda x: pl.BlockSpec(x.shape, fixed)
    return pl.pallas_call(
        functools.partial(weight_grads_kernel, tile // unit_rows, tiles),
        grid=(tiles + 1,),
        out_shape=jax.ShapeDtypeStruct((slots, unit_rows, width), jnp.bfloat16),
        in_specs=[
            pl.BlockSpec(memory_space=pltpu.SMEM),
            pl.BlockSpec((tile, tokens), lambda k: (jnp.minimum(k, tiles - 1), 0)),
        ]
        + [whole(x) for x in (rows, ids, zero, joint, normed, attended, grad)],
        out_specs=whole_any,
        scratch_shapes=[
            pltpu.VMEM((2, tile // unit_rows, unit_rows, width), jnp.bfloat16),
            pltpu.SemaphoreType.DMA((2,)),
        ],
        compiler_params=pltpu.CompilerParams(vmem_limit_bytes=60 << 20),
    )(place, slope, rows, ids, zero, joint, normed, attended, grad)


def adam_update(weight, moment_one, moment_two, gradient, step_rate, decay_factor):
    moment_new = beta_first * moment_one + (1.0 - beta_first) * gradient
    square_new = beta_second * moment_two + (1.0 - beta_second) * gradient * gradient
    moment_hat = moment_new / (1.0 - beta_first**STEP)
    square_hat = square_new / (1.0 - beta_second**STEP)
    weight_new = weight - step_rate * (
        moment_hat / (jnp.sqrt(square_hat) + adam_epsilon) + decay_factor * weight
    )
    return (weight_new, moment_new, square_new)


def norm_forward(values, gain_row):
    return values * inverse_rms(values) * gain_row


def slot_tables(owner_ids, owners, most_units):
    unit_count = owner_ids.shape[0]
    unit_index = jnp.arange(unit_count, dtype=jnp.int32)
    earlier = (owner_ids[None, :] == owner_ids[:, None]) & (
        unit_index[None, :] < unit_index[:, None]
    )
    unit_rank = jnp.sum(earlier.astype(jnp.int32), 1)
    placed = (owner_ids[None, None, :] == jnp.arange(owners, dtype=jnp.int32)[:, None, None]) & (
        unit_rank[None, None, :] == jnp.arange(most_units, dtype=jnp.int32)[None, :, None]
    )
    slot_filled = jnp.any(placed, 2)
    slot_unit = jnp.sum(jnp.where(placed, unit_index[None, None, :], 0), 2)
    return (unit_rank, slot_unit, slot_filled)


def unit_rates(unit_ids, table_units, query_units, value_units):
    return jnp.where(
        unit_ids < table_units,
        rate_table,
        jnp.where(
            unit_ids < query_units,
            rate_query,
            jnp.where(unit_ids < value_units, rate_values, rate_project),
        ),
    )


def pair_slots(route_pairs, priorities, experts, capacity):
    tokens_here = priorities.shape[0]
    pair_expert = route_pairs.T.reshape(-1)
    pair_key = (
        jnp.arange(2, dtype=jnp.int32)[:, None] * tokens_here + priorities[None, :]
    ).reshape(-1)
    before = (pair_expert[None, :] == pair_expert[:, None]) & (
        pair_key[None, :] < pair_key[:, None]
    )
    pair_rank = jnp.sum(before.astype(jnp.int32), 1)
    pair_kept = pair_rank < capacity
    pair_dest = pair_expert * capacity + jnp.minimum(pair_rank, capacity - 1)
    return (pair_kept, pair_dest)


def gelu_tanh(values):
    return jax.nn.gelu(values, approximate=True)


def gelu_slope(values):
    root = math.sqrt(2.0 / math.pi)
    bent = jnp.tanh(root * (values + 0.044715 * values * values * values))
    return 0.5 * (1.0 + bent) + 0.5 * values * (1.0 - bent * bent) * root * (
        1.0 + 3.0 * 0.044715 * values * values
    )


def plane_peer(step):
    chip, core = lax.axis_index("dp"), lax.axis_index("ctx")
    row = lax.rem(chip // 2 + step // 4, 2)
    column = lax.rem(lax.rem(chip, 2) + lax.rem(step // 2, 2), 2)
    place = {"dp": row * 2 + column, "ctx": lax.rem(core + lax.rem(step, 2), 2)}
    return place, place["dp"] * 2 + place["ctx"]


def greet_plane():
    barrier = pltpu.get_barrier_semaphore()
    for step in range(1, 8):
        place, _ = plane_peer(step)
        pl.semaphore_signal(barrier, inc=1, device_id=place, device_id_type=MESH_ID)
    pl.semaphore_wait(barrier, 7)


def plane_copy(source, target, send_sem, recv_sem, step):
    place, _ = plane_peer(step)
    return pltpu.make_async_remote_copy(
        src_ref=source.at[step],
        dst_ref=target.at[step],
        send_sem=send_sem.at[step],
        recv_sem=recv_sem.at[step],
        device_id=place,
        device_id_type=MESH_ID,
    )


def slot_hits(dest_rows, expert, capacity, tokens):
    slot = lax.broadcasted_iota(jnp.int32, (capacity, tokens), 0) + expert * capacity
    return (slot == dest_rows[0:1, :]) | (slot == dest_rows[1:2, :])


def token_hits(dest_columns, expert, capacity, tokens):
    slot = lax.broadcasted_iota(jnp.int32, (tokens, capacity), 1) + expert * capacity
    hit = (slot == dest_columns[:, 0:1]) | (slot == dest_columns[:, 1:2])
    return jnp.where(hit, 1.0, 0.0).astype(jnp.bfloat16)


def gate_of(routes, gates, expert, axis):
    pick = (lambda a, k: a[k : k + 1, :]) if axis == 0 else (lambda a, k: a[:, k : k + 1])
    return jnp.where(pick(routes, 0) == expert, pick(gates, 0), 0.0) + jnp.where(
        pick(routes, 1) == expert, pick(gates, 1), 0.0
    )


def arrival(i):
    return jnp.where(i < 2, i, 9 - i)


def experts_kernel(
    rows_ref, dest_rows, dest_columns, gates, routes, inner_ref, outer_ref, counts_ref,
    mix_ref, arrived, hidden, returned, totals_ref,
    outgoing, results, counts, send_one, recv_one, send_two, recv_two, send_count, recv_count,
):
    capacity = arrived.shape[1]
    tokens = rows_ref.shape[0]
    greet_plane()
    counts[0] = counts_ref[...]

    def send_counts(step, carry):
        place, _ = plane_peer(step)
        pltpu.make_async_remote_copy(
            src_ref=counts_ref,
            dst_ref=counts.at[step],
            send_sem=send_count.at[step],
            recv_sem=recv_count.at[step],
            device_id=place,
            device_id_type=MESH_ID,
        ).start()
        return carry

    def dispatch(i, carry):
        step = 7 - i
        _, expert = plane_peer(step)
        hit = jnp.where(slot_hits(dest_rows, expert, capacity, tokens), 1.0, 0.0).astype(jnp.bfloat16)
        rows = jnp.dot(hit, rows_ref[...], preferred_element_type=jnp.float32).astype(jnp.bfloat16)

        @pl.when(step > 0)
        def _():
            outgoing[step] = rows
            plane_copy(outgoing, arrived, send_one, recv_one, step).start()

        @pl.when(step == 0)
        def _():
            arrived[0] = rows

        return carry

    def work(i, carry):
        step = arrival(i)

        @pl.when(step > 0)
        def _():
            plane_copy(outgoing, arrived, send_one, recv_one, step).wait_recv()

        before = jnp.dot(arrived[step], inner_ref[...], preferred_element_type=jnp.float32)
        hidden[step] = before
        active = gelu_tanh(before).astype(jnp.bfloat16)
        part = jnp.dot(active, outer_ref[...], preferred_element_type=jnp.float32).astype(jnp.bfloat16)

        @pl.when(step > 0)
        def _():
            results[step] = part
            plane_copy(results, returned, send_two, recv_two, step).start()

        @pl.when(step == 0)
        def _():
            returned[0] = part

        return carry

    def combine(i, carry):
        step = arrival(i)
        _, expert = plane_peer(step)
        hit = token_hits(dest_columns, expert, capacity, tokens)
        gate = gate_of(routes, gates, expert, 1)

        @pl.when(step > 0)
        def _():
            plane_copy(results, returned, send_two, recv_two, step).wait_recv()

        part = gate * jnp.dot(hit, returned[step], preferred_element_type=jnp.float32)

        @pl.when(i == 0)
        def _():
            mix_ref[...] = part

        @pl.when(i > 0)
        def _():
            mix_ref[...] += part

        return carry

    def finish(step, carry):
        plane_copy(outgoing, arrived, send_one, recv_one, step).wait_send()
        plane_copy(results, returned, send_two, recv_two, step).wait_send()
        place, _ = plane_peer(step)
        pltpu.make_async_remote_copy(
            src_ref=counts_ref,
            dst_ref=counts.at[step],
            send_sem=send_count.at[step],
            recv_sem=recv_count.at[step],
            device_id=place,
            device_id_type=MESH_ID,
        ).wait()
        return carry

    lax.fori_loop(0, 8, dispatch, 0)
    lax.fori_loop(1, 8, send_counts, 0)
    lax.fori_loop(0, 8, work, 0)
    lax.fori_loop(0, 8, combine, 0)
    lax.fori_loop(1, 8, finish, 0)
    totals_ref[...] = jnp.sum(counts[...], 0)


def experts_forward(rows, dest, gates, routes, inner, outer, counts, capacity, collective_id):
    tokens, width = rows.shape
    hidden = inner.shape[1]
    buffer = pltpu.VMEM((8, capacity, width), jnp.bfloat16)
    return pl.pallas_call(
        experts_kernel,
        out_shape=[
            jax.ShapeDtypeStruct((tokens, width), jnp.float32),
            jax.ShapeDtypeStruct((8, capacity, width), jnp.bfloat16),
            jax.ShapeDtypeStruct((8, capacity, hidden), jnp.float32),
            jax.ShapeDtypeStruct((8, capacity, width), jnp.bfloat16),
            jax.ShapeDtypeStruct(counts.shape, jnp.float32),
        ],
        in_specs=[whole_vmem] * 8,
        out_specs=[whole_vmem] * 5,
        scratch_shapes=[buffer, buffer, pltpu.VMEM((8,) + counts.shape, jnp.float32)]
        + [pltpu.SemaphoreType.DMA((8,))] * 6,
        compiler_params=pltpu.CompilerParams(
            collective_id=collective_id, has_side_effects=True, vmem_limit_bytes=60 << 20
        ),
    )(rows, dest, dest.T, gates, routes, inner, outer, counts)


def experts_back_kernel(
    rows_ref, dest_rows, dest_columns, gates, routes, returned, arrived, hidden, inner_ref, outer_ref,
    grad_ref, gate_ref, inner_grad, outer_grad,
    outgoing, landed, results, landed_two, active, slopes, send_one, recv_one, send_two, recv_two,
):
    capacity = arrived.shape[1]
    tokens = rows_ref.shape[0]
    greet_plane()
    gate_ref[...] = jnp.zeros_like(gate_ref)

    def dispatch(i, carry):
        step = 7 - i
        _, expert = plane_peer(step)
        hit = slot_hits(dest_rows, expert, capacity, tokens)
        rows = jnp.dot(
            jnp.where(hit, 1.0, 0.0).astype(jnp.bfloat16), rows_ref[...], preferred_element_type=jnp.float32
        )
        scale = jnp.sum(jnp.where(hit, gate_of(routes, gates, expert, 0), 0.0), 1, keepdims=True)
        sent = (rows * scale).astype(jnp.bfloat16)

        @pl.when(step > 0)
        def _():
            outgoing[step] = sent
            plane_copy(outgoing, landed, send_one, recv_one, step).start()

        @pl.when(step == 0)
        def _():
            landed[0] = sent

        dots = jnp.sum(rows * returned[step].astype(jnp.float32), 1, keepdims=True)
        part = jnp.sum(jnp.where(hit, dots, 0.0), 0, keepdims=True)
        for k in range(2):
            gate_ref[k : k + 1, :] += jnp.where(routes[k : k + 1, :] == expert, part, 0.0)
        return carry

    def work(i, carry):
        step = arrival(i)

        @pl.when(step > 0)
        def _():
            plane_copy(outgoing, landed, send_one, recv_one, step).wait_recv()

        grad_active = lax.dot_general(
            landed[step], outer_ref[...], (((1,), (1,)), ((), ())), preferred_element_type=jnp.float32
        )
        before = hidden[step]
        slope = (grad_active * gelu_slope(before)).astype(jnp.bfloat16)
        back = lax.dot_general(
            slope, inner_ref[...], (((1,), (1,)), ((), ())), preferred_element_type=jnp.float32
        ).astype(jnp.bfloat16)

        @pl.when(step > 0)
        def _():
            results[step] = back
            plane_copy(results, landed_two, send_two, recv_two, step).start()

        @pl.when(step == 0)
        def _():
            landed_two[0] = back

        slopes[step] = slope
        active[step] = gelu_tanh(before).astype(jnp.bfloat16)
        return carry

    def weigh(step, carry):
        outer_part = lax.dot_general(
            active[step], landed[step], (((0,), (0,)), ((), ())), preferred_element_type=jnp.float32
        )
        inner_part = lax.dot_general(
            arrived[step], slopes[step], (((0,), (0,)), ((), ())), preferred_element_type=jnp.float32
        )

        @pl.when(step == 0)
        def _():
            outer_grad[...] = outer_part
            inner_grad[...] = inner_part

        @pl.when(step > 0)
        def _():
            outer_grad[...] += outer_part
            inner_grad[...] += inner_part

        return carry

    def combine(i, carry):
        step = arrival(i)
        _, expert = plane_peer(step)
        hit = token_hits(dest_columns, expert, capacity, tokens)

        @pl.when(step > 0)
        def _():
            plane_copy(results, landed_two, send_two, recv_two, step).wait_recv()

        part = jnp.dot(hit, landed_two[step], preferred_element_type=jnp.float32)

        @pl.when(i == 0)
        def _():
            grad_ref[...] = part

        @pl.when(i > 0)
        def _():
            grad_ref[...] += part

        return carry

    def finish(step, carry):
        plane_copy(outgoing, landed, send_one, recv_one, step).wait_send()
        plane_copy(results, landed_two, send_two, recv_two, step).wait_send()
        return carry

    lax.fori_loop(0, 8, dispatch, 0)
    lax.fori_loop(0, 8, work, 0)
    lax.fori_loop(0, 8, weigh, 0)
    lax.fori_loop(0, 8, combine, 0)
    lax.fori_loop(1, 8, finish, 0)


def experts_backward(rows, dest, gates, routes, returned, arrived, hidden, inner, outer, collective_id):
    tokens, width = rows.shape
    capacity = arrived.shape[1]
    inside = inner.shape[1]
    buffer = pltpu.VMEM((8, capacity, width), jnp.bfloat16)
    inside_buffer = pltpu.VMEM((8, capacity, inside), jnp.bfloat16)
    return pl.pallas_call(
        experts_back_kernel,
        out_shape=[
            jax.ShapeDtypeStruct((tokens, width), jnp.float32),
            jax.ShapeDtypeStruct((2, tokens), jnp.float32),
            jax.ShapeDtypeStruct((width, inside), jnp.float32),
            jax.ShapeDtypeStruct((inside, width), jnp.float32),
        ],
        in_specs=[whole_vmem] * 10,
        out_specs=[whole_vmem] * 4,
        scratch_shapes=[buffer] * 4
        + [inside_buffer] * 2
        + [pltpu.SemaphoreType.DMA((8,))] * 4,
        compiler_params=pltpu.CompilerParams(
            collective_id=collective_id, has_side_effects=True, vmem_limit_bytes=63 << 20
        ),
    )(rows, dest, dest.T, gates, routes, returned, arrived, hidden, inner, outer)


def own_units_kernel(
    chunks, parts_ref, small_ref, grads_ref, small_out,
    own, other, relay, landed, small_landed,
    own_sem, other_send, other_recv, relay_send, relay_recv, landed_send, landed_recv, small_send, small_recv,
):
    chip, core = lax.axis_index("dp"), lax.axis_index("ctx")
    beside = chip + 1 - 2 * lax.rem(chip, 2)
    across = lax.rem(chip + 2, 4)
    opposite = across + 1 - 2 * lax.rem(across, 2)
    places = (opposite, beside, across, chip)
    slots = grads_ref.shape[0]
    size = slots // chunks
    split = (chunks + 1) // 2
    greet_plane()

    def span(q):
        return pl.ds(q * size, size)

    def fetch(k):
        first = (places[k] * 2 + core) * slots
        return pltpu.make_async_copy(parts_ref.at[pl.ds(first, slots)], own.at[k], own_sem.at[k])

    def pass_over(k, q):
        first = (places[k] * 2 + 1 - core) * slots + q * size
        return pltpu.make_async_remote_copy(
            src_ref=parts_ref.at[pl.ds(first, size)],
            dst_ref=other.at[k, span(q)],
            send_sem=other_send.at[k, q],
            recv_sem=other_recv.at[k, q],
            device_id={"ctx": 1 - core},
            device_id_type=MESH_ID,
        )

    def to_relay(q, place):
        return pltpu.make_async_remote_copy(
            src_ref=own.at[0, span(q)],
            dst_ref=relay.at[span(q)],
            send_sem=relay_send.at[q],
            recv_sem=relay_recv.at[q],
            device_id={"dp": place},
            device_id_type=MESH_ID,
        )

    def to_owner(k, q):
        return pltpu.make_async_remote_copy(
            src_ref=own.at[k, span(q)],
            dst_ref=landed.at[k - 1, span(q)],
            send_sem=landed_send.at[k - 1, q],
            recv_sem=landed_recv.at[k - 1, q],
            device_id={"dp": places[k]},
            device_id_type=MESH_ID,
        )

    def small_copy(step):
        place, _ = plane_peer(step)
        return pltpu.make_async_remote_copy(
            src_ref=small_ref,
            dst_ref=small_landed.at[chip * 2 + core],
            send_sem=small_send.at[step],
            recv_sem=small_recv.at[step],
            device_id=place,
            device_id_type=MESH_ID,
        )

    for k in range(4):
        fetch(k).start()

        def start(q, carry):
            pass_over(k, q).start()
            return carry

        lax.fori_loop(0, chunks, start, 0)

    def joined(k, q):
        pass_over(k, q).wait_recv()
        return own[k, span(q)].astype(jnp.float32) + other[k, span(q)].astype(jnp.float32)

    fetch(0).wait()

    def first_leg(place):
        def leg(q, carry):
            own[0, span(q)] = joined(0, q).astype(jnp.bfloat16)
            to_relay(q, place).start()
            return carry

        return leg

    lax.fori_loop(0, split, first_leg(beside), 0)
    lax.fori_loop(split, chunks, first_leg(across), 0)
    lax.fori_loop(1, 8, lambda step, carry: (small_copy(step).start(), carry)[1], 0)
    small_landed[chip * 2 + core] = small_ref[...]
    fetch(1).wait()
    fetch(2).wait()

    def direct(k):
        def leg(q, carry):
            own[k, span(q)] = joined(k, q).astype(jnp.bfloat16)
            to_owner(k, q).start()
            return carry

        return leg

    def relayed(k, place):
        def leg(q, carry):
            to_relay(q, place).wait_recv()
            total = joined(k, q) + relay[span(q)].astype(jnp.float32)
            own[k, span(q)] = total.astype(jnp.bfloat16)
            to_owner(k, q).start()
            return carry

        return leg

    lax.fori_loop(0, split, direct(1), 0)
    lax.fori_loop(split, chunks, direct(2), 0)
    lax.fori_loop(0, split, relayed(2, beside), 0)
    lax.fori_loop(split, chunks, relayed(1, across), 0)
    fetch(3).wait()

    def keep(q, carry):
        total = joined(3, q)
        to_owner(1, q).wait_recv()
        to_owner(2, q).wait_recv()
        grads_ref[span(q)] = (
            total + landed[0, span(q)].astype(jnp.float32) + landed[1, span(q)].astype(jnp.float32)
        )
        return carry

    lax.fori_loop(0, split, keep, 0)
    lax.fori_loop(split, chunks, keep, 0)

    def finish(q, carry):
        for k in range(4):
            pass_over(k, q).wait_send()
        to_owner(1, q).wait_send()
        to_owner(2, q).wait_send()
        return carry

    lax.fori_loop(0, chunks, finish, 0)
    lax.fori_loop(0, split, lambda q, carry: (to_relay(q, beside).wait_send(), carry)[1], 0)
    lax.fori_loop(split, chunks, lambda q, carry: (to_relay(q, across).wait_send(), carry)[1], 0)
    lax.fori_loop(1, 8, lambda step, carry: (small_copy(step).wait(), carry)[1], 0)
    total = small_landed[0]
    for source in range(1, 8):
        total = total + small_landed[source]
    small_out[...] = total


def own_units(parts, small, slots, collective_id):
    unit = parts.shape[1:]
    chunks = max(k for k in range(1, 8) if slots % k == 0)
    block = pltpu.VMEM((4, slots) + unit, jnp.bfloat16)
    return pl.pallas_call(
        functools.partial(own_units_kernel, chunks),
        out_shape=[
            jax.ShapeDtypeStruct((slots,) + unit, jnp.float32),
            jax.ShapeDtypeStruct(small.shape, jnp.float32),
        ],
        in_specs=[whole_any, whole_vmem],
        out_specs=[whole_vmem] * 2,
        scratch_shapes=[
            block,
            block,
            pltpu.VMEM((slots,) + unit, jnp.bfloat16),
            pltpu.VMEM((2, slots) + unit, jnp.bfloat16),
            pltpu.VMEM((8,) + small.shape, jnp.float32),
            pltpu.SemaphoreType.DMA((4,)),
            pltpu.SemaphoreType.DMA((4, chunks)),
            pltpu.SemaphoreType.DMA((4, chunks)),
            pltpu.SemaphoreType.DMA((chunks,)),
            pltpu.SemaphoreType.DMA((chunks,)),
            pltpu.SemaphoreType.DMA((2, chunks)),
            pltpu.SemaphoreType.DMA((2, chunks)),
            pltpu.SemaphoreType.DMA((8,)),
            pltpu.SemaphoreType.DMA((8,)),
        ],
        compiler_params=pltpu.CompilerParams(
            collective_id=collective_id, has_side_effects=True, vmem_limit_bytes=56 << 20
        ),
    )(parts, small)


def to_plane(buffer):
    return lax.all_to_all(buffer, ("dp", "ctx"), split_axis=0, concat_axis=0, tiled=True)


def plain_hits(dest, experts, capacity):
    slots = lax.broadcasted_iota(jnp.int32, (experts * capacity, dest.shape[1]), 0)
    return [slots == dest[k : k + 1] for k in range(2)]


def plain_forward(rows, dest, gates, inner, outer, owners, capacity):
    width = rows.shape[1]
    hits = plain_hits(dest, owners, capacity)
    both = (hits[0] | hits[1]).astype(jnp.bfloat16)
    sent = jnp.dot(both, rows, preferred_element_type=jnp.float32).astype(jnp.bfloat16)
    arrived = to_plane(sent.reshape(owners, capacity, width))
    hidden = jnp.einsum("ocd,df->ocf", arrived, inner, preferred_element_type=jnp.float32)
    active = gelu_tanh(hidden).astype(jnp.bfloat16)
    part = jnp.einsum("ocf,fd->ocd", active, outer, preferred_element_type=jnp.float32)
    returned = to_plane(part.astype(jnp.bfloat16))
    flat = returned.reshape(owners * capacity, width)
    mix = sum(
        gates[:, k : k + 1]
        * lax.dot_general(
            hits[k].astype(jnp.bfloat16),
            flat,
            (((0,), (0,)), ((), ())),
            preferred_element_type=jnp.float32,
        )
        for k in range(2)
    )
    return (mix, arrived, hidden, returned)


def plain_backward(rows, dest, gates, returned, arrived, hidden, inner, outer):
    owners, capacity, width = arrived.shape
    hits = plain_hits(dest, owners, capacity)
    both = (hits[0] | hits[1]).astype(jnp.bfloat16)
    slot_scale = jnp.sum(
        jnp.where(hits[0], gates[0:1], 0.0) + jnp.where(hits[1], gates[1:2], 0.0), 1, keepdims=True
    )
    slot_grads = jnp.dot(both, rows, preferred_element_type=jnp.float32)
    sent = (slot_grads * slot_scale).astype(jnp.bfloat16)
    flat = returned.reshape(owners * capacity, width)
    dots = jnp.sum(slot_grads * flat.astype(jnp.float32), 1, keepdims=True)
    gate_part = jnp.concatenate(
        [jnp.sum(jnp.where(hit, dots, 0.0), 0, keepdims=True) for hit in hits], 0
    )
    landed = to_plane(sent.reshape(owners, capacity, width))
    grad_active = jnp.einsum("ocd,fd->ocf", landed, outer, preferred_element_type=jnp.float32)
    active = gelu_tanh(hidden).astype(jnp.bfloat16)
    slope = (grad_active * gelu_slope(hidden)).astype(jnp.bfloat16)
    outer_grad = jnp.einsum("ocf,ocd->fd", active, landed, preferred_element_type=jnp.float32)
    inner_grad = jnp.einsum("ocd,ocf->df", arrived, slope, preferred_element_type=jnp.float32)
    back = jnp.einsum("ocf,df->ocd", slope, inner, preferred_element_type=jnp.float32)
    back = to_plane(back.astype(jnp.bfloat16)).reshape(owners * capacity, width)
    grad = lax.dot_general(
        both, back, (((0,), (0,)), ((), ())), preferred_element_type=jnp.float32
    )
    return (grad, gate_part, inner_grad, outer_grad)


def on_device(
    token_ids,
    targets,
    counted,
    routes,
    priority,
    owner_of,
    master,
    master_first,
    master_second,
    expert_in,
    expert_in_first,
    expert_in_second,
    expert_out,
    expert_out_first,
    expert_out_second,
    norm_gains,
    norm_gains_first,
    norm_gains_second,
    router,
    router_first,
    router_second,
    rel_bias,
    rel_bias_first,
    rel_bias_second,
):
    owners = lax.axis_size(("dp", "ctx"))
    tensor_ranks = lax.axis_size("tensor")
    my_owner = lax.axis_index(("dp", "ctx"))
    my_rank = lax.axis_index("tensor")
    my_context = lax.axis_index("ctx")
    sequences, half_length = token_ids.shape
    tokens_here = sequences * half_length
    most_units = master.shape[2]
    unit_rows = master.shape[3]
    model_width = master.shape[4]
    vocab_here = VOCAB // tensor_ranks
    heads_here = rel_bias.shape[0]
    head_size = model_width // (heads_here * tensor_ranks)
    hidden_here = heads_here * head_size
    experts = router.shape[1]
    capacity = (18 * tokens_here + 8 * experts - 1) // (8 * experts)
    table_units = vocab_here // unit_rows
    query_units = table_units + 2 * hidden_here // unit_rows
    value_units = table_units + 3 * hidden_here // unit_rows
    embed_scale = math.sqrt(model_width)
    owner_ids = owner_of[:, 0]
    unit_rank, slot_unit, slot_filled = slot_tables(owner_ids, owners, most_units)
    on_square = lax.axis_size("dp") == 4 and lax.axis_size("ctx") == 2
    counted_rows = counted.reshape(tokens_here, 2).T.astype(jnp.float32)
    loss_weights = counted_rows * jnp.array([[1.0], [ahead_weight]], jnp.float32)
    counts = jnp.zeros((8, 128), jnp.float32).at[0:2].set(jnp.sum(counted_rows, 1, keepdims=True))
    gathered = lax.all_gather(master[0, 0].astype(jnp.bfloat16), ("dp", "ctx"), axis=0, tiled=True)
    unit_slots = owner_ids * most_units + unit_rank
    weights_low = pull_units(gathered, unit_slots).reshape(-1, model_width)
    joint_low = weights_low[vocab_here : vocab_here + 3 * hidden_here]
    project_low = weights_low[vocab_here + 3 * hidden_here :]
    rolled = [project_low] + [
        lax.ppermute(project_low, "tensor", [(source, (source + step) % 4) for source in range(4)])
        for step in (1, 2, 3)
    ]
    project_full = lax.dynamic_slice_in_dim(
        jnp.concatenate(rolled[::-1] + rolled[::-1], 0), (3 - my_rank) * hidden_here, model_width, 0
    )
    local_ids = token_ids.reshape(-1) - my_rank * vocab_here
    inside = (local_ids >= 0) & (local_ids < vocab_here)
    clipped_ids = jnp.clip(local_ids, 0, vocab_here - 1)
    looked = jnp.where(inside[:, None], jnp.take(weights_low, clipped_ids, axis=0), 0)
    gain_rows = [norm_gains[k : k + 1] for k in range(3)]
    stream_shape = jax.ShapeDtypeStruct((tokens_here, model_width), jnp.float32)
    gain_shape = jax.ShapeDtypeStruct((1, model_width), jnp.float32)
    (embedded,) = sum_line(looked, [], [], keep_total, 1)
    stream_zero = embedded.astype(jnp.float32) * embed_scale
    first_normalized = norm_forward(stream_zero, norm_gains[0])
    normed_one_low = first_normalized.astype(jnp.bfloat16)
    joint = lax.dot_general(
        joint_low, normed_one_low, (((1,), (1,)), ((), ())), preferred_element_type=jnp.float32
    ).astype(jnp.bfloat16)
    pairs_before = passed_along(joint[hidden_here:], "ctx", 1)
    attended, logsum_rows = attention(rel_bias, joint, pairs_before, heads_here, head_size)
    (attended_all,) = gather_line([attended], 2)
    stream_one = stream_zero + lax.dot_general(
        attended_all.reshape(model_width, tokens_here),
        project_full,
        (((0,), (0,)), ((), ())),
        preferred_element_type=jnp.float32,
    )
    second_normalized = norm_forward(stream_one, norm_gains[1])
    normed_two_low = second_normalized.astype(jnp.bfloat16)
    router_low = router.astype(jnp.bfloat16)
    router_scores_raw = jnp.dot(normed_two_low, router_low, preferred_element_type=jnp.float32)
    route_pairs = routes.reshape(tokens_here, 2)
    route_onehot = (route_pairs[:, :, None] == jnp.arange(experts, dtype=jnp.int32)).astype(
        jnp.float32
    )
    chosen = jnp.einsum("tke,te->tk", route_onehot, router_scores_raw, precision=highest_precision)
    gate_values = jax.nn.softmax(chosen, -1)
    pair_kept, pair_dest = pair_slots(route_pairs, priority[0], experts, capacity)
    dest = jnp.where(pair_kept, pair_dest, -1).reshape(2, tokens_here)
    inner_low = expert_in[0].astype(jnp.bfloat16)
    outer_low = expert_out[0].astype(jnp.bfloat16)
    if on_square:
        moe_partial, arrived, hidden_pre, returned, counts = experts_forward(
            normed_two_low, dest, gate_values, route_pairs, inner_low, outer_low, counts, capacity, 8
        )
    else:
        moe_partial, arrived, hidden_pre, returned = plain_forward(
            normed_two_low, dest, gate_values, inner_low, outer_low, owners, capacity
        )
        counts = lax.psum(counts, ("dp", "ctx"))
    weight_total = counts[0, 0] + ahead_weight * counts[1, 0]
    head_low, stream_two = sum_line(
        moe_partial, [stream_one, gain_rows[2]], [stream_shape], finish_mixture, 3
    )
    stats = head_sums(weights_low, head_low, vocab_here)
    logsum_vocab = join_sums(stats, 7)
    local_targets = targets.reshape(tokens_here, 2).T - my_rank * vocab_here
    weight_rows = jnp.concatenate(
        [
            loss_weights,
            loss_weights[0:1] + loss_weights[1:2],
            jnp.broadcast_to(1.0 / weight_total, (1, tokens_here)),
        ],
        0,
    )
    slopes, grad_head, target_sums = head_back(
        weights_low, head_low, logsum_vocab, local_targets, weight_rows, vocab_here
    )
    grad_two_low, grad_two, gain_grad_three = sum_line(
        grad_head,
        [stream_two, gain_rows[2]],
        [stream_shape, gain_shape],
        finish_head_grad,
        4,
        prologue=clear_gain,
    )
    gate_rows = gate_values.T
    if on_square:
        moe_grad_part, gate_part, inner_grad, outer_grad = experts_backward(
            grad_two_low,
            dest,
            gate_rows,
            route_pairs.T,
            returned,
            arrived,
            hidden_pre,
            inner_low,
            outer_low,
            9,
        )
    else:
        moe_grad_part, gate_part, inner_grad, outer_grad = plain_backward(
            grad_two_low, dest, gate_rows, returned, arrived, hidden_pre, inner_low, outer_low
        )
    gate_part = jnp.concatenate([gate_part, target_sums, jnp.zeros_like(target_sums)], 0)
    gate_block = pltpu.VMEM((3, 4, tokens_here), jnp.float32)
    grad_one_low, grad_one, logit_grad, target_total, gain_grad_two = sum_line(
        moe_grad_part,
        [
            stream_one,
            gain_rows[1],
            grad_two,
            gate_part,
            gate_rows,
            route_pairs.T,
            router_low,
        ],
        [
            stream_shape,
            jax.ShapeDtypeStruct((experts, tokens_here), jnp.bfloat16),
            jax.ShapeDtypeStruct((1, tokens_here), jnp.float32),
            gain_shape,
        ],
        finish_expert_grad,
        5,
        prologue=start_router_grad,
        scratch=(gate_block, pltpu.SemaphoreType.DMA((3,)), pltpu.SemaphoreType.DMA((3,))),
        meets_all=True,
    )
    router_grad = jnp.dot(logit_grad, normed_two_low, preferred_element_type=jnp.float32)
    loss_local = jnp.sum(weight_rows[2:3] * logsum_vocab) - jnp.sum(target_total)
    query_grad, pair_grad, before_grad, bias_lines = attention_back(
        rel_bias,
        joint,
        pairs_before,
        logsum_rows,
        grad_one_low,
        project_low,
        heads_here,
        head_size,
    )
    grad_after = passed_along(before_grad, "ctx", -1)
    pair_grad_low = (pair_grad + grad_after.astype(jnp.float32)).astype(jnp.bfloat16)
    joint_grad = jnp.concatenate([query_grad, pair_grad_low], 0)
    distances = 2 * (half_length // BLOCK)
    bias_grad = jnp.sum(bias_lines, 1).reshape(heads_here, distances)
    zero_grad_low, gain_grads = sum_line(
        lax.dot_general(
            joint_grad, joint_low, (((0,), (0,)), ((), ())), preferred_element_type=jnp.float32
        ),
        [embedded, gain_rows[0], grad_one, gain_grad_two, gain_grad_three],
        [jax.ShapeDtypeStruct((8, model_width), jnp.float32)],
        functools.partial(finish_input_grad, embed_scale),
        6,
        prologue=clear_gain,
        scratch=(pltpu.SemaphoreType.DMA, pltpu.SemaphoreType.DMA),
        ending=share_gains,
    )
    my_units = jnp.take(slot_unit, my_owner, axis=0)
    my_filled = jnp.take(slot_filled, my_owner, axis=0)[:, None, None]
    outgoing = weight_grads(
        unit_slots,
        owners * most_units,
        unit_rows,
        slopes,
        head_low,
        local_ids[None, :],
        zero_grad_low,
        joint_grad,
        normed_one_low,
        attended,
        grad_one_low,
    )
    bias_row = jnp.concatenate([bias_grad.reshape(-1), loss_local[None]])
    bias_row = jnp.pad(bias_row, (0, model_width - bias_row.shape[0]))[None]
    small = jnp.concatenate([gain_grads[:3], router_grad, bias_row], 0)
    small = jnp.pad(small, ((0, -small.shape[0] % 8), (0, 0)))
    if on_square:
        mine, small = own_units(outgoing, small, most_units, 10)
    else:
        mine = lax.psum_scatter(
            outgoing.astype(jnp.float32), ("dp", "ctx"), scatter_dimension=0, tiled=True
        )
        small = lax.psum(small, ("dp", "ctx"))
    mine = jnp.where(my_filled, mine, 0.0)
    gains_grad = small[:3]
    router_grad = small[3 : 3 + experts].T
    bias_grad = small[3 + experts, : rel_bias.size].reshape(rel_bias.shape)
    loss_totals = jnp.stack([small[3 + experts, rel_bias.size], weight_total])
    slot_rates = unit_rates(my_units, table_units, query_units, value_units)[:, None, None]
    master_new, master_first_new, master_second_new = adam_update(
        master[0, 0], master_first[0, 0], master_second[0, 0], mine, slot_rates, decay_rate
    )
    inner_new, inner_first_new, inner_second_new = adam_update(
        expert_in, expert_in_first, expert_in_second, inner_grad[None], rate_inner, decay_rate
    )
    outer_new, outer_first_new, outer_second_new = adam_update(
        expert_out, expert_out_first, expert_out_second, outer_grad[None], rate_outer, decay_rate
    )
    gains_new, gains_first_new, gains_second_new = adam_update(
        norm_gains, norm_gains_first, norm_gains_second, gains_grad, rate_gains, 0.0
    )
    router_new, router_first_new, router_second_new = adam_update(
        router, router_first, router_second, router_grad, rate_router, decay_rate
    )
    biases_new, biases_first_new, biases_second_new = adam_update(
        rel_bias, rel_bias_first, rel_bias_second, bias_grad, rate_biases, 0.0
    )
    return (
        loss_totals,
        master_new[None, None],
        master_first_new[None, None],
        master_second_new[None, None],
        inner_new,
        inner_first_new,
        inner_second_new,
        outer_new,
        outer_first_new,
        outer_second_new,
        gains_new,
        gains_first_new,
        gains_second_new,
        router_new,
        router_first_new,
        router_second_new,
        biases_new,
        biases_first_new,
        biases_second_new,
    )


def solution(mesh):
    in_specs = (
        P("dp", "ctx"),
        P("dp", "ctx", None),
        P("dp", "ctx", None),
        P("dp", "ctx", None),
        P(("dp", "ctx"), None),
        P(),
        P("tensor", ("dp", "ctx"), None, None, None),
        P("tensor", ("dp", "ctx"), None, None, None),
        P("tensor", ("dp", "ctx"), None, None, None),
        P(("dp", "ctx"), None, "tensor"),
        P(("dp", "ctx"), None, "tensor"),
        P(("dp", "ctx"), None, "tensor"),
        P(("dp", "ctx"), "tensor", None),
        P(("dp", "ctx"), "tensor", None),
        P(("dp", "ctx"), "tensor", None),
        P(),
        P(),
        P(),
        P(),
        P(),
        P(),
        P("tensor", None),
        P("tensor", None),
        P("tensor", None),
    )
    out_specs = (
        P(),
        P("tensor", ("dp", "ctx"), None, None, None),
        P("tensor", ("dp", "ctx"), None, None, None),
        P("tensor", ("dp", "ctx"), None, None, None),
        P(("dp", "ctx"), None, "tensor"),
        P(("dp", "ctx"), None, "tensor"),
        P(("dp", "ctx"), None, "tensor"),
        P(("dp", "ctx"), "tensor", None),
        P(("dp", "ctx"), "tensor", None),
        P(("dp", "ctx"), "tensor", None),
        P(),
        P(),
        P(),
        P(),
        P(),
        P(),
        P("tensor", None),
        P("tensor", None),
        P("tensor", None),
    )
    return jax.shard_map(
        on_device, mesh=mesh, in_specs=in_specs, out_specs=out_specs, check_vma=False
    )
```

```python
import functools
import math

import jax
import jax.numpy as jnp
from jax import lax
from jax.experimental import pallas as pl
from jax.experimental.pallas import tpu as pltpu
from jax.sharding import PartitionSpec as P

VOCAB = 32000
BLOCK = 256
STEP = 10


highest_precision = lax.Precision.HIGHEST
beta_first = 0.9
beta_second = 0.95
adam_epsilon = 1e-08
norm_epsilon = 1e-06
ahead_weight = 0.3
masked_score = -1e30
rate_table = 0.1
rate_query = 0.05
rate_values = 0.05
rate_project = 0.5
rate_inner = 0.05
rate_outer = 0.03
rate_gains = 0.5
rate_router = 0.05
rate_biases = 0.5
decay_rate = 0.1
column_parts = 3


def passed_along(value, axis, steps):
    count = lax.axis_size(axis)
    initial, last = (max(0, -steps), min(count, count - steps))
    return lax.ppermute(value, axis, [(source, source + steps) for source in range(initial, last)])

MESH_ID = pl.DeviceIdType.MESH
whole_vmem = pl.BlockSpec(memory_space=pltpu.VMEM)
whole_any = pl.BlockSpec(memory_space=pl.ANY)
line_lag = 2


def sum_line_kernel(
    rows, count, opening, prologue, epilogue, ending, n_extra, n_aux, n_scratch, part_ref, *refs
):
    extras = refs[:n_extra]
    out_ref = refs[n_extra]
    aux = refs[n_extra + 1 : n_extra + 1 + n_aux]
    rest = refs[n_extra + 1 + n_aux :]
    scratch = rest[:n_scratch]
    stage, from_end, from_mid, send_sem, end_sem, mid_sem, back_sem, back_recv = rest[n_scratch:]
    rank = lax.axis_index("tensor")
    inner = (rank == 1) | (rank == 2)
    end_peer = jnp.where(rank < 2, 1 - rank, 5 - rank)
    mid_peer = 3 - rank
    barrier = pltpu.get_barrier_semaphore()
    if opening is None:
        pl.semaphore_signal(barrier, inc=1, device_id={"tensor": end_peer}, device_id_type=MESH_ID)

        @pl.when(inner)
        def _():
            pl.semaphore_signal(
                barrier, inc=1, device_id={"tensor": mid_peer}, device_id_type=MESH_ID
            )
            pl.semaphore_wait(barrier, 2)

        @pl.when(jnp.logical_not(inner))
        def _():
            pl.semaphore_wait(barrier, 1)
    else:
        for step in (1, 2, 3):
            other = lax.rem(rank + step, 4)
            pl.semaphore_signal(barrier, inc=1, device_id={"tensor": other}, device_id_type=MESH_ID)
        pl.semaphore_wait(barrier, 3)

    def span(i):
        return pl.ds(pl.multiple_of(i * rows, rows), rows)

    def to_inner(i):
        return pltpu.make_async_remote_copy(
            src_ref=stage.at[i],
            dst_ref=from_end.at[i],
            send_sem=send_sem.at[i],
            recv_sem=end_sem.at[i],
            device_id={"tensor": end_peer},
            device_id_type=MESH_ID,
        )

    def to_middle(i):
        return pltpu.make_async_remote_copy(
            src_ref=stage.at[i],
            dst_ref=from_mid.at[i],
            send_sem=send_sem.at[i],
            recv_sem=mid_sem.at[i],
            device_id={"tensor": mid_peer},
            device_id_type=MESH_ID,
        )

    def to_end(i):
        return pltpu.make_async_remote_copy(
            src_ref=out_ref.at[span(i)],
            dst_ref=out_ref.at[span(i)],
            send_sem=back_sem.at[i],
            recv_sem=back_recv.at[i],
            device_id={"tensor": end_peer},
            device_id_type=MESH_ID,
        )

    if opening is not None:
        opening(rank, extras, scratch)

    @pl.when(jnp.logical_not(inner))
    def _():
        def push(i, carry):
            stage[i] = part_ref[span(i)].astype(jnp.bfloat16)
            to_inner(i).start()
            return carry

        lax.fori_loop(0, count, push, 0)

    if prologue is not None:
        prologue(rank, inner, extras, aux, scratch)

    @pl.when(inner)
    def _():
        def step(i, carry):
            @pl.when(i < count)
            def _():
                to_inner(i).wait_recv()
                mine = part_ref[span(i)].astype(jnp.float32) + from_end[i].astype(jnp.float32)
                stage[i] = mine.astype(jnp.bfloat16)
                to_middle(i).start()

            @pl.when(i >= line_lag)
            def _():
                j = i - line_lag
                to_middle(j).wait_recv()
                total = stage[j].astype(jnp.float32) + from_mid[j].astype(jnp.float32)
                out_ref[span(j)] = epilogue(total, span(j), rank, extras, aux, scratch)
                to_end(j).start()

            return carry

        lax.fori_loop(0, count + line_lag, step, 0)

        def drain(i, carry):
            to_middle(i).wait_send()
            to_end(i).wait_send()
            return carry

        lax.fori_loop(0, count, drain, 0)

    @pl.when(jnp.logical_not(inner))
    def _():
        def finish(i, carry):
            to_end(i).wait_recv()
            to_inner(i).wait_send()
            return carry

        lax.fori_loop(0, count, finish, 0)

    if ending is not None:
        ending(inner, end_peer, extras, aux, scratch)


def sum_line(
    part,
    extras,
    aux_shapes,
    epilogue,
    collective_id,
    prologue=None,
    scratch=(),
    opening=None,
    ending=None,
    rows=64,
):
    tokens, width = part.shape
    count = tokens // rows
    chunks = pltpu.VMEM((count, rows, width), jnp.bfloat16)
    return pl.pallas_call(
        functools.partial(
            sum_line_kernel,
            rows,
            count,
            opening,
            prologue,
            epilogue,
            ending,
            len(extras),
            len(aux_shapes),
            len(scratch),
        ),
        out_shape=[jax.ShapeDtypeStruct((tokens, width), jnp.bfloat16)] + list(aux_shapes),
        in_specs=[whole_vmem] * (1 + len(extras)),
        out_specs=[whole_vmem] * (1 + len(aux_shapes)),
        scratch_shapes=list(scratch)
        + [chunks, chunks, chunks]
        + [pltpu.SemaphoreType.DMA((count,))] * 5,
        compiler_params=pltpu.CompilerParams(
            collective_id=collective_id, has_side_effects=True, vmem_limit_bytes=48 << 20
        ),
    )(part, *extras)


def keep_total(total, span, rank, extras, aux, scratch):
    return total.astype(jnp.bfloat16)


def inverse_rms(values):
    return lax.rsqrt(jnp.mean(values * values, -1, keepdims=True) + norm_epsilon)


def finish_mixture(total, span, rank, extras, aux, scratch):
    stream_one, gain = extras
    stream_two = stream_one[span] + total
    aux[0][span] = stream_two
    return (stream_two * inverse_rms(stream_two) * gain[...]).astype(jnp.bfloat16)


def norm_back_rows(values, gain, upstream):
    inverse = inverse_rms(values)
    normed = values * inverse
    scaled = upstream * gain
    gain_grad = jnp.sum(upstream * normed, 0, keepdims=True)
    inputs_grad = inverse * (scaled - normed * jnp.mean(scaled * normed, -1, keepdims=True))
    return (inputs_grad, gain_grad)


def clear_gain(rank, inner, extras, aux, scratch):
    @pl.when(inner)
    def _():
        aux[-1][...] = jnp.zeros_like(aux[-1])


def share_gains(inner, end_peer, extras, aux, scratch):
    gains = aux[0]
    copy = pltpu.make_async_remote_copy(
        src_ref=gains,
        dst_ref=gains,
        send_sem=scratch[0],
        recv_sem=scratch[1],
        device_id={"tensor": end_peer},
        device_id_type=MESH_ID,
    )

    @pl.when(inner)
    def _():
        gains[1:2, :] = extras[3][...]
        gains[2:3, :] = extras[4][...]
        copy.start()
        copy.wait_send()

    @pl.when(jnp.logical_not(inner))
    def _():
        copy.wait_recv()


def finish_head_grad(total, span, rank, extras, aux, scratch):
    stream_two, gain = extras
    grad_two, gain_grad = norm_back_rows(stream_two[span], gain[...], total)
    aux[0][span] = grad_two
    aux[1][...] += gain_grad
    return grad_two.astype(jnp.bfloat16)


def gate_copies(rank, extras, scratch):
    gate_part = extras[3]
    landed, gate_send, gate_recv = scratch
    return [
        pltpu.make_async_remote_copy(
            src_ref=gate_part,
            dst_ref=landed.at[step - 1],
            send_sem=gate_send.at[step - 1],
            recv_sem=gate_recv.at[step - 1],
            device_id={"tensor": lax.rem(rank + step, 4)},
            device_id_type=MESH_ID,
        )
        for step in (1, 2, 3)
    ]


def send_gate_parts(rank, extras, scratch):
    for copy in gate_copies(rank, extras, scratch):
        copy.start()


def start_router_grad(rank, inner, extras, aux, scratch):
    stream_one, gain, grad_two, gate_part, gates, routes, router_low = extras
    grad_one, logit_grad, target_total, gain_grad = aux
    landed = scratch[0]
    clear_gain(rank, inner, extras, aux, scratch)
    for copy in gate_copies(rank, extras, scratch):
        copy.wait()
    gate_grad = jnp.zeros(gate_part.shape, jnp.float32)
    for source in range(4):
        piece = jnp.zeros(gate_part.shape, jnp.float32)
        for step in (1, 2, 3):
            piece = jnp.where(lax.rem(source + step, 4) == rank, landed[step - 1], piece)
        gate_grad = gate_grad + jnp.where(rank == source, gate_part[...], piece)
    target_total[...] = gate_grad[2:3]
    gate_grad = gate_grad[0:2]
    weighted = gates[...] * gate_grad
    chosen = gates[...] * (gate_grad - (weighted[0:1] + weighted[1:2]))
    experts, tokens = logit_grad.shape
    row = lax.broadcasted_iota(jnp.int32, (experts, tokens), 0)
    placed = jnp.where(row == routes[0:1], chosen[0:1], 0.0) + jnp.where(
        row == routes[1:2], chosen[1:2], 0.0
    )
    logit_grad[...] = placed.astype(jnp.bfloat16)

    @pl.when(inner)
    def _():
        grad_one[...] = lax.dot_general(
            logit_grad[...],
            router_low[...],
            (((0,), (1,)), ((), ())),
            preferred_element_type=jnp.float32,
        )


def finish_expert_grad(total, span, rank, extras, aux, scratch):
    stream_one, gain, grad_two, gate_part, gates, routes, router_low = extras
    grad_one, logit_grad, target_total, gain_grad = aux
    part, gain_part = norm_back_rows(
        stream_one[span], gain[...], total + grad_one[span]
    )
    result = grad_two[span] + part
    grad_one[span] = result
    gain_grad[...] += gain_part
    return result.astype(jnp.bfloat16)


def finish_input_grad(scale, total, span, rank, extras, aux, scratch):
    embedded, gain, grad_one = extras[:3]
    stream_zero = embedded[span].astype(jnp.float32) * scale
    part, gain_part = norm_back_rows(stream_zero, gain[...], total)
    aux[0][0:1, :] += gain_part
    return ((grad_one[span] + part) * scale).astype(jnp.bfloat16)


def gather_line_kernel(count, *refs):
    ins = refs[:count]
    outs = refs[count : 2 * count]
    local_sem, send_sem, recv_sem = refs[2 * count :]
    rank = lax.axis_index("tensor")
    barrier = pltpu.get_barrier_semaphore()
    for step in (1, 2, 3):
        other = lax.rem(rank + step, 4)
        pl.semaphore_signal(barrier, inc=1, device_id={"tensor": other}, device_id_type=MESH_ID)
    pl.semaphore_wait(barrier, 3)
    copies = []
    for k in range(count):
        for step in (1, 2, 3):
            copy = pltpu.make_async_remote_copy(
                src_ref=ins[k],
                dst_ref=outs[k].at[rank],
                send_sem=send_sem.at[k, step - 1],
                recv_sem=recv_sem.at[k, step - 1],
                device_id={"tensor": lax.rem(rank + step, 4)},
                device_id_type=MESH_ID,
            )
            copy.start()
            copies.append(copy)
        own = pltpu.make_async_copy(ins[k], outs[k].at[rank], local_sem.at[k])
        own.start()
        own.wait()
    for copy in copies:
        copy.wait()


def gather_line(arrays, collective_id):
    count = len(arrays)
    return pl.pallas_call(
        functools.partial(gather_line_kernel, count),
        out_shape=[jax.ShapeDtypeStruct((4,) + x.shape, x.dtype) for x in arrays],
        in_specs=[whole_vmem] * count,
        out_specs=[whole_vmem] * count,
        scratch_shapes=[
            pltpu.SemaphoreType.DMA((count,)),
            pltpu.SemaphoreType.DMA((count, 3)),
            pltpu.SemaphoreType.DMA((count, 3)),
        ],
        compiler_params=pltpu.CompilerParams(
            collective_id=collective_id, has_side_effects=True, vmem_limit_bytes=40 << 20
        ),
    )(*arrays)


def pull_units_kernel(parts, slots_ref, *refs):
    sources, out_ref, sem = refs[:parts], refs[parts], refs[parts + 1]
    width = out_ref.shape[-1] // parts

    def push(u, carry):
        for part in range(parts):
            pltpu.make_async_copy(
                sources[part].at[slots_ref[u]],
                out_ref.at[u, :, part * width : (part + 1) * width],
                sem,
            ).start()
        return carry

    lax.fori_loop(0, out_ref.shape[0], push, 0)
    pltpu.make_async_copy(out_ref, out_ref, sem).wait()


def pull_units(sources, slots):
    count = slots.shape[0]
    rows, width = sources[0].shape[1:]
    return pl.pallas_call(
        functools.partial(pull_units_kernel, len(sources)),
        out_shape=jax.ShapeDtypeStruct((count, rows, width * len(sources)), sources[0].dtype),
        in_specs=[pl.BlockSpec(memory_space=pltpu.SMEM)] + [whole_any] * len(sources),
        out_specs=whole_vmem,
        scratch_shapes=[pltpu.SemaphoreType.DMA],
        compiler_params=pltpu.CompilerParams(vmem_limit_bytes=40 << 20),
    )(slots, *sources)


def attention_kernel(heads, size, bias_ref, own_ref, before_ref, out_ref, logsum_ref, scores, peak, total):
    tokens = own_ref.shape[1]
    blocks = tokens // BLOCK
    hidden = heads * size
    later = lax.axis_index("ctx") > 0

    for head in range(heads):
        query = own_ref[head * size : (head + 1) * size, :].astype(jnp.float32).T * size**-0.5
        query = query.astype(jnp.bfloat16)
        own_keys = own_ref[hidden + head * size : hidden + (head + 1) * size, :]
        old_keys = before_ref[head * size : (head + 1) * size, :]
        own_values = own_ref[2 * hidden + head * size : 2 * hidden + (head + 1) * size, :]
        own_values = own_values.astype(jnp.float32).T.astype(jnp.bfloat16)
        old_values = before_ref[hidden + head * size : hidden + (head + 1) * size, :]
        old_values = old_values.astype(jnp.float32).T.astype(jnp.bfloat16)
        for block in range(blocks):
            rows = query[block * BLOCK : (block + 1) * BLOCK]
            width = (block + 1) * BLOCK
            mine = jnp.dot(rows, own_keys[:, :width], preferred_element_type=jnp.float32)
            top = None
            parts = []
            for k in range(block + 1):
                part = mine[:, k * BLOCK : (k + 1) * BLOCK] + bias_ref[head, block - k]
                parts.append(part)
                high = jnp.max(part, 1, keepdims=True)
                top = high if top is None else jnp.maximum(top, high)
            peak[...] = top

            @pl.when(later)
            def _():
                old = jnp.dot(rows, old_keys, preferred_element_type=jnp.float32)
                top_old = None
                for k in range(blocks):
                    part = old[:, k * BLOCK : (k + 1) * BLOCK] + bias_ref[head, block + blocks - k]
                    scores[:, k * BLOCK : (k + 1) * BLOCK] = part
                    high = jnp.max(part, 1, keepdims=True)
                    top_old = high if top_old is None else jnp.maximum(top_old, high)
                peak[...] = jnp.maximum(peak[...], top_old)

            top = peak[...]
            parts = [jnp.exp(part - top) for part in parts]
            own_sum = None
            for part in parts:
                part_sum = jnp.sum(part, 1, keepdims=True)
                own_sum = part_sum if own_sum is None else own_sum + part_sum
            total[...] = own_sum

            @pl.when(later)
            def _():
                old_exp = jnp.exp(scores[...] - top)
                scores[...] = old_exp
                total[...] += jnp.sum(old_exp, 1, keepdims=True)

            full = total[...]
            inverse = 1.0 / full
            low = jnp.concatenate([(part * inverse).astype(jnp.bfloat16) for part in parts], 1)
            result = jnp.dot(low, own_values[:width], preferred_element_type=jnp.float32)
            peak[...] = top + jnp.log(full)
            logsum_ref[head, block * BLOCK : (block + 1) * BLOCK, :] = peak[...]
            place = (slice(head * size, (head + 1) * size), slice(block * BLOCK, (block + 1) * BLOCK))

            @pl.when(later)
            def _():
                low_old = (scores[...] * inverse).astype(jnp.bfloat16)
                both = result + jnp.dot(low_old, old_values, preferred_element_type=jnp.float32)
                out_ref[place] = both.T.astype(jnp.bfloat16)

            @pl.when(jnp.logical_not(later))
            def _():
                out_ref[place] = result.T.astype(jnp.bfloat16)


def attention(biases, own, before, heads, size):
    tokens = own.shape[1]
    return pl.pallas_call(
        functools.partial(attention_kernel, heads, size),
        out_shape=[
            jax.ShapeDtypeStruct((heads * size, tokens), jnp.bfloat16),
            jax.ShapeDtypeStruct((heads, tokens, 1), jnp.float32),
        ],
        in_specs=[pl.BlockSpec(memory_space=pltpu.SMEM), whole_vmem, whole_vmem],
        out_specs=[whole_vmem, whole_vmem],
        scratch_shapes=[
            pltpu.VMEM((BLOCK, tokens), jnp.float32),
            pltpu.VMEM((BLOCK, 1), jnp.float32),
            pltpu.VMEM((BLOCK, 1), jnp.float32),
        ],
        compiler_params=pltpu.CompilerParams(vmem_limit_bytes=40 << 20),
    )(biases, own, before)


def attention_back_kernel(
    heads, size, bias_ref, own_ref, before_ref, logsum_ref, grad_ref, project_ref,
    query_out, own_out, before_out, bias_out, probs, slopes, inner, query_sum, own_sum, before_sum,
):
    tokens = own_ref.shape[1]
    blocks = tokens // BLOCK
    hidden = heads * size
    later = lax.axis_index("ctx") > 0
    bias_out[...] = jnp.zeros_like(bias_out)

    def flipped(rows):
        return rows.astype(jnp.float32).T.astype(jnp.bfloat16)

    for head in range(heads):
        span = slice(head * size, (head + 1) * size)
        value_span = slice(hidden + head * size, hidden + (head + 1) * size)
        query_rows = own_ref[span, :]
        query = flipped(query_rows) * jnp.bfloat16(size**-0.5)
        own_keys = own_ref[hidden + head * size : hidden + (head + 1) * size, :]
        own_values = own_ref[2 * hidden + head * size : 2 * hidden + (head + 1) * size, :]
        old_keys = before_ref[span, :]
        old_values = before_ref[value_span, :]
        own_keys_flip = flipped(own_keys)
        grad = lax.dot_general(
            grad_ref[...], project_ref[span, :], (((1,), (1,)), ((), ())), preferred_element_type=jnp.float32
        )
        grad_rows = grad.T.astype(jnp.bfloat16)
        grad = grad.astype(jnp.bfloat16)
        own_sum[...] = jnp.zeros_like(own_sum)

        @pl.when(later)
        def _():
            before_sum[...] = jnp.zeros_like(before_sum)

        for block in range(blocks):
            at = slice(block * BLOCK, (block + 1) * BLOCK)
            width = (block + 1) * BLOCK
            rows, up = query[at], grad[at]
            lse = logsum_ref[head, at, :]
            score = jnp.dot(rows, own_keys[:, :width], preferred_element_type=jnp.float32)
            prob = jnp.concatenate(
                [
                    jnp.exp(score[:, k * BLOCK : (k + 1) * BLOCK] + (bias_ref[head, block - k] - lse))
                    for k in range(block + 1)
                ],
                1,
            )
            slope = jnp.dot(up, own_values[:, :width], preferred_element_type=jnp.float32)
            inner[...] = jnp.sum(prob * slope, 1, keepdims=True)

            @pl.when(later)
            def _():
                score = jnp.dot(rows, old_keys, preferred_element_type=jnp.float32)
                old_slope = jnp.dot(up, old_values, preferred_element_type=jnp.float32)
                old_prob = jnp.concatenate(
                    [
                        jnp.exp(
                            score[:, k * BLOCK : (k + 1) * BLOCK]
                            + (bias_ref[head, block + blocks - k] - lse)
                        )
                        for k in range(blocks)
                    ],
                    1,
                )
                probs[...] = old_prob
                slopes[...] = old_slope
                inner[...] += jnp.sum(old_prob * old_slope, 1, keepdims=True)

            row_inner = inner[...]
            low_grad = (prob * (slope - row_inner)).astype(jnp.bfloat16)
            query_sum[...] = jnp.dot(
                low_grad, own_keys_flip[:width], preferred_element_type=jnp.float32
            )
            own_sum[:size, :width] += jnp.dot(
                query_rows[:, at], low_grad, preferred_element_type=jnp.float32
            )
            own_sum[size:, :width] += jnp.dot(
                grad_rows[:, at], prob.astype(jnp.bfloat16), preferred_element_type=jnp.float32
            )
            for k in range(block + 1):
                line = head * 2 * blocks + block - k
                bias_out[line : line + 1, :] += jnp.sum(
                    low_grad[:, k * BLOCK : (k + 1) * BLOCK].astype(jnp.float32), 0, keepdims=True
                )

            @pl.when(later)
            def _():
                old_prob = probs[...]
                low_old = (old_prob * (slopes[...] - row_inner)).astype(jnp.bfloat16)
                query_sum[...] += jnp.dot(
                    low_old, flipped(old_keys), preferred_element_type=jnp.float32
                )
                before_sum[:size, :] += jnp.dot(
                    query_rows[:, at], low_old, preferred_element_type=jnp.float32
                )
                before_sum[size:, :] += jnp.dot(
                    grad_rows[:, at], old_prob.astype(jnp.bfloat16), preferred_element_type=jnp.float32
                )
                for k in range(blocks):
                    line = head * 2 * blocks + block + blocks - k
                    bias_out[line : line + 1, :] += jnp.sum(
                        low_old[:, k * BLOCK : (k + 1) * BLOCK].astype(jnp.float32), 0, keepdims=True
                    )

            query_out[span, at] = (query_sum[...].T * size**-0.5).astype(jnp.bfloat16)

        own_out[span, :] = own_sum[:size, :] * size**-0.5
        own_out[value_span, :] = own_sum[size:, :]

        @pl.when(later)
        def _():
            before_out[span, :] = (before_sum[:size, :] * size**-0.5).astype(jnp.bfloat16)
            before_out[value_span, :] = before_sum[size:, :].astype(jnp.bfloat16)

    @pl.when(jnp.logical_not(later))
    def _():
        before_out[...] = jnp.zeros_like(before_out)


def attention_back(biases, own, before, logsum, grad, project, heads, size):
    tokens = own.shape[1]
    hidden = heads * size
    return pl.pallas_call(
        functools.partial(attention_back_kernel, heads, size),
        out_shape=[
            jax.ShapeDtypeStruct((hidden, tokens), jnp.bfloat16),
            jax.ShapeDtypeStruct((2 * hidden, tokens), jnp.float32),
            jax.ShapeDtypeStruct((2 * hidden, tokens), jnp.bfloat16),
            jax.ShapeDtypeStruct((heads * 2 * (tokens // BLOCK), BLOCK), jnp.float32),
        ],
        in_specs=[pl.BlockSpec(memory_space=pltpu.SMEM)] + [whole_vmem] * 5,
        out_specs=[whole_vmem] * 4,
        scratch_shapes=[
            pltpu.VMEM((BLOCK, tokens), jnp.float32),
            pltpu.VMEM((BLOCK, tokens), jnp.float32),
            pltpu.VMEM((BLOCK, 1), jnp.float32),
            pltpu.VMEM((BLOCK, size), jnp.float32),
            pltpu.VMEM((2 * size, tokens), jnp.float32),
            pltpu.VMEM((2 * size, tokens), jnp.float32),
        ],
        compiler_params=pltpu.CompilerParams(vmem_limit_bytes=48 << 20),
    )(biases, own, before, logsum, grad, project)


def head_sums_kernel(table_ref, rows_ref, stats_ref, turned):
    @pl.when(pl.program_id(0) == 0)
    def _():
        turned[...] = rows_ref[...].astype(jnp.float32).T.astype(jnp.bfloat16)
        stats_ref[0:1, :] = jnp.full_like(stats_ref[0:1, :], masked_score)
        stats_ref[1:2, :] = jnp.zeros_like(stats_ref[1:2, :])

    logits = jnp.dot(table_ref[...], turned[...], preferred_element_type=jnp.float32)
    before = stats_ref[0:1, :]
    top = jnp.maximum(before, jnp.max(logits, 0, keepdims=True))
    stats_ref[1:2, :] = stats_ref[1:2, :] * jnp.exp(before - top) + jnp.sum(
        jnp.exp(logits - top), 0, keepdims=True
    )
    stats_ref[0:1, :] = top


def vocab_tile(vocab):
    return max(k for k in range(16, 1601, 16) if vocab % k == 0)


def head_sums(weights, rows, vocab):
    tokens, width = rows.shape
    tile = vocab_tile(vocab)
    return pl.pallas_call(
        head_sums_kernel,
        grid=(vocab // tile,),
        out_shape=jax.ShapeDtypeStruct((2, tokens), jnp.float32),
        in_specs=[pl.BlockSpec((tile, width), lambda k: (k, 0)), pl.BlockSpec((tokens, width), lambda k: (0, 0))],
        out_specs=pl.BlockSpec((2, tokens), lambda k: (0, 0)),
        scratch_shapes=[pltpu.VMEM((width, tokens), jnp.bfloat16)],
        compiler_params=pltpu.CompilerParams(vmem_limit_bytes=56 << 20),
    )(weights, rows)


def join_sums_kernel(stats_ref, logsum_ref, landed, send_sem, recv_sem):
    rank = lax.axis_index("tensor")
    barrier = pltpu.get_barrier_semaphore()
    for step in (1, 2, 3):
        other = lax.rem(rank + step, 4)
        pl.semaphore_signal(barrier, inc=1, device_id={"tensor": other}, device_id_type=MESH_ID)
    pl.semaphore_wait(barrier, 3)
    copies = []
    for step in (1, 2, 3):
        copy = pltpu.make_async_remote_copy(
            src_ref=stats_ref,
            dst_ref=landed.at[step - 1],
            send_sem=send_sem.at[step - 1],
            recv_sem=recv_sem.at[step - 1],
            device_id={"tensor": lax.rem(rank + step, 4)},
            device_id_type=MESH_ID,
        )
        copy.start()
        copies.append(copy)
    for copy in copies:
        copy.wait()
    tops, sums = [], []
    for source in range(4):
        piece = stats_ref[...]
        for step in (1, 2, 3):
            piece = jnp.where(lax.rem(source + step, 4) == rank, landed[step - 1], piece)
        tops.append(piece[0:1])
        sums.append(piece[1:2])
    top = jnp.maximum(jnp.maximum(tops[0], tops[1]), jnp.maximum(tops[2], tops[3]))
    total = sums[0] * jnp.exp(tops[0] - top)
    for source in (1, 2, 3):
        total = total + sums[source] * jnp.exp(tops[source] - top)
    logsum_ref[...] = top + jnp.log(total)


def join_sums(stats, collective_id):
    tokens = stats.shape[1]
    return pl.pallas_call(
        join_sums_kernel,
        out_shape=jax.ShapeDtypeStruct((1, tokens), jnp.float32),
        in_specs=[whole_vmem],
        out_specs=whole_vmem,
        scratch_shapes=[
            pltpu.VMEM((3, 2, tokens), jnp.float32),
            pltpu.SemaphoreType.DMA((3,)),
            pltpu.SemaphoreType.DMA((3,)),
        ],
        compiler_params=pltpu.CompilerParams(collective_id=collective_id, has_side_effects=True),
    )(stats)


def head_back_kernel(
    tile, table_ref, rows_ref, logsum_ref, wanted_ref, weight_ref, slope_ref, grad_ref, picked_ref, turned
):
    step = pl.program_id(0)

    @pl.when(step == 0)
    def _():
        turned[...] = rows_ref[...].astype(jnp.float32).T.astype(jnp.bfloat16)
        picked_ref[...] = jnp.zeros_like(picked_ref)
        grad_ref[...] = jnp.zeros_like(grad_ref)

    logits = jnp.dot(table_ref[...], turned[...], preferred_element_type=jnp.float32)
    row = lax.broadcasted_iota(jnp.int32, logits.shape, 0)
    base = step * tile
    hits = jnp.where(row == wanted_ref[0:1, :] - base, weight_ref[0:1, :], 0.0) + jnp.where(
        row == wanted_ref[1:2, :] - base, weight_ref[1:2, :], 0.0
    )
    picked_ref[...] += jnp.sum(hits * logits, 0, keepdims=True)
    softmax = jnp.exp(logits - logsum_ref[...])
    slope = ((weight_ref[2:3, :] * softmax - hits) * weight_ref[3:4, :]).astype(jnp.bfloat16)
    slope_ref[...] = slope
    grad_ref[...] += lax.dot_general(
        slope, table_ref[...], (((0,), (0,)), ((), ())), preferred_element_type=jnp.float32
    )


def head_back(weights, rows, logsum, wanted, weight_rows, vocab):
    tokens, width = rows.shape
    tile = vocab_tile(vocab)
    fixed = lambda k: (0, 0)
    return pl.pallas_call(
        functools.partial(head_back_kernel, tile),
        grid=(vocab // tile,),
        out_shape=[
            jax.ShapeDtypeStruct((vocab, tokens), jnp.bfloat16),
            jax.ShapeDtypeStruct((tokens, width), jnp.float32),
            jax.ShapeDtypeStruct((1, tokens), jnp.float32),
        ],
        in_specs=[
            pl.BlockSpec((tile, width), lambda k: (k, 0)),
            pl.BlockSpec((tokens, width), fixed),
            pl.BlockSpec((1, tokens), fixed),
            pl.BlockSpec((2, tokens), fixed),
            pl.BlockSpec((4, tokens), fixed),
        ],
        out_specs=[
            pl.BlockSpec((tile, tokens), lambda k: (k, 0)),
            pl.BlockSpec((tokens, width), fixed),
            pl.BlockSpec((1, tokens), fixed),
        ],
        scratch_shapes=[pltpu.VMEM((width, tokens), jnp.bfloat16)],
        compiler_params=pltpu.CompilerParams(vmem_limit_bytes=60 << 20),
    )(weights, rows, logsum, wanted, weight_rows)


def weight_grads_kernel(
    tile_units, tiles, place_ref, slope_ref, rows_ref, ids_ref, zero_ref, joint_ref, normed_ref,
    attended_ref, grad_ref, out_ref, made, sem,
):
    step = pl.program_id(0)
    unit_rows = out_ref.shape[1]
    buffer = lax.rem(step, 2)
    last_units = joint_ref.shape[0] // unit_rows + attended_ref.shape[0] // unit_rows

    def settle(which, count):
        pltpu.make_async_copy(
            made.at[which, pl.ds(0, count)], made.at[which, pl.ds(0, count)], sem.at[which]
        ).wait()

    def send(first, count):
        def push(u, carry):
            pltpu.make_async_copy(
                made.at[buffer, u], out_ref.at[place_ref[first + u]], sem.at[buffer]
            ).start()
            return carry

        lax.fori_loop(0, count, push, 0)

    @pl.when(step >= 2)
    def _():
        settle(buffer, tile_units)

    @pl.when(step < tiles)
    def _():
        row = lax.broadcasted_iota(jnp.int32, slope_ref.shape, 0)
        seen = jnp.where(row == ids_ref[...] - step * slope_ref.shape[0], 1.0, 0.0).astype(jnp.bfloat16)
        made[buffer] = (
            jnp.dot(slope_ref[...], rows_ref[...], preferred_element_type=jnp.float32)
            + jnp.dot(seen, zero_ref[...], preferred_element_type=jnp.float32)
        ).astype(jnp.bfloat16).reshape(tile_units, unit_rows, -1)
        send(step * tile_units, tile_units)

    @pl.when(step == tiles)
    def _():
        joint_units = joint_ref.shape[0] // unit_rows
        made[buffer, pl.ds(0, joint_units)] = jnp.dot(
            joint_ref[...], normed_ref[...], preferred_element_type=jnp.float32
        ).astype(jnp.bfloat16).reshape(joint_units, unit_rows, -1)
        made[buffer, pl.ds(joint_units, last_units - joint_units)] = jnp.dot(
            attended_ref[...], grad_ref[...], preferred_element_type=jnp.float32
        ).astype(jnp.bfloat16).reshape(last_units - joint_units, unit_rows, -1)
        send(tiles * tile_units, last_units)
        settle(1 - buffer, tile_units)
        settle(buffer, last_units)


def weight_grads(place, slots, unit_rows, slope, rows, ids, zero, joint, normed, attended, grad):
    vocab, tokens = slope.shape
    width = rows.shape[1]
    tile = vocab_tile(vocab)
    tiles = vocab // tile
    fixed = lambda k: (0, 0)
    whole = lambda x: pl.BlockSpec(x.shape, fixed)
    return pl.pallas_call(
        functools.partial(weight_grads_kernel, tile // unit_rows, tiles),
        grid=(tiles + 1,),
        out_shape=jax.ShapeDtypeStruct((slots, unit_rows, width), jnp.bfloat16),
        in_specs=[
            pl.BlockSpec(memory_space=pltpu.SMEM),
            pl.BlockSpec((tile, tokens), lambda k: (jnp.minimum(k, tiles - 1), 0)),
        ]
        + [whole(x) for x in (rows, ids, zero, joint, normed, attended, grad)],
        out_specs=whole_any,
        scratch_shapes=[
            pltpu.VMEM((2, tile // unit_rows, unit_rows, width), jnp.bfloat16),
            pltpu.SemaphoreType.DMA((2,)),
        ],
        compiler_params=pltpu.CompilerParams(vmem_limit_bytes=60 << 20),
    )(place, slope, rows, ids, zero, joint, normed, attended, grad)


def adam_update(weight, moment_one, moment_two, gradient, step_rate, decay_factor):
    moment_new = beta_first * moment_one + (1.0 - beta_first) * gradient
    square_new = beta_second * moment_two + (1.0 - beta_second) * gradient * gradient
    moment_hat = moment_new / (1.0 - beta_first**STEP)
    square_hat = square_new / (1.0 - beta_second**STEP)
    weight_new = weight - step_rate * (
        moment_hat / (jnp.sqrt(square_hat) + adam_epsilon) + decay_factor * weight
    )
    return (weight_new, moment_new, square_new)


def norm_forward(values, gain_row):
    return values * inverse_rms(values) * gain_row


def slot_tables(owner_ids, owners, most_units):
    unit_count = owner_ids.shape[0]
    unit_index = jnp.arange(unit_count, dtype=jnp.int32)
    earlier = (owner_ids[None, :] == owner_ids[:, None]) & (
        unit_index[None, :] < unit_index[:, None]
    )
    unit_rank = jnp.sum(earlier.astype(jnp.int32), 1)
    placed = (owner_ids[None, None, :] == jnp.arange(owners, dtype=jnp.int32)[:, None, None]) & (
        unit_rank[None, None, :] == jnp.arange(most_units, dtype=jnp.int32)[None, :, None]
    )
    slot_filled = jnp.any(placed, 2)
    slot_unit = jnp.sum(jnp.where(placed, unit_index[None, None, :], 0), 2)
    return (unit_rank, slot_unit, slot_filled)


def unit_rates(unit_ids, table_units, query_units, value_units):
    return jnp.where(
        unit_ids < table_units,
        rate_table,
        jnp.where(
            unit_ids < query_units,
            rate_query,
            jnp.where(unit_ids < value_units, rate_values, rate_project),
        ),
    )


def pair_slots(route_pairs, priorities, experts, capacity):
    tokens_here = priorities.shape[0]
    pair_expert = route_pairs.T.reshape(-1)
    pair_key = (
        jnp.arange(2, dtype=jnp.int32)[:, None] * tokens_here + priorities[None, :]
    ).reshape(-1)
    before = (pair_expert[None, :] == pair_expert[:, None]) & (
        pair_key[None, :] < pair_key[:, None]
    )
    pair_rank = jnp.sum(before.astype(jnp.int32), 1)
    pair_kept = pair_rank < capacity
    pair_dest = pair_expert * capacity + jnp.minimum(pair_rank, capacity - 1)
    return (pair_kept, pair_dest)


def gelu_tanh(values):
    return jax.nn.gelu(values, approximate=True)


def gelu_slope(values):
    root = math.sqrt(2.0 / math.pi)
    bent = jnp.tanh(root * (values + 0.044715 * values * values * values))
    return 0.5 * (1.0 + bent) + 0.5 * values * (1.0 - bent * bent) * root * (
        1.0 + 3.0 * 0.044715 * values * values
    )


def plane_peer(step):
    chip, core = lax.axis_index("dp"), lax.axis_index("ctx")
    row = lax.rem(chip // 2 + step // 4, 2)
    column = lax.rem(lax.rem(chip, 2) + lax.rem(step // 2, 2), 2)
    place = {"dp": row * 2 + column, "ctx": lax.rem(core + lax.rem(step, 2), 2)}
    return place, place["dp"] * 2 + place["ctx"]


def greet_plane():
    barrier = pltpu.get_barrier_semaphore()
    for step in range(1, 8):
        place, _ = plane_peer(step)
        pl.semaphore_signal(barrier, inc=1, device_id=place, device_id_type=MESH_ID)
    pl.semaphore_wait(barrier, 7)


def plane_copy(source, target, send_sem, recv_sem, step):
    place, _ = plane_peer(step)
    return pltpu.make_async_remote_copy(
        src_ref=source.at[step],
        dst_ref=target.at[step],
        send_sem=send_sem.at[step],
        recv_sem=recv_sem.at[step],
        device_id=place,
        device_id_type=MESH_ID,
    )


def slot_hits(dest_rows, expert, capacity, tokens):
    slot = lax.broadcasted_iota(jnp.int32, (capacity, tokens), 0) + expert * capacity
    return (slot == dest_rows[0:1, :]) | (slot == dest_rows[1:2, :])


def token_hits(dest_columns, expert, capacity, tokens):
    slot = lax.broadcasted_iota(jnp.int32, (tokens, capacity), 1) + expert * capacity
    hit = (slot == dest_columns[:, 0:1]) | (slot == dest_columns[:, 1:2])
    return jnp.where(hit, 1.0, 0.0).astype(jnp.bfloat16)


def gate_of(routes, gates, expert, axis):
    pick = (lambda a, k: a[k : k + 1, :]) if axis == 0 else (lambda a, k: a[:, k : k + 1])
    return jnp.where(pick(routes, 0) == expert, pick(gates, 0), 0.0) + jnp.where(
        pick(routes, 1) == expert, pick(gates, 1), 0.0
    )


def arrival(i):
    return jnp.where(i < 2, i, 9 - i)


def experts_kernel(
    rows_ref, dest_rows, dest_columns, gates, routes, inner_ref, outer_ref, counts_ref,
    mix_ref, arrived, returned, totals_ref,
    outgoing, results, counts, send_one, recv_one, send_two, recv_two, send_count, recv_count,
):
    capacity = arrived.shape[1]
    tokens = rows_ref.shape[0]
    greet_plane()
    counts[0] = counts_ref[...]

    def send_counts(step, carry):
        place, _ = plane_peer(step)
        pltpu.make_async_remote_copy(
            src_ref=counts_ref,
            dst_ref=counts.at[step],
            send_sem=send_count.at[step],
            recv_sem=recv_count.at[step],
            device_id=place,
            device_id_type=MESH_ID,
        ).start()
        return carry

    def dispatch(i, carry):
        step = 7 - i
        _, expert = plane_peer(step)
        hit = jnp.where(slot_hits(dest_rows, expert, capacity, tokens), 1.0, 0.0).astype(jnp.bfloat16)
        rows = jnp.dot(hit, rows_ref[...], preferred_element_type=jnp.float32).astype(jnp.bfloat16)

        @pl.when(step > 0)
        def _():
            outgoing[step] = rows
            plane_copy(outgoing, arrived, send_one, recv_one, step).start()

        @pl.when(step == 0)
        def _():
            arrived[0] = rows

        return carry

    def work(i, carry):
        step = arrival(i)

        @pl.when(step > 0)
        def _():
            plane_copy(outgoing, arrived, send_one, recv_one, step).wait_recv()

        before = jnp.dot(arrived[step], inner_ref[...], preferred_element_type=jnp.float32)
        active = gelu_tanh(before).astype(jnp.bfloat16)
        part = jnp.dot(active, outer_ref[...], preferred_element_type=jnp.float32).astype(jnp.bfloat16)

        @pl.when(step > 0)
        def _():
            results[step] = part
            plane_copy(results, returned, send_two, recv_two, step).start()

        @pl.when(step == 0)
        def _():
            returned[0] = part

        return carry

    def combine(i, carry):
        step = arrival(i)
        _, expert = plane_peer(step)
        hit = token_hits(dest_columns, expert, capacity, tokens)
        gate = gate_of(routes, gates, expert, 1)

        @pl.when(step > 0)
        def _():
            plane_copy(results, returned, send_two, recv_two, step).wait_recv()

        part = gate * jnp.dot(hit, returned[step], preferred_element_type=jnp.float32)

        @pl.when(i == 0)
        def _():
            mix_ref[...] = part

        @pl.when(i > 0)
        def _():
            mix_ref[...] += part

        return carry

    def finish(step, carry):
        plane_copy(outgoing, arrived, send_one, recv_one, step).wait_send()
        plane_copy(results, returned, send_two, recv_two, step).wait_send()
        place, _ = plane_peer(step)
        pltpu.make_async_remote_copy(
            src_ref=counts_ref,
            dst_ref=counts.at[step],
            send_sem=send_count.at[step],
            recv_sem=recv_count.at[step],
            device_id=place,
            device_id_type=MESH_ID,
        ).wait()
        return carry

    lax.fori_loop(0, 8, dispatch, 0)
    lax.fori_loop(1, 8, send_counts, 0)
    lax.fori_loop(0, 8, work, 0)
    lax.fori_loop(0, 8, combine, 0)
    lax.fori_loop(1, 8, finish, 0)
    totals_ref[...] = jnp.sum(counts[...], 0)


def experts_forward(rows, dest, gates, routes, inner, outer, counts, capacity, collective_id):
    tokens, width = rows.shape
    buffer = pltpu.VMEM((8, capacity, width), jnp.bfloat16)
    return pl.pallas_call(
        experts_kernel,
        out_shape=[
            jax.ShapeDtypeStruct((tokens, width), jnp.float32),
            jax.ShapeDtypeStruct((8, capacity, width), jnp.bfloat16),
            jax.ShapeDtypeStruct((8, capacity, width), jnp.bfloat16),
            jax.ShapeDtypeStruct(counts.shape, jnp.float32),
        ],
        in_specs=[whole_vmem] * 8,
        out_specs=[whole_vmem] * 4,
        scratch_shapes=[buffer, buffer, pltpu.VMEM((8,) + counts.shape, jnp.float32)]
        + [pltpu.SemaphoreType.DMA((8,))] * 6,
        compiler_params=pltpu.CompilerParams(
            collective_id=collective_id, has_side_effects=True, vmem_limit_bytes=60 << 20
        ),
    )(rows, dest, dest.T, gates, routes, inner, outer, counts)


def experts_back_kernel(
    rows_ref, dest_rows, dest_columns, gates, routes, returned, arrived, *refs
):
    states, (grad_ref, gate_ref), updated = refs[:6], refs[6:8], refs[8:14]
    held, grads, low, outgoing, landed, results, landed_two, active, slopes = refs[14:23]
    send_one, recv_one, send_two, recv_two, load_sem, store_sem = refs[23:]
    inner_ref, outer_ref = low.at[0], low.at[1]
    capacity = arrived.shape[1]
    tokens = rows_ref.shape[0]
    loads = [pltpu.make_async_copy(states[k], held.at[k], load_sem.at[k]) for k in range(6)]
    for load in loads:
        load.start()
    greet_plane()
    gate_ref[...] = jnp.zeros_like(gate_ref)

    def dispatch(i, carry):
        step = 7 - i
        _, expert = plane_peer(step)
        hit = slot_hits(dest_rows, expert, capacity, tokens)
        rows = jnp.dot(
            jnp.where(hit, 1.0, 0.0).astype(jnp.bfloat16), rows_ref[...], preferred_element_type=jnp.float32
        )
        scale = jnp.sum(jnp.where(hit, gate_of(routes, gates, expert, 0), 0.0), 1, keepdims=True)
        sent = (rows * scale).astype(jnp.bfloat16)

        @pl.when(step > 0)
        def _():
            outgoing[step] = sent
            plane_copy(outgoing, landed, send_one, recv_one, step).start()

        @pl.when(step == 0)
        def _():
            landed[0] = sent

        dots = jnp.sum(rows * returned[step].astype(jnp.float32), 1, keepdims=True)
        part = jnp.sum(jnp.where(hit, dots, 0.0), 0, keepdims=True)
        for k in range(2):
            gate_ref[k : k + 1, :] += jnp.where(routes[k : k + 1, :] == expert, part, 0.0)
        return carry

    def work(i, carry):
        step = arrival(i)

        @pl.when(step > 0)
        def _():
            plane_copy(outgoing, landed, send_one, recv_one, step).wait_recv()

        grad_active = lax.dot_general(
            landed[step], outer_ref[...], (((1,), (1,)), ((), ())), preferred_element_type=jnp.float32
        )
        before = jnp.dot(arrived[step], inner_ref[...], preferred_element_type=jnp.float32)
        slope = (grad_active * gelu_slope(before)).astype(jnp.bfloat16)
        back = lax.dot_general(
            slope, inner_ref[...], (((1,), (1,)), ((), ())), preferred_element_type=jnp.float32
        ).astype(jnp.bfloat16)

        @pl.when(step > 0)
        def _():
            results[step] = back
            plane_copy(results, landed_two, send_two, recv_two, step).start()

        @pl.when(step == 0)
        def _():
            landed_two[0] = back

        slopes[step] = slope
        active[step] = gelu_tanh(before).astype(jnp.bfloat16)
        return carry

    def weigh(step, carry):
        outer_part = lax.dot_general(
            active[step], landed[step], (((0,), (0,)), ((), ())), preferred_element_type=jnp.float32
        )
        inner_part = lax.dot_general(
            arrived[step], slopes[step], (((0,), (0,)), ((), ())), preferred_element_type=jnp.float32
        )

        @pl.when(step == 0)
        def _():
            grads[0] = inner_part
            grads[1] = outer_part

        @pl.when(step > 0)
        def _():
            grads[0] += inner_part
            grads[1] += outer_part

        return carry

    def update(i, carry):
        lines = grads.shape[1] // 8
        span = pl.ds(pl.multiple_of(i * lines, lines), lines)
        for k, rate in enumerate((rate_inner, rate_outer)):
            fresh = adam_update(
                held[3 * k, span], held[3 * k + 1, span], held[3 * k + 2, span], grads[k, span], rate, decay_rate
            )
            for n in range(3):
                held[3 * k + n, span] = fresh[n]
        return carry

    def combine(i, carry):
        step = arrival(i)
        _, expert = plane_peer(step)
        hit = token_hits(dest_columns, expert, capacity, tokens)

        @pl.when(step > 0)
        def _():
            plane_copy(results, landed_two, send_two, recv_two, step).wait_recv()

        part = jnp.dot(hit, landed_two[step], preferred_element_type=jnp.float32)

        @pl.when(i == 0)
        def _():
            grad_ref[...] = part

        @pl.when(i > 0)
        def _():
            grad_ref[...] += part

        return carry

    def finish(step, carry):
        plane_copy(outgoing, landed, send_one, recv_one, step).wait_send()
        plane_copy(results, landed_two, send_two, recv_two, step).wait_send()
        return carry

    lax.fori_loop(0, 8, dispatch, 0)
    for load in loads:
        load.wait()
    for k in range(2):
        low[k] = held[3 * k].astype(jnp.bfloat16)
    lax.fori_loop(0, 8, work, 0)
    lax.fori_loop(0, 8, weigh, 0)
    lax.fori_loop(0, 8, update, 0)
    stores = [pltpu.make_async_copy(held.at[k], updated[k], store_sem.at[k]) for k in range(6)]
    for store in stores:
        store.start()
    lax.fori_loop(0, 8, combine, 0)
    lax.fori_loop(1, 8, finish, 0)
    for store in stores:
        store.wait()


def experts_backward(rows, dest, gates, routes, returned, arrived, states, collective_id):
    tokens, width = rows.shape
    capacity = arrived.shape[1]
    square = states[0].shape
    buffer = pltpu.VMEM((8, capacity, width), jnp.bfloat16)
    inside_buffer = pltpu.VMEM((8, capacity, square[1]), jnp.bfloat16)
    state = jax.ShapeDtypeStruct(square, jnp.float32)
    return pl.pallas_call(
        experts_back_kernel,
        out_shape=[
            jax.ShapeDtypeStruct((tokens, width), jnp.float32),
            jax.ShapeDtypeStruct((2, tokens), jnp.float32),
        ]
        + [state] * 6,
        in_specs=[whole_vmem] * 7 + [whole_any] * 6,
        out_specs=[whole_vmem] * 2 + [whole_any] * 6,
        scratch_shapes=[
            pltpu.VMEM((6,) + square, jnp.float32),
            pltpu.VMEM((2,) + square, jnp.float32),
            pltpu.VMEM((2,) + square, jnp.bfloat16),
        ]
        + [buffer] * 4
        + [inside_buffer] * 2
        + [pltpu.SemaphoreType.DMA((8,))] * 4
        + [pltpu.SemaphoreType.DMA((6,))] * 2,
        compiler_params=pltpu.CompilerParams(
            collective_id=collective_id, has_side_effects=True, vmem_limit_bytes=63 << 20
        ),
    )(rows, dest, dest.T, gates, routes, returned, arrived, *states)


def own_units_kernel(
    chunks, parts_ref, small_ref, rates_ref, filled_ref, *refs
):
    chip, core = lax.axis_index("dp"), lax.axis_index("ctx")
    beside = chip + 1 - 2 * lax.rem(chip, 2)
    across = lax.rem(chip + 2, 4)
    opposite = across + 1 - 2 * lax.rem(across, 2)
    places = (opposite, beside, across, chip)
    states, (small_out, *updated) = refs[:3], refs[3:7]
    own, other, relay, landed, small_landed, held = refs[7:13]
    own_sem, other_send, other_recv, relay_send, relay_recv, landed_send, landed_recv = refs[13:20]
    small_send, small_recv, load_sem, store_sem = refs[20:]
    slots = held.shape[1]
    size = slots // chunks
    split = (chunks + 1) // 2
    greet_plane()

    def span(q):
        return pl.ds(q * size, size)

    def fetch(k):
        first = (places[k] * 2 + core) * slots
        return pltpu.make_async_copy(parts_ref.at[pl.ds(first, slots)], own.at[k], own_sem.at[k])

    def pass_over(k, q):
        first = (places[k] * 2 + 1 - core) * slots + q * size
        return pltpu.make_async_remote_copy(
            src_ref=parts_ref.at[pl.ds(first, size)],
            dst_ref=other.at[k, span(q)],
            send_sem=other_send.at[k, q],
            recv_sem=other_recv.at[k, q],
            device_id={"ctx": 1 - core},
            device_id_type=MESH_ID,
        )

    def to_relay(q, place):
        return pltpu.make_async_remote_copy(
            src_ref=own.at[0, span(q)],
            dst_ref=relay.at[span(q)],
            send_sem=relay_send.at[q],
            recv_sem=relay_recv.at[q],
            device_id={"dp": place},
            device_id_type=MESH_ID,
        )

    def to_owner(k, q):
        return pltpu.make_async_remote_copy(
            src_ref=own.at[k, span(q)],
            dst_ref=landed.at[k - 1, span(q)],
            send_sem=landed_send.at[k - 1, q],
            recv_sem=landed_recv.at[k - 1, q],
            device_id={"dp": places[k]},
            device_id_type=MESH_ID,
        )

    def small_copy(step):
        place, _ = plane_peer(step)
        return pltpu.make_async_remote_copy(
            src_ref=small_ref,
            dst_ref=small_landed.at[chip * 2 + core],
            send_sem=small_send.at[step],
            recv_sem=small_recv.at[step],
            device_id=place,
            device_id_type=MESH_ID,
        )

    def store(n, q):
        return pltpu.make_async_copy(
            held.at[n, span(q)], updated[n].at[span(q)], store_sem.at[n, q]
        )

    loads = [pltpu.make_async_copy(states[n], held.at[n], load_sem.at[n]) for n in range(3)]
    for k in range(4):
        fetch(k).start()

        def start(q, carry):
            pass_over(k, q).start()
            return carry

        lax.fori_loop(0, chunks, start, 0)

    def joined(k, q):
        pass_over(k, q).wait_recv()
        return own[k, span(q)].astype(jnp.float32) + other[k, span(q)].astype(jnp.float32)

    for load in loads:
        load.start()
    fetch(0).wait()

    def first_leg(place):
        def leg(q, carry):
            own[0, span(q)] = joined(0, q).astype(jnp.bfloat16)
            to_relay(q, place).start()
            return carry

        return leg

    lax.fori_loop(0, split, first_leg(beside), 0)
    lax.fori_loop(split, chunks, first_leg(across), 0)
    lax.fori_loop(1, 8, lambda step, carry: (small_copy(step).start(), carry)[1], 0)
    small_landed[chip * 2 + core] = small_ref[...]
    fetch(1).wait()
    fetch(2).wait()

    def direct(k):
        def leg(q, carry):
            own[k, span(q)] = joined(k, q).astype(jnp.bfloat16)
            to_owner(k, q).start()
            return carry

        return leg

    def relayed(k, place):
        def leg(q, carry):
            to_relay(q, place).wait_recv()
            total = joined(k, q) + relay[span(q)].astype(jnp.float32)
            own[k, span(q)] = total.astype(jnp.bfloat16)
            to_owner(k, q).start()
            return carry

        return leg

    lax.fori_loop(0, split, direct(1), 0)
    lax.fori_loop(split, chunks, direct(2), 0)
    lax.fori_loop(0, split, relayed(2, beside), 0)
    lax.fori_loop(split, chunks, relayed(1, across), 0)
    fetch(3).wait()
    for load in loads:
        load.wait()

    def keep(q, carry):
        total = joined(3, q)
        to_owner(1, q).wait_recv()
        to_owner(2, q).wait_recv()
        total = total + landed[0, span(q)].astype(jnp.float32) + landed[1, span(q)].astype(jnp.float32)
        total = jnp.where(filled_ref[span(q)] > 0.5, total, 0.0)
        fresh = adam_update(
            held[0, span(q)], held[1, span(q)], held[2, span(q)], total, rates_ref[span(q)], decay_rate
        )
        for n in range(3):
            held[n, span(q)] = fresh[n]
            store(n, q).start()
        return carry

    lax.fori_loop(0, split, keep, 0)
    lax.fori_loop(split, chunks, keep, 0)

    def finish(q, carry):
        for k in range(4):
            pass_over(k, q).wait_send()
        to_owner(1, q).wait_send()
        to_owner(2, q).wait_send()
        for n in range(3):
            store(n, q).wait()
        return carry

    lax.fori_loop(0, chunks, finish, 0)
    lax.fori_loop(0, split, lambda q, carry: (to_relay(q, beside).wait_send(), carry)[1], 0)
    lax.fori_loop(split, chunks, lambda q, carry: (to_relay(q, across).wait_send(), carry)[1], 0)
    lax.fori_loop(1, 8, lambda step, carry: (small_copy(step).wait(), carry)[1], 0)
    total = small_landed[0]
    for source in range(1, 8):
        total = total + small_landed[source]
    small_out[...] = total


def own_units(parts, small, rates, filled, states, collective_id):
    slots = states[0].shape[0]
    unit = parts.shape[1:]
    chunks = max(k for k in range(1, 8) if slots % k == 0)
    block = pltpu.VMEM((4, slots) + unit, jnp.bfloat16)
    return pl.pallas_call(
        functools.partial(own_units_kernel, chunks),
        out_shape=[jax.ShapeDtypeStruct(small.shape, jnp.float32)]
        + [jax.ShapeDtypeStruct((slots,) + unit, jnp.float32)] * 3,
        in_specs=[whole_any] + [whole_vmem] * 3 + [whole_any] * 3,
        out_specs=[whole_vmem] + [whole_any] * 3,
        scratch_shapes=[
            block,
            block,
            pltpu.VMEM((slots,) + unit, jnp.bfloat16),
            pltpu.VMEM((2, slots) + unit, jnp.bfloat16),
            pltpu.VMEM((8,) + small.shape, jnp.float32),
            pltpu.VMEM((3, slots) + unit, jnp.float32),
            pltpu.SemaphoreType.DMA((4,)),
            pltpu.SemaphoreType.DMA((4, chunks)),
            pltpu.SemaphoreType.DMA((4, chunks)),
            pltpu.SemaphoreType.DMA((chunks,)),
            pltpu.SemaphoreType.DMA((chunks,)),
            pltpu.SemaphoreType.DMA((2, chunks)),
            pltpu.SemaphoreType.DMA((2, chunks)),
            pltpu.SemaphoreType.DMA((8,)),
            pltpu.SemaphoreType.DMA((8,)),
            pltpu.SemaphoreType.DMA((3,)),
            pltpu.SemaphoreType.DMA((3, chunks)),
        ],
        compiler_params=pltpu.CompilerParams(
            collective_id=collective_id, has_side_effects=True, vmem_limit_bytes=56 << 20
        ),
    )(parts, small, rates, filled, *states)


def to_plane(buffer):
    return lax.all_to_all(buffer, ("dp", "ctx"), split_axis=0, concat_axis=0, tiled=True)


def plain_hits(dest, experts, capacity):
    slots = lax.broadcasted_iota(jnp.int32, (experts * capacity, dest.shape[1]), 0)
    return [slots == dest[k : k + 1] for k in range(2)]


def plain_forward(rows, dest, gates, inner, outer, owners, capacity):
    width = rows.shape[1]
    hits = plain_hits(dest, owners, capacity)
    both = (hits[0] | hits[1]).astype(jnp.bfloat16)
    sent = jnp.dot(both, rows, preferred_element_type=jnp.float32).astype(jnp.bfloat16)
    arrived = to_plane(sent.reshape(owners, capacity, width))
    hidden = jnp.einsum("ocd,df->ocf", arrived, inner, preferred_element_type=jnp.float32)
    active = gelu_tanh(hidden).astype(jnp.bfloat16)
    part = jnp.einsum("ocf,fd->ocd", active, outer, preferred_element_type=jnp.float32)
    returned = to_plane(part.astype(jnp.bfloat16))
    flat = returned.reshape(owners * capacity, width)
    mix = sum(
        gates[:, k : k + 1]
        * lax.dot_general(
            hits[k].astype(jnp.bfloat16),
            flat,
            (((0,), (0,)), ((), ())),
            preferred_element_type=jnp.float32,
        )
        for k in range(2)
    )
    return (mix, arrived, hidden, returned)


def plain_backward(rows, dest, gates, returned, arrived, hidden, inner, outer):
    owners, capacity, width = arrived.shape
    hits = plain_hits(dest, owners, capacity)
    both = (hits[0] | hits[1]).astype(jnp.bfloat16)
    slot_scale = jnp.sum(
        jnp.where(hits[0], gates[0:1], 0.0) + jnp.where(hits[1], gates[1:2], 0.0), 1, keepdims=True
    )
    slot_grads = jnp.dot(both, rows, preferred_element_type=jnp.float32)
    sent = (slot_grads * slot_scale).astype(jnp.bfloat16)
    flat = returned.reshape(owners * capacity, width)
    dots = jnp.sum(slot_grads * flat.astype(jnp.float32), 1, keepdims=True)
    gate_part = jnp.concatenate(
        [jnp.sum(jnp.where(hit, dots, 0.0), 0, keepdims=True) for hit in hits], 0
    )
    landed = to_plane(sent.reshape(owners, capacity, width))
    grad_active = jnp.einsum("ocd,fd->ocf", landed, outer, preferred_element_type=jnp.float32)
    active = gelu_tanh(hidden).astype(jnp.bfloat16)
    slope = (grad_active * gelu_slope(hidden)).astype(jnp.bfloat16)
    outer_grad = jnp.einsum("ocf,ocd->fd", active, landed, preferred_element_type=jnp.float32)
    inner_grad = jnp.einsum("ocd,ocf->df", arrived, slope, preferred_element_type=jnp.float32)
    back = jnp.einsum("ocf,df->ocd", slope, inner, preferred_element_type=jnp.float32)
    back = to_plane(back.astype(jnp.bfloat16)).reshape(owners * capacity, width)
    grad = lax.dot_general(
        both, back, (((0,), (0,)), ((), ())), preferred_element_type=jnp.float32
    )
    return (grad, gate_part, inner_grad, outer_grad)


def on_device(
    token_ids,
    targets,
    counted,
    routes,
    priority,
    owner_of,
    master,
    master_first,
    master_second,
    expert_in,
    expert_in_first,
    expert_in_second,
    expert_out,
    expert_out_first,
    expert_out_second,
    norm_gains,
    norm_gains_first,
    norm_gains_second,
    router,
    router_first,
    router_second,
    rel_bias,
    rel_bias_first,
    rel_bias_second,
):
    owners = lax.axis_size(("dp", "ctx"))
    tensor_ranks = lax.axis_size("tensor")
    my_owner = lax.axis_index(("dp", "ctx"))
    my_rank = lax.axis_index("tensor")
    my_context = lax.axis_index("ctx")
    sequences, half_length = token_ids.shape
    tokens_here = sequences * half_length
    most_units = master.shape[2]
    unit_rows = master.shape[3]
    model_width = master.shape[4]
    vocab_here = VOCAB // tensor_ranks
    heads_here = rel_bias.shape[0]
    head_size = model_width // (heads_here * tensor_ranks)
    hidden_here = heads_here * head_size
    experts = router.shape[1]
    capacity = (18 * tokens_here + 8 * experts - 1) // (8 * experts)
    table_units = vocab_here // unit_rows
    query_units = table_units + 2 * hidden_here // unit_rows
    value_units = table_units + 3 * hidden_here // unit_rows
    embed_scale = math.sqrt(model_width)
    owner_ids = owner_of[:, 0]
    unit_rank, slot_unit, slot_filled = slot_tables(owner_ids, owners, most_units)
    on_square = lax.axis_size("dp") == 4 and lax.axis_size("ctx") == 2
    counted_rows = counted.reshape(tokens_here, 2).T.astype(jnp.float32)
    loss_weights = counted_rows * jnp.array([[1.0], [ahead_weight]], jnp.float32)
    counts = jnp.zeros((8, 128), jnp.float32).at[0:2].set(jnp.sum(counted_rows, 1, keepdims=True))
    unit_slots = owner_ids * most_units + unit_rank
    route_pairs = routes.reshape(tokens_here, 2)
    pair_kept, pair_dest = pair_slots(route_pairs, priority[0], experts, capacity)
    dest = jnp.where(pair_kept, pair_dest, -1).reshape(2, tokens_here)
    unit_slots, dest = lax.optimization_barrier((unit_slots, dest))
    local_ids = token_ids.reshape(-1) - my_rank * vocab_here
    inside = (local_ids >= 0) & (local_ids < vocab_here)
    clipped_ids = jnp.clip(local_ids, 0, vocab_here - 1)
    master_low = master[0, 0].astype(jnp.bfloat16)
    part_width = model_width // column_parts
    unit_starts = jnp.sum(
        jnp.where(
            (clipped_ids // unit_rows)[None, :] == jnp.arange(unit_slots.shape[0])[:, None],
            unit_slots[:, None] * unit_rows,
            0,
        ),
        0,
    )
    slot_rows = unit_starts + clipped_ids % unit_rows
    gathered, embedded = [], []

    def embed(part):
        if part > 0:
            gathered[part], embedded[-1] = lax.optimization_barrier((gathered[part], embedded[-1]))
        table_part = gathered[part].reshape(-1, part_width)
        looked = jnp.where(inside[:, None], jnp.take(table_part, slot_rows, axis=0), 0)
        embedded.extend(sum_line(looked, [], [], keep_total, 11 + part, rows=128))

    for part in range(column_parts):
        columns = master_low[:, :, part * part_width : (part + 1) * part_width]
        if part > 0:
            columns, gathered[-1] = lax.optimization_barrier((columns, gathered[-1]))
        if part > 1:
            columns, embedded[-1] = lax.optimization_barrier((columns, embedded[-1]))
        gathered.append(lax.all_gather(columns, ("dp", "ctx"), axis=0, tiled=True))
        if part > 0:
            embed(part - 1)
    embed(column_parts - 1)
    embedded = jnp.concatenate(embedded, 1)
    weights_low = pull_units(gathered, unit_slots).reshape(-1, model_width)
    joint_low = weights_low[vocab_here : vocab_here + 3 * hidden_here]
    project_low = weights_low[vocab_here + 3 * hidden_here :]
    rolled = [project_low] + [
        lax.ppermute(project_low, "tensor", [(source, (source + step) % 4) for source in range(4)])
        for step in (1, 2, 3)
    ]
    project_full = lax.dynamic_slice_in_dim(
        jnp.concatenate(rolled[::-1] + rolled[::-1], 0), (3 - my_rank) * hidden_here, model_width, 0
    )
    gain_rows = [norm_gains[k : k + 1] for k in range(3)]
    stream_shape = jax.ShapeDtypeStruct((tokens_here, model_width), jnp.float32)
    gain_shape = jax.ShapeDtypeStruct((1, model_width), jnp.float32)
    stream_zero = embedded.astype(jnp.float32) * embed_scale
    first_normalized = norm_forward(stream_zero, norm_gains[0])
    normed_one_low = first_normalized.astype(jnp.bfloat16)
    joint = lax.dot_general(
        joint_low, normed_one_low, (((1,), (1,)), ((), ())), preferred_element_type=jnp.float32
    ).astype(jnp.bfloat16)
    pairs_before = passed_along(joint[hidden_here:], "ctx", 1)
    attended, logsum_rows = attention(rel_bias, joint, pairs_before, heads_here, head_size)
    (attended_all,) = gather_line([attended], 2)
    stream_one = stream_zero + lax.dot_general(
        attended_all.reshape(model_width, tokens_here),
        project_full,
        (((0,), (0,)), ((), ())),
        preferred_element_type=jnp.float32,
    )
    second_normalized = norm_forward(stream_one, norm_gains[1])
    normed_two_low = second_normalized.astype(jnp.bfloat16)
    router_low = router.astype(jnp.bfloat16)
    router_scores_raw = jnp.dot(normed_two_low, router_low, preferred_element_type=jnp.float32)
    route_onehot = (route_pairs[:, :, None] == jnp.arange(experts, dtype=jnp.int32)).astype(
        jnp.float32
    )
    chosen = jnp.einsum("tke,te->tk", route_onehot, router_scores_raw, precision=highest_precision)
    gate_values = jax.nn.softmax(chosen, -1)
    inner_low = expert_in[0].astype(jnp.bfloat16)
    outer_low = expert_out[0].astype(jnp.bfloat16)
    if on_square:
        moe_partial, arrived, returned, counts = experts_forward(
            normed_two_low, dest, gate_values, route_pairs, inner_low, outer_low, counts, capacity, 8
        )
    else:
        moe_partial, arrived, hidden_pre, returned = plain_forward(
            normed_two_low, dest, gate_values, inner_low, outer_low, owners, capacity
        )
        counts = lax.psum(counts, ("dp", "ctx"))
    weight_total = counts[0, 0] + ahead_weight * counts[1, 0]
    head_low, stream_two = sum_line(
        moe_partial, [stream_one, gain_rows[2]], [stream_shape], finish_mixture, 3
    )
    stats = head_sums(weights_low, head_low, vocab_here)
    logsum_vocab = join_sums(stats, 7)
    local_targets = targets.reshape(tokens_here, 2).T - my_rank * vocab_here
    weight_rows = jnp.concatenate(
        [
            loss_weights,
            loss_weights[0:1] + loss_weights[1:2],
            jnp.broadcast_to(1.0 / weight_total, (1, tokens_here)),
        ],
        0,
    )
    slopes, grad_head, target_sums = head_back(
        weights_low, head_low, logsum_vocab, local_targets, weight_rows, vocab_here
    )
    grad_two_low, grad_two, gain_grad_three = sum_line(
        grad_head,
        [stream_two, gain_rows[2]],
        [stream_shape, gain_shape],
        finish_head_grad,
        4,
        prologue=clear_gain,
    )
    gate_rows = gate_values.T
    expert_states = (
        expert_in[0],
        expert_in_first[0],
        expert_in_second[0],
        expert_out[0],
        expert_out_first[0],
        expert_out_second[0],
    )
    if on_square:
        moe_grad_part, gate_part, *expert_states = experts_backward(
            grad_two_low, dest, gate_rows, route_pairs.T, returned, arrived, expert_states, 9
        )
    else:
        moe_grad_part, gate_part, inner_grad, outer_grad = plain_backward(
            grad_two_low, dest, gate_rows, returned, arrived, hidden_pre, inner_low, outer_low
        )
        expert_states = adam_update(
            *expert_states[:3], inner_grad, rate_inner, decay_rate
        ) + adam_update(*expert_states[3:], outer_grad, rate_outer, decay_rate)
    gate_part = jnp.concatenate([gate_part, target_sums, jnp.zeros_like(target_sums)], 0)
    gate_block = pltpu.VMEM((3, 4, tokens_here), jnp.float32)
    grad_one_low, grad_one, logit_grad, target_total, gain_grad_two = sum_line(
        moe_grad_part,
        [
            stream_one,
            gain_rows[1],
            grad_two,
            gate_part,
            gate_rows,
            route_pairs.T,
            router_low,
        ],
        [
            stream_shape,
            jax.ShapeDtypeStruct((experts, tokens_here), jnp.bfloat16),
            jax.ShapeDtypeStruct((1, tokens_here), jnp.float32),
            gain_shape,
        ],
        finish_expert_grad,
        5,
        prologue=start_router_grad,
        scratch=(gate_block, pltpu.SemaphoreType.DMA((3,)), pltpu.SemaphoreType.DMA((3,))),
        opening=send_gate_parts,
    )
    router_grad = jnp.dot(logit_grad, normed_two_low, preferred_element_type=jnp.float32)
    loss_local = jnp.sum(weight_rows[2:3] * logsum_vocab) - jnp.sum(target_total)
    query_grad, pair_grad, before_grad, bias_lines = attention_back(
        rel_bias,
        joint,
        pairs_before,
        logsum_rows,
        grad_one_low,
        project_low,
        heads_here,
        head_size,
    )
    grad_after = passed_along(before_grad, "ctx", -1)
    pair_grad_low = (pair_grad + grad_after.astype(jnp.float32)).astype(jnp.bfloat16)
    joint_grad = jnp.concatenate([query_grad, pair_grad_low], 0)
    distances = 2 * (half_length // BLOCK)
    bias_grad = jnp.sum(bias_lines, 1).reshape(heads_here, distances)
    zero_grad_low, gain_grads = sum_line(
        lax.dot_general(
            joint_grad, joint_low, (((0,), (0,)), ((), ())), preferred_element_type=jnp.float32
        ),
        [embedded, gain_rows[0], grad_one, gain_grad_two, gain_grad_three],
        [jax.ShapeDtypeStruct((8, model_width), jnp.float32)],
        functools.partial(finish_input_grad, embed_scale),
        6,
        prologue=clear_gain,
        scratch=(pltpu.SemaphoreType.DMA, pltpu.SemaphoreType.DMA),
        ending=share_gains,
    )
    my_units = jnp.take(slot_unit, my_owner, axis=0)
    my_filled = jnp.take(slot_filled, my_owner, axis=0)[:, None, None]
    outgoing = weight_grads(
        unit_slots,
        owners * most_units,
        unit_rows,
        slopes,
        head_low,
        local_ids[None, :],
        zero_grad_low,
        joint_grad,
        normed_one_low,
        attended,
        grad_one_low,
    )
    bias_row = jnp.concatenate([bias_grad.reshape(-1), loss_local[None]])
    bias_row = jnp.pad(bias_row, (0, model_width - bias_row.shape[0]))[None]
    small = jnp.concatenate([gain_grads[:3], router_grad, bias_row], 0)
    small = jnp.pad(small, ((0, -small.shape[0] % 8), (0, 0)))
    slot_rates = unit_rates(my_units, table_units, query_units, value_units)[:, None, None]
    states = (master[0, 0], master_first[0, 0], master_second[0, 0])
    if on_square:
        spread = (most_units, 1, model_width)
        small, *states = own_units(
            outgoing,
            small,
            jnp.broadcast_to(slot_rates, spread),
            jnp.broadcast_to(my_filled.astype(jnp.float32), spread),
            states,
            10,
        )
    else:
        mine = lax.psum_scatter(
            outgoing.astype(jnp.float32), ("dp", "ctx"), scatter_dimension=0, tiled=True
        )
        small = lax.psum(small, ("dp", "ctx"))
        states = adam_update(*states, jnp.where(my_filled, mine, 0.0), slot_rates, decay_rate)
    gains_grad = small[:3]
    router_grad = small[3 : 3 + experts].T
    bias_grad = small[3 + experts, : rel_bias.size].reshape(rel_bias.shape)
    loss_totals = jnp.stack([small[3 + experts, rel_bias.size], weight_total])
    gains_new, gains_first_new, gains_second_new = adam_update(
        norm_gains, norm_gains_first, norm_gains_second, gains_grad, rate_gains, 0.0
    )
    router_new, router_first_new, router_second_new = adam_update(
        router, router_first, router_second, router_grad, rate_router, decay_rate
    )
    biases_new, biases_first_new, biases_second_new = adam_update(
        rel_bias, rel_bias_first, rel_bias_second, bias_grad, rate_biases, 0.0
    )
    return (
        loss_totals,
        *(state[None, None] for state in states),
        *(state[None] for state in expert_states),
        gains_new,
        gains_first_new,
        gains_second_new,
        router_new,
        router_first_new,
        router_second_new,
        biases_new,
        biases_first_new,
        biases_second_new,
    )


def solution(mesh):
    in_specs = (
        P("dp", "ctx"),
        P("dp", "ctx", None),
        P("dp", "ctx", None),
        P("dp", "ctx", None),
        P(("dp", "ctx"), None),
        P(),
        P("tensor", ("dp", "ctx"), None, None, None),
        P("tensor", ("dp", "ctx"), None, None, None),
        P("tensor", ("dp", "ctx"), None, None, None),
        P(("dp", "ctx"), None, "tensor"),
        P(("dp", "ctx"), None, "tensor"),
        P(("dp", "ctx"), None, "tensor"),
        P(("dp", "ctx"), "tensor", None),
        P(("dp", "ctx"), "tensor", None),
        P(("dp", "ctx"), "tensor", None),
        P(),
        P(),
        P(),
        P(),
        P(),
        P(),
        P("tensor", None),
        P("tensor", None),
        P("tensor", None),
    )
    out_specs = (
        P(),
        P("tensor", ("dp", "ctx"), None, None, None),
        P("tensor", ("dp", "ctx"), None, None, None),
        P("tensor", ("dp", "ctx"), None, None, None),
        P(("dp", "ctx"), None, "tensor"),
        P(("dp", "ctx"), None, "tensor"),
        P(("dp", "ctx"), None, "tensor"),
        P(("dp", "ctx"), "tensor", None),
        P(("dp", "ctx"), "tensor", None),
        P(("dp", "ctx"), "tensor", None),
        P(),
        P(),
        P(),
        P(),
        P(),
        P(),
        P("tensor", None),
        P("tensor", None),
        P("tensor", None),
    )
    return jax.shard_map(
        on_device, mesh=mesh, in_specs=in_specs, out_specs=out_specs, check_vma=False
    )
```

```python
import functools
import math

import jax
import jax.numpy as jnp
from jax import lax
from jax.experimental import pallas as pl
from jax.experimental.pallas import tpu as pltpu
from jax.sharding import PartitionSpec as P

VOCAB = 32000
BLOCK = 256
STEP = 10


highest_precision = lax.Precision.HIGHEST
beta_first = 0.9
beta_second = 0.95
adam_epsilon = 1e-08
norm_epsilon = 1e-06
ahead_weight = 0.3
masked_score = -1e30
rate_table = 0.1
rate_query = 0.05
rate_values = 0.05
rate_project = 0.5
rate_inner = 0.05
rate_outer = 0.03
rate_gains = 0.5
rate_router = 0.05
rate_biases = 0.5
decay_rate = 0.1


def passed_along(value, axis, steps):
    count = lax.axis_size(axis)
    initial, last = (max(0, -steps), min(count, count - steps))
    return lax.ppermute(value, axis, [(source, source + steps) for source in range(initial, last)])

MESH_ID = pl.DeviceIdType.MESH
whole_vmem = pl.BlockSpec(memory_space=pltpu.VMEM)
whole_any = pl.BlockSpec(memory_space=pl.ANY)
line_lag = 2


def sum_line_kernel(
    rows, count, opening, prologue, epilogue, ending, n_extra, n_aux, n_scratch, part_ref, *refs
):
    extras = refs[:n_extra]
    out_ref = refs[n_extra]
    aux = refs[n_extra + 1 : n_extra + 1 + n_aux]
    rest = refs[n_extra + 1 + n_aux :]
    scratch = rest[:n_scratch]
    stage, from_end, from_mid, send_sem, end_sem, mid_sem, back_sem, back_recv = rest[n_scratch:]
    rank = lax.axis_index("tensor")
    inner = (rank == 1) | (rank == 2)
    end_peer = jnp.where(rank < 2, 1 - rank, 5 - rank)
    mid_peer = 3 - rank
    barrier = pltpu.get_barrier_semaphore()
    if opening is None:
        pl.semaphore_signal(barrier, inc=1, device_id={"tensor": end_peer}, device_id_type=MESH_ID)

        @pl.when(inner)
        def _():
            pl.semaphore_signal(
                barrier, inc=1, device_id={"tensor": mid_peer}, device_id_type=MESH_ID
            )
            pl.semaphore_wait(barrier, 2)

        @pl.when(jnp.logical_not(inner))
        def _():
            pl.semaphore_wait(barrier, 1)
    else:
        for step in (1, 2, 3):
            other = lax.rem(rank + step, 4)
            pl.semaphore_signal(barrier, inc=1, device_id={"tensor": other}, device_id_type=MESH_ID)
        pl.semaphore_wait(barrier, 3)

    def span(i):
        return pl.ds(pl.multiple_of(i * rows, rows), rows)

    def to_inner(i):
        return pltpu.make_async_remote_copy(
            src_ref=stage.at[i],
            dst_ref=from_end.at[i],
            send_sem=send_sem.at[i],
            recv_sem=end_sem.at[i],
            device_id={"tensor": end_peer},
            device_id_type=MESH_ID,
        )

    def to_middle(i):
        return pltpu.make_async_remote_copy(
            src_ref=stage.at[i],
            dst_ref=from_mid.at[i],
            send_sem=send_sem.at[i],
            recv_sem=mid_sem.at[i],
            device_id={"tensor": mid_peer},
            device_id_type=MESH_ID,
        )

    def to_end(i):
        return pltpu.make_async_remote_copy(
            src_ref=out_ref.at[span(i)],
            dst_ref=out_ref.at[span(i)],
            send_sem=back_sem.at[i],
            recv_sem=back_recv.at[i],
            device_id={"tensor": end_peer},
            device_id_type=MESH_ID,
        )

    if opening is not None:
        opening(rank, extras, scratch)

    @pl.when(jnp.logical_not(inner))
    def _():
        def push(i, carry):
            stage[i] = part_ref[span(i)].astype(jnp.bfloat16)
            to_inner(i).start()
            return carry

        lax.fori_loop(0, count, push, 0)

    if prologue is not None:
        prologue(rank, inner, extras, aux, scratch)

    @pl.when(inner)
    def _():
        def step(i, carry):
            @pl.when(i < count)
            def _():
                to_inner(i).wait_recv()
                mine = part_ref[span(i)].astype(jnp.float32) + from_end[i].astype(jnp.float32)
                stage[i] = mine.astype(jnp.bfloat16)
                to_middle(i).start()

            @pl.when(i >= line_lag)
            def _():
                j = i - line_lag
                to_middle(j).wait_recv()
                total = stage[j].astype(jnp.float32) + from_mid[j].astype(jnp.float32)
                out_ref[span(j)] = epilogue(total, span(j), rank, extras, aux, scratch)
                to_end(j).start()

            return carry

        lax.fori_loop(0, count + line_lag, step, 0)

        def drain(i, carry):
            to_middle(i).wait_send()
            to_end(i).wait_send()
            return carry

        lax.fori_loop(0, count, drain, 0)

    @pl.when(jnp.logical_not(inner))
    def _():
        def finish(i, carry):
            to_end(i).wait_recv()
            to_inner(i).wait_send()
            return carry

        lax.fori_loop(0, count, finish, 0)

    if ending is not None:
        ending(inner, end_peer, extras, aux, scratch)


def sum_line(
    part,
    extras,
    aux_shapes,
    epilogue,
    collective_id,
    prologue=None,
    scratch=(),
    opening=None,
    ending=None,
    rows=64,
):
    tokens, width = part.shape
    count = tokens // rows
    chunks = pltpu.VMEM((count, rows, width), jnp.bfloat16)
    return pl.pallas_call(
        functools.partial(
            sum_line_kernel,
            rows,
            count,
            opening,
            prologue,
            epilogue,
            ending,
            len(extras),
            len(aux_shapes),
            len(scratch),
        ),
        out_shape=[jax.ShapeDtypeStruct((tokens, width), jnp.bfloat16)] + list(aux_shapes),
        in_specs=[whole_vmem] * (1 + len(extras)),
        out_specs=[whole_vmem] * (1 + len(aux_shapes)),
        scratch_shapes=list(scratch)
        + [chunks, chunks, chunks]
        + [pltpu.SemaphoreType.DMA((count,))] * 5,
        compiler_params=pltpu.CompilerParams(
            collective_id=collective_id, has_side_effects=True, vmem_limit_bytes=48 << 20
        ),
    )(part, *extras)


def keep_total(total, span, rank, extras, aux, scratch):
    return total.astype(jnp.bfloat16)


def inverse_rms(values):
    return lax.rsqrt(jnp.mean(values * values, -1, keepdims=True) + norm_epsilon)


def finish_mixture(total, span, rank, extras, aux, scratch):
    stream_one, gain = extras
    stream_two = stream_one[span] + total
    aux[0][span] = stream_two
    return (stream_two * inverse_rms(stream_two) * gain[...]).astype(jnp.bfloat16)


def norm_back_rows(values, gain, upstream):
    inverse = inverse_rms(values)
    normed = values * inverse
    scaled = upstream * gain
    gain_grad = jnp.sum(upstream * normed, 0, keepdims=True)
    inputs_grad = inverse * (scaled - normed * jnp.mean(scaled * normed, -1, keepdims=True))
    return (inputs_grad, gain_grad)


def clear_gain(rank, inner, extras, aux, scratch):
    @pl.when(inner)
    def _():
        aux[-1][...] = jnp.zeros_like(aux[-1])


def share_gains(inner, end_peer, extras, aux, scratch):
    gains = aux[0]
    copy = pltpu.make_async_remote_copy(
        src_ref=gains,
        dst_ref=gains,
        send_sem=scratch[0],
        recv_sem=scratch[1],
        device_id={"tensor": end_peer},
        device_id_type=MESH_ID,
    )

    @pl.when(inner)
    def _():
        gains[1:2, :] = extras[3][...]
        gains[2:3, :] = extras[4][...]
        copy.start()
        copy.wait_send()

    @pl.when(jnp.logical_not(inner))
    def _():
        copy.wait_recv()


def finish_head_grad(total, span, rank, extras, aux, scratch):
    stream_two, gain = extras
    grad_two, gain_grad = norm_back_rows(stream_two[span], gain[...], total)
    aux[0][span] = grad_two
    aux[1][...] += gain_grad
    return grad_two.astype(jnp.bfloat16)


def gate_copies(rank, extras, scratch):
    gate_part = extras[3]
    landed, gate_send, gate_recv = scratch
    return [
        pltpu.make_async_remote_copy(
            src_ref=gate_part,
            dst_ref=landed.at[step - 1],
            send_sem=gate_send.at[step - 1],
            recv_sem=gate_recv.at[step - 1],
            device_id={"tensor": lax.rem(rank + step, 4)},
            device_id_type=MESH_ID,
        )
        for step in (1, 2, 3)
    ]


def send_gate_parts(rank, extras, scratch):
    for copy in gate_copies(rank, extras, scratch):
        copy.start()


def start_router_grad(rank, inner, extras, aux, scratch):
    stream_one, gain, grad_two, gate_part, gates, routes, router_low = extras
    grad_one, logit_grad, target_total, gain_grad = aux
    landed = scratch[0]
    clear_gain(rank, inner, extras, aux, scratch)
    for copy in gate_copies(rank, extras, scratch):
        copy.wait()
    gate_grad = jnp.zeros(gate_part.shape, jnp.float32)
    for source in range(4):
        piece = jnp.zeros(gate_part.shape, jnp.float32)
        for step in (1, 2, 3):
            piece = jnp.where(lax.rem(source + step, 4) == rank, landed[step - 1], piece)
        gate_grad = gate_grad + jnp.where(rank == source, gate_part[...], piece)
    target_total[...] = gate_grad[2:3]
    gate_grad = gate_grad[0:2]
    weighted = gates[...] * gate_grad
    chosen = gates[...] * (gate_grad - (weighted[0:1] + weighted[1:2]))
    experts, tokens = logit_grad.shape
    row = lax.broadcasted_iota(jnp.int32, (experts, tokens), 0)
    placed = jnp.where(row == routes[0:1], chosen[0:1], 0.0) + jnp.where(
        row == routes[1:2], chosen[1:2], 0.0
    )
    logit_grad[...] = placed.astype(jnp.bfloat16)

    @pl.when(inner)
    def _():
        grad_one[...] = lax.dot_general(
            logit_grad[...],
            router_low[...],
            (((0,), (1,)), ((), ())),
            preferred_element_type=jnp.float32,
        )


def finish_expert_grad(total, span, rank, extras, aux, scratch):
    stream_one, gain, grad_two, gate_part, gates, routes, router_low = extras
    grad_one, logit_grad, target_total, gain_grad = aux
    part, gain_part = norm_back_rows(
        stream_one[span], gain[...], total + grad_one[span]
    )
    result = grad_two[span] + part
    grad_one[span] = result
    gain_grad[...] += gain_part
    return result.astype(jnp.bfloat16)


def finish_input_grad(scale, total, span, rank, extras, aux, scratch):
    embedded, gain, grad_one = extras[:3]
    stream_zero = embedded[span].astype(jnp.float32) * scale
    part, gain_part = norm_back_rows(stream_zero, gain[...], total)
    aux[0][0:1, :] += gain_part
    return ((grad_one[span] + part) * scale).astype(jnp.bfloat16)


def gather_line_kernel(count, *refs):
    ins = refs[:count]
    outs = refs[count : 2 * count]
    local_sem, send_sem, recv_sem = refs[2 * count :]
    rank = lax.axis_index("tensor")
    barrier = pltpu.get_barrier_semaphore()
    for step in (1, 2, 3):
        other = lax.rem(rank + step, 4)
        pl.semaphore_signal(barrier, inc=1, device_id={"tensor": other}, device_id_type=MESH_ID)
    pl.semaphore_wait(barrier, 3)
    copies = []
    for k in range(count):
        for step in (1, 2, 3):
            copy = pltpu.make_async_remote_copy(
                src_ref=ins[k],
                dst_ref=outs[k].at[rank],
                send_sem=send_sem.at[k, step - 1],
                recv_sem=recv_sem.at[k, step - 1],
                device_id={"tensor": lax.rem(rank + step, 4)},
                device_id_type=MESH_ID,
            )
            copy.start()
            copies.append(copy)
        own = pltpu.make_async_copy(ins[k], outs[k].at[rank], local_sem.at[k])
        own.start()
        own.wait()
    for copy in copies:
        copy.wait()


def gather_line(arrays, collective_id):
    count = len(arrays)
    return pl.pallas_call(
        functools.partial(gather_line_kernel, count),
        out_shape=[jax.ShapeDtypeStruct((4,) + x.shape, x.dtype) for x in arrays],
        in_specs=[whole_vmem] * count,
        out_specs=[whole_vmem] * count,
        scratch_shapes=[
            pltpu.SemaphoreType.DMA((count,)),
            pltpu.SemaphoreType.DMA((count, 3)),
            pltpu.SemaphoreType.DMA((count, 3)),
        ],
        compiler_params=pltpu.CompilerParams(
            collective_id=collective_id, has_side_effects=True, vmem_limit_bytes=40 << 20
        ),
    )(*arrays)


def middle_kernel(
    attended_ref, project_ref, embedded_ref, gain_ref, router_ref, routes_ref,
    stream_ref, normed_ref, rows_ref, columns_ref,
):
    scale = math.sqrt(embedded_ref.shape[1])
    stream = embedded_ref[...].astype(jnp.float32) * scale + lax.dot_general(
        attended_ref[...], project_ref[...], (((0,), (0,)), ((), ())), preferred_element_type=jnp.float32
    )
    stream_ref[...] = stream
    normed = (stream * inverse_rms(stream) * gain_ref[...]).astype(jnp.bfloat16)
    normed_ref[...] = normed
    scores = lax.dot_general(
        router_ref[...], normed, (((1,), (1,)), ((), ())), preferred_element_type=jnp.float32
    )
    expert = lax.broadcasted_iota(jnp.int32, scores.shape, 0)
    first, second = (
        jnp.sum(jnp.where(expert == routes_ref[k : k + 1, :], scores, 0.0), 0, keepdims=True)
        for k in range(2)
    )
    top = jnp.maximum(first, second)
    first, second = jnp.exp(first - top), jnp.exp(second - top)
    total = first + second
    gates = jnp.concatenate([first / total, second / total], 0)
    rows_ref[...] = gates
    columns_ref[...] = jnp.concatenate([gates, jnp.zeros((6, gates.shape[1]), jnp.float32)], 0).T


def middle(attended, project, embedded, gain, router, routes):
    tokens, width = embedded.shape
    tile = 256
    fixed = lambda k: (0, 0)
    whole = lambda x: pl.BlockSpec(x.shape, fixed)
    down = lambda n: pl.BlockSpec((tile, n), lambda k: (k, 0))
    along = lambda n: pl.BlockSpec((n, tile), lambda k: (0, k))
    return pl.pallas_call(
        middle_kernel,
        grid=(tokens // tile,),
        out_shape=[
            jax.ShapeDtypeStruct((tokens, width), jnp.float32),
            jax.ShapeDtypeStruct((tokens, width), jnp.bfloat16),
            jax.ShapeDtypeStruct((2, tokens), jnp.float32),
            jax.ShapeDtypeStruct((tokens, 8), jnp.float32),
        ],
        in_specs=[along(width), whole(project), down(width), whole(gain), whole(router), along(2)],
        out_specs=[down(width), down(width), along(2), down(8)],
        compiler_params=pltpu.CompilerParams(vmem_limit_bytes=40 << 20),
    )(attended, project, embedded, gain, router, routes)


def gather_units_kernel(
    chunks, slots_ref, mine_ref, rows_ref, units_ref, looked_ref,
    held, total, send_x, recv_x, send_y, recv_y, send_z, recv_z, send_core, recv_core,
):
    chip, core = lax.axis_index("dp"), lax.axis_index("ctx")
    beside = chip + 1 - 2 * lax.rem(chip, 2)
    across = lax.rem(chip + 2, 4)
    opposite = across + 1 - 2 * lax.rem(across, 2)
    places = (chip, beside, across, opposite)
    slots, unit_rows, width = mine_ref.shape
    size = slots // chunks
    split = (chunks + 1) // 2
    tokens = rows_ref.shape[0]
    barrier = pltpu.get_barrier_semaphore()
    for place in ({"ctx": 1 - core}, {"dp": beside}, {"dp": across}):
        pl.semaphore_signal(barrier, inc=1, device_id=place, device_id_type=MESH_ID)
    pl.semaphore_wait(barrier, 3)

    def piece(place, which, q):
        return held.at[pl.ds((place * 2 + which) * slots + q * size, size)]

    def copy(place, q, send, recv, target):
        return pltpu.make_async_remote_copy(
            src_ref=piece(place, core, q),
            dst_ref=piece(place, core, q),
            send_sem=send,
            recv_sem=recv,
            device_id=target,
            device_id_type=MESH_ID,
        )

    def to_beside(q):
        return copy(chip, q, send_x.at[q], recv_x.at[q], {"dp": beside})

    def to_across(q):
        return copy(chip, q, send_y.at[q], recv_y.at[q], {"dp": across})

    def passed_on(q, source, target):
        return copy(source, q, send_z.at[q], recv_z.at[q], {"dp": target})

    def to_core(k, q):
        return copy(places[k], q, send_core.at[k, q], recv_core.at[k, q], {"ctx": 1 - core})

    held[pl.ds((chip * 2 + core) * slots, slots)] = mine_ref[...]

    def start(i, carry):
        to_beside(i).start()
        to_across(lax.rem(i + split, chunks)).start()
        return carry

    lax.fori_loop(0, chunks, start, 0)

    def start_core(q, carry):
        to_core(0, q).start()
        return carry

    lax.fori_loop(0, chunks, start_core, 0)
    total[...] = jnp.zeros_like(total)

    def look(place, which, first, count):
        lines = count * unit_rows
        begin = (place * 2 + which) * slots + first
        column = lax.broadcasted_iota(jnp.int32, (tokens, lines), 1) + begin * unit_rows
        hit = jnp.where(column == rows_ref[...], 1.0, 0.0).astype(jnp.bfloat16)
        block = held[pl.ds(begin, count)].reshape(lines, width)
        total[...] += jnp.dot(hit, block, preferred_element_type=jnp.float32)

    def look_block(place, which):
        def one(q, carry):
            look(place, which, q * size, size)
            return carry

        lax.fori_loop(0, chunks, one, 0)

    look_block(chip, core)

    def relay(i, carry):
        to_beside(i).wait_recv()

        @pl.when(i < split)
        def _():
            passed_on(i, beside, across).start()

        to_core(1, i).start()
        j = lax.rem(i + split, chunks)
        to_across(j).wait_recv()

        @pl.when(j >= split)
        def _():
            passed_on(j, across, beside).start()

        to_core(2, j).start()
        to_core(0, i).wait_recv()
        look(chip, 1 - core, i * size, size)
        return carry

    lax.fori_loop(0, chunks, relay, 0)
    look_block(beside, core)
    look_block(across, core)

    def last(q, carry):
        passed_on(q, opposite, opposite).wait_recv()
        to_core(3, q).start()
        to_core(1, q).wait_recv()
        look(beside, 1 - core, q * size, size)
        to_core(2, q).wait_recv()
        look(across, 1 - core, q * size, size)
        look(opposite, core, q * size, size)
        return carry

    lax.fori_loop(0, chunks, last, 0)

    def ending(q, carry):
        to_core(3, q).wait_recv()
        look(opposite, 1 - core, q * size, size)
        return carry

    lax.fori_loop(0, chunks, ending, 0)
    looked_ref[...] = total[...].astype(jnp.bfloat16)

    def place_unit(u, carry):
        units_ref[u] = held[slots_ref[u]]
        return carry

    lax.fori_loop(0, units_ref.shape[0], place_unit, 0)

    def finish(q, carry):
        to_beside(q).wait_send()
        to_across(q).wait_send()
        for k in range(4):
            to_core(k, q).wait_send()
        passed_on(q, opposite, opposite).wait_send()
        return carry

    lax.fori_loop(0, chunks, finish, 0)


def gather_units(unit_slots, mine, slot_rows, collective_id):
    slots = mine.shape[0]
    unit = mine.shape[1:]
    tokens = slot_rows.shape[0]
    chunks = max(k for k in range(1, 8) if slots % k == 0)
    sems = pltpu.SemaphoreType.DMA((chunks,))
    core_sems = pltpu.SemaphoreType.DMA((4, chunks))
    return pl.pallas_call(
        functools.partial(gather_units_kernel, chunks),
        out_shape=[
            jax.ShapeDtypeStruct((unit_slots.shape[0],) + unit, jnp.bfloat16),
            jax.ShapeDtypeStruct((tokens, unit[1]), jnp.bfloat16),
        ],
        in_specs=[pl.BlockSpec(memory_space=pltpu.SMEM), whole_vmem, whole_vmem],
        out_specs=[whole_vmem] * 2,
        scratch_shapes=[
            pltpu.VMEM((8 * slots,) + unit, jnp.bfloat16),
            pltpu.VMEM((tokens, unit[1]), jnp.float32),
        ]
        + [sems] * 6
        + [core_sems] * 2,
        compiler_params=pltpu.CompilerParams(
            collective_id=collective_id, has_side_effects=True, vmem_limit_bytes=56 << 20
        ),
    )(unit_slots, mine, slot_rows)


def pull_units_kernel(parts, slots_ref, *refs):
    sources, out_ref, sem = refs[:parts], refs[parts], refs[parts + 1]
    width = out_ref.shape[-1] // parts

    def push(u, carry):
        for part in range(parts):
            pltpu.make_async_copy(
                sources[part].at[slots_ref[u]],
                out_ref.at[u, :, part * width : (part + 1) * width],
                sem,
            ).start()
        return carry

    lax.fori_loop(0, out_ref.shape[0], push, 0)
    pltpu.make_async_copy(out_ref, out_ref, sem).wait()


def pull_units(sources, slots):
    count = slots.shape[0]
    rows, width = sources[0].shape[1:]
    return pl.pallas_call(
        functools.partial(pull_units_kernel, len(sources)),
        out_shape=jax.ShapeDtypeStruct((count, rows, width * len(sources)), sources[0].dtype),
        in_specs=[pl.BlockSpec(memory_space=pltpu.SMEM)] + [whole_any] * len(sources),
        out_specs=whole_vmem,
        scratch_shapes=[pltpu.SemaphoreType.DMA],
        compiler_params=pltpu.CompilerParams(vmem_limit_bytes=40 << 20),
    )(slots, *sources)


def attention_kernel(heads, size, bias_ref, own_ref, before_ref, out_ref, logsum_ref, scores, peak, total):
    tokens = own_ref.shape[1]
    blocks = tokens // BLOCK
    hidden = heads * size
    later = lax.axis_index("ctx") > 0

    for head in range(heads):
        query = own_ref[head * size : (head + 1) * size, :].astype(jnp.float32).T * size**-0.5
        query = query.astype(jnp.bfloat16)
        own_keys = own_ref[hidden + head * size : hidden + (head + 1) * size, :]
        old_keys = before_ref[head * size : (head + 1) * size, :]
        own_values = own_ref[2 * hidden + head * size : 2 * hidden + (head + 1) * size, :]
        own_values = own_values.astype(jnp.float32).T.astype(jnp.bfloat16)
        old_values = before_ref[hidden + head * size : hidden + (head + 1) * size, :]
        old_values = old_values.astype(jnp.float32).T.astype(jnp.bfloat16)
        for block in range(blocks):
            rows = query[block * BLOCK : (block + 1) * BLOCK]
            width = (block + 1) * BLOCK
            mine = jnp.dot(rows, own_keys[:, :width], preferred_element_type=jnp.float32)
            top = None
            parts = []
            for k in range(block + 1):
                part = mine[:, k * BLOCK : (k + 1) * BLOCK] + bias_ref[head, block - k]
                parts.append(part)
                high = jnp.max(part, 1, keepdims=True)
                top = high if top is None else jnp.maximum(top, high)
            peak[...] = top

            @pl.when(later)
            def _():
                old = jnp.dot(rows, old_keys, preferred_element_type=jnp.float32)
                top_old = None
                for k in range(blocks):
                    part = old[:, k * BLOCK : (k + 1) * BLOCK] + bias_ref[head, block + blocks - k]
                    scores[:, k * BLOCK : (k + 1) * BLOCK] = part
                    high = jnp.max(part, 1, keepdims=True)
                    top_old = high if top_old is None else jnp.maximum(top_old, high)
                peak[...] = jnp.maximum(peak[...], top_old)

            top = peak[...]
            parts = [jnp.exp(part - top) for part in parts]
            own_sum = None
            for part in parts:
                part_sum = jnp.sum(part, 1, keepdims=True)
                own_sum = part_sum if own_sum is None else own_sum + part_sum
            total[...] = own_sum

            @pl.when(later)
            def _():
                old_exp = jnp.exp(scores[...] - top)
                scores[...] = old_exp
                total[...] += jnp.sum(old_exp, 1, keepdims=True)

            full = total[...]
            inverse = 1.0 / full
            low = jnp.concatenate([(part * inverse).astype(jnp.bfloat16) for part in parts], 1)
            result = jnp.dot(low, own_values[:width], preferred_element_type=jnp.float32)
            peak[...] = top + jnp.log(full)
            logsum_ref[head, block * BLOCK : (block + 1) * BLOCK, :] = peak[...]
            place = (slice(head * size, (head + 1) * size), slice(block * BLOCK, (block + 1) * BLOCK))

            @pl.when(later)
            def _():
                low_old = (scores[...] * inverse).astype(jnp.bfloat16)
                both = result + jnp.dot(low_old, old_values, preferred_element_type=jnp.float32)
                out_ref[place] = both.T.astype(jnp.bfloat16)

            @pl.when(jnp.logical_not(later))
            def _():
                out_ref[place] = result.T.astype(jnp.bfloat16)


def attention(biases, own, before, heads, size):
    tokens = own.shape[1]
    return pl.pallas_call(
        functools.partial(attention_kernel, heads, size),
        out_shape=[
            jax.ShapeDtypeStruct((heads * size, tokens), jnp.bfloat16),
            jax.ShapeDtypeStruct((heads, tokens, 1), jnp.float32),
        ],
        in_specs=[pl.BlockSpec(memory_space=pltpu.SMEM), whole_vmem, whole_vmem],
        out_specs=[whole_vmem, whole_vmem],
        scratch_shapes=[
            pltpu.VMEM((BLOCK, tokens), jnp.float32),
            pltpu.VMEM((BLOCK, 1), jnp.float32),
            pltpu.VMEM((BLOCK, 1), jnp.float32),
        ],
        compiler_params=pltpu.CompilerParams(vmem_limit_bytes=40 << 20),
    )(biases, own, before)


def attention_back_kernel(
    heads, size, bias_ref, own_ref, before_ref, logsum_ref, grad_ref, project_ref,
    query_out, own_out, before_out, bias_out, probs, slopes, inner, query_sum, own_sum, before_sum,
):
    tokens = own_ref.shape[1]
    blocks = tokens // BLOCK
    hidden = heads * size
    later = lax.axis_index("ctx") > 0
    bias_out[...] = jnp.zeros_like(bias_out)

    def flipped(rows):
        return rows.astype(jnp.float32).T.astype(jnp.bfloat16)

    for head in range(heads):
        span = slice(head * size, (head + 1) * size)
        value_span = slice(hidden + head * size, hidden + (head + 1) * size)
        query_rows = own_ref[span, :]
        query = flipped(query_rows) * jnp.bfloat16(size**-0.5)
        own_keys = own_ref[hidden + head * size : hidden + (head + 1) * size, :]
        own_values = own_ref[2 * hidden + head * size : 2 * hidden + (head + 1) * size, :]
        old_keys = before_ref[span, :]
        old_values = before_ref[value_span, :]
        own_keys_flip = flipped(own_keys)
        grad = lax.dot_general(
            grad_ref[...], project_ref[span, :], (((1,), (1,)), ((), ())), preferred_element_type=jnp.float32
        )
        grad_rows = grad.T.astype(jnp.bfloat16)
        grad = grad.astype(jnp.bfloat16)
        own_sum[...] = jnp.zeros_like(own_sum)

        @pl.when(later)
        def _():
            before_sum[...] = jnp.zeros_like(before_sum)

        for block in range(blocks):
            at = slice(block * BLOCK, (block + 1) * BLOCK)
            width = (block + 1) * BLOCK
            rows, up = query[at], grad[at]
            lse = logsum_ref[head, at, :]
            score = jnp.dot(rows, own_keys[:, :width], preferred_element_type=jnp.float32)
            prob = jnp.concatenate(
                [
                    jnp.exp(score[:, k * BLOCK : (k + 1) * BLOCK] + (bias_ref[head, block - k] - lse))
                    for k in range(block + 1)
                ],
                1,
            )
            slope = jnp.dot(up, own_values[:, :width], preferred_element_type=jnp.float32)
            inner[...] = jnp.sum(prob * slope, 1, keepdims=True)

            @pl.when(later)
            def _():
                score = jnp.dot(rows, old_keys, preferred_element_type=jnp.float32)
                old_slope = jnp.dot(up, old_values, preferred_element_type=jnp.float32)
                old_prob = jnp.concatenate(
                    [
                        jnp.exp(
                            score[:, k * BLOCK : (k + 1) * BLOCK]
                            + (bias_ref[head, block + blocks - k] - lse)
                        )
                        for k in range(blocks)
                    ],
                    1,
                )
                probs[...] = old_prob
                slopes[...] = old_slope
                inner[...] += jnp.sum(old_prob * old_slope, 1, keepdims=True)

            row_inner = inner[...]
            low_grad = (prob * (slope - row_inner)).astype(jnp.bfloat16)
            query_sum[...] = jnp.dot(
                low_grad, own_keys_flip[:width], preferred_element_type=jnp.float32
            )
            own_sum[:size, :width] += jnp.dot(
                query_rows[:, at], low_grad, preferred_element_type=jnp.float32
            )
            own_sum[size:, :width] += jnp.dot(
                grad_rows[:, at], prob.astype(jnp.bfloat16), preferred_element_type=jnp.float32
            )
            for k in range(block + 1):
                line = head * 2 * blocks + block - k
                bias_out[line : line + 1, :] += jnp.sum(
                    low_grad[:, k * BLOCK : (k + 1) * BLOCK].astype(jnp.float32), 0, keepdims=True
                )

            @pl.when(later)
            def _():
                old_prob = probs[...]
                low_old = (old_prob * (slopes[...] - row_inner)).astype(jnp.bfloat16)
                query_sum[...] += jnp.dot(
                    low_old, flipped(old_keys), preferred_element_type=jnp.float32
                )
                before_sum[:size, :] += jnp.dot(
                    query_rows[:, at], low_old, preferred_element_type=jnp.float32
                )
                before_sum[size:, :] += jnp.dot(
                    grad_rows[:, at], old_prob.astype(jnp.bfloat16), preferred_element_type=jnp.float32
                )
                for k in range(blocks):
                    line = head * 2 * blocks + block + blocks - k
                    bias_out[line : line + 1, :] += jnp.sum(
                        low_old[:, k * BLOCK : (k + 1) * BLOCK].astype(jnp.float32), 0, keepdims=True
                    )

            query_out[span, at] = (query_sum[...].T * size**-0.5).astype(jnp.bfloat16)

        own_out[span, :] = own_sum[:size, :] * size**-0.5
        own_out[value_span, :] = own_sum[size:, :]

        @pl.when(later)
        def _():
            before_out[span, :] = (before_sum[:size, :] * size**-0.5).astype(jnp.bfloat16)
            before_out[value_span, :] = before_sum[size:, :].astype(jnp.bfloat16)

    @pl.when(jnp.logical_not(later))
    def _():
        before_out[...] = jnp.zeros_like(before_out)


def attention_back(biases, own, before, logsum, grad, project, heads, size):
    tokens = own.shape[1]
    hidden = heads * size
    return pl.pallas_call(
        functools.partial(attention_back_kernel, heads, size),
        out_shape=[
            jax.ShapeDtypeStruct((hidden, tokens), jnp.bfloat16),
            jax.ShapeDtypeStruct((2 * hidden, tokens), jnp.float32),
            jax.ShapeDtypeStruct((2 * hidden, tokens), jnp.bfloat16),
            jax.ShapeDtypeStruct((heads * 2 * (tokens // BLOCK), BLOCK), jnp.float32),
        ],
        in_specs=[pl.BlockSpec(memory_space=pltpu.SMEM)] + [whole_vmem] * 5,
        out_specs=[whole_vmem] * 4,
        scratch_shapes=[
            pltpu.VMEM((BLOCK, tokens), jnp.float32),
            pltpu.VMEM((BLOCK, tokens), jnp.float32),
            pltpu.VMEM((BLOCK, 1), jnp.float32),
            pltpu.VMEM((BLOCK, size), jnp.float32),
            pltpu.VMEM((2 * size, tokens), jnp.float32),
            pltpu.VMEM((2 * size, tokens), jnp.float32),
        ],
        compiler_params=pltpu.CompilerParams(vmem_limit_bytes=48 << 20),
    )(biases, own, before, logsum, grad, project)


def head_sums_kernel(table_ref, rows_ref, stats_ref, turned):
    @pl.when(pl.program_id(0) == 0)
    def _():
        turned[...] = rows_ref[...].astype(jnp.float32).T.astype(jnp.bfloat16)
        stats_ref[0:1, :] = jnp.full_like(stats_ref[0:1, :], masked_score)
        stats_ref[1:2, :] = jnp.zeros_like(stats_ref[1:2, :])

    logits = jnp.dot(table_ref[...], turned[...], preferred_element_type=jnp.float32)
    before = stats_ref[0:1, :]
    top = jnp.maximum(before, jnp.max(logits, 0, keepdims=True))
    stats_ref[1:2, :] = stats_ref[1:2, :] * jnp.exp(before - top) + jnp.sum(
        jnp.exp(logits - top), 0, keepdims=True
    )
    stats_ref[0:1, :] = top


def vocab_tile(vocab):
    return max(k for k in range(16, 1601, 16) if vocab % k == 0)


def head_sums(weights, rows, vocab):
    tokens, width = rows.shape
    tile = vocab_tile(vocab)
    return pl.pallas_call(
        head_sums_kernel,
        grid=(vocab // tile,),
        out_shape=jax.ShapeDtypeStruct((2, tokens), jnp.float32),
        in_specs=[pl.BlockSpec((tile, width), lambda k: (k, 0)), pl.BlockSpec((tokens, width), lambda k: (0, 0))],
        out_specs=pl.BlockSpec((2, tokens), lambda k: (0, 0)),
        scratch_shapes=[pltpu.VMEM((width, tokens), jnp.bfloat16)],
        compiler_params=pltpu.CompilerParams(vmem_limit_bytes=56 << 20),
    )(weights, rows)


def join_sums_kernel(stats_ref, logsum_ref, landed, send_sem, recv_sem):
    rank = lax.axis_index("tensor")
    barrier = pltpu.get_barrier_semaphore()
    for step in (1, 2, 3):
        other = lax.rem(rank + step, 4)
        pl.semaphore_signal(barrier, inc=1, device_id={"tensor": other}, device_id_type=MESH_ID)
    pl.semaphore_wait(barrier, 3)
    copies = []
    for step in (1, 2, 3):
        copy = pltpu.make_async_remote_copy(
            src_ref=stats_ref,
            dst_ref=landed.at[step - 1],
            send_sem=send_sem.at[step - 1],
            recv_sem=recv_sem.at[step - 1],
            device_id={"tensor": lax.rem(rank + step, 4)},
            device_id_type=MESH_ID,
        )
        copy.start()
        copies.append(copy)
    for copy in copies:
        copy.wait()
    tops, sums = [], []
    for source in range(4):
        piece = stats_ref[...]
        for step in (1, 2, 3):
            piece = jnp.where(lax.rem(source + step, 4) == rank, landed[step - 1], piece)
        tops.append(piece[0:1])
        sums.append(piece[1:2])
    top = jnp.maximum(jnp.maximum(tops[0], tops[1]), jnp.maximum(tops[2], tops[3]))
    total = sums[0] * jnp.exp(tops[0] - top)
    for source in (1, 2, 3):
        total = total + sums[source] * jnp.exp(tops[source] - top)
    logsum_ref[...] = top + jnp.log(total)


def join_sums(stats, collective_id):
    tokens = stats.shape[1]
    return pl.pallas_call(
        join_sums_kernel,
        out_shape=jax.ShapeDtypeStruct((1, tokens), jnp.float32),
        in_specs=[whole_vmem],
        out_specs=whole_vmem,
        scratch_shapes=[
            pltpu.VMEM((3, 2, tokens), jnp.float32),
            pltpu.SemaphoreType.DMA((3,)),
            pltpu.SemaphoreType.DMA((3,)),
        ],
        compiler_params=pltpu.CompilerParams(collective_id=collective_id, has_side_effects=True),
    )(stats)


def head_back_kernel(
    tile, table_ref, rows_ref, logsum_ref, wanted_ref, weight_ref, slope_ref, grad_ref, picked_ref, turned
):
    step = pl.program_id(0)

    @pl.when(step == 0)
    def _():
        turned[...] = rows_ref[...].astype(jnp.float32).T.astype(jnp.bfloat16)
        picked_ref[...] = jnp.zeros_like(picked_ref)
        grad_ref[...] = jnp.zeros_like(grad_ref)

    logits = jnp.dot(table_ref[...], turned[...], preferred_element_type=jnp.float32)
    row = lax.broadcasted_iota(jnp.int32, logits.shape, 0)
    base = step * tile
    hits = jnp.where(row == wanted_ref[0:1, :] - base, weight_ref[0:1, :], 0.0) + jnp.where(
        row == wanted_ref[1:2, :] - base, weight_ref[1:2, :], 0.0
    )
    picked_ref[...] += jnp.sum(hits * logits, 0, keepdims=True)
    softmax = jnp.exp(logits - logsum_ref[...])
    slope = ((weight_ref[2:3, :] * softmax - hits) * weight_ref[3:4, :]).astype(jnp.bfloat16)
    slope_ref[...] = slope
    grad_ref[...] += lax.dot_general(
        slope, table_ref[...], (((0,), (0,)), ((), ())), preferred_element_type=jnp.float32
    )


def head_back(weights, rows, logsum, wanted, weight_rows, vocab):
    tokens, width = rows.shape
    tile = vocab_tile(vocab)
    fixed = lambda k: (0, 0)
    return pl.pallas_call(
        functools.partial(head_back_kernel, tile),
        grid=(vocab // tile,),
        out_shape=[
            jax.ShapeDtypeStruct((vocab, tokens), jnp.bfloat16),
            jax.ShapeDtypeStruct((tokens, width), jnp.float32),
            jax.ShapeDtypeStruct((1, tokens), jnp.float32),
        ],
        in_specs=[
            pl.BlockSpec((tile, width), lambda k: (k, 0)),
            pl.BlockSpec((tokens, width), fixed),
            pl.BlockSpec((1, tokens), fixed),
            pl.BlockSpec((2, tokens), fixed),
            pl.BlockSpec((4, tokens), fixed),
        ],
        out_specs=[
            pl.BlockSpec((tile, tokens), lambda k: (k, 0)),
            pl.BlockSpec((tokens, width), fixed),
            pl.BlockSpec((1, tokens), fixed),
        ],
        scratch_shapes=[pltpu.VMEM((width, tokens), jnp.bfloat16)],
        compiler_params=pltpu.CompilerParams(vmem_limit_bytes=60 << 20),
    )(weights, rows, logsum, wanted, weight_rows)


def weight_grads_kernel(
    tile_units, tiles, place_ref, slope_ref, rows_ref, ids_ref, zero_ref, joint_ref, normed_ref,
    attended_ref, grad_ref, *refs
):
    states, (out_ref, *updated), (made, sem) = refs[:8], refs[8:15], refs[15:]
    step = pl.program_id(0)
    for k, rate in enumerate((rate_inner, rate_outer)):
        fresh = adam_update(*(state[...] for state in states[4 * k : 4 * k + 4]), rate, decay_rate)
        for n in range(3):
            updated[3 * k + n][...] = fresh[n]
    unit_rows = out_ref.shape[1]
    buffer = lax.rem(step, 2)
    last_units = joint_ref.shape[0] // unit_rows + attended_ref.shape[0] // unit_rows

    def settle(which, count):
        pltpu.make_async_copy(
            made.at[which, pl.ds(0, count)], made.at[which, pl.ds(0, count)], sem.at[which]
        ).wait()

    def send(first, count):
        def push(u, carry):
            pltpu.make_async_copy(
                made.at[buffer, u], out_ref.at[place_ref[first + u]], sem.at[buffer]
            ).start()
            return carry

        lax.fori_loop(0, count, push, 0)

    @pl.when(step >= 2)
    def _():
        settle(buffer, tile_units)

    @pl.when(step < tiles)
    def _():
        row = lax.broadcasted_iota(jnp.int32, slope_ref.shape, 0)
        seen = jnp.where(row == ids_ref[...] - step * slope_ref.shape[0], 1.0, 0.0).astype(jnp.bfloat16)
        made[buffer] = (
            jnp.dot(slope_ref[...], rows_ref[...], preferred_element_type=jnp.float32)
            + jnp.dot(seen, zero_ref[...], preferred_element_type=jnp.float32)
        ).astype(jnp.bfloat16).reshape(tile_units, unit_rows, -1)
        send(step * tile_units, tile_units)

    @pl.when(step == tiles)
    def _():
        joint_units = joint_ref.shape[0] // unit_rows
        made[buffer, pl.ds(0, joint_units)] = jnp.dot(
            joint_ref[...], normed_ref[...], preferred_element_type=jnp.float32
        ).astype(jnp.bfloat16).reshape(joint_units, unit_rows, -1)
        made[buffer, pl.ds(joint_units, last_units - joint_units)] = jnp.dot(
            attended_ref[...], grad_ref[...], preferred_element_type=jnp.float32
        ).astype(jnp.bfloat16).reshape(last_units - joint_units, unit_rows, -1)
        send(tiles * tile_units, last_units)
        settle(1 - buffer, tile_units)
        settle(buffer, last_units)


def weight_grads(
    place, slots, unit_rows, slope, rows, ids, zero, joint, normed, attended, grad, states
):
    vocab, tokens = slope.shape
    width = rows.shape[1]
    tile = vocab_tile(vocab)
    tiles = vocab // tile
    fixed = lambda k: (0, 0)
    whole = lambda x: pl.BlockSpec(x.shape, fixed)
    piece = pl.BlockSpec((states[0].shape[0] // (tiles + 1), states[0].shape[1]), lambda k: (k, 0))
    return pl.pallas_call(
        functools.partial(weight_grads_kernel, tile // unit_rows, tiles),
        grid=(tiles + 1,),
        out_shape=[jax.ShapeDtypeStruct((slots, unit_rows, width), jnp.bfloat16)]
        + [jax.ShapeDtypeStruct(states[0].shape, jnp.float32)] * 6,
        in_specs=[
            pl.BlockSpec(memory_space=pltpu.SMEM),
            pl.BlockSpec((tile, tokens), lambda k: (jnp.minimum(k, tiles - 1), 0)),
        ]
        + [whole(x) for x in (rows, ids, zero, joint, normed, attended, grad)]
        + [piece] * 8,
        out_specs=[whole_any] + [piece] * 6,
        scratch_shapes=[
            pltpu.VMEM((2, tile // unit_rows, unit_rows, width), jnp.bfloat16),
            pltpu.SemaphoreType.DMA((2,)),
        ],
        compiler_params=pltpu.CompilerParams(vmem_limit_bytes=60 << 20),
    )(place, slope, rows, ids, zero, joint, normed, attended, grad, *states)


def adam_update(weight, moment_one, moment_two, gradient, step_rate, decay_factor):
    moment_new = beta_first * moment_one + (1.0 - beta_first) * gradient
    square_new = beta_second * moment_two + (1.0 - beta_second) * gradient * gradient
    moment_hat = moment_new / (1.0 - beta_first**STEP)
    square_hat = square_new / (1.0 - beta_second**STEP)
    weight_new = weight - step_rate * (
        moment_hat / (jnp.sqrt(square_hat) + adam_epsilon) + decay_factor * weight
    )
    return (weight_new, moment_new, square_new)


def norm_forward(values, gain_row):
    return values * inverse_rms(values) * gain_row


def slot_tables(owner_ids, owners, most_units):
    unit_count = owner_ids.shape[0]
    unit_index = jnp.arange(unit_count, dtype=jnp.int32)
    earlier = (owner_ids[None, :] == owner_ids[:, None]) & (
        unit_index[None, :] < unit_index[:, None]
    )
    unit_rank = jnp.sum(earlier.astype(jnp.int32), 1)
    placed = (owner_ids[None, None, :] == jnp.arange(owners, dtype=jnp.int32)[:, None, None]) & (
        unit_rank[None, None, :] == jnp.arange(most_units, dtype=jnp.int32)[None, :, None]
    )
    slot_filled = jnp.any(placed, 2)
    slot_unit = jnp.sum(jnp.where(placed, unit_index[None, None, :], 0), 2)
    return (unit_rank, slot_unit, slot_filled)


def unit_rates(unit_ids, table_units, query_units, value_units):
    return jnp.where(
        unit_ids < table_units,
        rate_table,
        jnp.where(
            unit_ids < query_units,
            rate_query,
            jnp.where(unit_ids < value_units, rate_values, rate_project),
        ),
    )


def pair_slots(route_pairs, priorities, experts, capacity):
    tokens_here = priorities.shape[0]
    pair_expert = route_pairs.T.reshape(-1)
    pair_key = (
        jnp.arange(2, dtype=jnp.int32)[:, None] * tokens_here + priorities[None, :]
    ).reshape(-1)
    before = (pair_expert[None, :] == pair_expert[:, None]) & (
        pair_key[None, :] < pair_key[:, None]
    )
    pair_rank = jnp.sum(before.astype(jnp.int32), 1)
    pair_kept = pair_rank < capacity
    pair_dest = pair_expert * capacity + jnp.minimum(pair_rank, capacity - 1)
    return (pair_kept, pair_dest)


def gelu_tanh(values):
    return jax.nn.gelu(values, approximate=True)


def gelu_slope(values):
    root = math.sqrt(2.0 / math.pi)
    bent = jnp.tanh(root * (values + 0.044715 * values * values * values))
    return 0.5 * (1.0 + bent) + 0.5 * values * (1.0 - bent * bent) * root * (
        1.0 + 3.0 * 0.044715 * values * values
    )


def plane_peer(step):
    chip, core = lax.axis_index("dp"), lax.axis_index("ctx")
    row = lax.rem(chip // 2 + step // 4, 2)
    column = lax.rem(lax.rem(chip, 2) + lax.rem(step // 2, 2), 2)
    place = {"dp": row * 2 + column, "ctx": lax.rem(core + lax.rem(step, 2), 2)}
    return place, place["dp"] * 2 + place["ctx"]


def greet_plane():
    barrier = pltpu.get_barrier_semaphore()
    for step in range(1, 8):
        place, _ = plane_peer(step)
        pl.semaphore_signal(barrier, inc=1, device_id=place, device_id_type=MESH_ID)
    pl.semaphore_wait(barrier, 7)


def plane_copy(source, target, send_sem, recv_sem, step):
    place, _ = plane_peer(step)
    return pltpu.make_async_remote_copy(
        src_ref=source.at[step],
        dst_ref=target.at[step],
        send_sem=send_sem.at[step],
        recv_sem=recv_sem.at[step],
        device_id=place,
        device_id_type=MESH_ID,
    )


def slot_hits(dest_rows, expert, capacity, tokens):
    slot = lax.broadcasted_iota(jnp.int32, (capacity, tokens), 0) + expert * capacity
    return (slot == dest_rows[0:1, :]) | (slot == dest_rows[1:2, :])


def token_hits(dest_columns, expert, capacity, tokens):
    slot = lax.broadcasted_iota(jnp.int32, (tokens, capacity), 1) + expert * capacity
    hit = (slot == dest_columns[:, 0:1]) | (slot == dest_columns[:, 1:2])
    return jnp.where(hit, 1.0, 0.0).astype(jnp.bfloat16)


def gate_of(routes, gates, expert, axis):
    pick = (lambda a, k: a[k : k + 1, :]) if axis == 0 else (lambda a, k: a[:, k : k + 1])
    return jnp.where(pick(routes, 0) == expert, pick(gates, 0), 0.0) + jnp.where(
        pick(routes, 1) == expert, pick(gates, 1), 0.0
    )


def arrival(i):
    return jnp.where(i < 2, i, 9 - i)


def experts_kernel(
    rows_ref, dest_rows, dest_columns, gates, routes, inner_ref, outer_ref, counts_ref,
    mix_ref, arrived, returned, totals_ref,
    outgoing, results, counts, send_one, recv_one, send_two, recv_two, send_count, recv_count,
):
    capacity = arrived.shape[1]
    tokens = rows_ref.shape[0]
    greet_plane()
    counts[0] = counts_ref[...]

    def send_counts(step, carry):
        place, _ = plane_peer(step)
        pltpu.make_async_remote_copy(
            src_ref=counts_ref,
            dst_ref=counts.at[step],
            send_sem=send_count.at[step],
            recv_sem=recv_count.at[step],
            device_id=place,
            device_id_type=MESH_ID,
        ).start()
        return carry

    def dispatch(i, carry):
        step = 7 - i
        _, expert = plane_peer(step)
        hit = jnp.where(slot_hits(dest_rows, expert, capacity, tokens), 1.0, 0.0).astype(jnp.bfloat16)
        rows = jnp.dot(hit, rows_ref[...], preferred_element_type=jnp.float32).astype(jnp.bfloat16)

        @pl.when(step > 0)
        def _():
            outgoing[step] = rows
            plane_copy(outgoing, arrived, send_one, recv_one, step).start()

        @pl.when(step == 0)
        def _():
            arrived[0] = rows

        return carry

    def work(i, carry):
        step = arrival(i)

        @pl.when(step > 0)
        def _():
            plane_copy(outgoing, arrived, send_one, recv_one, step).wait_recv()

        before = jnp.dot(arrived[step], inner_ref[...], preferred_element_type=jnp.float32)
        active = gelu_tanh(before).astype(jnp.bfloat16)
        part = jnp.dot(active, outer_ref[...], preferred_element_type=jnp.float32).astype(jnp.bfloat16)

        @pl.when(step > 0)
        def _():
            results[step] = part
            plane_copy(results, returned, send_two, recv_two, step).start()

        @pl.when(step == 0)
        def _():
            returned[0] = part

        return carry

    def combine(i, carry):
        step = arrival(i)
        _, expert = plane_peer(step)
        hit = token_hits(dest_columns, expert, capacity, tokens)
        gate = gate_of(routes, gates, expert, 1)

        @pl.when(step > 0)
        def _():
            plane_copy(results, returned, send_two, recv_two, step).wait_recv()

        part = gate * jnp.dot(hit, returned[step], preferred_element_type=jnp.float32)

        @pl.when(i == 0)
        def _():
            mix_ref[...] = part

        @pl.when(i > 0)
        def _():
            mix_ref[...] += part

        return carry

    def finish(step, carry):
        plane_copy(outgoing, arrived, send_one, recv_one, step).wait_send()
        plane_copy(results, returned, send_two, recv_two, step).wait_send()
        place, _ = plane_peer(step)
        pltpu.make_async_remote_copy(
            src_ref=counts_ref,
            dst_ref=counts.at[step],
            send_sem=send_count.at[step],
            recv_sem=recv_count.at[step],
            device_id=place,
            device_id_type=MESH_ID,
        ).wait()
        return carry

    lax.fori_loop(0, 8, dispatch, 0)
    lax.fori_loop(1, 8, send_counts, 0)
    lax.fori_loop(0, 8, work, 0)
    lax.fori_loop(0, 8, combine, 0)
    lax.fori_loop(1, 8, finish, 0)
    totals_ref[...] = jnp.sum(counts[...], 0)


def experts_forward(rows, dest, gates, routes, inner, outer, counts, capacity, collective_id):
    tokens, width = rows.shape
    buffer = pltpu.VMEM((8, capacity, width), jnp.bfloat16)
    return pl.pallas_call(
        experts_kernel,
        out_shape=[
            jax.ShapeDtypeStruct((tokens, width), jnp.float32),
            jax.ShapeDtypeStruct((8, capacity, width), jnp.bfloat16),
            jax.ShapeDtypeStruct((8, capacity, width), jnp.bfloat16),
            jax.ShapeDtypeStruct(counts.shape, jnp.float32),
        ],
        in_specs=[whole_vmem] * 8,
        out_specs=[whole_vmem] * 4,
        scratch_shapes=[buffer, buffer, pltpu.VMEM((8,) + counts.shape, jnp.float32)]
        + [pltpu.SemaphoreType.DMA((8,))] * 6,
        compiler_params=pltpu.CompilerParams(
            collective_id=collective_id, has_side_effects=True, vmem_limit_bytes=60 << 20
        ),
    )(rows, dest, dest.T, gates, routes, inner, outer, counts)


def experts_back_kernel(
    rows_ref, dest_rows, dest_columns, gates, routes, returned, arrived, *refs
):
    inner_ref, outer_ref, grad_ref, gate_ref, inner_grad, outer_grad = refs[:6]
    outgoing, landed, results, landed_two, active, slopes = refs[6:12]
    send_one, recv_one, send_two, recv_two = refs[12:]
    capacity = arrived.shape[1]
    tokens = rows_ref.shape[0]
    greet_plane()
    gate_ref[...] = jnp.zeros_like(gate_ref)

    def dispatch(i, carry):
        step = 7 - i
        _, expert = plane_peer(step)
        hit = slot_hits(dest_rows, expert, capacity, tokens)
        rows = jnp.dot(
            jnp.where(hit, 1.0, 0.0).astype(jnp.bfloat16), rows_ref[...], preferred_element_type=jnp.float32
        )
        scale = jnp.sum(jnp.where(hit, gate_of(routes, gates, expert, 0), 0.0), 1, keepdims=True)
        sent = (rows * scale).astype(jnp.bfloat16)

        @pl.when(step > 0)
        def _():
            outgoing[step] = sent
            plane_copy(outgoing, landed, send_one, recv_one, step).start()

        @pl.when(step == 0)
        def _():
            landed[0] = sent

        dots = jnp.sum(rows * returned[step].astype(jnp.float32), 1, keepdims=True)
        part = jnp.sum(jnp.where(hit, dots, 0.0), 0, keepdims=True)
        for k in range(2):
            gate_ref[k : k + 1, :] += jnp.where(routes[k : k + 1, :] == expert, part, 0.0)
        return carry

    def work(i, carry):
        step = arrival(i)

        @pl.when(step > 0)
        def _():
            plane_copy(outgoing, landed, send_one, recv_one, step).wait_recv()

        grad_active = lax.dot_general(
            landed[step], outer_ref[...], (((1,), (1,)), ((), ())), preferred_element_type=jnp.float32
        )
        before = jnp.dot(arrived[step], inner_ref[...], preferred_element_type=jnp.float32)
        slope = (grad_active * gelu_slope(before)).astype(jnp.bfloat16)
        back = lax.dot_general(
            slope, inner_ref[...], (((1,), (1,)), ((), ())), preferred_element_type=jnp.float32
        ).astype(jnp.bfloat16)

        @pl.when(step > 0)
        def _():
            results[step] = back
            plane_copy(results, landed_two, send_two, recv_two, step).start()

        @pl.when(step == 0)
        def _():
            landed_two[0] = back

        slopes[step] = slope
        active[step] = gelu_tanh(before).astype(jnp.bfloat16)
        return carry

    def weigh(step, carry):
        outer_part = lax.dot_general(
            active[step], landed[step], (((0,), (0,)), ((), ())), preferred_element_type=jnp.float32
        )
        inner_part = lax.dot_general(
            arrived[step], slopes[step], (((0,), (0,)), ((), ())), preferred_element_type=jnp.float32
        )

        @pl.when(step == 0)
        def _():
            inner_grad[...] = inner_part
            outer_grad[...] = outer_part

        @pl.when(step > 0)
        def _():
            inner_grad[...] += inner_part
            outer_grad[...] += outer_part

        return carry

    def combine(i, carry):
        step = arrival(i)
        _, expert = plane_peer(step)
        hit = token_hits(dest_columns, expert, capacity, tokens)

        @pl.when(step > 0)
        def _():
            plane_copy(results, landed_two, send_two, recv_two, step).wait_recv()

        part = jnp.dot(hit, landed_two[step], preferred_element_type=jnp.float32)

        @pl.when(i == 0)
        def _():
            grad_ref[...] = part

        @pl.when(i > 0)
        def _():
            grad_ref[...] += part

        return carry

    def finish(step, carry):
        plane_copy(outgoing, landed, send_one, recv_one, step).wait_send()
        plane_copy(results, landed_two, send_two, recv_two, step).wait_send()
        return carry

    lax.fori_loop(0, 8, dispatch, 0)
    lax.fori_loop(0, 8, work, 0)
    lax.fori_loop(0, 8, weigh, 0)
    lax.fori_loop(0, 8, combine, 0)
    lax.fori_loop(1, 8, finish, 0)


def experts_backward(rows, dest, gates, routes, returned, arrived, inner, outer, collective_id):
    tokens, width = rows.shape
    capacity = arrived.shape[1]
    inside = inner.shape[1]
    buffer = pltpu.VMEM((8, capacity, width), jnp.bfloat16)
    inside_buffer = pltpu.VMEM((8, capacity, inside), jnp.bfloat16)
    return pl.pallas_call(
        experts_back_kernel,
        out_shape=[
            jax.ShapeDtypeStruct((tokens, width), jnp.float32),
            jax.ShapeDtypeStruct((2, tokens), jnp.float32),
            jax.ShapeDtypeStruct((width, inside), jnp.float32),
            jax.ShapeDtypeStruct((inside, width), jnp.float32),
        ],
        in_specs=[whole_vmem] * 9,
        out_specs=[whole_vmem] * 4,
        scratch_shapes=[buffer] * 4 + [inside_buffer] * 2 + [pltpu.SemaphoreType.DMA((8,))] * 4,
        compiler_params=pltpu.CompilerParams(
            collective_id=collective_id, has_side_effects=True, vmem_limit_bytes=60 << 20
        ),
    )(rows, dest, dest.T, gates, routes, returned, arrived, inner, outer)


def own_units_kernel(
    chunks, parts_ref, small_ref, grads_ref, small_out,
    own, other, relay, landed, small_landed,
    own_sem, other_send, other_recv, relay_send, relay_recv, landed_send, landed_recv, small_send, small_recv,
):
    chip, core = lax.axis_index("dp"), lax.axis_index("ctx")
    beside = chip + 1 - 2 * lax.rem(chip, 2)
    across = lax.rem(chip + 2, 4)
    opposite = across + 1 - 2 * lax.rem(across, 2)
    places = (opposite, beside, across, chip)
    slots = grads_ref.shape[0]
    size = slots // chunks
    split = (chunks + 1) // 2
    greet_plane()

    def span(q):
        return pl.ds(q * size, size)

    def fetch(k):
        first = (places[k] * 2 + core) * slots
        return pltpu.make_async_copy(parts_ref.at[pl.ds(first, slots)], own.at[k], own_sem.at[k])

    def pass_over(k, q):
        first = (places[k] * 2 + 1 - core) * slots + q * size
        return pltpu.make_async_remote_copy(
            src_ref=parts_ref.at[pl.ds(first, size)],
            dst_ref=other.at[k, span(q)],
            send_sem=other_send.at[k, q],
            recv_sem=other_recv.at[k, q],
            device_id={"ctx": 1 - core},
            device_id_type=MESH_ID,
        )

    def to_relay(q, place):
        return pltpu.make_async_remote_copy(
            src_ref=own.at[0, span(q)],
            dst_ref=relay.at[span(q)],
            send_sem=relay_send.at[q],
            recv_sem=relay_recv.at[q],
            device_id={"dp": place},
            device_id_type=MESH_ID,
        )

    def to_owner(k, q):
        return pltpu.make_async_remote_copy(
            src_ref=own.at[k, span(q)],
            dst_ref=landed.at[k - 1, span(q)],
            send_sem=landed_send.at[k - 1, q],
            recv_sem=landed_recv.at[k - 1, q],
            device_id={"dp": places[k]},
            device_id_type=MESH_ID,
        )

    def small_copy(step):
        place, _ = plane_peer(step)
        return pltpu.make_async_remote_copy(
            src_ref=small_ref,
            dst_ref=small_landed.at[chip * 2 + core],
            send_sem=small_send.at[step],
            recv_sem=small_recv.at[step],
            device_id=place,
            device_id_type=MESH_ID,
        )

    for k in range(4):
        fetch(k).start()

        def start(q, carry):
            pass_over(k, q).start()
            return carry

        lax.fori_loop(0, chunks, start, 0)

    def joined(k, q):
        pass_over(k, q).wait_recv()
        return own[k, span(q)].astype(jnp.float32) + other[k, span(q)].astype(jnp.float32)

    fetch(0).wait()

    def first_leg(place):
        def leg(q, carry):
            own[0, span(q)] = joined(0, q).astype(jnp.bfloat16)
            to_relay(q, place).start()
            return carry

        return leg

    lax.fori_loop(0, split, first_leg(beside), 0)
    lax.fori_loop(split, chunks, first_leg(across), 0)
    lax.fori_loop(1, 8, lambda step, carry: (small_copy(step).start(), carry)[1], 0)
    small_landed[chip * 2 + core] = small_ref[...]
    fetch(1).wait()
    fetch(2).wait()

    def direct(k):
        def leg(q, carry):
            own[k, span(q)] = joined(k, q).astype(jnp.bfloat16)
            to_owner(k, q).start()
            return carry

        return leg

    def relayed(k, place):
        def leg(q, carry):
            to_relay(q, place).wait_recv()
            total = joined(k, q) + relay[span(q)].astype(jnp.float32)
            own[k, span(q)] = total.astype(jnp.bfloat16)
            to_owner(k, q).start()
            return carry

        return leg

    lax.fori_loop(0, split, direct(1), 0)
    lax.fori_loop(split, chunks, direct(2), 0)
    lax.fori_loop(0, split, relayed(2, beside), 0)
    lax.fori_loop(split, chunks, relayed(1, across), 0)
    fetch(3).wait()

    def keep(q, carry):
        total = joined(3, q)
        to_owner(1, q).wait_recv()
        to_owner(2, q).wait_recv()
        grads_ref[span(q)] = (
            total + landed[0, span(q)].astype(jnp.float32) + landed[1, span(q)].astype(jnp.float32)
        )
        return carry

    lax.fori_loop(0, split, keep, 0)
    lax.fori_loop(split, chunks, keep, 0)

    def finish(q, carry):
        for k in range(4):
            pass_over(k, q).wait_send()
        to_owner(1, q).wait_send()
        to_owner(2, q).wait_send()
        return carry

    lax.fori_loop(0, chunks, finish, 0)
    lax.fori_loop(0, split, lambda q, carry: (to_relay(q, beside).wait_send(), carry)[1], 0)
    lax.fori_loop(split, chunks, lambda q, carry: (to_relay(q, across).wait_send(), carry)[1], 0)
    lax.fori_loop(1, 8, lambda step, carry: (small_copy(step).wait(), carry)[1], 0)
    total = small_landed[0]
    for source in range(1, 8):
        total = total + small_landed[source]
    small_out[...] = total


def own_units(parts, small, slots, collective_id):
    unit = parts.shape[1:]
    chunks = max(k for k in range(1, 8) if slots % k == 0)
    block = pltpu.VMEM((4, slots) + unit, jnp.bfloat16)
    return pl.pallas_call(
        functools.partial(own_units_kernel, chunks),
        out_shape=[
            jax.ShapeDtypeStruct((slots,) + unit, jnp.float32),
            jax.ShapeDtypeStruct(small.shape, jnp.float32),
        ],
        in_specs=[whole_any, whole_vmem],
        out_specs=[whole_vmem] * 2,
        scratch_shapes=[
            block,
            block,
            pltpu.VMEM((slots,) + unit, jnp.bfloat16),
            pltpu.VMEM((2, slots) + unit, jnp.bfloat16),
            pltpu.VMEM((8,) + small.shape, jnp.float32),
            pltpu.SemaphoreType.DMA((4,)),
            pltpu.SemaphoreType.DMA((4, chunks)),
            pltpu.SemaphoreType.DMA((4, chunks)),
            pltpu.SemaphoreType.DMA((chunks,)),
            pltpu.SemaphoreType.DMA((chunks,)),
            pltpu.SemaphoreType.DMA((2, chunks)),
            pltpu.SemaphoreType.DMA((2, chunks)),
            pltpu.SemaphoreType.DMA((8,)),
            pltpu.SemaphoreType.DMA((8,)),
        ],
        compiler_params=pltpu.CompilerParams(
            collective_id=collective_id, has_side_effects=True, vmem_limit_bytes=56 << 20
        ),
    )(parts, small)


def to_plane(buffer):
    return lax.all_to_all(buffer, ("dp", "ctx"), split_axis=0, concat_axis=0, tiled=True)


def plain_hits(dest, experts, capacity):
    slots = lax.broadcasted_iota(jnp.int32, (experts * capacity, dest.shape[1]), 0)
    return [slots == dest[k : k + 1] for k in range(2)]


def plain_forward(rows, dest, gates, inner, outer, owners, capacity):
    width = rows.shape[1]
    hits = plain_hits(dest, owners, capacity)
    both = (hits[0] | hits[1]).astype(jnp.bfloat16)
    sent = jnp.dot(both, rows, preferred_element_type=jnp.float32).astype(jnp.bfloat16)
    arrived = to_plane(sent.reshape(owners, capacity, width))
    hidden = jnp.einsum("ocd,df->ocf", arrived, inner, preferred_element_type=jnp.float32)
    active = gelu_tanh(hidden).astype(jnp.bfloat16)
    part = jnp.einsum("ocf,fd->ocd", active, outer, preferred_element_type=jnp.float32)
    returned = to_plane(part.astype(jnp.bfloat16))
    flat = returned.reshape(owners * capacity, width)
    mix = sum(
        gates[:, k : k + 1]
        * lax.dot_general(
            hits[k].astype(jnp.bfloat16),
            flat,
            (((0,), (0,)), ((), ())),
            preferred_element_type=jnp.float32,
        )
        for k in range(2)
    )
    return (mix, arrived, returned)


def plain_backward(rows, dest, gates, returned, arrived, inner, outer):
    owners, capacity, width = arrived.shape
    hits = plain_hits(dest, owners, capacity)
    both = (hits[0] | hits[1]).astype(jnp.bfloat16)
    slot_scale = jnp.sum(
        jnp.where(hits[0], gates[0:1], 0.0) + jnp.where(hits[1], gates[1:2], 0.0), 1, keepdims=True
    )
    slot_grads = jnp.dot(both, rows, preferred_element_type=jnp.float32)
    sent = (slot_grads * slot_scale).astype(jnp.bfloat16)
    flat = returned.reshape(owners * capacity, width)
    dots = jnp.sum(slot_grads * flat.astype(jnp.float32), 1, keepdims=True)
    gate_part = jnp.concatenate(
        [jnp.sum(jnp.where(hit, dots, 0.0), 0, keepdims=True) for hit in hits], 0
    )
    landed = to_plane(sent.reshape(owners, capacity, width))
    grad_active = jnp.einsum("ocd,fd->ocf", landed, outer, preferred_element_type=jnp.float32)
    hidden = jnp.einsum("ocd,df->ocf", arrived, inner, preferred_element_type=jnp.float32)
    active = gelu_tanh(hidden).astype(jnp.bfloat16)
    slope = (grad_active * gelu_slope(hidden)).astype(jnp.bfloat16)
    outer_grad = jnp.einsum("ocf,ocd->fd", active, landed, preferred_element_type=jnp.float32)
    inner_grad = jnp.einsum("ocd,ocf->df", arrived, slope, preferred_element_type=jnp.float32)
    back = jnp.einsum("ocf,df->ocd", slope, inner, preferred_element_type=jnp.float32)
    back = to_plane(back.astype(jnp.bfloat16)).reshape(owners * capacity, width)
    grad = lax.dot_general(
        both, back, (((0,), (0,)), ((), ())), preferred_element_type=jnp.float32
    )
    return (grad, gate_part, inner_grad, outer_grad)


def on_device(
    token_ids,
    targets,
    counted,
    routes,
    priority,
    owner_of,
    master,
    master_first,
    master_second,
    expert_in,
    expert_in_first,
    expert_in_second,
    expert_out,
    expert_out_first,
    expert_out_second,
    norm_gains,
    norm_gains_first,
    norm_gains_second,
    router,
    router_first,
    router_second,
    rel_bias,
    rel_bias_first,
    rel_bias_second,
):
    owners = lax.axis_size(("dp", "ctx"))
    tensor_ranks = lax.axis_size("tensor")
    my_owner = lax.axis_index(("dp", "ctx"))
    my_rank = lax.axis_index("tensor")
    my_context = lax.axis_index("ctx")
    sequences, half_length = token_ids.shape
    tokens_here = sequences * half_length
    most_units = master.shape[2]
    unit_rows = master.shape[3]
    model_width = master.shape[4]
    vocab_here = VOCAB // tensor_ranks
    heads_here = rel_bias.shape[0]
    head_size = model_width // (heads_here * tensor_ranks)
    hidden_here = heads_here * head_size
    experts = router.shape[1]
    capacity = (18 * tokens_here + 8 * experts - 1) // (8 * experts)
    table_units = vocab_here // unit_rows
    query_units = table_units + 2 * hidden_here // unit_rows
    value_units = table_units + 3 * hidden_here // unit_rows
    embed_scale = math.sqrt(model_width)
    owner_ids = owner_of[:, 0]
    on_square = lax.axis_size("dp") == 4 and lax.axis_size("ctx") == 2
    unit_rank, slot_unit, slot_filled = slot_tables(owner_ids, owners, most_units)
    counted_rows = counted.reshape(tokens_here, 2).T.astype(jnp.float32)
    loss_weights = counted_rows * jnp.array([[1.0], [ahead_weight]], jnp.float32)
    counts = jnp.zeros((8, 128), jnp.float32).at[0:2].set(jnp.sum(counted_rows, 1, keepdims=True))
    unit_slots = owner_ids * most_units + unit_rank
    route_pairs = routes.reshape(tokens_here, 2)
    pair_kept, pair_dest = pair_slots(route_pairs, priority[0], experts, capacity)
    dest = jnp.where(pair_kept, pair_dest, -1).reshape(2, tokens_here)
    unit_slots, dest = lax.optimization_barrier((unit_slots, dest))
    local_ids = token_ids.reshape(-1) - my_rank * vocab_here
    inside = (local_ids >= 0) & (local_ids < vocab_here)
    clipped_ids = jnp.clip(local_ids, 0, vocab_here - 1)
    master_low = master[0, 0].astype(jnp.bfloat16)
    unit_starts = jnp.sum(
        jnp.where(
            (clipped_ids // unit_rows)[None, :] == jnp.arange(unit_slots.shape[0])[:, None],
            unit_slots[:, None] * unit_rows,
            0,
        ),
        0,
    )
    slot_rows = unit_starts + clipped_ids % unit_rows
    if on_square:
        slot_rows = jnp.where(inside, slot_rows, -1)[:, None]
        weights_low, looked = gather_units(unit_slots, master_low, slot_rows, 11)
    else:
        gathered = lax.all_gather(master_low, ("dp", "ctx"), axis=0, tiled=True)
        looked = jnp.take(gathered.reshape(-1, model_width), slot_rows, axis=0)
        looked = jnp.where(inside[:, None], looked, 0)
        weights_low = pull_units([gathered], unit_slots)
    weights_low = weights_low.reshape(-1, model_width)
    (embedded,) = sum_line(looked, [], [], keep_total, 1)
    joint_low = weights_low[vocab_here : vocab_here + 3 * hidden_here]
    project_low = weights_low[vocab_here + 3 * hidden_here :]
    rolled = [project_low] + [
        lax.ppermute(project_low, "tensor", [(source, (source + step) % 4) for source in range(4)])
        for step in (1, 2, 3)
    ]
    project_full = lax.dynamic_slice_in_dim(
        jnp.concatenate(rolled[::-1] + rolled[::-1], 0), (3 - my_rank) * hidden_here, model_width, 0
    )
    gain_rows = [norm_gains[k : k + 1] for k in range(3)]
    stream_shape = jax.ShapeDtypeStruct((tokens_here, model_width), jnp.float32)
    gain_shape = jax.ShapeDtypeStruct((1, model_width), jnp.float32)
    stream_zero = embedded.astype(jnp.float32) * embed_scale
    first_normalized = norm_forward(stream_zero, norm_gains[0])
    normed_one_low = first_normalized.astype(jnp.bfloat16)
    joint = lax.dot_general(
        joint_low, normed_one_low, (((1,), (1,)), ((), ())), preferred_element_type=jnp.float32
    ).astype(jnp.bfloat16)
    pairs_before = passed_along(joint[hidden_here:], "ctx", 1)
    attended, logsum_rows = attention(rel_bias, joint, pairs_before, heads_here, head_size)
    (attended_all,) = gather_line([attended], 2)
    router_low = router.astype(jnp.bfloat16)
    stream_one, normed_two_low, gate_rows, gate_columns = middle(
        attended_all.reshape(model_width, tokens_here),
        project_full,
        embedded,
        gain_rows[1],
        router_low.T,
        route_pairs.T,
    )
    inner_low = expert_in[0].astype(jnp.bfloat16)
    outer_low = expert_out[0].astype(jnp.bfloat16)
    if on_square:
        moe_partial, arrived, returned, counts = experts_forward(
            normed_two_low, dest, gate_columns, route_pairs, inner_low, outer_low, counts, capacity, 8
        )
    else:
        moe_partial, arrived, returned = plain_forward(
            normed_two_low, dest, gate_columns, inner_low, outer_low, owners, capacity
        )
        counts = lax.psum(counts, ("dp", "ctx"))
    weight_total = counts[0, 0] + ahead_weight * counts[1, 0]
    head_low, stream_two = sum_line(
        moe_partial, [stream_one, gain_rows[2]], [stream_shape], finish_mixture, 3
    )
    stats = head_sums(weights_low, head_low, vocab_here)
    logsum_vocab = join_sums(stats, 7)
    local_targets = targets.reshape(tokens_here, 2).T - my_rank * vocab_here
    weight_rows = jnp.concatenate(
        [
            loss_weights,
            loss_weights[0:1] + loss_weights[1:2],
            jnp.broadcast_to(1.0 / weight_total, (1, tokens_here)),
        ],
        0,
    )
    slopes, grad_head, target_sums = head_back(
        weights_low, head_low, logsum_vocab, local_targets, weight_rows, vocab_here
    )
    grad_two_low, grad_two, gain_grad_three = sum_line(
        grad_head,
        [stream_two, gain_rows[2]],
        [stream_shape, gain_shape],
        finish_head_grad,
        4,
        prologue=clear_gain,
    )
    if on_square:
        moe_grad_part, gate_part, inner_grad, outer_grad = experts_backward(
            grad_two_low,
            dest,
            gate_rows,
            route_pairs.T,
            returned,
            arrived,
            inner_low,
            outer_low,
            9,
        )
    else:
        moe_grad_part, gate_part, inner_grad, outer_grad = plain_backward(
            grad_two_low, dest, gate_rows, returned, arrived, inner_low, outer_low
        )
    gate_part = jnp.concatenate([gate_part, target_sums, jnp.zeros_like(target_sums)], 0)
    gate_block = pltpu.VMEM((3, 4, tokens_here), jnp.float32)
    grad_one_low, grad_one, logit_grad, target_total, gain_grad_two = sum_line(
        moe_grad_part,
        [
            stream_one,
            gain_rows[1],
            grad_two,
            gate_part,
            gate_rows,
            route_pairs.T,
            router_low,
        ],
        [
            stream_shape,
            jax.ShapeDtypeStruct((experts, tokens_here), jnp.bfloat16),
            jax.ShapeDtypeStruct((1, tokens_here), jnp.float32),
            gain_shape,
        ],
        finish_expert_grad,
        5,
        prologue=start_router_grad,
        scratch=(gate_block, pltpu.SemaphoreType.DMA((3,)), pltpu.SemaphoreType.DMA((3,))),
        opening=send_gate_parts,
    )
    router_grad = jnp.dot(logit_grad, normed_two_low, preferred_element_type=jnp.float32)
    loss_local = jnp.sum(weight_rows[2:3] * logsum_vocab) - jnp.sum(target_total)
    query_grad, pair_grad, before_grad, bias_lines = attention_back(
        rel_bias,
        joint,
        pairs_before,
        logsum_rows,
        grad_one_low,
        project_low,
        heads_here,
        head_size,
    )
    grad_after = passed_along(before_grad, "ctx", -1)
    pair_grad_low = (pair_grad + grad_after.astype(jnp.float32)).astype(jnp.bfloat16)
    joint_grad = jnp.concatenate([query_grad, pair_grad_low], 0)
    distances = 2 * (half_length // BLOCK)
    bias_grad = jnp.sum(bias_lines, 1).reshape(heads_here, distances)
    zero_grad_low, gain_grads = sum_line(
        lax.dot_general(
            joint_grad, joint_low, (((0,), (0,)), ((), ())), preferred_element_type=jnp.float32
        ),
        [embedded, gain_rows[0], grad_one, gain_grad_two, gain_grad_three],
        [jax.ShapeDtypeStruct((8, model_width), jnp.float32)],
        functools.partial(finish_input_grad, embed_scale),
        6,
        prologue=clear_gain,
        scratch=(pltpu.SemaphoreType.DMA, pltpu.SemaphoreType.DMA),
        ending=share_gains,
    )
    my_units = jnp.take(slot_unit, my_owner, axis=0)
    my_filled = jnp.take(slot_filled, my_owner, axis=0)[:, None, None]
    outgoing, *expert_states = weight_grads(
        unit_slots,
        owners * most_units,
        unit_rows,
        slopes,
        head_low,
        local_ids[None, :],
        zero_grad_low,
        joint_grad,
        normed_one_low,
        attended,
        grad_one_low,
        (
            expert_in[0],
            expert_in_first[0],
            expert_in_second[0],
            inner_grad,
            expert_out[0],
            expert_out_first[0],
            expert_out_second[0],
            outer_grad,
        ),
    )
    bias_row = jnp.concatenate([bias_grad.reshape(-1), loss_local[None]])
    bias_row = jnp.pad(bias_row, (0, model_width - bias_row.shape[0]))[None]
    small = jnp.concatenate([gain_grads[:3], router_grad, bias_row], 0)
    small = jnp.pad(small, ((0, -small.shape[0] % 8), (0, 0)))
    slot_rates = unit_rates(my_units, table_units, query_units, value_units)[:, None, None]
    states = (master[0, 0], master_first[0, 0], master_second[0, 0])
    if on_square:
        mine, small = own_units(outgoing, small, most_units, 10)
    else:
        mine = lax.psum_scatter(
            outgoing.astype(jnp.float32), ("dp", "ctx"), scatter_dimension=0, tiled=True
        )
        small = lax.psum(small, ("dp", "ctx"))
    states = adam_update(*states, jnp.where(my_filled, mine, 0.0), slot_rates, decay_rate)
    gains_grad = small[:3]
    router_grad = small[3 : 3 + experts].T
    bias_grad = small[3 + experts, : rel_bias.size].reshape(rel_bias.shape)
    loss_totals = jnp.stack([small[3 + experts, rel_bias.size], weight_total])
    gains_new, gains_first_new, gains_second_new = adam_update(
        norm_gains, norm_gains_first, norm_gains_second, gains_grad, rate_gains, 0.0
    )
    router_new, router_first_new, router_second_new = adam_update(
        router, router_first, router_second, router_grad, rate_router, decay_rate
    )
    biases_new, biases_first_new, biases_second_new = adam_update(
        rel_bias, rel_bias_first, rel_bias_second, bias_grad, rate_biases, 0.0
    )
    return (
        loss_totals,
        *(state[None, None] for state in states),
        *(state[None] for state in expert_states),
        gains_new,
        gains_first_new,
        gains_second_new,
        router_new,
        router_first_new,
        router_second_new,
        biases_new,
        biases_first_new,
        biases_second_new,
    )


def solution(mesh):
    in_specs = (
        P("dp", "ctx"),
        P("dp", "ctx", None),
        P("dp", "ctx", None),
        P("dp", "ctx", None),
        P(("dp", "ctx"), None),
        P(),
        P("tensor", ("dp", "ctx"), None, None, None),
        P("tensor", ("dp", "ctx"), None, None, None),
        P("tensor", ("dp", "ctx"), None, None, None),
        P(("dp", "ctx"), None, "tensor"),
        P(("dp", "ctx"), None, "tensor"),
        P(("dp", "ctx"), None, "tensor"),
        P(("dp", "ctx"), "tensor", None),
        P(("dp", "ctx"), "tensor", None),
        P(("dp", "ctx"), "tensor", None),
        P(),
        P(),
        P(),
        P(),
        P(),
        P(),
        P("tensor", None),
        P("tensor", None),
        P("tensor", None),
    )
    out_specs = (
        P(),
        P("tensor", ("dp", "ctx"), None, None, None),
        P("tensor", ("dp", "ctx"), None, None, None),
        P("tensor", ("dp", "ctx"), None, None, None),
        P(("dp", "ctx"), None, "tensor"),
        P(("dp", "ctx"), None, "tensor"),
        P(("dp", "ctx"), None, "tensor"),
        P(("dp", "ctx"), "tensor", None),
        P(("dp", "ctx"), "tensor", None),
        P(("dp", "ctx"), "tensor", None),
        P(),
        P(),
        P(),
        P(),
        P(),
        P(),
        P("tensor", None),
        P("tensor", None),
        P("tensor", None),
    )
    return jax.shard_map(
        on_device, mesh=mesh, in_specs=in_specs, out_specs=out_specs, check_vma=False
    )
```

```python
import functools
import math

import jax
import jax.numpy as jnp
from jax import lax
from jax.experimental import pallas as pl
from jax.experimental.pallas import tpu as pltpu
from jax.sharding import PartitionSpec as P

VOCAB = 32000
BLOCK = 256
STEP = 10


highest_precision = lax.Precision.HIGHEST
beta_first = 0.9
beta_second = 0.95
adam_epsilon = 1e-08
norm_epsilon = 1e-06
ahead_weight = 0.3
masked_score = -1e30
rate_table = 0.1
rate_query = 0.05
rate_values = 0.05
rate_project = 0.5
rate_inner = 0.05
rate_outer = 0.03
rate_gains = 0.5
rate_router = 0.05
rate_biases = 0.5
decay_rate = 0.1


def passed_along(value, axis, steps):
    count = lax.axis_size(axis)
    initial, last = (max(0, -steps), min(count, count - steps))
    return lax.ppermute(value, axis, [(source, source + steps) for source in range(initial, last)])

MESH_ID = pl.DeviceIdType.MESH
whole_vmem = pl.BlockSpec(memory_space=pltpu.VMEM)
whole_any = pl.BlockSpec(memory_space=pl.ANY)
line_lag = 2


def sum_line_kernel(
    rows, count, opening, prologue, epilogue, ending, n_extra, n_aux, n_scratch, part_ref, *refs
):
    extras = refs[:n_extra]
    out_ref = refs[n_extra]
    aux = refs[n_extra + 1 : n_extra + 1 + n_aux]
    rest = refs[n_extra + 1 + n_aux :]
    scratch = rest[:n_scratch]
    stage, from_end, from_mid, send_sem, end_sem, mid_sem, back_sem, back_recv = rest[n_scratch:]
    rank = lax.axis_index("tensor")
    inner = (rank == 1) | (rank == 2)
    end_peer = jnp.where(rank < 2, 1 - rank, 5 - rank)
    mid_peer = 3 - rank
    barrier = pltpu.get_barrier_semaphore()
    if opening is None:
        pl.semaphore_signal(barrier, inc=1, device_id={"tensor": end_peer}, device_id_type=MESH_ID)

        @pl.when(inner)
        def _():
            pl.semaphore_signal(
                barrier, inc=1, device_id={"tensor": mid_peer}, device_id_type=MESH_ID
            )
            pl.semaphore_wait(barrier, 2)

        @pl.when(jnp.logical_not(inner))
        def _():
            pl.semaphore_wait(barrier, 1)
    else:
        for step in (1, 2, 3):
            other = lax.rem(rank + step, 4)
            pl.semaphore_signal(barrier, inc=1, device_id={"tensor": other}, device_id_type=MESH_ID)
        pl.semaphore_wait(barrier, 3)

    def span(i):
        return pl.ds(pl.multiple_of(i * rows, rows), rows)

    def to_inner(i):
        return pltpu.make_async_remote_copy(
            src_ref=stage.at[i],
            dst_ref=from_end.at[i],
            send_sem=send_sem.at[i],
            recv_sem=end_sem.at[i],
            device_id={"tensor": end_peer},
            device_id_type=MESH_ID,
        )

    def to_middle(i):
        return pltpu.make_async_remote_copy(
            src_ref=stage.at[i],
            dst_ref=from_mid.at[i],
            send_sem=send_sem.at[i],
            recv_sem=mid_sem.at[i],
            device_id={"tensor": mid_peer},
            device_id_type=MESH_ID,
        )

    def to_end(i):
        return pltpu.make_async_remote_copy(
            src_ref=out_ref.at[span(i)],
            dst_ref=out_ref.at[span(i)],
            send_sem=back_sem.at[i],
            recv_sem=back_recv.at[i],
            device_id={"tensor": end_peer},
            device_id_type=MESH_ID,
        )

    if opening is not None:
        opening(rank, extras, scratch)

    @pl.when(jnp.logical_not(inner))
    def _():
        def push(i, carry):
            stage[i] = part_ref[span(i)].astype(jnp.bfloat16)
            to_inner(i).start()
            return carry

        lax.fori_loop(0, count, push, 0)

    if prologue is not None:
        prologue(rank, inner, extras, aux, scratch)

    @pl.when(inner)
    def _():
        def step(i, carry):
            @pl.when(i < count)
            def _():
                to_inner(i).wait_recv()
                mine = part_ref[span(i)].astype(jnp.float32) + from_end[i].astype(jnp.float32)
                stage[i] = mine.astype(jnp.bfloat16)
                to_middle(i).start()

            @pl.when(i >= line_lag)
            def _():
                j = i - line_lag
                to_middle(j).wait_recv()
                total = stage[j].astype(jnp.float32) + from_mid[j].astype(jnp.float32)
                out_ref[span(j)] = epilogue(total, span(j), rank, extras, aux, scratch)
                to_end(j).start()

            return carry

        lax.fori_loop(0, count + line_lag, step, 0)

        def drain(i, carry):
            to_middle(i).wait_send()
            to_end(i).wait_send()
            return carry

        lax.fori_loop(0, count, drain, 0)

    @pl.when(jnp.logical_not(inner))
    def _():
        def finish(i, carry):
            to_end(i).wait_recv()
            to_inner(i).wait_send()
            return carry

        lax.fori_loop(0, count, finish, 0)

    if ending is not None:
        ending(inner, end_peer, extras, aux, scratch)


def sum_line(
    part,
    extras,
    aux_shapes,
    epilogue,
    collective_id,
    prologue=None,
    scratch=(),
    opening=None,
    ending=None,
    rows=64,
):
    tokens, width = part.shape
    count = tokens // rows
    chunks = pltpu.VMEM((count, rows, width), jnp.bfloat16)
    return pl.pallas_call(
        functools.partial(
            sum_line_kernel,
            rows,
            count,
            opening,
            prologue,
            epilogue,
            ending,
            len(extras),
            len(aux_shapes),
            len(scratch),
        ),
        out_shape=[jax.ShapeDtypeStruct((tokens, width), jnp.bfloat16)] + list(aux_shapes),
        in_specs=[whole_vmem] * (1 + len(extras)),
        out_specs=[whole_vmem] * (1 + len(aux_shapes)),
        scratch_shapes=list(scratch)
        + [chunks, chunks, chunks]
        + [pltpu.SemaphoreType.DMA((count,))] * 5,
        compiler_params=pltpu.CompilerParams(
            collective_id=collective_id, has_side_effects=True, vmem_limit_bytes=48 << 20
        ),
    )(part, *extras)


def keep_total(total, span, rank, extras, aux, scratch):
    return total.astype(jnp.bfloat16)


def inverse_rms(values):
    return lax.rsqrt(jnp.mean(values * values, -1, keepdims=True) + norm_epsilon)


def norm_back_rows(values, gain, upstream):
    inverse = inverse_rms(values)
    normed = values * inverse
    scaled = upstream * gain
    gain_grad = jnp.sum(upstream * normed, 0, keepdims=True)
    inputs_grad = inverse * (scaled - normed * jnp.mean(scaled * normed, -1, keepdims=True))
    return (inputs_grad, gain_grad)


def clear_gain(rank, inner, extras, aux, scratch):
    @pl.when(inner)
    def _():
        aux[-1][...] = jnp.zeros_like(aux[-1])


def share_gains(inner, end_peer, extras, aux, scratch):
    gains = aux[0]
    copy = pltpu.make_async_remote_copy(
        src_ref=gains,
        dst_ref=gains,
        send_sem=scratch[0],
        recv_sem=scratch[1],
        device_id={"tensor": end_peer},
        device_id_type=MESH_ID,
    )

    @pl.when(inner)
    def _():
        gains[1:2, :] = extras[3][...]
        gains[2:3, :] = extras[4][...]
        copy.start()
        copy.wait_send()

    @pl.when(jnp.logical_not(inner))
    def _():
        copy.wait_recv()


def gate_copies(rank, extras, scratch):
    gate_part = extras[3]
    landed, gate_send, gate_recv = scratch
    return [
        pltpu.make_async_remote_copy(
            src_ref=gate_part,
            dst_ref=landed.at[step - 1],
            send_sem=gate_send.at[step - 1],
            recv_sem=gate_recv.at[step - 1],
            device_id={"tensor": lax.rem(rank + step, 4)},
            device_id_type=MESH_ID,
        )
        for step in (1, 2, 3)
    ]


def send_gate_parts(rank, extras, scratch):
    for copy in gate_copies(rank, extras, scratch):
        copy.start()


def start_router_grad(rank, inner, extras, aux, scratch):
    stream_one, gain, grad_two, gate_part, gates, routes, router_low = extras
    grad_one, logit_grad, target_total, gain_grad = aux
    landed = scratch[0]
    clear_gain(rank, inner, extras, aux, scratch)
    for copy in gate_copies(rank, extras, scratch):
        copy.wait()
    gate_grad = jnp.zeros(gate_part.shape, jnp.float32)
    for source in range(4):
        piece = jnp.zeros(gate_part.shape, jnp.float32)
        for step in (1, 2, 3):
            piece = jnp.where(lax.rem(source + step, 4) == rank, landed[step - 1], piece)
        gate_grad = gate_grad + jnp.where(rank == source, gate_part[...], piece)
    target_total[...] = gate_grad[2:3]
    gate_grad = gate_grad[0:2]
    weighted = gates[...] * gate_grad
    chosen = gates[...] * (gate_grad - (weighted[0:1] + weighted[1:2]))
    experts, tokens = logit_grad.shape
    row = lax.broadcasted_iota(jnp.int32, (experts, tokens), 0)
    placed = jnp.where(row == routes[0:1], chosen[0:1], 0.0) + jnp.where(
        row == routes[1:2], chosen[1:2], 0.0
    )
    logit_grad[...] = placed.astype(jnp.bfloat16)

    @pl.when(inner)
    def _():
        grad_one[...] = lax.dot_general(
            logit_grad[...],
            router_low[...],
            (((0,), (1,)), ((), ())),
            preferred_element_type=jnp.float32,
        )


def finish_expert_grad(total, span, rank, extras, aux, scratch):
    stream_one, gain, grad_two, gate_part, gates, routes, router_low = extras
    grad_one, logit_grad, target_total, gain_grad = aux
    part, gain_part = norm_back_rows(
        stream_one[span], gain[...], total + grad_one[span]
    )
    result = grad_two[span] + part
    grad_one[span] = result
    gain_grad[...] += gain_part
    return result.astype(jnp.bfloat16)


def finish_input_grad(scale, total, span, rank, extras, aux, scratch):
    embedded, gain, grad_one = extras[:3]
    stream_zero = embedded[span].astype(jnp.float32) * scale
    part, gain_part = norm_back_rows(stream_zero, gain[...], total)
    aux[0][0:1, :] += gain_part
    return ((grad_one[span] + part) * scale).astype(jnp.bfloat16)


def gather_line_kernel(count, *refs):
    ins = refs[:count]
    outs = refs[count : 2 * count]
    local_sem, send_sem, recv_sem = refs[2 * count :]
    rank = lax.axis_index("tensor")
    barrier = pltpu.get_barrier_semaphore()
    for step in (1, 2, 3):
        other = lax.rem(rank + step, 4)
        pl.semaphore_signal(barrier, inc=1, device_id={"tensor": other}, device_id_type=MESH_ID)
    pl.semaphore_wait(barrier, 3)
    copies = []
    for k in range(count):
        for step in (1, 2, 3):
            copy = pltpu.make_async_remote_copy(
                src_ref=ins[k],
                dst_ref=outs[k].at[rank],
                send_sem=send_sem.at[k, step - 1],
                recv_sem=recv_sem.at[k, step - 1],
                device_id={"tensor": lax.rem(rank + step, 4)},
                device_id_type=MESH_ID,
            )
            copy.start()
            copies.append(copy)
        own = pltpu.make_async_copy(ins[k], outs[k].at[rank], local_sem.at[k])
        own.start()
        own.wait()
    for copy in copies:
        copy.wait()


def gather_line(arrays, collective_id):
    count = len(arrays)
    return pl.pallas_call(
        functools.partial(gather_line_kernel, count),
        out_shape=[jax.ShapeDtypeStruct((4,) + x.shape, x.dtype) for x in arrays],
        in_specs=[whole_vmem] * count,
        out_specs=[whole_vmem] * count,
        scratch_shapes=[
            pltpu.SemaphoreType.DMA((count,)),
            pltpu.SemaphoreType.DMA((count, 3)),
            pltpu.SemaphoreType.DMA((count, 3)),
        ],
        compiler_params=pltpu.CompilerParams(
            collective_id=collective_id, has_side_effects=True, vmem_limit_bytes=40 << 20
        ),
    )(*arrays)


def middle_kernel(
    attended_ref, embedded_ref, gain_ref, router_ref, routes_ref, *refs
):
    rolled, (stream_ref, normed_ref, rows_ref, columns_ref, project_ref) = refs[:4], refs[4:]

    @pl.when(pl.program_id(0) == 0)
    def _():
        for step in range(4):
            lines = rolled[step].shape[0]
            owner = lax.rem(lax.axis_index("tensor") + 4 - step, 4)
            project_ref[pl.ds(pl.multiple_of(owner * lines, lines), lines)] = rolled[step][...]

    scale = math.sqrt(embedded_ref.shape[1])
    stream = embedded_ref[...].astype(jnp.float32) * scale + lax.dot_general(
        attended_ref[...], project_ref[...], (((0,), (0,)), ((), ())), preferred_element_type=jnp.float32
    )
    stream_ref[...] = stream
    normed = (stream * inverse_rms(stream) * gain_ref[...]).astype(jnp.bfloat16)
    normed_ref[...] = normed
    scores = lax.dot_general(
        router_ref[...], normed, (((1,), (1,)), ((), ())), preferred_element_type=jnp.float32
    )
    expert = lax.broadcasted_iota(jnp.int32, scores.shape, 0)
    first, second = (
        jnp.sum(jnp.where(expert == routes_ref[k : k + 1, :], scores, 0.0), 0, keepdims=True)
        for k in range(2)
    )
    top = jnp.maximum(first, second)
    first, second = jnp.exp(first - top), jnp.exp(second - top)
    total = first + second
    gates = jnp.concatenate([first / total, second / total], 0)
    rows_ref[...] = gates
    columns_ref[...] = jnp.concatenate([gates, jnp.zeros((6, gates.shape[1]), jnp.float32)], 0).T


def middle(attended, rolled, embedded, gain, router, routes):
    tokens, width = embedded.shape
    tile = 256
    fixed = lambda k: (0, 0)
    whole = lambda x: pl.BlockSpec(x.shape, fixed)
    down = lambda n: pl.BlockSpec((tile, n), lambda k: (k, 0))
    along = lambda n: pl.BlockSpec((n, tile), lambda k: (0, k))
    return pl.pallas_call(
        middle_kernel,
        grid=(tokens // tile,),
        out_shape=[
            jax.ShapeDtypeStruct((tokens, width), jnp.float32),
            jax.ShapeDtypeStruct((tokens, width), jnp.bfloat16),
            jax.ShapeDtypeStruct((2, tokens), jnp.float32),
            jax.ShapeDtypeStruct((tokens, 8), jnp.float32),
        ],
        in_specs=[along(width), down(width), whole(gain), whole(router), along(2)]
        + [whole(x) for x in rolled],
        out_specs=[down(width), down(width), along(2), down(8)],
        scratch_shapes=[pltpu.VMEM((width, width), jnp.bfloat16)],
        compiler_params=pltpu.CompilerParams(vmem_limit_bytes=40 << 20),
    )(attended, embedded, gain, router, routes, *rolled)


def gather_units_kernel(
    chunks, slots_ref, mine_ref, rows_ref, units_ref, looked_ref,
    held, total, send_x, recv_x, send_y, recv_y, send_z, recv_z, send_core, recv_core,
):
    chip, core = lax.axis_index("dp"), lax.axis_index("ctx")
    beside = chip + 1 - 2 * lax.rem(chip, 2)
    across = lax.rem(chip + 2, 4)
    opposite = across + 1 - 2 * lax.rem(across, 2)
    places = (chip, beside, across, opposite)
    slots, unit_rows, width = mine_ref.shape
    size = slots // chunks
    split = (chunks + 1) // 2
    tokens = rows_ref.shape[0]
    barrier = pltpu.get_barrier_semaphore()
    for place in ({"ctx": 1 - core}, {"dp": beside}, {"dp": across}):
        pl.semaphore_signal(barrier, inc=1, device_id=place, device_id_type=MESH_ID)
    pl.semaphore_wait(barrier, 3)

    def piece(place, which, q):
        return held.at[pl.ds((place * 2 + which) * slots + q * size, size)]

    def copy(place, q, send, recv, target):
        return pltpu.make_async_remote_copy(
            src_ref=piece(place, core, q),
            dst_ref=piece(place, core, q),
            send_sem=send,
            recv_sem=recv,
            device_id=target,
            device_id_type=MESH_ID,
        )

    def to_beside(q):
        return copy(chip, q, send_x.at[q], recv_x.at[q], {"dp": beside})

    def to_across(q):
        return copy(chip, q, send_y.at[q], recv_y.at[q], {"dp": across})

    def passed_on(q, source, target):
        return copy(source, q, send_z.at[q], recv_z.at[q], {"dp": target})

    def to_core(k, q):
        return copy(places[k], q, send_core.at[k, q], recv_core.at[k, q], {"ctx": 1 - core})

    held[pl.ds((chip * 2 + core) * slots, slots)] = mine_ref[...]

    def start(i, carry):
        to_beside(i).start()
        to_across(lax.rem(i + split, chunks)).start()
        return carry

    lax.fori_loop(0, chunks, start, 0)

    def start_core(q, carry):
        to_core(0, q).start()
        return carry

    lax.fori_loop(0, chunks, start_core, 0)
    total[...] = jnp.zeros_like(total)

    def look(place, which):
        begin = (place * 2 + which) * slots
        lines = slots * unit_rows
        column = lax.broadcasted_iota(jnp.int32, (tokens, lines), 1) + begin * unit_rows
        hit = jnp.where(column == rows_ref[...], 1.0, 0.0).astype(jnp.bfloat16)
        block = held[pl.ds(begin, slots)].reshape(lines, width)
        total[...] += jnp.dot(hit, block, preferred_element_type=jnp.float32)

    look(chip, core)

    def relay(i, carry):
        to_beside(i).wait_recv()

        @pl.when(i < split)
        def _():
            passed_on(i, beside, across).start()

        to_core(1, i).start()
        j = lax.rem(i + split, chunks)
        to_across(j).wait_recv()

        @pl.when(j >= split)
        def _():
            passed_on(j, across, beside).start()

        to_core(2, j).start()
        to_core(0, i).wait_recv()
        return carry

    lax.fori_loop(0, chunks, relay, 0)
    look(chip, 1 - core)
    look(beside, core)
    look(across, core)

    def last(q, carry):
        passed_on(q, opposite, opposite).wait_recv()
        to_core(3, q).start()
        to_core(1, q).wait_recv()
        to_core(2, q).wait_recv()
        return carry

    lax.fori_loop(0, chunks, last, 0)
    for source in (beside, across):
        look(source, 1 - core)
    look(opposite, core)

    def ending(q, carry):
        to_core(3, q).wait_recv()
        return carry

    lax.fori_loop(0, chunks, ending, 0)
    look(opposite, 1 - core)
    looked_ref[...] = total[...].astype(jnp.bfloat16)

    def place_unit(u, carry):
        units_ref[u] = held[slots_ref[u]]
        return carry

    lax.fori_loop(0, units_ref.shape[0], place_unit, 0)

    def finish(q, carry):
        to_beside(q).wait_send()
        to_across(q).wait_send()
        for k in range(4):
            to_core(k, q).wait_send()
        passed_on(q, opposite, opposite).wait_send()
        return carry

    lax.fori_loop(0, chunks, finish, 0)


def gather_units(unit_slots, mine, slot_rows, collective_id):
    slots = mine.shape[0]
    unit = mine.shape[1:]
    tokens = slot_rows.shape[0]
    chunks = max(k for k in range(1, 8) if slots % k == 0)
    sems = pltpu.SemaphoreType.DMA((chunks,))
    core_sems = pltpu.SemaphoreType.DMA((4, chunks))
    return pl.pallas_call(
        functools.partial(gather_units_kernel, chunks),
        out_shape=[
            jax.ShapeDtypeStruct((unit_slots.shape[0],) + unit, jnp.bfloat16),
            jax.ShapeDtypeStruct((tokens, unit[1]), jnp.bfloat16),
        ],
        in_specs=[pl.BlockSpec(memory_space=pltpu.SMEM), whole_vmem, whole_vmem],
        out_specs=[whole_vmem] * 2,
        scratch_shapes=[
            pltpu.VMEM((8 * slots,) + unit, jnp.bfloat16),
            pltpu.VMEM((tokens, unit[1]), jnp.float32),
        ]
        + [sems] * 6
        + [core_sems] * 2,
        compiler_params=pltpu.CompilerParams(
            collective_id=collective_id, has_side_effects=True, vmem_limit_bytes=56 << 20
        ),
    )(unit_slots, mine, slot_rows)


def pull_units_kernel(parts, slots_ref, *refs):
    sources, out_ref, sem = refs[:parts], refs[parts], refs[parts + 1]
    width = out_ref.shape[-1] // parts

    def push(u, carry):
        for part in range(parts):
            pltpu.make_async_copy(
                sources[part].at[slots_ref[u]],
                out_ref.at[u, :, part * width : (part + 1) * width],
                sem,
            ).start()
        return carry

    lax.fori_loop(0, out_ref.shape[0], push, 0)
    pltpu.make_async_copy(out_ref, out_ref, sem).wait()


def pull_units(sources, slots):
    count = slots.shape[0]
    rows, width = sources[0].shape[1:]
    return pl.pallas_call(
        functools.partial(pull_units_kernel, len(sources)),
        out_shape=jax.ShapeDtypeStruct((count, rows, width * len(sources)), sources[0].dtype),
        in_specs=[pl.BlockSpec(memory_space=pltpu.SMEM)] + [whole_any] * len(sources),
        out_specs=whole_vmem,
        scratch_shapes=[pltpu.SemaphoreType.DMA],
        compiler_params=pltpu.CompilerParams(vmem_limit_bytes=40 << 20),
    )(slots, *sources)


def attention_kernel(heads, size, bias_ref, own_ref, before_ref, out_ref, logsum_ref, scores, peak, total):
    tokens = own_ref.shape[1]
    blocks = tokens // BLOCK
    hidden = heads * size
    later = lax.axis_index("ctx") > 0

    for head in range(heads):
        query = own_ref[head * size : (head + 1) * size, :].astype(jnp.float32).T * size**-0.5
        query = query.astype(jnp.bfloat16)
        own_keys = own_ref[hidden + head * size : hidden + (head + 1) * size, :]
        old_keys = before_ref[head * size : (head + 1) * size, :]
        own_values = own_ref[2 * hidden + head * size : 2 * hidden + (head + 1) * size, :]
        own_values = own_values.astype(jnp.float32).T.astype(jnp.bfloat16)
        old_values = before_ref[hidden + head * size : hidden + (head + 1) * size, :]
        old_values = old_values.astype(jnp.float32).T.astype(jnp.bfloat16)
        for block in range(blocks):
            rows = query[block * BLOCK : (block + 1) * BLOCK]
            width = (block + 1) * BLOCK
            mine = jnp.dot(rows, own_keys[:, :width], preferred_element_type=jnp.float32)
            top = None
            parts = []
            for k in range(block + 1):
                part = mine[:, k * BLOCK : (k + 1) * BLOCK] + bias_ref[head, block - k]
                parts.append(part)
                high = jnp.max(part, 1, keepdims=True)
                top = high if top is None else jnp.maximum(top, high)
            peak[...] = top

            @pl.when(later)
            def _():
                old = jnp.dot(rows, old_keys, preferred_element_type=jnp.float32)
                top_old = None
                for k in range(blocks):
                    part = old[:, k * BLOCK : (k + 1) * BLOCK] + bias_ref[head, block + blocks - k]
                    scores[:, k * BLOCK : (k + 1) * BLOCK] = part
                    high = jnp.max(part, 1, keepdims=True)
                    top_old = high if top_old is None else jnp.maximum(top_old, high)
                peak[...] = jnp.maximum(peak[...], top_old)

            top = peak[...]
            parts = [jnp.exp(part - top) for part in parts]
            own_sum = None
            for part in parts:
                part_sum = jnp.sum(part, 1, keepdims=True)
                own_sum = part_sum if own_sum is None else own_sum + part_sum
            total[...] = own_sum

            @pl.when(later)
            def _():
                old_exp = jnp.exp(scores[...] - top)
                scores[...] = old_exp
                total[...] += jnp.sum(old_exp, 1, keepdims=True)

            full = total[...]
            inverse = 1.0 / full
            low = jnp.concatenate([(part * inverse).astype(jnp.bfloat16) for part in parts], 1)
            result = jnp.dot(low, own_values[:width], preferred_element_type=jnp.float32)
            peak[...] = top + jnp.log(full)
            logsum_ref[head, block * BLOCK : (block + 1) * BLOCK, :] = peak[...]
            place = (slice(head * size, (head + 1) * size), slice(block * BLOCK, (block + 1) * BLOCK))

            @pl.when(later)
            def _():
                low_old = (scores[...] * inverse).astype(jnp.bfloat16)
                both = result + jnp.dot(low_old, old_values, preferred_element_type=jnp.float32)
                out_ref[place] = both.T.astype(jnp.bfloat16)

            @pl.when(jnp.logical_not(later))
            def _():
                out_ref[place] = result.T.astype(jnp.bfloat16)


def attention(biases, own, before, heads, size):
    tokens = own.shape[1]
    return pl.pallas_call(
        functools.partial(attention_kernel, heads, size),
        out_shape=[
            jax.ShapeDtypeStruct((heads * size, tokens), jnp.bfloat16),
            jax.ShapeDtypeStruct((heads, tokens, 1), jnp.float32),
        ],
        in_specs=[pl.BlockSpec(memory_space=pltpu.SMEM), whole_vmem, whole_vmem],
        out_specs=[whole_vmem, whole_vmem],
        scratch_shapes=[
            pltpu.VMEM((BLOCK, tokens), jnp.float32),
            pltpu.VMEM((BLOCK, 1), jnp.float32),
            pltpu.VMEM((BLOCK, 1), jnp.float32),
        ],
        compiler_params=pltpu.CompilerParams(vmem_limit_bytes=40 << 20),
    )(biases, own, before)


def attention_back_kernel(
    heads, size, bias_ref, own_ref, before_ref, logsum_ref, grad_ref, project_ref,
    query_out, own_out, before_out, bias_out, probs, slopes, inner, query_sum, own_sum, before_sum,
):
    tokens = own_ref.shape[1]
    blocks = tokens // BLOCK
    hidden = heads * size
    later = lax.axis_index("ctx") > 0
    bias_out[...] = jnp.zeros_like(bias_out)

    def flipped(rows):
        return rows.astype(jnp.float32).T.astype(jnp.bfloat16)

    for head in range(heads):
        span = slice(head * size, (head + 1) * size)
        value_span = slice(hidden + head * size, hidden + (head + 1) * size)
        query_rows = own_ref[span, :]
        query = flipped(query_rows) * jnp.bfloat16(size**-0.5)
        own_keys = own_ref[hidden + head * size : hidden + (head + 1) * size, :]
        own_values = own_ref[2 * hidden + head * size : 2 * hidden + (head + 1) * size, :]
        old_keys = before_ref[span, :]
        old_values = before_ref[value_span, :]
        own_keys_flip = flipped(own_keys)
        grad = lax.dot_general(
            grad_ref[...], project_ref[span, :], (((1,), (1,)), ((), ())), preferred_element_type=jnp.float32
        )
        grad_rows = grad.T.astype(jnp.bfloat16)
        grad = grad.astype(jnp.bfloat16)
        own_sum[...] = jnp.zeros_like(own_sum)

        @pl.when(later)
        def _():
            before_sum[...] = jnp.zeros_like(before_sum)

        for block in range(blocks):
            at = slice(block * BLOCK, (block + 1) * BLOCK)
            width = (block + 1) * BLOCK
            rows, up = query[at], grad[at]
            lse = logsum_ref[head, at, :]
            score = jnp.dot(rows, own_keys[:, :width], preferred_element_type=jnp.float32)
            prob = jnp.concatenate(
                [
                    jnp.exp(score[:, k * BLOCK : (k + 1) * BLOCK] + (bias_ref[head, block - k] - lse))
                    for k in range(block + 1)
                ],
                1,
            )
            slope = jnp.dot(up, own_values[:, :width], preferred_element_type=jnp.float32)
            inner[...] = jnp.sum(prob * slope, 1, keepdims=True)

            @pl.when(later)
            def _():
                score = jnp.dot(rows, old_keys, preferred_element_type=jnp.float32)
                old_slope = jnp.dot(up, old_values, preferred_element_type=jnp.float32)
                old_prob = jnp.concatenate(
                    [
                        jnp.exp(
                            score[:, k * BLOCK : (k + 1) * BLOCK]
                            + (bias_ref[head, block + blocks - k] - lse)
                        )
                        for k in range(blocks)
                    ],
                    1,
                )
                probs[...] = old_prob
                slopes[...] = old_slope
                inner[...] += jnp.sum(old_prob * old_slope, 1, keepdims=True)

            row_inner = inner[...]
            low_grad = (prob * (slope - row_inner)).astype(jnp.bfloat16)
            query_sum[...] = jnp.dot(
                low_grad, own_keys_flip[:width], preferred_element_type=jnp.float32
            )
            own_sum[:size, :width] += jnp.dot(
                query_rows[:, at], low_grad, preferred_element_type=jnp.float32
            )
            own_sum[size:, :width] += jnp.dot(
                grad_rows[:, at], prob.astype(jnp.bfloat16), preferred_element_type=jnp.float32
            )
            for k in range(block + 1):
                line = head * 2 * blocks + block - k
                bias_out[line : line + 1, :] += jnp.sum(
                    low_grad[:, k * BLOCK : (k + 1) * BLOCK].astype(jnp.float32), 0, keepdims=True
                )

            @pl.when(later)
            def _():
                old_prob = probs[...]
                low_old = (old_prob * (slopes[...] - row_inner)).astype(jnp.bfloat16)
                query_sum[...] += jnp.dot(
                    low_old, flipped(old_keys), preferred_element_type=jnp.float32
                )
                before_sum[:size, :] += jnp.dot(
                    query_rows[:, at], low_old, preferred_element_type=jnp.float32
                )
                before_sum[size:, :] += jnp.dot(
                    grad_rows[:, at], old_prob.astype(jnp.bfloat16), preferred_element_type=jnp.float32
                )
                for k in range(blocks):
                    line = head * 2 * blocks + block + blocks - k
                    bias_out[line : line + 1, :] += jnp.sum(
                        low_old[:, k * BLOCK : (k + 1) * BLOCK].astype(jnp.float32), 0, keepdims=True
                    )

            query_out[span, at] = (query_sum[...].T * size**-0.5).astype(jnp.bfloat16)

        own_out[span, :] = own_sum[:size, :] * size**-0.5
        own_out[value_span, :] = own_sum[size:, :]

        @pl.when(later)
        def _():
            before_out[span, :] = (before_sum[:size, :] * size**-0.5).astype(jnp.bfloat16)
            before_out[value_span, :] = before_sum[size:, :].astype(jnp.bfloat16)

    @pl.when(jnp.logical_not(later))
    def _():
        before_out[...] = jnp.zeros_like(before_out)


def attention_back(biases, own, before, logsum, grad, project, heads, size):
    tokens = own.shape[1]
    hidden = heads * size
    return pl.pallas_call(
        functools.partial(attention_back_kernel, heads, size),
        out_shape=[
            jax.ShapeDtypeStruct((hidden, tokens), jnp.bfloat16),
            jax.ShapeDtypeStruct((2 * hidden, tokens), jnp.float32),
            jax.ShapeDtypeStruct((2 * hidden, tokens), jnp.bfloat16),
            jax.ShapeDtypeStruct((heads * 2 * (tokens // BLOCK), BLOCK), jnp.float32),
        ],
        in_specs=[pl.BlockSpec(memory_space=pltpu.SMEM)] + [whole_vmem] * 5,
        out_specs=[whole_vmem] * 4,
        scratch_shapes=[
            pltpu.VMEM((BLOCK, tokens), jnp.float32),
            pltpu.VMEM((BLOCK, tokens), jnp.float32),
            pltpu.VMEM((BLOCK, 1), jnp.float32),
            pltpu.VMEM((BLOCK, size), jnp.float32),
            pltpu.VMEM((2 * size, tokens), jnp.float32),
            pltpu.VMEM((2 * size, tokens), jnp.float32),
        ],
        compiler_params=pltpu.CompilerParams(vmem_limit_bytes=48 << 20),
    )(biases, own, before, logsum, grad, project)


def vocab_tile(vocab):
    return max(k for k in range(16, 1601, 16) if vocab % k == 0)


def head_line_kernel(
    tile, part_ref, stream_ref, gain_ref, table_ref, wanted_ref, weight_ref,
    low_ref, grad_low_ref, grad_ref, gain_grad, logsum_ref, picked_ref, slopes_ref,
    table, stage, from_end, from_mid, own, turned, stats, landed, slope_tiles, total,
    load_sem, send_sem, end_sem, mid_sem, back_sem, back_recv, stat_send, stat_recv, store_sem,
):
    rank = lax.axis_index("tensor")
    inner = (rank == 1) | (rank == 2)
    end_peer = jnp.where(rank < 2, 1 - rank, 5 - rank)
    mid_peer = 3 - rank
    count, rows = stage.shape[:2]
    columns = turned.shape[1]
    pieces = table.shape[0] // tile
    group = columns // rows
    tiles = count // group
    units = tiles * pieces
    vocab = table.shape[0]
    load = pltpu.make_async_copy(table_ref.at[pl.ds(0, vocab)], table, load_sem)
    load.start()
    barrier = pltpu.get_barrier_semaphore()
    for step in (1, 2, 3):
        other = lax.rem(rank + step, 4)
        pl.semaphore_signal(barrier, inc=1, device_id={"tensor": other}, device_id_type=MESH_ID)
    pl.semaphore_wait(barrier, 3)

    def span(i):
        return pl.ds(pl.multiple_of(i * rows, rows), rows)

    def over(t):
        return pl.ds(pl.multiple_of(t * columns, columns), columns)

    def line_copy(source, target, send, recv, peer):
        return pltpu.make_async_remote_copy(
            src_ref=source,
            dst_ref=target,
            send_sem=send,
            recv_sem=recv,
            device_id={"tensor": peer},
            device_id_type=MESH_ID,
        )

    def to_inner(i):
        return line_copy(stage.at[i], from_end.at[i], send_sem.at[i], end_sem.at[i], end_peer)

    def to_middle(i):
        return line_copy(stage.at[i], from_mid.at[i], send_sem.at[i], mid_sem.at[i], mid_peer)

    def to_end(ref, i):
        rows_of = ref.at[span(i)]
        return line_copy(rows_of, rows_of, back_sem.at[i], back_recv.at[i], end_peer)

    def repeat(first, last, body):
        def step(i, carry):
            body(i)
            return carry

        lax.fori_loop(first, last, step, 0)

    def turn(t):
        turned[...] = low_ref[over(t)].astype(jnp.float32).T.astype(jnp.bfloat16)

    def table_rows(k):
        return table[pl.ds(pl.multiple_of(k * tile, tile), tile)]

    def sums_unit(n):
        t, k = n // pieces, lax.rem(n, pieces)

        @pl.when(k == 0)
        def _():
            turn(t)

        logits = jnp.dot(table_rows(k), turned[...], preferred_element_type=jnp.float32)
        before = stats[0:1, over(t)]
        top = jnp.maximum(before, jnp.max(logits, 0, keepdims=True))
        stats[1:2, over(t)] = stats[1:2, over(t)] * jnp.exp(before - top) + jnp.sum(
            jnp.exp(logits - top), 0, keepdims=True
        )
        stats[0:1, over(t)] = top

    stats[0:1, :] = jnp.full_like(stats[0:1, :], masked_score)
    stats[1:2, :] = jnp.zeros_like(stats[1:2, :])

    @pl.when(jnp.logical_not(inner))
    def _():
        def push(i):
            stage[i] = part_ref[span(i)].astype(jnp.bfloat16)
            to_inner(i).start()

        repeat(0, count, push)
        load.wait()

        def forward(t):
            repeat(0, group, lambda c: to_end(low_ref, t * group + c).wait_recv())
            repeat(0, pieces, lambda k: sums_unit(t * pieces + k))

        repeat(0, tiles, forward)
        repeat(0, count, lambda i: to_inner(i).wait_send())

    @pl.when(inner)
    def _():
        gain_grad[...] = jnp.zeros_like(gain_grad)
        load.wait()
        ahead = group + line_lag

        def step(i):
            @pl.when(i < count)
            def _():
                to_inner(i).wait_recv()
                mine = part_ref[span(i)] + from_end[i].astype(jnp.float32)
                stage[i] = mine.astype(jnp.bfloat16)
                to_middle(i).start()

            @pl.when(i >= line_lag)
            def _():
                j = i - line_lag
                to_middle(j).wait_recv()
                stream_two = stream_ref[span(j)] + (
                    stage[j].astype(jnp.float32) + from_mid[j].astype(jnp.float32)
                )
                grad_ref[span(j)] = stream_two
                low_ref[span(j)] = (stream_two * inverse_rms(stream_two) * gain_ref[...]).astype(
                    jnp.bfloat16
                )
                to_end(low_ref, j).start()

            @pl.when(i >= ahead)
            def _():
                sums_unit(i - ahead)

        repeat(0, count + line_lag, step)
        repeat(count + line_lag - ahead, units, sums_unit)

        def drain(i):
            to_middle(i).wait_send()
            to_end(low_ref, i).wait_send()

        repeat(0, count, drain)

    copies = [
        line_copy(
            stats, landed.at[step - 1], stat_send.at[step - 1], stat_recv.at[step - 1], lax.rem(rank + step, 4)
        )
        for step in (1, 2, 3)
    ]
    for copy in copies:
        copy.start()
    for copy in copies:
        copy.wait()
    tops, sums = [], []
    for source in range(4):
        piece = stats[...]
        for step in (1, 2, 3):
            piece = jnp.where(lax.rem(source + step, 4) == rank, landed[step - 1], piece)
        tops.append(piece[0:1])
        sums.append(piece[1:2])
    top = jnp.maximum(jnp.maximum(tops[0], tops[1]), jnp.maximum(tops[2], tops[3]))
    whole = sums[0] * jnp.exp(tops[0] - top)
    for source in (1, 2, 3):
        whole = whole + sums[source] * jnp.exp(tops[source] - top)
    logsum_ref[...] = top + jnp.log(whole)
    picked_ref[...] = jnp.zeros_like(picked_ref)

    def store(t):
        return pltpu.make_async_copy(
            slope_tiles.at[lax.rem(t, 2)], slopes_ref.at[:, over(t)], store_sem.at[lax.rem(t, 2)]
        )

    def back_unit(n):
        t, k = n // pieces, lax.rem(n, pieces)

        @pl.when(k == 0)
        def _():
            turn(t)
            total[...] = jnp.zeros_like(total)

            @pl.when(t >= 2)
            def _():
                store(t - 2).wait()

        lines = table_rows(k)
        logits = jnp.dot(lines, turned[...], preferred_element_type=jnp.float32)
        row = lax.broadcasted_iota(jnp.int32, logits.shape, 0)
        base = k * tile
        hits = jnp.where(row == wanted_ref[0:1, over(t)] - base, weight_ref[0:1, over(t)], 0.0)
        hits = hits + jnp.where(
            row == wanted_ref[1:2, over(t)] - base, weight_ref[1:2, over(t)], 0.0
        )
        picked_ref[:, over(t)] += jnp.sum(hits * logits, 0, keepdims=True)
        softmax = jnp.exp(logits - logsum_ref[:, over(t)])
        slope = (
            (weight_ref[2:3, over(t)] * softmax - hits) * weight_ref[3:4, over(t)]
        ).astype(jnp.bfloat16)
        slope_tiles[lax.rem(t, 2), pl.ds(pl.multiple_of(base, tile), tile)] = slope
        total[...] += lax.dot_general(
            slope, lines, (((0,), (0,)), ((), ())), preferred_element_type=jnp.float32
        )

        @pl.when(k == pieces - 1)
        def _():
            store(t).start()

    @pl.when(jnp.logical_not(inner))
    def _():
        def unit(n):
            back_unit(n)

            @pl.when(lax.rem(n, pieces) == pieces - 1)
            def _():
                first = (n // pieces) * group

                def push(c):
                    stage[first + c] = total[span(c)].astype(jnp.bfloat16)
                    to_inner(first + c).start()

                repeat(0, group, push)

        repeat(0, units, unit)

        def finish(i):
            to_end(grad_low_ref, i).wait_recv()
            to_inner(i).wait_send()

        repeat(0, count, finish)

    @pl.when(inner)
    def _():
        def settle(j):
            to_middle(j).wait_recv()
            upstream = stage[j].astype(jnp.float32) + from_mid[j].astype(jnp.float32)
            grad_two, gain_part = norm_back_rows(grad_ref[span(j)], gain_ref[...], upstream)
            grad_ref[span(j)] = grad_two
            gain_grad[...] += gain_part
            grad_low_ref[span(j)] = grad_two.astype(jnp.bfloat16)
            to_end(grad_low_ref, j).start()

        def exchange(i):
            to_inner(i).wait_recv()
            stage[i] = (own[span(i)] + from_end[i].astype(jnp.float32)).astype(jnp.bfloat16)
            to_middle(i).start()

            @pl.when(i >= line_lag)
            def _():
                settle(i - line_lag)

        def unit(n):
            back_unit(n)
            t, k = n // pieces, lax.rem(n, pieces)

            @pl.when(k == pieces - 1)
            def _():
                own[over(t)] = total[...]

            @pl.when((t >= 1) & (k >= pieces - group))
            def _():
                exchange((t - 1) * group + k - (pieces - group))

        repeat(0, units, unit)
        repeat(count - group, count, exchange)
        repeat(count - line_lag, count, settle)

        def drain(i):
            to_middle(i).wait_send()
            to_end(grad_low_ref, i).wait_send()

        repeat(0, count, drain)

    store(tiles - 2).wait()
    store(tiles - 1).wait()


def head_line(part, stream, gain, weights, wanted, weight_rows, vocab, collective_id):
    tokens, width = part.shape
    rows, columns = 64, 256
    count = tokens // rows
    chunks = pltpu.VMEM((count, rows, width), jnp.bfloat16)
    rows_low = jax.ShapeDtypeStruct((tokens, width), jnp.bfloat16)
    along = jax.ShapeDtypeStruct((1, tokens), jnp.float32)
    line_sems = pltpu.SemaphoreType.DMA((count,))
    return pl.pallas_call(
        functools.partial(head_line_kernel, vocab_tile(vocab)),
        out_shape=[
            rows_low,
            rows_low,
            jax.ShapeDtypeStruct((tokens, width), jnp.float32),
            jax.ShapeDtypeStruct((1, width), jnp.float32),
            along,
            along,
            jax.ShapeDtypeStruct((vocab, tokens), jnp.bfloat16),
        ],
        in_specs=[whole_vmem] * 3 + [whole_any] + [whole_vmem] * 2,
        out_specs=[whole_vmem] * 6 + [whole_any],
        scratch_shapes=[
            pltpu.VMEM((vocab, width), jnp.bfloat16),
            chunks,
            chunks,
            chunks,
            pltpu.VMEM((tokens, width), jnp.float32),
            pltpu.VMEM((width, columns), jnp.bfloat16),
            pltpu.VMEM((2, tokens), jnp.float32),
            pltpu.VMEM((3, 2, tokens), jnp.float32),
            pltpu.VMEM((2, vocab, columns), jnp.bfloat16),
            pltpu.VMEM((columns, width), jnp.float32),
            pltpu.SemaphoreType.DMA,
        ]
        + [line_sems] * 5
        + [pltpu.SemaphoreType.DMA((3,))] * 2
        + [pltpu.SemaphoreType.DMA((2,))],
        compiler_params=pltpu.CompilerParams(
            collective_id=collective_id, has_side_effects=True, vmem_limit_bytes=62 << 20
        ),
    )(part, stream, gain, weights, wanted, weight_rows)


def weight_grads_kernel(
    tile_units, tiles, place_ref, slope_ref, rows_ref, ids_ref, zero_ref, joint_ref, normed_ref,
    attended_ref, grad_ref, *refs
):
    states, (out_ref, *updated), (made, sem) = refs[:8], refs[8:15], refs[15:]
    step = pl.program_id(0)
    for k, rate in enumerate((rate_inner, rate_outer)):
        fresh = adam_update(*(state[...] for state in states[4 * k : 4 * k + 4]), rate, decay_rate)
        for n in range(3):
            updated[3 * k + n][...] = fresh[n]
    unit_rows = out_ref.shape[1]
    buffer = lax.rem(step, 2)
    last_units = joint_ref.shape[0] // unit_rows + attended_ref.shape[0] // unit_rows

    def settle(which, count):
        pltpu.make_async_copy(
            made.at[which, pl.ds(0, count)], made.at[which, pl.ds(0, count)], sem.at[which]
        ).wait()

    def send(first, count):
        def push(u, carry):
            pltpu.make_async_copy(
                made.at[buffer, u], out_ref.at[place_ref[first + u]], sem.at[buffer]
            ).start()
            return carry

        lax.fori_loop(0, count, push, 0)

    @pl.when(step >= 2)
    def _():
        settle(buffer, tile_units)

    @pl.when(step < tiles)
    def _():
        row = lax.broadcasted_iota(jnp.int32, slope_ref.shape, 0)
        seen = jnp.where(row == ids_ref[...] - step * slope_ref.shape[0], 1.0, 0.0).astype(jnp.bfloat16)
        made[buffer] = (
            jnp.dot(slope_ref[...], rows_ref[...], preferred_element_type=jnp.float32)
            + jnp.dot(seen, zero_ref[...], preferred_element_type=jnp.float32)
        ).astype(jnp.bfloat16).reshape(tile_units, unit_rows, -1)
        send(step * tile_units, tile_units)

    @pl.when(step == tiles)
    def _():
        joint_units = joint_ref.shape[0] // unit_rows
        made[buffer, pl.ds(0, joint_units)] = jnp.dot(
            joint_ref[...], normed_ref[...], preferred_element_type=jnp.float32
        ).astype(jnp.bfloat16).reshape(joint_units, unit_rows, -1)
        made[buffer, pl.ds(joint_units, last_units - joint_units)] = jnp.dot(
            attended_ref[...], grad_ref[...], preferred_element_type=jnp.float32
        ).astype(jnp.bfloat16).reshape(last_units - joint_units, unit_rows, -1)
        send(tiles * tile_units, last_units)
        settle(1 - buffer, tile_units)
        settle(buffer, last_units)


def weight_grads(
    place, slots, unit_rows, slope, rows, ids, zero, joint, normed, attended, grad, states
):
    vocab, tokens = slope.shape
    width = rows.shape[1]
    tile = vocab_tile(vocab)
    tiles = vocab // tile
    fixed = lambda k: (0, 0)
    whole = lambda x: pl.BlockSpec(x.shape, fixed)
    piece = pl.BlockSpec((states[0].shape[0] // (tiles + 1), states[0].shape[1]), lambda k: (k, 0))
    return pl.pallas_call(
        functools.partial(weight_grads_kernel, tile // unit_rows, tiles),
        grid=(tiles + 1,),
        out_shape=[jax.ShapeDtypeStruct((slots, unit_rows, width), jnp.bfloat16)]
        + [jax.ShapeDtypeStruct(states[0].shape, jnp.float32)] * 6,
        in_specs=[
            pl.BlockSpec(memory_space=pltpu.SMEM),
            pl.BlockSpec((tile, tokens), lambda k: (jnp.minimum(k, tiles - 1), 0)),
        ]
        + [whole(x) for x in (rows, ids, zero, joint, normed, attended, grad)]
        + [piece] * 8,
        out_specs=[whole_any] + [piece] * 6,
        scratch_shapes=[
            pltpu.VMEM((2, tile // unit_rows, unit_rows, width), jnp.bfloat16),
            pltpu.SemaphoreType.DMA((2,)),
        ],
        compiler_params=pltpu.CompilerParams(vmem_limit_bytes=60 << 20),
    )(place, slope, rows, ids, zero, joint, normed, attended, grad, *states)


def adam_update(weight, moment_one, moment_two, gradient, step_rate, decay_factor):
    moment_new = beta_first * moment_one + (1.0 - beta_first) * gradient
    square_new = beta_second * moment_two + (1.0 - beta_second) * gradient * gradient
    moment_hat = moment_new / (1.0 - beta_first**STEP)
    square_hat = square_new / (1.0 - beta_second**STEP)
    weight_new = weight - step_rate * (
        moment_hat / (jnp.sqrt(square_hat) + adam_epsilon) + decay_factor * weight
    )
    return (weight_new, moment_new, square_new)


def norm_forward(values, gain_row):
    return values * inverse_rms(values) * gain_row


def slot_tables(owner_ids, owners, most_units):
    unit_count = owner_ids.shape[0]
    unit_index = jnp.arange(unit_count, dtype=jnp.int32)
    earlier = (owner_ids[None, :] == owner_ids[:, None]) & (
        unit_index[None, :] < unit_index[:, None]
    )
    unit_rank = jnp.sum(earlier.astype(jnp.int32), 1)
    placed = (owner_ids[None, None, :] == jnp.arange(owners, dtype=jnp.int32)[:, None, None]) & (
        unit_rank[None, None, :] == jnp.arange(most_units, dtype=jnp.int32)[None, :, None]
    )
    slot_filled = jnp.any(placed, 2)
    slot_unit = jnp.sum(jnp.where(placed, unit_index[None, None, :], 0), 2)
    return (unit_rank, slot_unit, slot_filled)


def unit_rates(unit_ids, table_units, query_units, value_units):
    return jnp.where(
        unit_ids < table_units,
        rate_table,
        jnp.where(
            unit_ids < query_units,
            rate_query,
            jnp.where(unit_ids < value_units, rate_values, rate_project),
        ),
    )


def pair_slots(route_pairs, priorities, experts, capacity):
    tokens_here = priorities.shape[0]
    pair_expert = route_pairs.T.reshape(-1)
    pair_key = (
        jnp.arange(2, dtype=jnp.int32)[:, None] * tokens_here + priorities[None, :]
    ).reshape(-1)
    before = (pair_expert[None, :] == pair_expert[:, None]) & (
        pair_key[None, :] < pair_key[:, None]
    )
    pair_rank = jnp.sum(before.astype(jnp.int32), 1)
    pair_kept = pair_rank < capacity
    pair_dest = pair_expert * capacity + jnp.minimum(pair_rank, capacity - 1)
    return (pair_kept, pair_dest)


def gelu_tanh(values):
    return jax.nn.gelu(values, approximate=True)


def gelu_slope(values):
    root = math.sqrt(2.0 / math.pi)
    bent = jnp.tanh(root * (values + 0.044715 * values * values * values))
    return 0.5 * (1.0 + bent) + 0.5 * values * (1.0 - bent * bent) * root * (
        1.0 + 3.0 * 0.044715 * values * values
    )


def plane_peer(step):
    chip, core = lax.axis_index("dp"), lax.axis_index("ctx")
    row = lax.rem(chip // 2 + step // 4, 2)
    column = lax.rem(lax.rem(chip, 2) + lax.rem(step // 2, 2), 2)
    place = {"dp": row * 2 + column, "ctx": lax.rem(core + lax.rem(step, 2), 2)}
    return place, place["dp"] * 2 + place["ctx"]


def greet_plane():
    barrier = pltpu.get_barrier_semaphore()
    for step in range(1, 8):
        place, _ = plane_peer(step)
        pl.semaphore_signal(barrier, inc=1, device_id=place, device_id_type=MESH_ID)
    pl.semaphore_wait(barrier, 7)


def plane_copy(source, target, send_sem, recv_sem, step):
    place, _ = plane_peer(step)
    return pltpu.make_async_remote_copy(
        src_ref=source.at[step],
        dst_ref=target.at[step],
        send_sem=send_sem.at[step],
        recv_sem=recv_sem.at[step],
        device_id=place,
        device_id_type=MESH_ID,
    )


def slot_hits(dest_rows, expert, capacity, tokens):
    slot = lax.broadcasted_iota(jnp.int32, (capacity, tokens), 0) + expert * capacity
    return (slot == dest_rows[0:1, :]) | (slot == dest_rows[1:2, :])


def token_hits(dest_columns, expert, capacity, tokens):
    slot = lax.broadcasted_iota(jnp.int32, (tokens, capacity), 1) + expert * capacity
    hit = (slot == dest_columns[:, 0:1]) | (slot == dest_columns[:, 1:2])
    return jnp.where(hit, 1.0, 0.0).astype(jnp.bfloat16)


def gate_of(routes, gates, expert, axis):
    pick = (lambda a, k: a[k : k + 1, :]) if axis == 0 else (lambda a, k: a[:, k : k + 1])
    return jnp.where(pick(routes, 0) == expert, pick(gates, 0), 0.0) + jnp.where(
        pick(routes, 1) == expert, pick(gates, 1), 0.0
    )


def arrival(i):
    return jnp.where(i < 2, i, 9 - i)


def experts_kernel(
    rows_ref, dest_rows, dest_columns, gates, routes, inner_ref, outer_ref, counts_ref,
    mix_ref, arrived, returned, totals_ref,
    outgoing, results, counts, send_one, recv_one, send_two, recv_two, send_count, recv_count,
):
    capacity = arrived.shape[1]
    tokens = rows_ref.shape[0]
    greet_plane()
    counts[0] = counts_ref[...]

    def send_counts(step, carry):
        place, _ = plane_peer(step)
        pltpu.make_async_remote_copy(
            src_ref=counts_ref,
            dst_ref=counts.at[step],
            send_sem=send_count.at[step],
            recv_sem=recv_count.at[step],
            device_id=place,
            device_id_type=MESH_ID,
        ).start()
        return carry

    def dispatch(i, carry):
        step = 7 - i
        _, expert = plane_peer(step)
        hit = jnp.where(slot_hits(dest_rows, expert, capacity, tokens), 1.0, 0.0).astype(jnp.bfloat16)
        rows = jnp.dot(hit, rows_ref[...], preferred_element_type=jnp.float32).astype(jnp.bfloat16)

        @pl.when(step > 0)
        def _():
            outgoing[step] = rows
            plane_copy(outgoing, arrived, send_one, recv_one, step).start()

        @pl.when(step == 0)
        def _():
            arrived[0] = rows

        return carry

    def work(i, carry):
        step = arrival(i)

        @pl.when(step > 0)
        def _():
            plane_copy(outgoing, arrived, send_one, recv_one, step).wait_recv()

        before = jnp.dot(arrived[step], inner_ref[...], preferred_element_type=jnp.float32)
        active = gelu_tanh(before).astype(jnp.bfloat16)
        part = jnp.dot(active, outer_ref[...], preferred_element_type=jnp.float32).astype(jnp.bfloat16)

        @pl.when(step > 0)
        def _():
            results[step] = part
            plane_copy(results, returned, send_two, recv_two, step).start()

        @pl.when(step == 0)
        def _():
            returned[0] = part

        return carry

    def combine(i, carry):
        step = arrival(i)
        _, expert = plane_peer(step)
        hit = token_hits(dest_columns, expert, capacity, tokens)
        gate = gate_of(routes, gates, expert, 1)

        @pl.when(step > 0)
        def _():
            plane_copy(results, returned, send_two, recv_two, step).wait_recv()

        part = gate * jnp.dot(hit, returned[step], preferred_element_type=jnp.float32)

        @pl.when(i == 0)
        def _():
            mix_ref[...] = part

        @pl.when(i > 0)
        def _():
            mix_ref[...] += part

        return carry

    def finish(step, carry):
        plane_copy(outgoing, arrived, send_one, recv_one, step).wait_send()
        plane_copy(results, returned, send_two, recv_two, step).wait_send()
        place, _ = plane_peer(step)
        pltpu.make_async_remote_copy(
            src_ref=counts_ref,
            dst_ref=counts.at[step],
            send_sem=send_count.at[step],
            recv_sem=recv_count.at[step],
            device_id=place,
            device_id_type=MESH_ID,
        ).wait()
        return carry

    lax.fori_loop(0, 8, dispatch, 0)
    lax.fori_loop(1, 8, send_counts, 0)
    lax.fori_loop(0, 8, work, 0)
    lax.fori_loop(0, 8, combine, 0)
    lax.fori_loop(1, 8, finish, 0)
    totals_ref[...] = jnp.sum(counts[...], 0)


def experts_forward(rows, dest, gates, routes, inner, outer, counts, capacity, collective_id):
    tokens, width = rows.shape
    buffer = pltpu.VMEM((8, capacity, width), jnp.bfloat16)
    return pl.pallas_call(
        experts_kernel,
        out_shape=[
            jax.ShapeDtypeStruct((tokens, width), jnp.float32),
            jax.ShapeDtypeStruct((8, capacity, width), jnp.bfloat16),
            jax.ShapeDtypeStruct((8, capacity, width), jnp.bfloat16),
            jax.ShapeDtypeStruct(counts.shape, jnp.float32),
        ],
        in_specs=[whole_vmem] * 8,
        out_specs=[whole_vmem] * 4,
        scratch_shapes=[buffer, buffer, pltpu.VMEM((8,) + counts.shape, jnp.float32)]
        + [pltpu.SemaphoreType.DMA((8,))] * 6,
        compiler_params=pltpu.CompilerParams(
            collective_id=collective_id, has_side_effects=True, vmem_limit_bytes=60 << 20
        ),
    )(rows, dest, dest.T, gates, routes, inner, outer, counts)


def experts_back_kernel(
    rows_ref, dest_rows, dest_columns, gates, routes, returned, arrived, *refs
):
    inner_ref, outer_ref, grad_ref, gate_ref, inner_grad, outer_grad = refs[:6]
    outgoing, landed, results, landed_two, active, slopes = refs[6:12]
    send_one, recv_one, send_two, recv_two = refs[12:]
    capacity = arrived.shape[1]
    tokens = rows_ref.shape[0]
    greet_plane()
    gate_ref[...] = jnp.zeros_like(gate_ref)

    def dispatch(i, carry):
        step = 7 - i
        _, expert = plane_peer(step)
        hit = slot_hits(dest_rows, expert, capacity, tokens)
        rows = jnp.dot(
            jnp.where(hit, 1.0, 0.0).astype(jnp.bfloat16), rows_ref[...], preferred_element_type=jnp.float32
        )
        scale = jnp.sum(jnp.where(hit, gate_of(routes, gates, expert, 0), 0.0), 1, keepdims=True)
        sent = (rows * scale).astype(jnp.bfloat16)

        @pl.when(step > 0)
        def _():
            outgoing[step] = sent
            plane_copy(outgoing, landed, send_one, recv_one, step).start()

        @pl.when(step == 0)
        def _():
            landed[0] = sent

        dots = jnp.sum(rows * returned[step].astype(jnp.float32), 1, keepdims=True)
        part = jnp.sum(jnp.where(hit, dots, 0.0), 0, keepdims=True)
        for k in range(2):
            gate_ref[k : k + 1, :] += jnp.where(routes[k : k + 1, :] == expert, part, 0.0)
        return carry

    def work(i, carry):
        step = arrival(i)

        @pl.when(step > 0)
        def _():
            plane_copy(outgoing, landed, send_one, recv_one, step).wait_recv()

        grad_active = lax.dot_general(
            landed[step], outer_ref[...], (((1,), (1,)), ((), ())), preferred_element_type=jnp.float32
        )
        before = jnp.dot(arrived[step], inner_ref[...], preferred_element_type=jnp.float32)
        slope = (grad_active * gelu_slope(before)).astype(jnp.bfloat16)
        back = lax.dot_general(
            slope, inner_ref[...], (((1,), (1,)), ((), ())), preferred_element_type=jnp.float32
        ).astype(jnp.bfloat16)

        @pl.when(step > 0)
        def _():
            results[step] = back
            plane_copy(results, landed_two, send_two, recv_two, step).start()

        @pl.when(step == 0)
        def _():
            landed_two[0] = back

        slopes[step] = slope
        active[step] = gelu_tanh(before).astype(jnp.bfloat16)
        return carry

    def weigh(step, carry):
        outer_part = lax.dot_general(
            active[step], landed[step], (((0,), (0,)), ((), ())), preferred_element_type=jnp.float32
        )
        inner_part = lax.dot_general(
            arrived[step], slopes[step], (((0,), (0,)), ((), ())), preferred_element_type=jnp.float32
        )

        @pl.when(step == 0)
        def _():
            inner_grad[...] = inner_part
            outer_grad[...] = outer_part

        @pl.when(step > 0)
        def _():
            inner_grad[...] += inner_part
            outer_grad[...] += outer_part

        return carry

    def combine(i, carry):
        step = arrival(i)
        _, expert = plane_peer(step)
        hit = token_hits(dest_columns, expert, capacity, tokens)

        @pl.when(step > 0)
        def _():
            plane_copy(results, landed_two, send_two, recv_two, step).wait_recv()

        part = jnp.dot(hit, landed_two[step], preferred_element_type=jnp.float32)

        @pl.when(i == 0)
        def _():
            grad_ref[...] = part

        @pl.when(i > 0)
        def _():
            grad_ref[...] += part

        return carry

    def finish(step, carry):
        plane_copy(outgoing, landed, send_one, recv_one, step).wait_send()
        plane_copy(results, landed_two, send_two, recv_two, step).wait_send()
        return carry

    lax.fori_loop(0, 8, dispatch, 0)
    lax.fori_loop(0, 8, work, 0)
    lax.fori_loop(0, 8, weigh, 0)
    lax.fori_loop(0, 8, combine, 0)
    lax.fori_loop(1, 8, finish, 0)


def experts_backward(rows, dest, gates, routes, returned, arrived, inner, outer, collective_id):
    tokens, width = rows.shape
    capacity = arrived.shape[1]
    inside = inner.shape[1]
    buffer = pltpu.VMEM((8, capacity, width), jnp.bfloat16)
    inside_buffer = pltpu.VMEM((8, capacity, inside), jnp.bfloat16)
    return pl.pallas_call(
        experts_back_kernel,
        out_shape=[
            jax.ShapeDtypeStruct((tokens, width), jnp.float32),
            jax.ShapeDtypeStruct((2, tokens), jnp.float32),
            jax.ShapeDtypeStruct((width, inside), jnp.float32),
            jax.ShapeDtypeStruct((inside, width), jnp.float32),
        ],
        in_specs=[whole_vmem] * 9,
        out_specs=[whole_vmem] * 4,
        scratch_shapes=[buffer] * 4 + [inside_buffer] * 2 + [pltpu.SemaphoreType.DMA((8,))] * 4,
        compiler_params=pltpu.CompilerParams(
            collective_id=collective_id, has_side_effects=True, vmem_limit_bytes=60 << 20
        ),
    )(rows, dest, dest.T, gates, routes, returned, arrived, inner, outer)


def own_units_kernel(
    chunks, parts_ref, small_ref, grads_ref, small_out,
    own, other, relay, landed, small_landed,
    own_sem, other_send, other_recv, relay_send, relay_recv, landed_send, landed_recv, small_send, small_recv,
):
    chip, core = lax.axis_index("dp"), lax.axis_index("ctx")
    beside = chip + 1 - 2 * lax.rem(chip, 2)
    across = lax.rem(chip + 2, 4)
    opposite = across + 1 - 2 * lax.rem(across, 2)
    places = (opposite, beside, across, chip)
    slots = grads_ref.shape[0]
    size = slots // chunks
    split = (chunks + 1) // 2
    greet_plane()

    def span(q):
        return pl.ds(q * size, size)

    def fetch(k):
        first = (places[k] * 2 + core) * slots
        return pltpu.make_async_copy(parts_ref.at[pl.ds(first, slots)], own.at[k], own_sem.at[k])

    def pass_over(k, q):
        first = (places[k] * 2 + 1 - core) * slots + q * size
        return pltpu.make_async_remote_copy(
            src_ref=parts_ref.at[pl.ds(first, size)],
            dst_ref=other.at[k, span(q)],
            send_sem=other_send.at[k, q],
            recv_sem=other_recv.at[k, q],
            device_id={"ctx": 1 - core},
            device_id_type=MESH_ID,
        )

    def to_relay(q, place):
        return pltpu.make_async_remote_copy(
            src_ref=own.at[0, span(q)],
            dst_ref=relay.at[span(q)],
            send_sem=relay_send.at[q],
            recv_sem=relay_recv.at[q],
            device_id={"dp": place},
            device_id_type=MESH_ID,
        )

    def to_owner(k, q):
        return pltpu.make_async_remote_copy(
            src_ref=own.at[k, span(q)],
            dst_ref=landed.at[k - 1, span(q)],
            send_sem=landed_send.at[k - 1, q],
            recv_sem=landed_recv.at[k - 1, q],
            device_id={"dp": places[k]},
            device_id_type=MESH_ID,
        )

    def small_copy(step):
        place, _ = plane_peer(step)
        return pltpu.make_async_remote_copy(
            src_ref=small_ref,
            dst_ref=small_landed.at[chip * 2 + core],
            send_sem=small_send.at[step],
            recv_sem=small_recv.at[step],
            device_id=place,
            device_id_type=MESH_ID,
        )

    for k in range(4):
        fetch(k).start()

        def start(q, carry):
            pass_over(k, q).start()
            return carry

        lax.fori_loop(0, chunks, start, 0)

    def joined(k, q):
        pass_over(k, q).wait_recv()
        return own[k, span(q)].astype(jnp.float32) + other[k, span(q)].astype(jnp.float32)

    fetch(0).wait()

    def first_leg(place):
        def leg(q, carry):
            own[0, span(q)] = joined(0, q).astype(jnp.bfloat16)
            to_relay(q, place).start()
            return carry

        return leg

    lax.fori_loop(0, split, first_leg(beside), 0)
    lax.fori_loop(split, chunks, first_leg(across), 0)
    lax.fori_loop(1, 8, lambda step, carry: (small_copy(step).start(), carry)[1], 0)
    small_landed[chip * 2 + core] = small_ref[...]
    fetch(1).wait()
    fetch(2).wait()

    def direct(k):
        def leg(q, carry):
            own[k, span(q)] = joined(k, q).astype(jnp.bfloat16)
            to_owner(k, q).start()
            return carry

        return leg

    def relayed(k, place):
        def leg(q, carry):
            to_relay(q, place).wait_recv()
            total = joined(k, q) + relay[span(q)].astype(jnp.float32)
            own[k, span(q)] = total.astype(jnp.bfloat16)
            to_owner(k, q).start()
            return carry

        return leg

    lax.fori_loop(0, split, direct(1), 0)
    lax.fori_loop(split, chunks, direct(2), 0)
    lax.fori_loop(0, split, relayed(2, beside), 0)
    lax.fori_loop(split, chunks, relayed(1, across), 0)
    fetch(3).wait()

    def keep(q, carry):
        total = joined(3, q)
        to_owner(1, q).wait_recv()
        to_owner(2, q).wait_recv()
        grads_ref[span(q)] = (
            total + landed[0, span(q)].astype(jnp.float32) + landed[1, span(q)].astype(jnp.float32)
        )
        return carry

    lax.fori_loop(0, split, keep, 0)
    lax.fori_loop(split, chunks, keep, 0)

    def finish(q, carry):
        for k in range(4):
            pass_over(k, q).wait_send()
        to_owner(1, q).wait_send()
        to_owner(2, q).wait_send()
        return carry

    lax.fori_loop(0, chunks, finish, 0)
    lax.fori_loop(0, split, lambda q, carry: (to_relay(q, beside).wait_send(), carry)[1], 0)
    lax.fori_loop(split, chunks, lambda q, carry: (to_relay(q, across).wait_send(), carry)[1], 0)
    lax.fori_loop(1, 8, lambda step, carry: (small_copy(step).wait(), carry)[1], 0)
    total = small_landed[0]
    for source in range(1, 8):
        total = total + small_landed[source]
    small_out[...] = total


def own_units(parts, small, slots, collective_id):
    unit = parts.shape[1:]
    chunks = max(k for k in range(1, 8) if slots % k == 0)
    block = pltpu.VMEM((4, slots) + unit, jnp.bfloat16)
    return pl.pallas_call(
        functools.partial(own_units_kernel, chunks),
        out_shape=[
            jax.ShapeDtypeStruct((slots,) + unit, jnp.float32),
            jax.ShapeDtypeStruct(small.shape, jnp.float32),
        ],
        in_specs=[whole_any, whole_vmem],
        out_specs=[whole_vmem] * 2,
        scratch_shapes=[
            block,
            block,
            pltpu.VMEM((slots,) + unit, jnp.bfloat16),
            pltpu.VMEM((2, slots) + unit, jnp.bfloat16),
            pltpu.VMEM((8,) + small.shape, jnp.float32),
            pltpu.SemaphoreType.DMA((4,)),
            pltpu.SemaphoreType.DMA((4, chunks)),
            pltpu.SemaphoreType.DMA((4, chunks)),
            pltpu.SemaphoreType.DMA((chunks,)),
            pltpu.SemaphoreType.DMA((chunks,)),
            pltpu.SemaphoreType.DMA((2, chunks)),
            pltpu.SemaphoreType.DMA((2, chunks)),
            pltpu.SemaphoreType.DMA((8,)),
            pltpu.SemaphoreType.DMA((8,)),
        ],
        compiler_params=pltpu.CompilerParams(
            collective_id=collective_id, has_side_effects=True, vmem_limit_bytes=56 << 20
        ),
    )(parts, small)


def to_plane(buffer):
    return lax.all_to_all(buffer, ("dp", "ctx"), split_axis=0, concat_axis=0, tiled=True)


def plain_hits(dest, experts, capacity):
    slots = lax.broadcasted_iota(jnp.int32, (experts * capacity, dest.shape[1]), 0)
    return [slots == dest[k : k + 1] for k in range(2)]


def plain_forward(rows, dest, gates, inner, outer, owners, capacity):
    width = rows.shape[1]
    hits = plain_hits(dest, owners, capacity)
    both = (hits[0] | hits[1]).astype(jnp.bfloat16)
    sent = jnp.dot(both, rows, preferred_element_type=jnp.float32).astype(jnp.bfloat16)
    arrived = to_plane(sent.reshape(owners, capacity, width))
    hidden = jnp.einsum("ocd,df->ocf", arrived, inner, preferred_element_type=jnp.float32)
    active = gelu_tanh(hidden).astype(jnp.bfloat16)
    part = jnp.einsum("ocf,fd->ocd", active, outer, preferred_element_type=jnp.float32)
    returned = to_plane(part.astype(jnp.bfloat16))
    flat = returned.reshape(owners * capacity, width)
    mix = sum(
        gates[:, k : k + 1]
        * lax.dot_general(
            hits[k].astype(jnp.bfloat16),
            flat,
            (((0,), (0,)), ((), ())),
            preferred_element_type=jnp.float32,
        )
        for k in range(2)
    )
    return (mix, arrived, returned)


def plain_backward(rows, dest, gates, returned, arrived, inner, outer):
    owners, capacity, width = arrived.shape
    hits = plain_hits(dest, owners, capacity)
    both = (hits[0] | hits[1]).astype(jnp.bfloat16)
    slot_scale = jnp.sum(
        jnp.where(hits[0], gates[0:1], 0.0) + jnp.where(hits[1], gates[1:2], 0.0), 1, keepdims=True
    )
    slot_grads = jnp.dot(both, rows, preferred_element_type=jnp.float32)
    sent = (slot_grads * slot_scale).astype(jnp.bfloat16)
    flat = returned.reshape(owners * capacity, width)
    dots = jnp.sum(slot_grads * flat.astype(jnp.float32), 1, keepdims=True)
    gate_part = jnp.concatenate(
        [jnp.sum(jnp.where(hit, dots, 0.0), 0, keepdims=True) for hit in hits], 0
    )
    landed = to_plane(sent.reshape(owners, capacity, width))
    grad_active = jnp.einsum("ocd,fd->ocf", landed, outer, preferred_element_type=jnp.float32)
    hidden = jnp.einsum("ocd,df->ocf", arrived, inner, preferred_element_type=jnp.float32)
    active = gelu_tanh(hidden).astype(jnp.bfloat16)
    slope = (grad_active * gelu_slope(hidden)).astype(jnp.bfloat16)
    outer_grad = jnp.einsum("ocf,ocd->fd", active, landed, preferred_element_type=jnp.float32)
    inner_grad = jnp.einsum("ocd,ocf->df", arrived, slope, preferred_element_type=jnp.float32)
    back = jnp.einsum("ocf,df->ocd", slope, inner, preferred_element_type=jnp.float32)
    back = to_plane(back.astype(jnp.bfloat16)).reshape(owners * capacity, width)
    grad = lax.dot_general(
        both, back, (((0,), (0,)), ((), ())), preferred_element_type=jnp.float32
    )
    return (grad, gate_part, inner_grad, outer_grad)


def on_device(
    token_ids,
    targets,
    counted,
    routes,
    priority,
    owner_of,
    master,
    master_first,
    master_second,
    expert_in,
    expert_in_first,
    expert_in_second,
    expert_out,
    expert_out_first,
    expert_out_second,
    norm_gains,
    norm_gains_first,
    norm_gains_second,
    router,
    router_first,
    router_second,
    rel_bias,
    rel_bias_first,
    rel_bias_second,
):
    owners = lax.axis_size(("dp", "ctx"))
    tensor_ranks = lax.axis_size("tensor")
    my_owner = lax.axis_index(("dp", "ctx"))
    my_rank = lax.axis_index("tensor")
    my_context = lax.axis_index("ctx")
    sequences, half_length = token_ids.shape
    tokens_here = sequences * half_length
    most_units = master.shape[2]
    unit_rows = master.shape[3]
    model_width = master.shape[4]
    vocab_here = VOCAB // tensor_ranks
    heads_here = rel_bias.shape[0]
    head_size = model_width // (heads_here * tensor_ranks)
    hidden_here = heads_here * head_size
    experts = router.shape[1]
    capacity = (18 * tokens_here + 8 * experts - 1) // (8 * experts)
    table_units = vocab_here // unit_rows
    query_units = table_units + 2 * hidden_here // unit_rows
    value_units = table_units + 3 * hidden_here // unit_rows
    embed_scale = math.sqrt(model_width)
    owner_ids = owner_of[:, 0]
    on_square = lax.axis_size("dp") == 4 and lax.axis_size("ctx") == 2
    unit_rank, slot_unit, slot_filled = slot_tables(owner_ids, owners, most_units)
    counted_rows = counted.reshape(tokens_here, 2).T.astype(jnp.float32)
    loss_weights = counted_rows * jnp.array([[1.0], [ahead_weight]], jnp.float32)
    counts = jnp.zeros((8, 128), jnp.float32).at[0:2].set(jnp.sum(counted_rows, 1, keepdims=True))
    unit_slots = owner_ids * most_units + unit_rank
    route_pairs = routes.reshape(tokens_here, 2)
    pair_kept, pair_dest = pair_slots(route_pairs, priority[0], experts, capacity)
    dest = jnp.where(pair_kept, pair_dest, -1).reshape(2, tokens_here)
    unit_slots, dest = lax.optimization_barrier((unit_slots, dest))
    local_ids = token_ids.reshape(-1) - my_rank * vocab_here
    inside = (local_ids >= 0) & (local_ids < vocab_here)
    clipped_ids = jnp.clip(local_ids, 0, vocab_here - 1)
    master_low = master[0, 0].astype(jnp.bfloat16)
    unit_starts = jnp.sum(
        jnp.where(
            (clipped_ids // unit_rows)[None, :] == jnp.arange(unit_slots.shape[0])[:, None],
            unit_slots[:, None] * unit_rows,
            0,
        ),
        0,
    )
    slot_rows = unit_starts + clipped_ids % unit_rows
    if on_square:
        slot_rows = jnp.where(inside, slot_rows, -1)[:, None]
        weights_low, looked = gather_units(unit_slots, master_low, slot_rows, 11)
    else:
        gathered = lax.all_gather(master_low, ("dp", "ctx"), axis=0, tiled=True)
        looked = jnp.take(gathered.reshape(-1, model_width), slot_rows, axis=0)
        looked = jnp.where(inside[:, None], looked, 0)
        weights_low = pull_units([gathered], unit_slots)
    weights_low = weights_low.reshape(-1, model_width)
    (embedded,) = sum_line(looked, [], [], keep_total, 1)
    joint_low = weights_low[vocab_here : vocab_here + 3 * hidden_here]
    project_low = weights_low[vocab_here + 3 * hidden_here :]
    rolled = [project_low] + [
        lax.ppermute(project_low, "tensor", [(source, (source + step) % 4) for source in range(4)])
        for step in (1, 2, 3)
    ]
    gain_rows = [norm_gains[k : k + 1] for k in range(3)]
    stream_shape = jax.ShapeDtypeStruct((tokens_here, model_width), jnp.float32)
    gain_shape = jax.ShapeDtypeStruct((1, model_width), jnp.float32)
    stream_zero = embedded.astype(jnp.float32) * embed_scale
    first_normalized = norm_forward(stream_zero, norm_gains[0])
    normed_one_low = first_normalized.astype(jnp.bfloat16)
    joint = lax.dot_general(
        joint_low, normed_one_low, (((1,), (1,)), ((), ())), preferred_element_type=jnp.float32
    ).astype(jnp.bfloat16)
    pairs_before = passed_along(joint[hidden_here:], "ctx", 1)
    attended, logsum_rows = attention(rel_bias, joint, pairs_before, heads_here, head_size)
    (attended_all,) = gather_line([attended], 2)
    router_low = router.astype(jnp.bfloat16)
    stream_one, normed_two_low, gate_rows, gate_columns = middle(
        attended_all.reshape(model_width, tokens_here),
        rolled,
        embedded,
        gain_rows[1],
        router_low.T,
        route_pairs.T,
    )
    inner_low = expert_in[0].astype(jnp.bfloat16)
    outer_low = expert_out[0].astype(jnp.bfloat16)
    if on_square:
        moe_partial, arrived, returned, counts = experts_forward(
            normed_two_low, dest, gate_columns, route_pairs, inner_low, outer_low, counts, capacity, 8
        )
    else:
        moe_partial, arrived, returned = plain_forward(
            normed_two_low, dest, gate_columns, inner_low, outer_low, owners, capacity
        )
        counts = lax.psum(counts, ("dp", "ctx"))
    weight_total = counts[0, 0] + ahead_weight * counts[1, 0]
    local_targets = targets.reshape(tokens_here, 2).T - my_rank * vocab_here
    weight_rows = jnp.concatenate(
        [
            loss_weights,
            loss_weights[0:1] + loss_weights[1:2],
            jnp.broadcast_to(1.0 / weight_total, (1, tokens_here)),
        ],
        0,
    )
    head_low, grad_two_low, grad_two, gain_grad_three, logsum_vocab, target_sums, slopes = head_line(
        moe_partial, stream_one, gain_rows[2], weights_low, local_targets, weight_rows, vocab_here, 3
    )
    if on_square:
        moe_grad_part, gate_part, inner_grad, outer_grad = experts_backward(
            grad_two_low,
            dest,
            gate_rows,
            route_pairs.T,
            returned,
            arrived,
            inner_low,
            outer_low,
            9,
        )
    else:
        moe_grad_part, gate_part, inner_grad, outer_grad = plain_backward(
            grad_two_low, dest, gate_rows, returned, arrived, inner_low, outer_low
        )
    gate_part = jnp.concatenate([gate_part, target_sums, jnp.zeros_like(target_sums)], 0)
    gate_block = pltpu.VMEM((3, 4, tokens_here), jnp.float32)
    grad_one_low, grad_one, logit_grad, target_total, gain_grad_two = sum_line(
        moe_grad_part,
        [
            stream_one,
            gain_rows[1],
            grad_two,
            gate_part,
            gate_rows,
            route_pairs.T,
            router_low,
        ],
        [
            stream_shape,
            jax.ShapeDtypeStruct((experts, tokens_here), jnp.bfloat16),
            jax.ShapeDtypeStruct((1, tokens_here), jnp.float32),
            gain_shape,
        ],
        finish_expert_grad,
        5,
        prologue=start_router_grad,
        scratch=(gate_block, pltpu.SemaphoreType.DMA((3,)), pltpu.SemaphoreType.DMA((3,))),
        opening=send_gate_parts,
    )
    router_grad = jnp.dot(logit_grad, normed_two_low, preferred_element_type=jnp.float32)
    loss_local = jnp.sum(weight_rows[2:3] * logsum_vocab) - jnp.sum(target_total)
    query_grad, pair_grad, before_grad, bias_lines = attention_back(
        rel_bias,
        joint,
        pairs_before,
        logsum_rows,
        grad_one_low,
        project_low,
        heads_here,
        head_size,
    )
    grad_after = passed_along(before_grad, "ctx", -1)
    pair_grad_low = (pair_grad + grad_after.astype(jnp.float32)).astype(jnp.bfloat16)
    joint_grad = jnp.concatenate([query_grad, pair_grad_low], 0)
    distances = 2 * (half_length // BLOCK)
    bias_grad = jnp.sum(bias_lines, 1).reshape(heads_here, distances)
    zero_grad_low, gain_grads = sum_line(
        lax.dot_general(
            joint_grad, joint_low, (((0,), (0,)), ((), ())), preferred_element_type=jnp.float32
        ),
        [embedded, gain_rows[0], grad_one, gain_grad_two, gain_grad_three],
        [jax.ShapeDtypeStruct((8, model_width), jnp.float32)],
        functools.partial(finish_input_grad, embed_scale),
        6,
        prologue=clear_gain,
        scratch=(pltpu.SemaphoreType.DMA, pltpu.SemaphoreType.DMA),
        ending=share_gains,
    )
    my_units = jnp.take(slot_unit, my_owner, axis=0)
    my_filled = jnp.take(slot_filled, my_owner, axis=0)[:, None, None]
    outgoing, *expert_states = weight_grads(
        unit_slots,
        owners * most_units,
        unit_rows,
        slopes,
        head_low,
        local_ids[None, :],
        zero_grad_low,
        joint_grad,
        normed_one_low,
        attended,
        grad_one_low,
        (
            expert_in[0],
            expert_in_first[0],
            expert_in_second[0],
            inner_grad,
            expert_out[0],
            expert_out_first[0],
            expert_out_second[0],
            outer_grad,
        ),
    )
    bias_row = jnp.concatenate([bias_grad.reshape(-1), loss_local[None]])
    bias_row = jnp.pad(bias_row, (0, model_width - bias_row.shape[0]))[None]
    small = jnp.concatenate([gain_grads[:3], router_grad, bias_row], 0)
    small = jnp.pad(small, ((0, -small.shape[0] % 8), (0, 0)))
    slot_rates = unit_rates(my_units, table_units, query_units, value_units)[:, None, None]
    states = (master[0, 0], master_first[0, 0], master_second[0, 0])
    if on_square:
        mine, small = own_units(outgoing, small, most_units, 10)
    else:
        mine = lax.psum_scatter(
            outgoing.astype(jnp.float32), ("dp", "ctx"), scatter_dimension=0, tiled=True
        )
        small = lax.psum(small, ("dp", "ctx"))
    states = adam_update(*states, jnp.where(my_filled, mine, 0.0), slot_rates, decay_rate)
    gains_grad = small[:3]
    router_grad = small[3 : 3 + experts].T
    bias_grad = small[3 + experts, : rel_bias.size].reshape(rel_bias.shape)
    loss_totals = jnp.stack([small[3 + experts, rel_bias.size], weight_total])
    gains_new, gains_first_new, gains_second_new = adam_update(
        norm_gains, norm_gains_first, norm_gains_second, gains_grad, rate_gains, 0.0
    )
    router_new, router_first_new, router_second_new = adam_update(
        router, router_first, router_second, router_grad, rate_router, decay_rate
    )
    biases_new, biases_first_new, biases_second_new = adam_update(
        rel_bias, rel_bias_first, rel_bias_second, bias_grad, rate_biases, 0.0
    )
    return (
        loss_totals,
        *(state[None, None] for state in states),
        *(state[None] for state in expert_states),
        gains_new,
        gains_first_new,
        gains_second_new,
        router_new,
        router_first_new,
        router_second_new,
        biases_new,
        biases_first_new,
        biases_second_new,
    )


def solution(mesh):
    in_specs = (
        P("dp", "ctx"),
        P("dp", "ctx", None),
        P("dp", "ctx", None),
        P("dp", "ctx", None),
        P(("dp", "ctx"), None),
        P(),
        P("tensor", ("dp", "ctx"), None, None, None),
        P("tensor", ("dp", "ctx"), None, None, None),
        P("tensor", ("dp", "ctx"), None, None, None),
        P(("dp", "ctx"), None, "tensor"),
        P(("dp", "ctx"), None, "tensor"),
        P(("dp", "ctx"), None, "tensor"),
        P(("dp", "ctx"), "tensor", None),
        P(("dp", "ctx"), "tensor", None),
        P(("dp", "ctx"), "tensor", None),
        P(),
        P(),
        P(),
        P(),
        P(),
        P(),
        P("tensor", None),
        P("tensor", None),
        P("tensor", None),
    )
    out_specs = (
        P(),
        P("tensor", ("dp", "ctx"), None, None, None),
        P("tensor", ("dp", "ctx"), None, None, None),
        P("tensor", ("dp", "ctx"), None, None, None),
        P(("dp", "ctx"), None, "tensor"),
        P(("dp", "ctx"), None, "tensor"),
        P(("dp", "ctx"), None, "tensor"),
        P(("dp", "ctx"), "tensor", None),
        P(("dp", "ctx"), "tensor", None),
        P(("dp", "ctx"), "tensor", None),
        P(),
        P(),
        P(),
        P(),
        P(),
        P(),
        P("tensor", None),
        P("tensor", None),
        P("tensor", None),
    )
    return jax.shard_map(
        on_device, mesh=mesh, in_specs=in_specs, out_specs=out_specs, check_vma=False
    )
```

```python
import functools
import math

import jax
import jax.numpy as jnp
from jax import lax
from jax.experimental import pallas as pl
from jax.experimental.pallas import tpu as pltpu
from jax.sharding import PartitionSpec as P

VOCAB = 32000
BLOCK = 256
STEP = 10


highest_precision = lax.Precision.HIGHEST
beta_first = 0.9
beta_second = 0.95
adam_epsilon = 1e-08
norm_epsilon = 1e-06
ahead_weight = 0.3
masked_score = -1e30
rate_table = 0.1
rate_query = 0.05
rate_values = 0.05
rate_project = 0.5
rate_inner = 0.05
rate_outer = 0.03
rate_gains = 0.5
rate_router = 0.05
rate_biases = 0.5
decay_rate = 0.1


def passed_along(value, axis, steps):
    count = lax.axis_size(axis)
    initial, last = (max(0, -steps), min(count, count - steps))
    return lax.ppermute(value, axis, [(source, source + steps) for source in range(initial, last)])

MESH_ID = pl.DeviceIdType.MESH
whole_vmem = pl.BlockSpec(memory_space=pltpu.VMEM)
whole_any = pl.BlockSpec(memory_space=pl.ANY)
line_lag = 2


def sum_line_kernel(
    rows, count, opening, prologue, epilogue, ending, n_extra, n_aux, n_scratch, part_ref, *refs
):
    extras = refs[:n_extra]
    out_ref = refs[n_extra]
    aux = refs[n_extra + 1 : n_extra + 1 + n_aux]
    rest = refs[n_extra + 1 + n_aux :]
    scratch = rest[:n_scratch]
    stage, from_end, from_mid, send_sem, end_sem, mid_sem, back_sem, back_recv = rest[n_scratch:]
    rank = lax.axis_index("tensor")
    inner = (rank == 1) | (rank == 2)
    end_peer = jnp.where(rank < 2, 1 - rank, 5 - rank)
    mid_peer = 3 - rank
    barrier = pltpu.get_barrier_semaphore()
    if opening is None:
        pl.semaphore_signal(barrier, inc=1, device_id={"tensor": end_peer}, device_id_type=MESH_ID)

        @pl.when(inner)
        def _():
            pl.semaphore_signal(
                barrier, inc=1, device_id={"tensor": mid_peer}, device_id_type=MESH_ID
            )
            pl.semaphore_wait(barrier, 2)

        @pl.when(jnp.logical_not(inner))
        def _():
            pl.semaphore_wait(barrier, 1)
    else:
        for step in (1, 2, 3):
            other = lax.rem(rank + step, 4)
            pl.semaphore_signal(barrier, inc=1, device_id={"tensor": other}, device_id_type=MESH_ID)
        pl.semaphore_wait(barrier, 3)

    def span(i):
        return pl.ds(pl.multiple_of(i * rows, rows), rows)

    def to_inner(i):
        return pltpu.make_async_remote_copy(
            src_ref=stage.at[i],
            dst_ref=from_end.at[i],
            send_sem=send_sem.at[i],
            recv_sem=end_sem.at[i],
            device_id={"tensor": end_peer},
            device_id_type=MESH_ID,
        )

    def to_middle(i):
        return pltpu.make_async_remote_copy(
            src_ref=stage.at[i],
            dst_ref=from_mid.at[i],
            send_sem=send_sem.at[i],
            recv_sem=mid_sem.at[i],
            device_id={"tensor": mid_peer},
            device_id_type=MESH_ID,
        )

    def to_end(i):
        return pltpu.make_async_remote_copy(
            src_ref=out_ref.at[span(i)],
            dst_ref=out_ref.at[span(i)],
            send_sem=back_sem.at[i],
            recv_sem=back_recv.at[i],
            device_id={"tensor": end_peer},
            device_id_type=MESH_ID,
        )

    if opening is not None:
        opening(rank, extras, scratch)

    @pl.when(jnp.logical_not(inner))
    def _():
        def push(i, carry):
            stage[i] = part_ref[span(i)].astype(jnp.bfloat16)
            to_inner(i).start()
            return carry

        lax.fori_loop(0, count, push, 0)

    if prologue is not None:
        prologue(rank, inner, extras, aux, scratch)

    @pl.when(inner)
    def _():
        def step(i, carry):
            @pl.when(i < count)
            def _():
                to_inner(i).wait_recv()
                mine = part_ref[span(i)].astype(jnp.float32) + from_end[i].astype(jnp.float32)
                stage[i] = mine.astype(jnp.bfloat16)
                to_middle(i).start()

            @pl.when(i >= line_lag)
            def _():
                j = i - line_lag
                to_middle(j).wait_recv()
                total = stage[j].astype(jnp.float32) + from_mid[j].astype(jnp.float32)
                out_ref[span(j)] = epilogue(total, span(j), rank, extras, aux, scratch)
                to_end(j).start()

            return carry

        lax.fori_loop(0, count + line_lag, step, 0)

        def drain(i, carry):
            to_middle(i).wait_send()
            to_end(i).wait_send()
            return carry

        lax.fori_loop(0, count, drain, 0)

    @pl.when(jnp.logical_not(inner))
    def _():
        def finish(i, carry):
            to_end(i).wait_recv()
            to_inner(i).wait_send()
            return carry

        lax.fori_loop(0, count, finish, 0)

    if ending is not None:
        ending(inner, end_peer, extras, aux, scratch)


def sum_line(
    part,
    extras,
    aux_shapes,
    epilogue,
    collective_id,
    prologue=None,
    scratch=(),
    opening=None,
    ending=None,
    rows=64,
):
    tokens, width = part.shape
    count = tokens // rows
    chunks = pltpu.VMEM((count, rows, width), jnp.bfloat16)
    return pl.pallas_call(
        functools.partial(
            sum_line_kernel,
            rows,
            count,
            opening,
            prologue,
            epilogue,
            ending,
            len(extras),
            len(aux_shapes),
            len(scratch),
        ),
        out_shape=[jax.ShapeDtypeStruct((tokens, width), jnp.bfloat16)] + list(aux_shapes),
        in_specs=[whole_vmem] * (1 + len(extras)),
        out_specs=[whole_vmem] * (1 + len(aux_shapes)),
        scratch_shapes=list(scratch)
        + [chunks, chunks, chunks]
        + [pltpu.SemaphoreType.DMA((count,))] * 5,
        compiler_params=pltpu.CompilerParams(
            collective_id=collective_id, has_side_effects=True, vmem_limit_bytes=48 << 20
        ),
    )(part, *extras)


def keep_total(total, span, rank, extras, aux, scratch):
    return total.astype(jnp.bfloat16)


def inverse_rms(values):
    return lax.rsqrt(jnp.mean(values * values, -1, keepdims=True) + norm_epsilon)


def norm_back_rows(values, gain, upstream):
    inverse = inverse_rms(values)
    normed = values * inverse
    scaled = upstream * gain
    gain_grad = jnp.sum(upstream * normed, 0, keepdims=True)
    inputs_grad = inverse * (scaled - normed * jnp.mean(scaled * normed, -1, keepdims=True))
    return (inputs_grad, gain_grad)


def clear_gain(rank, inner, extras, aux, scratch):
    @pl.when(inner)
    def _():
        aux[-1][...] = jnp.zeros_like(aux[-1])


def share_gains(inner, end_peer, extras, aux, scratch):
    gains = aux[0]
    copy = pltpu.make_async_remote_copy(
        src_ref=gains,
        dst_ref=gains,
        send_sem=scratch[0],
        recv_sem=scratch[1],
        device_id={"tensor": end_peer},
        device_id_type=MESH_ID,
    )

    @pl.when(inner)
    def _():
        gains[1:2, :] = extras[3][...]
        gains[2:3, :] = extras[4][...]
        copy.start()
        copy.wait_send()

    @pl.when(jnp.logical_not(inner))
    def _():
        copy.wait_recv()


def gate_copies(rank, extras, scratch):
    gate_part = extras[3]
    landed, gate_send, gate_recv = scratch
    return [
        pltpu.make_async_remote_copy(
            src_ref=gate_part,
            dst_ref=landed.at[step - 1],
            send_sem=gate_send.at[step - 1],
            recv_sem=gate_recv.at[step - 1],
            device_id={"tensor": lax.rem(rank + step, 4)},
            device_id_type=MESH_ID,
        )
        for step in (1, 2, 3)
    ]


def send_gate_parts(rank, extras, scratch):
    for copy in gate_copies(rank, extras, scratch):
        copy.start()


def start_router_grad(rank, inner, extras, aux, scratch):
    stream_one, gain, grad_two, gate_part, gates, routes, router_low = extras
    grad_one, logit_grad, target_total, gain_grad = aux
    landed = scratch[0]
    clear_gain(rank, inner, extras, aux, scratch)
    for copy in gate_copies(rank, extras, scratch):
        copy.wait()
    gate_grad = jnp.zeros(gate_part.shape, jnp.float32)
    for source in range(4):
        piece = jnp.zeros(gate_part.shape, jnp.float32)
        for step in (1, 2, 3):
            piece = jnp.where(lax.rem(source + step, 4) == rank, landed[step - 1], piece)
        gate_grad = gate_grad + jnp.where(rank == source, gate_part[...], piece)
    target_total[...] = gate_grad[2:3]
    gate_grad = gate_grad[0:2]
    weighted = gates[...] * gate_grad
    chosen = gates[...] * (gate_grad - (weighted[0:1] + weighted[1:2]))
    experts, tokens = logit_grad.shape
    row = lax.broadcasted_iota(jnp.int32, (experts, tokens), 0)
    placed = jnp.where(row == routes[0:1], chosen[0:1], 0.0) + jnp.where(
        row == routes[1:2], chosen[1:2], 0.0
    )
    logit_grad[...] = placed.astype(jnp.bfloat16)

    @pl.when(inner)
    def _():
        grad_one[...] = lax.dot_general(
            logit_grad[...],
            router_low[...],
            (((0,), (1,)), ((), ())),
            preferred_element_type=jnp.float32,
        )


def finish_expert_grad(total, span, rank, extras, aux, scratch):
    stream_one, gain, grad_two, gate_part, gates, routes, router_low = extras
    grad_one, logit_grad, target_total, gain_grad = aux
    part, gain_part = norm_back_rows(
        stream_one[span], gain[...], total + grad_one[span]
    )
    result = grad_two[span] + part
    grad_one[span] = result
    gain_grad[...] += gain_part
    return result.astype(jnp.bfloat16)


def finish_input_grad(scale, total, span, rank, extras, aux, scratch):
    embedded, gain, grad_one = extras[:3]
    stream_zero = embedded[span].astype(jnp.float32) * scale
    part, gain_part = norm_back_rows(stream_zero, gain[...], total)
    aux[0][0:1, :] += gain_part
    return ((grad_one[span] + part) * scale).astype(jnp.bfloat16)


def gather_line_kernel(count, *refs):
    ins = refs[:count]
    outs = refs[count : 2 * count]
    local_sem, send_sem, recv_sem = refs[2 * count :]
    rank = lax.axis_index("tensor")
    barrier = pltpu.get_barrier_semaphore()
    for step in (1, 2, 3):
        other = lax.rem(rank + step, 4)
        pl.semaphore_signal(barrier, inc=1, device_id={"tensor": other}, device_id_type=MESH_ID)
    pl.semaphore_wait(barrier, 3)
    copies = []
    for k in range(count):
        for step in (1, 2, 3):
            copy = pltpu.make_async_remote_copy(
                src_ref=ins[k],
                dst_ref=outs[k].at[rank],
                send_sem=send_sem.at[k, step - 1],
                recv_sem=recv_sem.at[k, step - 1],
                device_id={"tensor": lax.rem(rank + step, 4)},
                device_id_type=MESH_ID,
            )
            copy.start()
            copies.append(copy)
        own = pltpu.make_async_copy(ins[k], outs[k].at[rank], local_sem.at[k])
        own.start()
        own.wait()
    for copy in copies:
        copy.wait()


def gather_line(arrays, collective_id):
    count = len(arrays)
    return pl.pallas_call(
        functools.partial(gather_line_kernel, count),
        out_shape=[jax.ShapeDtypeStruct((4,) + x.shape, x.dtype) for x in arrays],
        in_specs=[whole_vmem] * count,
        out_specs=[whole_vmem] * count,
        scratch_shapes=[
            pltpu.SemaphoreType.DMA((count,)),
            pltpu.SemaphoreType.DMA((count, 3)),
            pltpu.SemaphoreType.DMA((count, 3)),
        ],
        compiler_params=pltpu.CompilerParams(
            collective_id=collective_id, has_side_effects=True, vmem_limit_bytes=40 << 20
        ),
    )(*arrays)


def middle_kernel(
    attended_ref, embedded_ref, gain_ref, router_ref, routes_ref, *refs
):
    rolled, (stream_ref, normed_ref, rows_ref, columns_ref, project_ref) = refs[:4], refs[4:]

    @pl.when(pl.program_id(0) == 0)
    def _():
        for step in range(4):
            lines = rolled[step].shape[0]
            owner = lax.rem(lax.axis_index("tensor") + 4 - step, 4)
            project_ref[pl.ds(pl.multiple_of(owner * lines, lines), lines)] = rolled[step][...]

    scale = math.sqrt(embedded_ref.shape[1])
    stream = embedded_ref[...].astype(jnp.float32) * scale + lax.dot_general(
        attended_ref[...], project_ref[...], (((0,), (0,)), ((), ())), preferred_element_type=jnp.float32
    )
    stream_ref[...] = stream
    normed = (stream * inverse_rms(stream) * gain_ref[...]).astype(jnp.bfloat16)
    normed_ref[...] = normed
    scores = lax.dot_general(
        router_ref[...], normed, (((1,), (1,)), ((), ())), preferred_element_type=jnp.float32
    )
    expert = lax.broadcasted_iota(jnp.int32, scores.shape, 0)
    first, second = (
        jnp.sum(jnp.where(expert == routes_ref[k : k + 1, :], scores, 0.0), 0, keepdims=True)
        for k in range(2)
    )
    top = jnp.maximum(first, second)
    first, second = jnp.exp(first - top), jnp.exp(second - top)
    total = first + second
    gates = jnp.concatenate([first / total, second / total], 0)
    rows_ref[...] = gates
    columns_ref[...] = jnp.concatenate([gates, jnp.zeros((6, gates.shape[1]), jnp.float32)], 0).T


def middle(attended, rolled, embedded, gain, router, routes):
    tokens, width = embedded.shape
    tile = 256
    fixed = lambda k: (0, 0)
    whole = lambda x: pl.BlockSpec(x.shape, fixed)
    down = lambda n: pl.BlockSpec((tile, n), lambda k: (k, 0))
    along = lambda n: pl.BlockSpec((n, tile), lambda k: (0, k))
    return pl.pallas_call(
        middle_kernel,
        grid=(tokens // tile,),
        out_shape=[
            jax.ShapeDtypeStruct((tokens, width), jnp.float32),
            jax.ShapeDtypeStruct((tokens, width), jnp.bfloat16),
            jax.ShapeDtypeStruct((2, tokens), jnp.float32),
            jax.ShapeDtypeStruct((tokens, 8), jnp.float32),
        ],
        in_specs=[along(width), down(width), whole(gain), whole(router), along(2)]
        + [whole(x) for x in rolled],
        out_specs=[down(width), down(width), along(2), down(8)],
        scratch_shapes=[pltpu.VMEM((width, width), jnp.bfloat16)],
        compiler_params=pltpu.CompilerParams(vmem_limit_bytes=40 << 20),
    )(attended, embedded, gain, router, routes, *rolled)


def embed_kernel(chunks, slots_ref, mine_ref, rows_ref, units_ref, embedded_ref, *refs):
    held, total, stage, from_end, from_mid = refs[:5]
    send_x, recv_x, send_y, recv_y, send_z, recv_z, send_core, recv_core = refs[5:13]
    send_sem, end_sem, mid_sem, back_sem, back_recv = refs[13:]
    chip, core = lax.axis_index("dp"), lax.axis_index("ctx")
    beside = chip + 1 - 2 * lax.rem(chip, 2)
    across = lax.rem(chip + 2, 4)
    opposite = across + 1 - 2 * lax.rem(across, 2)
    places = (chip, beside, across, opposite)
    rank = lax.axis_index("tensor")
    inner = (rank == 1) | (rank == 2)
    end_peer = jnp.where(rank < 2, 1 - rank, 5 - rank)
    mid_peer = 3 - rank
    slots, unit_rows = mine_ref.shape[:2]
    width = total.shape[2]
    size = slots // chunks
    split = (chunks + 1) // 2
    tokens = rows_ref.shape[0]
    count, rows = stage.shape[1:3]

    def repeat(first, last, body):
        def step(i, carry):
            body(i)
            return carry

        lax.fori_loop(first, last, step, 0)

    def columns(h):
        return slice(h * width, (h + 1) * width)

    own = (chip * 2 + core) * slots
    for h in range(2):
        held[h, pl.ds(own, slots)] = mine_ref[:, :, columns(h)].astype(jnp.bfloat16)
    barrier = pltpu.get_barrier_semaphore()
    for place in ({"ctx": 1 - core}, {"dp": beside}, {"dp": across}, {"tensor": end_peer}):
        pl.semaphore_signal(barrier, inc=1, device_id=place, device_id_type=MESH_ID)

    @pl.when(inner)
    def _():
        pl.semaphore_signal(barrier, inc=1, device_id={"tensor": mid_peer}, device_id_type=MESH_ID)
        pl.semaphore_wait(barrier, 5)

    @pl.when(jnp.logical_not(inner))
    def _():
        pl.semaphore_wait(barrier, 4)

    def remote(source, target, send, recv, place):
        return pltpu.make_async_remote_copy(
            src_ref=source,
            dst_ref=target,
            send_sem=send,
            recv_sem=recv,
            device_id=place,
            device_id_type=MESH_ID,
        )

    def copy(h, place, q, send, recv, target):
        piece = held.at[h, pl.ds((place * 2 + core) * slots + q * size, size)]
        return remote(piece, piece, send, recv, target)

    def to_beside(h, q):
        return copy(h, chip, q, send_x.at[h, q], recv_x.at[h, q], {"dp": beside})

    def to_across(h, q):
        return copy(h, chip, q, send_y.at[h, q], recv_y.at[h, q], {"dp": across})

    def passed_on(h, q, source, target):
        return copy(h, source, q, send_z.at[h, q], recv_z.at[h, q], {"dp": target})

    def to_core(h, k, q):
        return copy(h, places[k], q, send_core.at[h, k, q], recv_core.at[h, k, q], {"ctx": 1 - core})

    def start(h):
        def both(i):
            to_beside(h, i).start()
            to_across(h, lax.rem(i + split, chunks)).start()

        repeat(0, chunks, both)
        repeat(0, chunks, lambda q: to_core(h, 0, q).start())

    def look(h, place, which):
        begin = (place * 2 + which) * slots
        lines = slots * unit_rows
        column = lax.broadcasted_iota(jnp.int32, (tokens, lines), 1) + begin * unit_rows
        hit = jnp.where(column == rows_ref[...], 1.0, 0.0).astype(jnp.bfloat16)
        block = held[h, pl.ds(begin, slots)].reshape(lines, width)
        total[h] += jnp.dot(hit, block, preferred_element_type=jnp.float32)

    def relay(h, i):
        to_beside(h, i).wait_recv()

        @pl.when(i < split)
        def _():
            passed_on(h, i, beside, across).start()

        to_core(h, 1, i).start()
        j = lax.rem(i + split, chunks)
        to_across(h, j).wait_recv()

        @pl.when(j >= split)
        def _():
            passed_on(h, j, across, beside).start()

        to_core(h, 2, j).start()

    def rest(h):
        repeat(0, chunks, lambda q: to_core(h, 0, q).wait_recv())
        look(h, chip, 1 - core)
        look(h, beside, core)
        look(h, across, core)

        def last(q):
            passed_on(h, q, opposite, opposite).wait_recv()
            to_core(h, 3, q).start()
            to_core(h, 1, q).wait_recv()
            to_core(h, 2, q).wait_recv()

        repeat(0, chunks, last)
        look(h, beside, 1 - core)
        look(h, across, 1 - core)
        look(h, opposite, core)
        repeat(0, chunks, lambda q: to_core(h, 3, q).wait_recv())
        look(h, opposite, 1 - core)

    def span(i):
        return pl.ds(pl.multiple_of(i * rows, rows), rows)

    def to_inner(h, i):
        return remote(
            stage.at[h, i], from_end.at[h, i], send_sem.at[h, i], end_sem.at[h, i], {"tensor": end_peer}
        )

    def to_middle(h, i):
        return remote(
            stage.at[h, i], from_mid.at[h, i], send_sem.at[h, i], mid_sem.at[h, i], {"tensor": mid_peer}
        )

    def to_end(h, i):
        piece = embedded_ref.at[span(i), columns(h)]
        return remote(piece, piece, back_sem.at[h, i], back_recv.at[h, i], {"tensor": end_peer})

    def push(h):
        @pl.when(jnp.logical_not(inner))
        def _():
            def one(i):
                stage[h, i] = total[h, span(i)].astype(jnp.bfloat16)
                to_inner(h, i).start()

            repeat(0, count, one)

    def exchange(h, i):
        @pl.when(inner & (i < count))
        def _():
            to_inner(h, i).wait_recv()
            stage[h, i] = (total[h, span(i)] + from_end[h, i].astype(jnp.float32)).astype(jnp.bfloat16)
            to_middle(h, i).start()

        @pl.when(inner & (i >= line_lag))
        def _():
            j = i - line_lag
            to_middle(h, j).wait_recv()
            both = stage[h, j].astype(jnp.float32) + from_mid[h, j].astype(jnp.float32)
            embedded_ref[span(j), columns(h)] = both.astype(jnp.bfloat16)
            to_end(h, j).start()

    total[...] = jnp.zeros_like(total)
    start(0)
    look(0, chip, core)
    repeat(0, chunks, lambda i: relay(0, i))
    start(1)
    rest(0)
    push(0)
    look(1, chip, core)

    def between(i):
        exchange(0, i)

        @pl.when(i < chunks)
        def _():
            relay(1, i)

    repeat(0, count + line_lag, between)
    rest(1)
    push(1)

    def place_unit(u):
        for h in range(2):
            units_ref[u, :, columns(h)] = held[h, slots_ref[u]]

    @pl.when(jnp.logical_not(inner))
    def _():
        repeat(0, units_ref.shape[0], place_unit)

    repeat(0, count + line_lag, lambda i: exchange(1, i))

    @pl.when(inner)
    def _():
        repeat(0, units_ref.shape[0], place_unit)

    def finish(q):
        for h in range(2):
            to_beside(h, q).wait_send()
            to_across(h, q).wait_send()
            for k in range(4):
                to_core(h, k, q).wait_send()
            passed_on(h, q, opposite, opposite).wait_send()

    repeat(0, chunks, finish)

    @pl.when(inner)
    def _():
        def drain(i):
            for h in range(2):
                to_middle(h, i).wait_send()
                to_end(h, i).wait_send()

        repeat(0, count, drain)

    @pl.when(jnp.logical_not(inner))
    def _():
        def drain(i):
            for h in range(2):
                to_end(h, i).wait_recv()
                to_inner(h, i).wait_send()

        repeat(0, count, drain)


def embed(unit_slots, mine, slot_rows, collective_id):
    slots, unit_rows, width = mine.shape
    tokens = slot_rows.shape[0]
    chunks = max(k for k in range(1, 8) if slots % k == 0)
    rows = 128
    half = width // 2
    sems = pltpu.SemaphoreType.DMA((2, chunks))
    line = pltpu.VMEM((2, tokens // rows, rows, half), jnp.bfloat16)
    return pl.pallas_call(
        functools.partial(embed_kernel, chunks),
        out_shape=[
            jax.ShapeDtypeStruct((unit_slots.shape[0], unit_rows, width), jnp.bfloat16),
            jax.ShapeDtypeStruct((tokens, width), jnp.bfloat16),
        ],
        in_specs=[pl.BlockSpec(memory_space=pltpu.SMEM), whole_vmem, whole_vmem],
        out_specs=[whole_vmem] * 2,
        scratch_shapes=[
            pltpu.VMEM((2, 8 * slots, unit_rows, half), jnp.bfloat16),
            pltpu.VMEM((2, tokens, half), jnp.float32),
            line,
            line,
            line,
        ]
        + [sems] * 6
        + [pltpu.SemaphoreType.DMA((2, 4, chunks))] * 2
        + [pltpu.SemaphoreType.DMA((2, tokens // rows))] * 5,
        compiler_params=pltpu.CompilerParams(
            collective_id=collective_id, has_side_effects=True, vmem_limit_bytes=60 << 20
        ),
    )(unit_slots, mine, slot_rows)


def pull_units_kernel(parts, slots_ref, *refs):
    sources, out_ref, sem = refs[:parts], refs[parts], refs[parts + 1]
    width = out_ref.shape[-1] // parts

    def push(u, carry):
        for part in range(parts):
            pltpu.make_async_copy(
                sources[part].at[slots_ref[u]],
                out_ref.at[u, :, part * width : (part + 1) * width],
                sem,
            ).start()
        return carry

    lax.fori_loop(0, out_ref.shape[0], push, 0)
    pltpu.make_async_copy(out_ref, out_ref, sem).wait()


def pull_units(sources, slots):
    count = slots.shape[0]
    rows, width = sources[0].shape[1:]
    return pl.pallas_call(
        functools.partial(pull_units_kernel, len(sources)),
        out_shape=jax.ShapeDtypeStruct((count, rows, width * len(sources)), sources[0].dtype),
        in_specs=[pl.BlockSpec(memory_space=pltpu.SMEM)] + [whole_any] * len(sources),
        out_specs=whole_vmem,
        scratch_shapes=[pltpu.SemaphoreType.DMA],
        compiler_params=pltpu.CompilerParams(vmem_limit_bytes=40 << 20),
    )(slots, *sources)


def attention_kernel(heads, size, bias_ref, own_ref, before_ref, out_ref, logsum_ref, scores, peak, total):
    tokens = own_ref.shape[1]
    blocks = tokens // BLOCK
    hidden = heads * size
    later = lax.axis_index("ctx") > 0

    for head in range(heads):
        query = own_ref[head * size : (head + 1) * size, :].astype(jnp.float32).T * size**-0.5
        query = query.astype(jnp.bfloat16)
        own_keys = own_ref[hidden + head * size : hidden + (head + 1) * size, :]
        old_keys = before_ref[head * size : (head + 1) * size, :]
        own_values = own_ref[2 * hidden + head * size : 2 * hidden + (head + 1) * size, :]
        own_values = own_values.astype(jnp.float32).T.astype(jnp.bfloat16)
        old_values = before_ref[hidden + head * size : hidden + (head + 1) * size, :]
        old_values = old_values.astype(jnp.float32).T.astype(jnp.bfloat16)
        for block in range(blocks):
            rows = query[block * BLOCK : (block + 1) * BLOCK]
            width = (block + 1) * BLOCK
            mine = jnp.dot(rows, own_keys[:, :width], preferred_element_type=jnp.float32)
            top = None
            parts = []
            for k in range(block + 1):
                part = mine[:, k * BLOCK : (k + 1) * BLOCK] + bias_ref[head, block - k]
                parts.append(part)
                high = jnp.max(part, 1, keepdims=True)
                top = high if top is None else jnp.maximum(top, high)
            peak[...] = top

            @pl.when(later)
            def _():
                old = jnp.dot(rows, old_keys, preferred_element_type=jnp.float32)
                top_old = None
                for k in range(blocks):
                    part = old[:, k * BLOCK : (k + 1) * BLOCK] + bias_ref[head, block + blocks - k]
                    scores[:, k * BLOCK : (k + 1) * BLOCK] = part
                    high = jnp.max(part, 1, keepdims=True)
                    top_old = high if top_old is None else jnp.maximum(top_old, high)
                peak[...] = jnp.maximum(peak[...], top_old)

            top = peak[...]
            parts = [jnp.exp(part - top) for part in parts]
            own_sum = None
            for part in parts:
                part_sum = jnp.sum(part, 1, keepdims=True)
                own_sum = part_sum if own_sum is None else own_sum + part_sum
            total[...] = own_sum

            @pl.when(later)
            def _():
                old_exp = jnp.exp(scores[...] - top)
                scores[...] = old_exp
                total[...] += jnp.sum(old_exp, 1, keepdims=True)

            full = total[...]
            inverse = 1.0 / full
            low = jnp.concatenate([(part * inverse).astype(jnp.bfloat16) for part in parts], 1)
            result = jnp.dot(low, own_values[:width], preferred_element_type=jnp.float32)
            peak[...] = top + jnp.log(full)
            logsum_ref[head, block * BLOCK : (block + 1) * BLOCK, :] = peak[...]
            place = (slice(head * size, (head + 1) * size), slice(block * BLOCK, (block + 1) * BLOCK))

            @pl.when(later)
            def _():
                low_old = (scores[...] * inverse).astype(jnp.bfloat16)
                both = result + jnp.dot(low_old, old_values, preferred_element_type=jnp.float32)
                out_ref[place] = both.T.astype(jnp.bfloat16)

            @pl.when(jnp.logical_not(later))
            def _():
                out_ref[place] = result.T.astype(jnp.bfloat16)


def attention(biases, own, before, heads, size):
    tokens = own.shape[1]
    return pl.pallas_call(
        functools.partial(attention_kernel, heads, size),
        out_shape=[
            jax.ShapeDtypeStruct((heads * size, tokens), jnp.bfloat16),
            jax.ShapeDtypeStruct((heads, tokens, 1), jnp.float32),
        ],
        in_specs=[pl.BlockSpec(memory_space=pltpu.SMEM), whole_vmem, whole_vmem],
        out_specs=[whole_vmem, whole_vmem],
        scratch_shapes=[
            pltpu.VMEM((BLOCK, tokens), jnp.float32),
            pltpu.VMEM((BLOCK, 1), jnp.float32),
            pltpu.VMEM((BLOCK, 1), jnp.float32),
        ],
        compiler_params=pltpu.CompilerParams(vmem_limit_bytes=40 << 20),
    )(biases, own, before)


def attention_back_kernel(
    heads, size, bias_ref, own_ref, before_ref, logsum_ref, grad_ref, project_ref,
    query_out, own_out, before_out, bias_out, probs, slopes, inner, query_sum, own_sum, before_sum,
):
    tokens = own_ref.shape[1]
    blocks = tokens // BLOCK
    hidden = heads * size
    later = lax.axis_index("ctx") > 0
    bias_out[...] = jnp.zeros_like(bias_out)

    def flipped(rows):
        return rows.astype(jnp.float32).T.astype(jnp.bfloat16)

    for head in range(heads):
        span = slice(head * size, (head + 1) * size)
        value_span = slice(hidden + head * size, hidden + (head + 1) * size)
        query_rows = own_ref[span, :]
        query = flipped(query_rows) * jnp.bfloat16(size**-0.5)
        own_keys = own_ref[hidden + head * size : hidden + (head + 1) * size, :]
        own_values = own_ref[2 * hidden + head * size : 2 * hidden + (head + 1) * size, :]
        old_keys = before_ref[span, :]
        old_values = before_ref[value_span, :]
        own_keys_flip = flipped(own_keys)
        grad = lax.dot_general(
            grad_ref[...], project_ref[span, :], (((1,), (1,)), ((), ())), preferred_element_type=jnp.float32
        )
        grad_rows = grad.T.astype(jnp.bfloat16)
        grad = grad.astype(jnp.bfloat16)
        own_sum[...] = jnp.zeros_like(own_sum)

        @pl.when(later)
        def _():
            before_sum[...] = jnp.zeros_like(before_sum)

        for block in range(blocks):
            at = slice(block * BLOCK, (block + 1) * BLOCK)
            width = (block + 1) * BLOCK
            rows, up = query[at], grad[at]
            lse = logsum_ref[head, at, :]
            score = jnp.dot(rows, own_keys[:, :width], preferred_element_type=jnp.float32)
            prob = jnp.concatenate(
                [
                    jnp.exp(score[:, k * BLOCK : (k + 1) * BLOCK] + (bias_ref[head, block - k] - lse))
                    for k in range(block + 1)
                ],
                1,
            )
            slope = jnp.dot(up, own_values[:, :width], preferred_element_type=jnp.float32)
            inner[...] = jnp.sum(prob * slope, 1, keepdims=True)

            @pl.when(later)
            def _():
                score = jnp.dot(rows, old_keys, preferred_element_type=jnp.float32)
                old_slope = jnp.dot(up, old_values, preferred_element_type=jnp.float32)
                old_prob = jnp.concatenate(
                    [
                        jnp.exp(
                            score[:, k * BLOCK : (k + 1) * BLOCK]
                            + (bias_ref[head, block + blocks - k] - lse)
                        )
                        for k in range(blocks)
                    ],
                    1,
                )
                probs[...] = old_prob
                slopes[...] = old_slope
                inner[...] += jnp.sum(old_prob * old_slope, 1, keepdims=True)

            row_inner = inner[...]
            low_grad = (prob * (slope - row_inner)).astype(jnp.bfloat16)
            query_sum[...] = jnp.dot(
                low_grad, own_keys_flip[:width], preferred_element_type=jnp.float32
            )
            own_sum[:size, :width] += jnp.dot(
                query_rows[:, at], low_grad, preferred_element_type=jnp.float32
            )
            own_sum[size:, :width] += jnp.dot(
                grad_rows[:, at], prob.astype(jnp.bfloat16), preferred_element_type=jnp.float32
            )
            for k in range(block + 1):
                line = head * 2 * blocks + block - k
                bias_out[line : line + 1, :] += jnp.sum(
                    low_grad[:, k * BLOCK : (k + 1) * BLOCK].astype(jnp.float32), 0, keepdims=True
                )

            @pl.when(later)
            def _():
                old_prob = probs[...]
                low_old = (old_prob * (slopes[...] - row_inner)).astype(jnp.bfloat16)
                query_sum[...] += jnp.dot(
                    low_old, flipped(old_keys), preferred_element_type=jnp.float32
                )
                before_sum[:size, :] += jnp.dot(
                    query_rows[:, at], low_old, preferred_element_type=jnp.float32
                )
                before_sum[size:, :] += jnp.dot(
                    grad_rows[:, at], old_prob.astype(jnp.bfloat16), preferred_element_type=jnp.float32
                )
                for k in range(blocks):
                    line = head * 2 * blocks + block + blocks - k
                    bias_out[line : line + 1, :] += jnp.sum(
                        low_old[:, k * BLOCK : (k + 1) * BLOCK].astype(jnp.float32), 0, keepdims=True
                    )

            query_out[span, at] = (query_sum[...].T * size**-0.5).astype(jnp.bfloat16)

        own_out[span, :] = own_sum[:size, :] * size**-0.5
        own_out[value_span, :] = own_sum[size:, :]

        @pl.when(later)
        def _():
            before_out[span, :] = (before_sum[:size, :] * size**-0.5).astype(jnp.bfloat16)
            before_out[value_span, :] = before_sum[size:, :].astype(jnp.bfloat16)

    @pl.when(jnp.logical_not(later))
    def _():
        before_out[...] = jnp.zeros_like(before_out)


def attention_back(biases, own, before, logsum, grad, project, heads, size):
    tokens = own.shape[1]
    hidden = heads * size
    return pl.pallas_call(
        functools.partial(attention_back_kernel, heads, size),
        out_shape=[
            jax.ShapeDtypeStruct((hidden, tokens), jnp.bfloat16),
            jax.ShapeDtypeStruct((2 * hidden, tokens), jnp.float32),
            jax.ShapeDtypeStruct((2 * hidden, tokens), jnp.bfloat16),
            jax.ShapeDtypeStruct((heads * 2 * (tokens // BLOCK), BLOCK), jnp.float32),
        ],
        in_specs=[pl.BlockSpec(memory_space=pltpu.SMEM)] + [whole_vmem] * 5,
        out_specs=[whole_vmem] * 4,
        scratch_shapes=[
            pltpu.VMEM((BLOCK, tokens), jnp.float32),
            pltpu.VMEM((BLOCK, tokens), jnp.float32),
            pltpu.VMEM((BLOCK, 1), jnp.float32),
            pltpu.VMEM((BLOCK, size), jnp.float32),
            pltpu.VMEM((2 * size, tokens), jnp.float32),
            pltpu.VMEM((2 * size, tokens), jnp.float32),
        ],
        compiler_params=pltpu.CompilerParams(vmem_limit_bytes=48 << 20),
    )(biases, own, before, logsum, grad, project)


def vocab_tile(vocab):
    return max(k for k in range(16, 1601, 16) if vocab % k == 0)


def head_line_kernel(
    tile, part_ref, stream_ref, gain_ref, table_ref, wanted_ref, weight_ref,
    low_ref, grad_low_ref, grad_ref, gain_grad, logsum_ref, picked_ref, slopes_ref,
    table, stage, from_end, from_mid, own, turned, stats, landed, slope_tiles, total,
    load_sem, send_sem, end_sem, mid_sem, back_sem, back_recv, stat_send, stat_recv, store_sem,
):
    rank = lax.axis_index("tensor")
    inner = (rank == 1) | (rank == 2)
    end_peer = jnp.where(rank < 2, 1 - rank, 5 - rank)
    mid_peer = 3 - rank
    count, rows = stage.shape[:2]
    columns = turned.shape[1]
    pieces = table.shape[0] // tile
    group = columns // rows
    tiles = count // group
    units = tiles * pieces
    vocab = table.shape[0]
    load = pltpu.make_async_copy(table_ref.at[pl.ds(0, vocab)], table, load_sem)
    load.start()
    barrier = pltpu.get_barrier_semaphore()
    for step in (1, 2, 3):
        other = lax.rem(rank + step, 4)
        pl.semaphore_signal(barrier, inc=1, device_id={"tensor": other}, device_id_type=MESH_ID)
    pl.semaphore_wait(barrier, 3)

    def span(i):
        return pl.ds(pl.multiple_of(i * rows, rows), rows)

    def over(t):
        return pl.ds(pl.multiple_of(t * columns, columns), columns)

    def line_copy(source, target, send, recv, peer):
        return pltpu.make_async_remote_copy(
            src_ref=source,
            dst_ref=target,
            send_sem=send,
            recv_sem=recv,
            device_id={"tensor": peer},
            device_id_type=MESH_ID,
        )

    def to_inner(i):
        return line_copy(stage.at[i], from_end.at[i], send_sem.at[i], end_sem.at[i], end_peer)

    def to_middle(i):
        return line_copy(stage.at[i], from_mid.at[i], send_sem.at[i], mid_sem.at[i], mid_peer)

    def to_end(ref, i):
        rows_of = ref.at[span(i)]
        return line_copy(rows_of, rows_of, back_sem.at[i], back_recv.at[i], end_peer)

    def repeat(first, last, body):
        def step(i, carry):
            body(i)
            return carry

        lax.fori_loop(first, last, step, 0)

    def turn(t):
        turned[...] = low_ref[over(t)].astype(jnp.float32).T.astype(jnp.bfloat16)

    def table_rows(k):
        return table[pl.ds(pl.multiple_of(k * tile, tile), tile)]

    def sums_unit(n):
        t, k = n // pieces, lax.rem(n, pieces)

        @pl.when(k == 0)
        def _():
            turn(t)

        logits = jnp.dot(table_rows(k), turned[...], preferred_element_type=jnp.float32)
        before = stats[0:1, over(t)]
        top = jnp.maximum(before, jnp.max(logits, 0, keepdims=True))
        stats[1:2, over(t)] = stats[1:2, over(t)] * jnp.exp(before - top) + jnp.sum(
            jnp.exp(logits - top), 0, keepdims=True
        )
        stats[0:1, over(t)] = top

    stats[0:1, :] = jnp.full_like(stats[0:1, :], masked_score)
    stats[1:2, :] = jnp.zeros_like(stats[1:2, :])

    @pl.when(jnp.logical_not(inner))
    def _():
        def push(i):
            stage[i] = part_ref[span(i)].astype(jnp.bfloat16)
            to_inner(i).start()

        repeat(0, count, push)
        load.wait()

        def forward(t):
            repeat(0, group, lambda c: to_end(low_ref, t * group + c).wait_recv())
            repeat(0, pieces, lambda k: sums_unit(t * pieces + k))

        repeat(0, tiles, forward)
        repeat(0, count, lambda i: to_inner(i).wait_send())

    @pl.when(inner)
    def _():
        gain_grad[...] = jnp.zeros_like(gain_grad)
        load.wait()
        ahead = group + line_lag

        def step(i):
            @pl.when(i < count)
            def _():
                to_inner(i).wait_recv()
                mine = part_ref[span(i)] + from_end[i].astype(jnp.float32)
                stage[i] = mine.astype(jnp.bfloat16)
                to_middle(i).start()

            @pl.when(i >= line_lag)
            def _():
                j = i - line_lag
                to_middle(j).wait_recv()
                stream_two = stream_ref[span(j)] + (
                    stage[j].astype(jnp.float32) + from_mid[j].astype(jnp.float32)
                )
                grad_ref[span(j)] = stream_two
                low_ref[span(j)] = (stream_two * inverse_rms(stream_two) * gain_ref[...]).astype(
                    jnp.bfloat16
                )
                to_end(low_ref, j).start()

            @pl.when(i >= ahead)
            def _():
                sums_unit(i - ahead)

        repeat(0, count + line_lag, step)
        repeat(count + line_lag - ahead, units, sums_unit)

        def drain(i):
            to_middle(i).wait_send()
            to_end(low_ref, i).wait_send()

        repeat(0, count, drain)

    copies = [
        line_copy(
            stats, landed.at[step - 1], stat_send.at[step - 1], stat_recv.at[step - 1], lax.rem(rank + step, 4)
        )
        for step in (1, 2, 3)
    ]
    for copy in copies:
        copy.start()
    for copy in copies:
        copy.wait()
    tops, sums = [], []
    for source in range(4):
        piece = stats[...]
        for step in (1, 2, 3):
            piece = jnp.where(lax.rem(source + step, 4) == rank, landed[step - 1], piece)
        tops.append(piece[0:1])
        sums.append(piece[1:2])
    top = jnp.maximum(jnp.maximum(tops[0], tops[1]), jnp.maximum(tops[2], tops[3]))
    whole = sums[0] * jnp.exp(tops[0] - top)
    for source in (1, 2, 3):
        whole = whole + sums[source] * jnp.exp(tops[source] - top)
    logsum_ref[...] = top + jnp.log(whole)
    picked_ref[...] = jnp.zeros_like(picked_ref)

    def store(t):
        return pltpu.make_async_copy(
            slope_tiles.at[lax.rem(t, 2)], slopes_ref.at[:, over(t)], store_sem.at[lax.rem(t, 2)]
        )

    def back_unit(n):
        t, k = n // pieces, lax.rem(n, pieces)

        @pl.when(k == 0)
        def _():
            turn(t)
            total[...] = jnp.zeros_like(total)

            @pl.when(t >= 2)
            def _():
                store(t - 2).wait()

        lines = table_rows(k)
        logits = jnp.dot(lines, turned[...], preferred_element_type=jnp.float32)
        row = lax.broadcasted_iota(jnp.int32, logits.shape, 0)
        base = k * tile
        hits = jnp.where(row == wanted_ref[0:1, over(t)] - base, weight_ref[0:1, over(t)], 0.0)
        hits = hits + jnp.where(
            row == wanted_ref[1:2, over(t)] - base, weight_ref[1:2, over(t)], 0.0
        )
        picked_ref[:, over(t)] += jnp.sum(hits * logits, 0, keepdims=True)
        softmax = jnp.exp(logits - logsum_ref[:, over(t)])
        slope = (
            (weight_ref[2:3, over(t)] * softmax - hits) * weight_ref[3:4, over(t)]
        ).astype(jnp.bfloat16)
        slope_tiles[lax.rem(t, 2), pl.ds(pl.multiple_of(base, tile), tile)] = slope
        total[...] += lax.dot_general(
            slope, lines, (((0,), (0,)), ((), ())), preferred_element_type=jnp.float32
        )

        @pl.when(k == pieces - 1)
        def _():
            store(t).start()

    @pl.when(jnp.logical_not(inner))
    def _():
        def unit(n):
            back_unit(n)

            @pl.when(lax.rem(n, pieces) == pieces - 1)
            def _():
                first = (n // pieces) * group

                def push(c):
                    stage[first + c] = total[span(c)].astype(jnp.bfloat16)
                    to_inner(first + c).start()

                repeat(0, group, push)

        repeat(0, units, unit)

        def finish(i):
            to_end(grad_low_ref, i).wait_recv()
            to_inner(i).wait_send()

        repeat(0, count, finish)

    @pl.when(inner)
    def _():
        def settle(j):
            to_middle(j).wait_recv()
            upstream = stage[j].astype(jnp.float32) + from_mid[j].astype(jnp.float32)
            grad_two, gain_part = norm_back_rows(grad_ref[span(j)], gain_ref[...], upstream)
            grad_ref[span(j)] = grad_two
            gain_grad[...] += gain_part
            grad_low_ref[span(j)] = grad_two.astype(jnp.bfloat16)
            to_end(grad_low_ref, j).start()

        def exchange(i):
            to_inner(i).wait_recv()
            stage[i] = (own[span(i)] + from_end[i].astype(jnp.float32)).astype(jnp.bfloat16)
            to_middle(i).start()

            @pl.when(i >= line_lag)
            def _():
                settle(i - line_lag)

        def unit(n):
            back_unit(n)
            t, k = n // pieces, lax.rem(n, pieces)

            @pl.when(k == pieces - 1)
            def _():
                own[over(t)] = total[...]

            @pl.when((t >= 1) & (k >= pieces - group))
            def _():
                exchange((t - 1) * group + k - (pieces - group))

        repeat(0, units, unit)
        repeat(count - group, count, exchange)
        repeat(count - line_lag, count, settle)

        def drain(i):
            to_middle(i).wait_send()
            to_end(grad_low_ref, i).wait_send()

        repeat(0, count, drain)

    store(tiles - 2).wait()
    store(tiles - 1).wait()


def head_line(part, stream, gain, weights, wanted, weight_rows, vocab, collective_id):
    tokens, width = part.shape
    rows, columns = 64, 256
    count = tokens // rows
    chunks = pltpu.VMEM((count, rows, width), jnp.bfloat16)
    rows_low = jax.ShapeDtypeStruct((tokens, width), jnp.bfloat16)
    along = jax.ShapeDtypeStruct((1, tokens), jnp.float32)
    line_sems = pltpu.SemaphoreType.DMA((count,))
    return pl.pallas_call(
        functools.partial(head_line_kernel, vocab_tile(vocab)),
        out_shape=[
            rows_low,
            rows_low,
            jax.ShapeDtypeStruct((tokens, width), jnp.float32),
            jax.ShapeDtypeStruct((1, width), jnp.float32),
            along,
            along,
            jax.ShapeDtypeStruct((vocab, tokens), jnp.bfloat16),
        ],
        in_specs=[whole_vmem] * 3 + [whole_any] + [whole_vmem] * 2,
        out_specs=[whole_vmem] * 6 + [whole_any],
        scratch_shapes=[
            pltpu.VMEM((vocab, width), jnp.bfloat16),
            chunks,
            chunks,
            chunks,
            pltpu.VMEM((tokens, width), jnp.float32),
            pltpu.VMEM((width, columns), jnp.bfloat16),
            pltpu.VMEM((2, tokens), jnp.float32),
            pltpu.VMEM((3, 2, tokens), jnp.float32),
            pltpu.VMEM((2, vocab, columns), jnp.bfloat16),
            pltpu.VMEM((columns, width), jnp.float32),
            pltpu.SemaphoreType.DMA,
        ]
        + [line_sems] * 5
        + [pltpu.SemaphoreType.DMA((3,))] * 2
        + [pltpu.SemaphoreType.DMA((2,))],
        compiler_params=pltpu.CompilerParams(
            collective_id=collective_id, has_side_effects=True, vmem_limit_bytes=62 << 20
        ),
    )(part, stream, gain, weights, wanted, weight_rows)


def weight_grads_kernel(
    tile_units, tiles, place_ref, slope_ref, rows_ref, ids_ref, zero_ref, joint_ref, normed_ref,
    attended_ref, grad_ref, *refs
):
    states, (out_ref, *updated), (made, sem) = refs[:8], refs[8:15], refs[15:]
    step = pl.program_id(0)
    for k, rate in enumerate((rate_inner, rate_outer)):
        fresh = adam_update(*(state[...] for state in states[4 * k : 4 * k + 4]), rate, decay_rate)
        for n in range(3):
            updated[3 * k + n][...] = fresh[n]
    unit_rows = out_ref.shape[1]
    buffer = lax.rem(step, 2)
    last_units = joint_ref.shape[0] // unit_rows + attended_ref.shape[0] // unit_rows

    def settle(which, count):
        pltpu.make_async_copy(
            made.at[which, pl.ds(0, count)], made.at[which, pl.ds(0, count)], sem.at[which]
        ).wait()

    def send(first, count):
        def push(u, carry):
            pltpu.make_async_copy(
                made.at[buffer, u], out_ref.at[place_ref[first + u]], sem.at[buffer]
            ).start()
            return carry

        lax.fori_loop(0, count, push, 0)

    @pl.when(step >= 2)
    def _():
        settle(buffer, tile_units)

    @pl.when(step < tiles)
    def _():
        row = lax.broadcasted_iota(jnp.int32, slope_ref.shape, 0)
        seen = jnp.where(row == ids_ref[...] - step * slope_ref.shape[0], 1.0, 0.0).astype(jnp.bfloat16)
        made[buffer] = (
            jnp.dot(slope_ref[...], rows_ref[...], preferred_element_type=jnp.float32)
            + jnp.dot(seen, zero_ref[...], preferred_element_type=jnp.float32)
        ).astype(jnp.bfloat16).reshape(tile_units, unit_rows, -1)
        send(step * tile_units, tile_units)

    @pl.when(step == tiles)
    def _():
        joint_units = joint_ref.shape[0] // unit_rows
        made[buffer, pl.ds(0, joint_units)] = jnp.dot(
            joint_ref[...], normed_ref[...], preferred_element_type=jnp.float32
        ).astype(jnp.bfloat16).reshape(joint_units, unit_rows, -1)
        made[buffer, pl.ds(joint_units, last_units - joint_units)] = jnp.dot(
            attended_ref[...], grad_ref[...], preferred_element_type=jnp.float32
        ).astype(jnp.bfloat16).reshape(last_units - joint_units, unit_rows, -1)
        send(tiles * tile_units, last_units)
        settle(1 - buffer, tile_units)
        settle(buffer, last_units)


def weight_grads(
    place, slots, unit_rows, slope, rows, ids, zero, joint, normed, attended, grad, states
):
    vocab, tokens = slope.shape
    width = rows.shape[1]
    tile = vocab_tile(vocab)
    tiles = vocab // tile
    fixed = lambda k: (0, 0)
    whole = lambda x: pl.BlockSpec(x.shape, fixed)
    piece = pl.BlockSpec((states[0].shape[0] // (tiles + 1), states[0].shape[1]), lambda k: (k, 0))
    return pl.pallas_call(
        functools.partial(weight_grads_kernel, tile // unit_rows, tiles),
        grid=(tiles + 1,),
        out_shape=[jax.ShapeDtypeStruct((slots, unit_rows, width), jnp.bfloat16)]
        + [jax.ShapeDtypeStruct(states[0].shape, jnp.float32)] * 6,
        in_specs=[
            pl.BlockSpec(memory_space=pltpu.SMEM),
            pl.BlockSpec((tile, tokens), lambda k: (jnp.minimum(k, tiles - 1), 0)),
        ]
        + [whole(x) for x in (rows, ids, zero, joint, normed, attended, grad)]
        + [piece] * 8,
        out_specs=[whole_any] + [piece] * 6,
        scratch_shapes=[
            pltpu.VMEM((2, tile // unit_rows, unit_rows, width), jnp.bfloat16),
            pltpu.SemaphoreType.DMA((2,)),
        ],
        compiler_params=pltpu.CompilerParams(vmem_limit_bytes=60 << 20),
    )(place, slope, rows, ids, zero, joint, normed, attended, grad, *states)


def adam_update(weight, moment_one, moment_two, gradient, step_rate, decay_factor):
    moment_new = beta_first * moment_one + (1.0 - beta_first) * gradient
    square_new = beta_second * moment_two + (1.0 - beta_second) * gradient * gradient
    moment_hat = moment_new / (1.0 - beta_first**STEP)
    square_hat = square_new / (1.0 - beta_second**STEP)
    weight_new = weight - step_rate * (
        moment_hat / (jnp.sqrt(square_hat) + adam_epsilon) + decay_factor * weight
    )
    return (weight_new, moment_new, square_new)


def norm_forward(values, gain_row):
    return values * inverse_rms(values) * gain_row


def slot_tables(owner_ids, owners, most_units):
    unit_count = owner_ids.shape[0]
    unit_index = jnp.arange(unit_count, dtype=jnp.int32)
    earlier = (owner_ids[None, :] == owner_ids[:, None]) & (
        unit_index[None, :] < unit_index[:, None]
    )
    unit_rank = jnp.sum(earlier.astype(jnp.int32), 1)
    placed = (owner_ids[None, None, :] == jnp.arange(owners, dtype=jnp.int32)[:, None, None]) & (
        unit_rank[None, None, :] == jnp.arange(most_units, dtype=jnp.int32)[None, :, None]
    )
    slot_filled = jnp.any(placed, 2)
    slot_unit = jnp.sum(jnp.where(placed, unit_index[None, None, :], 0), 2)
    return (unit_rank, slot_unit, slot_filled)


def unit_rates(unit_ids, table_units, query_units, value_units):
    return jnp.where(
        unit_ids < table_units,
        rate_table,
        jnp.where(
            unit_ids < query_units,
            rate_query,
            jnp.where(unit_ids < value_units, rate_values, rate_project),
        ),
    )


def pair_slots(route_pairs, priorities, experts, capacity):
    tokens_here = priorities.shape[0]
    pair_expert = route_pairs.T.reshape(-1)
    pair_key = (
        jnp.arange(2, dtype=jnp.int32)[:, None] * tokens_here + priorities[None, :]
    ).reshape(-1)
    before = (pair_expert[None, :] == pair_expert[:, None]) & (
        pair_key[None, :] < pair_key[:, None]
    )
    pair_rank = jnp.sum(before.astype(jnp.int32), 1)
    pair_kept = pair_rank < capacity
    pair_dest = pair_expert * capacity + jnp.minimum(pair_rank, capacity - 1)
    return (pair_kept, pair_dest)


def gelu_tanh(values):
    return jax.nn.gelu(values, approximate=True)


def gelu_slope(values):
    root = math.sqrt(2.0 / math.pi)
    bent = jnp.tanh(root * (values + 0.044715 * values * values * values))
    return 0.5 * (1.0 + bent) + 0.5 * values * (1.0 - bent * bent) * root * (
        1.0 + 3.0 * 0.044715 * values * values
    )


def plane_peer(step):
    chip, core = lax.axis_index("dp"), lax.axis_index("ctx")
    row = lax.rem(chip // 2 + step // 4, 2)
    column = lax.rem(lax.rem(chip, 2) + lax.rem(step // 2, 2), 2)
    place = {"dp": row * 2 + column, "ctx": lax.rem(core + lax.rem(step, 2), 2)}
    return place, place["dp"] * 2 + place["ctx"]


def greet_plane():
    barrier = pltpu.get_barrier_semaphore()
    for step in range(1, 8):
        place, _ = plane_peer(step)
        pl.semaphore_signal(barrier, inc=1, device_id=place, device_id_type=MESH_ID)
    pl.semaphore_wait(barrier, 7)


def plane_copy(source, target, send_sem, recv_sem, step):
    place, _ = plane_peer(step)
    return pltpu.make_async_remote_copy(
        src_ref=source.at[step],
        dst_ref=target.at[step],
        send_sem=send_sem.at[step],
        recv_sem=recv_sem.at[step],
        device_id=place,
        device_id_type=MESH_ID,
    )


def slot_hits(dest_rows, expert, capacity, tokens):
    slot = lax.broadcasted_iota(jnp.int32, (capacity, tokens), 0) + expert * capacity
    return (slot == dest_rows[0:1, :]) | (slot == dest_rows[1:2, :])


def token_hits(dest_columns, expert, capacity, tokens):
    slot = lax.broadcasted_iota(jnp.int32, (tokens, capacity), 1) + expert * capacity
    hit = (slot == dest_columns[:, 0:1]) | (slot == dest_columns[:, 1:2])
    return jnp.where(hit, 1.0, 0.0).astype(jnp.bfloat16)


def gate_of(routes, gates, expert, axis):
    pick = (lambda a, k: a[k : k + 1, :]) if axis == 0 else (lambda a, k: a[:, k : k + 1])
    return jnp.where(pick(routes, 0) == expert, pick(gates, 0), 0.0) + jnp.where(
        pick(routes, 1) == expert, pick(gates, 1), 0.0
    )


def arrival(i):
    return jnp.where(i < 2, i, 9 - i)


def experts_kernel(
    rows_ref, dest_rows, dest_columns, gates, routes, inner_ref, outer_ref, counts_ref,
    mix_ref, arrived, returned, totals_ref,
    outgoing, results, counts, send_one, recv_one, send_two, recv_two, send_count, recv_count,
):
    capacity = arrived.shape[1]
    tokens = rows_ref.shape[0]
    greet_plane()
    counts[0] = counts_ref[...]

    def send_counts(step, carry):
        place, _ = plane_peer(step)
        pltpu.make_async_remote_copy(
            src_ref=counts_ref,
            dst_ref=counts.at[step],
            send_sem=send_count.at[step],
            recv_sem=recv_count.at[step],
            device_id=place,
            device_id_type=MESH_ID,
        ).start()
        return carry

    def dispatch(i, carry):
        step = 7 - i
        _, expert = plane_peer(step)
        hit = jnp.where(slot_hits(dest_rows, expert, capacity, tokens), 1.0, 0.0).astype(jnp.bfloat16)
        rows = jnp.dot(hit, rows_ref[...], preferred_element_type=jnp.float32).astype(jnp.bfloat16)

        @pl.when(step > 0)
        def _():
            outgoing[step] = rows
            plane_copy(outgoing, arrived, send_one, recv_one, step).start()

        @pl.when(step == 0)
        def _():
            arrived[0] = rows

        return carry

    def work(i, carry):
        step = arrival(i)

        @pl.when(step > 0)
        def _():
            plane_copy(outgoing, arrived, send_one, recv_one, step).wait_recv()

        before = jnp.dot(arrived[step], inner_ref[...], preferred_element_type=jnp.float32)
        active = gelu_tanh(before).astype(jnp.bfloat16)
        part = jnp.dot(active, outer_ref[...], preferred_element_type=jnp.float32).astype(jnp.bfloat16)

        @pl.when(step > 0)
        def _():
            results[step] = part
            plane_copy(results, returned, send_two, recv_two, step).start()

        @pl.when(step == 0)
        def _():
            returned[0] = part

        return carry

    def combine(i, carry):
        step = arrival(i)
        _, expert = plane_peer(step)
        hit = token_hits(dest_columns, expert, capacity, tokens)
        gate = gate_of(routes, gates, expert, 1)

        @pl.when(step > 0)
        def _():
            plane_copy(results, returned, send_two, recv_two, step).wait_recv()

        part = gate * jnp.dot(hit, returned[step], preferred_element_type=jnp.float32)

        @pl.when(i == 0)
        def _():
            mix_ref[...] = part

        @pl.when(i > 0)
        def _():
            mix_ref[...] += part

        return carry

    def finish(step, carry):
        plane_copy(outgoing, arrived, send_one, recv_one, step).wait_send()
        plane_copy(results, returned, send_two, recv_two, step).wait_send()
        place, _ = plane_peer(step)
        pltpu.make_async_remote_copy(
            src_ref=counts_ref,
            dst_ref=counts.at[step],
            send_sem=send_count.at[step],
            recv_sem=recv_count.at[step],
            device_id=place,
            device_id_type=MESH_ID,
        ).wait()
        return carry

    lax.fori_loop(0, 8, dispatch, 0)
    lax.fori_loop(1, 8, send_counts, 0)
    lax.fori_loop(0, 8, work, 0)
    lax.fori_loop(0, 8, combine, 0)
    lax.fori_loop(1, 8, finish, 0)
    totals_ref[...] = jnp.sum(counts[...], 0)


def experts_forward(rows, dest, gates, routes, inner, outer, counts, capacity, collective_id):
    tokens, width = rows.shape
    buffer = pltpu.VMEM((8, capacity, width), jnp.bfloat16)
    return pl.pallas_call(
        experts_kernel,
        out_shape=[
            jax.ShapeDtypeStruct((tokens, width), jnp.float32),
            jax.ShapeDtypeStruct((8, capacity, width), jnp.bfloat16),
            jax.ShapeDtypeStruct((8, capacity, width), jnp.bfloat16),
            jax.ShapeDtypeStruct(counts.shape, jnp.float32),
        ],
        in_specs=[whole_vmem] * 8,
        out_specs=[whole_vmem] * 4,
        scratch_shapes=[buffer, buffer, pltpu.VMEM((8,) + counts.shape, jnp.float32)]
        + [pltpu.SemaphoreType.DMA((8,))] * 6,
        compiler_params=pltpu.CompilerParams(
            collective_id=collective_id, has_side_effects=True, vmem_limit_bytes=60 << 20
        ),
    )(rows, dest, dest.T, gates, routes, inner, outer, counts)


def experts_back_kernel(
    rows_ref, dest_rows, dest_columns, gates, routes, returned, arrived, *refs
):
    inner_ref, outer_ref, grad_ref, gate_ref, inner_grad, outer_grad = refs[:6]
    outgoing, landed, results, landed_two, active, slopes = refs[6:12]
    send_one, recv_one, send_two, recv_two = refs[12:]
    capacity = arrived.shape[1]
    tokens = rows_ref.shape[0]
    greet_plane()
    gate_ref[...] = jnp.zeros_like(gate_ref)

    def dispatch(i, carry):
        step = 7 - i
        _, expert = plane_peer(step)
        hit = slot_hits(dest_rows, expert, capacity, tokens)
        rows = jnp.dot(
            jnp.where(hit, 1.0, 0.0).astype(jnp.bfloat16), rows_ref[...], preferred_element_type=jnp.float32
        )
        scale = jnp.sum(jnp.where(hit, gate_of(routes, gates, expert, 0), 0.0), 1, keepdims=True)
        sent = (rows * scale).astype(jnp.bfloat16)

        @pl.when(step > 0)
        def _():
            outgoing[step] = sent
            plane_copy(outgoing, landed, send_one, recv_one, step).start()

        @pl.when(step == 0)
        def _():
            landed[0] = sent

        dots = jnp.sum(rows * returned[step].astype(jnp.float32), 1, keepdims=True)
        part = jnp.sum(jnp.where(hit, dots, 0.0), 0, keepdims=True)
        for k in range(2):
            gate_ref[k : k + 1, :] += jnp.where(routes[k : k + 1, :] == expert, part, 0.0)
        return carry

    def work(i, carry):
        step = arrival(i)

        @pl.when(step > 0)
        def _():
            plane_copy(outgoing, landed, send_one, recv_one, step).wait_recv()

        grad_active = lax.dot_general(
            landed[step], outer_ref[...], (((1,), (1,)), ((), ())), preferred_element_type=jnp.float32
        )
        before = jnp.dot(arrived[step], inner_ref[...], preferred_element_type=jnp.float32)
        slope = (grad_active * gelu_slope(before)).astype(jnp.bfloat16)
        back = lax.dot_general(
            slope, inner_ref[...], (((1,), (1,)), ((), ())), preferred_element_type=jnp.float32
        ).astype(jnp.bfloat16)

        @pl.when(step > 0)
        def _():
            results[step] = back
            plane_copy(results, landed_two, send_two, recv_two, step).start()

        @pl.when(step == 0)
        def _():
            landed_two[0] = back

        slopes[step] = slope
        active[step] = gelu_tanh(before).astype(jnp.bfloat16)
        return carry

    def weigh(step, carry):
        outer_part = lax.dot_general(
            active[step], landed[step], (((0,), (0,)), ((), ())), preferred_element_type=jnp.float32
        )
        inner_part = lax.dot_general(
            arrived[step], slopes[step], (((0,), (0,)), ((), ())), preferred_element_type=jnp.float32
        )

        @pl.when(step == 0)
        def _():
            inner_grad[...] = inner_part
            outer_grad[...] = outer_part

        @pl.when(step > 0)
        def _():
            inner_grad[...] += inner_part
            outer_grad[...] += outer_part

        return carry

    def combine(i, carry):
        step = arrival(i)
        _, expert = plane_peer(step)
        hit = token_hits(dest_columns, expert, capacity, tokens)

        @pl.when(step > 0)
        def _():
            plane_copy(results, landed_two, send_two, recv_two, step).wait_recv()

        part = jnp.dot(hit, landed_two[step], preferred_element_type=jnp.float32)

        @pl.when(i == 0)
        def _():
            grad_ref[...] = part

        @pl.when(i > 0)
        def _():
            grad_ref[...] += part

        return carry

    def finish(step, carry):
        plane_copy(outgoing, landed, send_one, recv_one, step).wait_send()
        plane_copy(results, landed_two, send_two, recv_two, step).wait_send()
        return carry

    lax.fori_loop(0, 8, dispatch, 0)
    lax.fori_loop(0, 8, work, 0)
    lax.fori_loop(0, 8, weigh, 0)
    lax.fori_loop(0, 8, combine, 0)
    lax.fori_loop(1, 8, finish, 0)


def experts_backward(rows, dest, gates, routes, returned, arrived, inner, outer, collective_id):
    tokens, width = rows.shape
    capacity = arrived.shape[1]
    inside = inner.shape[1]
    buffer = pltpu.VMEM((8, capacity, width), jnp.bfloat16)
    inside_buffer = pltpu.VMEM((8, capacity, inside), jnp.bfloat16)
    return pl.pallas_call(
        experts_back_kernel,
        out_shape=[
            jax.ShapeDtypeStruct((tokens, width), jnp.float32),
            jax.ShapeDtypeStruct((2, tokens), jnp.float32),
            jax.ShapeDtypeStruct((width, inside), jnp.float32),
            jax.ShapeDtypeStruct((inside, width), jnp.float32),
        ],
        in_specs=[whole_vmem] * 9,
        out_specs=[whole_vmem] * 4,
        scratch_shapes=[buffer] * 4 + [inside_buffer] * 2 + [pltpu.SemaphoreType.DMA((8,))] * 4,
        compiler_params=pltpu.CompilerParams(
            collective_id=collective_id, has_side_effects=True, vmem_limit_bytes=60 << 20
        ),
    )(rows, dest, dest.T, gates, routes, returned, arrived, inner, outer)


def own_units_kernel(
    chunks, parts_ref, small_ref, grads_ref, small_out,
    own, other, relay, landed, small_landed,
    own_sem, other_send, other_recv, relay_send, relay_recv, landed_send, landed_recv, small_send, small_recv,
):
    chip, core = lax.axis_index("dp"), lax.axis_index("ctx")
    beside = chip + 1 - 2 * lax.rem(chip, 2)
    across = lax.rem(chip + 2, 4)
    opposite = across + 1 - 2 * lax.rem(across, 2)
    places = (opposite, beside, across, chip)
    slots = grads_ref.shape[0]
    size = slots // chunks
    split = (chunks + 1) // 2
    greet_plane()

    def span(q):
        return pl.ds(q * size, size)

    def fetch(k):
        first = (places[k] * 2 + core) * slots
        return pltpu.make_async_copy(parts_ref.at[pl.ds(first, slots)], own.at[k], own_sem.at[k])

    def pass_over(k, q):
        first = (places[k] * 2 + 1 - core) * slots + q * size
        return pltpu.make_async_remote_copy(
            src_ref=parts_ref.at[pl.ds(first, size)],
            dst_ref=other.at[k, span(q)],
            send_sem=other_send.at[k, q],
            recv_sem=other_recv.at[k, q],
            device_id={"ctx": 1 - core},
            device_id_type=MESH_ID,
        )

    def to_relay(q, place):
        return pltpu.make_async_remote_copy(
            src_ref=own.at[0, span(q)],
            dst_ref=relay.at[span(q)],
            send_sem=relay_send.at[q],
            recv_sem=relay_recv.at[q],
            device_id={"dp": place},
            device_id_type=MESH_ID,
        )

    def to_owner(k, q):
        return pltpu.make_async_remote_copy(
            src_ref=own.at[k, span(q)],
            dst_ref=landed.at[k - 1, span(q)],
            send_sem=landed_send.at[k - 1, q],
            recv_sem=landed_recv.at[k - 1, q],
            device_id={"dp": places[k]},
            device_id_type=MESH_ID,
        )

    def small_copy(step):
        place, _ = plane_peer(step)
        return pltpu.make_async_remote_copy(
            src_ref=small_ref,
            dst_ref=small_landed.at[chip * 2 + core],
            send_sem=small_send.at[step],
            recv_sem=small_recv.at[step],
            device_id=place,
            device_id_type=MESH_ID,
        )

    for k in range(4):
        fetch(k).start()

        def start(q, carry):
            pass_over(k, q).start()
            return carry

        lax.fori_loop(0, chunks, start, 0)

    def joined(k, q):
        pass_over(k, q).wait_recv()
        return own[k, span(q)].astype(jnp.float32) + other[k, span(q)].astype(jnp.float32)

    fetch(0).wait()

    def first_leg(place):
        def leg(q, carry):
            own[0, span(q)] = joined(0, q).astype(jnp.bfloat16)
            to_relay(q, place).start()
            return carry

        return leg

    lax.fori_loop(0, split, first_leg(beside), 0)
    lax.fori_loop(split, chunks, first_leg(across), 0)
    lax.fori_loop(1, 8, lambda step, carry: (small_copy(step).start(), carry)[1], 0)
    small_landed[chip * 2 + core] = small_ref[...]
    fetch(1).wait()
    fetch(2).wait()

    def direct(k):
        def leg(q, carry):
            own[k, span(q)] = joined(k, q).astype(jnp.bfloat16)
            to_owner(k, q).start()
            return carry

        return leg

    def relayed(k, place):
        def leg(q, carry):
            to_relay(q, place).wait_recv()
            total = joined(k, q) + relay[span(q)].astype(jnp.float32)
            own[k, span(q)] = total.astype(jnp.bfloat16)
            to_owner(k, q).start()
            return carry

        return leg

    lax.fori_loop(0, split, direct(1), 0)
    lax.fori_loop(split, chunks, direct(2), 0)
    lax.fori_loop(0, split, relayed(2, beside), 0)
    lax.fori_loop(split, chunks, relayed(1, across), 0)
    fetch(3).wait()

    def keep(q, carry):
        total = joined(3, q)
        to_owner(1, q).wait_recv()
        to_owner(2, q).wait_recv()
        grads_ref[span(q)] = (
            total + landed[0, span(q)].astype(jnp.float32) + landed[1, span(q)].astype(jnp.float32)
        )
        return carry

    lax.fori_loop(0, split, keep, 0)
    lax.fori_loop(split, chunks, keep, 0)

    def finish(q, carry):
        for k in range(4):
            pass_over(k, q).wait_send()
        to_owner(1, q).wait_send()
        to_owner(2, q).wait_send()
        return carry

    lax.fori_loop(0, chunks, finish, 0)
    lax.fori_loop(0, split, lambda q, carry: (to_relay(q, beside).wait_send(), carry)[1], 0)
    lax.fori_loop(split, chunks, lambda q, carry: (to_relay(q, across).wait_send(), carry)[1], 0)
    lax.fori_loop(1, 8, lambda step, carry: (small_copy(step).wait(), carry)[1], 0)
    total = small_landed[0]
    for source in range(1, 8):
        total = total + small_landed[source]
    small_out[...] = total


def own_units(parts, small, slots, collective_id):
    unit = parts.shape[1:]
    chunks = max(k for k in range(1, 8) if slots % k == 0)
    block = pltpu.VMEM((4, slots) + unit, jnp.bfloat16)
    return pl.pallas_call(
        functools.partial(own_units_kernel, chunks),
        out_shape=[
            jax.ShapeDtypeStruct((slots,) + unit, jnp.float32),
            jax.ShapeDtypeStruct(small.shape, jnp.float32),
        ],
        in_specs=[whole_any, whole_vmem],
        out_specs=[whole_vmem] * 2,
        scratch_shapes=[
            block,
            block,
            pltpu.VMEM((slots,) + unit, jnp.bfloat16),
            pltpu.VMEM((2, slots) + unit, jnp.bfloat16),
            pltpu.VMEM((8,) + small.shape, jnp.float32),
            pltpu.SemaphoreType.DMA((4,)),
            pltpu.SemaphoreType.DMA((4, chunks)),
            pltpu.SemaphoreType.DMA((4, chunks)),
            pltpu.SemaphoreType.DMA((chunks,)),
            pltpu.SemaphoreType.DMA((chunks,)),
            pltpu.SemaphoreType.DMA((2, chunks)),
            pltpu.SemaphoreType.DMA((2, chunks)),
            pltpu.SemaphoreType.DMA((8,)),
            pltpu.SemaphoreType.DMA((8,)),
        ],
        compiler_params=pltpu.CompilerParams(
            collective_id=collective_id, has_side_effects=True, vmem_limit_bytes=56 << 20
        ),
    )(parts, small)


def to_plane(buffer):
    return lax.all_to_all(buffer, ("dp", "ctx"), split_axis=0, concat_axis=0, tiled=True)


def plain_hits(dest, experts, capacity):
    slots = lax.broadcasted_iota(jnp.int32, (experts * capacity, dest.shape[1]), 0)
    return [slots == dest[k : k + 1] for k in range(2)]


def plain_forward(rows, dest, gates, inner, outer, owners, capacity):
    width = rows.shape[1]
    hits = plain_hits(dest, owners, capacity)
    both = (hits[0] | hits[1]).astype(jnp.bfloat16)
    sent = jnp.dot(both, rows, preferred_element_type=jnp.float32).astype(jnp.bfloat16)
    arrived = to_plane(sent.reshape(owners, capacity, width))
    hidden = jnp.einsum("ocd,df->ocf", arrived, inner, preferred_element_type=jnp.float32)
    active = gelu_tanh(hidden).astype(jnp.bfloat16)
    part = jnp.einsum("ocf,fd->ocd", active, outer, preferred_element_type=jnp.float32)
    returned = to_plane(part.astype(jnp.bfloat16))
    flat = returned.reshape(owners * capacity, width)
    mix = sum(
        gates[:, k : k + 1]
        * lax.dot_general(
            hits[k].astype(jnp.bfloat16),
            flat,
            (((0,), (0,)), ((), ())),
            preferred_element_type=jnp.float32,
        )
        for k in range(2)
    )
    return (mix, arrived, returned)


def plain_backward(rows, dest, gates, returned, arrived, inner, outer):
    owners, capacity, width = arrived.shape
    hits = plain_hits(dest, owners, capacity)
    both = (hits[0] | hits[1]).astype(jnp.bfloat16)
    slot_scale = jnp.sum(
        jnp.where(hits[0], gates[0:1], 0.0) + jnp.where(hits[1], gates[1:2], 0.0), 1, keepdims=True
    )
    slot_grads = jnp.dot(both, rows, preferred_element_type=jnp.float32)
    sent = (slot_grads * slot_scale).astype(jnp.bfloat16)
    flat = returned.reshape(owners * capacity, width)
    dots = jnp.sum(slot_grads * flat.astype(jnp.float32), 1, keepdims=True)
    gate_part = jnp.concatenate(
        [jnp.sum(jnp.where(hit, dots, 0.0), 0, keepdims=True) for hit in hits], 0
    )
    landed = to_plane(sent.reshape(owners, capacity, width))
    grad_active = jnp.einsum("ocd,fd->ocf", landed, outer, preferred_element_type=jnp.float32)
    hidden = jnp.einsum("ocd,df->ocf", arrived, inner, preferred_element_type=jnp.float32)
    active = gelu_tanh(hidden).astype(jnp.bfloat16)
    slope = (grad_active * gelu_slope(hidden)).astype(jnp.bfloat16)
    outer_grad = jnp.einsum("ocf,ocd->fd", active, landed, preferred_element_type=jnp.float32)
    inner_grad = jnp.einsum("ocd,ocf->df", arrived, slope, preferred_element_type=jnp.float32)
    back = jnp.einsum("ocf,df->ocd", slope, inner, preferred_element_type=jnp.float32)
    back = to_plane(back.astype(jnp.bfloat16)).reshape(owners * capacity, width)
    grad = lax.dot_general(
        both, back, (((0,), (0,)), ((), ())), preferred_element_type=jnp.float32
    )
    return (grad, gate_part, inner_grad, outer_grad)


def on_device(
    token_ids,
    targets,
    counted,
    routes,
    priority,
    owner_of,
    master,
    master_first,
    master_second,
    expert_in,
    expert_in_first,
    expert_in_second,
    expert_out,
    expert_out_first,
    expert_out_second,
    norm_gains,
    norm_gains_first,
    norm_gains_second,
    router,
    router_first,
    router_second,
    rel_bias,
    rel_bias_first,
    rel_bias_second,
):
    owners = lax.axis_size(("dp", "ctx"))
    tensor_ranks = lax.axis_size("tensor")
    my_owner = lax.axis_index(("dp", "ctx"))
    my_rank = lax.axis_index("tensor")
    my_context = lax.axis_index("ctx")
    sequences, half_length = token_ids.shape
    tokens_here = sequences * half_length
    most_units = master.shape[2]
    unit_rows = master.shape[3]
    model_width = master.shape[4]
    vocab_here = VOCAB // tensor_ranks
    heads_here = rel_bias.shape[0]
    head_size = model_width // (heads_here * tensor_ranks)
    hidden_here = heads_here * head_size
    experts = router.shape[1]
    capacity = (18 * tokens_here + 8 * experts - 1) // (8 * experts)
    table_units = vocab_here // unit_rows
    query_units = table_units + 2 * hidden_here // unit_rows
    value_units = table_units + 3 * hidden_here // unit_rows
    embed_scale = math.sqrt(model_width)
    owner_ids = owner_of[:, 0]
    on_square = lax.axis_size("dp") == 4 and lax.axis_size("ctx") == 2
    unit_rank, slot_unit, slot_filled = slot_tables(owner_ids, owners, most_units)
    counted_rows = counted.reshape(tokens_here, 2).T.astype(jnp.float32)
    loss_weights = counted_rows * jnp.array([[1.0], [ahead_weight]], jnp.float32)
    counts = jnp.zeros((8, 128), jnp.float32).at[0:2].set(jnp.sum(counted_rows, 1, keepdims=True))
    unit_slots = owner_ids * most_units + unit_rank
    route_pairs = routes.reshape(tokens_here, 2)
    pair_kept, pair_dest = pair_slots(route_pairs, priority[0], experts, capacity)
    dest = jnp.where(pair_kept, pair_dest, -1).reshape(2, tokens_here)
    unit_slots, dest = lax.optimization_barrier((unit_slots, dest))
    local_ids = token_ids.reshape(-1) - my_rank * vocab_here
    inside = (local_ids >= 0) & (local_ids < vocab_here)
    clipped_ids = jnp.clip(local_ids, 0, vocab_here - 1)
    unit_starts = jnp.sum(
        jnp.where(
            (clipped_ids // unit_rows)[None, :] == jnp.arange(unit_slots.shape[0])[:, None],
            unit_slots[:, None] * unit_rows,
            0,
        ),
        0,
    )
    slot_rows = unit_starts + clipped_ids % unit_rows
    if on_square:
        slot_rows = jnp.where(inside, slot_rows, -1)[:, None]
        weights_low, embedded = embed(unit_slots, master[0, 0], slot_rows, 11)
    else:
        master_low = master[0, 0].astype(jnp.bfloat16)
        gathered = lax.all_gather(master_low, ("dp", "ctx"), axis=0, tiled=True)
        looked = jnp.take(gathered.reshape(-1, model_width), slot_rows, axis=0)
        looked = jnp.where(inside[:, None], looked, 0)
        weights_low = pull_units([gathered], unit_slots)
        (embedded,) = sum_line(looked, [], [], keep_total, 1)
    weights_low = weights_low.reshape(-1, model_width)
    joint_low = weights_low[vocab_here : vocab_here + 3 * hidden_here]
    project_low = weights_low[vocab_here + 3 * hidden_here :]
    rolled = [project_low] + [
        lax.ppermute(project_low, "tensor", [(source, (source + step) % 4) for source in range(4)])
        for step in (1, 2, 3)
    ]
    gain_rows = [norm_gains[k : k + 1] for k in range(3)]
    stream_shape = jax.ShapeDtypeStruct((tokens_here, model_width), jnp.float32)
    gain_shape = jax.ShapeDtypeStruct((1, model_width), jnp.float32)
    stream_zero = embedded.astype(jnp.float32) * embed_scale
    first_normalized = norm_forward(stream_zero, norm_gains[0])
    normed_one_low = first_normalized.astype(jnp.bfloat16)
    joint = lax.dot_general(
        joint_low, normed_one_low, (((1,), (1,)), ((), ())), preferred_element_type=jnp.float32
    ).astype(jnp.bfloat16)
    pairs_before = passed_along(joint[hidden_here:], "ctx", 1)
    attended, logsum_rows = attention(rel_bias, joint, pairs_before, heads_here, head_size)
    (attended_all,) = gather_line([attended], 2)
    router_low = router.astype(jnp.bfloat16)
    stream_one, normed_two_low, gate_rows, gate_columns = middle(
        attended_all.reshape(model_width, tokens_here),
        rolled,
        embedded,
        gain_rows[1],
        router_low.T,
        route_pairs.T,
    )
    inner_low = expert_in[0].astype(jnp.bfloat16)
    outer_low = expert_out[0].astype(jnp.bfloat16)
    if on_square:
        moe_partial, arrived, returned, counts = experts_forward(
            normed_two_low, dest, gate_columns, route_pairs, inner_low, outer_low, counts, capacity, 8
        )
    else:
        moe_partial, arrived, returned = plain_forward(
            normed_two_low, dest, gate_columns, inner_low, outer_low, owners, capacity
        )
        counts = lax.psum(counts, ("dp", "ctx"))
    weight_total = counts[0, 0] + ahead_weight * counts[1, 0]
    local_targets = targets.reshape(tokens_here, 2).T - my_rank * vocab_here
    weight_rows = jnp.concatenate(
        [
            loss_weights,
            loss_weights[0:1] + loss_weights[1:2],
            jnp.broadcast_to(1.0 / weight_total, (1, tokens_here)),
        ],
        0,
    )
    head_low, grad_two_low, grad_two, gain_grad_three, logsum_vocab, target_sums, slopes = head_line(
        moe_partial, stream_one, gain_rows[2], weights_low, local_targets, weight_rows, vocab_here, 3
    )
    if on_square:
        moe_grad_part, gate_part, inner_grad, outer_grad = experts_backward(
            grad_two_low,
            dest,
            gate_rows,
            route_pairs.T,
            returned,
            arrived,
            inner_low,
            outer_low,
            9,
        )
    else:
        moe_grad_part, gate_part, inner_grad, outer_grad = plain_backward(
            grad_two_low, dest, gate_rows, returned, arrived, inner_low, outer_low
        )
    gate_part = jnp.concatenate([gate_part, target_sums, jnp.zeros_like(target_sums)], 0)
    gate_block = pltpu.VMEM((3, 4, tokens_here), jnp.float32)
    grad_one_low, grad_one, logit_grad, target_total, gain_grad_two = sum_line(
        moe_grad_part,
        [
            stream_one,
            gain_rows[1],
            grad_two,
            gate_part,
            gate_rows,
            route_pairs.T,
            router_low,
        ],
        [
            stream_shape,
            jax.ShapeDtypeStruct((experts, tokens_here), jnp.bfloat16),
            jax.ShapeDtypeStruct((1, tokens_here), jnp.float32),
            gain_shape,
        ],
        finish_expert_grad,
        5,
        prologue=start_router_grad,
        scratch=(gate_block, pltpu.SemaphoreType.DMA((3,)), pltpu.SemaphoreType.DMA((3,))),
        opening=send_gate_parts,
    )
    router_grad = jnp.dot(logit_grad, normed_two_low, preferred_element_type=jnp.float32)
    loss_local = jnp.sum(weight_rows[2:3] * logsum_vocab) - jnp.sum(target_total)
    query_grad, pair_grad, before_grad, bias_lines = attention_back(
        rel_bias,
        joint,
        pairs_before,
        logsum_rows,
        grad_one_low,
        project_low,
        heads_here,
        head_size,
    )
    grad_after = passed_along(before_grad, "ctx", -1)
    pair_grad_low = (pair_grad + grad_after.astype(jnp.float32)).astype(jnp.bfloat16)
    joint_grad = jnp.concatenate([query_grad, pair_grad_low], 0)
    distances = 2 * (half_length // BLOCK)
    bias_grad = jnp.sum(bias_lines, 1).reshape(heads_here, distances)
    zero_grad_low, gain_grads = sum_line(
        lax.dot_general(
            joint_grad, joint_low, (((0,), (0,)), ((), ())), preferred_element_type=jnp.float32
        ),
        [embedded, gain_rows[0], grad_one, gain_grad_two, gain_grad_three],
        [jax.ShapeDtypeStruct((8, model_width), jnp.float32)],
        functools.partial(finish_input_grad, embed_scale),
        6,
        prologue=clear_gain,
        scratch=(pltpu.SemaphoreType.DMA, pltpu.SemaphoreType.DMA),
        ending=share_gains,
    )
    my_units = jnp.take(slot_unit, my_owner, axis=0)
    my_filled = jnp.take(slot_filled, my_owner, axis=0)[:, None, None]
    outgoing, *expert_states = weight_grads(
        unit_slots,
        owners * most_units,
        unit_rows,
        slopes,
        head_low,
        local_ids[None, :],
        zero_grad_low,
        joint_grad,
        normed_one_low,
        attended,
        grad_one_low,
        (
            expert_in[0],
            expert_in_first[0],
            expert_in_second[0],
            inner_grad,
            expert_out[0],
            expert_out_first[0],
            expert_out_second[0],
            outer_grad,
        ),
    )
    bias_row = jnp.concatenate([bias_grad.reshape(-1), loss_local[None]])
    bias_row = jnp.pad(bias_row, (0, model_width - bias_row.shape[0]))[None]
    small = jnp.concatenate([gain_grads[:3], router_grad, bias_row], 0)
    small = jnp.pad(small, ((0, -small.shape[0] % 8), (0, 0)))
    slot_rates = unit_rates(my_units, table_units, query_units, value_units)[:, None, None]
    states = (master[0, 0], master_first[0, 0], master_second[0, 0])
    if on_square:
        mine, small = own_units(outgoing, small, most_units, 10)
    else:
        mine = lax.psum_scatter(
            outgoing.astype(jnp.float32), ("dp", "ctx"), scatter_dimension=0, tiled=True
        )
        small = lax.psum(small, ("dp", "ctx"))
    states = adam_update(*states, jnp.where(my_filled, mine, 0.0), slot_rates, decay_rate)
    gains_grad = small[:3]
    router_grad = small[3 : 3 + experts].T
    bias_grad = small[3 + experts, : rel_bias.size].reshape(rel_bias.shape)
    loss_totals = jnp.stack([small[3 + experts, rel_bias.size], weight_total])
    gains_new, gains_first_new, gains_second_new = adam_update(
        norm_gains, norm_gains_first, norm_gains_second, gains_grad, rate_gains, 0.0
    )
    router_new, router_first_new, router_second_new = adam_update(
        router, router_first, router_second, router_grad, rate_router, decay_rate
    )
    biases_new, biases_first_new, biases_second_new = adam_update(
        rel_bias, rel_bias_first, rel_bias_second, bias_grad, rate_biases, 0.0
    )
    return (
        loss_totals,
        *(state[None, None] for state in states),
        *(state[None] for state in expert_states),
        gains_new,
        gains_first_new,
        gains_second_new,
        router_new,
        router_first_new,
        router_second_new,
        biases_new,
        biases_first_new,
        biases_second_new,
    )


def solution(mesh):
    in_specs = (
        P("dp", "ctx"),
        P("dp", "ctx", None),
        P("dp", "ctx", None),
        P("dp", "ctx", None),
        P(("dp", "ctx"), None),
        P(),
        P("tensor", ("dp", "ctx"), None, None, None),
        P("tensor", ("dp", "ctx"), None, None, None),
        P("tensor", ("dp", "ctx"), None, None, None),
        P(("dp", "ctx"), None, "tensor"),
        P(("dp", "ctx"), None, "tensor"),
        P(("dp", "ctx"), None, "tensor"),
        P(("dp", "ctx"), "tensor", None),
        P(("dp", "ctx"), "tensor", None),
        P(("dp", "ctx"), "tensor", None),
        P(),
        P(),
        P(),
        P(),
        P(),
        P(),
        P("tensor", None),
        P("tensor", None),
        P("tensor", None),
    )
    out_specs = (
        P(),
        P("tensor", ("dp", "ctx"), None, None, None),
        P("tensor", ("dp", "ctx"), None, None, None),
        P("tensor", ("dp", "ctx"), None, None, None),
        P(("dp", "ctx"), None, "tensor"),
        P(("dp", "ctx"), None, "tensor"),
        P(("dp", "ctx"), None, "tensor"),
        P(("dp", "ctx"), "tensor", None),
        P(("dp", "ctx"), "tensor", None),
        P(("dp", "ctx"), "tensor", None),
        P(),
        P(),
        P(),
        P(),
        P(),
        P(),
        P("tensor", None),
        P("tensor", None),
        P("tensor", None),
    )
    return jax.shard_map(
        on_device, mesh=mesh, in_specs=in_specs, out_specs=out_specs, check_vma=False
    )
```

```python
import functools
import math

import jax
import jax.numpy as jnp
from jax import lax
from jax.experimental import pallas as pl
from jax.experimental.pallas import tpu as pltpu
from jax.sharding import PartitionSpec as P

VOCAB = 32000
BLOCK = 256
STEP = 10


highest_precision = lax.Precision.HIGHEST
beta_first = 0.9
beta_second = 0.95
adam_epsilon = 1e-08
norm_epsilon = 1e-06
ahead_weight = 0.3
masked_score = -1e30
rate_table = 0.1
rate_query = 0.05
rate_values = 0.05
rate_project = 0.5
rate_inner = 0.05
rate_outer = 0.03
rate_gains = 0.5
rate_router = 0.05
rate_biases = 0.5
decay_rate = 0.1


def passed_along(value, axis, steps):
    count = lax.axis_size(axis)
    initial, last = (max(0, -steps), min(count, count - steps))
    return lax.ppermute(value, axis, [(source, source + steps) for source in range(initial, last)])

MESH_ID = pl.DeviceIdType.MESH
whole_vmem = pl.BlockSpec(memory_space=pltpu.VMEM)
whole_any = pl.BlockSpec(memory_space=pl.ANY)
line_lag = 2


def sum_line_kernel(
    rows, count, opening, prologue, epilogue, ending, n_extra, n_aux, n_scratch, part_ref, *refs
):
    extras = refs[:n_extra]
    out_ref = refs[n_extra]
    aux = refs[n_extra + 1 : n_extra + 1 + n_aux]
    rest = refs[n_extra + 1 + n_aux :]
    scratch = rest[:n_scratch]
    stage, from_end, from_mid, send_sem, end_sem, mid_sem, back_sem, back_recv = rest[n_scratch:]
    rank = lax.axis_index("tensor")
    inner = (rank == 1) | (rank == 2)
    end_peer = jnp.where(rank < 2, 1 - rank, 5 - rank)
    mid_peer = 3 - rank
    barrier = pltpu.get_barrier_semaphore()
    if opening is None:
        pl.semaphore_signal(barrier, inc=1, device_id={"tensor": end_peer}, device_id_type=MESH_ID)

        @pl.when(inner)
        def _():
            pl.semaphore_signal(
                barrier, inc=1, device_id={"tensor": mid_peer}, device_id_type=MESH_ID
            )
            pl.semaphore_wait(barrier, 2)

        @pl.when(jnp.logical_not(inner))
        def _():
            pl.semaphore_wait(barrier, 1)
    else:
        for step in (1, 2, 3):
            other = lax.rem(rank + step, 4)
            pl.semaphore_signal(barrier, inc=1, device_id={"tensor": other}, device_id_type=MESH_ID)
        pl.semaphore_wait(barrier, 3)

    def span(i):
        return pl.ds(pl.multiple_of(i * rows, rows), rows)

    def to_inner(i):
        return pltpu.make_async_remote_copy(
            src_ref=stage.at[i],
            dst_ref=from_end.at[i],
            send_sem=send_sem.at[i],
            recv_sem=end_sem.at[i],
            device_id={"tensor": end_peer},
            device_id_type=MESH_ID,
        )

    def to_middle(i):
        return pltpu.make_async_remote_copy(
            src_ref=stage.at[i],
            dst_ref=from_mid.at[i],
            send_sem=send_sem.at[i],
            recv_sem=mid_sem.at[i],
            device_id={"tensor": mid_peer},
            device_id_type=MESH_ID,
        )

    def to_end(i):
        return pltpu.make_async_remote_copy(
            src_ref=out_ref.at[span(i)],
            dst_ref=out_ref.at[span(i)],
            send_sem=back_sem.at[i],
            recv_sem=back_recv.at[i],
            device_id={"tensor": end_peer},
            device_id_type=MESH_ID,
        )

    if opening is not None:
        opening(rank, extras, scratch)

    @pl.when(jnp.logical_not(inner))
    def _():
        def push(i, carry):
            stage[i] = part_ref[span(i)].astype(jnp.bfloat16)
            to_inner(i).start()
            return carry

        lax.fori_loop(0, count, push, 0)

    if prologue is not None:
        prologue(rank, inner, extras, aux, scratch)

    @pl.when(inner)
    def _():
        def step(i, carry):
            @pl.when(i < count)
            def _():
                to_inner(i).wait_recv()
                mine = part_ref[span(i)].astype(jnp.float32) + from_end[i].astype(jnp.float32)
                stage[i] = mine.astype(jnp.bfloat16)
                to_middle(i).start()

            @pl.when(i >= line_lag)
            def _():
                j = i - line_lag
                to_middle(j).wait_recv()
                total = stage[j].astype(jnp.float32) + from_mid[j].astype(jnp.float32)
                out_ref[span(j)] = epilogue(total, span(j), rank, extras, aux, scratch)
                to_end(j).start()

            return carry

        lax.fori_loop(0, count + line_lag, step, 0)

        def drain(i, carry):
            to_middle(i).wait_send()
            to_end(i).wait_send()
            return carry

        lax.fori_loop(0, count, drain, 0)

    @pl.when(jnp.logical_not(inner))
    def _():
        def finish(i, carry):
            to_end(i).wait_recv()
            to_inner(i).wait_send()
            return carry

        lax.fori_loop(0, count, finish, 0)

    if ending is not None:
        ending(inner, end_peer, extras, aux, scratch)


def sum_line(
    part,
    extras,
    aux_shapes,
    epilogue,
    collective_id,
    prologue=None,
    scratch=(),
    opening=None,
    ending=None,
    rows=64,
):
    tokens, width = part.shape
    count = tokens // rows
    chunks = pltpu.VMEM((count, rows, width), jnp.bfloat16)
    return pl.pallas_call(
        functools.partial(
            sum_line_kernel,
            rows,
            count,
            opening,
            prologue,
            epilogue,
            ending,
            len(extras),
            len(aux_shapes),
            len(scratch),
        ),
        out_shape=[jax.ShapeDtypeStruct((tokens, width), jnp.bfloat16)] + list(aux_shapes),
        in_specs=[whole_vmem] * (1 + len(extras)),
        out_specs=[whole_vmem] * (1 + len(aux_shapes)),
        scratch_shapes=list(scratch)
        + [chunks, chunks, chunks]
        + [pltpu.SemaphoreType.DMA((count,))] * 5,
        compiler_params=pltpu.CompilerParams(
            collective_id=collective_id, has_side_effects=True, vmem_limit_bytes=48 << 20
        ),
    )(part, *extras)


def keep_total(total, span, rank, extras, aux, scratch):
    return total.astype(jnp.bfloat16)


def inverse_rms(values):
    return lax.rsqrt(jnp.mean(values * values, -1, keepdims=True) + norm_epsilon)


def norm_back_rows(values, gain, upstream):
    inverse = inverse_rms(values)
    normed = values * inverse
    scaled = upstream * gain
    gain_grad = jnp.sum(upstream * normed, 0, keepdims=True)
    inputs_grad = inverse * (scaled - normed * jnp.mean(scaled * normed, -1, keepdims=True))
    return (inputs_grad, gain_grad)


def clear_gain(rank, inner, extras, aux, scratch):
    @pl.when(inner)
    def _():
        aux[-1][...] = jnp.zeros_like(aux[-1])


def share_gains(inner, end_peer, extras, aux, scratch):
    gains = aux[0]
    copy = pltpu.make_async_remote_copy(
        src_ref=gains,
        dst_ref=gains,
        send_sem=scratch[0],
        recv_sem=scratch[1],
        device_id={"tensor": end_peer},
        device_id_type=MESH_ID,
    )

    @pl.when(inner)
    def _():
        gains[1:2, :] = extras[3][...]
        gains[2:3, :] = extras[4][...]
        copy.start()
        copy.wait_send()

    @pl.when(jnp.logical_not(inner))
    def _():
        copy.wait_recv()


def gate_copies(rank, extras, scratch):
    gate_part = extras[3]
    landed, gate_send, gate_recv = scratch
    return [
        pltpu.make_async_remote_copy(
            src_ref=gate_part,
            dst_ref=landed.at[step - 1],
            send_sem=gate_send.at[step - 1],
            recv_sem=gate_recv.at[step - 1],
            device_id={"tensor": lax.rem(rank + step, 4)},
            device_id_type=MESH_ID,
        )
        for step in (1, 2, 3)
    ]


def send_gate_parts(rank, extras, scratch):
    for copy in gate_copies(rank, extras, scratch):
        copy.start()


def start_router_grad(rank, inner, extras, aux, scratch):
    stream_one, gain, grad_two, gate_part, gates, routes, router_low = extras
    grad_one, logit_grad, target_total, gain_grad = aux
    landed = scratch[0]
    clear_gain(rank, inner, extras, aux, scratch)
    for copy in gate_copies(rank, extras, scratch):
        copy.wait()
    gate_grad = jnp.zeros(gate_part.shape, jnp.float32)
    for source in range(4):
        piece = jnp.zeros(gate_part.shape, jnp.float32)
        for step in (1, 2, 3):
            piece = jnp.where(lax.rem(source + step, 4) == rank, landed[step - 1], piece)
        gate_grad = gate_grad + jnp.where(rank == source, gate_part[...], piece)
    target_total[...] = gate_grad[2:3]
    gate_grad = gate_grad[0:2]
    weighted = gates[...] * gate_grad
    chosen = gates[...] * (gate_grad - (weighted[0:1] + weighted[1:2]))
    experts, tokens = logit_grad.shape
    row = lax.broadcasted_iota(jnp.int32, (experts, tokens), 0)
    placed = jnp.where(row == routes[0:1], chosen[0:1], 0.0) + jnp.where(
        row == routes[1:2], chosen[1:2], 0.0
    )
    logit_grad[...] = placed.astype(jnp.bfloat16)

    @pl.when(inner)
    def _():
        grad_one[...] = lax.dot_general(
            logit_grad[...],
            router_low[...],
            (((0,), (1,)), ((), ())),
            preferred_element_type=jnp.float32,
        )


def finish_expert_grad(total, span, rank, extras, aux, scratch):
    stream_one, gain, grad_two, gate_part, gates, routes, router_low = extras
    grad_one, logit_grad, target_total, gain_grad = aux
    part, gain_part = norm_back_rows(
        stream_one[span], gain[...], total + grad_one[span]
    )
    result = grad_two[span] + part
    grad_one[span] = result
    gain_grad[...] += gain_part
    return result.astype(jnp.bfloat16)


def finish_input_grad(scale, total, span, rank, extras, aux, scratch):
    embedded, gain, grad_one = extras[:3]
    stream_zero = embedded[span].astype(jnp.float32) * scale
    part, gain_part = norm_back_rows(stream_zero, gain[...], total)
    aux[0][0:1, :] += gain_part
    return ((grad_one[span] + part) * scale).astype(jnp.bfloat16)


def gather_line_kernel(count, *refs):
    ins = refs[:count]
    outs = refs[count : 2 * count]
    local_sem, send_sem, recv_sem = refs[2 * count :]
    rank = lax.axis_index("tensor")
    barrier = pltpu.get_barrier_semaphore()
    for step in (1, 2, 3):
        other = lax.rem(rank + step, 4)
        pl.semaphore_signal(barrier, inc=1, device_id={"tensor": other}, device_id_type=MESH_ID)
    pl.semaphore_wait(barrier, 3)
    copies = []
    for k in range(count):
        for step in (1, 2, 3):
            copy = pltpu.make_async_remote_copy(
                src_ref=ins[k],
                dst_ref=outs[k].at[rank],
                send_sem=send_sem.at[k, step - 1],
                recv_sem=recv_sem.at[k, step - 1],
                device_id={"tensor": lax.rem(rank + step, 4)},
                device_id_type=MESH_ID,
            )
            copy.start()
            copies.append(copy)
        own = pltpu.make_async_copy(ins[k], outs[k].at[rank], local_sem.at[k])
        own.start()
        own.wait()
    for copy in copies:
        copy.wait()


def gather_line(arrays, collective_id):
    count = len(arrays)
    return pl.pallas_call(
        functools.partial(gather_line_kernel, count),
        out_shape=[jax.ShapeDtypeStruct((4,) + x.shape, x.dtype) for x in arrays],
        in_specs=[whole_vmem] * count,
        out_specs=[whole_vmem] * count,
        scratch_shapes=[
            pltpu.SemaphoreType.DMA((count,)),
            pltpu.SemaphoreType.DMA((count, 3)),
            pltpu.SemaphoreType.DMA((count, 3)),
        ],
        compiler_params=pltpu.CompilerParams(
            collective_id=collective_id, has_side_effects=True, vmem_limit_bytes=40 << 20
        ),
    )(*arrays)


def middle_kernel(
    attended_ref, embedded_ref, gain_ref, router_ref, routes_ref, *refs
):
    rolled, (stream_ref, normed_ref, rows_ref, columns_ref, project_ref) = refs[:4], refs[4:]

    @pl.when(pl.program_id(0) == 0)
    def _():
        for step in range(4):
            lines = rolled[step].shape[0]
            owner = lax.rem(lax.axis_index("tensor") + 4 - step, 4)
            project_ref[pl.ds(pl.multiple_of(owner * lines, lines), lines)] = rolled[step][...]

    scale = math.sqrt(embedded_ref.shape[1])
    stream = embedded_ref[...].astype(jnp.float32) * scale + lax.dot_general(
        attended_ref[...], project_ref[...], (((0,), (0,)), ((), ())), preferred_element_type=jnp.float32
    )
    stream_ref[...] = stream
    normed = (stream * inverse_rms(stream) * gain_ref[...]).astype(jnp.bfloat16)
    normed_ref[...] = normed
    scores = lax.dot_general(
        router_ref[...], normed, (((1,), (1,)), ((), ())), preferred_element_type=jnp.float32
    )
    expert = lax.broadcasted_iota(jnp.int32, scores.shape, 0)
    first, second = (
        jnp.sum(jnp.where(expert == routes_ref[k : k + 1, :], scores, 0.0), 0, keepdims=True)
        for k in range(2)
    )
    top = jnp.maximum(first, second)
    first, second = jnp.exp(first - top), jnp.exp(second - top)
    total = first + second
    gates = jnp.concatenate([first / total, second / total], 0)
    rows_ref[...] = gates
    columns_ref[...] = jnp.concatenate([gates, jnp.zeros((6, gates.shape[1]), jnp.float32)], 0).T


def middle(attended, rolled, embedded, gain, router, routes):
    tokens, width = embedded.shape
    tile = 256
    fixed = lambda k: (0, 0)
    whole = lambda x: pl.BlockSpec(x.shape, fixed)
    down = lambda n: pl.BlockSpec((tile, n), lambda k: (k, 0))
    along = lambda n: pl.BlockSpec((n, tile), lambda k: (0, k))
    return pl.pallas_call(
        middle_kernel,
        grid=(tokens // tile,),
        out_shape=[
            jax.ShapeDtypeStruct((tokens, width), jnp.float32),
            jax.ShapeDtypeStruct((tokens, width), jnp.bfloat16),
            jax.ShapeDtypeStruct((2, tokens), jnp.float32),
            jax.ShapeDtypeStruct((tokens, 8), jnp.float32),
        ],
        in_specs=[along(width), down(width), whole(gain), whole(router), along(2)]
        + [whole(x) for x in rolled],
        out_specs=[down(width), down(width), along(2), down(8)],
        scratch_shapes=[pltpu.VMEM((width, width), jnp.bfloat16)],
        compiler_params=pltpu.CompilerParams(vmem_limit_bytes=40 << 20),
    )(attended, embedded, gain, router, routes, *rolled)


def embed_kernel(chunks, slots_ref, mine_ref, rows_ref, units_ref, embedded_ref, *refs):
    held, total, stage, from_end, from_mid = refs[:5]
    send_x, recv_x, send_y, recv_y, send_z, recv_z, send_core, recv_core = refs[5:13]
    send_sem, end_sem, mid_sem, back_sem, back_recv = refs[13:]
    chip, core = lax.axis_index("dp"), lax.axis_index("ctx")
    beside = chip + 1 - 2 * lax.rem(chip, 2)
    across = lax.rem(chip + 2, 4)
    opposite = across + 1 - 2 * lax.rem(across, 2)
    places = (chip, beside, across, opposite)
    rank = lax.axis_index("tensor")
    inner = (rank == 1) | (rank == 2)
    end_peer = jnp.where(rank < 2, 1 - rank, 5 - rank)
    mid_peer = 3 - rank
    slots, unit_rows = mine_ref.shape[:2]
    width = total.shape[2]
    size = slots // chunks
    split = (chunks + 1) // 2
    tokens = rows_ref.shape[0]
    count, rows = stage.shape[1:3]

    def repeat(first, last, body):
        def step(i, carry):
            body(i)
            return carry

        lax.fori_loop(first, last, step, 0)

    def columns(h):
        return slice(h * width, (h + 1) * width)

    own = (chip * 2 + core) * slots
    for h in range(2):
        held[h, pl.ds(own, slots)] = mine_ref[:, :, columns(h)].astype(jnp.bfloat16)
    barrier = pltpu.get_barrier_semaphore()
    for place in ({"ctx": 1 - core}, {"dp": beside}, {"dp": across}, {"tensor": end_peer}):
        pl.semaphore_signal(barrier, inc=1, device_id=place, device_id_type=MESH_ID)

    @pl.when(inner)
    def _():
        pl.semaphore_signal(barrier, inc=1, device_id={"tensor": mid_peer}, device_id_type=MESH_ID)
        pl.semaphore_wait(barrier, 5)

    @pl.when(jnp.logical_not(inner))
    def _():
        pl.semaphore_wait(barrier, 4)

    def remote(source, target, send, recv, place):
        return pltpu.make_async_remote_copy(
            src_ref=source,
            dst_ref=target,
            send_sem=send,
            recv_sem=recv,
            device_id=place,
            device_id_type=MESH_ID,
        )

    def copy(h, place, q, send, recv, target):
        piece = held.at[h, pl.ds((place * 2 + core) * slots + q * size, size)]
        return remote(piece, piece, send, recv, target)

    def to_beside(h, q):
        return copy(h, chip, q, send_x.at[h, q], recv_x.at[h, q], {"dp": beside})

    def to_across(h, q):
        return copy(h, chip, q, send_y.at[h, q], recv_y.at[h, q], {"dp": across})

    def passed_on(h, q, source, target):
        return copy(h, source, q, send_z.at[h, q], recv_z.at[h, q], {"dp": target})

    def to_core(h, k, q):
        return copy(h, places[k], q, send_core.at[h, k, q], recv_core.at[h, k, q], {"ctx": 1 - core})

    def start(h):
        def both(i):
            to_beside(h, i).start()
            to_across(h, lax.rem(i + split, chunks)).start()

        repeat(0, chunks, both)
        repeat(0, chunks, lambda q: to_core(h, 0, q).start())

    def look(h, place, which):
        begin = (place * 2 + which) * slots
        lines = slots * unit_rows
        column = lax.broadcasted_iota(jnp.int32, (tokens, lines), 1) + begin * unit_rows
        hit = jnp.where(column == rows_ref[...], 1.0, 0.0).astype(jnp.bfloat16)
        block = held[h, pl.ds(begin, slots)].reshape(lines, width)
        total[h] += jnp.dot(hit, block, preferred_element_type=jnp.float32)

    def relay(h, i):
        to_beside(h, i).wait_recv()

        @pl.when(i < split)
        def _():
            passed_on(h, i, beside, across).start()

        to_core(h, 1, i).start()
        j = lax.rem(i + split, chunks)
        to_across(h, j).wait_recv()

        @pl.when(j >= split)
        def _():
            passed_on(h, j, across, beside).start()

        to_core(h, 2, j).start()

    def rest(h):
        repeat(0, chunks, lambda q: to_core(h, 0, q).wait_recv())
        look(h, chip, 1 - core)
        look(h, beside, core)
        look(h, across, core)

        def last(q):
            passed_on(h, q, opposite, opposite).wait_recv()
            to_core(h, 3, q).start()
            to_core(h, 1, q).wait_recv()
            to_core(h, 2, q).wait_recv()

        repeat(0, chunks, last)
        look(h, beside, 1 - core)
        look(h, across, 1 - core)
        look(h, opposite, core)
        repeat(0, chunks, lambda q: to_core(h, 3, q).wait_recv())
        look(h, opposite, 1 - core)

    def span(i):
        return pl.ds(pl.multiple_of(i * rows, rows), rows)

    def to_inner(h, i):
        return remote(
            stage.at[h, i], from_end.at[h, i], send_sem.at[h, i], end_sem.at[h, i], {"tensor": end_peer}
        )

    def to_middle(h, i):
        return remote(
            stage.at[h, i], from_mid.at[h, i], send_sem.at[h, i], mid_sem.at[h, i], {"tensor": mid_peer}
        )

    def to_end(h, i):
        piece = embedded_ref.at[span(i), columns(h)]
        return remote(piece, piece, back_sem.at[h, i], back_recv.at[h, i], {"tensor": end_peer})

    def push(h):
        @pl.when(jnp.logical_not(inner))
        def _():
            def one(i):
                stage[h, i] = total[h, span(i)].astype(jnp.bfloat16)
                to_inner(h, i).start()

            repeat(0, count, one)

    def exchange(h, i):
        @pl.when(inner & (i < count))
        def _():
            to_inner(h, i).wait_recv()
            stage[h, i] = (total[h, span(i)] + from_end[h, i].astype(jnp.float32)).astype(jnp.bfloat16)
            to_middle(h, i).start()

        @pl.when(inner & (i >= line_lag))
        def _():
            j = i - line_lag
            to_middle(h, j).wait_recv()
            both = stage[h, j].astype(jnp.float32) + from_mid[h, j].astype(jnp.float32)
            embedded_ref[span(j), columns(h)] = both.astype(jnp.bfloat16)
            to_end(h, j).start()

    total[...] = jnp.zeros_like(total)
    start(0)
    look(0, chip, core)
    repeat(0, chunks, lambda i: relay(0, i))
    start(1)
    rest(0)
    push(0)
    look(1, chip, core)

    def between(i):
        exchange(0, i)

        @pl.when(i < chunks)
        def _():
            relay(1, i)

    repeat(0, count + line_lag, between)
    rest(1)
    push(1)

    def place_unit(u):
        for h in range(2):
            units_ref[u, :, columns(h)] = held[h, slots_ref[u]]

    @pl.when(jnp.logical_not(inner))
    def _():
        repeat(0, units_ref.shape[0], place_unit)

    repeat(0, count + line_lag, lambda i: exchange(1, i))

    @pl.when(inner)
    def _():
        repeat(0, units_ref.shape[0], place_unit)

    def finish(q):
        for h in range(2):
            to_beside(h, q).wait_send()
            to_across(h, q).wait_send()
            for k in range(4):
                to_core(h, k, q).wait_send()
            passed_on(h, q, opposite, opposite).wait_send()

    repeat(0, chunks, finish)

    @pl.when(inner)
    def _():
        def drain(i):
            for h in range(2):
                to_middle(h, i).wait_send()
                to_end(h, i).wait_send()

        repeat(0, count, drain)

    @pl.when(jnp.logical_not(inner))
    def _():
        def drain(i):
            for h in range(2):
                to_end(h, i).wait_recv()
                to_inner(h, i).wait_send()

        repeat(0, count, drain)


def embed(unit_slots, mine, slot_rows, collective_id):
    slots, unit_rows, width = mine.shape
    tokens = slot_rows.shape[0]
    chunks = max(k for k in range(1, 8) if slots % k == 0)
    rows = 128
    half = width // 2
    sems = pltpu.SemaphoreType.DMA((2, chunks))
    line = pltpu.VMEM((2, tokens // rows, rows, half), jnp.bfloat16)
    return pl.pallas_call(
        functools.partial(embed_kernel, chunks),
        out_shape=[
            jax.ShapeDtypeStruct((unit_slots.shape[0], unit_rows, width), jnp.bfloat16),
            jax.ShapeDtypeStruct((tokens, width), jnp.bfloat16),
        ],
        in_specs=[pl.BlockSpec(memory_space=pltpu.SMEM), whole_vmem, whole_vmem],
        out_specs=[whole_vmem] * 2,
        scratch_shapes=[
            pltpu.VMEM((2, 8 * slots, unit_rows, half), jnp.bfloat16),
            pltpu.VMEM((2, tokens, half), jnp.float32),
            line,
            line,
            line,
        ]
        + [sems] * 6
        + [pltpu.SemaphoreType.DMA((2, 4, chunks))] * 2
        + [pltpu.SemaphoreType.DMA((2, tokens // rows))] * 5,
        compiler_params=pltpu.CompilerParams(
            collective_id=collective_id, has_side_effects=True, vmem_limit_bytes=60 << 20
        ),
    )(unit_slots, mine, slot_rows)


def pull_units_kernel(parts, slots_ref, *refs):
    sources, out_ref, sem = refs[:parts], refs[parts], refs[parts + 1]
    width = out_ref.shape[-1] // parts

    def push(u, carry):
        for part in range(parts):
            pltpu.make_async_copy(
                sources[part].at[slots_ref[u]],
                out_ref.at[u, :, part * width : (part + 1) * width],
                sem,
            ).start()
        return carry

    lax.fori_loop(0, out_ref.shape[0], push, 0)
    pltpu.make_async_copy(out_ref, out_ref, sem).wait()


def pull_units(sources, slots):
    count = slots.shape[0]
    rows, width = sources[0].shape[1:]
    return pl.pallas_call(
        functools.partial(pull_units_kernel, len(sources)),
        out_shape=jax.ShapeDtypeStruct((count, rows, width * len(sources)), sources[0].dtype),
        in_specs=[pl.BlockSpec(memory_space=pltpu.SMEM)] + [whole_any] * len(sources),
        out_specs=whole_vmem,
        scratch_shapes=[pltpu.SemaphoreType.DMA],
        compiler_params=pltpu.CompilerParams(vmem_limit_bytes=40 << 20),
    )(slots, *sources)


def attention_kernel(heads, size, bias_ref, own_ref, before_ref, out_ref, logsum_ref, scores, peak, total):
    tokens = own_ref.shape[1]
    blocks = tokens // BLOCK
    hidden = heads * size
    later = lax.axis_index("ctx") > 0

    for head in range(heads):
        query = own_ref[head * size : (head + 1) * size, :].astype(jnp.float32).T * size**-0.5
        query = query.astype(jnp.bfloat16)
        own_keys = own_ref[hidden + head * size : hidden + (head + 1) * size, :]
        old_keys = before_ref[head * size : (head + 1) * size, :]
        own_values = own_ref[2 * hidden + head * size : 2 * hidden + (head + 1) * size, :]
        own_values = own_values.astype(jnp.float32).T.astype(jnp.bfloat16)
        old_values = before_ref[hidden + head * size : hidden + (head + 1) * size, :]
        old_values = old_values.astype(jnp.float32).T.astype(jnp.bfloat16)
        for block in range(blocks):
            rows = query[block * BLOCK : (block + 1) * BLOCK]
            width = (block + 1) * BLOCK
            mine = jnp.dot(rows, own_keys[:, :width], preferred_element_type=jnp.float32)
            top = None
            parts = []
            for k in range(block + 1):
                part = mine[:, k * BLOCK : (k + 1) * BLOCK] + bias_ref[head, block - k]
                parts.append(part)
                high = jnp.max(part, 1, keepdims=True)
                top = high if top is None else jnp.maximum(top, high)
            peak[...] = top

            @pl.when(later)
            def _():
                old = jnp.dot(rows, old_keys, preferred_element_type=jnp.float32)
                top_old = None
                for k in range(blocks):
                    part = old[:, k * BLOCK : (k + 1) * BLOCK] + bias_ref[head, block + blocks - k]
                    scores[:, k * BLOCK : (k + 1) * BLOCK] = part
                    high = jnp.max(part, 1, keepdims=True)
                    top_old = high if top_old is None else jnp.maximum(top_old, high)
                peak[...] = jnp.maximum(peak[...], top_old)

            top = peak[...]
            parts = [jnp.exp(part - top) for part in parts]
            own_sum = None
            for part in parts:
                part_sum = jnp.sum(part, 1, keepdims=True)
                own_sum = part_sum if own_sum is None else own_sum + part_sum
            total[...] = own_sum

            @pl.when(later)
            def _():
                old_exp = jnp.exp(scores[...] - top)
                scores[...] = old_exp
                total[...] += jnp.sum(old_exp, 1, keepdims=True)

            full = total[...]
            inverse = 1.0 / full
            low = jnp.concatenate([(part * inverse).astype(jnp.bfloat16) for part in parts], 1)
            result = jnp.dot(low, own_values[:width], preferred_element_type=jnp.float32)
            peak[...] = top + jnp.log(full)
            logsum_ref[head, block * BLOCK : (block + 1) * BLOCK, :] = peak[...]
            place = (slice(head * size, (head + 1) * size), slice(block * BLOCK, (block + 1) * BLOCK))

            @pl.when(later)
            def _():
                low_old = (scores[...] * inverse).astype(jnp.bfloat16)
                both = result + jnp.dot(low_old, old_values, preferred_element_type=jnp.float32)
                out_ref[place] = both.T.astype(jnp.bfloat16)

            @pl.when(jnp.logical_not(later))
            def _():
                out_ref[place] = result.T.astype(jnp.bfloat16)


def attention(biases, own, before, heads, size):
    tokens = own.shape[1]
    return pl.pallas_call(
        functools.partial(attention_kernel, heads, size),
        out_shape=[
            jax.ShapeDtypeStruct((heads * size, tokens), jnp.bfloat16),
            jax.ShapeDtypeStruct((heads, tokens, 1), jnp.float32),
        ],
        in_specs=[pl.BlockSpec(memory_space=pltpu.SMEM), whole_vmem, whole_vmem],
        out_specs=[whole_vmem, whole_vmem],
        scratch_shapes=[
            pltpu.VMEM((BLOCK, tokens), jnp.float32),
            pltpu.VMEM((BLOCK, 1), jnp.float32),
            pltpu.VMEM((BLOCK, 1), jnp.float32),
        ],
        compiler_params=pltpu.CompilerParams(vmem_limit_bytes=40 << 20),
    )(biases, own, before)


def attention_back_kernel(
    heads, size, bias_ref, own_ref, before_ref, logsum_ref, grad_ref, project_ref,
    *refs
):
    states, (query_out, own_out, before_out, bias_out) = refs[:8], refs[8:12]
    updated, (probs, slopes, inner, query_sum, own_sum, before_sum) = refs[12:18], refs[18:24]
    held, load_sem, store_sem = refs[24:]
    loads = [pltpu.make_async_copy(states[k], held.at[k], load_sem.at[k]) for k in range(8)]
    stores = [
        pltpu.make_async_copy(held.at[4 * (k // 3) + k % 3], updated[k], store_sem.at[k])
        for k in range(6)
    ]
    for load in loads:
        load.start()

    def update(i, carry):
        lines = held.shape[1] // 16
        span = pl.ds(pl.multiple_of(i * lines, lines), lines)
        for k, rate in enumerate((rate_inner, rate_outer)):
            fresh = adam_update(*(held[4 * k + n, span] for n in range(4)), rate, decay_rate)
            for n in range(3):
                held[4 * k + n, span] = fresh[n]
        return carry

    tokens = own_ref.shape[1]
    blocks = tokens // BLOCK
    hidden = heads * size
    later = lax.axis_index("ctx") > 0
    bias_out[...] = jnp.zeros_like(bias_out)

    def flipped(rows):
        return rows.astype(jnp.float32).T.astype(jnp.bfloat16)

    for head in range(heads):
        span = slice(head * size, (head + 1) * size)
        value_span = slice(hidden + head * size, hidden + (head + 1) * size)
        query_rows = own_ref[span, :]
        query = flipped(query_rows) * jnp.bfloat16(size**-0.5)
        own_keys = own_ref[hidden + head * size : hidden + (head + 1) * size, :]
        own_values = own_ref[2 * hidden + head * size : 2 * hidden + (head + 1) * size, :]
        old_keys = before_ref[span, :]
        old_values = before_ref[value_span, :]
        own_keys_flip = flipped(own_keys)
        grad = lax.dot_general(
            grad_ref[...], project_ref[span, :], (((1,), (1,)), ((), ())), preferred_element_type=jnp.float32
        )
        grad_rows = grad.T.astype(jnp.bfloat16)
        grad = grad.astype(jnp.bfloat16)
        own_sum[...] = jnp.zeros_like(own_sum)

        @pl.when(later)
        def _():
            before_sum[...] = jnp.zeros_like(before_sum)

        for block in range(blocks):
            at = slice(block * BLOCK, (block + 1) * BLOCK)
            width = (block + 1) * BLOCK
            rows, up = query[at], grad[at]
            lse = logsum_ref[head, at, :]
            score = jnp.dot(rows, own_keys[:, :width], preferred_element_type=jnp.float32)
            prob = jnp.concatenate(
                [
                    jnp.exp(score[:, k * BLOCK : (k + 1) * BLOCK] + (bias_ref[head, block - k] - lse))
                    for k in range(block + 1)
                ],
                1,
            )
            slope = jnp.dot(up, own_values[:, :width], preferred_element_type=jnp.float32)
            inner[...] = jnp.sum(prob * slope, 1, keepdims=True)

            @pl.when(later)
            def _():
                score = jnp.dot(rows, old_keys, preferred_element_type=jnp.float32)
                old_slope = jnp.dot(up, old_values, preferred_element_type=jnp.float32)
                old_prob = jnp.concatenate(
                    [
                        jnp.exp(
                            score[:, k * BLOCK : (k + 1) * BLOCK]
                            + (bias_ref[head, block + blocks - k] - lse)
                        )
                        for k in range(blocks)
                    ],
                    1,
                )
                probs[...] = old_prob
                slopes[...] = old_slope
                inner[...] += jnp.sum(old_prob * old_slope, 1, keepdims=True)

            row_inner = inner[...]
            low_grad = (prob * (slope - row_inner)).astype(jnp.bfloat16)
            query_sum[...] = jnp.dot(
                low_grad, own_keys_flip[:width], preferred_element_type=jnp.float32
            )
            own_sum[:size, :width] += jnp.dot(
                query_rows[:, at], low_grad, preferred_element_type=jnp.float32
            )
            own_sum[size:, :width] += jnp.dot(
                grad_rows[:, at], prob.astype(jnp.bfloat16), preferred_element_type=jnp.float32
            )
            for k in range(block + 1):
                line = head * 2 * blocks + block - k
                bias_out[line : line + 1, :] += jnp.sum(
                    low_grad[:, k * BLOCK : (k + 1) * BLOCK].astype(jnp.float32), 0, keepdims=True
                )

            @pl.when(later)
            def _():
                old_prob = probs[...]
                low_old = (old_prob * (slopes[...] - row_inner)).astype(jnp.bfloat16)
                query_sum[...] += jnp.dot(
                    low_old, flipped(old_keys), preferred_element_type=jnp.float32
                )
                before_sum[:size, :] += jnp.dot(
                    query_rows[:, at], low_old, preferred_element_type=jnp.float32
                )
                before_sum[size:, :] += jnp.dot(
                    grad_rows[:, at], old_prob.astype(jnp.bfloat16), preferred_element_type=jnp.float32
                )
                for k in range(blocks):
                    line = head * 2 * blocks + block + blocks - k
                    bias_out[line : line + 1, :] += jnp.sum(
                        low_old[:, k * BLOCK : (k + 1) * BLOCK].astype(jnp.float32), 0, keepdims=True
                    )

            query_out[span, at] = (query_sum[...].T * size**-0.5).astype(jnp.bfloat16)

        own_out[span, :] = own_sum[:size, :] * size**-0.5
        own_out[value_span, :] = own_sum[size:, :]

        @pl.when(later)
        def _():
            before_out[span, :] = (before_sum[:size, :] * size**-0.5).astype(jnp.bfloat16)
            before_out[value_span, :] = before_sum[size:, :].astype(jnp.bfloat16)

        if head == 0:
            for load in loads:
                load.wait()
            lax.fori_loop(0, 16, update, 0)
            for store in stores:
                store.start()

    @pl.when(jnp.logical_not(later))
    def _():
        before_out[...] = jnp.zeros_like(before_out)

    for store in stores:
        store.wait()


def attention_back(biases, own, before, logsum, grad, project, states, heads, size):
    tokens = own.shape[1]
    hidden = heads * size
    return pl.pallas_call(
        functools.partial(attention_back_kernel, heads, size),
        out_shape=[
            jax.ShapeDtypeStruct((hidden, tokens), jnp.bfloat16),
            jax.ShapeDtypeStruct((2 * hidden, tokens), jnp.float32),
            jax.ShapeDtypeStruct((2 * hidden, tokens), jnp.bfloat16),
            jax.ShapeDtypeStruct((heads * 2 * (tokens // BLOCK), BLOCK), jnp.float32),
        ]
        + [jax.ShapeDtypeStruct(states[0].shape, jnp.float32)] * 6,
        in_specs=[pl.BlockSpec(memory_space=pltpu.SMEM)] + [whole_vmem] * 5 + [whole_any] * 8,
        out_specs=[whole_vmem] * 4 + [whole_any] * 6,
        scratch_shapes=[
            pltpu.VMEM((BLOCK, tokens), jnp.float32),
            pltpu.VMEM((BLOCK, tokens), jnp.float32),
            pltpu.VMEM((BLOCK, 1), jnp.float32),
            pltpu.VMEM((BLOCK, size), jnp.float32),
            pltpu.VMEM((2 * size, tokens), jnp.float32),
            pltpu.VMEM((2 * size, tokens), jnp.float32),
            pltpu.VMEM((8,) + states[0].shape, jnp.float32),
            pltpu.SemaphoreType.DMA((8,)),
            pltpu.SemaphoreType.DMA((6,)),
        ],
        compiler_params=pltpu.CompilerParams(vmem_limit_bytes=48 << 20),
    )(biases, own, before, logsum, grad, project, *states)


def vocab_tile(vocab):
    return max(k for k in range(16, 1601, 16) if vocab % k == 0)


def head_line_kernel(
    tile, part_ref, stream_ref, gain_ref, table_ref, wanted_ref, weight_ref,
    low_ref, grad_low_ref, grad_ref, gain_grad, logsum_ref, picked_ref, slopes_ref,
    table, stage, from_end, from_mid, own, turned, stats, landed, slope_tiles, total,
    load_sem, send_sem, end_sem, mid_sem, back_sem, back_recv, stat_send, stat_recv, store_sem,
):
    rank = lax.axis_index("tensor")
    inner = (rank == 1) | (rank == 2)
    end_peer = jnp.where(rank < 2, 1 - rank, 5 - rank)
    mid_peer = 3 - rank
    count, rows = stage.shape[:2]
    columns = turned.shape[1]
    pieces = table.shape[0] // tile
    group = columns // rows
    tiles = count // group
    units = tiles * pieces
    vocab = table.shape[0]
    load = pltpu.make_async_copy(table_ref.at[pl.ds(0, vocab)], table, load_sem)
    load.start()
    barrier = pltpu.get_barrier_semaphore()
    for step in (1, 2, 3):
        other = lax.rem(rank + step, 4)
        pl.semaphore_signal(barrier, inc=1, device_id={"tensor": other}, device_id_type=MESH_ID)
    pl.semaphore_wait(barrier, 3)

    def span(i):
        return pl.ds(pl.multiple_of(i * rows, rows), rows)

    def over(t):
        return pl.ds(pl.multiple_of(t * columns, columns), columns)

    def line_copy(source, target, send, recv, peer):
        return pltpu.make_async_remote_copy(
            src_ref=source,
            dst_ref=target,
            send_sem=send,
            recv_sem=recv,
            device_id={"tensor": peer},
            device_id_type=MESH_ID,
        )

    def to_inner(i):
        return line_copy(stage.at[i], from_end.at[i], send_sem.at[i], end_sem.at[i], end_peer)

    def to_middle(i):
        return line_copy(stage.at[i], from_mid.at[i], send_sem.at[i], mid_sem.at[i], mid_peer)

    def to_end(ref, i):
        rows_of = ref.at[span(i)]
        return line_copy(rows_of, rows_of, back_sem.at[i], back_recv.at[i], end_peer)

    def repeat(first, last, body):
        def step(i, carry):
            body(i)
            return carry

        lax.fori_loop(first, last, step, 0)

    def turn(t):
        turned[...] = low_ref[over(t)].astype(jnp.float32).T.astype(jnp.bfloat16)

    def table_rows(k):
        return table[pl.ds(pl.multiple_of(k * tile, tile), tile)]

    def sums_unit(n):
        t, k = n // pieces, lax.rem(n, pieces)

        @pl.when(k == 0)
        def _():
            turn(t)

        logits = jnp.dot(table_rows(k), turned[...], preferred_element_type=jnp.float32)
        before = stats[0:1, over(t)]
        top = jnp.maximum(before, jnp.max(logits, 0, keepdims=True))
        stats[1:2, over(t)] = stats[1:2, over(t)] * jnp.exp(before - top) + jnp.sum(
            jnp.exp(logits - top), 0, keepdims=True
        )
        stats[0:1, over(t)] = top

    stats[0:1, :] = jnp.full_like(stats[0:1, :], masked_score)
    stats[1:2, :] = jnp.zeros_like(stats[1:2, :])

    @pl.when(jnp.logical_not(inner))
    def _():
        def push(i):
            stage[i] = part_ref[span(i)].astype(jnp.bfloat16)
            to_inner(i).start()

        repeat(0, count, push)
        load.wait()

        def forward(t):
            repeat(0, group, lambda c: to_end(low_ref, t * group + c).wait_recv())
            repeat(0, pieces, lambda k: sums_unit(t * pieces + k))

        repeat(0, tiles, forward)
        repeat(0, count, lambda i: to_inner(i).wait_send())

    @pl.when(inner)
    def _():
        gain_grad[...] = jnp.zeros_like(gain_grad)
        load.wait()
        ahead = group + line_lag

        def step(i):
            @pl.when(i < count)
            def _():
                to_inner(i).wait_recv()
                mine = part_ref[span(i)] + from_end[i].astype(jnp.float32)
                stage[i] = mine.astype(jnp.bfloat16)
                to_middle(i).start()

            @pl.when(i >= line_lag)
            def _():
                j = i - line_lag
                to_middle(j).wait_recv()
                stream_two = stream_ref[span(j)] + (
                    stage[j].astype(jnp.float32) + from_mid[j].astype(jnp.float32)
                )
                grad_ref[span(j)] = stream_two
                low_ref[span(j)] = (stream_two * inverse_rms(stream_two) * gain_ref[...]).astype(
                    jnp.bfloat16
                )
                to_end(low_ref, j).start()

            @pl.when(i >= ahead)
            def _():
                sums_unit(i - ahead)

        repeat(0, count + line_lag, step)
        repeat(count + line_lag - ahead, units, sums_unit)

        def drain(i):
            to_middle(i).wait_send()
            to_end(low_ref, i).wait_send()

        repeat(0, count, drain)

    copies = [
        line_copy(
            stats, landed.at[step - 1], stat_send.at[step - 1], stat_recv.at[step - 1], lax.rem(rank + step, 4)
        )
        for step in (1, 2, 3)
    ]
    for copy in copies:
        copy.start()
    for copy in copies:
        copy.wait()
    tops, sums = [], []
    for source in range(4):
        piece = stats[...]
        for step in (1, 2, 3):
            piece = jnp.where(lax.rem(source + step, 4) == rank, landed[step - 1], piece)
        tops.append(piece[0:1])
        sums.append(piece[1:2])
    top = jnp.maximum(jnp.maximum(tops[0], tops[1]), jnp.maximum(tops[2], tops[3]))
    whole = sums[0] * jnp.exp(tops[0] - top)
    for source in (1, 2, 3):
        whole = whole + sums[source] * jnp.exp(tops[source] - top)
    logsum_ref[...] = top + jnp.log(whole)
    picked_ref[...] = jnp.zeros_like(picked_ref)

    def store(t):
        return pltpu.make_async_copy(
            slope_tiles.at[lax.rem(t, 2)], slopes_ref.at[:, over(t)], store_sem.at[lax.rem(t, 2)]
        )

    def back_unit(n):
        t, k = n // pieces, lax.rem(n, pieces)

        @pl.when(k == 0)
        def _():
            turn(t)
            total[...] = jnp.zeros_like(total)

            @pl.when(t >= 2)
            def _():
                store(t - 2).wait()

        lines = table_rows(k)
        logits = jnp.dot(lines, turned[...], preferred_element_type=jnp.float32)
        row = lax.broadcasted_iota(jnp.int32, logits.shape, 0)
        base = k * tile
        hits = jnp.where(row == wanted_ref[0:1, over(t)] - base, weight_ref[0:1, over(t)], 0.0)
        hits = hits + jnp.where(
            row == wanted_ref[1:2, over(t)] - base, weight_ref[1:2, over(t)], 0.0
        )
        picked_ref[:, over(t)] += jnp.sum(hits * logits, 0, keepdims=True)
        softmax = jnp.exp(logits - logsum_ref[:, over(t)])
        slope = (
            (weight_ref[2:3, over(t)] * softmax - hits) * weight_ref[3:4, over(t)]
        ).astype(jnp.bfloat16)
        slope_tiles[lax.rem(t, 2), pl.ds(pl.multiple_of(base, tile), tile)] = slope
        total[...] += lax.dot_general(
            slope, lines, (((0,), (0,)), ((), ())), preferred_element_type=jnp.float32
        )

        @pl.when(k == pieces - 1)
        def _():
            store(t).start()

    @pl.when(jnp.logical_not(inner))
    def _():
        def unit(n):
            back_unit(n)

            @pl.when(lax.rem(n, pieces) == pieces - 1)
            def _():
                first = (n // pieces) * group

                def push(c):
                    stage[first + c] = total[span(c)].astype(jnp.bfloat16)
                    to_inner(first + c).start()

                repeat(0, group, push)

        repeat(0, units, unit)

        def finish(i):
            to_end(grad_low_ref, i).wait_recv()
            to_inner(i).wait_send()

        repeat(0, count, finish)

    @pl.when(inner)
    def _():
        def settle(j):
            to_middle(j).wait_recv()
            upstream = stage[j].astype(jnp.float32) + from_mid[j].astype(jnp.float32)
            grad_two, gain_part = norm_back_rows(grad_ref[span(j)], gain_ref[...], upstream)
            grad_ref[span(j)] = grad_two
            gain_grad[...] += gain_part
            grad_low_ref[span(j)] = grad_two.astype(jnp.bfloat16)
            to_end(grad_low_ref, j).start()

        def exchange(i):
            to_inner(i).wait_recv()
            stage[i] = (own[span(i)] + from_end[i].astype(jnp.float32)).astype(jnp.bfloat16)
            to_middle(i).start()

            @pl.when(i >= line_lag)
            def _():
                settle(i - line_lag)

        def unit(n):
            back_unit(n)
            t, k = n // pieces, lax.rem(n, pieces)

            @pl.when(k == pieces - 1)
            def _():
                own[over(t)] = total[...]

            @pl.when((t >= 1) & (k >= pieces - group))
            def _():
                exchange((t - 1) * group + k - (pieces - group))

        repeat(0, units, unit)
        repeat(count - group, count, exchange)
        repeat(count - line_lag, count, settle)

        def drain(i):
            to_middle(i).wait_send()
            to_end(grad_low_ref, i).wait_send()

        repeat(0, count, drain)

    store(tiles - 2).wait()
    store(tiles - 1).wait()


def head_line(part, stream, gain, weights, wanted, weight_rows, vocab, collective_id):
    tokens, width = part.shape
    rows, columns = 64, 256
    count = tokens // rows
    chunks = pltpu.VMEM((count, rows, width), jnp.bfloat16)
    rows_low = jax.ShapeDtypeStruct((tokens, width), jnp.bfloat16)
    along = jax.ShapeDtypeStruct((1, tokens), jnp.float32)
    line_sems = pltpu.SemaphoreType.DMA((count,))
    return pl.pallas_call(
        functools.partial(head_line_kernel, vocab_tile(vocab)),
        out_shape=[
            rows_low,
            rows_low,
            jax.ShapeDtypeStruct((tokens, width), jnp.float32),
            jax.ShapeDtypeStruct((1, width), jnp.float32),
            along,
            along,
            jax.ShapeDtypeStruct((vocab, tokens), jnp.bfloat16),
        ],
        in_specs=[whole_vmem] * 3 + [whole_any] + [whole_vmem] * 2,
        out_specs=[whole_vmem] * 6 + [whole_any],
        scratch_shapes=[
            pltpu.VMEM((vocab, width), jnp.bfloat16),
            chunks,
            chunks,
            chunks,
            pltpu.VMEM((tokens, width), jnp.float32),
            pltpu.VMEM((width, columns), jnp.bfloat16),
            pltpu.VMEM((2, tokens), jnp.float32),
            pltpu.VMEM((3, 2, tokens), jnp.float32),
            pltpu.VMEM((2, vocab, columns), jnp.bfloat16),
            pltpu.VMEM((columns, width), jnp.float32),
            pltpu.SemaphoreType.DMA,
        ]
        + [line_sems] * 5
        + [pltpu.SemaphoreType.DMA((3,))] * 2
        + [pltpu.SemaphoreType.DMA((2,))],
        compiler_params=pltpu.CompilerParams(
            collective_id=collective_id, has_side_effects=True, vmem_limit_bytes=62 << 20
        ),
    )(part, stream, gain, weights, wanted, weight_rows)


def weight_grads_kernel(
    tile_units, tiles, place_ref, slope_ref, rows_ref, ids_ref, zero_ref, joint_ref, normed_ref,
    attended_ref, grad_ref, out_ref, made, sem,
):
    step = pl.program_id(0)
    unit_rows = out_ref.shape[1]
    buffer = lax.rem(step, 2)
    last_units = joint_ref.shape[0] // unit_rows + attended_ref.shape[0] // unit_rows

    def settle(which, count):
        pltpu.make_async_copy(
            made.at[which, pl.ds(0, count)], made.at[which, pl.ds(0, count)], sem.at[which]
        ).wait()

    def send(first, count):
        def push(u, carry):
            pltpu.make_async_copy(
                made.at[buffer, u], out_ref.at[place_ref[first + u]], sem.at[buffer]
            ).start()
            return carry

        lax.fori_loop(0, count, push, 0)

    @pl.when(step >= 2)
    def _():
        settle(buffer, tile_units)

    @pl.when(step < tiles)
    def _():
        row = lax.broadcasted_iota(jnp.int32, slope_ref.shape, 0)
        seen = jnp.where(row == ids_ref[...] - step * slope_ref.shape[0], 1.0, 0.0).astype(jnp.bfloat16)
        made[buffer] = (
            jnp.dot(slope_ref[...], rows_ref[...], preferred_element_type=jnp.float32)
            + jnp.dot(seen, zero_ref[...], preferred_element_type=jnp.float32)
        ).astype(jnp.bfloat16).reshape(tile_units, unit_rows, -1)
        send(step * tile_units, tile_units)

    @pl.when(step == tiles)
    def _():
        joint_units = joint_ref.shape[0] // unit_rows
        made[buffer, pl.ds(0, joint_units)] = jnp.dot(
            joint_ref[...], normed_ref[...], preferred_element_type=jnp.float32
        ).astype(jnp.bfloat16).reshape(joint_units, unit_rows, -1)
        made[buffer, pl.ds(joint_units, last_units - joint_units)] = jnp.dot(
            attended_ref[...], grad_ref[...], preferred_element_type=jnp.float32
        ).astype(jnp.bfloat16).reshape(last_units - joint_units, unit_rows, -1)
        send(tiles * tile_units, last_units)
        settle(1 - buffer, tile_units)
        settle(buffer, last_units)


def weight_grads(place, slots, unit_rows, slope, rows, ids, zero, joint, normed, attended, grad):
    vocab, tokens = slope.shape
    width = rows.shape[1]
    tile = vocab_tile(vocab)
    tiles = vocab // tile
    fixed = lambda k: (0, 0)
    whole = lambda x: pl.BlockSpec(x.shape, fixed)
    return pl.pallas_call(
        functools.partial(weight_grads_kernel, tile // unit_rows, tiles),
        grid=(tiles + 1,),
        out_shape=jax.ShapeDtypeStruct((slots, unit_rows, width), jnp.bfloat16),
        in_specs=[
            pl.BlockSpec(memory_space=pltpu.SMEM),
            pl.BlockSpec((tile, tokens), lambda k: (jnp.minimum(k, tiles - 1), 0)),
        ]
        + [whole(x) for x in (rows, ids, zero, joint, normed, attended, grad)],
        out_specs=whole_any,
        scratch_shapes=[
            pltpu.VMEM((2, tile // unit_rows, unit_rows, width), jnp.bfloat16),
            pltpu.SemaphoreType.DMA((2,)),
        ],
        compiler_params=pltpu.CompilerParams(vmem_limit_bytes=60 << 20),
    )(place, slope, rows, ids, zero, joint, normed, attended, grad)


def adam_update(weight, moment_one, moment_two, gradient, step_rate, decay_factor):
    moment_new = beta_first * moment_one + (1.0 - beta_first) * gradient
    square_new = beta_second * moment_two + (1.0 - beta_second) * gradient * gradient
    moment_hat = moment_new / (1.0 - beta_first**STEP)
    square_hat = square_new / (1.0 - beta_second**STEP)
    weight_new = weight - step_rate * (
        moment_hat / (jnp.sqrt(square_hat) + adam_epsilon) + decay_factor * weight
    )
    return (weight_new, moment_new, square_new)


def norm_forward(values, gain_row):
    return values * inverse_rms(values) * gain_row


def slot_tables(owner_ids, owners, most_units):
    unit_count = owner_ids.shape[0]
    unit_index = jnp.arange(unit_count, dtype=jnp.int32)
    earlier = (owner_ids[None, :] == owner_ids[:, None]) & (
        unit_index[None, :] < unit_index[:, None]
    )
    unit_rank = jnp.sum(earlier.astype(jnp.int32), 1)
    placed = (owner_ids[None, None, :] == jnp.arange(owners, dtype=jnp.int32)[:, None, None]) & (
        unit_rank[None, None, :] == jnp.arange(most_units, dtype=jnp.int32)[None, :, None]
    )
    slot_filled = jnp.any(placed, 2)
    slot_unit = jnp.sum(jnp.where(placed, unit_index[None, None, :], 0), 2)
    return (unit_rank, slot_unit, slot_filled)


def unit_rates(unit_ids, table_units, query_units, value_units):
    return jnp.where(
        unit_ids < table_units,
        rate_table,
        jnp.where(
            unit_ids < query_units,
            rate_query,
            jnp.where(unit_ids < value_units, rate_values, rate_project),
        ),
    )


def pair_slots(route_pairs, priorities, experts, capacity):
    tokens_here = priorities.shape[0]
    pair_expert = route_pairs.T.reshape(-1)
    pair_key = (
        jnp.arange(2, dtype=jnp.int32)[:, None] * tokens_here + priorities[None, :]
    ).reshape(-1)
    before = (pair_expert[None, :] == pair_expert[:, None]) & (
        pair_key[None, :] < pair_key[:, None]
    )
    pair_rank = jnp.sum(before.astype(jnp.int32), 1)
    pair_kept = pair_rank < capacity
    pair_dest = pair_expert * capacity + jnp.minimum(pair_rank, capacity - 1)
    return (pair_kept, pair_dest)


def gelu_tanh(values):
    return jax.nn.gelu(values, approximate=True)


def gelu_slope(values):
    root = math.sqrt(2.0 / math.pi)
    bent = jnp.tanh(root * (values + 0.044715 * values * values * values))
    return 0.5 * (1.0 + bent) + 0.5 * values * (1.0 - bent * bent) * root * (
        1.0 + 3.0 * 0.044715 * values * values
    )


def plane_peer(step):
    chip, core = lax.axis_index("dp"), lax.axis_index("ctx")
    row = lax.rem(chip // 2 + step // 4, 2)
    column = lax.rem(lax.rem(chip, 2) + lax.rem(step // 2, 2), 2)
    place = {"dp": row * 2 + column, "ctx": lax.rem(core + lax.rem(step, 2), 2)}
    return place, place["dp"] * 2 + place["ctx"]


def greet_plane():
    barrier = pltpu.get_barrier_semaphore()
    for step in range(1, 8):
        place, _ = plane_peer(step)
        pl.semaphore_signal(barrier, inc=1, device_id=place, device_id_type=MESH_ID)
    pl.semaphore_wait(barrier, 7)


def plane_copy(source, target, send_sem, recv_sem, step):
    place, _ = plane_peer(step)
    return pltpu.make_async_remote_copy(
        src_ref=source.at[step],
        dst_ref=target.at[step],
        send_sem=send_sem.at[step],
        recv_sem=recv_sem.at[step],
        device_id=place,
        device_id_type=MESH_ID,
    )


def slot_hits(dest_rows, expert, capacity, tokens):
    slot = lax.broadcasted_iota(jnp.int32, (capacity, tokens), 0) + expert * capacity
    return (slot == dest_rows[0:1, :]) | (slot == dest_rows[1:2, :])


def token_hits(dest_columns, expert, capacity, tokens):
    slot = lax.broadcasted_iota(jnp.int32, (tokens, capacity), 1) + expert * capacity
    hit = (slot == dest_columns[:, 0:1]) | (slot == dest_columns[:, 1:2])
    return jnp.where(hit, 1.0, 0.0).astype(jnp.bfloat16)


def gate_of(routes, gates, expert, axis):
    pick = (lambda a, k: a[k : k + 1, :]) if axis == 0 else (lambda a, k: a[:, k : k + 1])
    return jnp.where(pick(routes, 0) == expert, pick(gates, 0), 0.0) + jnp.where(
        pick(routes, 1) == expert, pick(gates, 1), 0.0
    )


def arrival(i):
    return jnp.where(i < 2, i, 9 - i)


def experts_kernel(
    rows_ref, dest_rows, dest_columns, gates, routes, inner_full, outer_full, counts_ref,
    mix_ref, arrived, returned, totals_ref,
    inner_ref, outer_ref, outgoing, results, counts, send_one, recv_one, send_two, recv_two, send_count, recv_count,
):
    capacity = arrived.shape[1]
    tokens = rows_ref.shape[0]
    greet_plane()
    counts[0] = counts_ref[...]

    def send_counts(step, carry):
        place, _ = plane_peer(step)
        pltpu.make_async_remote_copy(
            src_ref=counts_ref,
            dst_ref=counts.at[step],
            send_sem=send_count.at[step],
            recv_sem=recv_count.at[step],
            device_id=place,
            device_id_type=MESH_ID,
        ).start()
        return carry

    def dispatch(i, carry):
        step = 7 - i
        _, expert = plane_peer(step)
        hit = jnp.where(slot_hits(dest_rows, expert, capacity, tokens), 1.0, 0.0).astype(jnp.bfloat16)
        rows = jnp.dot(hit, rows_ref[...], preferred_element_type=jnp.float32).astype(jnp.bfloat16)

        @pl.when(step > 0)
        def _():
            outgoing[step] = rows
            plane_copy(outgoing, arrived, send_one, recv_one, step).start()

        @pl.when(step == 0)
        def _():
            arrived[0] = rows

        return carry

    def work(i, carry):
        step = arrival(i)

        @pl.when(step > 0)
        def _():
            plane_copy(outgoing, arrived, send_one, recv_one, step).wait_recv()

        before = jnp.dot(arrived[step], inner_ref[...], preferred_element_type=jnp.float32)
        active = gelu_tanh(before).astype(jnp.bfloat16)
        part = jnp.dot(active, outer_ref[...], preferred_element_type=jnp.float32).astype(jnp.bfloat16)

        @pl.when(step > 0)
        def _():
            results[step] = part
            plane_copy(results, returned, send_two, recv_two, step).start()

        @pl.when(step == 0)
        def _():
            returned[0] = part

        return carry

    def combine(i, carry):
        step = arrival(i)
        _, expert = plane_peer(step)
        hit = token_hits(dest_columns, expert, capacity, tokens)
        gate = gate_of(routes, gates, expert, 1)

        @pl.when(step > 0)
        def _():
            plane_copy(results, returned, send_two, recv_two, step).wait_recv()

        part = gate * jnp.dot(hit, returned[step], preferred_element_type=jnp.float32)

        @pl.when(i == 0)
        def _():
            mix_ref[...] = part

        @pl.when(i > 0)
        def _():
            mix_ref[...] += part

        return carry

    def finish(step, carry):
        plane_copy(outgoing, arrived, send_one, recv_one, step).wait_send()
        plane_copy(results, returned, send_two, recv_two, step).wait_send()
        place, _ = plane_peer(step)
        pltpu.make_async_remote_copy(
            src_ref=counts_ref,
            dst_ref=counts.at[step],
            send_sem=send_count.at[step],
            recv_sem=recv_count.at[step],
            device_id=place,
            device_id_type=MESH_ID,
        ).wait()
        return carry

    lax.fori_loop(0, 8, dispatch, 0)
    lax.fori_loop(1, 8, send_counts, 0)
    inner_ref[...] = inner_full[...].astype(jnp.bfloat16)
    outer_ref[...] = outer_full[...].astype(jnp.bfloat16)
    lax.fori_loop(0, 8, work, 0)
    lax.fori_loop(0, 8, combine, 0)
    lax.fori_loop(1, 8, finish, 0)
    totals_ref[...] = jnp.sum(counts[...], 0)


def experts_forward(rows, dest, gates, routes, inner, outer, counts, capacity, collective_id):
    tokens, width = rows.shape
    buffer = pltpu.VMEM((8, capacity, width), jnp.bfloat16)
    return pl.pallas_call(
        experts_kernel,
        out_shape=[
            jax.ShapeDtypeStruct((tokens, width), jnp.float32),
            jax.ShapeDtypeStruct((8, capacity, width), jnp.bfloat16),
            jax.ShapeDtypeStruct((8, capacity, width), jnp.bfloat16),
            jax.ShapeDtypeStruct(counts.shape, jnp.float32),
        ],
        in_specs=[whole_vmem] * 8,
        out_specs=[whole_vmem] * 4,
        scratch_shapes=[pltpu.VMEM(w.shape, jnp.bfloat16) for w in (inner, outer)]
        + [buffer, buffer, pltpu.VMEM((8,) + counts.shape, jnp.float32)]
        + [pltpu.SemaphoreType.DMA((8,))] * 6,
        compiler_params=pltpu.CompilerParams(
            collective_id=collective_id, has_side_effects=True, vmem_limit_bytes=60 << 20
        ),
    )(rows, dest, dest.T, gates, routes, inner, outer, counts)


def experts_back_kernel(
    rows_ref, dest_rows, dest_columns, gates, routes, returned, arrived, *refs
):
    inner_full, outer_full, grad_ref, gate_ref, inner_grad, outer_grad, inner_ref, outer_ref = refs[:8]
    outgoing, landed, results, landed_two, active, slopes = refs[8:14]
    send_one, recv_one, send_two, recv_two = refs[14:]
    capacity = arrived.shape[1]
    tokens = rows_ref.shape[0]
    greet_plane()
    gate_ref[...] = jnp.zeros_like(gate_ref)

    def dispatch(i, carry):
        step = 7 - i
        _, expert = plane_peer(step)
        hit = slot_hits(dest_rows, expert, capacity, tokens)
        rows = jnp.dot(
            jnp.where(hit, 1.0, 0.0).astype(jnp.bfloat16), rows_ref[...], preferred_element_type=jnp.float32
        )
        scale = jnp.sum(jnp.where(hit, gate_of(routes, gates, expert, 0), 0.0), 1, keepdims=True)
        sent = (rows * scale).astype(jnp.bfloat16)

        @pl.when(step > 0)
        def _():
            outgoing[step] = sent
            plane_copy(outgoing, landed, send_one, recv_one, step).start()

        @pl.when(step == 0)
        def _():
            landed[0] = sent

        dots = jnp.sum(rows * returned[step].astype(jnp.float32), 1, keepdims=True)
        part = jnp.sum(jnp.where(hit, dots, 0.0), 0, keepdims=True)
        for k in range(2):
            gate_ref[k : k + 1, :] += jnp.where(routes[k : k + 1, :] == expert, part, 0.0)
        return carry

    def work(i, carry):
        step = arrival(i)

        @pl.when(step > 0)
        def _():
            plane_copy(outgoing, landed, send_one, recv_one, step).wait_recv()

        grad_active = lax.dot_general(
            landed[step], outer_ref[...], (((1,), (1,)), ((), ())), preferred_element_type=jnp.float32
        )
        before = jnp.dot(arrived[step], inner_ref[...], preferred_element_type=jnp.float32)
        slope = (grad_active * gelu_slope(before)).astype(jnp.bfloat16)
        back = lax.dot_general(
            slope, inner_ref[...], (((1,), (1,)), ((), ())), preferred_element_type=jnp.float32
        ).astype(jnp.bfloat16)

        @pl.when(step > 0)
        def _():
            results[step] = back
            plane_copy(results, landed_two, send_two, recv_two, step).start()

        @pl.when(step == 0)
        def _():
            landed_two[0] = back

        slopes[step] = slope
        active[step] = gelu_tanh(before).astype(jnp.bfloat16)
        return carry

    def weigh(step, carry):
        outer_part = lax.dot_general(
            active[step], landed[step], (((0,), (0,)), ((), ())), preferred_element_type=jnp.float32
        )
        inner_part = lax.dot_general(
            arrived[step], slopes[step], (((0,), (0,)), ((), ())), preferred_element_type=jnp.float32
        )

        @pl.when(step == 0)
        def _():
            inner_grad[...] = inner_part
            outer_grad[...] = outer_part

        @pl.when(step > 0)
        def _():
            inner_grad[...] += inner_part
            outer_grad[...] += outer_part

        return carry

    def combine(i, carry):
        step = arrival(i)
        _, expert = plane_peer(step)
        hit = token_hits(dest_columns, expert, capacity, tokens)

        @pl.when(step > 0)
        def _():
            plane_copy(results, landed_two, send_two, recv_two, step).wait_recv()

        part = jnp.dot(hit, landed_two[step], preferred_element_type=jnp.float32)

        @pl.when(i == 0)
        def _():
            grad_ref[...] = part

        @pl.when(i > 0)
        def _():
            grad_ref[...] += part

        return carry

    def finish(step, carry):
        plane_copy(outgoing, landed, send_one, recv_one, step).wait_send()
        plane_copy(results, landed_two, send_two, recv_two, step).wait_send()
        return carry

    lax.fori_loop(0, 8, dispatch, 0)
    inner_ref[...] = inner_full[...].astype(jnp.bfloat16)
    outer_ref[...] = outer_full[...].astype(jnp.bfloat16)
    lax.fori_loop(0, 8, work, 0)
    lax.fori_loop(0, 8, weigh, 0)
    lax.fori_loop(0, 8, combine, 0)
    lax.fori_loop(1, 8, finish, 0)


def experts_backward(rows, dest, gates, routes, returned, arrived, inner, outer, collective_id):
    tokens, width = rows.shape
    capacity = arrived.shape[1]
    inside = inner.shape[1]
    buffer = pltpu.VMEM((8, capacity, width), jnp.bfloat16)
    inside_buffer = pltpu.VMEM((8, capacity, inside), jnp.bfloat16)
    return pl.pallas_call(
        experts_back_kernel,
        out_shape=[
            jax.ShapeDtypeStruct((tokens, width), jnp.float32),
            jax.ShapeDtypeStruct((2, tokens), jnp.float32),
            jax.ShapeDtypeStruct((width, inside), jnp.float32),
            jax.ShapeDtypeStruct((inside, width), jnp.float32),
        ],
        in_specs=[whole_vmem] * 9,
        out_specs=[whole_vmem] * 4,
        scratch_shapes=[pltpu.VMEM(w.shape, jnp.bfloat16) for w in (inner, outer)]
        + [buffer] * 4
        + [inside_buffer] * 2
        + [pltpu.SemaphoreType.DMA((8,))] * 4,
        compiler_params=pltpu.CompilerParams(
            collective_id=collective_id, has_side_effects=True, vmem_limit_bytes=60 << 20
        ),
    )(rows, dest, dest.T, gates, routes, returned, arrived, inner, outer)


def own_units_kernel(
    chunks, units_of, slopes_ref, rows_ref, ids_ref, zero_ref, joint_ref, normed_ref, attended_ref,
    grad_ref, small_ref, grads_ref, small_out, *refs
):
    slopes, late, mixed, made, passing, own, other, relay, landed, small_landed, ready = refs[:11]
    other_send, other_recv, relay_send, relay_recv, landed_send, landed_recv = refs[11:17]
    small_send, small_recv, load_sem, store_sem = refs[17:]
    chip, core = lax.axis_index("dp"), lax.axis_index("ctx")
    beside = chip + 1 - 2 * lax.rem(chip, 2)
    across = lax.rem(chip + 2, 4)
    opposite = across + 1 - 2 * lax.rem(across, 2)
    places = (opposite, beside, across, chip)
    slots, unit_rows = own.shape[1:3]
    table_units = slopes.shape[0]
    tokens = rows_ref.shape[0]
    size = slots // chunks
    split = (chunks + 1) // 2
    load = pltpu.make_async_copy(slopes_ref, slopes, load_sem)
    load.start()
    greet_plane()

    def repeat(first, last, body):
        def step(i, carry):
            body(i)
            return carry

        lax.fori_loop(first, last, step, 0)

    def span(q):
        return pl.ds(q * size, size)

    def remote(source, target, send, recv, place):
        return pltpu.make_async_remote_copy(
            src_ref=source,
            dst_ref=target,
            send_sem=send,
            recv_sem=recv,
            device_id=place,
            device_id_type=MESH_ID,
        )

    def pass_over(k, q):
        return remote(
            passing.at[k % 2, span(q)],
            other.at[k, span(q)],
            other_send.at[k, q],
            other_recv.at[k, q],
            {"ctx": 1 - core},
        )

    def to_relay(q, place):
        return remote(own.at[0, span(q)], relay.at[span(q)], relay_send.at[q], relay_recv.at[q], {"dp": place})

    def to_owner(k, q):
        return remote(
            own.at[k, span(q)],
            landed.at[k - 1, span(q)],
            landed_send.at[k - 1, q],
            landed_recv.at[k - 1, q],
            {"dp": places[k]},
        )

    def small_copy(step):
        place, _ = plane_peer(step)
        return remote(
            small_ref, small_landed.at[chip * 2 + core], small_send.at[step], small_recv.at[step], place
        )

    joint_units = joint_ref.shape[0] // unit_rows
    late[pl.ds(0, joint_units)] = jnp.dot(
        joint_ref[...], normed_ref[...], preferred_element_type=jnp.float32
    ).reshape(joint_units, unit_rows, -1)
    last_units = attended_ref.shape[0] // unit_rows
    late[pl.ds(joint_units, last_units)] = jnp.dot(
        attended_ref[...], grad_ref[...], preferred_element_type=jnp.float32
    ).reshape(last_units, unit_rows, -1)
    load.wait()
    group = made.shape[0] // unit_rows

    def form(owner, target):
        def some(g):
            first = owner * slots + g * group

            def fill(s):
                unit = units_of[first + s]
                lines = pl.ds(pl.multiple_of(s * unit_rows, unit_rows), unit_rows)
                mixed[lines, :tokens] = slopes[jnp.minimum(unit, table_units - 1)]
                row = lax.broadcasted_iota(jnp.int32, (unit_rows, tokens), 0) + unit * unit_rows
                mixed[lines, tokens:] = jnp.where(row == ids_ref[...], 1.0, 0.0).astype(jnp.bfloat16)

            repeat(0, group, fill)
            made[...] = jnp.dot(
                mixed[:, :tokens], rows_ref[...], preferred_element_type=jnp.float32
            ) + jnp.dot(mixed[:, tokens:], zero_ref[...], preferred_element_type=jnp.float32)

            def put(s):
                unit = units_of[first + s]
                table_piece = made[pl.ds(pl.multiple_of(s * unit_rows, unit_rows), unit_rows)]
                late_piece = late[jnp.clip(unit - table_units, 0, late.shape[0] - 1)]
                marks = jnp.zeros(table_piece.shape, jnp.int32) + unit
                piece = jnp.where(marks < table_units, table_piece, late_piece)
                target[g * group + s] = piece.astype(jnp.bfloat16)

            repeat(0, group, put)

        repeat(0, slots // group, some)

    def joined(k, q):
        pass_over(k, q).wait_recv()
        return own[k, span(q)].astype(jnp.float32) + other[k, span(q)].astype(jnp.float32)

    def first_leg(place):
        def leg(q):
            own[0, span(q)] = joined(0, q).astype(jnp.bfloat16)
            to_relay(q, place).start()

        return leg

    def direct(k):
        def leg(q):
            own[k, span(q)] = joined(k, q).astype(jnp.bfloat16)
            to_owner(k, q).start()

        return leg

    def relayed(k, place):
        def leg(q):
            to_relay(q, place).wait_recv()
            total = joined(k, q) + relay[span(q)].astype(jnp.float32)
            own[k, span(q)] = total.astype(jnp.bfloat16)
            to_owner(k, q).start()

        return leg

    def form_pair(k):
        if k >= 2:
            repeat(0, chunks, lambda q: pass_over(k - 2, q).wait_send())
        form(places[k] * 2 + 1 - core, passing.at[k % 2])
        repeat(0, chunks, lambda q: pass_over(k, q).start())
        form(places[k] * 2 + core, own.at[k])

    form_pair(0)
    repeat(0, split, first_leg(beside))
    repeat(split, chunks, first_leg(across))
    repeat(1, 8, lambda step: small_copy(step).start())
    small_landed[chip * 2 + core] = small_ref[...]
    form_pair(1)
    repeat(0, split, direct(1))
    form_pair(2)
    repeat(split, chunks, direct(2))
    repeat(0, split, relayed(2, beside))
    repeat(split, chunks, relayed(1, across))
    form_pair(3)

    def store(q):
        return pltpu.make_async_copy(
            ready.at[lax.rem(q, 2)], grads_ref.at[span(q)], store_sem.at[lax.rem(q, 2)]
        )

    def keep(q):
        total = joined(3, q)
        to_owner(1, q).wait_recv()
        to_owner(2, q).wait_recv()

        @pl.when(q >= 2)
        def _():
            store(q - 2).wait()

        ready[lax.rem(q, 2)] = (
            total + landed[0, span(q)].astype(jnp.float32) + landed[1, span(q)].astype(jnp.float32)
        )
        store(q).start()

    repeat(0, chunks, keep)

    def finish(q):
        for k in (2, 3):
            pass_over(k, q).wait_send()
        to_owner(1, q).wait_send()
        to_owner(2, q).wait_send()

    repeat(0, chunks, finish)
    repeat(0, split, lambda q: to_relay(q, beside).wait_send())
    repeat(split, chunks, lambda q: to_relay(q, across).wait_send())
    repeat(1, 8, lambda step: small_copy(step).wait())
    total = small_landed[0]
    for source in range(1, 8):
        total = total + small_landed[source]
    small_out[...] = total
    for q in range(max(0, chunks - 2), chunks):
        store(q).wait()


def own_units(units_of, slots, unit_rows, slopes, rows, ids, zero, joint, normed, attended, grad, small, collective_id):
    tokens, width = rows.shape
    unit = (unit_rows, width)
    chunks = max(k for k in range(1, 8) if slots % k == 0)
    group = max(k for k in range(1, 8) if slots % k == 0)
    late = (joint.shape[0] + attended.shape[0]) // unit_rows
    slopes = slopes.reshape(-1, unit_rows, tokens)
    return pl.pallas_call(
        functools.partial(own_units_kernel, chunks),
        out_shape=[
            jax.ShapeDtypeStruct((slots,) + unit, jnp.float32),
            jax.ShapeDtypeStruct(small.shape, jnp.float32),
        ],
        in_specs=[pl.BlockSpec(memory_space=pltpu.SMEM), whole_any] + [whole_vmem] * 8,
        out_specs=[whole_any, whole_vmem],
        scratch_shapes=[
            pltpu.VMEM(slopes.shape, jnp.bfloat16),
            pltpu.VMEM((late,) + unit, jnp.float32),
            pltpu.VMEM((group * unit_rows, 2 * tokens), jnp.bfloat16),
            pltpu.VMEM((group * unit_rows, width), jnp.float32),
            pltpu.VMEM((2, slots) + unit, jnp.bfloat16),
            pltpu.VMEM((4, slots) + unit, jnp.bfloat16),
            pltpu.VMEM((4, slots) + unit, jnp.bfloat16),
            pltpu.VMEM((slots,) + unit, jnp.bfloat16),
            pltpu.VMEM((2, slots) + unit, jnp.bfloat16),
            pltpu.VMEM((8,) + small.shape, jnp.float32),
            pltpu.VMEM((2, slots // chunks) + unit, jnp.float32),
            pltpu.SemaphoreType.DMA((4, chunks)),
            pltpu.SemaphoreType.DMA((4, chunks)),
            pltpu.SemaphoreType.DMA((chunks,)),
            pltpu.SemaphoreType.DMA((chunks,)),
            pltpu.SemaphoreType.DMA((2, chunks)),
            pltpu.SemaphoreType.DMA((2, chunks)),
            pltpu.SemaphoreType.DMA((8,)),
            pltpu.SemaphoreType.DMA((8,)),
            pltpu.SemaphoreType.DMA,
            pltpu.SemaphoreType.DMA((2,)),
        ],
        compiler_params=pltpu.CompilerParams(
            collective_id=collective_id, has_side_effects=True, vmem_limit_bytes=63 << 20
        ),
    )(units_of, slopes, rows, ids, zero, joint, normed, attended, grad, small)


def to_plane(buffer):
    return lax.all_to_all(buffer, ("dp", "ctx"), split_axis=0, concat_axis=0, tiled=True)


def plain_hits(dest, experts, capacity):
    slots = lax.broadcasted_iota(jnp.int32, (experts * capacity, dest.shape[1]), 0)
    return [slots == dest[k : k + 1] for k in range(2)]


def plain_forward(rows, dest, gates, inner, outer, owners, capacity):
    width = rows.shape[1]
    hits = plain_hits(dest, owners, capacity)
    both = (hits[0] | hits[1]).astype(jnp.bfloat16)
    sent = jnp.dot(both, rows, preferred_element_type=jnp.float32).astype(jnp.bfloat16)
    arrived = to_plane(sent.reshape(owners, capacity, width))
    hidden = jnp.einsum("ocd,df->ocf", arrived, inner, preferred_element_type=jnp.float32)
    active = gelu_tanh(hidden).astype(jnp.bfloat16)
    part = jnp.einsum("ocf,fd->ocd", active, outer, preferred_element_type=jnp.float32)
    returned = to_plane(part.astype(jnp.bfloat16))
    flat = returned.reshape(owners * capacity, width)
    mix = sum(
        gates[:, k : k + 1]
        * lax.dot_general(
            hits[k].astype(jnp.bfloat16),
            flat,
            (((0,), (0,)), ((), ())),
            preferred_element_type=jnp.float32,
        )
        for k in range(2)
    )
    return (mix, arrived, returned)


def plain_backward(rows, dest, gates, returned, arrived, inner, outer):
    owners, capacity, width = arrived.shape
    hits = plain_hits(dest, owners, capacity)
    both = (hits[0] | hits[1]).astype(jnp.bfloat16)
    slot_scale = jnp.sum(
        jnp.where(hits[0], gates[0:1], 0.0) + jnp.where(hits[1], gates[1:2], 0.0), 1, keepdims=True
    )
    slot_grads = jnp.dot(both, rows, preferred_element_type=jnp.float32)
    sent = (slot_grads * slot_scale).astype(jnp.bfloat16)
    flat = returned.reshape(owners * capacity, width)
    dots = jnp.sum(slot_grads * flat.astype(jnp.float32), 1, keepdims=True)
    gate_part = jnp.concatenate(
        [jnp.sum(jnp.where(hit, dots, 0.0), 0, keepdims=True) for hit in hits], 0
    )
    landed = to_plane(sent.reshape(owners, capacity, width))
    grad_active = jnp.einsum("ocd,fd->ocf", landed, outer, preferred_element_type=jnp.float32)
    hidden = jnp.einsum("ocd,df->ocf", arrived, inner, preferred_element_type=jnp.float32)
    active = gelu_tanh(hidden).astype(jnp.bfloat16)
    slope = (grad_active * gelu_slope(hidden)).astype(jnp.bfloat16)
    outer_grad = jnp.einsum("ocf,ocd->fd", active, landed, preferred_element_type=jnp.float32)
    inner_grad = jnp.einsum("ocd,ocf->df", arrived, slope, preferred_element_type=jnp.float32)
    back = jnp.einsum("ocf,df->ocd", slope, inner, preferred_element_type=jnp.float32)
    back = to_plane(back.astype(jnp.bfloat16)).reshape(owners * capacity, width)
    grad = lax.dot_general(
        both, back, (((0,), (0,)), ((), ())), preferred_element_type=jnp.float32
    )
    return (grad, gate_part, inner_grad, outer_grad)


def on_device(
    token_ids,
    targets,
    counted,
    routes,
    priority,
    owner_of,
    master,
    master_first,
    master_second,
    expert_in,
    expert_in_first,
    expert_in_second,
    expert_out,
    expert_out_first,
    expert_out_second,
    norm_gains,
    norm_gains_first,
    norm_gains_second,
    router,
    router_first,
    router_second,
    rel_bias,
    rel_bias_first,
    rel_bias_second,
):
    owners = lax.axis_size(("dp", "ctx"))
    tensor_ranks = lax.axis_size("tensor")
    my_owner = lax.axis_index(("dp", "ctx"))
    my_rank = lax.axis_index("tensor")
    my_context = lax.axis_index("ctx")
    sequences, half_length = token_ids.shape
    tokens_here = sequences * half_length
    most_units = master.shape[2]
    unit_rows = master.shape[3]
    model_width = master.shape[4]
    vocab_here = VOCAB // tensor_ranks
    heads_here = rel_bias.shape[0]
    head_size = model_width // (heads_here * tensor_ranks)
    hidden_here = heads_here * head_size
    experts = router.shape[1]
    capacity = (18 * tokens_here + 8 * experts - 1) // (8 * experts)
    table_units = vocab_here // unit_rows
    query_units = table_units + 2 * hidden_here // unit_rows
    value_units = table_units + 3 * hidden_here // unit_rows
    embed_scale = math.sqrt(model_width)
    owner_ids = owner_of[:, 0]
    on_square = lax.axis_size("dp") == 4 and lax.axis_size("ctx") == 2
    unit_rank, slot_unit, slot_filled = slot_tables(owner_ids, owners, most_units)
    counted_rows = counted.reshape(tokens_here, 2).T.astype(jnp.float32)
    loss_weights = counted_rows * jnp.array([[1.0], [ahead_weight]], jnp.float32)
    counts = jnp.zeros((8, 128), jnp.float32).at[0:2].set(jnp.sum(counted_rows, 1, keepdims=True))
    unit_slots = owner_ids * most_units + unit_rank
    route_pairs = routes.reshape(tokens_here, 2)
    pair_kept, pair_dest = pair_slots(route_pairs, priority[0], experts, capacity)
    dest = jnp.where(pair_kept, pair_dest, -1).reshape(2, tokens_here)
    unit_slots, dest = lax.optimization_barrier((unit_slots, dest))
    local_ids = token_ids.reshape(-1) - my_rank * vocab_here
    inside = (local_ids >= 0) & (local_ids < vocab_here)
    clipped_ids = jnp.clip(local_ids, 0, vocab_here - 1)
    unit_starts = jnp.sum(
        jnp.where(
            (clipped_ids // unit_rows)[None, :] == jnp.arange(unit_slots.shape[0])[:, None],
            unit_slots[:, None] * unit_rows,
            0,
        ),
        0,
    )
    slot_rows = unit_starts + clipped_ids % unit_rows
    if on_square:
        slot_rows = jnp.where(inside, slot_rows, -1)[:, None]
        weights_low, embedded = embed(unit_slots, master[0, 0], slot_rows, 11)
    else:
        master_low = master[0, 0].astype(jnp.bfloat16)
        gathered = lax.all_gather(master_low, ("dp", "ctx"), axis=0, tiled=True)
        looked = jnp.take(gathered.reshape(-1, model_width), slot_rows, axis=0)
        looked = jnp.where(inside[:, None], looked, 0)
        weights_low = pull_units([gathered], unit_slots)
        (embedded,) = sum_line(looked, [], [], keep_total, 1)
    weights_low = weights_low.reshape(-1, model_width)
    joint_low = weights_low[vocab_here : vocab_here + 3 * hidden_here]
    project_low = weights_low[vocab_here + 3 * hidden_here :]
    rolled = [project_low] + [
        lax.ppermute(project_low, "tensor", [(source, (source + step) % 4) for source in range(4)])
        for step in (1, 2, 3)
    ]
    gain_rows = [norm_gains[k : k + 1] for k in range(3)]
    stream_shape = jax.ShapeDtypeStruct((tokens_here, model_width), jnp.float32)
    gain_shape = jax.ShapeDtypeStruct((1, model_width), jnp.float32)
    stream_zero = embedded.astype(jnp.float32) * embed_scale
    first_normalized = norm_forward(stream_zero, norm_gains[0])
    normed_one_low = first_normalized.astype(jnp.bfloat16)
    joint = lax.dot_general(
        joint_low, normed_one_low, (((1,), (1,)), ((), ())), preferred_element_type=jnp.float32
    ).astype(jnp.bfloat16)
    pairs_before = passed_along(joint[hidden_here:], "ctx", 1)
    attended, logsum_rows = attention(rel_bias, joint, pairs_before, heads_here, head_size)
    (attended_all,) = gather_line([attended], 2)
    router_low = router.astype(jnp.bfloat16)
    stream_one, normed_two_low, gate_rows, gate_columns = middle(
        attended_all.reshape(model_width, tokens_here),
        rolled,
        embedded,
        gain_rows[1],
        router_low.T,
        route_pairs.T,
    )
    if on_square:
        moe_partial, arrived, returned, counts = experts_forward(
            normed_two_low, dest, gate_columns, route_pairs, expert_in[0], expert_out[0], counts, capacity, 8
        )
    else:
        inner_low, outer_low = expert_in[0].astype(jnp.bfloat16), expert_out[0].astype(jnp.bfloat16)
        moe_partial, arrived, returned = plain_forward(
            normed_two_low, dest, gate_columns, inner_low, outer_low, owners, capacity
        )
        counts = lax.psum(counts, ("dp", "ctx"))
    weight_total = counts[0, 0] + ahead_weight * counts[1, 0]
    local_targets = targets.reshape(tokens_here, 2).T - my_rank * vocab_here
    weight_rows = jnp.concatenate(
        [
            loss_weights,
            loss_weights[0:1] + loss_weights[1:2],
            jnp.broadcast_to(1.0 / weight_total, (1, tokens_here)),
        ],
        0,
    )
    head_low, grad_two_low, grad_two, gain_grad_three, logsum_vocab, target_sums, slopes = head_line(
        moe_partial, stream_one, gain_rows[2], weights_low, local_targets, weight_rows, vocab_here, 3
    )
    if on_square:
        moe_grad_part, gate_part, inner_grad, outer_grad = experts_backward(
            grad_two_low,
            dest,
            gate_rows,
            route_pairs.T,
            returned,
            arrived,
            expert_in[0],
            expert_out[0],
            9,
        )
    else:
        moe_grad_part, gate_part, inner_grad, outer_grad = plain_backward(
            grad_two_low, dest, gate_rows, returned, arrived, inner_low, outer_low
        )
    gate_part = jnp.concatenate([gate_part, target_sums, jnp.zeros_like(target_sums)], 0)
    gate_block = pltpu.VMEM((3, 4, tokens_here), jnp.float32)
    grad_one_low, grad_one, logit_grad, target_total, gain_grad_two = sum_line(
        moe_grad_part,
        [
            stream_one,
            gain_rows[1],
            grad_two,
            gate_part,
            gate_rows,
            route_pairs.T,
            router_low,
        ],
        [
            stream_shape,
            jax.ShapeDtypeStruct((experts, tokens_here), jnp.bfloat16),
            jax.ShapeDtypeStruct((1, tokens_here), jnp.float32),
            gain_shape,
        ],
        finish_expert_grad,
        5,
        prologue=start_router_grad,
        scratch=(gate_block, pltpu.SemaphoreType.DMA((3,)), pltpu.SemaphoreType.DMA((3,))),
        opening=send_gate_parts,
    )
    router_grad = jnp.dot(logit_grad, normed_two_low, preferred_element_type=jnp.float32)
    loss_local = jnp.sum(weight_rows[2:3] * logsum_vocab) - jnp.sum(target_total)
    query_grad, pair_grad, before_grad, bias_lines, *expert_states = attention_back(
        rel_bias,
        joint,
        pairs_before,
        logsum_rows,
        grad_one_low,
        project_low,
        (
            expert_in[0],
            expert_in_first[0],
            expert_in_second[0],
            inner_grad,
            expert_out[0],
            expert_out_first[0],
            expert_out_second[0],
            outer_grad,
        ),
        heads_here,
        head_size,
    )
    grad_after = passed_along(before_grad, "ctx", -1)
    pair_grad_low = (pair_grad + grad_after.astype(jnp.float32)).astype(jnp.bfloat16)
    joint_grad = jnp.concatenate([query_grad, pair_grad_low], 0)
    distances = 2 * (half_length // BLOCK)
    bias_grad = jnp.sum(bias_lines, 1).reshape(heads_here, distances)
    zero_grad_low, gain_grads = sum_line(
        lax.dot_general(
            joint_grad, joint_low, (((0,), (0,)), ((), ())), preferred_element_type=jnp.float32
        ),
        [embedded, gain_rows[0], grad_one, gain_grad_two, gain_grad_three],
        [jax.ShapeDtypeStruct((8, model_width), jnp.float32)],
        functools.partial(finish_input_grad, embed_scale),
        6,
        prologue=clear_gain,
        scratch=(pltpu.SemaphoreType.DMA, pltpu.SemaphoreType.DMA),
        ending=share_gains,
    )
    my_units = jnp.take(slot_unit, my_owner, axis=0)
    my_filled = jnp.take(slot_filled, my_owner, axis=0)[:, None, None]
    bias_row = jnp.concatenate([bias_grad.reshape(-1), loss_local[None]])
    bias_row = jnp.pad(bias_row, (0, model_width - bias_row.shape[0]))[None]
    small = jnp.concatenate([gain_grads[:3], router_grad, bias_row], 0)
    small = jnp.pad(small, ((0, -small.shape[0] % 8), (0, 0)))
    slot_rates = unit_rates(my_units, table_units, query_units, value_units)[:, None, None]
    states = (master[0, 0], master_first[0, 0], master_second[0, 0])
    grad_rows = (
        slopes,
        head_low,
        local_ids[None, :],
        zero_grad_low,
        joint_grad,
        normed_one_low,
        attended,
        grad_one_low,
    )
    if on_square:
        mine, small = own_units(slot_unit.reshape(-1), most_units, unit_rows, *grad_rows, small, 10)
    else:
        outgoing = weight_grads(unit_slots, owners * most_units, unit_rows, *grad_rows)
        mine = lax.psum_scatter(
            outgoing.astype(jnp.float32), ("dp", "ctx"), scatter_dimension=0, tiled=True
        )
        small = lax.psum(small, ("dp", "ctx"))
    states = adam_update(*states, jnp.where(my_filled, mine, 0.0), slot_rates, decay_rate)
    gains_grad = small[:3]
    router_grad = small[3 : 3 + experts].T
    bias_grad = small[3 + experts, : rel_bias.size].reshape(rel_bias.shape)
    loss_totals = jnp.stack([small[3 + experts, rel_bias.size], weight_total])
    gains_new, gains_first_new, gains_second_new = adam_update(
        norm_gains, norm_gains_first, norm_gains_second, gains_grad, rate_gains, 0.0
    )
    router_new, router_first_new, router_second_new = adam_update(
        router, router_first, router_second, router_grad, rate_router, decay_rate
    )
    biases_new, biases_first_new, biases_second_new = adam_update(
        rel_bias, rel_bias_first, rel_bias_second, bias_grad, rate_biases, 0.0
    )
    return (
        loss_totals,
        *(state[None, None] for state in states),
        *(state[None] for state in expert_states),
        gains_new,
        gains_first_new,
        gains_second_new,
        router_new,
        router_first_new,
        router_second_new,
        biases_new,
        biases_first_new,
        biases_second_new,
    )


def solution(mesh):
    in_specs = (
        P("dp", "ctx"),
        P("dp", "ctx", None),
        P("dp", "ctx", None),
        P("dp", "ctx", None),
        P(("dp", "ctx"), None),
        P(),
        P("tensor", ("dp", "ctx"), None, None, None),
        P("tensor", ("dp", "ctx"), None, None, None),
        P("tensor", ("dp", "ctx"), None, None, None),
        P(("dp", "ctx"), None, "tensor"),
        P(("dp", "ctx"), None, "tensor"),
        P(("dp", "ctx"), None, "tensor"),
        P(("dp", "ctx"), "tensor", None),
        P(("dp", "ctx"), "tensor", None),
        P(("dp", "ctx"), "tensor", None),
        P(),
        P(),
        P(),
        P(),
        P(),
        P(),
        P("tensor", None),
        P("tensor", None),
        P("tensor", None),
    )
    out_specs = (
        P(),
        P("tensor", ("dp", "ctx"), None, None, None),
        P("tensor", ("dp", "ctx"), None, None, None),
        P("tensor", ("dp", "ctx"), None, None, None),
        P(("dp", "ctx"), None, "tensor"),
        P(("dp", "ctx"), None, "tensor"),
        P(("dp", "ctx"), None, "tensor"),
        P(("dp", "ctx"), "tensor", None),
        P(("dp", "ctx"), "tensor", None),
        P(("dp", "ctx"), "tensor", None),
        P(),
        P(),
        P(),
        P(),
        P(),
        P(),
        P("tensor", None),
        P("tensor", None),
        P("tensor", None),
    )
    return jax.shard_map(
        on_device, mesh=mesh, in_specs=in_specs, out_specs=out_specs, check_vma=False
    )
```

```python
import functools
import math

import jax
import jax.numpy as jnp
from jax import lax
from jax.experimental import pallas as pl
from jax.experimental.pallas import tpu as pltpu
from jax.sharding import PartitionSpec as P

VOCAB = 32000
BLOCK = 256
STEP = 10


highest_precision = lax.Precision.HIGHEST
beta_first = 0.9
beta_second = 0.95
adam_epsilon = 1e-08
norm_epsilon = 1e-06
ahead_weight = 0.3
masked_score = -1e30
rate_table = 0.1
rate_query = 0.05
rate_values = 0.05
rate_project = 0.5
rate_inner = 0.05
rate_outer = 0.03
rate_gains = 0.5
rate_router = 0.05
rate_biases = 0.5
decay_rate = 0.1


def passed_along(value, axis, steps):
    count = lax.axis_size(axis)
    initial, last = (max(0, -steps), min(count, count - steps))
    return lax.ppermute(value, axis, [(source, source + steps) for source in range(initial, last)])

MESH_ID = pl.DeviceIdType.MESH
whole_vmem = pl.BlockSpec(memory_space=pltpu.VMEM)
whole_any = pl.BlockSpec(memory_space=pl.ANY)
line_lag = 2


def sum_line_kernel(
    rows, count, opening, prologue, epilogue, ending, n_extra, n_aux, n_scratch, part_ref, *refs
):
    extras = refs[:n_extra]
    out_ref = refs[n_extra]
    aux = refs[n_extra + 1 : n_extra + 1 + n_aux]
    rest = refs[n_extra + 1 + n_aux :]
    scratch = rest[:n_scratch]
    stage, from_end, from_mid, send_sem, end_sem, mid_sem, back_sem, back_recv = rest[n_scratch:]
    rank = lax.axis_index("tensor")
    inner = (rank == 1) | (rank == 2)
    end_peer = jnp.where(rank < 2, 1 - rank, 5 - rank)
    mid_peer = 3 - rank
    barrier = pltpu.get_barrier_semaphore()
    if opening is None:
        pl.semaphore_signal(barrier, inc=1, device_id={"tensor": end_peer}, device_id_type=MESH_ID)

        @pl.when(inner)
        def _():
            pl.semaphore_signal(
                barrier, inc=1, device_id={"tensor": mid_peer}, device_id_type=MESH_ID
            )
            pl.semaphore_wait(barrier, 2)

        @pl.when(jnp.logical_not(inner))
        def _():
            pl.semaphore_wait(barrier, 1)
    else:
        for step in (1, 2, 3):
            other = lax.rem(rank + step, 4)
            pl.semaphore_signal(barrier, inc=1, device_id={"tensor": other}, device_id_type=MESH_ID)
        pl.semaphore_wait(barrier, 3)

    def span(i):
        return pl.ds(pl.multiple_of(i * rows, rows), rows)

    def to_inner(i):
        return pltpu.make_async_remote_copy(
            src_ref=stage.at[i],
            dst_ref=from_end.at[i],
            send_sem=send_sem.at[i],
            recv_sem=end_sem.at[i],
            device_id={"tensor": end_peer},
            device_id_type=MESH_ID,
        )

    def to_middle(i):
        return pltpu.make_async_remote_copy(
            src_ref=stage.at[i],
            dst_ref=from_mid.at[i],
            send_sem=send_sem.at[i],
            recv_sem=mid_sem.at[i],
            device_id={"tensor": mid_peer},
            device_id_type=MESH_ID,
        )

    def to_end(i):
        return pltpu.make_async_remote_copy(
            src_ref=out_ref.at[span(i)],
            dst_ref=out_ref.at[span(i)],
            send_sem=back_sem.at[i],
            recv_sem=back_recv.at[i],
            device_id={"tensor": end_peer},
            device_id_type=MESH_ID,
        )

    if opening is not None:
        opening(rank, extras, scratch)

    @pl.when(jnp.logical_not(inner))
    def _():
        def push(i, carry):
            stage[i] = part_ref[span(i)].astype(jnp.bfloat16)
            to_inner(i).start()
            return carry

        lax.fori_loop(0, count, push, 0)

    if prologue is not None:
        prologue(rank, inner, extras, aux, scratch)

    @pl.when(inner)
    def _():
        def step(i, carry):
            @pl.when(i < count)
            def _():
                to_inner(i).wait_recv()
                mine = part_ref[span(i)].astype(jnp.float32) + from_end[i].astype(jnp.float32)
                stage[i] = mine.astype(jnp.bfloat16)
                to_middle(i).start()

            @pl.when(i >= line_lag)
            def _():
                j = i - line_lag
                to_middle(j).wait_recv()
                total = stage[j].astype(jnp.float32) + from_mid[j].astype(jnp.float32)
                out_ref[span(j)] = epilogue(total, span(j), rank, extras, aux, scratch)
                to_end(j).start()

            return carry

        lax.fori_loop(0, count + line_lag, step, 0)

        def drain(i, carry):
            to_middle(i).wait_send()
            to_end(i).wait_send()
            return carry

        lax.fori_loop(0, count, drain, 0)

    @pl.when(jnp.logical_not(inner))
    def _():
        def finish(i, carry):
            to_end(i).wait_recv()
            to_inner(i).wait_send()
            return carry

        lax.fori_loop(0, count, finish, 0)

    if ending is not None:
        ending(inner, end_peer, extras, aux, scratch)


def sum_line(
    part,
    extras,
    aux_shapes,
    epilogue,
    collective_id,
    prologue=None,
    scratch=(),
    opening=None,
    ending=None,
    rows=64,
):
    tokens, width = part.shape
    count = tokens // rows
    chunks = pltpu.VMEM((count, rows, width), jnp.bfloat16)
    return pl.pallas_call(
        functools.partial(
            sum_line_kernel,
            rows,
            count,
            opening,
            prologue,
            epilogue,
            ending,
            len(extras),
            len(aux_shapes),
            len(scratch),
        ),
        out_shape=[jax.ShapeDtypeStruct((tokens, width), jnp.bfloat16)] + list(aux_shapes),
        in_specs=[whole_vmem] * (1 + len(extras)),
        out_specs=[whole_vmem] * (1 + len(aux_shapes)),
        scratch_shapes=list(scratch)
        + [chunks, chunks, chunks]
        + [pltpu.SemaphoreType.DMA((count,))] * 5,
        compiler_params=pltpu.CompilerParams(
            collective_id=collective_id, has_side_effects=True, vmem_limit_bytes=48 << 20
        ),
    )(part, *extras)


def keep_total(total, span, rank, extras, aux, scratch):
    return total.astype(jnp.bfloat16)


def inverse_rms(values):
    return lax.rsqrt(jnp.mean(values * values, -1, keepdims=True) + norm_epsilon)


def norm_back_rows(values, gain, upstream):
    inverse = inverse_rms(values)
    normed = values * inverse
    scaled = upstream * gain
    gain_grad = jnp.sum(upstream * normed, 0, keepdims=True)
    inputs_grad = inverse * (scaled - normed * jnp.mean(scaled * normed, -1, keepdims=True))
    return (inputs_grad, gain_grad)


def clear_gain(rank, inner, extras, aux, scratch):
    @pl.when(inner)
    def _():
        aux[-1][...] = jnp.zeros_like(aux[-1])


def share_gains(inner, end_peer, extras, aux, scratch):
    gains = aux[0]
    copy = pltpu.make_async_remote_copy(
        src_ref=gains,
        dst_ref=gains,
        send_sem=scratch[0],
        recv_sem=scratch[1],
        device_id={"tensor": end_peer},
        device_id_type=MESH_ID,
    )

    @pl.when(inner)
    def _():
        gains[1:2, :] = extras[3][...]
        gains[2:3, :] = extras[4][...]
        copy.start()
        copy.wait_send()

    @pl.when(jnp.logical_not(inner))
    def _():
        copy.wait_recv()


def gate_copies(rank, extras, scratch):
    gate_part = extras[3]
    landed, gate_send, gate_recv = scratch
    return [
        pltpu.make_async_remote_copy(
            src_ref=gate_part,
            dst_ref=landed.at[step - 1],
            send_sem=gate_send.at[step - 1],
            recv_sem=gate_recv.at[step - 1],
            device_id={"tensor": lax.rem(rank + step, 4)},
            device_id_type=MESH_ID,
        )
        for step in (1, 2, 3)
    ]


def send_gate_parts(rank, extras, scratch):
    for copy in gate_copies(rank, extras, scratch):
        copy.start()


def start_router_grad(rank, inner, extras, aux, scratch):
    stream_one, gain, grad_two, gate_part, gates, routes, router_low = extras
    grad_one, logit_grad, target_total, gain_grad = aux
    landed = scratch[0]
    clear_gain(rank, inner, extras, aux, scratch)
    for copy in gate_copies(rank, extras, scratch):
        copy.wait()
    gate_grad = jnp.zeros(gate_part.shape, jnp.float32)
    for source in range(4):
        piece = jnp.zeros(gate_part.shape, jnp.float32)
        for step in (1, 2, 3):
            piece = jnp.where(lax.rem(source + step, 4) == rank, landed[step - 1], piece)
        gate_grad = gate_grad + jnp.where(rank == source, gate_part[...], piece)
    target_total[...] = gate_grad[2:3]
    gate_grad = gate_grad[0:2]
    weighted = gates[...] * gate_grad
    chosen = gates[...] * (gate_grad - (weighted[0:1] + weighted[1:2]))
    experts, tokens = logit_grad.shape
    row = lax.broadcasted_iota(jnp.int32, (experts, tokens), 0)
    placed = jnp.where(row == routes[0:1], chosen[0:1], 0.0) + jnp.where(
        row == routes[1:2], chosen[1:2], 0.0
    )
    logit_grad[...] = placed.astype(jnp.bfloat16)

    @pl.when(inner)
    def _():
        grad_one[...] = lax.dot_general(
            logit_grad[...],
            router_low[...],
            (((0,), (1,)), ((), ())),
            preferred_element_type=jnp.float32,
        )


def finish_expert_grad(total, span, rank, extras, aux, scratch):
    stream_one, gain, grad_two, gate_part, gates, routes, router_low = extras
    grad_one, logit_grad, target_total, gain_grad = aux
    part, gain_part = norm_back_rows(
        stream_one[span], gain[...], total + grad_one[span]
    )
    result = grad_two[span] + part
    grad_one[span] = result
    gain_grad[...] += gain_part
    return result.astype(jnp.bfloat16)


def finish_input_grad(scale, total, span, rank, extras, aux, scratch):
    embedded, gain, grad_one = extras[:3]
    stream_zero = embedded[span].astype(jnp.float32) * scale
    part, gain_part = norm_back_rows(stream_zero, gain[...], total)
    aux[0][0:1, :] += gain_part
    return ((grad_one[span] + part) * scale).astype(jnp.bfloat16)


def middle_kernel(
    attended_ref, embedded_ref, gain_ref, router_ref, routes_ref, *refs
):
    rolled, (stream_ref, normed_ref, rows_ref, columns_ref, project_ref) = refs[:4], refs[4:]

    @pl.when(pl.program_id(0) == 0)
    def _():
        for step in range(4):
            lines = rolled[step].shape[0]
            owner = lax.rem(lax.axis_index("tensor") + 4 - step, 4)
            project_ref[pl.ds(pl.multiple_of(owner * lines, lines), lines)] = rolled[step][...]

    scale = math.sqrt(embedded_ref.shape[1])
    stream = embedded_ref[...].astype(jnp.float32) * scale + lax.dot_general(
        attended_ref[...], project_ref[...], (((0,), (0,)), ((), ())), preferred_element_type=jnp.float32
    )
    stream_ref[...] = stream
    normed = (stream * inverse_rms(stream) * gain_ref[...]).astype(jnp.bfloat16)
    normed_ref[...] = normed
    scores = lax.dot_general(
        router_ref[...], normed, (((1,), (1,)), ((), ())), preferred_element_type=jnp.float32
    )
    expert = lax.broadcasted_iota(jnp.int32, scores.shape, 0)
    first, second = (
        jnp.sum(jnp.where(expert == routes_ref[k : k + 1, :], scores, 0.0), 0, keepdims=True)
        for k in range(2)
    )
    top = jnp.maximum(first, second)
    first, second = jnp.exp(first - top), jnp.exp(second - top)
    total = first + second
    gates = jnp.concatenate([first / total, second / total], 0)
    rows_ref[...] = gates
    columns_ref[...] = jnp.concatenate([gates, jnp.zeros((6, gates.shape[1]), jnp.float32)], 0).T


def middle(attended, rolled, embedded, gain, router, routes):
    tokens, width = embedded.shape
    tile = 256
    fixed = lambda k: (0, 0)
    whole = lambda x: pl.BlockSpec(x.shape, fixed)
    down = lambda n: pl.BlockSpec((tile, n), lambda k: (k, 0))
    along = lambda n: pl.BlockSpec((n, tile), lambda k: (0, k))
    return pl.pallas_call(
        middle_kernel,
        grid=(tokens // tile,),
        out_shape=[
            jax.ShapeDtypeStruct((tokens, width), jnp.float32),
            jax.ShapeDtypeStruct((tokens, width), jnp.bfloat16),
            jax.ShapeDtypeStruct((2, tokens), jnp.float32),
            jax.ShapeDtypeStruct((tokens, 8), jnp.float32),
        ],
        in_specs=[along(width), down(width), whole(gain), whole(router), along(2)]
        + [whole(x) for x in rolled],
        out_specs=[down(width), down(width), along(2), down(8)],
        scratch_shapes=[pltpu.VMEM((width, width), jnp.bfloat16)],
        compiler_params=pltpu.CompilerParams(vmem_limit_bytes=40 << 20),
    )(attended, embedded, gain, router, routes, *rolled)


def embed_kernel(
    chunks, first_unit, slots_ref, mine_ref, rows_ref, gain_ref, units_ref, embedded_ref, normed_ref, joint_ref, *refs
):
    held, total, stage, from_end, from_mid = refs[:5]
    send_x, recv_x, send_y, recv_y, send_z, recv_z, send_core, recv_core = refs[5:13]
    send_sem, end_sem, mid_sem, back_sem, back_recv = refs[13:]
    chip, core = lax.axis_index("dp"), lax.axis_index("ctx")
    beside = chip + 1 - 2 * lax.rem(chip, 2)
    across = lax.rem(chip + 2, 4)
    opposite = across + 1 - 2 * lax.rem(across, 2)
    places = (chip, beside, across, opposite)
    rank = lax.axis_index("tensor")
    inner = (rank == 1) | (rank == 2)
    end_peer = jnp.where(rank < 2, 1 - rank, 5 - rank)
    mid_peer = 3 - rank
    slots, unit_rows = mine_ref.shape[:2]
    width = total.shape[2]
    size = slots // chunks
    split = (chunks + 1) // 2
    tokens = rows_ref.shape[0]
    count, rows = stage.shape[1:3]

    def repeat(first, last, body):
        def step(i, carry):
            body(i)
            return carry

        lax.fori_loop(first, last, step, 0)

    def columns(h):
        return slice(h * width, (h + 1) * width)

    own = (chip * 2 + core) * slots
    for h in range(2):
        held[h, pl.ds(own, slots)] = mine_ref[:, :, columns(h)].astype(jnp.bfloat16)
    barrier = pltpu.get_barrier_semaphore()
    for place in ({"ctx": 1 - core}, {"dp": beside}, {"dp": across}, {"tensor": end_peer}):
        pl.semaphore_signal(barrier, inc=1, device_id=place, device_id_type=MESH_ID)

    @pl.when(inner)
    def _():
        pl.semaphore_signal(barrier, inc=1, device_id={"tensor": mid_peer}, device_id_type=MESH_ID)
        pl.semaphore_wait(barrier, 5)

    @pl.when(jnp.logical_not(inner))
    def _():
        pl.semaphore_wait(barrier, 4)

    def remote(source, target, send, recv, place):
        return pltpu.make_async_remote_copy(
            src_ref=source,
            dst_ref=target,
            send_sem=send,
            recv_sem=recv,
            device_id=place,
            device_id_type=MESH_ID,
        )

    def copy(h, place, q, send, recv, target):
        piece = held.at[h, pl.ds((place * 2 + core) * slots + q * size, size)]
        return remote(piece, piece, send, recv, target)

    def to_beside(h, q):
        return copy(h, chip, q, send_x.at[h, q], recv_x.at[h, q], {"dp": beside})

    def to_across(h, q):
        return copy(h, chip, q, send_y.at[h, q], recv_y.at[h, q], {"dp": across})

    def passed_on(h, q, source, target):
        return copy(h, source, q, send_z.at[h, q], recv_z.at[h, q], {"dp": target})

    def to_core(h, k, q):
        return copy(h, places[k], q, send_core.at[h, k, q], recv_core.at[h, k, q], {"ctx": 1 - core})

    def start(h):
        def both(i):
            to_beside(h, i).start()
            to_across(h, lax.rem(i + split, chunks)).start()

        repeat(0, chunks, both)
        repeat(0, chunks, lambda q: to_core(h, 0, q).start())

    def look(h, place, which):
        begin = (place * 2 + which) * slots
        lines = slots * unit_rows
        column = lax.broadcasted_iota(jnp.int32, (tokens, lines), 1) + begin * unit_rows
        hit = jnp.where(column == rows_ref[...], 1.0, 0.0).astype(jnp.bfloat16)
        block = held[h, pl.ds(begin, slots)].reshape(lines, width)
        total[h] += jnp.dot(hit, block, preferred_element_type=jnp.float32)

    def relay(h, i):
        to_beside(h, i).wait_recv()

        @pl.when(i < split)
        def _():
            passed_on(h, i, beside, across).start()

        to_core(h, 1, i).start()
        j = lax.rem(i + split, chunks)
        to_across(h, j).wait_recv()

        @pl.when(j >= split)
        def _():
            passed_on(h, j, across, beside).start()

        to_core(h, 2, j).start()

    def rest(h):
        repeat(0, chunks, lambda q: to_core(h, 0, q).wait_recv())
        look(h, chip, 1 - core)
        look(h, beside, core)
        look(h, across, core)

        def last(q):
            passed_on(h, q, opposite, opposite).wait_recv()
            to_core(h, 3, q).start()
            to_core(h, 1, q).wait_recv()
            to_core(h, 2, q).wait_recv()

        repeat(0, chunks, last)
        look(h, beside, 1 - core)
        look(h, across, 1 - core)
        look(h, opposite, core)
        repeat(0, chunks, lambda q: to_core(h, 3, q).wait_recv())
        look(h, opposite, 1 - core)

    def span(i):
        return pl.ds(pl.multiple_of(i * rows, rows), rows)

    def to_inner(h, i):
        return remote(
            stage.at[h, i], from_end.at[h, i], send_sem.at[h, i], end_sem.at[h, i], {"tensor": end_peer}
        )

    def to_middle(h, i):
        return remote(
            stage.at[h, i], from_mid.at[h, i], send_sem.at[h, i], mid_sem.at[h, i], {"tensor": mid_peer}
        )

    def to_end(h, i):
        piece = embedded_ref.at[span(i), columns(h)]
        return remote(piece, piece, back_sem.at[h, i], back_recv.at[h, i], {"tensor": end_peer})

    def push(h):
        @pl.when(jnp.logical_not(inner))
        def _():
            def one(i):
                stage[h, i] = total[h, span(i)].astype(jnp.bfloat16)
                to_inner(h, i).start()

            repeat(0, count, one)

    def exchange(h, i):
        @pl.when(inner & (i < count))
        def _():
            to_inner(h, i).wait_recv()
            stage[h, i] = (total[h, span(i)] + from_end[h, i].astype(jnp.float32)).astype(jnp.bfloat16)
            to_middle(h, i).start()

        @pl.when(inner & (i >= line_lag))
        def _():
            j = i - line_lag
            to_middle(h, j).wait_recv()
            both = stage[h, j].astype(jnp.float32) + from_mid[h, j].astype(jnp.float32)
            embedded_ref[span(j), columns(h)] = both.astype(jnp.bfloat16)
            to_end(h, j).start()

    total[...] = jnp.zeros_like(total)
    start(0)
    look(0, chip, core)
    repeat(0, chunks, lambda i: relay(0, i))
    start(1)
    rest(0)
    push(0)
    look(1, chip, core)

    def between(i):
        exchange(0, i)

        @pl.when(i < chunks)
        def _():
            relay(1, i)

    repeat(0, count + line_lag, between)
    rest(1)
    push(1)

    def place_unit(u):
        for h in range(2):
            units_ref[u, :, columns(h)] = held[h, slots_ref[u]]

    @pl.when(jnp.logical_not(inner))
    def _():
        repeat(0, units_ref.shape[0], place_unit)

    repeat(0, count + line_lag, lambda i: exchange(1, i))

    @pl.when(inner)
    def _():
        repeat(0, units_ref.shape[0], place_unit)

    def finish(q):
        for h in range(2):
            to_beside(h, q).wait_send()
            to_across(h, q).wait_send()
            for k in range(4):
                to_core(h, k, q).wait_send()
            passed_on(h, q, opposite, opposite).wait_send()

    repeat(0, chunks, finish)

    @pl.when(inner)
    def _():
        def drain(i):
            for h in range(2):
                to_middle(h, i).wait_send()
                to_end(h, i).wait_send()

        repeat(0, count, drain)

    @pl.when(jnp.logical_not(inner))
    def _():
        def drain(i):
            for h in range(2):
                to_end(h, i).wait_recv()
                to_inner(h, i).wait_send()

        repeat(0, count, drain)

    stream = embedded_ref[...].astype(jnp.float32) * math.sqrt(2 * width)
    normed = (stream * inverse_rms(stream) * gain_ref[...]).astype(jnp.bfloat16)
    normed_ref[...] = normed
    lines = joint_ref.shape[0]
    weights = units_ref[first_unit : first_unit + lines // unit_rows].reshape(lines, 2 * width)
    joint_ref[...] = lax.dot_general(
        weights, normed, (((1,), (1,)), ((), ())), preferred_element_type=jnp.float32
    ).astype(jnp.bfloat16)


def embed(unit_slots, mine, slot_rows, gain, first_unit, lines, collective_id):
    slots, unit_rows, width = mine.shape
    tokens = slot_rows.shape[0]
    chunks = max(k for k in range(1, 8) if slots % k == 0)
    rows = 128
    half = width // 2
    sems = pltpu.SemaphoreType.DMA((2, chunks))
    line = pltpu.VMEM((2, tokens // rows, rows, half), jnp.bfloat16)
    return pl.pallas_call(
        functools.partial(embed_kernel, chunks, first_unit),
        out_shape=[
            jax.ShapeDtypeStruct((unit_slots.shape[0], unit_rows, width), jnp.bfloat16),
            jax.ShapeDtypeStruct((tokens, width), jnp.bfloat16),
            jax.ShapeDtypeStruct((tokens, width), jnp.bfloat16),
            jax.ShapeDtypeStruct((lines, tokens), jnp.bfloat16),
        ],
        in_specs=[pl.BlockSpec(memory_space=pltpu.SMEM)] + [whole_vmem] * 3,
        out_specs=[whole_vmem] * 4,
        scratch_shapes=[
            pltpu.VMEM((2, 8 * slots, unit_rows, half), jnp.bfloat16),
            pltpu.VMEM((2, tokens, half), jnp.float32),
            line,
            line,
            line,
        ]
        + [sems] * 6
        + [pltpu.SemaphoreType.DMA((2, 4, chunks))] * 2
        + [pltpu.SemaphoreType.DMA((2, tokens // rows))] * 5,
        compiler_params=pltpu.CompilerParams(
            collective_id=collective_id, has_side_effects=True, vmem_limit_bytes=60 << 20
        ),
    )(unit_slots, mine, slot_rows, gain)


def pull_units_kernel(parts, slots_ref, *refs):
    sources, out_ref, sem = refs[:parts], refs[parts], refs[parts + 1]
    width = out_ref.shape[-1] // parts

    def push(u, carry):
        for part in range(parts):
            pltpu.make_async_copy(
                sources[part].at[slots_ref[u]],
                out_ref.at[u, :, part * width : (part + 1) * width],
                sem,
            ).start()
        return carry

    lax.fori_loop(0, out_ref.shape[0], push, 0)
    pltpu.make_async_copy(out_ref, out_ref, sem).wait()


def pull_units(sources, slots):
    count = slots.shape[0]
    rows, width = sources[0].shape[1:]
    return pl.pallas_call(
        functools.partial(pull_units_kernel, len(sources)),
        out_shape=jax.ShapeDtypeStruct((count, rows, width * len(sources)), sources[0].dtype),
        in_specs=[pl.BlockSpec(memory_space=pltpu.SMEM)] + [whole_any] * len(sources),
        out_specs=whole_vmem,
        scratch_shapes=[pltpu.SemaphoreType.DMA],
        compiler_params=pltpu.CompilerParams(vmem_limit_bytes=40 << 20),
    )(slots, *sources)


def attention_kernel(
    heads, size, bias_ref, own_ref, out_ref, logsum_ref, before_ref,
    queries, own_values, old_values, scores, peak, total, keys_sem, send_sem, recv_sem,
):
    tokens = own_ref.shape[1]
    blocks = tokens // BLOCK
    hidden = heads * size
    later = lax.axis_index("ctx") > 0
    rank = lax.axis_index("tensor")
    barrier = pltpu.get_barrier_semaphore()
    other_core = {"ctx": 1 - lax.axis_index("ctx")}
    pl.semaphore_signal(barrier, inc=1, device_id=other_core, device_id_type=MESH_ID)
    for step in (1, 2, 3):
        other = lax.rem(rank + step, 4)
        pl.semaphore_signal(barrier, inc=1, device_id={"tensor": other}, device_id_type=MESH_ID)
    pl.semaphore_wait(barrier, 4)
    pairs = pltpu.make_async_remote_copy(
        src_ref=own_ref.at[pl.ds(hidden, 2 * hidden)],
        dst_ref=before_ref,
        send_sem=keys_sem.at[0],
        recv_sem=keys_sem.at[1],
        device_id=other_core,
        device_id_type=MESH_ID,
    )

    @pl.when(jnp.logical_not(later))
    def _():
        pairs.start()
        before_ref[...] = jnp.zeros_like(before_ref)

    def flipped(rows):
        return rows.astype(jnp.float32).T.astype(jnp.bfloat16)

    for head in range(heads):
        span = slice(head * size, (head + 1) * size)
        queries[head] = flipped(own_ref[span, :]) * jnp.bfloat16(size**-0.5)
        own_values[head] = flipped(
            own_ref[2 * hidden + head * size : 2 * hidden + (head + 1) * size, :]
        )

    @pl.when(later)
    def _():
        pairs.wait_recv()
        for head in range(heads):
            old_values[head] = flipped(
                before_ref[hidden + head * size : hidden + (head + 1) * size, :]
            )

    def sent(block, step):
        piece = out_ref.at[rank, :, pl.ds(block * BLOCK, BLOCK)]
        return pltpu.make_async_remote_copy(
            src_ref=piece,
            dst_ref=piece,
            send_sem=send_sem.at[block, step - 1],
            recv_sem=recv_sem.at[block, step - 1],
            device_id={"tensor": lax.rem(rank + step, 4)},
            device_id_type=MESH_ID,
        )

    for block in range(blocks):
        for head in range(heads):
            span = slice(head * size, (head + 1) * size)
            rows = queries[head, block * BLOCK : (block + 1) * BLOCK]
            own_keys = own_ref[hidden + head * size : hidden + (head + 1) * size, :]
            width = (block + 1) * BLOCK
            mine = jnp.dot(rows, own_keys[:, :width], preferred_element_type=jnp.float32)
            top = None
            parts = []
            for k in range(block + 1):
                part = mine[:, k * BLOCK : (k + 1) * BLOCK] + bias_ref[head, block - k]
                parts.append(part)
                high = jnp.max(part, 1, keepdims=True)
                top = high if top is None else jnp.maximum(top, high)
            peak[...] = top

            @pl.when(later)
            def _():
                old = jnp.dot(rows, before_ref[span, :], preferred_element_type=jnp.float32)
                top_old = None
                for k in range(blocks):
                    part = old[:, k * BLOCK : (k + 1) * BLOCK] + bias_ref[head, block + blocks - k]
                    scores[:, k * BLOCK : (k + 1) * BLOCK] = part
                    high = jnp.max(part, 1, keepdims=True)
                    top_old = high if top_old is None else jnp.maximum(top_old, high)
                peak[...] = jnp.maximum(peak[...], top_old)

            top = peak[...]
            parts = [jnp.exp(part - top) for part in parts]
            own_sum = None
            for part in parts:
                part_sum = jnp.sum(part, 1, keepdims=True)
                own_sum = part_sum if own_sum is None else own_sum + part_sum
            total[...] = own_sum

            @pl.when(later)
            def _():
                old_exp = jnp.exp(scores[...] - top)
                scores[...] = old_exp
                total[...] += jnp.sum(old_exp, 1, keepdims=True)

            full = total[...]
            inverse = 1.0 / full
            low = jnp.concatenate([(part * inverse).astype(jnp.bfloat16) for part in parts], 1)
            result = jnp.dot(low, own_values[head, :width], preferred_element_type=jnp.float32)
            logsum_ref[head, block * BLOCK : (block + 1) * BLOCK, :] = top + jnp.log(full)
            place = (rank, span, slice(block * BLOCK, (block + 1) * BLOCK))

            @pl.when(later)
            def _():
                low_old = (scores[...] * inverse).astype(jnp.bfloat16)
                both = result + jnp.dot(low_old, old_values[head], preferred_element_type=jnp.float32)
                out_ref[place] = both.T.astype(jnp.bfloat16)

            @pl.when(jnp.logical_not(later))
            def _():
                out_ref[place] = result.T.astype(jnp.bfloat16)

        for step in (1, 2, 3):
            sent(block, step).start()

    for block in range(blocks):
        for step in (1, 2, 3):
            sent(block, step).wait()

    @pl.when(jnp.logical_not(later))
    def _():
        pairs.wait_send()


def attention(biases, own, heads, size, collective_id):
    tokens = own.shape[1]
    blocks = tokens // BLOCK
    flat = pltpu.VMEM((heads, tokens, size), jnp.bfloat16)
    return pl.pallas_call(
        functools.partial(attention_kernel, heads, size),
        out_shape=[
            jax.ShapeDtypeStruct((4, heads * size, tokens), jnp.bfloat16),
            jax.ShapeDtypeStruct((heads, tokens, 1), jnp.float32),
            jax.ShapeDtypeStruct((2 * heads * size, tokens), jnp.bfloat16),
        ],
        in_specs=[pl.BlockSpec(memory_space=pltpu.SMEM), whole_vmem],
        out_specs=[whole_vmem] * 3,
        scratch_shapes=[
            flat,
            flat,
            flat,
            pltpu.VMEM((BLOCK, tokens), jnp.float32),
            pltpu.VMEM((BLOCK, 1), jnp.float32),
            pltpu.VMEM((BLOCK, 1), jnp.float32),
            pltpu.SemaphoreType.DMA((2,)),
            pltpu.SemaphoreType.DMA((blocks, 3)),
            pltpu.SemaphoreType.DMA((blocks, 3)),
        ],
        compiler_params=pltpu.CompilerParams(
            collective_id=collective_id, has_side_effects=True, vmem_limit_bytes=40 << 20
        ),
    )(biases, own)


def attention_back_kernel(
    heads, size, bias_ref, own_ref, before_ref, logsum_ref, grad_ref, project_ref,
    *refs
):
    states, (query_out, own_out, before_out, bias_out) = refs[:8], refs[8:12]
    updated, (probs, slopes, inner, query_sum, own_sum, before_sum) = refs[12:18], refs[18:24]
    held, load_sem, store_sem = refs[24:]
    loads = [pltpu.make_async_copy(states[k], held.at[k], load_sem.at[k]) for k in range(8)]
    stores = [
        pltpu.make_async_copy(held.at[4 * (k // 3) + k % 3], updated[k], store_sem.at[k])
        for k in range(6)
    ]
    for load in loads:
        load.start()

    def update(i, carry):
        lines = held.shape[1] // 16
        span = pl.ds(pl.multiple_of(i * lines, lines), lines)
        for k, rate in enumerate((rate_inner, rate_outer)):
            fresh = adam_update(*(held[4 * k + n, span] for n in range(4)), rate, decay_rate)
            for n in range(3):
                held[4 * k + n, span] = fresh[n]
        return carry

    tokens = own_ref.shape[1]
    blocks = tokens // BLOCK
    hidden = heads * size
    later = lax.axis_index("ctx") > 0
    bias_out[...] = jnp.zeros_like(bias_out)

    def flipped(rows):
        return rows.astype(jnp.float32).T.astype(jnp.bfloat16)

    for head in range(heads):
        span = slice(head * size, (head + 1) * size)
        value_span = slice(hidden + head * size, hidden + (head + 1) * size)
        query_rows = own_ref[span, :]
        query = flipped(query_rows) * jnp.bfloat16(size**-0.5)
        own_keys = own_ref[hidden + head * size : hidden + (head + 1) * size, :]
        own_values = own_ref[2 * hidden + head * size : 2 * hidden + (head + 1) * size, :]
        old_keys = before_ref[span, :]
        old_values = before_ref[value_span, :]
        own_keys_flip = flipped(own_keys)
        grad = lax.dot_general(
            grad_ref[...], project_ref[span, :], (((1,), (1,)), ((), ())), preferred_element_type=jnp.float32
        )
        grad_rows = grad.T.astype(jnp.bfloat16)
        grad = grad.astype(jnp.bfloat16)
        own_sum[...] = jnp.zeros_like(own_sum)

        @pl.when(later)
        def _():
            before_sum[...] = jnp.zeros_like(before_sum)

        for block in range(blocks):
            at = slice(block * BLOCK, (block + 1) * BLOCK)
            width = (block + 1) * BLOCK
            rows, up = query[at], grad[at]
            lse = logsum_ref[head, at, :]
            score = jnp.dot(rows, own_keys[:, :width], preferred_element_type=jnp.float32)
            prob = jnp.concatenate(
                [
                    jnp.exp(score[:, k * BLOCK : (k + 1) * BLOCK] + (bias_ref[head, block - k] - lse))
                    for k in range(block + 1)
                ],
                1,
            )
            slope = jnp.dot(up, own_values[:, :width], preferred_element_type=jnp.float32)
            inner[...] = jnp.sum(prob * slope, 1, keepdims=True)

            @pl.when(later)
            def _():
                score = jnp.dot(rows, old_keys, preferred_element_type=jnp.float32)
                old_slope = jnp.dot(up, old_values, preferred_element_type=jnp.float32)
                old_prob = jnp.concatenate(
                    [
                        jnp.exp(
                            score[:, k * BLOCK : (k + 1) * BLOCK]
                            + (bias_ref[head, block + blocks - k] - lse)
                        )
                        for k in range(blocks)
                    ],
                    1,
                )
                probs[...] = old_prob
                slopes[...] = old_slope
                inner[...] += jnp.sum(old_prob * old_slope, 1, keepdims=True)

            row_inner = inner[...]
            low_grad = (prob * (slope - row_inner)).astype(jnp.bfloat16)
            query_sum[...] = jnp.dot(
                low_grad, own_keys_flip[:width], preferred_element_type=jnp.float32
            )
            own_sum[:size, :width] += jnp.dot(
                query_rows[:, at], low_grad, preferred_element_type=jnp.float32
            )
            own_sum[size:, :width] += jnp.dot(
                grad_rows[:, at], prob.astype(jnp.bfloat16), preferred_element_type=jnp.float32
            )
            for k in range(block + 1):
                line = head * 2 * blocks + block - k
                bias_out[line : line + 1, :] += jnp.sum(
                    low_grad[:, k * BLOCK : (k + 1) * BLOCK].astype(jnp.float32), 0, keepdims=True
                )

            @pl.when(later)
            def _():
                old_prob = probs[...]
                low_old = (old_prob * (slopes[...] - row_inner)).astype(jnp.bfloat16)
                query_sum[...] += jnp.dot(
                    low_old, flipped(old_keys), preferred_element_type=jnp.float32
                )
                before_sum[:size, :] += jnp.dot(
                    query_rows[:, at], low_old, preferred_element_type=jnp.float32
                )
                before_sum[size:, :] += jnp.dot(
                    grad_rows[:, at], old_prob.astype(jnp.bfloat16), preferred_element_type=jnp.float32
                )
                for k in range(blocks):
                    line = head * 2 * blocks + block + blocks - k
                    bias_out[line : line + 1, :] += jnp.sum(
                        low_old[:, k * BLOCK : (k + 1) * BLOCK].astype(jnp.float32), 0, keepdims=True
                    )

            query_out[span, at] = (query_sum[...].T * size**-0.5).astype(jnp.bfloat16)

        own_out[span, :] = own_sum[:size, :] * size**-0.5
        own_out[value_span, :] = own_sum[size:, :]

        @pl.when(later)
        def _():
            before_out[span, :] = (before_sum[:size, :] * size**-0.5).astype(jnp.bfloat16)
            before_out[value_span, :] = before_sum[size:, :].astype(jnp.bfloat16)

        if head == 0:
            for load in loads:
                load.wait()
            lax.fori_loop(0, 16, update, 0)
            for store in stores:
                store.start()

    @pl.when(jnp.logical_not(later))
    def _():
        before_out[...] = jnp.zeros_like(before_out)

    for store in stores:
        store.wait()


def attention_back(biases, own, before, logsum, grad, project, states, heads, size):
    tokens = own.shape[1]
    hidden = heads * size
    return pl.pallas_call(
        functools.partial(attention_back_kernel, heads, size),
        out_shape=[
            jax.ShapeDtypeStruct((hidden, tokens), jnp.bfloat16),
            jax.ShapeDtypeStruct((2 * hidden, tokens), jnp.float32),
            jax.ShapeDtypeStruct((2 * hidden, tokens), jnp.bfloat16),
            jax.ShapeDtypeStruct((heads * 2 * (tokens // BLOCK), BLOCK), jnp.float32),
        ]
        + [jax.ShapeDtypeStruct(states[0].shape, jnp.float32)] * 6,
        in_specs=[pl.BlockSpec(memory_space=pltpu.SMEM)] + [whole_vmem] * 5 + [whole_any] * 8,
        out_specs=[whole_vmem] * 4 + [whole_any] * 6,
        scratch_shapes=[
            pltpu.VMEM((BLOCK, tokens), jnp.float32),
            pltpu.VMEM((BLOCK, tokens), jnp.float32),
            pltpu.VMEM((BLOCK, 1), jnp.float32),
            pltpu.VMEM((BLOCK, size), jnp.float32),
            pltpu.VMEM((2 * size, tokens), jnp.float32),
            pltpu.VMEM((2 * size, tokens), jnp.float32),
            pltpu.VMEM((8,) + states[0].shape, jnp.float32),
            pltpu.SemaphoreType.DMA((8,)),
            pltpu.SemaphoreType.DMA((6,)),
        ],
        compiler_params=pltpu.CompilerParams(vmem_limit_bytes=48 << 20),
    )(biases, own, before, logsum, grad, project, *states)


def vocab_tile(vocab):
    return max(k for k in range(16, 1601, 16) if vocab % k == 0)


def head_line_kernel(
    tile, part_ref, stream_ref, gain_ref, table_ref, wanted_ref, weight_ref,
    low_ref, grad_low_ref, grad_ref, gain_grad, logsum_ref, picked_ref, slopes_ref,
    logits, table, stage, from_end, from_mid, own, turned, stats, landed, slope_tiles, total,
    load_sem, send_sem, end_sem, mid_sem, back_sem, back_recv, stat_send, stat_recv, store_sem,
):
    rank = lax.axis_index("tensor")
    inner = (rank == 1) | (rank == 2)
    end_peer = jnp.where(rank < 2, 1 - rank, 5 - rank)
    mid_peer = 3 - rank
    count, rows = stage.shape[:2]
    columns = turned.shape[1]
    pieces = table.shape[0] // tile
    group = columns // rows
    tiles = count // group
    vocab = table.shape[0]
    load = pltpu.make_async_copy(table_ref.at[pl.ds(0, vocab)], table, load_sem)
    load.start()
    barrier = pltpu.get_barrier_semaphore()
    for step in (1, 2, 3):
        other = lax.rem(rank + step, 4)
        pl.semaphore_signal(barrier, inc=1, device_id={"tensor": other}, device_id_type=MESH_ID)
    pl.semaphore_wait(barrier, 3)

    def span(i):
        return pl.ds(pl.multiple_of(i * rows, rows), rows)

    def over(t):
        return pl.ds(pl.multiple_of(t * columns, columns), columns)

    def line_copy(source, target, send, recv, peer):
        return pltpu.make_async_remote_copy(
            src_ref=source,
            dst_ref=target,
            send_sem=send,
            recv_sem=recv,
            device_id={"tensor": peer},
            device_id_type=MESH_ID,
        )

    def to_inner(i):
        return line_copy(stage.at[i], from_end.at[i], send_sem.at[i], end_sem.at[i], end_peer)

    def to_middle(i):
        return line_copy(stage.at[i], from_mid.at[i], send_sem.at[i], mid_sem.at[i], mid_peer)

    def to_end(ref, i):
        rows_of = ref.at[span(i)]
        return line_copy(rows_of, rows_of, back_sem.at[i], back_recv.at[i], end_peer)

    def repeat(first, last, body):
        def step(i, carry):
            body(i)
            return carry

        lax.fori_loop(first, last, step, 0)

    def turn(t):
        turned[...] = low_ref[over(t)].astype(jnp.float32).T.astype(jnp.bfloat16)

    def table_rows(k):
        return table[k * tile : (k + 1) * tile]

    def first_logits(t):
        turn(t)
        logits[0] = jnp.dot(table_rows(0), turned[...], preferred_element_type=jnp.float32)

    def next_logits(k):
        if k + 1 < pieces:
            logits[(k + 1) % 2] = jnp.dot(
                table_rows(k + 1), turned[...], preferred_element_type=jnp.float32
            )

    def sums_unit(t, k):
        next_logits(k)
        before = stats[0:1, over(t)]
        top = jnp.maximum(before, jnp.max(logits[k % 2], 0, keepdims=True))
        stats[1:2, over(t)] = stats[1:2, over(t)] * jnp.exp(before - top) + jnp.sum(
            jnp.exp(logits[k % 2] - top), 0, keepdims=True
        )
        stats[0:1, over(t)] = top

    def sums_tile(t):
        first_logits(t)
        for k in range(pieces):
            sums_unit(t, k)

    stats[0:1, :] = jnp.full_like(stats[0:1, :], masked_score)
    stats[1:2, :] = jnp.zeros_like(stats[1:2, :])

    @pl.when(jnp.logical_not(inner))
    def _():
        def push(i):
            stage[i] = part_ref[span(i)].astype(jnp.bfloat16)
            to_inner(i).start()

        repeat(0, count, push)
        load.wait()

        def forward(t):
            repeat(0, group, lambda c: to_end(low_ref, t * group + c).wait_recv())
            sums_tile(t)

        repeat(0, tiles, forward)
        repeat(0, count, lambda i: to_inner(i).wait_send())

    @pl.when(inner)
    def _():
        gain_grad[...] = jnp.zeros_like(gain_grad)
        load.wait()

        def gather(i):
            to_inner(i).wait_recv()
            mine = part_ref[span(i)] + from_end[i].astype(jnp.float32)
            stage[i] = mine.astype(jnp.bfloat16)
            to_middle(i).start()

        def settle_rows(j):
            to_middle(j).wait_recv()
            stream_two = stream_ref[span(j)] + (
                stage[j].astype(jnp.float32) + from_mid[j].astype(jnp.float32)
            )
            grad_ref[span(j)] = stream_two
            low_ref[span(j)] = (stream_two * inverse_rms(stream_two) * gain_ref[...]).astype(
                jnp.bfloat16
            )
            to_end(low_ref, j).start()

        turns = [[k for k in range(pieces) if k * (group - 1) // pieces == c - 1] for c in range(group)]

        def advance(t):
            for c in range(group):
                i = t * group + c
                gather(i)

                @pl.when(i >= line_lag)
                def _():
                    settle_rows(i - line_lag)

                if turns[c]:

                    @pl.when(t >= 1)
                    def _():
                        if c == 1:
                            first_logits(t - 1)
                        for k in turns[c]:
                            sums_unit(t - 1, k)

        repeat(0, tiles, advance)
        repeat(count - line_lag, count, settle_rows)
        sums_tile(tiles - 1)

        def drain(i):
            to_middle(i).wait_send()
            to_end(low_ref, i).wait_send()

        repeat(0, count, drain)

    copies = [
        line_copy(
            stats, landed.at[step - 1], stat_send.at[step - 1], stat_recv.at[step - 1], lax.rem(rank + step, 4)
        )
        for step in (1, 2, 3)
    ]
    for copy in copies:
        copy.start()
    for copy in copies:
        copy.wait()
    tops, sums = [], []
    for source in range(4):
        piece = stats[...]
        for step in (1, 2, 3):
            piece = jnp.where(lax.rem(source + step, 4) == rank, landed[step - 1], piece)
        tops.append(piece[0:1])
        sums.append(piece[1:2])
    top = jnp.maximum(jnp.maximum(tops[0], tops[1]), jnp.maximum(tops[2], tops[3]))
    whole = sums[0] * jnp.exp(tops[0] - top)
    for source in (1, 2, 3):
        whole = whole + sums[source] * jnp.exp(tops[source] - top)
    logsum_ref[...] = top + jnp.log(whole)
    picked_ref[...] = jnp.zeros_like(picked_ref)

    def store(t):
        return pltpu.make_async_copy(
            slope_tiles.at[lax.rem(t, 2)], slopes_ref.at[:, over(t)], store_sem.at[lax.rem(t, 2)]
        )

    def slope_unit(t, k):
        values = logits[k % 2]
        row = lax.broadcasted_iota(jnp.int32, values.shape, 0)
        base = k * tile
        hits = jnp.where(row == wanted_ref[0:1, over(t)] - base, weight_ref[0:1, over(t)], 0.0)
        hits = hits + jnp.where(
            row == wanted_ref[1:2, over(t)] - base, weight_ref[1:2, over(t)], 0.0
        )
        picked_ref[:, over(t)] += jnp.sum(hits * values, 0, keepdims=True)
        softmax = jnp.exp(values - logsum_ref[:, over(t)])
        slope_tiles[lax.rem(t, 2), base : base + tile] = (
            (weight_ref[2:3, over(t)] * softmax - hits) * weight_ref[3:4, over(t)]
        ).astype(jnp.bfloat16)

    def add_rows(t, k):
        total[...] += lax.dot_general(
            slope_tiles[lax.rem(t, 2), k * tile : (k + 1) * tile],
            table_rows(k),
            (((0,), (0,)), ((), ())),
            preferred_element_type=jnp.float32,
        )

    def settle(j):
        to_middle(j).wait_recv()
        upstream = stage[j].astype(jnp.float32) + from_mid[j].astype(jnp.float32)
        grad_two, gain_part = norm_back_rows(grad_ref[span(j)], gain_ref[...], upstream)
        grad_ref[span(j)] = grad_two
        gain_grad[...] += gain_part
        grad_low_ref[span(j)] = grad_two.astype(jnp.bfloat16)
        to_end(grad_low_ref, j).start()

    def exchange(i):
        to_inner(i).wait_recv()
        stage[i] = (own[span(i)] + from_end[i].astype(jnp.float32)).astype(jnp.bfloat16)
        to_middle(i).start()

        @pl.when(i >= line_lag)
        def _():
            settle(i - line_lag)

    def back_tile(t):
        @pl.when(t >= 2)
        def _():
            store(t - 2).wait()

        total[...] = jnp.zeros_like(total)
        first_logits(t)
        for k in range(pieces):
            next_logits(k)
            slope_unit(t, k)
            if k >= 1:
                add_rows(t, k - 1)
            if k >= pieces - group:

                @pl.when(inner & (t >= 1))
                def _():
                    exchange((t - 1) * group + k - (pieces - group))

        add_rows(t, pieces - 1)
        store(t).start()

        @pl.when(inner)
        def _():
            own[over(t)] = total[...]

        @pl.when(jnp.logical_not(inner))
        def _():
            def push(c):
                stage[t * group + c] = total[span(c)].astype(jnp.bfloat16)
                to_inner(t * group + c).start()

            repeat(0, group, push)

    repeat(0, tiles, back_tile)

    @pl.when(jnp.logical_not(inner))
    def _():
        def finish(i):
            to_end(grad_low_ref, i).wait_recv()
            to_inner(i).wait_send()

        repeat(0, count, finish)

    @pl.when(inner)
    def _():
        repeat(count - group, count, exchange)
        repeat(count - line_lag, count, settle)

        def drain(i):
            to_middle(i).wait_send()
            to_end(grad_low_ref, i).wait_send()

        repeat(0, count, drain)

    store(tiles - 2).wait()
    store(tiles - 1).wait()


def head_line(part, stream, gain, weights, wanted, weight_rows, vocab, collective_id):
    tokens, width = part.shape
    rows, columns = 64, 256
    count = tokens // rows
    chunks = pltpu.VMEM((count, rows, width), jnp.bfloat16)
    rows_low = jax.ShapeDtypeStruct((tokens, width), jnp.bfloat16)
    along = jax.ShapeDtypeStruct((1, tokens), jnp.float32)
    line_sems = pltpu.SemaphoreType.DMA((count,))
    return pl.pallas_call(
        functools.partial(head_line_kernel, vocab_tile(vocab)),
        out_shape=[
            rows_low,
            rows_low,
            jax.ShapeDtypeStruct((tokens, width), jnp.float32),
            jax.ShapeDtypeStruct((1, width), jnp.float32),
            along,
            along,
            jax.ShapeDtypeStruct((vocab, tokens), jnp.bfloat16),
        ],
        in_specs=[whole_vmem] * 3 + [whole_any] + [whole_vmem] * 2,
        out_specs=[whole_vmem] * 6 + [whole_any],
        scratch_shapes=[
            pltpu.VMEM((2, vocab_tile(vocab), columns), jnp.float32),
            pltpu.VMEM((vocab, width), jnp.bfloat16),
            chunks,
            chunks,
            chunks,
            pltpu.VMEM((tokens, width), jnp.float32),
            pltpu.VMEM((width, columns), jnp.bfloat16),
            pltpu.VMEM((2, tokens), jnp.float32),
            pltpu.VMEM((3, 2, tokens), jnp.float32),
            pltpu.VMEM((2, vocab, columns), jnp.bfloat16),
            pltpu.VMEM((columns, width), jnp.float32),
            pltpu.SemaphoreType.DMA,
        ]
        + [line_sems] * 5
        + [pltpu.SemaphoreType.DMA((3,))] * 2
        + [pltpu.SemaphoreType.DMA((2,))],
        compiler_params=pltpu.CompilerParams(
            collective_id=collective_id, has_side_effects=True, vmem_limit_bytes=62 << 20
        ),
    )(part, stream, gain, weights, wanted, weight_rows)


def weight_grads_kernel(
    tile_units, tiles, place_ref, slope_ref, rows_ref, ids_ref, zero_ref, joint_ref, normed_ref,
    attended_ref, grad_ref, out_ref, made, sem,
):
    step = pl.program_id(0)
    unit_rows = out_ref.shape[1]
    buffer = lax.rem(step, 2)
    last_units = joint_ref.shape[0] // unit_rows + attended_ref.shape[0] // unit_rows

    def settle(which, count):
        pltpu.make_async_copy(
            made.at[which, pl.ds(0, count)], made.at[which, pl.ds(0, count)], sem.at[which]
        ).wait()

    def send(first, count):
        def push(u, carry):
            pltpu.make_async_copy(
                made.at[buffer, u], out_ref.at[place_ref[first + u]], sem.at[buffer]
            ).start()
            return carry

        lax.fori_loop(0, count, push, 0)

    @pl.when(step >= 2)
    def _():
        settle(buffer, tile_units)

    @pl.when(step < tiles)
    def _():
        row = lax.broadcasted_iota(jnp.int32, slope_ref.shape, 0)
        seen = jnp.where(row == ids_ref[...] - step * slope_ref.shape[0], 1.0, 0.0).astype(jnp.bfloat16)
        made[buffer] = (
            jnp.dot(slope_ref[...], rows_ref[...], preferred_element_type=jnp.float32)
            + jnp.dot(seen, zero_ref[...], preferred_element_type=jnp.float32)
        ).astype(jnp.bfloat16).reshape(tile_units, unit_rows, -1)
        send(step * tile_units, tile_units)

    @pl.when(step == tiles)
    def _():
        joint_units = joint_ref.shape[0] // unit_rows
        made[buffer, pl.ds(0, joint_units)] = jnp.dot(
            joint_ref[...], normed_ref[...], preferred_element_type=jnp.float32
        ).astype(jnp.bfloat16).reshape(joint_units, unit_rows, -1)
        made[buffer, pl.ds(joint_units, last_units - joint_units)] = jnp.dot(
            attended_ref[...], grad_ref[...], preferred_element_type=jnp.float32
        ).astype(jnp.bfloat16).reshape(last_units - joint_units, unit_rows, -1)
        send(tiles * tile_units, last_units)
        settle(1 - buffer, tile_units)
        settle(buffer, last_units)


def weight_grads(place, slots, unit_rows, slope, rows, ids, zero, joint, normed, attended, grad):
    vocab, tokens = slope.shape
    width = rows.shape[1]
    tile = vocab_tile(vocab)
    tiles = vocab // tile
    fixed = lambda k: (0, 0)
    whole = lambda x: pl.BlockSpec(x.shape, fixed)
    return pl.pallas_call(
        functools.partial(weight_grads_kernel, tile // unit_rows, tiles),
        grid=(tiles + 1,),
        out_shape=jax.ShapeDtypeStruct((slots, unit_rows, width), jnp.bfloat16),
        in_specs=[
            pl.BlockSpec(memory_space=pltpu.SMEM),
            pl.BlockSpec((tile, tokens), lambda k: (jnp.minimum(k, tiles - 1), 0)),
        ]
        + [whole(x) for x in (rows, ids, zero, joint, normed, attended, grad)],
        out_specs=whole_any,
        scratch_shapes=[
            pltpu.VMEM((2, tile // unit_rows, unit_rows, width), jnp.bfloat16),
            pltpu.SemaphoreType.DMA((2,)),
        ],
        compiler_params=pltpu.CompilerParams(vmem_limit_bytes=60 << 20),
    )(place, slope, rows, ids, zero, joint, normed, attended, grad)


def adam_update(weight, moment_one, moment_two, gradient, step_rate, decay_factor):
    moment_new = beta_first * moment_one + (1.0 - beta_first) * gradient
    square_new = beta_second * moment_two + (1.0 - beta_second) * gradient * gradient
    moment_hat = moment_new / (1.0 - beta_first**STEP)
    square_hat = square_new / (1.0 - beta_second**STEP)
    weight_new = weight - step_rate * (
        moment_hat / (jnp.sqrt(square_hat) + adam_epsilon) + decay_factor * weight
    )
    return (weight_new, moment_new, square_new)


def norm_forward(values, gain_row):
    return values * inverse_rms(values) * gain_row


def slot_tables(owner_ids, owners, most_units):
    unit_count = owner_ids.shape[0]
    unit_index = jnp.arange(unit_count, dtype=jnp.int32)
    earlier = (owner_ids[None, :] == owner_ids[:, None]) & (
        unit_index[None, :] < unit_index[:, None]
    )
    unit_rank = jnp.sum(earlier.astype(jnp.int32), 1)
    placed = (owner_ids[None, None, :] == jnp.arange(owners, dtype=jnp.int32)[:, None, None]) & (
        unit_rank[None, None, :] == jnp.arange(most_units, dtype=jnp.int32)[None, :, None]
    )
    slot_filled = jnp.any(placed, 2)
    slot_unit = jnp.sum(jnp.where(placed, unit_index[None, None, :], 0), 2)
    return (unit_rank, slot_unit, slot_filled)


def unit_rates(unit_ids, table_units, query_units, value_units):
    return jnp.where(
        unit_ids < table_units,
        rate_table,
        jnp.where(
            unit_ids < query_units,
            rate_query,
            jnp.where(unit_ids < value_units, rate_values, rate_project),
        ),
    )


def pair_slots(route_pairs, priorities, experts, capacity):
    tokens_here = priorities.shape[0]
    pair_expert = route_pairs.T.reshape(-1)
    pair_key = (
        jnp.arange(2, dtype=jnp.int32)[:, None] * tokens_here + priorities[None, :]
    ).reshape(-1)
    before = (pair_expert[None, :] == pair_expert[:, None]) & (
        pair_key[None, :] < pair_key[:, None]
    )
    pair_rank = jnp.sum(before.astype(jnp.int32), 1)
    pair_kept = pair_rank < capacity
    pair_dest = pair_expert * capacity + jnp.minimum(pair_rank, capacity - 1)
    return (pair_kept, pair_dest)


def gelu_tanh(values):
    return jax.nn.gelu(values, approximate=True)


def gelu_slope(values):
    root = math.sqrt(2.0 / math.pi)
    bent = jnp.tanh(root * (values + 0.044715 * values * values * values))
    return 0.5 * (1.0 + bent) + 0.5 * values * (1.0 - bent * bent) * root * (
        1.0 + 3.0 * 0.044715 * values * values
    )


def plane_peer(step):
    chip, core = lax.axis_index("dp"), lax.axis_index("ctx")
    row = lax.rem(chip // 2 + step // 4, 2)
    column = lax.rem(lax.rem(chip, 2) + lax.rem(step // 2, 2), 2)
    place = {"dp": row * 2 + column, "ctx": lax.rem(core + lax.rem(step, 2), 2)}
    return place, place["dp"] * 2 + place["ctx"]


def greet_plane():
    barrier = pltpu.get_barrier_semaphore()
    for step in range(1, 8):
        place, _ = plane_peer(step)
        pl.semaphore_signal(barrier, inc=1, device_id=place, device_id_type=MESH_ID)
    pl.semaphore_wait(barrier, 7)


def plane_copy(source, target, send_sem, recv_sem, step):
    place, _ = plane_peer(step)
    return pltpu.make_async_remote_copy(
        src_ref=source.at[step],
        dst_ref=target.at[step],
        send_sem=send_sem.at[step],
        recv_sem=recv_sem.at[step],
        device_id=place,
        device_id_type=MESH_ID,
    )


def slot_hits(dest_rows, expert, capacity, tokens):
    slot = lax.broadcasted_iota(jnp.int32, (capacity, tokens), 0) + expert * capacity
    return (slot == dest_rows[0:1, :]) | (slot == dest_rows[1:2, :])


def token_hits(dest_columns, expert, capacity, tokens):
    slot = lax.broadcasted_iota(jnp.int32, (tokens, capacity), 1) + expert * capacity
    hit = (slot == dest_columns[:, 0:1]) | (slot == dest_columns[:, 1:2])
    return jnp.where(hit, 1.0, 0.0).astype(jnp.bfloat16)


def gate_of(routes, gates, expert, axis):
    pick = (lambda a, k: a[k : k + 1, :]) if axis == 0 else (lambda a, k: a[:, k : k + 1])
    return jnp.where(pick(routes, 0) == expert, pick(gates, 0), 0.0) + jnp.where(
        pick(routes, 1) == expert, pick(gates, 1), 0.0
    )


def arrival(i):
    return jnp.where(i < 2, i, 9 - i)


def experts_kernel(
    rows_ref, dest_rows, dest_columns, gates, routes, inner_full, outer_full, counts_ref,
    mix_ref, arrived, returned, totals_ref,
    inner_ref, outer_ref, outgoing, results, counts, send_one, recv_one, send_two, recv_two, send_count, recv_count,
):
    capacity = arrived.shape[1]
    tokens = rows_ref.shape[0]
    greet_plane()
    counts[0] = counts_ref[...]

    def send_counts(step, carry):
        place, _ = plane_peer(step)
        pltpu.make_async_remote_copy(
            src_ref=counts_ref,
            dst_ref=counts.at[step],
            send_sem=send_count.at[step],
            recv_sem=recv_count.at[step],
            device_id=place,
            device_id_type=MESH_ID,
        ).start()
        return carry

    def dispatch(i, carry):
        step = 7 - i
        _, expert = plane_peer(step)
        hit = jnp.where(slot_hits(dest_rows, expert, capacity, tokens), 1.0, 0.0).astype(jnp.bfloat16)
        rows = jnp.dot(hit, rows_ref[...], preferred_element_type=jnp.float32).astype(jnp.bfloat16)

        @pl.when(step > 0)
        def _():
            outgoing[step] = rows
            plane_copy(outgoing, arrived, send_one, recv_one, step).start()

        @pl.when(step == 0)
        def _():
            arrived[0] = rows

        return carry

    def work(i, carry):
        step = arrival(i)

        @pl.when(step > 0)
        def _():
            plane_copy(outgoing, arrived, send_one, recv_one, step).wait_recv()

        before = jnp.dot(arrived[step], inner_ref[...], preferred_element_type=jnp.float32)
        active = gelu_tanh(before).astype(jnp.bfloat16)
        part = jnp.dot(active, outer_ref[...], preferred_element_type=jnp.float32).astype(jnp.bfloat16)

        @pl.when(step > 0)
        def _():
            results[step] = part
            plane_copy(results, returned, send_two, recv_two, step).start()

        @pl.when(step == 0)
        def _():
            returned[0] = part

        return carry

    def combine(i, carry):
        step = arrival(i)
        _, expert = plane_peer(step)
        hit = token_hits(dest_columns, expert, capacity, tokens)
        gate = gate_of(routes, gates, expert, 1)

        @pl.when(step > 0)
        def _():
            plane_copy(results, returned, send_two, recv_two, step).wait_recv()

        part = gate * jnp.dot(hit, returned[step], preferred_element_type=jnp.float32)

        @pl.when(i == 0)
        def _():
            mix_ref[...] = part

        @pl.when(i > 0)
        def _():
            mix_ref[...] += part

        return carry

    def finish(step, carry):
        plane_copy(outgoing, arrived, send_one, recv_one, step).wait_send()
        plane_copy(results, returned, send_two, recv_two, step).wait_send()
        place, _ = plane_peer(step)
        pltpu.make_async_remote_copy(
            src_ref=counts_ref,
            dst_ref=counts.at[step],
            send_sem=send_count.at[step],
            recv_sem=recv_count.at[step],
            device_id=place,
            device_id_type=MESH_ID,
        ).wait()
        return carry

    lax.fori_loop(0, 8, dispatch, 0)
    lax.fori_loop(1, 8, send_counts, 0)
    inner_ref[...] = inner_full[...].astype(jnp.bfloat16)
    outer_ref[...] = outer_full[...].astype(jnp.bfloat16)
    lax.fori_loop(0, 8, work, 0)
    lax.fori_loop(0, 8, combine, 0)
    lax.fori_loop(1, 8, finish, 0)
    totals_ref[...] = jnp.sum(counts[...], 0)


def experts_forward(rows, dest, gates, routes, inner, outer, counts, capacity, collective_id):
    tokens, width = rows.shape
    buffer = pltpu.VMEM((8, capacity, width), jnp.bfloat16)
    return pl.pallas_call(
        experts_kernel,
        out_shape=[
            jax.ShapeDtypeStruct((tokens, width), jnp.float32),
            jax.ShapeDtypeStruct((8, capacity, width), jnp.bfloat16),
            jax.ShapeDtypeStruct((8, capacity, width), jnp.bfloat16),
            jax.ShapeDtypeStruct(counts.shape, jnp.float32),
        ],
        in_specs=[whole_vmem] * 8,
        out_specs=[whole_vmem] * 4,
        scratch_shapes=[pltpu.VMEM(w.shape, jnp.bfloat16) for w in (inner, outer)]
        + [buffer, buffer, pltpu.VMEM((8,) + counts.shape, jnp.float32)]
        + [pltpu.SemaphoreType.DMA((8,))] * 6,
        compiler_params=pltpu.CompilerParams(
            collective_id=collective_id, has_side_effects=True, vmem_limit_bytes=60 << 20
        ),
    )(rows, dest, dest.T, gates, routes, inner, outer, counts)


def experts_back_kernel(
    rows_ref, dest_rows, dest_columns, gates, routes, returned, arrived, *refs
):
    inner_full, outer_full, grad_ref, gate_ref, inner_grad, outer_grad, inner_ref, outer_ref = refs[:8]
    outgoing, landed, results, landed_two, active, slopes = refs[8:14]
    send_one, recv_one, send_two, recv_two = refs[14:]
    capacity = arrived.shape[1]
    tokens = rows_ref.shape[0]
    greet_plane()
    gate_ref[...] = jnp.zeros_like(gate_ref)

    def dispatch(i, carry):
        step = 7 - i
        _, expert = plane_peer(step)
        hit = slot_hits(dest_rows, expert, capacity, tokens)
        rows = jnp.dot(
            jnp.where(hit, 1.0, 0.0).astype(jnp.bfloat16), rows_ref[...], preferred_element_type=jnp.float32
        )
        scale = jnp.sum(jnp.where(hit, gate_of(routes, gates, expert, 0), 0.0), 1, keepdims=True)
        sent = (rows * scale).astype(jnp.bfloat16)

        @pl.when(step > 0)
        def _():
            outgoing[step] = sent
            plane_copy(outgoing, landed, send_one, recv_one, step).start()

        @pl.when(step == 0)
        def _():
            landed[0] = sent

        dots = jnp.sum(rows * returned[step].astype(jnp.float32), 1, keepdims=True)
        part = jnp.sum(jnp.where(hit, dots, 0.0), 0, keepdims=True)
        for k in range(2):
            gate_ref[k : k + 1, :] += jnp.where(routes[k : k + 1, :] == expert, part, 0.0)
        return carry

    def work(i, carry):
        step = arrival(i)

        @pl.when(step > 0)
        def _():
            plane_copy(outgoing, landed, send_one, recv_one, step).wait_recv()

        grad_active = lax.dot_general(
            landed[step], outer_ref[...], (((1,), (1,)), ((), ())), preferred_element_type=jnp.float32
        )
        before = jnp.dot(arrived[step], inner_ref[...], preferred_element_type=jnp.float32)
        slope = (grad_active * gelu_slope(before)).astype(jnp.bfloat16)
        back = lax.dot_general(
            slope, inner_ref[...], (((1,), (1,)), ((), ())), preferred_element_type=jnp.float32
        ).astype(jnp.bfloat16)

        @pl.when(step > 0)
        def _():
            results[step] = back
            plane_copy(results, landed_two, send_two, recv_two, step).start()

        @pl.when(step == 0)
        def _():
            landed_two[0] = back

        slopes[step] = slope
        active[step] = gelu_tanh(before).astype(jnp.bfloat16)
        return carry

    def weigh(step, carry):
        outer_part = lax.dot_general(
            active[step], landed[step], (((0,), (0,)), ((), ())), preferred_element_type=jnp.float32
        )
        inner_part = lax.dot_general(
            arrived[step], slopes[step], (((0,), (0,)), ((), ())), preferred_element_type=jnp.float32
        )

        @pl.when(step == 0)
        def _():
            inner_grad[...] = inner_part
            outer_grad[...] = outer_part

        @pl.when(step > 0)
        def _():
            inner_grad[...] += inner_part
            outer_grad[...] += outer_part

        return carry

    def combine(i, carry):
        step = arrival(i)
        _, expert = plane_peer(step)
        hit = token_hits(dest_columns, expert, capacity, tokens)

        @pl.when(step > 0)
        def _():
            plane_copy(results, landed_two, send_two, recv_two, step).wait_recv()

        part = jnp.dot(hit, landed_two[step], preferred_element_type=jnp.float32)

        @pl.when(i == 0)
        def _():
            grad_ref[...] = part

        @pl.when(i > 0)
        def _():
            grad_ref[...] += part

        return carry

    def finish(step, carry):
        plane_copy(outgoing, landed, send_one, recv_one, step).wait_send()
        plane_copy(results, landed_two, send_two, recv_two, step).wait_send()
        return carry

    lax.fori_loop(0, 8, dispatch, 0)
    inner_ref[...] = inner_full[...].astype(jnp.bfloat16)
    outer_ref[...] = outer_full[...].astype(jnp.bfloat16)
    lax.fori_loop(0, 8, work, 0)
    lax.fori_loop(0, 8, weigh, 0)
    lax.fori_loop(0, 8, combine, 0)
    lax.fori_loop(1, 8, finish, 0)


def experts_backward(rows, dest, gates, routes, returned, arrived, inner, outer, collective_id):
    tokens, width = rows.shape
    capacity = arrived.shape[1]
    inside = inner.shape[1]
    buffer = pltpu.VMEM((8, capacity, width), jnp.bfloat16)
    inside_buffer = pltpu.VMEM((8, capacity, inside), jnp.bfloat16)
    return pl.pallas_call(
        experts_back_kernel,
        out_shape=[
            jax.ShapeDtypeStruct((tokens, width), jnp.float32),
            jax.ShapeDtypeStruct((2, tokens), jnp.float32),
            jax.ShapeDtypeStruct((width, inside), jnp.float32),
            jax.ShapeDtypeStruct((inside, width), jnp.float32),
        ],
        in_specs=[whole_vmem] * 9,
        out_specs=[whole_vmem] * 4,
        scratch_shapes=[pltpu.VMEM(w.shape, jnp.bfloat16) for w in (inner, outer)]
        + [buffer] * 4
        + [inside_buffer] * 2
        + [pltpu.SemaphoreType.DMA((8,))] * 4,
        compiler_params=pltpu.CompilerParams(
            collective_id=collective_id, has_side_effects=True, vmem_limit_bytes=60 << 20
        ),
    )(rows, dest, dest.T, gates, routes, returned, arrived, inner, outer)


def own_units_kernel(
    chunks, units_of, slopes_ref, rows_ref, ids_ref, zero_ref, joint_ref, normed_ref, attended_ref,
    grad_ref, small_ref, grads_ref, small_out, *refs
):
    slopes, late, mixed, made, passing, own, other, relay, landed, small_landed, ready = refs[:11]
    other_send, other_recv, relay_send, relay_recv, landed_send, landed_recv = refs[11:17]
    small_send, small_recv, load_sem, store_sem = refs[17:]
    chip, core = lax.axis_index("dp"), lax.axis_index("ctx")
    beside = chip + 1 - 2 * lax.rem(chip, 2)
    across = lax.rem(chip + 2, 4)
    opposite = across + 1 - 2 * lax.rem(across, 2)
    places = (opposite, beside, across, chip)
    slots, unit_rows = own.shape[1:3]
    table_units = slopes.shape[0]
    tokens = rows_ref.shape[0]
    size = slots // chunks
    split = (chunks + 1) // 2
    load = pltpu.make_async_copy(slopes_ref, slopes, load_sem)
    load.start()
    greet_plane()

    def repeat(first, last, body):
        def step(i, carry):
            body(i)
            return carry

        lax.fori_loop(first, last, step, 0)

    def span(q):
        return pl.ds(q * size, size)

    def remote(source, target, send, recv, place):
        return pltpu.make_async_remote_copy(
            src_ref=source,
            dst_ref=target,
            send_sem=send,
            recv_sem=recv,
            device_id=place,
            device_id_type=MESH_ID,
        )

    def pass_over(k, q):
        return remote(
            passing.at[k % 2, span(q)],
            other.at[k, span(q)],
            other_send.at[k, q],
            other_recv.at[k, q],
            {"ctx": 1 - core},
        )

    def to_relay(q, place):
        return remote(own.at[0, span(q)], relay.at[span(q)], relay_send.at[q], relay_recv.at[q], {"dp": place})

    def to_owner(k, q):
        return remote(
            own.at[k, span(q)],
            landed.at[k - 1, span(q)],
            landed_send.at[k - 1, q],
            landed_recv.at[k - 1, q],
            {"dp": places[k]},
        )

    def small_copy(step):
        place, _ = plane_peer(step)
        return remote(
            small_ref, small_landed.at[chip * 2 + core], small_send.at[step], small_recv.at[step], place
        )

    joint_units = joint_ref.shape[0] // unit_rows
    late[pl.ds(0, joint_units)] = jnp.dot(
        joint_ref[...], normed_ref[...], preferred_element_type=jnp.float32
    ).reshape(joint_units, unit_rows, -1)
    last_units = attended_ref.shape[0] // unit_rows
    late[pl.ds(joint_units, last_units)] = jnp.dot(
        attended_ref[...], grad_ref[...], preferred_element_type=jnp.float32
    ).reshape(last_units, unit_rows, -1)
    load.wait()
    group = made.shape[0] // unit_rows

    def form(owner, target):
        def some(g):
            first = owner * slots + g * group

            def fill(s):
                unit = units_of[first + s]
                lines = pl.ds(pl.multiple_of(s * unit_rows, unit_rows), unit_rows)
                mixed[lines, :tokens] = slopes[jnp.minimum(unit, table_units - 1)]
                row = lax.broadcasted_iota(jnp.int32, (unit_rows, tokens), 0) + unit * unit_rows
                mixed[lines, tokens:] = jnp.where(row == ids_ref[...], 1.0, 0.0).astype(jnp.bfloat16)

            repeat(0, group, fill)
            made[...] = jnp.dot(
                mixed[:, :tokens], rows_ref[...], preferred_element_type=jnp.float32
            ) + jnp.dot(mixed[:, tokens:], zero_ref[...], preferred_element_type=jnp.float32)

            def put(s):
                unit = units_of[first + s]
                table_piece = made[pl.ds(pl.multiple_of(s * unit_rows, unit_rows), unit_rows)]
                late_piece = late[jnp.clip(unit - table_units, 0, late.shape[0] - 1)]
                marks = jnp.zeros(table_piece.shape, jnp.int32) + unit
                piece = jnp.where(marks < table_units, table_piece, late_piece)
                target[g * group + s] = piece.astype(jnp.bfloat16)

            repeat(0, group, put)

        repeat(0, slots // group, some)

    def joined(k, q):
        pass_over(k, q).wait_recv()
        return own[k, span(q)].astype(jnp.float32) + other[k, span(q)].astype(jnp.float32)

    def first_leg(place):
        def leg(q):
            own[0, span(q)] = joined(0, q).astype(jnp.bfloat16)
            to_relay(q, place).start()

        return leg

    def direct(k):
        def leg(q):
            own[k, span(q)] = joined(k, q).astype(jnp.bfloat16)
            to_owner(k, q).start()

        return leg

    def relayed(k, place):
        def leg(q):
            to_relay(q, place).wait_recv()
            total = joined(k, q) + relay[span(q)].astype(jnp.float32)
            own[k, span(q)] = total.astype(jnp.bfloat16)
            to_owner(k, q).start()

        return leg

    def form_pair(k):
        if k >= 2:
            repeat(0, chunks, lambda q: pass_over(k - 2, q).wait_send())
        form(places[k] * 2 + 1 - core, passing.at[k % 2])
        repeat(0, chunks, lambda q: pass_over(k, q).start())
        form(places[k] * 2 + core, own.at[k])

    form_pair(0)
    repeat(0, split, first_leg(beside))
    repeat(split, chunks, first_leg(across))
    repeat(1, 8, lambda step: small_copy(step).start())
    small_landed[chip * 2 + core] = small_ref[...]
    form_pair(1)
    repeat(0, split, direct(1))
    form_pair(2)
    repeat(split, chunks, direct(2))
    repeat(0, split, relayed(2, beside))
    repeat(split, chunks, relayed(1, across))
    form_pair(3)

    def store(q):
        return pltpu.make_async_copy(
            ready.at[lax.rem(q, 2)], grads_ref.at[span(q)], store_sem.at[lax.rem(q, 2)]
        )

    def keep(q):
        total = joined(3, q)
        to_owner(1, q).wait_recv()
        to_owner(2, q).wait_recv()

        @pl.when(q >= 2)
        def _():
            store(q - 2).wait()

        ready[lax.rem(q, 2)] = (
            total + landed[0, span(q)].astype(jnp.float32) + landed[1, span(q)].astype(jnp.float32)
        )
        store(q).start()

    repeat(0, chunks, keep)

    def finish(q):
        for k in (2, 3):
            pass_over(k, q).wait_send()
        to_owner(1, q).wait_send()
        to_owner(2, q).wait_send()

    repeat(0, chunks, finish)
    repeat(0, split, lambda q: to_relay(q, beside).wait_send())
    repeat(split, chunks, lambda q: to_relay(q, across).wait_send())
    repeat(1, 8, lambda step: small_copy(step).wait())
    total = small_landed[0]
    for source in range(1, 8):
        total = total + small_landed[source]
    small_out[...] = total
    for q in range(max(0, chunks - 2), chunks):
        store(q).wait()


def own_units(units_of, slots, unit_rows, slopes, rows, ids, zero, joint, normed, attended, grad, small, collective_id):
    tokens, width = rows.shape
    unit = (unit_rows, width)
    chunks = max(k for k in range(1, 8) if slots % k == 0)
    group = max(k for k in range(1, 8) if slots % k == 0)
    late = (joint.shape[0] + attended.shape[0]) // unit_rows
    slopes = slopes.reshape(-1, unit_rows, tokens)
    return pl.pallas_call(
        functools.partial(own_units_kernel, chunks),
        out_shape=[
            jax.ShapeDtypeStruct((slots,) + unit, jnp.float32),
            jax.ShapeDtypeStruct(small.shape, jnp.float32),
        ],
        in_specs=[pl.BlockSpec(memory_space=pltpu.SMEM), whole_any] + [whole_vmem] * 8,
        out_specs=[whole_any, whole_vmem],
        scratch_shapes=[
            pltpu.VMEM(slopes.shape, jnp.bfloat16),
            pltpu.VMEM((late,) + unit, jnp.float32),
            pltpu.VMEM((group * unit_rows, 2 * tokens), jnp.bfloat16),
            pltpu.VMEM((group * unit_rows, width), jnp.float32),
            pltpu.VMEM((2, slots) + unit, jnp.bfloat16),
            pltpu.VMEM((4, slots) + unit, jnp.bfloat16),
            pltpu.VMEM((4, slots) + unit, jnp.bfloat16),
            pltpu.VMEM((slots,) + unit, jnp.bfloat16),
            pltpu.VMEM((2, slots) + unit, jnp.bfloat16),
            pltpu.VMEM((8,) + small.shape, jnp.float32),
            pltpu.VMEM((2, slots // chunks) + unit, jnp.float32),
            pltpu.SemaphoreType.DMA((4, chunks)),
            pltpu.SemaphoreType.DMA((4, chunks)),
            pltpu.SemaphoreType.DMA((chunks,)),
            pltpu.SemaphoreType.DMA((chunks,)),
            pltpu.SemaphoreType.DMA((2, chunks)),
            pltpu.SemaphoreType.DMA((2, chunks)),
            pltpu.SemaphoreType.DMA((8,)),
            pltpu.SemaphoreType.DMA((8,)),
            pltpu.SemaphoreType.DMA,
            pltpu.SemaphoreType.DMA((2,)),
        ],
        compiler_params=pltpu.CompilerParams(
            collective_id=collective_id, has_side_effects=True, vmem_limit_bytes=63 << 20
        ),
    )(units_of, slopes, rows, ids, zero, joint, normed, attended, grad, small)


def to_plane(buffer):
    return lax.all_to_all(buffer, ("dp", "ctx"), split_axis=0, concat_axis=0, tiled=True)


def plain_hits(dest, experts, capacity):
    slots = lax.broadcasted_iota(jnp.int32, (experts * capacity, dest.shape[1]), 0)
    return [slots == dest[k : k + 1] for k in range(2)]


def plain_forward(rows, dest, gates, inner, outer, owners, capacity):
    width = rows.shape[1]
    hits = plain_hits(dest, owners, capacity)
    both = (hits[0] | hits[1]).astype(jnp.bfloat16)
    sent = jnp.dot(both, rows, preferred_element_type=jnp.float32).astype(jnp.bfloat16)
    arrived = to_plane(sent.reshape(owners, capacity, width))
    hidden = jnp.einsum("ocd,df->ocf", arrived, inner, preferred_element_type=jnp.float32)
    active = gelu_tanh(hidden).astype(jnp.bfloat16)
    part = jnp.einsum("ocf,fd->ocd", active, outer, preferred_element_type=jnp.float32)
    returned = to_plane(part.astype(jnp.bfloat16))
    flat = returned.reshape(owners * capacity, width)
    mix = sum(
        gates[:, k : k + 1]
        * lax.dot_general(
            hits[k].astype(jnp.bfloat16),
            flat,
            (((0,), (0,)), ((), ())),
            preferred_element_type=jnp.float32,
        )
        for k in range(2)
    )
    return (mix, arrived, returned)


def plain_backward(rows, dest, gates, returned, arrived, inner, outer):
    owners, capacity, width = arrived.shape
    hits = plain_hits(dest, owners, capacity)
    both = (hits[0] | hits[1]).astype(jnp.bfloat16)
    slot_scale = jnp.sum(
        jnp.where(hits[0], gates[0:1], 0.0) + jnp.where(hits[1], gates[1:2], 0.0), 1, keepdims=True
    )
    slot_grads = jnp.dot(both, rows, preferred_element_type=jnp.float32)
    sent = (slot_grads * slot_scale).astype(jnp.bfloat16)
    flat = returned.reshape(owners * capacity, width)
    dots = jnp.sum(slot_grads * flat.astype(jnp.float32), 1, keepdims=True)
    gate_part = jnp.concatenate(
        [jnp.sum(jnp.where(hit, dots, 0.0), 0, keepdims=True) for hit in hits], 0
    )
    landed = to_plane(sent.reshape(owners, capacity, width))
    grad_active = jnp.einsum("ocd,fd->ocf", landed, outer, preferred_element_type=jnp.float32)
    hidden = jnp.einsum("ocd,df->ocf", arrived, inner, preferred_element_type=jnp.float32)
    active = gelu_tanh(hidden).astype(jnp.bfloat16)
    slope = (grad_active * gelu_slope(hidden)).astype(jnp.bfloat16)
    outer_grad = jnp.einsum("ocf,ocd->fd", active, landed, preferred_element_type=jnp.float32)
    inner_grad = jnp.einsum("ocd,ocf->df", arrived, slope, preferred_element_type=jnp.float32)
    back = jnp.einsum("ocf,df->ocd", slope, inner, preferred_element_type=jnp.float32)
    back = to_plane(back.astype(jnp.bfloat16)).reshape(owners * capacity, width)
    grad = lax.dot_general(
        both, back, (((0,), (0,)), ((), ())), preferred_element_type=jnp.float32
    )
    return (grad, gate_part, inner_grad, outer_grad)


def on_device(
    token_ids,
    targets,
    counted,
    routes,
    priority,
    owner_of,
    master,
    master_first,
    master_second,
    expert_in,
    expert_in_first,
    expert_in_second,
    expert_out,
    expert_out_first,
    expert_out_second,
    norm_gains,
    norm_gains_first,
    norm_gains_second,
    router,
    router_first,
    router_second,
    rel_bias,
    rel_bias_first,
    rel_bias_second,
):
    owners = lax.axis_size(("dp", "ctx"))
    tensor_ranks = lax.axis_size("tensor")
    my_owner = lax.axis_index(("dp", "ctx"))
    my_rank = lax.axis_index("tensor")
    my_context = lax.axis_index("ctx")
    sequences, half_length = token_ids.shape
    tokens_here = sequences * half_length
    most_units = master.shape[2]
    unit_rows = master.shape[3]
    model_width = master.shape[4]
    vocab_here = VOCAB // tensor_ranks
    heads_here = rel_bias.shape[0]
    head_size = model_width // (heads_here * tensor_ranks)
    hidden_here = heads_here * head_size
    experts = router.shape[1]
    capacity = (18 * tokens_here + 8 * experts - 1) // (8 * experts)
    table_units = vocab_here // unit_rows
    query_units = table_units + 2 * hidden_here // unit_rows
    value_units = table_units + 3 * hidden_here // unit_rows
    embed_scale = math.sqrt(model_width)
    owner_ids = owner_of[:, 0]
    on_square = lax.axis_size("dp") == 4 and lax.axis_size("ctx") == 2
    unit_rank, slot_unit, slot_filled = slot_tables(owner_ids, owners, most_units)
    counted_rows = counted.reshape(tokens_here, 2).T.astype(jnp.float32)
    loss_weights = counted_rows * jnp.array([[1.0], [ahead_weight]], jnp.float32)
    counts = jnp.zeros((8, 128), jnp.float32).at[0:2].set(jnp.sum(counted_rows, 1, keepdims=True))
    unit_slots = owner_ids * most_units + unit_rank
    route_pairs = routes.reshape(tokens_here, 2)
    pair_kept, pair_dest = pair_slots(route_pairs, priority[0], experts, capacity)
    dest = jnp.where(pair_kept, pair_dest, -1).reshape(2, tokens_here)
    unit_slots, dest = lax.optimization_barrier((unit_slots, dest))
    local_ids = token_ids.reshape(-1) - my_rank * vocab_here
    inside = (local_ids >= 0) & (local_ids < vocab_here)
    clipped_ids = jnp.clip(local_ids, 0, vocab_here - 1)
    unit_starts = jnp.sum(
        jnp.where(
            (clipped_ids // unit_rows)[None, :] == jnp.arange(unit_slots.shape[0])[:, None],
            unit_slots[:, None] * unit_rows,
            0,
        ),
        0,
    )
    slot_rows = unit_starts + clipped_ids % unit_rows
    if on_square:
        slot_rows = jnp.where(inside, slot_rows, -1)[:, None]
        weights_low, embedded, normed_one_low, joint = embed(
            unit_slots,
            master[0, 0],
            slot_rows,
            norm_gains[0:1],
            table_units,
            3 * hidden_here,
            11,
        )
    else:
        master_low = master[0, 0].astype(jnp.bfloat16)
        gathered = lax.all_gather(master_low, ("dp", "ctx"), axis=0, tiled=True)
        looked = jnp.take(gathered.reshape(-1, model_width), slot_rows, axis=0)
        looked = jnp.where(inside[:, None], looked, 0)
        weights_low = pull_units([gathered], unit_slots)
        (embedded,) = sum_line(looked, [], [], keep_total, 1)
    weights_low = weights_low.reshape(-1, model_width)
    joint_low = weights_low[vocab_here : vocab_here + 3 * hidden_here]
    project_low = weights_low[vocab_here + 3 * hidden_here :]
    rolled = [project_low] + [
        lax.ppermute(project_low, "tensor", [(source, (source + step) % 4) for source in range(4)])
        for step in (1, 2, 3)
    ]
    gain_rows = [norm_gains[k : k + 1] for k in range(3)]
    stream_shape = jax.ShapeDtypeStruct((tokens_here, model_width), jnp.float32)
    gain_shape = jax.ShapeDtypeStruct((1, model_width), jnp.float32)
    if not on_square:
        stream_zero = embedded.astype(jnp.float32) * embed_scale
        normed_one_low = norm_forward(stream_zero, norm_gains[0]).astype(jnp.bfloat16)
        joint = lax.dot_general(
            joint_low, normed_one_low, (((1,), (1,)), ((), ())), preferred_element_type=jnp.float32
        ).astype(jnp.bfloat16)
    attended_all, logsum_rows, pairs_before = attention(rel_bias, joint, heads_here, head_size, 2)
    attended = lax.dynamic_index_in_dim(attended_all, my_rank, 0, keepdims=False)
    router_low = router.astype(jnp.bfloat16)
    stream_one, normed_two_low, gate_rows, gate_columns = middle(
        attended_all.reshape(model_width, tokens_here),
        rolled,
        embedded,
        gain_rows[1],
        router_low.T,
        route_pairs.T,
    )
    if on_square:
        moe_partial, arrived, returned, counts = experts_forward(
            normed_two_low, dest, gate_columns, route_pairs, expert_in[0], expert_out[0], counts, capacity, 8
        )
    else:
        inner_low, outer_low = expert_in[0].astype(jnp.bfloat16), expert_out[0].astype(jnp.bfloat16)
        moe_partial, arrived, returned = plain_forward(
            normed_two_low, dest, gate_columns, inner_low, outer_low, owners, capacity
        )
        counts = lax.psum(counts, ("dp", "ctx"))
    weight_total = counts[0, 0] + ahead_weight * counts[1, 0]
    local_targets = targets.reshape(tokens_here, 2).T - my_rank * vocab_here
    weight_rows = jnp.concatenate(
        [
            loss_weights,
            loss_weights[0:1] + loss_weights[1:2],
            jnp.broadcast_to(1.0 / weight_total, (1, tokens_here)),
        ],
        0,
    )
    head_low, grad_two_low, grad_two, gain_grad_three, logsum_vocab, target_sums, slopes = head_line(
        moe_partial, stream_one, gain_rows[2], weights_low, local_targets, weight_rows, vocab_here, 3
    )
    if on_square:
        moe_grad_part, gate_part, inner_grad, outer_grad = experts_backward(
            grad_two_low,
            dest,
            gate_rows,
            route_pairs.T,
            returned,
            arrived,
            expert_in[0],
            expert_out[0],
            9,
        )
    else:
        moe_grad_part, gate_part, inner_grad, outer_grad = plain_backward(
            grad_two_low, dest, gate_rows, returned, arrived, inner_low, outer_low
        )
    gate_part = jnp.concatenate([gate_part, target_sums, jnp.zeros_like(target_sums)], 0)
    gate_block = pltpu.VMEM((3, 4, tokens_here), jnp.float32)
    grad_one_low, grad_one, logit_grad, target_total, gain_grad_two = sum_line(
        moe_grad_part,
        [
            stream_one,
            gain_rows[1],
            grad_two,
            gate_part,
            gate_rows,
            route_pairs.T,
            router_low,
        ],
        [
            stream_shape,
            jax.ShapeDtypeStruct((experts, tokens_here), jnp.bfloat16),
            jax.ShapeDtypeStruct((1, tokens_here), jnp.float32),
            gain_shape,
        ],
        finish_expert_grad,
        5,
        prologue=start_router_grad,
        scratch=(gate_block, pltpu.SemaphoreType.DMA((3,)), pltpu.SemaphoreType.DMA((3,))),
        opening=send_gate_parts,
    )
    router_grad = jnp.dot(logit_grad, normed_two_low, preferred_element_type=jnp.float32)
    loss_local = jnp.sum(weight_rows[2:3] * logsum_vocab) - jnp.sum(target_total)
    query_grad, pair_grad, before_grad, bias_lines, *expert_states = attention_back(
        rel_bias,
        joint,
        pairs_before,
        logsum_rows,
        grad_one_low,
        project_low,
        (
            expert_in[0],
            expert_in_first[0],
            expert_in_second[0],
            inner_grad,
            expert_out[0],
            expert_out_first[0],
            expert_out_second[0],
            outer_grad,
        ),
        heads_here,
        head_size,
    )
    grad_after = passed_along(before_grad, "ctx", -1)
    pair_grad_low = (pair_grad + grad_after.astype(jnp.float32)).astype(jnp.bfloat16)
    joint_grad = jnp.concatenate([query_grad, pair_grad_low], 0)
    distances = 2 * (half_length // BLOCK)
    bias_grad = jnp.sum(bias_lines, 1).reshape(heads_here, distances)
    zero_grad_low, gain_grads = sum_line(
        lax.dot_general(
            joint_grad, joint_low, (((0,), (0,)), ((), ())), preferred_element_type=jnp.float32
        ),
        [embedded, gain_rows[0], grad_one, gain_grad_two, gain_grad_three],
        [jax.ShapeDtypeStruct((8, model_width), jnp.float32)],
        functools.partial(finish_input_grad, embed_scale),
        6,
        prologue=clear_gain,
        scratch=(pltpu.SemaphoreType.DMA, pltpu.SemaphoreType.DMA),
        ending=share_gains,
    )
    my_units = jnp.take(slot_unit, my_owner, axis=0)
    my_filled = jnp.take(slot_filled, my_owner, axis=0)[:, None, None]
    bias_row = jnp.concatenate([bias_grad.reshape(-1), loss_local[None]])
    bias_row = jnp.pad(bias_row, (0, model_width - bias_row.shape[0]))[None]
    small = jnp.concatenate([gain_grads[:3], router_grad, bias_row], 0)
    small = jnp.pad(small, ((0, -small.shape[0] % 8), (0, 0)))
    slot_rates = unit_rates(my_units, table_units, query_units, value_units)[:, None, None]
    states = (master[0, 0], master_first[0, 0], master_second[0, 0])
    grad_rows = (
        slopes,
        head_low,
        local_ids[None, :],
        zero_grad_low,
        joint_grad,
        normed_one_low,
        attended,
        grad_one_low,
    )
    if on_square:
        mine, small = own_units(slot_unit.reshape(-1), most_units, unit_rows, *grad_rows, small, 10)
    else:
        outgoing = weight_grads(unit_slots, owners * most_units, unit_rows, *grad_rows)
        mine = lax.psum_scatter(
            outgoing.astype(jnp.float32), ("dp", "ctx"), scatter_dimension=0, tiled=True
        )
        small = lax.psum(small, ("dp", "ctx"))
    states = adam_update(*states, jnp.where(my_filled, mine, 0.0), slot_rates, decay_rate)
    gains_grad = small[:3]
    router_grad = small[3 : 3 + experts].T
    bias_grad = small[3 + experts, : rel_bias.size].reshape(rel_bias.shape)
    loss_totals = jnp.stack([small[3 + experts, rel_bias.size], weight_total])
    gains_new, gains_first_new, gains_second_new = adam_update(
        norm_gains, norm_gains_first, norm_gains_second, gains_grad, rate_gains, 0.0
    )
    router_new, router_first_new, router_second_new = adam_update(
        router, router_first, router_second, router_grad, rate_router, decay_rate
    )
    biases_new, biases_first_new, biases_second_new = adam_update(
        rel_bias, rel_bias_first, rel_bias_second, bias_grad, rate_biases, 0.0
    )
    return (
        loss_totals,
        *(state[None, None] for state in states),
        *(state[None] for state in expert_states),
        gains_new,
        gains_first_new,
        gains_second_new,
        router_new,
        router_first_new,
        router_second_new,
        biases_new,
        biases_first_new,
        biases_second_new,
    )


def solution(mesh):
    in_specs = (
        P("dp", "ctx"),
        P("dp", "ctx", None),
        P("dp", "ctx", None),
        P("dp", "ctx", None),
        P(("dp", "ctx"), None),
        P(),
        P("tensor", ("dp", "ctx"), None, None, None),
        P("tensor", ("dp", "ctx"), None, None, None),
        P("tensor", ("dp", "ctx"), None, None, None),
        P(("dp", "ctx"), None, "tensor"),
        P(("dp", "ctx"), None, "tensor"),
        P(("dp", "ctx"), None, "tensor"),
        P(("dp", "ctx"), "tensor", None),
        P(("dp", "ctx"), "tensor", None),
        P(("dp", "ctx"), "tensor", None),
        P(),
        P(),
        P(),
        P(),
        P(),
        P(),
        P("tensor", None),
        P("tensor", None),
        P("tensor", None),
    )
    out_specs = (
        P(),
        P("tensor", ("dp", "ctx"), None, None, None),
        P("tensor", ("dp", "ctx"), None, None, None),
        P("tensor", ("dp", "ctx"), None, None, None),
        P(("dp", "ctx"), None, "tensor"),
        P(("dp", "ctx"), None, "tensor"),
        P(("dp", "ctx"), None, "tensor"),
        P(("dp", "ctx"), "tensor", None),
        P(("dp", "ctx"), "tensor", None),
        P(("dp", "ctx"), "tensor", None),
        P(),
        P(),
        P(),
        P(),
        P(),
        P(),
        P("tensor", None),
        P("tensor", None),
        P("tensor", None),
    )
    return jax.shard_map(
        on_device, mesh=mesh, in_specs=in_specs, out_specs=out_specs, check_vma=False
    )
```

```python
import functools
import math

import jax
import jax.numpy as jnp
from jax import lax
from jax.experimental import pallas as pl
from jax.experimental.pallas import tpu as pltpu
from jax.sharding import PartitionSpec as P

VOCAB = 32000
BLOCK = 256
STEP = 10


highest_precision = lax.Precision.HIGHEST
beta_first = 0.9
beta_second = 0.95
adam_epsilon = 1e-08
norm_epsilon = 1e-06
ahead_weight = 0.3
masked_score = -1e30
rate_table = 0.1
rate_query = 0.05
rate_values = 0.05
rate_project = 0.5
rate_inner = 0.05
rate_outer = 0.03
rate_gains = 0.5
rate_router = 0.05
rate_biases = 0.5
decay_rate = 0.1


MESH_ID = pl.DeviceIdType.MESH
whole_vmem = pl.BlockSpec(memory_space=pltpu.VMEM)
whole_any = pl.BlockSpec(memory_space=pl.ANY)
line_lag = 2


def sum_line_kernel(
    rows, count, opening, with_core, prologue, epilogue, ending, n_extra, n_aux, n_scratch, *refs
):
    extras = refs[:n_extra]
    out_ref = refs[n_extra]
    aux = refs[n_extra + 1 : n_extra + 1 + n_aux]
    rest = refs[n_extra + 1 + n_aux :]
    scratch = rest[:n_scratch]
    part_ref = scratch[-1] if with_core else extras[0]
    extras = extras if with_core else extras[1:]
    stage, from_end, from_mid, send_sem, end_sem, mid_sem, back_sem, back_recv = rest[n_scratch:]
    rank = lax.axis_index("tensor")
    inner = (rank == 1) | (rank == 2)
    end_peer = jnp.where(rank < 2, 1 - rank, 5 - rank)
    mid_peer = 3 - rank
    barrier = pltpu.get_barrier_semaphore()
    if opening is None or with_core:
        pl.semaphore_signal(barrier, inc=1, device_id={"tensor": end_peer}, device_id_type=MESH_ID)
        if with_core:
            other_core = {"ctx": 1 - lax.axis_index("ctx")}
            pl.semaphore_signal(barrier, inc=1, device_id=other_core, device_id_type=MESH_ID)

        @pl.when(inner)
        def _():
            pl.semaphore_signal(
                barrier, inc=1, device_id={"tensor": mid_peer}, device_id_type=MESH_ID
            )
            pl.semaphore_wait(barrier, 2 + with_core)

        @pl.when(jnp.logical_not(inner))
        def _():
            pl.semaphore_wait(barrier, 1 + with_core)
    else:
        for step in (1, 2, 3):
            other = lax.rem(rank + step, 4)
            pl.semaphore_signal(barrier, inc=1, device_id={"tensor": other}, device_id_type=MESH_ID)
        pl.semaphore_wait(barrier, 3)

    def span(i):
        return pl.ds(pl.multiple_of(i * rows, rows), rows)

    def to_inner(i):
        return pltpu.make_async_remote_copy(
            src_ref=stage.at[i],
            dst_ref=from_end.at[i],
            send_sem=send_sem.at[i],
            recv_sem=end_sem.at[i],
            device_id={"tensor": end_peer},
            device_id_type=MESH_ID,
        )

    def to_middle(i):
        return pltpu.make_async_remote_copy(
            src_ref=stage.at[i],
            dst_ref=from_mid.at[i],
            send_sem=send_sem.at[i],
            recv_sem=mid_sem.at[i],
            device_id={"tensor": mid_peer},
            device_id_type=MESH_ID,
        )

    def to_end(i):
        return pltpu.make_async_remote_copy(
            src_ref=out_ref.at[span(i)],
            dst_ref=out_ref.at[span(i)],
            send_sem=back_sem.at[i],
            recv_sem=back_recv.at[i],
            device_id={"tensor": end_peer},
            device_id_type=MESH_ID,
        )

    if opening is not None:
        opening(rank, extras, aux, scratch)

    @pl.when(jnp.logical_not(inner))
    def _():
        def push(i, carry):
            stage[i] = part_ref[span(i)].astype(jnp.bfloat16)
            to_inner(i).start()
            return carry

        lax.fori_loop(0, count, push, 0)

    if prologue is not None:
        prologue(rank, inner, extras, aux, scratch)

    @pl.when(inner)
    def _():
        def step(i, carry):
            @pl.when(i < count)
            def _():
                to_inner(i).wait_recv()
                mine = part_ref[span(i)].astype(jnp.float32) + from_end[i].astype(jnp.float32)
                stage[i] = mine.astype(jnp.bfloat16)
                to_middle(i).start()

            @pl.when(i >= line_lag)
            def _():
                j = i - line_lag
                to_middle(j).wait_recv()
                total = stage[j].astype(jnp.float32) + from_mid[j].astype(jnp.float32)
                out_ref[span(j)] = epilogue(total, span(j), rank, extras, aux, scratch)
                to_end(j).start()

            return carry

        lax.fori_loop(0, count + line_lag, step, 0)

        def drain(i, carry):
            to_middle(i).wait_send()
            to_end(i).wait_send()
            return carry

        lax.fori_loop(0, count, drain, 0)

    @pl.when(jnp.logical_not(inner))
    def _():
        def finish(i, carry):
            to_end(i).wait_recv()
            to_inner(i).wait_send()
            return carry

        lax.fori_loop(0, count, finish, 0)

    if ending is not None:
        ending(inner, end_peer, extras, aux, scratch)


def sum_line(
    part,
    extras,
    aux_shapes,
    epilogue,
    collective_id,
    prologue=None,
    scratch=(),
    opening=None,
    ending=None,
    rows=64,
):
    tokens, width = scratch[-1].shape if part is None else part.shape
    inputs = list(extras) if part is None else [part, *extras]
    count = tokens // rows
    chunks = pltpu.VMEM((count, rows, width), jnp.bfloat16)
    return pl.pallas_call(
        functools.partial(
            sum_line_kernel,
            rows,
            count,
            opening,
            part is None,
            prologue,
            epilogue,
            ending,
            len(inputs),
            len(aux_shapes),
            len(scratch),
        ),
        out_shape=[jax.ShapeDtypeStruct((tokens, width), jnp.bfloat16)] + list(aux_shapes),
        in_specs=[whole_vmem] * len(inputs),
        out_specs=[whole_vmem] * (1 + len(aux_shapes)),
        scratch_shapes=list(scratch)
        + [chunks, chunks, chunks]
        + [pltpu.SemaphoreType.DMA((count,))] * 5,
        compiler_params=pltpu.CompilerParams(
            collective_id=collective_id, has_side_effects=True, vmem_limit_bytes=48 << 20
        ),
    )(*inputs)


def keep_total(total, span, rank, extras, aux, scratch):
    return total.astype(jnp.bfloat16)


def inverse_rms(values):
    return lax.rsqrt(jnp.mean(values * values, -1, keepdims=True) + norm_epsilon)


def norm_back_rows(values, gain, upstream):
    inverse = inverse_rms(values)
    normed = values * inverse
    scaled = upstream * gain
    gain_grad = jnp.sum(upstream * normed, 0, keepdims=True)
    inputs_grad = inverse * (scaled - normed * jnp.mean(scaled * normed, -1, keepdims=True))
    return (inputs_grad, gain_grad)


def clear_gain(rank, inner, extras, aux, scratch):
    @pl.when(inner)
    def _():
        aux[-1][...] = jnp.zeros_like(aux[-1])


def share_gains(inner, end_peer, extras, aux, scratch):
    gains = aux[-1]
    copy = pltpu.make_async_remote_copy(
        src_ref=gains,
        dst_ref=gains,
        send_sem=scratch[0],
        recv_sem=scratch[1],
        device_id={"tensor": end_peer},
        device_id_type=MESH_ID,
    )

    @pl.when(inner)
    def _():
        gains[1:2, :] = extras[3][...]
        gains[2:3, :] = extras[4][...]
        copy.start()
        copy.wait_send()

    @pl.when(jnp.logical_not(inner))
    def _():
        copy.wait_recv()


def gate_copies(rank, extras, scratch):
    gate_part = extras[3]
    landed, gate_send, gate_recv = scratch
    return [
        pltpu.make_async_remote_copy(
            src_ref=gate_part,
            dst_ref=landed.at[step - 1],
            send_sem=gate_send.at[step - 1],
            recv_sem=gate_recv.at[step - 1],
            device_id={"tensor": lax.rem(rank + step, 4)},
            device_id_type=MESH_ID,
        )
        for step in (1, 2, 3)
    ]


def send_gate_parts(rank, extras, aux, scratch):
    for copy in gate_copies(rank, extras, scratch):
        copy.start()


def start_router_grad(rank, inner, extras, aux, scratch):
    stream_one, gain, grad_two, gate_part, gates, routes, router_low = extras
    grad_one, logit_grad, target_total, gain_grad = aux
    landed = scratch[0]
    clear_gain(rank, inner, extras, aux, scratch)
    for copy in gate_copies(rank, extras, scratch):
        copy.wait()
    gate_grad = jnp.zeros(gate_part.shape, jnp.float32)
    for source in range(4):
        piece = jnp.zeros(gate_part.shape, jnp.float32)
        for step in (1, 2, 3):
            piece = jnp.where(lax.rem(source + step, 4) == rank, landed[step - 1], piece)
        gate_grad = gate_grad + jnp.where(rank == source, gate_part[...], piece)
    target_total[...] = gate_grad[2:3]
    gate_grad = gate_grad[0:2]
    weighted = gates[...] * gate_grad
    chosen = gates[...] * (gate_grad - (weighted[0:1] + weighted[1:2]))
    experts, tokens = logit_grad.shape
    row = lax.broadcasted_iota(jnp.int32, (experts, tokens), 0)
    placed = jnp.where(row == routes[0:1], chosen[0:1], 0.0) + jnp.where(
        row == routes[1:2], chosen[1:2], 0.0
    )
    logit_grad[...] = placed.astype(jnp.bfloat16)

    @pl.when(inner)
    def _():
        grad_one[...] = lax.dot_general(
            logit_grad[...],
            router_low[...],
            (((0,), (1,)), ((), ())),
            preferred_element_type=jnp.float32,
        )


def finish_expert_grad(total, span, rank, extras, aux, scratch):
    stream_one, gain, grad_two, gate_part, gates, routes, router_low = extras
    grad_one, logit_grad, target_total, gain_grad = aux
    part, gain_part = norm_back_rows(
        stream_one[span], gain[...], total + grad_one[span]
    )
    result = grad_two[span] + part
    grad_one[span] = result
    gain_grad[...] += gain_part
    return result.astype(jnp.bfloat16)


def form_joint_grad(rank, extras, aux, scratch):
    query_grad, pair_grad, before_grad, joint_weights = extras[5:]
    joint_grad = aux[0]
    landed, pair_sem, part = scratch[2:]
    hidden = query_grad.shape[0]
    later = lax.axis_index("ctx") > 0
    copy = pltpu.make_async_remote_copy(
        src_ref=before_grad,
        dst_ref=landed,
        send_sem=pair_sem.at[0],
        recv_sem=pair_sem.at[1],
        device_id={"ctx": 1 - lax.axis_index("ctx")},
        device_id_type=MESH_ID,
    )
    joint_grad[0:hidden, :] = query_grad[...]

    @pl.when(later)
    def _():
        copy.start()
        joint_grad[hidden:, :] = pair_grad[...].astype(jnp.bfloat16)

    @pl.when(jnp.logical_not(later))
    def _():
        copy.wait_recv()
        both = pair_grad[...] + landed[...].astype(jnp.float32)
        joint_grad[hidden:, :] = both.astype(jnp.bfloat16)

    part[...] = lax.dot_general(
        joint_grad[...], joint_weights[...], (((0,), (0,)), ((), ())), preferred_element_type=jnp.float32
    )

    @pl.when(later)
    def _():
        copy.wait_send()


def finish_input_grad(scale, total, span, rank, extras, aux, scratch):
    embedded, gain, grad_one = extras[:3]
    stream_zero = embedded[span].astype(jnp.float32) * scale
    part, gain_part = norm_back_rows(stream_zero, gain[...], total)
    aux[-1][0:1, :] += gain_part
    return ((grad_one[span] + part) * scale).astype(jnp.bfloat16)


def middle_kernel(
    attended_ref, embedded_ref, gain_ref, router_ref, routes_ref, dest_ref, *refs
):
    rolled, (stream_ref, normed_ref, rows_ref, columns_ref, places_ref, project_ref) = (
        refs[:4],
        refs[4:],
    )

    @pl.when(pl.program_id(0) == 0)
    def _():
        for step in range(4):
            lines = rolled[step].shape[0]
            owner = lax.rem(lax.axis_index("tensor") + 4 - step, 4)
            project_ref[pl.ds(pl.multiple_of(owner * lines, lines), lines)] = rolled[step][...]

    scale = math.sqrt(embedded_ref.shape[1])
    stream = embedded_ref[...].astype(jnp.float32) * scale + lax.dot_general(
        attended_ref[...], project_ref[...], (((0,), (0,)), ((), ())), preferred_element_type=jnp.float32
    )
    stream_ref[...] = stream
    normed = (stream * inverse_rms(stream) * gain_ref[...]).astype(jnp.bfloat16)
    normed_ref[...] = normed
    scores = lax.dot_general(
        router_ref[...], normed, (((1,), (1,)), ((), ())), preferred_element_type=jnp.float32
    )
    expert = lax.broadcasted_iota(jnp.int32, scores.shape, 0)
    first, second = (
        jnp.sum(jnp.where(expert == routes_ref[k : k + 1, :], scores, 0.0), 0, keepdims=True)
        for k in range(2)
    )
    top = jnp.maximum(first, second)
    first, second = jnp.exp(first - top), jnp.exp(second - top)
    total = first + second
    gates = jnp.concatenate([first / total, second / total], 0)
    rows_ref[...] = gates
    places = jnp.concatenate([routes_ref[...], dest_ref[...]], 0).astype(jnp.float32)
    turned = jnp.concatenate([gates, places, jnp.zeros_like(gates)], 0).T
    columns_ref[...] = turned
    places_ref[...] = turned.astype(jnp.int32)


def middle(attended, rolled, embedded, gain, router, routes, dest):
    tokens, width = embedded.shape
    tile = 256
    fixed = lambda k: (0, 0)
    whole = lambda x: pl.BlockSpec(x.shape, fixed)
    down = lambda n: pl.BlockSpec((tile, n), lambda k: (k, 0))
    along = lambda n: pl.BlockSpec((n, tile), lambda k: (0, k))
    return pl.pallas_call(
        middle_kernel,
        grid=(tokens // tile,),
        out_shape=[
            jax.ShapeDtypeStruct((tokens, width), jnp.float32),
            jax.ShapeDtypeStruct((tokens, width), jnp.bfloat16),
            jax.ShapeDtypeStruct((2, tokens), jnp.float32),
            jax.ShapeDtypeStruct((tokens, 8), jnp.float32),
            jax.ShapeDtypeStruct((tokens, 8), jnp.int32),
        ],
        in_specs=[along(width), down(width), whole(gain), whole(router), along(2), along(2)]
        + [whole(x) for x in rolled],
        out_specs=[down(width), down(width), along(2), down(8), down(8)],
        scratch_shapes=[pltpu.VMEM((width, width), jnp.bfloat16)],
        compiler_params=pltpu.CompilerParams(vmem_limit_bytes=40 << 20),
    )(attended, embedded, gain, router, routes, dest, *rolled)


def embed_kernel(
    chunks, first_unit, slots_ref, mine_ref, rows_ref, gain_ref, units_ref, embedded_ref, normed_ref, joint_ref,
    joint_weights, project_weights, *refs
):
    held, total, stage, from_end, from_mid = refs[:5]
    send_x, recv_x, send_y, recv_y, send_z, recv_z, send_core, recv_core = refs[5:13]
    send_sem, end_sem, mid_sem, back_sem, back_recv = refs[13:]
    chip, core = lax.axis_index("dp"), lax.axis_index("ctx")
    beside = chip + 1 - 2 * lax.rem(chip, 2)
    across = lax.rem(chip + 2, 4)
    opposite = across + 1 - 2 * lax.rem(across, 2)
    places = (chip, beside, across, opposite)
    rank = lax.axis_index("tensor")
    inner = (rank == 1) | (rank == 2)
    end_peer = jnp.where(rank < 2, 1 - rank, 5 - rank)
    mid_peer = 3 - rank
    slots, unit_rows = mine_ref.shape[:2]
    width = total.shape[2]
    size = slots // chunks
    split = (chunks + 1) // 2
    tokens = rows_ref.shape[0]
    count, rows = stage.shape[1:3]

    def repeat(first, last, body):
        def step(i, carry):
            body(i)
            return carry

        lax.fori_loop(first, last, step, 0)

    def columns(h):
        return slice(h * width, (h + 1) * width)

    own = (chip * 2 + core) * slots
    for h in range(2):
        held[h, pl.ds(own, slots)] = mine_ref[:, :, columns(h)].astype(jnp.bfloat16)
    barrier = pltpu.get_barrier_semaphore()
    for place in ({"ctx": 1 - core}, {"dp": beside}, {"dp": across}, {"tensor": end_peer}):
        pl.semaphore_signal(barrier, inc=1, device_id=place, device_id_type=MESH_ID)

    @pl.when(inner)
    def _():
        pl.semaphore_signal(barrier, inc=1, device_id={"tensor": mid_peer}, device_id_type=MESH_ID)
        pl.semaphore_wait(barrier, 5)

    @pl.when(jnp.logical_not(inner))
    def _():
        pl.semaphore_wait(barrier, 4)

    def remote(source, target, send, recv, place):
        return pltpu.make_async_remote_copy(
            src_ref=source,
            dst_ref=target,
            send_sem=send,
            recv_sem=recv,
            device_id=place,
            device_id_type=MESH_ID,
        )

    def copy(h, place, q, send, recv, target):
        piece = held.at[h, pl.ds((place * 2 + core) * slots + q * size, size)]
        return remote(piece, piece, send, recv, target)

    def to_beside(h, q):
        return copy(h, chip, q, send_x.at[h, q], recv_x.at[h, q], {"dp": beside})

    def to_across(h, q):
        return copy(h, chip, q, send_y.at[h, q], recv_y.at[h, q], {"dp": across})

    def passed_on(h, q, source, target):
        return copy(h, source, q, send_z.at[h, q], recv_z.at[h, q], {"dp": target})

    def to_core(h, k, q):
        return copy(h, places[k], q, send_core.at[h, k, q], recv_core.at[h, k, q], {"ctx": 1 - core})

    def start(h):
        def both(i):
            to_beside(h, i).start()
            to_across(h, lax.rem(i + split, chunks)).start()

        repeat(0, chunks, both)
        repeat(0, chunks, lambda q: to_core(h, 0, q).start())

    def look(h, place, which):
        begin = (place * 2 + which) * slots
        lines = slots * unit_rows
        column = lax.broadcasted_iota(jnp.int32, (tokens, lines), 1) + begin * unit_rows
        hit = jnp.where(column == rows_ref[...], 1.0, 0.0).astype(jnp.bfloat16)
        block = held[h, pl.ds(begin, slots)].reshape(lines, width)
        total[h] += jnp.dot(hit, block, preferred_element_type=jnp.float32)

    def relay(h, i):
        to_beside(h, i).wait_recv()

        @pl.when(i < split)
        def _():
            passed_on(h, i, beside, across).start()

        to_core(h, 1, i).start()
        j = lax.rem(i + split, chunks)
        to_across(h, j).wait_recv()

        @pl.when(j >= split)
        def _():
            passed_on(h, j, across, beside).start()

        to_core(h, 2, j).start()

    def rest(h):
        repeat(0, chunks, lambda q: to_core(h, 0, q).wait_recv())
        look(h, chip, 1 - core)
        look(h, beside, core)
        look(h, across, core)

        def last(q):
            passed_on(h, q, opposite, opposite).wait_recv()
            to_core(h, 3, q).start()
            to_core(h, 1, q).wait_recv()
            to_core(h, 2, q).wait_recv()

        repeat(0, chunks, last)
        look(h, beside, 1 - core)
        look(h, across, 1 - core)
        look(h, opposite, core)
        repeat(0, chunks, lambda q: to_core(h, 3, q).wait_recv())
        look(h, opposite, 1 - core)

    def span(i):
        return pl.ds(pl.multiple_of(i * rows, rows), rows)

    def to_inner(h, i):
        return remote(
            stage.at[h, i], from_end.at[h, i], send_sem.at[h, i], end_sem.at[h, i], {"tensor": end_peer}
        )

    def to_middle(h, i):
        return remote(
            stage.at[h, i], from_mid.at[h, i], send_sem.at[h, i], mid_sem.at[h, i], {"tensor": mid_peer}
        )

    def to_end(h, i):
        piece = embedded_ref.at[span(i), columns(h)]
        return remote(piece, piece, back_sem.at[h, i], back_recv.at[h, i], {"tensor": end_peer})

    def push(h):
        @pl.when(jnp.logical_not(inner))
        def _():
            def one(i):
                stage[h, i] = total[h, span(i)].astype(jnp.bfloat16)
                to_inner(h, i).start()

            repeat(0, count, one)

    def exchange(h, i):
        @pl.when(inner & (i < count))
        def _():
            to_inner(h, i).wait_recv()
            stage[h, i] = (total[h, span(i)] + from_end[h, i].astype(jnp.float32)).astype(jnp.bfloat16)
            to_middle(h, i).start()

        @pl.when(inner & (i >= line_lag))
        def _():
            j = i - line_lag
            to_middle(h, j).wait_recv()
            both = stage[h, j].astype(jnp.float32) + from_mid[h, j].astype(jnp.float32)
            embedded_ref[span(j), columns(h)] = both.astype(jnp.bfloat16)
            to_end(h, j).start()

    total[...] = jnp.zeros_like(total)
    start(0)
    look(0, chip, core)
    repeat(0, chunks, lambda i: relay(0, i))
    start(1)
    rest(0)
    push(0)
    look(1, chip, core)

    def between(i):
        exchange(0, i)

        @pl.when(i < chunks)
        def _():
            relay(1, i)

    repeat(0, count + line_lag, between)
    rest(1)
    push(1)

    def place_unit(u):
        for h in range(2):
            units_ref[u, :, columns(h)] = held[h, slots_ref[u]]

    @pl.when(jnp.logical_not(inner))
    def _():
        repeat(0, units_ref.shape[0], place_unit)

    repeat(0, count + line_lag, lambda i: exchange(1, i))

    @pl.when(inner)
    def _():
        repeat(0, units_ref.shape[0], place_unit)

    def finish(q):
        for h in range(2):
            to_beside(h, q).wait_send()
            to_across(h, q).wait_send()
            for k in range(4):
                to_core(h, k, q).wait_send()
            passed_on(h, q, opposite, opposite).wait_send()

    repeat(0, chunks, finish)

    @pl.when(inner)
    def _():
        def drain(i):
            for h in range(2):
                to_middle(h, i).wait_send()
                to_end(h, i).wait_send()

        repeat(0, count, drain)

    @pl.when(jnp.logical_not(inner))
    def _():
        def drain(i):
            for h in range(2):
                to_end(h, i).wait_recv()
                to_inner(h, i).wait_send()

        repeat(0, count, drain)

    stream = embedded_ref[...].astype(jnp.float32) * math.sqrt(2 * width)
    normed = (stream * inverse_rms(stream) * gain_ref[...]).astype(jnp.bfloat16)
    normed_ref[...] = normed
    lines = joint_ref.shape[0]
    weights = units_ref[first_unit : first_unit + lines // unit_rows].reshape(lines, 2 * width)
    joint_weights[...] = weights
    project_weights[...] = units_ref[first_unit + lines // unit_rows :].reshape(
        project_weights.shape
    )
    joint_ref[...] = lax.dot_general(
        weights, normed, (((1,), (1,)), ((), ())), preferred_element_type=jnp.float32
    ).astype(jnp.bfloat16)


def embed(unit_slots, mine, slot_rows, gain, first_unit, lines, collective_id):
    slots, unit_rows, width = mine.shape
    tokens = slot_rows.shape[0]
    chunks = max(k for k in range(1, 8) if slots % k == 0)
    rows = 128
    half = width // 2
    sems = pltpu.SemaphoreType.DMA((2, chunks))
    line = pltpu.VMEM((2, tokens // rows, rows, half), jnp.bfloat16)
    return pl.pallas_call(
        functools.partial(embed_kernel, chunks, first_unit),
        out_shape=[
            jax.ShapeDtypeStruct((unit_slots.shape[0], unit_rows, width), jnp.bfloat16),
            jax.ShapeDtypeStruct((tokens, width), jnp.bfloat16),
            jax.ShapeDtypeStruct((tokens, width), jnp.bfloat16),
            jax.ShapeDtypeStruct((lines, tokens), jnp.bfloat16),
            jax.ShapeDtypeStruct((lines, width), jnp.bfloat16),
            jax.ShapeDtypeStruct((lines // 3, width), jnp.bfloat16),
        ],
        in_specs=[pl.BlockSpec(memory_space=pltpu.SMEM)] + [whole_vmem] * 3,
        out_specs=[whole_vmem] * 6,
        scratch_shapes=[
            pltpu.VMEM((2, 8 * slots, unit_rows, half), jnp.bfloat16),
            pltpu.VMEM((2, tokens, half), jnp.float32),
            line,
            line,
            line,
        ]
        + [sems] * 6
        + [pltpu.SemaphoreType.DMA((2, 4, chunks))] * 2
        + [pltpu.SemaphoreType.DMA((2, tokens // rows))] * 5,
        compiler_params=pltpu.CompilerParams(
            collective_id=collective_id, has_side_effects=True, vmem_limit_bytes=60 << 20
        ),
    )(unit_slots, mine, slot_rows, gain)


def pull_units_kernel(parts, slots_ref, *refs):
    sources, out_ref, sem = refs[:parts], refs[parts], refs[parts + 1]
    width = out_ref.shape[-1] // parts

    def push(u, carry):
        for part in range(parts):
            pltpu.make_async_copy(
                sources[part].at[slots_ref[u]],
                out_ref.at[u, :, part * width : (part + 1) * width],
                sem,
            ).start()
        return carry

    lax.fori_loop(0, out_ref.shape[0], push, 0)
    pltpu.make_async_copy(out_ref, out_ref, sem).wait()


def pull_units(sources, slots):
    count = slots.shape[0]
    rows, width = sources[0].shape[1:]
    return pl.pallas_call(
        functools.partial(pull_units_kernel, len(sources)),
        out_shape=jax.ShapeDtypeStruct((count, rows, width * len(sources)), sources[0].dtype),
        in_specs=[pl.BlockSpec(memory_space=pltpu.SMEM)] + [whole_any] * len(sources),
        out_specs=whole_vmem,
        scratch_shapes=[pltpu.SemaphoreType.DMA],
        compiler_params=pltpu.CompilerParams(vmem_limit_bytes=40 << 20),
    )(slots, *sources)


def attention_kernel(
    heads, size, bias_ref, own_ref, out_ref, logsum_ref, before_ref, mine_ref,
    queries, own_values, old_values, scores, peak, total, keys_sem, send_sem, recv_sem,
):
    tokens = own_ref.shape[1]
    blocks = tokens // BLOCK
    hidden = heads * size
    later = lax.axis_index("ctx") > 0
    rank = lax.axis_index("tensor")
    barrier = pltpu.get_barrier_semaphore()
    other_core = {"ctx": 1 - lax.axis_index("ctx")}
    pl.semaphore_signal(barrier, inc=1, device_id=other_core, device_id_type=MESH_ID)
    for step in (1, 2, 3):
        other = lax.rem(rank + step, 4)
        pl.semaphore_signal(barrier, inc=1, device_id={"tensor": other}, device_id_type=MESH_ID)
    pl.semaphore_wait(barrier, 4)
    pairs = pltpu.make_async_remote_copy(
        src_ref=own_ref.at[pl.ds(hidden, 2 * hidden)],
        dst_ref=before_ref,
        send_sem=keys_sem.at[0],
        recv_sem=keys_sem.at[1],
        device_id=other_core,
        device_id_type=MESH_ID,
    )

    @pl.when(jnp.logical_not(later))
    def _():
        pairs.start()
        before_ref[...] = jnp.zeros_like(before_ref)

    def flipped(rows):
        return rows.astype(jnp.float32).T.astype(jnp.bfloat16)

    for head in range(heads):
        span = slice(head * size, (head + 1) * size)
        queries[head] = flipped(own_ref[span, :]) * jnp.bfloat16(size**-0.5)
        own_values[head] = flipped(
            own_ref[2 * hidden + head * size : 2 * hidden + (head + 1) * size, :]
        )

    @pl.when(later)
    def _():
        pairs.wait_recv()
        for head in range(heads):
            old_values[head] = flipped(
                before_ref[hidden + head * size : hidden + (head + 1) * size, :]
            )

    def sent(block, step):
        piece = out_ref.at[rank, :, pl.ds(block * BLOCK, BLOCK)]
        return pltpu.make_async_remote_copy(
            src_ref=piece,
            dst_ref=piece,
            send_sem=send_sem.at[block, step - 1],
            recv_sem=recv_sem.at[block, step - 1],
            device_id={"tensor": lax.rem(rank + step, 4)},
            device_id_type=MESH_ID,
        )

    for block in range(blocks):
        for head in range(heads):
            span = slice(head * size, (head + 1) * size)
            rows = queries[head, block * BLOCK : (block + 1) * BLOCK]
            own_keys = own_ref[hidden + head * size : hidden + (head + 1) * size, :]
            width = (block + 1) * BLOCK
            mine = jnp.dot(rows, own_keys[:, :width], preferred_element_type=jnp.float32)
            top = None
            parts = []
            for k in range(block + 1):
                part = mine[:, k * BLOCK : (k + 1) * BLOCK] + bias_ref[head, block - k]
                parts.append(part)
                high = jnp.max(part, 1, keepdims=True)
                top = high if top is None else jnp.maximum(top, high)
            peak[...] = top

            @pl.when(later)
            def _():
                old = jnp.dot(rows, before_ref[span, :], preferred_element_type=jnp.float32)
                top_old = None
                for k in range(blocks):
                    part = old[:, k * BLOCK : (k + 1) * BLOCK] + bias_ref[head, block + blocks - k]
                    scores[:, k * BLOCK : (k + 1) * BLOCK] = part
                    high = jnp.max(part, 1, keepdims=True)
                    top_old = high if top_old is None else jnp.maximum(top_old, high)
                peak[...] = jnp.maximum(peak[...], top_old)

            top = peak[...]
            parts = [jnp.exp(part - top) for part in parts]
            own_sum = None
            for part in parts:
                part_sum = jnp.sum(part, 1, keepdims=True)
                own_sum = part_sum if own_sum is None else own_sum + part_sum
            total[...] = own_sum

            @pl.when(later)
            def _():
                old_exp = jnp.exp(scores[...] - top)
                scores[...] = old_exp
                total[...] += jnp.sum(old_exp, 1, keepdims=True)

            full = total[...]
            inverse = 1.0 / full
            low = jnp.concatenate([(part * inverse).astype(jnp.bfloat16) for part in parts], 1)
            result = jnp.dot(low, own_values[head, :width], preferred_element_type=jnp.float32)
            logsum_ref[head, block * BLOCK : (block + 1) * BLOCK, :] = top + jnp.log(full)
            place = (rank, span, slice(block * BLOCK, (block + 1) * BLOCK))

            @pl.when(later)
            def _():
                low_old = (scores[...] * inverse).astype(jnp.bfloat16)
                both = result + jnp.dot(low_old, old_values[head], preferred_element_type=jnp.float32)
                out_ref[place] = both.T.astype(jnp.bfloat16)
                mine_ref[place[1:]] = both.T.astype(jnp.bfloat16)

            @pl.when(jnp.logical_not(later))
            def _():
                out_ref[place] = result.T.astype(jnp.bfloat16)
                mine_ref[place[1:]] = result.T.astype(jnp.bfloat16)

        for step in (1, 2, 3):
            sent(block, step).start()

    for block in range(blocks):
        for step in (1, 2, 3):
            sent(block, step).wait()

    @pl.when(jnp.logical_not(later))
    def _():
        pairs.wait_send()


def attention(biases, own, heads, size, collective_id):
    tokens = own.shape[1]
    blocks = tokens // BLOCK
    flat = pltpu.VMEM((heads, tokens, size), jnp.bfloat16)
    return pl.pallas_call(
        functools.partial(attention_kernel, heads, size),
        out_shape=[
            jax.ShapeDtypeStruct((4, heads * size, tokens), jnp.bfloat16),
            jax.ShapeDtypeStruct((heads, tokens, 1), jnp.float32),
            jax.ShapeDtypeStruct((2 * heads * size, tokens), jnp.bfloat16),
            jax.ShapeDtypeStruct((heads * size, tokens), jnp.bfloat16),
        ],
        in_specs=[pl.BlockSpec(memory_space=pltpu.SMEM), whole_vmem],
        out_specs=[whole_vmem] * 4,
        scratch_shapes=[
            flat,
            flat,
            flat,
            pltpu.VMEM((BLOCK, tokens), jnp.float32),
            pltpu.VMEM((BLOCK, 1), jnp.float32),
            pltpu.VMEM((BLOCK, 1), jnp.float32),
            pltpu.SemaphoreType.DMA((2,)),
            pltpu.SemaphoreType.DMA((blocks, 3)),
            pltpu.SemaphoreType.DMA((blocks, 3)),
        ],
        compiler_params=pltpu.CompilerParams(
            collective_id=collective_id, has_side_effects=True, vmem_limit_bytes=40 << 20
        ),
    )(biases, own)


def attention_back_kernel(
    heads, size, bias_ref, own_ref, before_ref, logsum_ref, grad_ref, project_ref,
    *refs
):
    states, (query_out, own_out, before_out, bias_out) = refs[:8], refs[8:12]
    updated, (probs, slopes, inner, query_sum, own_sum, before_sum) = refs[12:18], refs[18:24]
    held, load_sem, store_sem = refs[24:]
    loads = [pltpu.make_async_copy(states[k], held.at[k], load_sem.at[k]) for k in range(8)]
    stores = [
        pltpu.make_async_copy(held.at[4 * (k // 3) + k % 3], updated[k], store_sem.at[k])
        for k in range(6)
    ]
    for load in loads:
        load.start()

    def update(i, carry):
        lines = held.shape[1] // 16
        span = pl.ds(pl.multiple_of(i * lines, lines), lines)
        for k, rate in enumerate((rate_inner, rate_outer)):
            fresh = adam_update(*(held[4 * k + n, span] for n in range(4)), rate, decay_rate)
            for n in range(3):
                held[4 * k + n, span] = fresh[n]
        return carry

    tokens = own_ref.shape[1]
    blocks = tokens // BLOCK
    hidden = heads * size
    later = lax.axis_index("ctx") > 0
    bias_out[...] = jnp.zeros_like(bias_out)

    def flipped(rows):
        return rows.astype(jnp.float32).T.astype(jnp.bfloat16)

    for head in range(heads):
        span = slice(head * size, (head + 1) * size)
        value_span = slice(hidden + head * size, hidden + (head + 1) * size)
        query_rows = own_ref[span, :]
        query = flipped(query_rows) * jnp.bfloat16(size**-0.5)
        own_keys = own_ref[hidden + head * size : hidden + (head + 1) * size, :]
        own_values = own_ref[2 * hidden + head * size : 2 * hidden + (head + 1) * size, :]
        old_keys = before_ref[span, :]
        old_values = before_ref[value_span, :]
        own_keys_flip = flipped(own_keys)
        grad = lax.dot_general(
            grad_ref[...], project_ref[span, :], (((1,), (1,)), ((), ())), preferred_element_type=jnp.float32
        )
        grad_rows = grad.T.astype(jnp.bfloat16)
        grad = grad.astype(jnp.bfloat16)
        own_sum[...] = jnp.zeros_like(own_sum)

        @pl.when(later)
        def _():
            before_sum[...] = jnp.zeros_like(before_sum)

        for block in range(blocks):
            at = slice(block * BLOCK, (block + 1) * BLOCK)
            width = (block + 1) * BLOCK
            rows, up = query[at], grad[at]
            lse = logsum_ref[head, at, :]
            score = jnp.dot(rows, own_keys[:, :width], preferred_element_type=jnp.float32)
            prob = jnp.concatenate(
                [
                    jnp.exp(score[:, k * BLOCK : (k + 1) * BLOCK] + (bias_ref[head, block - k] - lse))
                    for k in range(block + 1)
                ],
                1,
            )
            slope = jnp.dot(up, own_values[:, :width], preferred_element_type=jnp.float32)
            inner[...] = jnp.sum(prob * slope, 1, keepdims=True)

            @pl.when(later)
            def _():
                score = jnp.dot(rows, old_keys, preferred_element_type=jnp.float32)
                old_slope = jnp.dot(up, old_values, preferred_element_type=jnp.float32)
                old_prob = jnp.concatenate(
                    [
                        jnp.exp(
                            score[:, k * BLOCK : (k + 1) * BLOCK]
                            + (bias_ref[head, block + blocks - k] - lse)
                        )
                        for k in range(blocks)
                    ],
                    1,
                )
                probs[...] = old_prob
                slopes[...] = old_slope
                inner[...] += jnp.sum(old_prob * old_slope, 1, keepdims=True)

            row_inner = inner[...]
            low_grad = (prob * (slope - row_inner)).astype(jnp.bfloat16)
            query_sum[...] = jnp.dot(
                low_grad, own_keys_flip[:width], preferred_element_type=jnp.float32
            )
            own_sum[:size, :width] += jnp.dot(
                query_rows[:, at], low_grad, preferred_element_type=jnp.float32
            )
            own_sum[size:, :width] += jnp.dot(
                grad_rows[:, at], prob.astype(jnp.bfloat16), preferred_element_type=jnp.float32
            )
            for k in range(block + 1):
                line = head * 2 * blocks + block - k
                bias_out[line : line + 1, :] += jnp.sum(
                    low_grad[:, k * BLOCK : (k + 1) * BLOCK].astype(jnp.float32), 0, keepdims=True
                )

            @pl.when(later)
            def _():
                old_prob = probs[...]
                low_old = (old_prob * (slopes[...] - row_inner)).astype(jnp.bfloat16)
                query_sum[...] += jnp.dot(
                    low_old, flipped(old_keys), preferred_element_type=jnp.float32
                )
                before_sum[:size, :] += jnp.dot(
                    query_rows[:, at], low_old, preferred_element_type=jnp.float32
                )
                before_sum[size:, :] += jnp.dot(
                    grad_rows[:, at], old_prob.astype(jnp.bfloat16), preferred_element_type=jnp.float32
                )
                for k in range(blocks):
                    line = head * 2 * blocks + block + blocks - k
                    bias_out[line : line + 1, :] += jnp.sum(
                        low_old[:, k * BLOCK : (k + 1) * BLOCK].astype(jnp.float32), 0, keepdims=True
                    )

            query_out[span, at] = (query_sum[...].T * size**-0.5).astype(jnp.bfloat16)

        own_out[span, :] = own_sum[:size, :] * size**-0.5
        own_out[value_span, :] = own_sum[size:, :]

        @pl.when(later)
        def _():
            before_out[span, :] = (before_sum[:size, :] * size**-0.5).astype(jnp.bfloat16)
            before_out[value_span, :] = before_sum[size:, :].astype(jnp.bfloat16)

        if head == 0:
            for load in loads:
                load.wait()
            lax.fori_loop(0, 16, update, 0)
            for store in stores:
                store.start()

    @pl.when(jnp.logical_not(later))
    def _():
        before_out[...] = jnp.zeros_like(before_out)

    for store in stores:
        store.wait()


def attention_back(biases, own, before, logsum, grad, project, states, heads, size):
    tokens = own.shape[1]
    hidden = heads * size
    return pl.pallas_call(
        functools.partial(attention_back_kernel, heads, size),
        out_shape=[
            jax.ShapeDtypeStruct((hidden, tokens), jnp.bfloat16),
            jax.ShapeDtypeStruct((2 * hidden, tokens), jnp.float32),
            jax.ShapeDtypeStruct((2 * hidden, tokens), jnp.bfloat16),
            jax.ShapeDtypeStruct((heads * 2 * (tokens // BLOCK), BLOCK), jnp.float32),
        ]
        + [jax.ShapeDtypeStruct(states[0].shape, jnp.float32)] * 6,
        in_specs=[pl.BlockSpec(memory_space=pltpu.SMEM)] + [whole_vmem] * 5 + [whole_any] * 8,
        out_specs=[whole_vmem] * 4 + [whole_any] * 6,
        scratch_shapes=[
            pltpu.VMEM((BLOCK, tokens), jnp.float32),
            pltpu.VMEM((BLOCK, tokens), jnp.float32),
            pltpu.VMEM((BLOCK, 1), jnp.float32),
            pltpu.VMEM((BLOCK, size), jnp.float32),
            pltpu.VMEM((2 * size, tokens), jnp.float32),
            pltpu.VMEM((2 * size, tokens), jnp.float32),
            pltpu.VMEM((8,) + states[0].shape, jnp.float32),
            pltpu.SemaphoreType.DMA((8,)),
            pltpu.SemaphoreType.DMA((6,)),
        ],
        compiler_params=pltpu.CompilerParams(vmem_limit_bytes=48 << 20),
    )(biases, own, before, logsum, grad, project, *states)


def vocab_tile(vocab):
    return max(k for k in range(16, 1601, 16) if vocab % k == 0)


def head_line_kernel(
    tile, part_ref, stream_ref, gain_ref, table_ref, wanted_ref, weight_ref,
    low_ref, grad_low_ref, grad_ref, gain_grad, logsum_ref, picked_ref, slopes_ref,
    logits, table, stage, from_end, from_mid, own, turned, stats, landed, slope_tiles, total,
    load_sem, send_sem, end_sem, mid_sem, back_sem, back_recv, stat_send, stat_recv, store_sem,
):
    rank = lax.axis_index("tensor")
    inner = (rank == 1) | (rank == 2)
    end_peer = jnp.where(rank < 2, 1 - rank, 5 - rank)
    mid_peer = 3 - rank
    count, rows = stage.shape[:2]
    columns = turned.shape[1]
    pieces = table.shape[0] // tile
    group = columns // rows
    tiles = count // group
    vocab = table.shape[0]
    load = pltpu.make_async_copy(table_ref.at[pl.ds(0, vocab)], table, load_sem)
    load.start()
    barrier = pltpu.get_barrier_semaphore()
    for step in (1, 2, 3):
        other = lax.rem(rank + step, 4)
        pl.semaphore_signal(barrier, inc=1, device_id={"tensor": other}, device_id_type=MESH_ID)
    pl.semaphore_wait(barrier, 3)

    def span(i):
        return pl.ds(pl.multiple_of(i * rows, rows), rows)

    def over(t):
        return pl.ds(pl.multiple_of(t * columns, columns), columns)

    def line_copy(source, target, send, recv, peer):
        return pltpu.make_async_remote_copy(
            src_ref=source,
            dst_ref=target,
            send_sem=send,
            recv_sem=recv,
            device_id={"tensor": peer},
            device_id_type=MESH_ID,
        )

    def to_inner(i):
        return line_copy(stage.at[i], from_end.at[i], send_sem.at[i], end_sem.at[i], end_peer)

    def to_middle(i):
        return line_copy(stage.at[i], from_mid.at[i], send_sem.at[i], mid_sem.at[i], mid_peer)

    def to_end(ref, i):
        rows_of = ref.at[span(i)]
        return line_copy(rows_of, rows_of, back_sem.at[i], back_recv.at[i], end_peer)

    def repeat(first, last, body):
        def step(i, carry):
            body(i)
            return carry

        lax.fori_loop(first, last, step, 0)

    def turn(t):
        turned[...] = low_ref[over(t)].astype(jnp.float32).T.astype(jnp.bfloat16)

    def table_rows(k):
        return table[k * tile : (k + 1) * tile]

    def first_logits(t):
        turn(t)
        logits[0] = jnp.dot(table_rows(0), turned[...], preferred_element_type=jnp.float32)

    def next_logits(k):
        if k + 1 < pieces:
            logits[(k + 1) % 2] = jnp.dot(
                table_rows(k + 1), turned[...], preferred_element_type=jnp.float32
            )

    def sums_unit(t, k):
        next_logits(k)
        before = stats[0:1, over(t)]
        top = jnp.maximum(before, jnp.max(logits[k % 2], 0, keepdims=True))
        stats[1:2, over(t)] = stats[1:2, over(t)] * jnp.exp(before - top) + jnp.sum(
            jnp.exp(logits[k % 2] - top), 0, keepdims=True
        )
        stats[0:1, over(t)] = top

    def sums_tile(t):
        first_logits(t)
        for k in range(pieces):
            sums_unit(t, k)

    stats[0:1, :] = jnp.full_like(stats[0:1, :], masked_score)
    stats[1:2, :] = jnp.zeros_like(stats[1:2, :])

    @pl.when(jnp.logical_not(inner))
    def _():
        def push(i):
            stage[i] = part_ref[span(i)].astype(jnp.bfloat16)
            to_inner(i).start()

        repeat(0, count, push)
        load.wait()

        def forward(t):
            repeat(0, group, lambda c: to_end(low_ref, t * group + c).wait_recv())
            sums_tile(t)

        repeat(0, tiles, forward)
        repeat(0, count, lambda i: to_inner(i).wait_send())

    @pl.when(inner)
    def _():
        gain_grad[...] = jnp.zeros_like(gain_grad)
        load.wait()

        def gather(i):
            to_inner(i).wait_recv()
            mine = part_ref[span(i)] + from_end[i].astype(jnp.float32)
            stage[i] = mine.astype(jnp.bfloat16)
            to_middle(i).start()

        def settle_rows(j):
            to_middle(j).wait_recv()
            stream_two = stream_ref[span(j)] + (
                stage[j].astype(jnp.float32) + from_mid[j].astype(jnp.float32)
            )
            grad_ref[span(j)] = stream_two
            low_ref[span(j)] = (stream_two * inverse_rms(stream_two) * gain_ref[...]).astype(
                jnp.bfloat16
            )
            to_end(low_ref, j).start()

        turns = [[k for k in range(pieces) if k * (group - 1) // pieces == c - 1] for c in range(group)]

        def advance(t):
            for c in range(group):
                i = t * group + c
                gather(i)

                @pl.when(i >= line_lag)
                def _():
                    settle_rows(i - line_lag)

                if turns[c]:

                    @pl.when(t >= 1)
                    def _():
                        if c == 1:
                            first_logits(t - 1)
                        for k in turns[c]:
                            sums_unit(t - 1, k)

        repeat(0, tiles, advance)
        repeat(count - line_lag, count, settle_rows)
        sums_tile(tiles - 1)

        def drain(i):
            to_middle(i).wait_send()
            to_end(low_ref, i).wait_send()

        repeat(0, count, drain)

    copies = [
        line_copy(
            stats, landed.at[step - 1], stat_send.at[step - 1], stat_recv.at[step - 1], lax.rem(rank + step, 4)
        )
        for step in (1, 2, 3)
    ]
    for copy in copies:
        copy.start()
    for copy in copies:
        copy.wait()
    tops, sums = [], []
    for source in range(4):
        piece = stats[...]
        for step in (1, 2, 3):
            piece = jnp.where(lax.rem(source + step, 4) == rank, landed[step - 1], piece)
        tops.append(piece[0:1])
        sums.append(piece[1:2])
    top = jnp.maximum(jnp.maximum(tops[0], tops[1]), jnp.maximum(tops[2], tops[3]))
    whole = sums[0] * jnp.exp(tops[0] - top)
    for source in (1, 2, 3):
        whole = whole + sums[source] * jnp.exp(tops[source] - top)
    logsum_ref[...] = top + jnp.log(whole)
    picked_ref[...] = jnp.zeros_like(picked_ref)

    def store(t):
        return pltpu.make_async_copy(
            slope_tiles.at[lax.rem(t, 2)], slopes_ref.at[:, over(t)], store_sem.at[lax.rem(t, 2)]
        )

    def slope_unit(t, k):
        values = logits[k % 2]
        row = lax.broadcasted_iota(jnp.int32, values.shape, 0)
        base = k * tile
        hits = jnp.where(row == wanted_ref[0:1, over(t)] - base, weight_ref[0:1, over(t)], 0.0)
        hits = hits + jnp.where(
            row == wanted_ref[1:2, over(t)] - base, weight_ref[1:2, over(t)], 0.0
        )
        picked_ref[:, over(t)] += jnp.sum(hits * values, 0, keepdims=True)
        softmax = jnp.exp(values - logsum_ref[:, over(t)])
        slope_tiles[lax.rem(t, 2), base : base + tile] = (
            (weight_ref[2:3, over(t)] * softmax - hits) * weight_ref[3:4, over(t)]
        ).astype(jnp.bfloat16)

    def add_rows(t, k):
        total[...] += lax.dot_general(
            slope_tiles[lax.rem(t, 2), k * tile : (k + 1) * tile],
            table_rows(k),
            (((0,), (0,)), ((), ())),
            preferred_element_type=jnp.float32,
        )

    def settle(j):
        to_middle(j).wait_recv()
        upstream = stage[j].astype(jnp.float32) + from_mid[j].astype(jnp.float32)
        grad_two, gain_part = norm_back_rows(grad_ref[span(j)], gain_ref[...], upstream)
        grad_ref[span(j)] = grad_two
        gain_grad[...] += gain_part
        grad_low_ref[span(j)] = grad_two.astype(jnp.bfloat16)
        to_end(grad_low_ref, j).start()

    def exchange(i):
        to_inner(i).wait_recv()
        stage[i] = (own[span(i)] + from_end[i].astype(jnp.float32)).astype(jnp.bfloat16)
        to_middle(i).start()

        @pl.when(i >= line_lag)
        def _():
            settle(i - line_lag)

    def back_tile(t):
        @pl.when(t >= 2)
        def _():
            store(t - 2).wait()

        total[...] = jnp.zeros_like(total)
        first_logits(t)
        for k in range(pieces):
            next_logits(k)
            slope_unit(t, k)
            if k >= 1:
                add_rows(t, k - 1)
            if k >= pieces - group:

                @pl.when(inner & (t >= 1))
                def _():
                    exchange((t - 1) * group + k - (pieces - group))

        add_rows(t, pieces - 1)
        store(t).start()

        @pl.when(inner)
        def _():
            own[over(t)] = total[...]

        @pl.when(jnp.logical_not(inner))
        def _():
            def push(c):
                stage[t * group + c] = total[span(c)].astype(jnp.bfloat16)
                to_inner(t * group + c).start()

            repeat(0, group, push)

    repeat(0, tiles, back_tile)

    @pl.when(jnp.logical_not(inner))
    def _():
        def finish(i):
            to_end(grad_low_ref, i).wait_recv()
            to_inner(i).wait_send()

        repeat(0, count, finish)

    @pl.when(inner)
    def _():
        repeat(count - group, count, exchange)
        repeat(count - line_lag, count, settle)

        def drain(i):
            to_middle(i).wait_send()
            to_end(grad_low_ref, i).wait_send()

        repeat(0, count, drain)

    store(tiles - 2).wait()
    store(tiles - 1).wait()


def head_line(part, stream, gain, weights, wanted, weight_rows, vocab, collective_id):
    tokens, width = part.shape
    rows, columns = 64, 256
    count = tokens // rows
    chunks = pltpu.VMEM((count, rows, width), jnp.bfloat16)
    rows_low = jax.ShapeDtypeStruct((tokens, width), jnp.bfloat16)
    along = jax.ShapeDtypeStruct((1, tokens), jnp.float32)
    line_sems = pltpu.SemaphoreType.DMA((count,))
    return pl.pallas_call(
        functools.partial(head_line_kernel, vocab_tile(vocab)),
        out_shape=[
            rows_low,
            rows_low,
            jax.ShapeDtypeStruct((tokens, width), jnp.float32),
            jax.ShapeDtypeStruct((1, width), jnp.float32),
            along,
            along,
            jax.ShapeDtypeStruct((vocab, tokens), jnp.bfloat16),
        ],
        in_specs=[whole_vmem] * 3 + [whole_any] + [whole_vmem] * 2,
        out_specs=[whole_vmem] * 6 + [whole_any],
        scratch_shapes=[
            pltpu.VMEM((2, vocab_tile(vocab), columns), jnp.float32),
            pltpu.VMEM((vocab, width), jnp.bfloat16),
            chunks,
            chunks,
            chunks,
            pltpu.VMEM((tokens, width), jnp.float32),
            pltpu.VMEM((width, columns), jnp.bfloat16),
            pltpu.VMEM((2, tokens), jnp.float32),
            pltpu.VMEM((3, 2, tokens), jnp.float32),
            pltpu.VMEM((2, vocab, columns), jnp.bfloat16),
            pltpu.VMEM((columns, width), jnp.float32),
            pltpu.SemaphoreType.DMA,
        ]
        + [line_sems] * 5
        + [pltpu.SemaphoreType.DMA((3,))] * 2
        + [pltpu.SemaphoreType.DMA((2,))],
        compiler_params=pltpu.CompilerParams(
            collective_id=collective_id, has_side_effects=True, vmem_limit_bytes=62 << 20
        ),
    )(part, stream, gain, weights, wanted, weight_rows)


def weight_grads_kernel(
    tile_units, tiles, place_ref, slope_ref, rows_ref, ids_ref, zero_ref, joint_ref, normed_ref,
    attended_ref, grad_ref, out_ref, made, sem,
):
    step = pl.program_id(0)
    unit_rows = out_ref.shape[1]
    buffer = lax.rem(step, 2)
    last_units = joint_ref.shape[0] // unit_rows + attended_ref.shape[0] // unit_rows

    def settle(which, count):
        pltpu.make_async_copy(
            made.at[which, pl.ds(0, count)], made.at[which, pl.ds(0, count)], sem.at[which]
        ).wait()

    def send(first, count):
        def push(u, carry):
            pltpu.make_async_copy(
                made.at[buffer, u], out_ref.at[place_ref[first + u]], sem.at[buffer]
            ).start()
            return carry

        lax.fori_loop(0, count, push, 0)

    @pl.when(step >= 2)
    def _():
        settle(buffer, tile_units)

    @pl.when(step < tiles)
    def _():
        row = lax.broadcasted_iota(jnp.int32, slope_ref.shape, 0)
        seen = jnp.where(row == ids_ref[...] - step * slope_ref.shape[0], 1.0, 0.0).astype(jnp.bfloat16)
        made[buffer] = (
            jnp.dot(slope_ref[...], rows_ref[...], preferred_element_type=jnp.float32)
            + jnp.dot(seen, zero_ref[...], preferred_element_type=jnp.float32)
        ).astype(jnp.bfloat16).reshape(tile_units, unit_rows, -1)
        send(step * tile_units, tile_units)

    @pl.when(step == tiles)
    def _():
        joint_units = joint_ref.shape[0] // unit_rows
        made[buffer, pl.ds(0, joint_units)] = jnp.dot(
            joint_ref[...], normed_ref[...], preferred_element_type=jnp.float32
        ).astype(jnp.bfloat16).reshape(joint_units, unit_rows, -1)
        made[buffer, pl.ds(joint_units, last_units - joint_units)] = jnp.dot(
            attended_ref[...], grad_ref[...], preferred_element_type=jnp.float32
        ).astype(jnp.bfloat16).reshape(last_units - joint_units, unit_rows, -1)
        send(tiles * tile_units, last_units)
        settle(1 - buffer, tile_units)
        settle(buffer, last_units)


def weight_grads(place, slots, unit_rows, slope, rows, ids, zero, joint, normed, attended, grad):
    vocab, tokens = slope.shape
    width = rows.shape[1]
    tile = vocab_tile(vocab)
    tiles = vocab // tile
    fixed = lambda k: (0, 0)
    whole = lambda x: pl.BlockSpec(x.shape, fixed)
    return pl.pallas_call(
        functools.partial(weight_grads_kernel, tile // unit_rows, tiles),
        grid=(tiles + 1,),
        out_shape=jax.ShapeDtypeStruct((slots, unit_rows, width), jnp.bfloat16),
        in_specs=[
            pl.BlockSpec(memory_space=pltpu.SMEM),
            pl.BlockSpec((tile, tokens), lambda k: (jnp.minimum(k, tiles - 1), 0)),
        ]
        + [whole(x) for x in (rows, ids, zero, joint, normed, attended, grad)],
        out_specs=whole_any,
        scratch_shapes=[
            pltpu.VMEM((2, tile // unit_rows, unit_rows, width), jnp.bfloat16),
            pltpu.SemaphoreType.DMA((2,)),
        ],
        compiler_params=pltpu.CompilerParams(vmem_limit_bytes=60 << 20),
    )(place, slope, rows, ids, zero, joint, normed, attended, grad)


def adam_update(weight, moment_one, moment_two, gradient, step_rate, decay_factor):
    moment_new = beta_first * moment_one + (1.0 - beta_first) * gradient
    square_new = beta_second * moment_two + (1.0 - beta_second) * gradient * gradient
    moment_hat = moment_new / (1.0 - beta_first**STEP)
    square_hat = square_new / (1.0 - beta_second**STEP)
    weight_new = weight - step_rate * (
        moment_hat / (jnp.sqrt(square_hat) + adam_epsilon) + decay_factor * weight
    )
    return (weight_new, moment_new, square_new)


def norm_forward(values, gain_row):
    return values * inverse_rms(values) * gain_row


def slot_tables(owner_ids, owners, most_units):
    unit_count = owner_ids.shape[0]
    unit_index = jnp.arange(unit_count, dtype=jnp.int32)
    earlier = (owner_ids[None, :] == owner_ids[:, None]) & (
        unit_index[None, :] < unit_index[:, None]
    )
    unit_rank = jnp.sum(earlier.astype(jnp.int32), 1)
    placed = (owner_ids[None, None, :] == jnp.arange(owners, dtype=jnp.int32)[:, None, None]) & (
        unit_rank[None, None, :] == jnp.arange(most_units, dtype=jnp.int32)[None, :, None]
    )
    slot_filled = jnp.any(placed, 2)
    slot_unit = jnp.sum(jnp.where(placed, unit_index[None, None, :], 0), 2)
    return (unit_rank, slot_unit, slot_filled)


def unit_rates(unit_ids, table_units, query_units, value_units):
    return jnp.where(
        unit_ids < table_units,
        rate_table,
        jnp.where(
            unit_ids < query_units,
            rate_query,
            jnp.where(unit_ids < value_units, rate_values, rate_project),
        ),
    )


def pair_slots(route_pairs, priorities, experts, capacity):
    tokens_here = priorities.shape[0]
    pair_expert = route_pairs.T.reshape(-1)
    pair_key = (
        jnp.arange(2, dtype=jnp.int32)[:, None] * tokens_here + priorities[None, :]
    ).reshape(-1)
    before = (pair_expert[None, :] == pair_expert[:, None]) & (
        pair_key[None, :] < pair_key[:, None]
    )
    pair_rank = jnp.sum(before.astype(jnp.int32), 1)
    pair_kept = pair_rank < capacity
    pair_dest = pair_expert * capacity + jnp.minimum(pair_rank, capacity - 1)
    return (pair_kept, pair_dest)


def gelu_tanh(values):
    return jax.nn.gelu(values, approximate=True)


def gelu_slope(values):
    root = math.sqrt(2.0 / math.pi)
    bent = jnp.tanh(root * (values + 0.044715 * values * values * values))
    return 0.5 * (1.0 + bent) + 0.5 * values * (1.0 - bent * bent) * root * (
        1.0 + 3.0 * 0.044715 * values * values
    )


def plane_peer(step):
    chip, core = lax.axis_index("dp"), lax.axis_index("ctx")
    row = lax.rem(chip // 2 + step // 4, 2)
    column = lax.rem(lax.rem(chip, 2) + lax.rem(step // 2, 2), 2)
    place = {"dp": row * 2 + column, "ctx": lax.rem(core + lax.rem(step, 2), 2)}
    return place, place["dp"] * 2 + place["ctx"]


def greet_plane():
    barrier = pltpu.get_barrier_semaphore()
    for step in range(1, 8):
        place, _ = plane_peer(step)
        pl.semaphore_signal(barrier, inc=1, device_id=place, device_id_type=MESH_ID)
    pl.semaphore_wait(barrier, 7)


def plane_copy(source, target, send_sem, recv_sem, step):
    place, _ = plane_peer(step)
    return pltpu.make_async_remote_copy(
        src_ref=source.at[step],
        dst_ref=target.at[step],
        send_sem=send_sem.at[step],
        recv_sem=recv_sem.at[step],
        device_id=place,
        device_id_type=MESH_ID,
    )


def slot_hits(dest_rows, expert, capacity, tokens):
    slot = lax.broadcasted_iota(jnp.int32, (capacity, tokens), 0) + expert * capacity
    return (slot == dest_rows[0:1, :]) | (slot == dest_rows[1:2, :])


def token_hits(places, expert, capacity, tokens):
    slot = lax.broadcasted_iota(jnp.int32, (tokens, capacity), 1) + expert * capacity
    hit = (slot == places[:, 4:5]) | (slot == places[:, 5:6])
    return jnp.where(hit, 1.0, 0.0).astype(jnp.bfloat16)


def gate_of_rows(routes, gates, expert):
    return jnp.where(routes[0:1, :] == expert, gates[0:1, :], 0.0) + jnp.where(
        routes[1:2, :] == expert, gates[1:2, :], 0.0
    )


def gate_of_columns(places, gates, expert):
    return jnp.where(places[:, 2:3] == expert, gates[:, 0:1], 0.0) + jnp.where(
        places[:, 3:4] == expert, gates[:, 1:2], 0.0
    )


def arrival(i):
    return jnp.where(i < 2, i, 9 - i)


def experts_kernel(
    rows_ref, dest_rows, places, gates, inner_full, outer_full, counts_ref,
    mix_ref, arrived, returned, totals_ref,
    inner_ref, outer_ref, outgoing, results, counts, send_one, recv_one, send_two, recv_two, send_count, recv_count,
):
    capacity = arrived.shape[1]
    tokens = rows_ref.shape[0]
    greet_plane()
    counts[0] = counts_ref[...]

    def send_counts(step, carry):
        place, _ = plane_peer(step)
        pltpu.make_async_remote_copy(
            src_ref=counts_ref,
            dst_ref=counts.at[step],
            send_sem=send_count.at[step],
            recv_sem=recv_count.at[step],
            device_id=place,
            device_id_type=MESH_ID,
        ).start()
        return carry

    def dispatch(i, carry):
        step = 7 - i
        _, expert = plane_peer(step)
        hit = jnp.where(slot_hits(dest_rows, expert, capacity, tokens), 1.0, 0.0).astype(jnp.bfloat16)
        rows = jnp.dot(hit, rows_ref[...], preferred_element_type=jnp.float32).astype(jnp.bfloat16)

        @pl.when(step > 0)
        def _():
            outgoing[step] = rows
            plane_copy(outgoing, arrived, send_one, recv_one, step).start()

        @pl.when(step == 0)
        def _():
            arrived[0] = rows

        return carry

    def work(i, carry):
        step = arrival(i)

        @pl.when(step > 0)
        def _():
            plane_copy(outgoing, arrived, send_one, recv_one, step).wait_recv()

        before = jnp.dot(arrived[step], inner_ref[...], preferred_element_type=jnp.float32)
        active = gelu_tanh(before).astype(jnp.bfloat16)
        part = jnp.dot(active, outer_ref[...], preferred_element_type=jnp.float32).astype(jnp.bfloat16)

        @pl.when(step > 0)
        def _():
            results[step] = part
            plane_copy(results, returned, send_two, recv_two, step).start()

        @pl.when(step == 0)
        def _():
            returned[0] = part

        return carry

    def combine(i, carry):
        step = arrival(i)
        _, expert = plane_peer(step)
        hit = token_hits(places, expert, capacity, tokens)
        gate = gate_of_columns(places, gates, expert)

        @pl.when(step > 0)
        def _():
            plane_copy(results, returned, send_two, recv_two, step).wait_recv()

        part = gate * jnp.dot(hit, returned[step], preferred_element_type=jnp.float32)

        @pl.when(i == 0)
        def _():
            mix_ref[...] = part

        @pl.when(i > 0)
        def _():
            mix_ref[...] += part

        return carry

    def finish(step, carry):
        plane_copy(outgoing, arrived, send_one, recv_one, step).wait_send()
        plane_copy(results, returned, send_two, recv_two, step).wait_send()
        place, _ = plane_peer(step)
        pltpu.make_async_remote_copy(
            src_ref=counts_ref,
            dst_ref=counts.at[step],
            send_sem=send_count.at[step],
            recv_sem=recv_count.at[step],
            device_id=place,
            device_id_type=MESH_ID,
        ).wait()
        return carry

    lax.fori_loop(0, 8, dispatch, 0)
    lax.fori_loop(1, 8, send_counts, 0)
    inner_ref[...] = inner_full[...].astype(jnp.bfloat16)
    outer_ref[...] = outer_full[...].astype(jnp.bfloat16)
    lax.fori_loop(0, 8, work, 0)
    lax.fori_loop(0, 8, combine, 0)
    lax.fori_loop(1, 8, finish, 0)
    totals_ref[...] = jnp.sum(counts[...], 0)


def experts_forward(rows, dest, places, gates, inner, outer, counts, capacity, collective_id):
    tokens, width = rows.shape
    buffer = pltpu.VMEM((8, capacity, width), jnp.bfloat16)
    return pl.pallas_call(
        experts_kernel,
        out_shape=[
            jax.ShapeDtypeStruct((tokens, width), jnp.float32),
            jax.ShapeDtypeStruct((8, capacity, width), jnp.bfloat16),
            jax.ShapeDtypeStruct((8, capacity, width), jnp.bfloat16),
            jax.ShapeDtypeStruct(counts.shape, jnp.float32),
        ],
        in_specs=[whole_vmem] * 7,
        out_specs=[whole_vmem] * 4,
        scratch_shapes=[pltpu.VMEM(w.shape, jnp.bfloat16) for w in (inner, outer)]
        + [buffer, buffer, pltpu.VMEM((8,) + counts.shape, jnp.float32)]
        + [pltpu.SemaphoreType.DMA((8,))] * 6,
        compiler_params=pltpu.CompilerParams(
            collective_id=collective_id, has_side_effects=True, vmem_limit_bytes=60 << 20
        ),
    )(rows, dest, places, gates, inner, outer, counts)


def experts_back_kernel(
    rows_ref, dest_rows, places, gates, routes, returned, arrived, *refs
):
    inner_full, outer_full, grad_ref, gate_ref, inner_grad, outer_grad, inner_ref, outer_ref = refs[:8]
    outgoing, landed, results, landed_two, active, slopes = refs[8:14]
    send_one, recv_one, send_two, recv_two = refs[14:]
    capacity = arrived.shape[1]
    tokens = rows_ref.shape[0]
    greet_plane()
    gate_ref[...] = jnp.zeros_like(gate_ref)

    def dispatch(i, carry):
        step = 7 - i
        _, expert = plane_peer(step)
        hit = slot_hits(dest_rows, expert, capacity, tokens)
        rows = jnp.dot(
            jnp.where(hit, 1.0, 0.0).astype(jnp.bfloat16), rows_ref[...], preferred_element_type=jnp.float32
        )
        scale = jnp.sum(jnp.where(hit, gate_of_rows(routes, gates, expert), 0.0), 1, keepdims=True)
        sent = (rows * scale).astype(jnp.bfloat16)

        @pl.when(step > 0)
        def _():
            outgoing[step] = sent
            plane_copy(outgoing, landed, send_one, recv_one, step).start()

        @pl.when(step == 0)
        def _():
            landed[0] = sent

        dots = jnp.sum(rows * returned[step].astype(jnp.float32), 1, keepdims=True)
        part = jnp.sum(jnp.where(hit, dots, 0.0), 0, keepdims=True)
        for k in range(2):
            gate_ref[k : k + 1, :] += jnp.where(routes[k : k + 1, :] == expert, part, 0.0)
        return carry

    def work(i, carry):
        step = arrival(i)

        @pl.when(step > 0)
        def _():
            plane_copy(outgoing, landed, send_one, recv_one, step).wait_recv()

        grad_active = lax.dot_general(
            landed[step], outer_ref[...], (((1,), (1,)), ((), ())), preferred_element_type=jnp.float32
        )
        before = jnp.dot(arrived[step], inner_ref[...], preferred_element_type=jnp.float32)
        slope = (grad_active * gelu_slope(before)).astype(jnp.bfloat16)
        back = lax.dot_general(
            slope, inner_ref[...], (((1,), (1,)), ((), ())), preferred_element_type=jnp.float32
        ).astype(jnp.bfloat16)

        @pl.when(step > 0)
        def _():
            results[step] = back
            plane_copy(results, landed_two, send_two, recv_two, step).start()

        @pl.when(step == 0)
        def _():
            landed_two[0] = back

        slopes[step] = slope
        active[step] = gelu_tanh(before).astype(jnp.bfloat16)
        return carry

    def weigh(step, carry):
        outer_part = lax.dot_general(
            active[step], landed[step], (((0,), (0,)), ((), ())), preferred_element_type=jnp.float32
        )
        inner_part = lax.dot_general(
            arrived[step], slopes[step], (((0,), (0,)), ((), ())), preferred_element_type=jnp.float32
        )

        @pl.when(step == 0)
        def _():
            inner_grad[...] = inner_part
            outer_grad[...] = outer_part

        @pl.when(step > 0)
        def _():
            inner_grad[...] += inner_part
            outer_grad[...] += outer_part

        return carry

    def combine(i, carry):
        step = arrival(i)
        _, expert = plane_peer(step)
        hit = token_hits(places, expert, capacity, tokens)

        @pl.when(step > 0)
        def _():
            plane_copy(results, landed_two, send_two, recv_two, step).wait_recv()

        part = jnp.dot(hit, landed_two[step], preferred_element_type=jnp.float32)

        @pl.when(i == 0)
        def _():
            grad_ref[...] = part

        @pl.when(i > 0)
        def _():
            grad_ref[...] += part

        return carry

    def finish(step, carry):
        plane_copy(outgoing, landed, send_one, recv_one, step).wait_send()
        plane_copy(results, landed_two, send_two, recv_two, step).wait_send()
        return carry

    lax.fori_loop(0, 8, dispatch, 0)
    inner_ref[...] = inner_full[...].astype(jnp.bfloat16)
    outer_ref[...] = outer_full[...].astype(jnp.bfloat16)
    lax.fori_loop(0, 8, work, 0)
    lax.fori_loop(0, 8, weigh, 0)
    lax.fori_loop(0, 8, combine, 0)
    lax.fori_loop(1, 8, finish, 0)


def experts_backward(
    rows, dest, places, gates, routes, returned, arrived, inner, outer, collective_id
):
    tokens, width = rows.shape
    capacity = arrived.shape[1]
    inside = inner.shape[1]
    buffer = pltpu.VMEM((8, capacity, width), jnp.bfloat16)
    inside_buffer = pltpu.VMEM((8, capacity, inside), jnp.bfloat16)
    return pl.pallas_call(
        experts_back_kernel,
        out_shape=[
            jax.ShapeDtypeStruct((tokens, width), jnp.float32),
            jax.ShapeDtypeStruct((2, tokens), jnp.float32),
            jax.ShapeDtypeStruct((width, inside), jnp.float32),
            jax.ShapeDtypeStruct((inside, width), jnp.float32),
        ],
        in_specs=[whole_vmem] * 9,
        out_specs=[whole_vmem] * 4,
        scratch_shapes=[pltpu.VMEM(w.shape, jnp.bfloat16) for w in (inner, outer)]
        + [buffer] * 4
        + [inside_buffer] * 2
        + [pltpu.SemaphoreType.DMA((8,))] * 4,
        compiler_params=pltpu.CompilerParams(
            collective_id=collective_id, has_side_effects=True, vmem_limit_bytes=60 << 20
        ),
    )(rows, dest, places, gates, routes, returned, arrived, inner, outer)


def own_units_kernel(
    chunks, units_of, slopes_ref, rows_ref, ids_ref, zero_ref, joint_ref, normed_ref, attended_ref,
    grad_ref, small_ref, grads_ref, small_out, *refs
):
    slopes, late, mixed, made, passing, own, other, relay, landed, small_landed, ready = refs[:11]
    other_send, other_recv, relay_send, relay_recv, landed_send, landed_recv = refs[11:17]
    small_send, small_recv, load_sem, store_sem = refs[17:]
    chip, core = lax.axis_index("dp"), lax.axis_index("ctx")
    beside = chip + 1 - 2 * lax.rem(chip, 2)
    across = lax.rem(chip + 2, 4)
    opposite = across + 1 - 2 * lax.rem(across, 2)
    places = (opposite, beside, across, chip)
    slots, unit_rows = own.shape[1:3]
    table_units = slopes.shape[0]
    tokens = rows_ref.shape[0]
    size = slots // chunks
    split = (chunks + 1) // 2
    load = pltpu.make_async_copy(slopes_ref, slopes, load_sem)
    load.start()
    greet_plane()

    def repeat(first, last, body):
        def step(i, carry):
            body(i)
            return carry

        lax.fori_loop(first, last, step, 0)

    def span(q):
        return pl.ds(q * size, size)

    def remote(source, target, send, recv, place):
        return pltpu.make_async_remote_copy(
            src_ref=source,
            dst_ref=target,
            send_sem=send,
            recv_sem=recv,
            device_id=place,
            device_id_type=MESH_ID,
        )

    def pass_over(k, q):
        return remote(
            passing.at[k % 2, span(q)],
            other.at[k, span(q)],
            other_send.at[k, q],
            other_recv.at[k, q],
            {"ctx": 1 - core},
        )

    def to_relay(q, place):
        return remote(own.at[0, span(q)], relay.at[span(q)], relay_send.at[q], relay_recv.at[q], {"dp": place})

    def to_owner(k, q):
        return remote(
            own.at[k, span(q)],
            landed.at[k - 1, span(q)],
            landed_send.at[k - 1, q],
            landed_recv.at[k - 1, q],
            {"dp": places[k]},
        )

    def small_copy(step):
        place, _ = plane_peer(step)
        return remote(
            small_ref, small_landed.at[chip * 2 + core], small_send.at[step], small_recv.at[step], place
        )

    joint_units = joint_ref.shape[0] // unit_rows
    late[pl.ds(0, joint_units)] = jnp.dot(
        joint_ref[...], normed_ref[...], preferred_element_type=jnp.float32
    ).reshape(joint_units, unit_rows, -1)
    last_units = attended_ref.shape[0] // unit_rows
    late[pl.ds(joint_units, last_units)] = jnp.dot(
        attended_ref[...], grad_ref[...], preferred_element_type=jnp.float32
    ).reshape(last_units, unit_rows, -1)
    load.wait()
    group = made.shape[0] // unit_rows

    def form(owner, target):
        def some(g):
            first = owner * slots + g * group

            def fill(s):
                unit = units_of[first + s]
                lines = pl.ds(pl.multiple_of(s * unit_rows, unit_rows), unit_rows)
                mixed[lines, :tokens] = slopes[jnp.minimum(unit, table_units - 1)]
                row = lax.broadcasted_iota(jnp.int32, (unit_rows, tokens), 0) + unit * unit_rows
                mixed[lines, tokens:] = jnp.where(row == ids_ref[...], 1.0, 0.0).astype(jnp.bfloat16)

            repeat(0, group, fill)
            made[...] = jnp.dot(
                mixed[:, :tokens], rows_ref[...], preferred_element_type=jnp.float32
            ) + jnp.dot(mixed[:, tokens:], zero_ref[...], preferred_element_type=jnp.float32)

            def put(s):
                unit = units_of[first + s]
                table_piece = made[pl.ds(pl.multiple_of(s * unit_rows, unit_rows), unit_rows)]
                late_piece = late[jnp.clip(unit - table_units, 0, late.shape[0] - 1)]
                marks = jnp.zeros(table_piece.shape, jnp.int32) + unit
                piece = jnp.where(marks < table_units, table_piece, late_piece)
                target[g * group + s] = piece.astype(jnp.bfloat16)

            repeat(0, group, put)

        repeat(0, slots // group, some)

    def joined(k, q):
        pass_over(k, q).wait_recv()
        return own[k, span(q)].astype(jnp.float32) + other[k, span(q)].astype(jnp.float32)

    def first_leg(place):
        def leg(q):
            own[0, span(q)] = joined(0, q).astype(jnp.bfloat16)
            to_relay(q, place).start()

        return leg

    def direct(k):
        def leg(q):
            own[k, span(q)] = joined(k, q).astype(jnp.bfloat16)
            to_owner(k, q).start()

        return leg

    def relayed(k, place):
        def leg(q):
            to_relay(q, place).wait_recv()
            total = joined(k, q) + relay[span(q)].astype(jnp.float32)
            own[k, span(q)] = total.astype(jnp.bfloat16)
            to_owner(k, q).start()

        return leg

    def form_pair(k):
        if k >= 2:
            repeat(0, chunks, lambda q: pass_over(k - 2, q).wait_send())
        form(places[k] * 2 + 1 - core, passing.at[k % 2])
        repeat(0, chunks, lambda q: pass_over(k, q).start())
        form(places[k] * 2 + core, own.at[k])

    form_pair(0)
    repeat(0, split, first_leg(beside))
    repeat(split, chunks, first_leg(across))
    repeat(1, 8, lambda step: small_copy(step).start())
    small_landed[chip * 2 + core] = small_ref[...]
    form_pair(1)
    repeat(0, split, direct(1))
    form_pair(2)
    repeat(split, chunks, direct(2))
    repeat(0, split, relayed(2, beside))
    repeat(split, chunks, relayed(1, across))
    form_pair(3)

    def store(q):
        return pltpu.make_async_copy(
            ready.at[lax.rem(q, 2)], grads_ref.at[span(q)], store_sem.at[lax.rem(q, 2)]
        )

    def keep(q):
        total = joined(3, q)
        to_owner(1, q).wait_recv()
        to_owner(2, q).wait_recv()

        @pl.when(q >= 2)
        def _():
            store(q - 2).wait()

        ready[lax.rem(q, 2)] = (
            total + landed[0, span(q)].astype(jnp.float32) + landed[1, span(q)].astype(jnp.float32)
        )
        store(q).start()

    repeat(0, chunks, keep)

    def finish(q):
        for k in (2, 3):
            pass_over(k, q).wait_send()
        to_owner(1, q).wait_send()
        to_owner(2, q).wait_send()

    repeat(0, chunks, finish)
    repeat(0, split, lambda q: to_relay(q, beside).wait_send())
    repeat(split, chunks, lambda q: to_relay(q, across).wait_send())
    repeat(1, 8, lambda step: small_copy(step).wait())
    total = small_landed[0]
    for source in range(1, 8):
        total = total + small_landed[source]
    small_out[...] = total
    for q in range(max(0, chunks - 2), chunks):
        store(q).wait()


def own_units(units_of, slots, unit_rows, slopes, rows, ids, zero, joint, normed, attended, grad, small, collective_id):
    tokens, width = rows.shape
    unit = (unit_rows, width)
    chunks = max(k for k in range(1, 8) if slots % k == 0)
    group = max(k for k in range(1, 8) if slots % k == 0)
    late = (joint.shape[0] + attended.shape[0]) // unit_rows
    slopes = slopes.reshape(-1, unit_rows, tokens)
    return pl.pallas_call(
        functools.partial(own_units_kernel, chunks),
        out_shape=[
            jax.ShapeDtypeStruct((slots,) + unit, jnp.float32),
            jax.ShapeDtypeStruct(small.shape, jnp.float32),
        ],
        in_specs=[pl.BlockSpec(memory_space=pltpu.SMEM), whole_any] + [whole_vmem] * 8,
        out_specs=[whole_any, whole_vmem],
        scratch_shapes=[
            pltpu.VMEM(slopes.shape, jnp.bfloat16),
            pltpu.VMEM((late,) + unit, jnp.float32),
            pltpu.VMEM((group * unit_rows, 2 * tokens), jnp.bfloat16),
            pltpu.VMEM((group * unit_rows, width), jnp.float32),
            pltpu.VMEM((2, slots) + unit, jnp.bfloat16),
            pltpu.VMEM((4, slots) + unit, jnp.bfloat16),
            pltpu.VMEM((4, slots) + unit, jnp.bfloat16),
            pltpu.VMEM((slots,) + unit, jnp.bfloat16),
            pltpu.VMEM((2, slots) + unit, jnp.bfloat16),
            pltpu.VMEM((8,) + small.shape, jnp.float32),
            pltpu.VMEM((2, slots // chunks) + unit, jnp.float32),
            pltpu.SemaphoreType.DMA((4, chunks)),
            pltpu.SemaphoreType.DMA((4, chunks)),
            pltpu.SemaphoreType.DMA((chunks,)),
            pltpu.SemaphoreType.DMA((chunks,)),
            pltpu.SemaphoreType.DMA((2, chunks)),
            pltpu.SemaphoreType.DMA((2, chunks)),
            pltpu.SemaphoreType.DMA((8,)),
            pltpu.SemaphoreType.DMA((8,)),
            pltpu.SemaphoreType.DMA,
            pltpu.SemaphoreType.DMA((2,)),
        ],
        compiler_params=pltpu.CompilerParams(
            collective_id=collective_id, has_side_effects=True, vmem_limit_bytes=63 << 20
        ),
    )(units_of, slopes, rows, ids, zero, joint, normed, attended, grad, small)


def update_kernel(rates_ref, filled_ref, grad_ref, small_ref, *refs):
    states, shared = refs[:3], refs[3:12]
    updated, renewed = refs[12:15], refs[15:]
    step = pl.program_id(0)
    size = grad_ref.shape[0]
    for n in range(size):
        slot = step * size + n
        marks = jnp.zeros(grad_ref.shape[1:], jnp.int32) + filled_ref[slot]
        gradient = jnp.where(marks > 0, grad_ref[n], 0.0)
        fresh = adam_update(*(state[n] for state in states), gradient, rates_ref[slot], decay_rate)
        for k in range(3):
            updated[k][n] = fresh[k]

    @pl.when(step == 0)
    def _():
        experts = shared[3].shape[1]
        heads, buckets = shared[6].shape
        line = small_ref[3 + experts : 4 + experts, :]
        biases = [line[:, h * buckets : (h + 1) * buckets] for h in range(heads)]
        gradients = (
            small_ref[0:3, :],
            small_ref[3 : 3 + experts, :].T,
            jnp.concatenate(biases, 0),
        )
        rates = ((rate_gains, 0.0), (rate_router, decay_rate), (rate_biases, 0.0))
        for j in range(3):
            fresh = adam_update(*(x[...] for x in shared[3 * j : 3 * j + 3]), gradients[j], *rates[j])
            for k in range(3):
                renewed[3 * j + k][...] = fresh[k]


def update_all(rates, filled, grad, small, states, shared):
    slots = grad.shape[0]
    size = max(k for k in range(1, 5) if slots % k == 0)
    block = pl.BlockSpec((size,) + grad.shape[1:], lambda k: (k, 0, 0))
    whole = lambda x: pl.BlockSpec(x.shape, lambda k: (0,) * x.ndim)
    scalars = pl.BlockSpec(memory_space=pltpu.SMEM)
    return pl.pallas_call(
        update_kernel,
        grid=(slots // size,),
        out_shape=[jax.ShapeDtypeStruct(x.shape, jnp.float32) for x in (*states, *shared)],
        in_specs=[scalars] * 2 + [block, whole(small)] + [block] * 3 + [whole(x) for x in shared],
        out_specs=[block] * 3 + [whole(x) for x in shared],
        compiler_params=pltpu.CompilerParams(vmem_limit_bytes=40 << 20),
    )(rates, filled, grad, small, *states, *shared)


def to_plane(buffer):
    return lax.all_to_all(buffer, ("dp", "ctx"), split_axis=0, concat_axis=0, tiled=True)


def plain_hits(dest, experts, capacity):
    slots = lax.broadcasted_iota(jnp.int32, (experts * capacity, dest.shape[1]), 0)
    return [slots == dest[k : k + 1] for k in range(2)]


def plain_forward(rows, dest, gates, inner, outer, owners, capacity):
    width = rows.shape[1]
    hits = plain_hits(dest, owners, capacity)
    both = (hits[0] | hits[1]).astype(jnp.bfloat16)
    sent = jnp.dot(both, rows, preferred_element_type=jnp.float32).astype(jnp.bfloat16)
    arrived = to_plane(sent.reshape(owners, capacity, width))
    hidden = jnp.einsum("ocd,df->ocf", arrived, inner, preferred_element_type=jnp.float32)
    active = gelu_tanh(hidden).astype(jnp.bfloat16)
    part = jnp.einsum("ocf,fd->ocd", active, outer, preferred_element_type=jnp.float32)
    returned = to_plane(part.astype(jnp.bfloat16))
    flat = returned.reshape(owners * capacity, width)
    mix = sum(
        gates[:, k : k + 1]
        * lax.dot_general(
            hits[k].astype(jnp.bfloat16),
            flat,
            (((0,), (0,)), ((), ())),
            preferred_element_type=jnp.float32,
        )
        for k in range(2)
    )
    return (mix, arrived, returned)


def plain_backward(rows, dest, gates, returned, arrived, inner, outer):
    owners, capacity, width = arrived.shape
    hits = plain_hits(dest, owners, capacity)
    both = (hits[0] | hits[1]).astype(jnp.bfloat16)
    slot_scale = jnp.sum(
        jnp.where(hits[0], gates[0:1], 0.0) + jnp.where(hits[1], gates[1:2], 0.0), 1, keepdims=True
    )
    slot_grads = jnp.dot(both, rows, preferred_element_type=jnp.float32)
    sent = (slot_grads * slot_scale).astype(jnp.bfloat16)
    flat = returned.reshape(owners * capacity, width)
    dots = jnp.sum(slot_grads * flat.astype(jnp.float32), 1, keepdims=True)
    gate_part = jnp.concatenate(
        [jnp.sum(jnp.where(hit, dots, 0.0), 0, keepdims=True) for hit in hits], 0
    )
    landed = to_plane(sent.reshape(owners, capacity, width))
    grad_active = jnp.einsum("ocd,fd->ocf", landed, outer, preferred_element_type=jnp.float32)
    hidden = jnp.einsum("ocd,df->ocf", arrived, inner, preferred_element_type=jnp.float32)
    active = gelu_tanh(hidden).astype(jnp.bfloat16)
    slope = (grad_active * gelu_slope(hidden)).astype(jnp.bfloat16)
    outer_grad = jnp.einsum("ocf,ocd->fd", active, landed, preferred_element_type=jnp.float32)
    inner_grad = jnp.einsum("ocd,ocf->df", arrived, slope, preferred_element_type=jnp.float32)
    back = jnp.einsum("ocf,df->ocd", slope, inner, preferred_element_type=jnp.float32)
    back = to_plane(back.astype(jnp.bfloat16)).reshape(owners * capacity, width)
    grad = lax.dot_general(
        both, back, (((0,), (0,)), ((), ())), preferred_element_type=jnp.float32
    )
    return (grad, gate_part, inner_grad, outer_grad)


def on_device(
    token_ids,
    targets,
    counted,
    routes,
    priority,
    owner_of,
    master,
    master_first,
    master_second,
    expert_in,
    expert_in_first,
    expert_in_second,
    expert_out,
    expert_out_first,
    expert_out_second,
    norm_gains,
    norm_gains_first,
    norm_gains_second,
    router,
    router_first,
    router_second,
    rel_bias,
    rel_bias_first,
    rel_bias_second,
):
    owners = lax.axis_size(("dp", "ctx"))
    tensor_ranks = lax.axis_size("tensor")
    my_owner = lax.axis_index(("dp", "ctx"))
    my_rank = lax.axis_index("tensor")
    my_context = lax.axis_index("ctx")
    sequences, half_length = token_ids.shape
    tokens_here = sequences * half_length
    most_units = master.shape[2]
    unit_rows = master.shape[3]
    model_width = master.shape[4]
    vocab_here = VOCAB // tensor_ranks
    heads_here = rel_bias.shape[0]
    head_size = model_width // (heads_here * tensor_ranks)
    hidden_here = heads_here * head_size
    experts = router.shape[1]
    capacity = (18 * tokens_here + 8 * experts - 1) // (8 * experts)
    table_units = vocab_here // unit_rows
    query_units = table_units + 2 * hidden_here // unit_rows
    value_units = table_units + 3 * hidden_here // unit_rows
    embed_scale = math.sqrt(model_width)
    owner_ids = owner_of[:, 0]
    on_square = lax.axis_size("dp") == 4 and lax.axis_size("ctx") == 2
    unit_rank, slot_unit, slot_filled = slot_tables(owner_ids, owners, most_units)
    counted_rows = counted.reshape(tokens_here, 2).T.astype(jnp.float32)
    loss_weights = counted_rows * jnp.array([[1.0], [ahead_weight]], jnp.float32)
    counts = jnp.zeros((8, 128), jnp.float32).at[0:2].set(jnp.sum(counted_rows, 1, keepdims=True))
    unit_slots = owner_ids * most_units + unit_rank
    route_pairs = routes.reshape(tokens_here, 2)
    pair_kept, pair_dest = pair_slots(route_pairs, priority[0], experts, capacity)
    dest = jnp.where(pair_kept, pair_dest, -1).reshape(2, tokens_here)
    unit_slots, dest = lax.optimization_barrier((unit_slots, dest))
    local_ids = token_ids.reshape(-1) - my_rank * vocab_here
    inside = (local_ids >= 0) & (local_ids < vocab_here)
    clipped_ids = jnp.clip(local_ids, 0, vocab_here - 1)
    unit_starts = jnp.sum(
        jnp.where(
            (clipped_ids // unit_rows)[None, :] == jnp.arange(unit_slots.shape[0])[:, None],
            unit_slots[:, None] * unit_rows,
            0,
        ),
        0,
    )
    slot_rows = unit_starts + clipped_ids % unit_rows
    if on_square:
        slot_rows = jnp.where(inside, slot_rows, -1)[:, None]
        weights_low, embedded, normed_one_low, joint, joint_low, project_low = embed(
            unit_slots,
            master[0, 0],
            slot_rows,
            norm_gains[0:1],
            table_units,
            3 * hidden_here,
            11,
        )
    else:
        master_low = master[0, 0].astype(jnp.bfloat16)
        gathered = lax.all_gather(master_low, ("dp", "ctx"), axis=0, tiled=True)
        looked = jnp.take(gathered.reshape(-1, model_width), slot_rows, axis=0)
        looked = jnp.where(inside[:, None], looked, 0)
        weights_low = pull_units([gathered], unit_slots)
        (embedded,) = sum_line(looked, [], [], keep_total, 1)
    weights_low = weights_low.reshape(-1, model_width)
    if not on_square:
        joint_low = weights_low[vocab_here : vocab_here + 3 * hidden_here]
        project_low = weights_low[vocab_here + 3 * hidden_here :]
    rolled = [project_low] + [
        lax.ppermute(project_low, "tensor", [(source, (source + step) % 4) for source in range(4)])
        for step in (1, 2, 3)
    ]
    gain_rows = [norm_gains[k : k + 1] for k in range(3)]
    stream_shape = jax.ShapeDtypeStruct((tokens_here, model_width), jnp.float32)
    gain_shape = jax.ShapeDtypeStruct((1, model_width), jnp.float32)
    if not on_square:
        stream_zero = embedded.astype(jnp.float32) * embed_scale
        normed_one_low = norm_forward(stream_zero, norm_gains[0]).astype(jnp.bfloat16)
        joint = lax.dot_general(
            joint_low, normed_one_low, (((1,), (1,)), ((), ())), preferred_element_type=jnp.float32
        ).astype(jnp.bfloat16)
    attended_all, logsum_rows, pairs_before, attended = attention(
        rel_bias, joint, heads_here, head_size, 2
    )
    router_low = router.astype(jnp.bfloat16)
    stream_one, normed_two_low, gate_rows, gate_columns, places = middle(
        attended_all.reshape(model_width, tokens_here),
        rolled,
        embedded,
        gain_rows[1],
        router_low.T,
        route_pairs.T,
        dest,
    )
    if on_square:
        moe_partial, arrived, returned, counts = experts_forward(
            normed_two_low, dest, places, gate_columns, expert_in[0], expert_out[0], counts, capacity, 8
        )
    else:
        inner_low, outer_low = expert_in[0].astype(jnp.bfloat16), expert_out[0].astype(jnp.bfloat16)
        moe_partial, arrived, returned = plain_forward(
            normed_two_low, dest, gate_columns, inner_low, outer_low, owners, capacity
        )
        counts = lax.psum(counts, ("dp", "ctx"))
    weight_total = counts[0, 0] + ahead_weight * counts[1, 0]
    local_targets = targets.reshape(tokens_here, 2).T - my_rank * vocab_here
    weight_rows = jnp.concatenate(
        [
            loss_weights,
            loss_weights[0:1] + loss_weights[1:2],
            jnp.broadcast_to(1.0 / weight_total, (1, tokens_here)),
        ],
        0,
    )
    head_low, grad_two_low, grad_two, gain_grad_three, logsum_vocab, target_sums, slopes = head_line(
        moe_partial, stream_one, gain_rows[2], weights_low, local_targets, weight_rows, vocab_here, 3
    )
    if on_square:
        moe_grad_part, gate_part, inner_grad, outer_grad = experts_backward(
            grad_two_low,
            dest,
            places,
            gate_rows,
            route_pairs.T,
            returned,
            arrived,
            expert_in[0],
            expert_out[0],
            9,
        )
    else:
        moe_grad_part, gate_part, inner_grad, outer_grad = plain_backward(
            grad_two_low, dest, gate_rows, returned, arrived, inner_low, outer_low
        )
    gate_part = jnp.concatenate([gate_part, target_sums, jnp.zeros_like(target_sums)], 0)
    gate_block = pltpu.VMEM((3, 4, tokens_here), jnp.float32)
    grad_one_low, grad_one, logit_grad, target_total, gain_grad_two = sum_line(
        moe_grad_part,
        [
            stream_one,
            gain_rows[1],
            grad_two,
            gate_part,
            gate_rows,
            route_pairs.T,
            router_low,
        ],
        [
            stream_shape,
            jax.ShapeDtypeStruct((experts, tokens_here), jnp.bfloat16),
            jax.ShapeDtypeStruct((1, tokens_here), jnp.float32),
            gain_shape,
        ],
        finish_expert_grad,
        5,
        prologue=start_router_grad,
        scratch=(gate_block, pltpu.SemaphoreType.DMA((3,)), pltpu.SemaphoreType.DMA((3,))),
        opening=send_gate_parts,
    )
    router_grad = jnp.dot(logit_grad, normed_two_low, preferred_element_type=jnp.float32)
    loss_local = jnp.sum(weight_rows[2:3] * logsum_vocab) - jnp.sum(target_total)
    query_grad, pair_grad, before_grad, bias_lines, *expert_states = attention_back(
        rel_bias,
        joint,
        pairs_before,
        logsum_rows,
        grad_one_low,
        project_low,
        (
            expert_in[0],
            expert_in_first[0],
            expert_in_second[0],
            inner_grad,
            expert_out[0],
            expert_out_first[0],
            expert_out_second[0],
            outer_grad,
        ),
        heads_here,
        head_size,
    )
    distances = 2 * (half_length // BLOCK)
    bias_grad = jnp.sum(bias_lines, 1).reshape(heads_here, distances)
    pair_shape = pltpu.VMEM((2 * hidden_here, tokens_here), jnp.bfloat16)
    zero_grad_low, joint_grad, gain_grads = sum_line(
        None,
        [
            embedded,
            gain_rows[0],
            grad_one,
            gain_grad_two,
            gain_grad_three,
            query_grad,
            pair_grad,
            before_grad,
            joint_low,
        ],
        [
            jax.ShapeDtypeStruct((3 * hidden_here, tokens_here), jnp.bfloat16),
            jax.ShapeDtypeStruct((8, model_width), jnp.float32),
        ],
        functools.partial(finish_input_grad, embed_scale),
        6,
        prologue=clear_gain,
        scratch=(
            pltpu.SemaphoreType.DMA,
            pltpu.SemaphoreType.DMA,
            pair_shape,
            pltpu.SemaphoreType.DMA((2,)),
            pltpu.VMEM((tokens_here, model_width), jnp.float32),
        ),
        opening=form_joint_grad,
        ending=share_gains,
    )
    my_units = jnp.take(slot_unit, my_owner, axis=0)
    my_filled = jnp.take(slot_filled, my_owner, axis=0).astype(jnp.int32)
    bias_row = jnp.concatenate([bias_grad.reshape(-1), loss_local[None]])
    bias_row = jnp.pad(bias_row, (0, model_width - bias_row.shape[0]))[None]
    small = jnp.concatenate([gain_grads[:3], router_grad, bias_row], 0)
    small = jnp.pad(small, ((0, -small.shape[0] % 8), (0, 0)))
    slot_rates = unit_rates(my_units, table_units, query_units, value_units)
    states = (master[0, 0], master_first[0, 0], master_second[0, 0])
    grad_rows = (
        slopes,
        head_low,
        local_ids[None, :],
        zero_grad_low,
        joint_grad,
        normed_one_low,
        attended,
        grad_one_low,
    )
    if on_square:
        mine, small = own_units(slot_unit.reshape(-1), most_units, unit_rows, *grad_rows, small, 10)
    else:
        outgoing = weight_grads(unit_slots, owners * most_units, unit_rows, *grad_rows)
        mine = lax.psum_scatter(
            outgoing.astype(jnp.float32), ("dp", "ctx"), scatter_dimension=0, tiled=True
        )
        small = lax.psum(small, ("dp", "ctx"))
    shared = (
        norm_gains,
        norm_gains_first,
        norm_gains_second,
        router,
        router_first,
        router_second,
        rel_bias,
        rel_bias_first,
        rel_bias_second,
    )
    fresh = update_all(slot_rates, my_filled, mine, small, states, shared)
    states, shared = fresh[:3], fresh[3:]
    loss_totals = jnp.stack([small[3 + experts, rel_bias.size], weight_total])
    return (
        loss_totals,
        *(state[None, None] for state in states),
        *(state[None] for state in expert_states),
        *shared,
    )


def solution(mesh):
    in_specs = (
        P("dp", "ctx"),
        P("dp", "ctx", None),
        P("dp", "ctx", None),
        P("dp", "ctx", None),
        P(("dp", "ctx"), None),
        P(),
        P("tensor", ("dp", "ctx"), None, None, None),
        P("tensor", ("dp", "ctx"), None, None, None),
        P("tensor", ("dp", "ctx"), None, None, None),
        P(("dp", "ctx"), None, "tensor"),
        P(("dp", "ctx"), None, "tensor"),
        P(("dp", "ctx"), None, "tensor"),
        P(("dp", "ctx"), "tensor", None),
        P(("dp", "ctx"), "tensor", None),
        P(("dp", "ctx"), "tensor", None),
        P(),
        P(),
        P(),
        P(),
        P(),
        P(),
        P("tensor", None),
        P("tensor", None),
        P("tensor", None),
    )
    out_specs = (
        P(),
        P("tensor", ("dp", "ctx"), None, None, None),
        P("tensor", ("dp", "ctx"), None, None, None),
        P("tensor", ("dp", "ctx"), None, None, None),
        P(("dp", "ctx"), None, "tensor"),
        P(("dp", "ctx"), None, "tensor"),
        P(("dp", "ctx"), None, "tensor"),
        P(("dp", "ctx"), "tensor", None),
        P(("dp", "ctx"), "tensor", None),
        P(("dp", "ctx"), "tensor", None),
        P(),
        P(),
        P(),
        P(),
        P(),
        P(),
        P("tensor", None),
        P("tensor", None),
        P("tensor", None),
    )
    return jax.shard_map(
        on_device, mesh=mesh, in_specs=in_specs, out_specs=out_specs, check_vma=False
    )
```

```python
import functools
import math

import jax
import jax.numpy as jnp
from jax import lax
from jax.experimental import pallas as pl
from jax.experimental.pallas import tpu as pltpu
from jax.sharding import PartitionSpec as P

VOCAB = 32000
BLOCK = 256
STEP = 10


highest_precision = lax.Precision.HIGHEST
beta_first = 0.9
beta_second = 0.95
adam_epsilon = 1e-08
norm_epsilon = 1e-06
ahead_weight = 0.3
masked_score = -1e30
rate_table = 0.1
rate_query = 0.05
rate_values = 0.05
rate_project = 0.5
rate_inner = 0.05
rate_outer = 0.03
rate_gains = 0.5
rate_router = 0.05
rate_biases = 0.5
decay_rate = 0.1


MESH_ID = pl.DeviceIdType.MESH
whole_vmem = pl.BlockSpec(memory_space=pltpu.VMEM)
whole_any = pl.BlockSpec(memory_space=pl.ANY)
line_lag = 2


def sum_line_kernel(
    rows, count, opening, with_core, prologue, epilogue, ending, n_extra, n_aux, n_scratch, *refs
):
    extras = refs[:n_extra]
    out_ref = refs[n_extra]
    aux = refs[n_extra + 1 : n_extra + 1 + n_aux]
    rest = refs[n_extra + 1 + n_aux :]
    scratch = rest[:n_scratch]
    part_ref = scratch[-1] if with_core else extras[0]
    extras = extras if with_core else extras[1:]
    stage, from_end, from_mid, send_sem, end_sem, mid_sem, back_sem, back_recv = rest[n_scratch:]
    rank = lax.axis_index("tensor")
    inner = (rank == 1) | (rank == 2)
    end_peer = jnp.where(rank < 2, 1 - rank, 5 - rank)
    mid_peer = 3 - rank
    barrier = pltpu.get_barrier_semaphore()
    if opening is None or with_core:
        pl.semaphore_signal(barrier, inc=1, device_id={"tensor": end_peer}, device_id_type=MESH_ID)
        if with_core:
            other_core = {"ctx": 1 - lax.axis_index("ctx")}
            pl.semaphore_signal(barrier, inc=1, device_id=other_core, device_id_type=MESH_ID)

        @pl.when(inner)
        def _():
            pl.semaphore_signal(
                barrier, inc=1, device_id={"tensor": mid_peer}, device_id_type=MESH_ID
            )
            pl.semaphore_wait(barrier, 2 + with_core)

        @pl.when(jnp.logical_not(inner))
        def _():
            pl.semaphore_wait(barrier, 1 + with_core)
    else:
        for step in (1, 2, 3):
            other = lax.rem(rank + step, 4)
            pl.semaphore_signal(barrier, inc=1, device_id={"tensor": other}, device_id_type=MESH_ID)
        pl.semaphore_wait(barrier, 3)

    def span(i):
        return pl.ds(pl.multiple_of(i * rows, rows), rows)

    def to_inner(i):
        return pltpu.make_async_remote_copy(
            src_ref=stage.at[i],
            dst_ref=from_end.at[i],
            send_sem=send_sem.at[i],
            recv_sem=end_sem.at[i],
            device_id={"tensor": end_peer},
            device_id_type=MESH_ID,
        )

    def to_middle(i):
        return pltpu.make_async_remote_copy(
            src_ref=stage.at[i],
            dst_ref=from_mid.at[i],
            send_sem=send_sem.at[i],
            recv_sem=mid_sem.at[i],
            device_id={"tensor": mid_peer},
            device_id_type=MESH_ID,
        )

    def to_end(i):
        return pltpu.make_async_remote_copy(
            src_ref=out_ref.at[span(i)],
            dst_ref=out_ref.at[span(i)],
            send_sem=back_sem.at[i],
            recv_sem=back_recv.at[i],
            device_id={"tensor": end_peer},
            device_id_type=MESH_ID,
        )

    if opening is not None:
        opening(rank, extras, aux, scratch)

    @pl.when(jnp.logical_not(inner))
    def _():
        def push(i, carry):
            stage[i] = part_ref[span(i)].astype(jnp.bfloat16)
            to_inner(i).start()
            return carry

        lax.fori_loop(0, count, push, 0)

    if prologue is not None:
        prologue(rank, inner, extras, aux, scratch)

    @pl.when(inner)
    def _():
        def step(i, carry):
            @pl.when(i < count)
            def _():
                to_inner(i).wait_recv()
                mine = part_ref[span(i)].astype(jnp.float32) + from_end[i].astype(jnp.float32)
                stage[i] = mine.astype(jnp.bfloat16)
                to_middle(i).start()

            @pl.when(i >= line_lag)
            def _():
                j = i - line_lag
                to_middle(j).wait_recv()
                total = stage[j].astype(jnp.float32) + from_mid[j].astype(jnp.float32)
                out_ref[span(j)] = epilogue(total, span(j), rank, extras, aux, scratch)
                to_end(j).start()

            return carry

        lax.fori_loop(0, count + line_lag, step, 0)

        def drain(i, carry):
            to_middle(i).wait_send()
            to_end(i).wait_send()
            return carry

        lax.fori_loop(0, count, drain, 0)

    @pl.when(jnp.logical_not(inner))
    def _():
        def finish(i, carry):
            to_end(i).wait_recv()
            to_inner(i).wait_send()
            return carry

        lax.fori_loop(0, count, finish, 0)

    if ending is not None:
        ending(inner, end_peer, extras, aux, scratch)


def sum_line(
    part,
    extras,
    aux_shapes,
    epilogue,
    collective_id,
    prologue=None,
    scratch=(),
    opening=None,
    ending=None,
    rows=64,
):
    tokens, width = scratch[-1].shape if part is None else part.shape
    inputs = list(extras) if part is None else [part, *extras]
    count = tokens // rows
    chunks = pltpu.VMEM((count, rows, width), jnp.bfloat16)
    return pl.pallas_call(
        functools.partial(
            sum_line_kernel,
            rows,
            count,
            opening,
            part is None,
            prologue,
            epilogue,
            ending,
            len(inputs),
            len(aux_shapes),
            len(scratch),
        ),
        out_shape=[jax.ShapeDtypeStruct((tokens, width), jnp.bfloat16)] + list(aux_shapes),
        in_specs=[whole_vmem] * len(inputs),
        out_specs=[whole_vmem] * (1 + len(aux_shapes)),
        scratch_shapes=list(scratch)
        + [chunks, chunks, chunks]
        + [pltpu.SemaphoreType.DMA((count,))] * 5,
        compiler_params=pltpu.CompilerParams(
            collective_id=collective_id, has_side_effects=True, vmem_limit_bytes=48 << 20
        ),
    )(*inputs)


def keep_total(total, span, rank, extras, aux, scratch):
    return total.astype(jnp.bfloat16)


def inverse_rms(values):
    return lax.rsqrt(jnp.mean(values * values, -1, keepdims=True) + norm_epsilon)


def norm_back_rows(values, gain, upstream):
    inverse = inverse_rms(values)
    normed = values * inverse
    scaled = upstream * gain
    gain_grad = jnp.sum(upstream * normed, 0, keepdims=True)
    inputs_grad = inverse * (scaled - normed * jnp.mean(scaled * normed, -1, keepdims=True))
    return (inputs_grad, gain_grad)


def clear_gain(rank, inner, extras, aux, scratch):
    @pl.when(inner)
    def _():
        aux[-1][...] = jnp.zeros_like(aux[-1])


def share_gains(inner, end_peer, extras, aux, scratch):
    gains = aux[-1]
    copy = pltpu.make_async_remote_copy(
        src_ref=gains,
        dst_ref=gains,
        send_sem=scratch[0],
        recv_sem=scratch[1],
        device_id={"tensor": end_peer},
        device_id_type=MESH_ID,
    )

    @pl.when(inner)
    def _():
        gains[1:2, :] = extras[3][...]
        gains[2:3, :] = extras[4][...]
        copy.start()
        copy.wait_send()

    @pl.when(jnp.logical_not(inner))
    def _():
        copy.wait_recv()


def gate_copies(rank, extras, scratch):
    gate_part = extras[3]
    landed, gate_send, gate_recv = scratch
    return [
        pltpu.make_async_remote_copy(
            src_ref=gate_part,
            dst_ref=landed.at[step - 1],
            send_sem=gate_send.at[step - 1],
            recv_sem=gate_recv.at[step - 1],
            device_id={"tensor": lax.rem(rank + step, 4)},
            device_id_type=MESH_ID,
        )
        for step in (1, 2, 3)
    ]


def send_gate_parts(rank, extras, aux, scratch):
    for copy in gate_copies(rank, extras, scratch):
        copy.start()


def start_router_grad(rank, inner, extras, aux, scratch):
    stream_one, gain, grad_two, gate_part, gates, routes, router_low = extras
    grad_one, logit_grad, target_total, gain_grad = aux
    landed = scratch[0]
    clear_gain(rank, inner, extras, aux, scratch)
    for copy in gate_copies(rank, extras, scratch):
        copy.wait()
    gate_grad = jnp.zeros(gate_part.shape, jnp.float32)
    for source in range(4):
        piece = jnp.zeros(gate_part.shape, jnp.float32)
        for step in (1, 2, 3):
            piece = jnp.where(lax.rem(source + step, 4) == rank, landed[step - 1], piece)
        gate_grad = gate_grad + jnp.where(rank == source, gate_part[...], piece)
    target_total[...] = gate_grad[2:3]
    gate_grad = gate_grad[0:2]
    weighted = gates[...] * gate_grad
    chosen = gates[...] * (gate_grad - (weighted[0:1] + weighted[1:2]))
    experts, tokens = logit_grad.shape
    row = lax.broadcasted_iota(jnp.int32, (experts, tokens), 0)
    placed = jnp.where(row == routes[0:1], chosen[0:1], 0.0) + jnp.where(
        row == routes[1:2], chosen[1:2], 0.0
    )
    logit_grad[...] = placed.astype(jnp.bfloat16)

    @pl.when(inner)
    def _():
        grad_one[...] = lax.dot_general(
            logit_grad[...],
            router_low[...],
            (((0,), (1,)), ((), ())),
            preferred_element_type=jnp.float32,
        )


def finish_expert_grad(total, span, rank, extras, aux, scratch):
    stream_one, gain, grad_two, gate_part, gates, routes, router_low = extras
    grad_one, logit_grad, target_total, gain_grad = aux
    part, gain_part = norm_back_rows(
        stream_one[span], gain[...], total + grad_one[span]
    )
    result = grad_two[span] + part
    grad_one[span] = result
    gain_grad[...] += gain_part
    return result.astype(jnp.bfloat16)


def form_joint_grad(rank, extras, aux, scratch):
    query_grad, pair_grad, before_grad, joint_weights = extras[5:]
    joint_grad = aux[0]
    landed, pair_sem, part = scratch[2:]
    hidden = query_grad.shape[0]
    later = lax.axis_index("ctx") > 0
    copy = pltpu.make_async_remote_copy(
        src_ref=before_grad,
        dst_ref=landed,
        send_sem=pair_sem.at[0],
        recv_sem=pair_sem.at[1],
        device_id={"ctx": 1 - lax.axis_index("ctx")},
        device_id_type=MESH_ID,
    )
    joint_grad[0:hidden, :] = query_grad[...]

    @pl.when(later)
    def _():
        copy.start()
        joint_grad[hidden:, :] = pair_grad[...].astype(jnp.bfloat16)

    @pl.when(jnp.logical_not(later))
    def _():
        copy.wait_recv()
        both = pair_grad[...] + landed[...].astype(jnp.float32)
        joint_grad[hidden:, :] = both.astype(jnp.bfloat16)

    part[...] = lax.dot_general(
        joint_grad[...], joint_weights[...], (((0,), (0,)), ((), ())), preferred_element_type=jnp.float32
    )

    @pl.when(later)
    def _():
        copy.wait_send()


def finish_input_grad(scale, total, span, rank, extras, aux, scratch):
    embedded, gain, grad_one = extras[:3]
    stream_zero = embedded[span].astype(jnp.float32) * scale
    part, gain_part = norm_back_rows(stream_zero, gain[...], total)
    aux[-1][0:1, :] += gain_part
    return ((grad_one[span] + part) * scale).astype(jnp.bfloat16)


def middle_kernel(
    attended_ref, embedded_ref, gain_ref, router_ref, routes_ref, *refs
):
    rolled, (stream_ref, normed_ref, rows_ref, columns_ref, project_ref) = refs[:4], refs[4:]

    @pl.when(pl.program_id(0) == 0)
    def _():
        for step in range(4):
            lines = rolled[step].shape[0]
            owner = lax.rem(lax.axis_index("tensor") + 4 - step, 4)
            project_ref[pl.ds(pl.multiple_of(owner * lines, lines), lines)] = rolled[step][...]

    scale = math.sqrt(embedded_ref.shape[1])
    stream = embedded_ref[...].astype(jnp.float32) * scale + lax.dot_general(
        attended_ref[...], project_ref[...], (((0,), (0,)), ((), ())), preferred_element_type=jnp.float32
    )
    stream_ref[...] = stream
    normed = (stream * inverse_rms(stream) * gain_ref[...]).astype(jnp.bfloat16)
    normed_ref[...] = normed
    scores = lax.dot_general(
        router_ref[...], normed, (((1,), (1,)), ((), ())), preferred_element_type=jnp.float32
    )
    expert = lax.broadcasted_iota(jnp.int32, scores.shape, 0)
    first, second = (
        jnp.sum(jnp.where(expert == routes_ref[k : k + 1, :], scores, 0.0), 0, keepdims=True)
        for k in range(2)
    )
    top = jnp.maximum(first, second)
    first, second = jnp.exp(first - top), jnp.exp(second - top)
    total = first + second
    gates = jnp.concatenate([first / total, second / total], 0)
    rows_ref[...] = gates
    columns_ref[...] = jnp.concatenate([gates, jnp.zeros((6, gates.shape[1]), jnp.float32)], 0).T


def middle(attended, rolled, embedded, gain, router, routes):
    tokens, width = embedded.shape
    tile = 256
    fixed = lambda k: (0, 0)
    whole = lambda x: pl.BlockSpec(x.shape, fixed)
    down = lambda n: pl.BlockSpec((tile, n), lambda k: (k, 0))
    along = lambda n: pl.BlockSpec((n, tile), lambda k: (0, k))
    return pl.pallas_call(
        middle_kernel,
        grid=(tokens // tile,),
        out_shape=[
            jax.ShapeDtypeStruct((tokens, width), jnp.float32),
            jax.ShapeDtypeStruct((tokens, width), jnp.bfloat16),
            jax.ShapeDtypeStruct((2, tokens), jnp.float32),
            jax.ShapeDtypeStruct((tokens, 8), jnp.float32),
        ],
        in_specs=[along(width), down(width), whole(gain), whole(router), along(2)]
        + [whole(x) for x in rolled],
        out_specs=[down(width), down(width), along(2), down(8)],
        scratch_shapes=[pltpu.VMEM((width, width), jnp.bfloat16)],
        compiler_params=pltpu.CompilerParams(vmem_limit_bytes=40 << 20),
    )(attended, embedded, gain, router, routes, *rolled)


def embed_kernel(
    chunks, first_unit, slots_ref, mine_ref, rows_ref, gain_ref, units_ref, embedded_ref, normed_ref, joint_ref,
    joint_weights, project_weights, *refs
):
    held, total, stage, from_end, from_mid = refs[:5]
    send_x, recv_x, send_y, recv_y, send_z, recv_z, send_core, recv_core = refs[5:13]
    send_sem, end_sem, mid_sem, back_sem, back_recv = refs[13:]
    chip, core = lax.axis_index("dp"), lax.axis_index("ctx")
    beside = chip + 1 - 2 * lax.rem(chip, 2)
    across = lax.rem(chip + 2, 4)
    opposite = across + 1 - 2 * lax.rem(across, 2)
    places = (chip, beside, across, opposite)
    rank = lax.axis_index("tensor")
    inner = (rank == 1) | (rank == 2)
    end_peer = jnp.where(rank < 2, 1 - rank, 5 - rank)
    mid_peer = 3 - rank
    slots, unit_rows = mine_ref.shape[:2]
    width = total.shape[2]
    size = slots // chunks
    split = (chunks + 1) // 2
    tokens = rows_ref.shape[0]
    count, rows = stage.shape[1:3]

    def repeat(first, last, body):
        def step(i, carry):
            body(i)
            return carry

        lax.fori_loop(first, last, step, 0)

    def columns(h):
        return slice(h * width, (h + 1) * width)

    own = (chip * 2 + core) * slots
    for h in range(2):
        held[h, pl.ds(own, slots)] = mine_ref[:, :, columns(h)].astype(jnp.bfloat16)
    barrier = pltpu.get_barrier_semaphore()
    for place in ({"ctx": 1 - core}, {"dp": beside}, {"dp": across}, {"tensor": end_peer}):
        pl.semaphore_signal(barrier, inc=1, device_id=place, device_id_type=MESH_ID)

    @pl.when(inner)
    def _():
        pl.semaphore_signal(barrier, inc=1, device_id={"tensor": mid_peer}, device_id_type=MESH_ID)
        pl.semaphore_wait(barrier, 5)

    @pl.when(jnp.logical_not(inner))
    def _():
        pl.semaphore_wait(barrier, 4)

    def remote(source, target, send, recv, place):
        return pltpu.make_async_remote_copy(
            src_ref=source,
            dst_ref=target,
            send_sem=send,
            recv_sem=recv,
            device_id=place,
            device_id_type=MESH_ID,
        )

    def copy(h, place, q, send, recv, target):
        piece = held.at[h, pl.ds((place * 2 + core) * slots + q * size, size)]
        return remote(piece, piece, send, recv, target)

    def to_beside(h, q):
        return copy(h, chip, q, send_x.at[h, q], recv_x.at[h, q], {"dp": beside})

    def to_across(h, q):
        return copy(h, chip, q, send_y.at[h, q], recv_y.at[h, q], {"dp": across})

    def passed_on(h, q, source, target):
        return copy(h, source, q, send_z.at[h, q], recv_z.at[h, q], {"dp": target})

    def to_core(h, k, q):
        return copy(h, places[k], q, send_core.at[h, k, q], recv_core.at[h, k, q], {"ctx": 1 - core})

    def start(h):
        def both(i):
            to_beside(h, i).start()
            to_across(h, lax.rem(i + split, chunks)).start()

        repeat(0, chunks, both)
        repeat(0, chunks, lambda q: to_core(h, 0, q).start())

    def look(h, place, which):
        begin = (place * 2 + which) * slots
        lines = slots * unit_rows
        column = lax.broadcasted_iota(jnp.int32, (tokens, lines), 1) + begin * unit_rows
        hit = jnp.where(column == rows_ref[...], 1.0, 0.0).astype(jnp.bfloat16)
        block = held[h, pl.ds(begin, slots)].reshape(lines, width)
        total[h] += jnp.dot(hit, block, preferred_element_type=jnp.float32)

    def relay(h, i):
        to_beside(h, i).wait_recv()

        @pl.when(i < split)
        def _():
            passed_on(h, i, beside, across).start()

        to_core(h, 1, i).start()
        j = lax.rem(i + split, chunks)
        to_across(h, j).wait_recv()

        @pl.when(j >= split)
        def _():
            passed_on(h, j, across, beside).start()

        to_core(h, 2, j).start()

    def rest(h):
        repeat(0, chunks, lambda q: to_core(h, 0, q).wait_recv())
        look(h, chip, 1 - core)
        look(h, beside, core)
        look(h, across, core)

        def last(q):
            passed_on(h, q, opposite, opposite).wait_recv()
            to_core(h, 3, q).start()
            to_core(h, 1, q).wait_recv()
            to_core(h, 2, q).wait_recv()

        repeat(0, chunks, last)
        look(h, beside, 1 - core)
        look(h, across, 1 - core)
        look(h, opposite, core)
        repeat(0, chunks, lambda q: to_core(h, 3, q).wait_recv())
        look(h, opposite, 1 - core)

    def span(i):
        return pl.ds(pl.multiple_of(i * rows, rows), rows)

    def to_inner(h, i):
        return remote(
            stage.at[h, i], from_end.at[h, i], send_sem.at[h, i], end_sem.at[h, i], {"tensor": end_peer}
        )

    def to_middle(h, i):
        return remote(
            stage.at[h, i], from_mid.at[h, i], send_sem.at[h, i], mid_sem.at[h, i], {"tensor": mid_peer}
        )

    def to_end(h, i):
        piece = embedded_ref.at[span(i), columns(h)]
        return remote(piece, piece, back_sem.at[h, i], back_recv.at[h, i], {"tensor": end_peer})

    def push(h):
        @pl.when(jnp.logical_not(inner))
        def _():
            def one(i):
                stage[h, i] = total[h, span(i)].astype(jnp.bfloat16)
                to_inner(h, i).start()

            repeat(0, count, one)

    def exchange(h, i):
        @pl.when(inner & (i < count))
        def _():
            to_inner(h, i).wait_recv()
            stage[h, i] = (total[h, span(i)] + from_end[h, i].astype(jnp.float32)).astype(jnp.bfloat16)
            to_middle(h, i).start()

        @pl.when(inner & (i >= line_lag))
        def _():
            j = i - line_lag
            to_middle(h, j).wait_recv()
            both = stage[h, j].astype(jnp.float32) + from_mid[h, j].astype(jnp.float32)
            embedded_ref[span(j), columns(h)] = both.astype(jnp.bfloat16)
            to_end(h, j).start()

    total[...] = jnp.zeros_like(total)
    start(0)
    look(0, chip, core)
    repeat(0, chunks, lambda i: relay(0, i))
    start(1)
    rest(0)
    push(0)
    look(1, chip, core)

    def between(i):
        exchange(0, i)

        @pl.when(i < chunks)
        def _():
            relay(1, i)

    repeat(0, count + line_lag, between)
    rest(1)
    push(1)

    def place_unit(u):
        for h in range(2):
            units_ref[u, :, columns(h)] = held[h, slots_ref[u]]

    @pl.when(jnp.logical_not(inner))
    def _():
        repeat(0, units_ref.shape[0], place_unit)

    repeat(0, count + line_lag, lambda i: exchange(1, i))

    @pl.when(inner)
    def _():
        repeat(0, units_ref.shape[0], place_unit)

    def finish(q):
        for h in range(2):
            to_beside(h, q).wait_send()
            to_across(h, q).wait_send()
            for k in range(4):
                to_core(h, k, q).wait_send()
            passed_on(h, q, opposite, opposite).wait_send()

    repeat(0, chunks, finish)

    @pl.when(inner)
    def _():
        def drain(i):
            for h in range(2):
                to_middle(h, i).wait_send()
                to_end(h, i).wait_send()

        repeat(0, count, drain)

    @pl.when(jnp.logical_not(inner))
    def _():
        def drain(i):
            for h in range(2):
                to_end(h, i).wait_recv()
                to_inner(h, i).wait_send()

        repeat(0, count, drain)

    stream = embedded_ref[...].astype(jnp.float32) * math.sqrt(2 * width)
    normed = (stream * inverse_rms(stream) * gain_ref[...]).astype(jnp.bfloat16)
    normed_ref[...] = normed
    lines = joint_ref.shape[0]
    weights = units_ref[first_unit : first_unit + lines // unit_rows].reshape(lines, 2 * width)
    joint_weights[...] = weights
    project_weights[...] = units_ref[first_unit + lines // unit_rows :].reshape(
        project_weights.shape
    )
    joint_ref[...] = lax.dot_general(
        weights, normed, (((1,), (1,)), ((), ())), preferred_element_type=jnp.float32
    ).astype(jnp.bfloat16)


def embed(unit_slots, mine, slot_rows, gain, first_unit, lines, collective_id):
    slots, unit_rows, width = mine.shape
    tokens = slot_rows.shape[0]
    chunks = max(k for k in range(1, 8) if slots % k == 0)
    rows = 128
    half = width // 2
    sems = pltpu.SemaphoreType.DMA((2, chunks))
    line = pltpu.VMEM((2, tokens // rows, rows, half), jnp.bfloat16)
    return pl.pallas_call(
        functools.partial(embed_kernel, chunks, first_unit),
        out_shape=[
            jax.ShapeDtypeStruct((unit_slots.shape[0], unit_rows, width), jnp.bfloat16),
            jax.ShapeDtypeStruct((tokens, width), jnp.bfloat16),
            jax.ShapeDtypeStruct((tokens, width), jnp.bfloat16),
            jax.ShapeDtypeStruct((lines, tokens), jnp.bfloat16),
            jax.ShapeDtypeStruct((lines, width), jnp.bfloat16),
            jax.ShapeDtypeStruct((lines // 3, width), jnp.bfloat16),
        ],
        in_specs=[pl.BlockSpec(memory_space=pltpu.SMEM)] + [whole_vmem] * 3,
        out_specs=[whole_vmem] * 6,
        scratch_shapes=[
            pltpu.VMEM((2, 8 * slots, unit_rows, half), jnp.bfloat16),
            pltpu.VMEM((2, tokens, half), jnp.float32),
            line,
            line,
            line,
        ]
        + [sems] * 6
        + [pltpu.SemaphoreType.DMA((2, 4, chunks))] * 2
        + [pltpu.SemaphoreType.DMA((2, tokens // rows))] * 5,
        compiler_params=pltpu.CompilerParams(
            collective_id=collective_id, has_side_effects=True, vmem_limit_bytes=60 << 20
        ),
    )(unit_slots, mine, slot_rows, gain)


def pull_units_kernel(parts, slots_ref, *refs):
    sources, out_ref, sem = refs[:parts], refs[parts], refs[parts + 1]
    width = out_ref.shape[-1] // parts

    def push(u, carry):
        for part in range(parts):
            pltpu.make_async_copy(
                sources[part].at[slots_ref[u]],
                out_ref.at[u, :, part * width : (part + 1) * width],
                sem,
            ).start()
        return carry

    lax.fori_loop(0, out_ref.shape[0], push, 0)
    pltpu.make_async_copy(out_ref, out_ref, sem).wait()


def pull_units(sources, slots):
    count = slots.shape[0]
    rows, width = sources[0].shape[1:]
    return pl.pallas_call(
        functools.partial(pull_units_kernel, len(sources)),
        out_shape=jax.ShapeDtypeStruct((count, rows, width * len(sources)), sources[0].dtype),
        in_specs=[pl.BlockSpec(memory_space=pltpu.SMEM)] + [whole_any] * len(sources),
        out_specs=whole_vmem,
        scratch_shapes=[pltpu.SemaphoreType.DMA],
        compiler_params=pltpu.CompilerParams(vmem_limit_bytes=40 << 20),
    )(slots, *sources)


def attention_kernel(
    heads, size, bias_ref, own_ref, out_ref, logsum_ref, before_ref, mine_ref,
    queries, own_values, old_values, scores, peak, total, keys_sem, send_sem, recv_sem,
):
    tokens = own_ref.shape[1]
    blocks = tokens // BLOCK
    hidden = heads * size
    later = lax.axis_index("ctx") > 0
    rank = lax.axis_index("tensor")
    inner = (rank == 1) | (rank == 2)
    end_peer = jnp.where(rank < 2, 1 - rank, 5 - rank)
    mid_peer = 3 - rank
    mid_owner = jnp.where(inner, mid_peer, 3 - end_peer)
    far_owner = jnp.where(inner, 3 - end_peer, 3 - rank)
    other_core = {"ctx": 1 - lax.axis_index("ctx")}
    barrier = pltpu.get_barrier_semaphore()
    for place in (other_core, {"tensor": end_peer}):
        pl.semaphore_signal(barrier, inc=1, device_id=place, device_id_type=MESH_ID)

    @pl.when(inner)
    def _():
        pl.semaphore_signal(barrier, inc=1, device_id={"tensor": mid_peer}, device_id_type=MESH_ID)
        pl.semaphore_wait(barrier, 3)

    @pl.when(jnp.logical_not(inner))
    def _():
        pl.semaphore_wait(barrier, 2)

    pairs = pltpu.make_async_remote_copy(
        src_ref=own_ref.at[pl.ds(hidden, 2 * hidden)],
        dst_ref=before_ref,
        send_sem=keys_sem.at[0],
        recv_sem=keys_sem.at[1],
        device_id=other_core,
        device_id_type=MESH_ID,
    )

    @pl.when(jnp.logical_not(later))
    def _():
        pairs.start()
        before_ref[...] = jnp.zeros_like(before_ref)

    def flipped(rows):
        return rows.astype(jnp.float32).T.astype(jnp.bfloat16)

    for head in range(heads):
        span = slice(head * size, (head + 1) * size)
        queries[head] = flipped(own_ref[span, :]) * jnp.bfloat16(size**-0.5)
        own_values[head] = flipped(
            own_ref[2 * hidden + head * size : 2 * hidden + (head + 1) * size, :]
        )

    @pl.when(later)
    def _():
        pairs.wait_recv()
        for head in range(heads):
            old_values[head] = flipped(
                before_ref[hidden + head * size : hidden + (head + 1) * size, :]
            )

    def sent(owner, block, peer, send, recv):
        piece = out_ref.at[owner, :, pl.ds(block * BLOCK, BLOCK)]
        return pltpu.make_async_remote_copy(
            src_ref=piece,
            dst_ref=piece,
            send_sem=send_sem.at[block, send],
            recv_sem=recv_sem.at[block, recv],
            device_id={"tensor": peer},
            device_id_type=MESH_ID,
        )

    def own_to_end(block):
        return sent(rank, block, end_peer, 0, 0)

    def from_end(block):
        return sent(end_peer, block, end_peer, 0, 0)

    def own_to_middle(block):
        return sent(rank, block, mid_peer, 1, 1)

    def end_to_middle(block):
        return sent(end_peer, block, mid_peer, 2, 2)

    def middle_to_end(block):
        return sent(mid_owner, block, end_peer, 3, 1)

    def far_to_end(block):
        return sent(far_owner, block, end_peer, 4, 2)

    def hand_on(block, stages):
        @pl.when(inner)
        def _():
            if 0 in stages:
                from_end(block).wait_recv()
                end_to_middle(block).start()
                middle_to_end(block).wait_recv()
                middle_to_end(block).start()
            if 1 in stages:
                far_to_end(block).wait_recv()
                far_to_end(block).start()

    for block in range(blocks):
        for head in range(heads):
            span = slice(head * size, (head + 1) * size)
            rows = queries[head, block * BLOCK : (block + 1) * BLOCK]
            own_keys = own_ref[hidden + head * size : hidden + (head + 1) * size, :]
            width = (block + 1) * BLOCK
            mine = jnp.dot(rows, own_keys[:, :width], preferred_element_type=jnp.float32)
            top = None
            parts = []
            for k in range(block + 1):
                part = mine[:, k * BLOCK : (k + 1) * BLOCK] + bias_ref[head, block - k]
                parts.append(part)
                high = jnp.max(part, 1, keepdims=True)
                top = high if top is None else jnp.maximum(top, high)
            peak[...] = top

            @pl.when(later)
            def _():
                old = jnp.dot(rows, before_ref[span, :], preferred_element_type=jnp.float32)
                top_old = None
                for k in range(blocks):
                    part = old[:, k * BLOCK : (k + 1) * BLOCK] + bias_ref[head, block + blocks - k]
                    scores[:, k * BLOCK : (k + 1) * BLOCK] = part
                    high = jnp.max(part, 1, keepdims=True)
                    top_old = high if top_old is None else jnp.maximum(top_old, high)
                peak[...] = jnp.maximum(peak[...], top_old)

            top = peak[...]
            parts = [jnp.exp(part - top) for part in parts]
            own_sum = None
            for part in parts:
                part_sum = jnp.sum(part, 1, keepdims=True)
                own_sum = part_sum if own_sum is None else own_sum + part_sum
            total[...] = own_sum

            @pl.when(later)
            def _():
                old_exp = jnp.exp(scores[...] - top)
                scores[...] = old_exp
                total[...] += jnp.sum(old_exp, 1, keepdims=True)

            full = total[...]
            inverse = 1.0 / full
            low = jnp.concatenate([(part * inverse).astype(jnp.bfloat16) for part in parts], 1)
            result = jnp.dot(low, own_values[head, :width], preferred_element_type=jnp.float32)
            logsum_ref[head, block * BLOCK : (block + 1) * BLOCK, :] = top + jnp.log(full)
            place = (rank, span, slice(block * BLOCK, (block + 1) * BLOCK))

            @pl.when(later)
            def _():
                low_old = (scores[...] * inverse).astype(jnp.bfloat16)
                both = result + jnp.dot(low_old, old_values[head], preferred_element_type=jnp.float32)
                out_ref[place] = both.T.astype(jnp.bfloat16)
                mine_ref[place[1:]] = both.T.astype(jnp.bfloat16)

            @pl.when(jnp.logical_not(later))
            def _():
                out_ref[place] = result.T.astype(jnp.bfloat16)
                mine_ref[place[1:]] = result.T.astype(jnp.bfloat16)

        own_to_end(block).start()

        @pl.when(inner)
        def _():
            own_to_middle(block).start()

        if block >= 1:
            hand_on(block - 1, (0,))
        if block >= 2:
            hand_on(block - 2, (1,))

    hand_on(blocks - 1, (0,))
    hand_on(blocks - 2, (1,))
    hand_on(blocks - 1, (1,))
    for block in range(blocks):
        own_to_end(block).wait_send()

        @pl.when(inner)
        def _():
            for copy in (own_to_middle, end_to_middle, middle_to_end, far_to_end):
                copy(block).wait_send()

        @pl.when(jnp.logical_not(inner))
        def _():
            from_end(block).wait_recv()
            middle_to_end(block).wait_recv()
            far_to_end(block).wait_recv()

    @pl.when(jnp.logical_not(later))
    def _():
        pairs.wait_send()


def attention(biases, own, heads, size, collective_id):
    tokens = own.shape[1]
    blocks = tokens // BLOCK
    flat = pltpu.VMEM((heads, tokens, size), jnp.bfloat16)
    return pl.pallas_call(
        functools.partial(attention_kernel, heads, size),
        out_shape=[
            jax.ShapeDtypeStruct((4, heads * size, tokens), jnp.bfloat16),
            jax.ShapeDtypeStruct((heads, tokens, 1), jnp.float32),
            jax.ShapeDtypeStruct((2 * heads * size, tokens), jnp.bfloat16),
            jax.ShapeDtypeStruct((heads * size, tokens), jnp.bfloat16),
        ],
        in_specs=[pl.BlockSpec(memory_space=pltpu.SMEM), whole_vmem],
        out_specs=[whole_vmem] * 4,
        scratch_shapes=[
            flat,
            flat,
            flat,
            pltpu.VMEM((BLOCK, tokens), jnp.float32),
            pltpu.VMEM((BLOCK, 1), jnp.float32),
            pltpu.VMEM((BLOCK, 1), jnp.float32),
            pltpu.SemaphoreType.DMA((2,)),
            pltpu.SemaphoreType.DMA((blocks, 5)),
            pltpu.SemaphoreType.DMA((blocks, 3)),
        ],
        compiler_params=pltpu.CompilerParams(
            collective_id=collective_id, has_side_effects=True, vmem_limit_bytes=40 << 20
        ),
    )(biases, own)


def attention_back_kernel(
    heads, size, bias_ref, own_ref, before_ref, logsum_ref, grad_ref, project_ref,
    *refs
):
    states, (query_out, own_out, before_out, bias_out) = refs[:8], refs[8:12]
    updated, (probs, slopes, inner, query_sum, own_sum, before_sum) = refs[12:18], refs[18:24]
    held, load_sem, store_sem = refs[24:]
    loads = [pltpu.make_async_copy(states[k], held.at[k], load_sem.at[k]) for k in range(8)]
    stores = [
        pltpu.make_async_copy(held.at[4 * (k // 3) + k % 3], updated[k], store_sem.at[k])
        for k in range(6)
    ]
    for load in loads:
        load.start()

    def update(i, carry):
        lines = held.shape[1] // 16
        span = pl.ds(pl.multiple_of(i * lines, lines), lines)
        for k, rate in enumerate((rate_inner, rate_outer)):
            fresh = adam_update(*(held[4 * k + n, span] for n in range(4)), rate, decay_rate)
            for n in range(3):
                held[4 * k + n, span] = fresh[n]
        return carry

    tokens = own_ref.shape[1]
    blocks = tokens // BLOCK
    hidden = heads * size
    later = lax.axis_index("ctx") > 0
    bias_out[...] = jnp.zeros_like(bias_out)

    def flipped(rows):
        return rows.astype(jnp.float32).T.astype(jnp.bfloat16)

    for head in range(heads):
        span = slice(head * size, (head + 1) * size)
        value_span = slice(hidden + head * size, hidden + (head + 1) * size)
        query_rows = own_ref[span, :]
        query = flipped(query_rows) * jnp.bfloat16(size**-0.5)
        own_keys = own_ref[hidden + head * size : hidden + (head + 1) * size, :]
        own_values = own_ref[2 * hidden + head * size : 2 * hidden + (head + 1) * size, :]
        old_keys = before_ref[span, :]
        old_values = before_ref[value_span, :]
        own_keys_flip = flipped(own_keys)
        grad = lax.dot_general(
            grad_ref[...], project_ref[span, :], (((1,), (1,)), ((), ())), preferred_element_type=jnp.float32
        )
        grad_rows = grad.T.astype(jnp.bfloat16)
        grad = grad.astype(jnp.bfloat16)
        own_sum[...] = jnp.zeros_like(own_sum)

        @pl.when(later)
        def _():
            before_sum[...] = jnp.zeros_like(before_sum)

        for block in range(blocks):
            at = slice(block * BLOCK, (block + 1) * BLOCK)
            width = (block + 1) * BLOCK
            rows, up = query[at], grad[at]
            lse = logsum_ref[head, at, :]
            score = jnp.dot(rows, own_keys[:, :width], preferred_element_type=jnp.float32)
            prob = jnp.concatenate(
                [
                    jnp.exp(score[:, k * BLOCK : (k + 1) * BLOCK] + (bias_ref[head, block - k] - lse))
                    for k in range(block + 1)
                ],
                1,
            )
            slope = jnp.dot(up, own_values[:, :width], preferred_element_type=jnp.float32)
            inner[...] = jnp.sum(prob * slope, 1, keepdims=True)

            @pl.when(later)
            def _():
                score = jnp.dot(rows, old_keys, preferred_element_type=jnp.float32)
                old_slope = jnp.dot(up, old_values, preferred_element_type=jnp.float32)
                old_prob = jnp.concatenate(
                    [
                        jnp.exp(
                            score[:, k * BLOCK : (k + 1) * BLOCK]
                            + (bias_ref[head, block + blocks - k] - lse)
                        )
                        for k in range(blocks)
                    ],
                    1,
                )
                probs[...] = old_prob
                slopes[...] = old_slope
                inner[...] += jnp.sum(old_prob * old_slope, 1, keepdims=True)

            row_inner = inner[...]
            low_grad = (prob * (slope - row_inner)).astype(jnp.bfloat16)
            query_sum[...] = jnp.dot(
                low_grad, own_keys_flip[:width], preferred_element_type=jnp.float32
            )
            own_sum[:size, :width] += jnp.dot(
                query_rows[:, at], low_grad, preferred_element_type=jnp.float32
            )
            own_sum[size:, :width] += jnp.dot(
                grad_rows[:, at], prob.astype(jnp.bfloat16), preferred_element_type=jnp.float32
            )
            for k in range(block + 1):
                line = head * 2 * blocks + block - k
                bias_out[line : line + 1, :] += jnp.sum(
                    low_grad[:, k * BLOCK : (k + 1) * BLOCK].astype(jnp.float32), 0, keepdims=True
                )

            @pl.when(later)
            def _():
                old_prob = probs[...]
                low_old = (old_prob * (slopes[...] - row_inner)).astype(jnp.bfloat16)
                query_sum[...] += jnp.dot(
                    low_old, flipped(old_keys), preferred_element_type=jnp.float32
                )
                before_sum[:size, :] += jnp.dot(
                    query_rows[:, at], low_old, preferred_element_type=jnp.float32
                )
                before_sum[size:, :] += jnp.dot(
                    grad_rows[:, at], old_prob.astype(jnp.bfloat16), preferred_element_type=jnp.float32
                )
                for k in range(blocks):
                    line = head * 2 * blocks + block + blocks - k
                    bias_out[line : line + 1, :] += jnp.sum(
                        low_old[:, k * BLOCK : (k + 1) * BLOCK].astype(jnp.float32), 0, keepdims=True
                    )

            query_out[span, at] = (query_sum[...].T * size**-0.5).astype(jnp.bfloat16)

        own_out[span, :] = own_sum[:size, :] * size**-0.5
        own_out[value_span, :] = own_sum[size:, :]

        @pl.when(later)
        def _():
            before_out[span, :] = (before_sum[:size, :] * size**-0.5).astype(jnp.bfloat16)
            before_out[value_span, :] = before_sum[size:, :].astype(jnp.bfloat16)

        if head == 0:
            for load in loads:
                load.wait()
            lax.fori_loop(0, 16, update, 0)
            for store in stores:
                store.start()

    @pl.when(jnp.logical_not(later))
    def _():
        before_out[...] = jnp.zeros_like(before_out)

    for store in stores:
        store.wait()


def attention_back(biases, own, before, logsum, grad, project, states, heads, size):
    tokens = own.shape[1]
    hidden = heads * size
    return pl.pallas_call(
        functools.partial(attention_back_kernel, heads, size),
        out_shape=[
            jax.ShapeDtypeStruct((hidden, tokens), jnp.bfloat16),
            jax.ShapeDtypeStruct((2 * hidden, tokens), jnp.float32),
            jax.ShapeDtypeStruct((2 * hidden, tokens), jnp.bfloat16),
            jax.ShapeDtypeStruct((heads * 2 * (tokens // BLOCK), BLOCK), jnp.float32),
        ]
        + [jax.ShapeDtypeStruct(states[0].shape, jnp.float32)] * 6,
        in_specs=[pl.BlockSpec(memory_space=pltpu.SMEM)] + [whole_vmem] * 5 + [whole_any] * 8,
        out_specs=[whole_vmem] * 4 + [whole_any] * 6,
        scratch_shapes=[
            pltpu.VMEM((BLOCK, tokens), jnp.float32),
            pltpu.VMEM((BLOCK, tokens), jnp.float32),
            pltpu.VMEM((BLOCK, 1), jnp.float32),
            pltpu.VMEM((BLOCK, size), jnp.float32),
            pltpu.VMEM((2 * size, tokens), jnp.float32),
            pltpu.VMEM((2 * size, tokens), jnp.float32),
            pltpu.VMEM((8,) + states[0].shape, jnp.float32),
            pltpu.SemaphoreType.DMA((8,)),
            pltpu.SemaphoreType.DMA((6,)),
        ],
        compiler_params=pltpu.CompilerParams(vmem_limit_bytes=48 << 20),
    )(biases, own, before, logsum, grad, project, *states)


def vocab_tile(vocab):
    return max(k for k in range(16, 1601, 16) if vocab % k == 0)


def head_line_kernel(
    tile, part_ref, stream_ref, gain_ref, table_ref, wanted_ref, weight_ref,
    low_ref, grad_low_ref, grad_ref, gain_grad, logsum_ref, picked_ref, slopes_ref,
    logits, table, stage, from_end, from_mid, own, turned, stats, landed, slope_tiles, total,
    load_sem, send_sem, end_sem, mid_sem, back_sem, back_recv, stat_send, stat_recv, store_sem,
):
    rank = lax.axis_index("tensor")
    inner = (rank == 1) | (rank == 2)
    end_peer = jnp.where(rank < 2, 1 - rank, 5 - rank)
    mid_peer = 3 - rank
    count, rows = stage.shape[:2]
    columns = turned.shape[1]
    pieces = table.shape[0] // tile
    group = columns // rows
    tiles = count // group
    vocab = table.shape[0]
    load = pltpu.make_async_copy(table_ref.at[pl.ds(0, vocab)], table, load_sem)
    load.start()
    barrier = pltpu.get_barrier_semaphore()
    for step in (1, 2, 3):
        other = lax.rem(rank + step, 4)
        pl.semaphore_signal(barrier, inc=1, device_id={"tensor": other}, device_id_type=MESH_ID)
    pl.semaphore_wait(barrier, 3)

    def span(i):
        return pl.ds(pl.multiple_of(i * rows, rows), rows)

    def over(t):
        return pl.ds(pl.multiple_of(t * columns, columns), columns)

    def line_copy(source, target, send, recv, peer):
        return pltpu.make_async_remote_copy(
            src_ref=source,
            dst_ref=target,
            send_sem=send,
            recv_sem=recv,
            device_id={"tensor": peer},
            device_id_type=MESH_ID,
        )

    def to_inner(i):
        return line_copy(stage.at[i], from_end.at[i], send_sem.at[i], end_sem.at[i], end_peer)

    def to_middle(i):
        return line_copy(stage.at[i], from_mid.at[i], send_sem.at[i], mid_sem.at[i], mid_peer)

    def to_end(ref, i):
        rows_of = ref.at[span(i)]
        return line_copy(rows_of, rows_of, back_sem.at[i], back_recv.at[i], end_peer)

    def repeat(first, last, body):
        def step(i, carry):
            body(i)
            return carry

        lax.fori_loop(first, last, step, 0)

    def turn(t):
        turned[...] = low_ref[over(t)].astype(jnp.float32).T.astype(jnp.bfloat16)

    def table_rows(k):
        return table[k * tile : (k + 1) * tile]

    def first_logits(t):
        turn(t)
        logits[0] = jnp.dot(table_rows(0), turned[...], preferred_element_type=jnp.float32)

    def next_logits(k):
        if k + 1 < pieces:
            logits[(k + 1) % 2] = jnp.dot(
                table_rows(k + 1), turned[...], preferred_element_type=jnp.float32
            )

    def sums_unit(t, k):
        next_logits(k)
        before = stats[0:1, over(t)]
        top = jnp.maximum(before, jnp.max(logits[k % 2], 0, keepdims=True))
        stats[1:2, over(t)] = stats[1:2, over(t)] * jnp.exp(before - top) + jnp.sum(
            jnp.exp(logits[k % 2] - top), 0, keepdims=True
        )
        stats[0:1, over(t)] = top

    def sums_tile(t):
        first_logits(t)
        for k in range(pieces):
            sums_unit(t, k)

    stats[0:1, :] = jnp.full_like(stats[0:1, :], masked_score)
    stats[1:2, :] = jnp.zeros_like(stats[1:2, :])

    @pl.when(jnp.logical_not(inner))
    def _():
        def push(i):
            stage[i] = part_ref[span(i)].astype(jnp.bfloat16)
            to_inner(i).start()

        repeat(0, count, push)
        load.wait()

        def forward(t):
            repeat(0, group, lambda c: to_end(low_ref, t * group + c).wait_recv())
            sums_tile(t)

        repeat(0, tiles, forward)
        repeat(0, count, lambda i: to_inner(i).wait_send())

    @pl.when(inner)
    def _():
        gain_grad[...] = jnp.zeros_like(gain_grad)
        load.wait()

        def gather(i):
            to_inner(i).wait_recv()
            mine = part_ref[span(i)] + from_end[i].astype(jnp.float32)
            stage[i] = mine.astype(jnp.bfloat16)
            to_middle(i).start()

        def settle_rows(j):
            to_middle(j).wait_recv()
            stream_two = stream_ref[span(j)] + (
                stage[j].astype(jnp.float32) + from_mid[j].astype(jnp.float32)
            )
            grad_ref[span(j)] = stream_two
            low_ref[span(j)] = (stream_two * inverse_rms(stream_two) * gain_ref[...]).astype(
                jnp.bfloat16
            )
            to_end(low_ref, j).start()

        turns = [[k for k in range(pieces) if k * (group - 1) // pieces == c - 1] for c in range(group)]

        def advance(t):
            for c in range(group):
                i = t * group + c
                gather(i)

                @pl.when(i >= line_lag)
                def _():
                    settle_rows(i - line_lag)

                if turns[c]:

                    @pl.when(t >= 1)
                    def _():
                        if c == 1:
                            first_logits(t - 1)
                        for k in turns[c]:
                            sums_unit(t - 1, k)

        repeat(0, tiles, advance)
        repeat(count - line_lag, count, settle_rows)
        sums_tile(tiles - 1)

        def drain(i):
            to_middle(i).wait_send()
            to_end(low_ref, i).wait_send()

        repeat(0, count, drain)

    copies = [
        line_copy(
            stats, landed.at[step - 1], stat_send.at[step - 1], stat_recv.at[step - 1], lax.rem(rank + step, 4)
        )
        for step in (1, 2, 3)
    ]
    for copy in copies:
        copy.start()
    for copy in copies:
        copy.wait()
    tops, sums = [], []
    for source in range(4):
        piece = stats[...]
        for step in (1, 2, 3):
            piece = jnp.where(lax.rem(source + step, 4) == rank, landed[step - 1], piece)
        tops.append(piece[0:1])
        sums.append(piece[1:2])
    top = jnp.maximum(jnp.maximum(tops[0], tops[1]), jnp.maximum(tops[2], tops[3]))
    whole = sums[0] * jnp.exp(tops[0] - top)
    for source in (1, 2, 3):
        whole = whole + sums[source] * jnp.exp(tops[source] - top)
    logsum_ref[...] = top + jnp.log(whole)
    picked_ref[...] = jnp.zeros_like(picked_ref)

    def store(t):
        return pltpu.make_async_copy(
            slope_tiles.at[lax.rem(t, 2)], slopes_ref.at[:, over(t)], store_sem.at[lax.rem(t, 2)]
        )

    def slope_unit(t, k):
        values = logits[k % 2]
        row = lax.broadcasted_iota(jnp.int32, values.shape, 0)
        base = k * tile
        hits = jnp.where(row == wanted_ref[0:1, over(t)] - base, weight_ref[0:1, over(t)], 0.0)
        hits = hits + jnp.where(
            row == wanted_ref[1:2, over(t)] - base, weight_ref[1:2, over(t)], 0.0
        )
        picked_ref[:, over(t)] += jnp.sum(hits * values, 0, keepdims=True)
        softmax = jnp.exp(values - logsum_ref[:, over(t)])
        slope_tiles[lax.rem(t, 2), base : base + tile] = (
            (weight_ref[2:3, over(t)] * softmax - hits) * weight_ref[3:4, over(t)]
        ).astype(jnp.bfloat16)

    def add_rows(t, k):
        total[...] += lax.dot_general(
            slope_tiles[lax.rem(t, 2), k * tile : (k + 1) * tile],
            table_rows(k),
            (((0,), (0,)), ((), ())),
            preferred_element_type=jnp.float32,
        )

    def settle(j):
        to_middle(j).wait_recv()
        upstream = stage[j].astype(jnp.float32) + from_mid[j].astype(jnp.float32)
        grad_two, gain_part = norm_back_rows(grad_ref[span(j)], gain_ref[...], upstream)
        grad_ref[span(j)] = grad_two
        gain_grad[...] += gain_part
        grad_low_ref[span(j)] = grad_two.astype(jnp.bfloat16)
        to_end(grad_low_ref, j).start()

    def exchange(i):
        to_inner(i).wait_recv()
        stage[i] = (own[span(i)] + from_end[i].astype(jnp.float32)).astype(jnp.bfloat16)
        to_middle(i).start()

        @pl.when(i >= line_lag)
        def _():
            settle(i - line_lag)

    def back_tile(t):
        @pl.when(t >= 2)
        def _():
            store(t - 2).wait()

        total[...] = jnp.zeros_like(total)
        first_logits(t)
        for k in range(pieces):
            next_logits(k)
            slope_unit(t, k)
            if k >= 1:
                add_rows(t, k - 1)
            if k >= pieces - group:

                @pl.when(inner & (t >= 1))
                def _():
                    exchange((t - 1) * group + k - (pieces - group))

        add_rows(t, pieces - 1)
        store(t).start()

        @pl.when(inner)
        def _():
            own[over(t)] = total[...]

        @pl.when(jnp.logical_not(inner))
        def _():
            def push(c):
                stage[t * group + c] = total[span(c)].astype(jnp.bfloat16)
                to_inner(t * group + c).start()

            repeat(0, group, push)

    repeat(0, tiles, back_tile)

    @pl.when(jnp.logical_not(inner))
    def _():
        def finish(i):
            to_end(grad_low_ref, i).wait_recv()
            to_inner(i).wait_send()

        repeat(0, count, finish)

    @pl.when(inner)
    def _():
        repeat(count - group, count, exchange)
        repeat(count - line_lag, count, settle)

        def drain(i):
            to_middle(i).wait_send()
            to_end(grad_low_ref, i).wait_send()

        repeat(0, count, drain)

    store(tiles - 2).wait()
    store(tiles - 1).wait()


def head_line(part, stream, gain, weights, wanted, weight_rows, vocab, collective_id):
    tokens, width = part.shape
    rows, columns = 64, 256
    count = tokens // rows
    chunks = pltpu.VMEM((count, rows, width), jnp.bfloat16)
    rows_low = jax.ShapeDtypeStruct((tokens, width), jnp.bfloat16)
    along = jax.ShapeDtypeStruct((1, tokens), jnp.float32)
    line_sems = pltpu.SemaphoreType.DMA((count,))
    return pl.pallas_call(
        functools.partial(head_line_kernel, vocab_tile(vocab)),
        out_shape=[
            rows_low,
            rows_low,
            jax.ShapeDtypeStruct((tokens, width), jnp.float32),
            jax.ShapeDtypeStruct((1, width), jnp.float32),
            along,
            along,
            jax.ShapeDtypeStruct((vocab, tokens), jnp.bfloat16),
        ],
        in_specs=[whole_vmem] * 3 + [whole_any] + [whole_vmem] * 2,
        out_specs=[whole_vmem] * 6 + [whole_any],
        scratch_shapes=[
            pltpu.VMEM((2, vocab_tile(vocab), columns), jnp.float32),
            pltpu.VMEM((vocab, width), jnp.bfloat16),
            chunks,
            chunks,
            chunks,
            pltpu.VMEM((tokens, width), jnp.float32),
            pltpu.VMEM((width, columns), jnp.bfloat16),
            pltpu.VMEM((2, tokens), jnp.float32),
            pltpu.VMEM((3, 2, tokens), jnp.float32),
            pltpu.VMEM((2, vocab, columns), jnp.bfloat16),
            pltpu.VMEM((columns, width), jnp.float32),
            pltpu.SemaphoreType.DMA,
        ]
        + [line_sems] * 5
        + [pltpu.SemaphoreType.DMA((3,))] * 2
        + [pltpu.SemaphoreType.DMA((2,))],
        compiler_params=pltpu.CompilerParams(
            collective_id=collective_id, has_side_effects=True, vmem_limit_bytes=62 << 20
        ),
    )(part, stream, gain, weights, wanted, weight_rows)


def weight_grads_kernel(
    tile_units, tiles, place_ref, slope_ref, rows_ref, ids_ref, zero_ref, joint_ref, normed_ref,
    attended_ref, grad_ref, out_ref, made, sem,
):
    step = pl.program_id(0)
    unit_rows = out_ref.shape[1]
    buffer = lax.rem(step, 2)
    last_units = joint_ref.shape[0] // unit_rows + attended_ref.shape[0] // unit_rows

    def settle(which, count):
        pltpu.make_async_copy(
            made.at[which, pl.ds(0, count)], made.at[which, pl.ds(0, count)], sem.at[which]
        ).wait()

    def send(first, count):
        def push(u, carry):
            pltpu.make_async_copy(
                made.at[buffer, u], out_ref.at[place_ref[first + u]], sem.at[buffer]
            ).start()
            return carry

        lax.fori_loop(0, count, push, 0)

    @pl.when(step >= 2)
    def _():
        settle(buffer, tile_units)

    @pl.when(step < tiles)
    def _():
        row = lax.broadcasted_iota(jnp.int32, slope_ref.shape, 0)
        seen = jnp.where(row == ids_ref[...] - step * slope_ref.shape[0], 1.0, 0.0).astype(jnp.bfloat16)
        made[buffer] = (
            jnp.dot(slope_ref[...], rows_ref[...], preferred_element_type=jnp.float32)
            + jnp.dot(seen, zero_ref[...], preferred_element_type=jnp.float32)
        ).astype(jnp.bfloat16).reshape(tile_units, unit_rows, -1)
        send(step * tile_units, tile_units)

    @pl.when(step == tiles)
    def _():
        joint_units = joint_ref.shape[0] // unit_rows
        made[buffer, pl.ds(0, joint_units)] = jnp.dot(
            joint_ref[...], normed_ref[...], preferred_element_type=jnp.float32
        ).astype(jnp.bfloat16).reshape(joint_units, unit_rows, -1)
        made[buffer, pl.ds(joint_units, last_units - joint_units)] = jnp.dot(
            attended_ref[...], grad_ref[...], preferred_element_type=jnp.float32
        ).astype(jnp.bfloat16).reshape(last_units - joint_units, unit_rows, -1)
        send(tiles * tile_units, last_units)
        settle(1 - buffer, tile_units)
        settle(buffer, last_units)


def weight_grads(place, slots, unit_rows, slope, rows, ids, zero, joint, normed, attended, grad):
    vocab, tokens = slope.shape
    width = rows.shape[1]
    tile = vocab_tile(vocab)
    tiles = vocab // tile
    fixed = lambda k: (0, 0)
    whole = lambda x: pl.BlockSpec(x.shape, fixed)
    return pl.pallas_call(
        functools.partial(weight_grads_kernel, tile // unit_rows, tiles),
        grid=(tiles + 1,),
        out_shape=jax.ShapeDtypeStruct((slots, unit_rows, width), jnp.bfloat16),
        in_specs=[
            pl.BlockSpec(memory_space=pltpu.SMEM),
            pl.BlockSpec((tile, tokens), lambda k: (jnp.minimum(k, tiles - 1), 0)),
        ]
        + [whole(x) for x in (rows, ids, zero, joint, normed, attended, grad)],
        out_specs=whole_any,
        scratch_shapes=[
            pltpu.VMEM((2, tile // unit_rows, unit_rows, width), jnp.bfloat16),
            pltpu.SemaphoreType.DMA((2,)),
        ],
        compiler_params=pltpu.CompilerParams(vmem_limit_bytes=60 << 20),
    )(place, slope, rows, ids, zero, joint, normed, attended, grad)


def adam_update(weight, moment_one, moment_two, gradient, step_rate, decay_factor):
    moment_new = beta_first * moment_one + (1.0 - beta_first) * gradient
    square_new = beta_second * moment_two + (1.0 - beta_second) * gradient * gradient
    moment_hat = moment_new / (1.0 - beta_first**STEP)
    square_hat = square_new / (1.0 - beta_second**STEP)
    weight_new = weight - step_rate * (
        moment_hat / (jnp.sqrt(square_hat) + adam_epsilon) + decay_factor * weight
    )
    return (weight_new, moment_new, square_new)


def norm_forward(values, gain_row):
    return values * inverse_rms(values) * gain_row


def slot_tables(owner_ids, owners, most_units):
    unit_count = owner_ids.shape[0]
    unit_index = jnp.arange(unit_count, dtype=jnp.int32)
    earlier = (owner_ids[None, :] == owner_ids[:, None]) & (
        unit_index[None, :] < unit_index[:, None]
    )
    unit_rank = jnp.sum(earlier.astype(jnp.int32), 1)
    placed = (owner_ids[None, None, :] == jnp.arange(owners, dtype=jnp.int32)[:, None, None]) & (
        unit_rank[None, None, :] == jnp.arange(most_units, dtype=jnp.int32)[None, :, None]
    )
    slot_filled = jnp.any(placed, 2)
    slot_unit = jnp.sum(jnp.where(placed, unit_index[None, None, :], 0), 2)
    return (unit_rank, slot_unit, slot_filled)


def unit_rates(unit_ids, table_units, query_units, value_units):
    return jnp.where(
        unit_ids < table_units,
        rate_table,
        jnp.where(
            unit_ids < query_units,
            rate_query,
            jnp.where(unit_ids < value_units, rate_values, rate_project),
        ),
    )


def pair_slots(route_pairs, priorities, experts, capacity):
    tokens_here = priorities.shape[0]
    pair_expert = route_pairs.T.reshape(-1)
    pair_key = (
        jnp.arange(2, dtype=jnp.int32)[:, None] * tokens_here + priorities[None, :]
    ).reshape(-1)
    before = (pair_expert[None, :] == pair_expert[:, None]) & (
        pair_key[None, :] < pair_key[:, None]
    )
    pair_rank = jnp.sum(before.astype(jnp.int32), 1)
    pair_kept = pair_rank < capacity
    pair_dest = pair_expert * capacity + jnp.minimum(pair_rank, capacity - 1)
    return (pair_kept, pair_dest)


def gelu_tanh(values):
    return jax.nn.gelu(values, approximate=True)


def gelu_slope(values):
    root = math.sqrt(2.0 / math.pi)
    bent = jnp.tanh(root * (values + 0.044715 * values * values * values))
    return 0.5 * (1.0 + bent) + 0.5 * values * (1.0 - bent * bent) * root * (
        1.0 + 3.0 * 0.044715 * values * values
    )


def plane_peer(step):
    chip, core = lax.axis_index("dp"), lax.axis_index("ctx")
    row = lax.rem(chip // 2 + step // 4, 2)
    column = lax.rem(lax.rem(chip, 2) + lax.rem(step // 2, 2), 2)
    place = {"dp": row * 2 + column, "ctx": lax.rem(core + lax.rem(step, 2), 2)}
    return place, place["dp"] * 2 + place["ctx"]


def greet_plane():
    barrier = pltpu.get_barrier_semaphore()
    for step in range(1, 8):
        place, _ = plane_peer(step)
        pl.semaphore_signal(barrier, inc=1, device_id=place, device_id_type=MESH_ID)
    pl.semaphore_wait(barrier, 7)


def plane_copy(source, target, send_sem, recv_sem, step):
    place, _ = plane_peer(step)
    return pltpu.make_async_remote_copy(
        src_ref=source.at[step],
        dst_ref=target.at[step],
        send_sem=send_sem.at[step],
        recv_sem=recv_sem.at[step],
        device_id=place,
        device_id_type=MESH_ID,
    )


def slot_hits(dest_rows, expert, capacity, tokens):
    slot = lax.broadcasted_iota(jnp.int32, (capacity, tokens), 0) + expert * capacity
    return (slot == dest_rows[0:1, :]) | (slot == dest_rows[1:2, :])


def token_hits(dest_columns, expert, capacity, tokens):
    slot = lax.broadcasted_iota(jnp.int32, (tokens, capacity), 1) + expert * capacity
    hit = (slot == dest_columns[:, 0:1]) | (slot == dest_columns[:, 1:2])
    return jnp.where(hit, 1.0, 0.0).astype(jnp.bfloat16)


def gate_of(routes, gates, expert, axis):
    pick = (lambda a, k: a[k : k + 1, :]) if axis == 0 else (lambda a, k: a[:, k : k + 1])
    return jnp.where(pick(routes, 0) == expert, pick(gates, 0), 0.0) + jnp.where(
        pick(routes, 1) == expert, pick(gates, 1), 0.0
    )


def arrival(i):
    return jnp.where(i < 2, i, 9 - i)


def experts_kernel(
    rows_ref, dest_rows, dest_columns, gates, routes, inner_full, outer_full, counts_ref,
    mix_ref, arrived, returned, totals_ref,
    inner_ref, outer_ref, outgoing, results, counts, send_one, recv_one, send_two, recv_two, send_count, recv_count,
):
    capacity = arrived.shape[1]
    tokens = rows_ref.shape[0]
    greet_plane()
    counts[0] = counts_ref[...]

    def send_counts(step, carry):
        place, _ = plane_peer(step)
        pltpu.make_async_remote_copy(
            src_ref=counts_ref,
            dst_ref=counts.at[step],
            send_sem=send_count.at[step],
            recv_sem=recv_count.at[step],
            device_id=place,
            device_id_type=MESH_ID,
        ).start()
        return carry

    def dispatch(i, carry):
        step = 7 - i
        _, expert = plane_peer(step)
        hit = jnp.where(slot_hits(dest_rows, expert, capacity, tokens), 1.0, 0.0).astype(jnp.bfloat16)
        rows = jnp.dot(hit, rows_ref[...], preferred_element_type=jnp.float32).astype(jnp.bfloat16)

        @pl.when(step > 0)
        def _():
            outgoing[step] = rows
            plane_copy(outgoing, arrived, send_one, recv_one, step).start()

        @pl.when(step == 0)
        def _():
            arrived[0] = rows

        return carry

    def work(i, carry):
        step = arrival(i)

        @pl.when(step > 0)
        def _():
            plane_copy(outgoing, arrived, send_one, recv_one, step).wait_recv()

        before = jnp.dot(arrived[step], inner_ref[...], preferred_element_type=jnp.float32)
        active = gelu_tanh(before).astype(jnp.bfloat16)
        part = jnp.dot(active, outer_ref[...], preferred_element_type=jnp.float32).astype(jnp.bfloat16)

        @pl.when(step > 0)
        def _():
            results[step] = part
            plane_copy(results, returned, send_two, recv_two, step).start()

        @pl.when(step == 0)
        def _():
            returned[0] = part

        return carry

    def combine(i, carry):
        step = arrival(i)
        _, expert = plane_peer(step)
        hit = token_hits(dest_columns, expert, capacity, tokens)
        gate = gate_of(routes, gates, expert, 1)

        @pl.when(step > 0)
        def _():
            plane_copy(results, returned, send_two, recv_two, step).wait_recv()

        part = gate * jnp.dot(hit, returned[step], preferred_element_type=jnp.float32)

        @pl.when(i == 0)
        def _():
            mix_ref[...] = part

        @pl.when(i > 0)
        def _():
            mix_ref[...] += part

        return carry

    def finish(step, carry):
        plane_copy(outgoing, arrived, send_one, recv_one, step).wait_send()
        plane_copy(results, returned, send_two, recv_two, step).wait_send()
        place, _ = plane_peer(step)
        pltpu.make_async_remote_copy(
            src_ref=counts_ref,
            dst_ref=counts.at[step],
            send_sem=send_count.at[step],
            recv_sem=recv_count.at[step],
            device_id=place,
            device_id_type=MESH_ID,
        ).wait()
        return carry

    lax.fori_loop(0, 8, dispatch, 0)
    lax.fori_loop(1, 8, send_counts, 0)
    inner_ref[...] = inner_full[...].astype(jnp.bfloat16)
    outer_ref[...] = outer_full[...].astype(jnp.bfloat16)
    lax.fori_loop(0, 8, work, 0)
    lax.fori_loop(0, 8, combine, 0)
    lax.fori_loop(1, 8, finish, 0)
    totals_ref[...] = jnp.sum(counts[...], 0)


def experts_forward(rows, dest, gates, routes, inner, outer, counts, capacity, collective_id):
    tokens, width = rows.shape
    buffer = pltpu.VMEM((8, capacity, width), jnp.bfloat16)
    return pl.pallas_call(
        experts_kernel,
        out_shape=[
            jax.ShapeDtypeStruct((tokens, width), jnp.float32),
            jax.ShapeDtypeStruct((8, capacity, width), jnp.bfloat16),
            jax.ShapeDtypeStruct((8, capacity, width), jnp.bfloat16),
            jax.ShapeDtypeStruct(counts.shape, jnp.float32),
        ],
        in_specs=[whole_vmem] * 8,
        out_specs=[whole_vmem] * 4,
        scratch_shapes=[pltpu.VMEM(w.shape, jnp.bfloat16) for w in (inner, outer)]
        + [buffer, buffer, pltpu.VMEM((8,) + counts.shape, jnp.float32)]
        + [pltpu.SemaphoreType.DMA((8,))] * 6,
        compiler_params=pltpu.CompilerParams(
            collective_id=collective_id, has_side_effects=True, vmem_limit_bytes=60 << 20
        ),
    )(rows, dest, dest.T, gates, routes, inner, outer, counts)


def experts_back_kernel(
    rows_ref, dest_rows, dest_columns, gates, routes, returned, arrived, *refs
):
    inner_full, outer_full, grad_ref, gate_ref, inner_grad, outer_grad, inner_ref, outer_ref = refs[:8]
    outgoing, landed, results, landed_two, active, slopes = refs[8:14]
    send_one, recv_one, send_two, recv_two = refs[14:]
    capacity = arrived.shape[1]
    tokens = rows_ref.shape[0]
    greet_plane()
    gate_ref[...] = jnp.zeros_like(gate_ref)

    def dispatch(i, carry):
        step = 7 - i
        _, expert = plane_peer(step)
        hit = slot_hits(dest_rows, expert, capacity, tokens)
        rows = jnp.dot(
            jnp.where(hit, 1.0, 0.0).astype(jnp.bfloat16), rows_ref[...], preferred_element_type=jnp.float32
        )
        scale = jnp.sum(jnp.where(hit, gate_of(routes, gates, expert, 0), 0.0), 1, keepdims=True)
        sent = (rows * scale).astype(jnp.bfloat16)

        @pl.when(step > 0)
        def _():
            outgoing[step] = sent
            plane_copy(outgoing, landed, send_one, recv_one, step).start()

        @pl.when(step == 0)
        def _():
            landed[0] = sent

        dots = jnp.sum(rows * returned[step].astype(jnp.float32), 1, keepdims=True)
        part = jnp.sum(jnp.where(hit, dots, 0.0), 0, keepdims=True)
        for k in range(2):
            gate_ref[k : k + 1, :] += jnp.where(routes[k : k + 1, :] == expert, part, 0.0)
        return carry

    def work(i, carry):
        step = arrival(i)

        @pl.when(step > 0)
        def _():
            plane_copy(outgoing, landed, send_one, recv_one, step).wait_recv()

        grad_active = lax.dot_general(
            landed[step], outer_ref[...], (((1,), (1,)), ((), ())), preferred_element_type=jnp.float32
        )
        before = jnp.dot(arrived[step], inner_ref[...], preferred_element_type=jnp.float32)
        slope = (grad_active * gelu_slope(before)).astype(jnp.bfloat16)
        back = lax.dot_general(
            slope, inner_ref[...], (((1,), (1,)), ((), ())), preferred_element_type=jnp.float32
        ).astype(jnp.bfloat16)

        @pl.when(step > 0)
        def _():
            results[step] = back
            plane_copy(results, landed_two, send_two, recv_two, step).start()

        @pl.when(step == 0)
        def _():
            landed_two[0] = back

        slopes[step] = slope
        active[step] = gelu_tanh(before).astype(jnp.bfloat16)
        return carry

    def weigh(step, carry):
        outer_part = lax.dot_general(
            active[step], landed[step], (((0,), (0,)), ((), ())), preferred_element_type=jnp.float32
        )
        inner_part = lax.dot_general(
            arrived[step], slopes[step], (((0,), (0,)), ((), ())), preferred_element_type=jnp.float32
        )

        @pl.when(step == 0)
        def _():
            inner_grad[...] = inner_part
            outer_grad[...] = outer_part

        @pl.when(step > 0)
        def _():
            inner_grad[...] += inner_part
            outer_grad[...] += outer_part

        return carry

    def combine(i, carry):
        step = arrival(i)
        _, expert = plane_peer(step)
        hit = token_hits(dest_columns, expert, capacity, tokens)

        @pl.when(step > 0)
        def _():
            plane_copy(results, landed_two, send_two, recv_two, step).wait_recv()

        part = jnp.dot(hit, landed_two[step], preferred_element_type=jnp.float32)

        @pl.when(i == 0)
        def _():
            grad_ref[...] = part

        @pl.when(i > 0)
        def _():
            grad_ref[...] += part

        return carry

    def finish(step, carry):
        plane_copy(outgoing, landed, send_one, recv_one, step).wait_send()
        plane_copy(results, landed_two, send_two, recv_two, step).wait_send()
        return carry

    lax.fori_loop(0, 8, dispatch, 0)
    inner_ref[...] = inner_full[...].astype(jnp.bfloat16)
    outer_ref[...] = outer_full[...].astype(jnp.bfloat16)
    lax.fori_loop(0, 8, work, 0)
    lax.fori_loop(0, 8, weigh, 0)
    lax.fori_loop(0, 8, combine, 0)
    lax.fori_loop(1, 8, finish, 0)


def experts_backward(rows, dest, gates, routes, returned, arrived, inner, outer, collective_id):
    tokens, width = rows.shape
    capacity = arrived.shape[1]
    inside = inner.shape[1]
    buffer = pltpu.VMEM((8, capacity, width), jnp.bfloat16)
    inside_buffer = pltpu.VMEM((8, capacity, inside), jnp.bfloat16)
    return pl.pallas_call(
        experts_back_kernel,
        out_shape=[
            jax.ShapeDtypeStruct((tokens, width), jnp.float32),
            jax.ShapeDtypeStruct((2, tokens), jnp.float32),
            jax.ShapeDtypeStruct((width, inside), jnp.float32),
            jax.ShapeDtypeStruct((inside, width), jnp.float32),
        ],
        in_specs=[whole_vmem] * 9,
        out_specs=[whole_vmem] * 4,
        scratch_shapes=[pltpu.VMEM(w.shape, jnp.bfloat16) for w in (inner, outer)]
        + [buffer] * 4
        + [inside_buffer] * 2
        + [pltpu.SemaphoreType.DMA((8,))] * 4,
        compiler_params=pltpu.CompilerParams(
            collective_id=collective_id, has_side_effects=True, vmem_limit_bytes=60 << 20
        ),
    )(rows, dest, dest.T, gates, routes, returned, arrived, inner, outer)


def own_units_kernel(
    chunks, units_of, slopes_ref, rows_ref, ids_ref, zero_ref, joint_ref, normed_ref, attended_ref,
    grad_ref, small_ref, grads_ref, small_out, *refs
):
    slopes, late, mixed, made, passing, own, other, relay, landed, small_landed, ready = refs[:11]
    other_send, other_recv, relay_send, relay_recv, landed_send, landed_recv = refs[11:17]
    small_send, small_recv, load_sem, store_sem = refs[17:]
    chip, core = lax.axis_index("dp"), lax.axis_index("ctx")
    beside = chip + 1 - 2 * lax.rem(chip, 2)
    across = lax.rem(chip + 2, 4)
    opposite = across + 1 - 2 * lax.rem(across, 2)
    places = (opposite, beside, across, chip)
    slots, unit_rows = own.shape[1:3]
    table_units = slopes.shape[0]
    tokens = rows_ref.shape[0]
    size = slots // chunks
    split = (chunks + 1) // 2
    load = pltpu.make_async_copy(slopes_ref, slopes, load_sem)
    load.start()
    greet_plane()

    def repeat(first, last, body):
        def step(i, carry):
            body(i)
            return carry

        lax.fori_loop(first, last, step, 0)

    def span(q):
        return pl.ds(q * size, size)

    def remote(source, target, send, recv, place):
        return pltpu.make_async_remote_copy(
            src_ref=source,
            dst_ref=target,
            send_sem=send,
            recv_sem=recv,
            device_id=place,
            device_id_type=MESH_ID,
        )

    def pass_over(k, q):
        return remote(
            passing.at[k % 2, span(q)],
            other.at[k, span(q)],
            other_send.at[k, q],
            other_recv.at[k, q],
            {"ctx": 1 - core},
        )

    def to_relay(q, place):
        return remote(own.at[0, span(q)], relay.at[span(q)], relay_send.at[q], relay_recv.at[q], {"dp": place})

    def to_owner(k, q):
        return remote(
            own.at[k, span(q)],
            landed.at[k - 1, span(q)],
            landed_send.at[k - 1, q],
            landed_recv.at[k - 1, q],
            {"dp": places[k]},
        )

    def small_copy(step):
        place, _ = plane_peer(step)
        return remote(
            small_ref, small_landed.at[chip * 2 + core], small_send.at[step], small_recv.at[step], place
        )

    joint_units = joint_ref.shape[0] // unit_rows
    late[pl.ds(0, joint_units)] = jnp.dot(
        joint_ref[...], normed_ref[...], preferred_element_type=jnp.float32
    ).reshape(joint_units, unit_rows, -1)
    last_units = attended_ref.shape[0] // unit_rows
    late[pl.ds(joint_units, last_units)] = jnp.dot(
        attended_ref[...], grad_ref[...], preferred_element_type=jnp.float32
    ).reshape(last_units, unit_rows, -1)
    load.wait()
    group = made.shape[0] // unit_rows

    def form(owner, target):
        def some(g):
            first = owner * slots + g * group

            def fill(s):
                unit = units_of[first + s]
                lines = pl.ds(pl.multiple_of(s * unit_rows, unit_rows), unit_rows)
                mixed[lines, :tokens] = slopes[jnp.minimum(unit, table_units - 1)]
                row = lax.broadcasted_iota(jnp.int32, (unit_rows, tokens), 0) + unit * unit_rows
                mixed[lines, tokens:] = jnp.where(row == ids_ref[...], 1.0, 0.0).astype(jnp.bfloat16)

            repeat(0, group, fill)
            made[...] = jnp.dot(
                mixed[:, :tokens], rows_ref[...], preferred_element_type=jnp.float32
            ) + jnp.dot(mixed[:, tokens:], zero_ref[...], preferred_element_type=jnp.float32)

            def put(s):
                unit = units_of[first + s]
                table_piece = made[pl.ds(pl.multiple_of(s * unit_rows, unit_rows), unit_rows)]
                late_piece = late[jnp.clip(unit - table_units, 0, late.shape[0] - 1)]
                marks = jnp.zeros(table_piece.shape, jnp.int32) + unit
                piece = jnp.where(marks < table_units, table_piece, late_piece)
                target[g * group + s] = piece.astype(jnp.bfloat16)

            repeat(0, group, put)

        repeat(0, slots // group, some)

    def joined(k, q):
        pass_over(k, q).wait_recv()
        return own[k, span(q)].astype(jnp.float32) + other[k, span(q)].astype(jnp.float32)

    def first_leg(place):
        def leg(q):
            own[0, span(q)] = joined(0, q).astype(jnp.bfloat16)
            to_relay(q, place).start()

        return leg

    def direct(k):
        def leg(q):
            own[k, span(q)] = joined(k, q).astype(jnp.bfloat16)
            to_owner(k, q).start()

        return leg

    def relayed(k, place):
        def leg(q):
            to_relay(q, place).wait_recv()
            total = joined(k, q) + relay[span(q)].astype(jnp.float32)
            own[k, span(q)] = total.astype(jnp.bfloat16)
            to_owner(k, q).start()

        return leg

    def form_pair(k):
        if k >= 2:
            repeat(0, chunks, lambda q: pass_over(k - 2, q).wait_send())
        form(places[k] * 2 + 1 - core, passing.at[k % 2])
        repeat(0, chunks, lambda q: pass_over(k, q).start())
        form(places[k] * 2 + core, own.at[k])

    form_pair(0)
    repeat(0, split, first_leg(beside))
    repeat(split, chunks, first_leg(across))
    repeat(1, 8, lambda step: small_copy(step).start())
    small_landed[chip * 2 + core] = small_ref[...]
    form_pair(1)
    repeat(0, split, direct(1))
    form_pair(2)
    repeat(split, chunks, direct(2))
    repeat(0, split, relayed(2, beside))
    repeat(split, chunks, relayed(1, across))
    form_pair(3)

    def store(q):
        return pltpu.make_async_copy(
            ready.at[lax.rem(q, 2)], grads_ref.at[span(q)], store_sem.at[lax.rem(q, 2)]
        )

    def keep(q):
        total = joined(3, q)
        to_owner(1, q).wait_recv()
        to_owner(2, q).wait_recv()

        @pl.when(q >= 2)
        def _():
            store(q - 2).wait()

        ready[lax.rem(q, 2)] = (
            total + landed[0, span(q)].astype(jnp.float32) + landed[1, span(q)].astype(jnp.float32)
        )
        store(q).start()

    repeat(0, chunks, keep)

    def finish(q):
        for k in (2, 3):
            pass_over(k, q).wait_send()
        to_owner(1, q).wait_send()
        to_owner(2, q).wait_send()

    repeat(0, chunks, finish)
    repeat(0, split, lambda q: to_relay(q, beside).wait_send())
    repeat(split, chunks, lambda q: to_relay(q, across).wait_send())
    repeat(1, 8, lambda step: small_copy(step).wait())
    total = small_landed[0]
    for source in range(1, 8):
        total = total + small_landed[source]
    small_out[...] = total
    for q in range(max(0, chunks - 2), chunks):
        store(q).wait()


def own_units(units_of, slots, unit_rows, slopes, rows, ids, zero, joint, normed, attended, grad, small, collective_id):
    tokens, width = rows.shape
    unit = (unit_rows, width)
    chunks = max(k for k in range(1, 8) if slots % k == 0)
    group = max(k for k in range(1, 8) if slots % k == 0)
    late = (joint.shape[0] + attended.shape[0]) // unit_rows
    slopes = slopes.reshape(-1, unit_rows, tokens)
    return pl.pallas_call(
        functools.partial(own_units_kernel, chunks),
        out_shape=[
            jax.ShapeDtypeStruct((slots,) + unit, jnp.float32),
            jax.ShapeDtypeStruct(small.shape, jnp.float32),
        ],
        in_specs=[pl.BlockSpec(memory_space=pltpu.SMEM), whole_any] + [whole_vmem] * 8,
        out_specs=[whole_any, whole_vmem],
        scratch_shapes=[
            pltpu.VMEM(slopes.shape, jnp.bfloat16),
            pltpu.VMEM((late,) + unit, jnp.float32),
            pltpu.VMEM((group * unit_rows, 2 * tokens), jnp.bfloat16),
            pltpu.VMEM((group * unit_rows, width), jnp.float32),
            pltpu.VMEM((2, slots) + unit, jnp.bfloat16),
            pltpu.VMEM((4, slots) + unit, jnp.bfloat16),
            pltpu.VMEM((4, slots) + unit, jnp.bfloat16),
            pltpu.VMEM((slots,) + unit, jnp.bfloat16),
            pltpu.VMEM((2, slots) + unit, jnp.bfloat16),
            pltpu.VMEM((8,) + small.shape, jnp.float32),
            pltpu.VMEM((2, slots // chunks) + unit, jnp.float32),
            pltpu.SemaphoreType.DMA((4, chunks)),
            pltpu.SemaphoreType.DMA((4, chunks)),
            pltpu.SemaphoreType.DMA((chunks,)),
            pltpu.SemaphoreType.DMA((chunks,)),
            pltpu.SemaphoreType.DMA((2, chunks)),
            pltpu.SemaphoreType.DMA((2, chunks)),
            pltpu.SemaphoreType.DMA((8,)),
            pltpu.SemaphoreType.DMA((8,)),
            pltpu.SemaphoreType.DMA,
            pltpu.SemaphoreType.DMA((2,)),
        ],
        compiler_params=pltpu.CompilerParams(
            collective_id=collective_id, has_side_effects=True, vmem_limit_bytes=63 << 20
        ),
    )(units_of, slopes, rows, ids, zero, joint, normed, attended, grad, small)


def to_plane(buffer):
    return lax.all_to_all(buffer, ("dp", "ctx"), split_axis=0, concat_axis=0, tiled=True)


def plain_hits(dest, experts, capacity):
    slots = lax.broadcasted_iota(jnp.int32, (experts * capacity, dest.shape[1]), 0)
    return [slots == dest[k : k + 1] for k in range(2)]


def plain_forward(rows, dest, gates, inner, outer, owners, capacity):
    width = rows.shape[1]
    hits = plain_hits(dest, owners, capacity)
    both = (hits[0] | hits[1]).astype(jnp.bfloat16)
    sent = jnp.dot(both, rows, preferred_element_type=jnp.float32).astype(jnp.bfloat16)
    arrived = to_plane(sent.reshape(owners, capacity, width))
    hidden = jnp.einsum("ocd,df->ocf", arrived, inner, preferred_element_type=jnp.float32)
    active = gelu_tanh(hidden).astype(jnp.bfloat16)
    part = jnp.einsum("ocf,fd->ocd", active, outer, preferred_element_type=jnp.float32)
    returned = to_plane(part.astype(jnp.bfloat16))
    flat = returned.reshape(owners * capacity, width)
    mix = sum(
        gates[:, k : k + 1]
        * lax.dot_general(
            hits[k].astype(jnp.bfloat16),
            flat,
            (((0,), (0,)), ((), ())),
            preferred_element_type=jnp.float32,
        )
        for k in range(2)
    )
    return (mix, arrived, returned)


def plain_backward(rows, dest, gates, returned, arrived, inner, outer):
    owners, capacity, width = arrived.shape
    hits = plain_hits(dest, owners, capacity)
    both = (hits[0] | hits[1]).astype(jnp.bfloat16)
    slot_scale = jnp.sum(
        jnp.where(hits[0], gates[0:1], 0.0) + jnp.where(hits[1], gates[1:2], 0.0), 1, keepdims=True
    )
    slot_grads = jnp.dot(both, rows, preferred_element_type=jnp.float32)
    sent = (slot_grads * slot_scale).astype(jnp.bfloat16)
    flat = returned.reshape(owners * capacity, width)
    dots = jnp.sum(slot_grads * flat.astype(jnp.float32), 1, keepdims=True)
    gate_part = jnp.concatenate(
        [jnp.sum(jnp.where(hit, dots, 0.0), 0, keepdims=True) for hit in hits], 0
    )
    landed = to_plane(sent.reshape(owners, capacity, width))
    grad_active = jnp.einsum("ocd,fd->ocf", landed, outer, preferred_element_type=jnp.float32)
    hidden = jnp.einsum("ocd,df->ocf", arrived, inner, preferred_element_type=jnp.float32)
    active = gelu_tanh(hidden).astype(jnp.bfloat16)
    slope = (grad_active * gelu_slope(hidden)).astype(jnp.bfloat16)
    outer_grad = jnp.einsum("ocf,ocd->fd", active, landed, preferred_element_type=jnp.float32)
    inner_grad = jnp.einsum("ocd,ocf->df", arrived, slope, preferred_element_type=jnp.float32)
    back = jnp.einsum("ocf,df->ocd", slope, inner, preferred_element_type=jnp.float32)
    back = to_plane(back.astype(jnp.bfloat16)).reshape(owners * capacity, width)
    grad = lax.dot_general(
        both, back, (((0,), (0,)), ((), ())), preferred_element_type=jnp.float32
    )
    return (grad, gate_part, inner_grad, outer_grad)


def on_device(
    token_ids,
    targets,
    counted,
    routes,
    priority,
    owner_of,
    master,
    master_first,
    master_second,
    expert_in,
    expert_in_first,
    expert_in_second,
    expert_out,
    expert_out_first,
    expert_out_second,
    norm_gains,
    norm_gains_first,
    norm_gains_second,
    router,
    router_first,
    router_second,
    rel_bias,
    rel_bias_first,
    rel_bias_second,
):
    owners = lax.axis_size(("dp", "ctx"))
    tensor_ranks = lax.axis_size("tensor")
    my_owner = lax.axis_index(("dp", "ctx"))
    my_rank = lax.axis_index("tensor")
    my_context = lax.axis_index("ctx")
    sequences, half_length = token_ids.shape
    tokens_here = sequences * half_length
    most_units = master.shape[2]
    unit_rows = master.shape[3]
    model_width = master.shape[4]
    vocab_here = VOCAB // tensor_ranks
    heads_here = rel_bias.shape[0]
    head_size = model_width // (heads_here * tensor_ranks)
    hidden_here = heads_here * head_size
    experts = router.shape[1]
    capacity = (18 * tokens_here + 8 * experts - 1) // (8 * experts)
    table_units = vocab_here // unit_rows
    query_units = table_units + 2 * hidden_here // unit_rows
    value_units = table_units + 3 * hidden_here // unit_rows
    embed_scale = math.sqrt(model_width)
    owner_ids = owner_of[:, 0]
    on_square = lax.axis_size("dp") == 4 and lax.axis_size("ctx") == 2
    unit_rank, slot_unit, slot_filled = slot_tables(owner_ids, owners, most_units)
    counted_rows = counted.reshape(tokens_here, 2).T.astype(jnp.float32)
    loss_weights = counted_rows * jnp.array([[1.0], [ahead_weight]], jnp.float32)
    counts = jnp.zeros((8, 128), jnp.float32).at[0:2].set(jnp.sum(counted_rows, 1, keepdims=True))
    unit_slots = owner_ids * most_units + unit_rank
    route_pairs = routes.reshape(tokens_here, 2)
    pair_kept, pair_dest = pair_slots(route_pairs, priority[0], experts, capacity)
    dest = jnp.where(pair_kept, pair_dest, -1).reshape(2, tokens_here)
    unit_slots, dest = lax.optimization_barrier((unit_slots, dest))
    local_ids = token_ids.reshape(-1) - my_rank * vocab_here
    inside = (local_ids >= 0) & (local_ids < vocab_here)
    clipped_ids = jnp.clip(local_ids, 0, vocab_here - 1)
    unit_starts = jnp.sum(
        jnp.where(
            (clipped_ids // unit_rows)[None, :] == jnp.arange(unit_slots.shape[0])[:, None],
            unit_slots[:, None] * unit_rows,
            0,
        ),
        0,
    )
    slot_rows = unit_starts + clipped_ids % unit_rows
    if on_square:
        slot_rows = jnp.where(inside, slot_rows, -1)[:, None]
        weights_low, embedded, normed_one_low, joint, joint_low, project_low = embed(
            unit_slots,
            master[0, 0],
            slot_rows,
            norm_gains[0:1],
            table_units,
            3 * hidden_here,
            11,
        )
    else:
        master_low = master[0, 0].astype(jnp.bfloat16)
        gathered = lax.all_gather(master_low, ("dp", "ctx"), axis=0, tiled=True)
        looked = jnp.take(gathered.reshape(-1, model_width), slot_rows, axis=0)
        looked = jnp.where(inside[:, None], looked, 0)
        weights_low = pull_units([gathered], unit_slots)
        (embedded,) = sum_line(looked, [], [], keep_total, 1)
    weights_low = weights_low.reshape(-1, model_width)
    if not on_square:
        joint_low = weights_low[vocab_here : vocab_here + 3 * hidden_here]
        project_low = weights_low[vocab_here + 3 * hidden_here :]
    rolled = [project_low] + [
        lax.ppermute(project_low, "tensor", [(source, (source + step) % 4) for source in range(4)])
        for step in (1, 2, 3)
    ]
    gain_rows = [norm_gains[k : k + 1] for k in range(3)]
    stream_shape = jax.ShapeDtypeStruct((tokens_here, model_width), jnp.float32)
    gain_shape = jax.ShapeDtypeStruct((1, model_width), jnp.float32)
    if not on_square:
        stream_zero = embedded.astype(jnp.float32) * embed_scale
        normed_one_low = norm_forward(stream_zero, norm_gains[0]).astype(jnp.bfloat16)
        joint = lax.dot_general(
            joint_low, normed_one_low, (((1,), (1,)), ((), ())), preferred_element_type=jnp.float32
        ).astype(jnp.bfloat16)
    attended_all, logsum_rows, pairs_before, attended = attention(
        rel_bias, joint, heads_here, head_size, 2
    )
    router_low = router.astype(jnp.bfloat16)
    stream_one, normed_two_low, gate_rows, gate_columns = middle(
        attended_all.reshape(model_width, tokens_here),
        rolled,
        embedded,
        gain_rows[1],
        router_low.T,
        route_pairs.T,
    )
    if on_square:
        moe_partial, arrived, returned, counts = experts_forward(
            normed_two_low, dest, gate_columns, route_pairs, expert_in[0], expert_out[0], counts, capacity, 8
        )
    else:
        inner_low, outer_low = expert_in[0].astype(jnp.bfloat16), expert_out[0].astype(jnp.bfloat16)
        moe_partial, arrived, returned = plain_forward(
            normed_two_low, dest, gate_columns, inner_low, outer_low, owners, capacity
        )
        counts = lax.psum(counts, ("dp", "ctx"))
    weight_total = counts[0, 0] + ahead_weight * counts[1, 0]
    local_targets = targets.reshape(tokens_here, 2).T - my_rank * vocab_here
    weight_rows = jnp.concatenate(
        [
            loss_weights,
            loss_weights[0:1] + loss_weights[1:2],
            jnp.broadcast_to(1.0 / weight_total, (1, tokens_here)),
        ],
        0,
    )
    head_low, grad_two_low, grad_two, gain_grad_three, logsum_vocab, target_sums, slopes = head_line(
        moe_partial, stream_one, gain_rows[2], weights_low, local_targets, weight_rows, vocab_here, 3
    )
    if on_square:
        moe_grad_part, gate_part, inner_grad, outer_grad = experts_backward(
            grad_two_low,
            dest,
            gate_rows,
            route_pairs.T,
            returned,
            arrived,
            expert_in[0],
            expert_out[0],
            9,
        )
    else:
        moe_grad_part, gate_part, inner_grad, outer_grad = plain_backward(
            grad_two_low, dest, gate_rows, returned, arrived, inner_low, outer_low
        )
    gate_part = jnp.concatenate([gate_part, target_sums, jnp.zeros_like(target_sums)], 0)
    gate_block = pltpu.VMEM((3, 4, tokens_here), jnp.float32)
    grad_one_low, grad_one, logit_grad, target_total, gain_grad_two = sum_line(
        moe_grad_part,
        [
            stream_one,
            gain_rows[1],
            grad_two,
            gate_part,
            gate_rows,
            route_pairs.T,
            router_low,
        ],
        [
            stream_shape,
            jax.ShapeDtypeStruct((experts, tokens_here), jnp.bfloat16),
            jax.ShapeDtypeStruct((1, tokens_here), jnp.float32),
            gain_shape,
        ],
        finish_expert_grad,
        5,
        prologue=start_router_grad,
        scratch=(gate_block, pltpu.SemaphoreType.DMA((3,)), pltpu.SemaphoreType.DMA((3,))),
        opening=send_gate_parts,
    )
    router_grad = jnp.dot(logit_grad, normed_two_low, preferred_element_type=jnp.float32)
    loss_local = jnp.sum(weight_rows[2:3] * logsum_vocab) - jnp.sum(target_total)
    query_grad, pair_grad, before_grad, bias_lines, *expert_states = attention_back(
        rel_bias,
        joint,
        pairs_before,
        logsum_rows,
        grad_one_low,
        project_low,
        (
            expert_in[0],
            expert_in_first[0],
            expert_in_second[0],
            inner_grad,
            expert_out[0],
            expert_out_first[0],
            expert_out_second[0],
            outer_grad,
        ),
        heads_here,
        head_size,
    )
    distances = 2 * (half_length // BLOCK)
    bias_grad = jnp.sum(bias_lines, 1).reshape(heads_here, distances)
    pair_shape = pltpu.VMEM((2 * hidden_here, tokens_here), jnp.bfloat16)
    zero_grad_low, joint_grad, gain_grads = sum_line(
        None,
        [
            embedded,
            gain_rows[0],
            grad_one,
            gain_grad_two,
            gain_grad_three,
            query_grad,
            pair_grad,
            before_grad,
            joint_low,
        ],
        [
            jax.ShapeDtypeStruct((3 * hidden_here, tokens_here), jnp.bfloat16),
            jax.ShapeDtypeStruct((8, model_width), jnp.float32),
        ],
        functools.partial(finish_input_grad, embed_scale),
        6,
        prologue=clear_gain,
        scratch=(
            pltpu.SemaphoreType.DMA,
            pltpu.SemaphoreType.DMA,
            pair_shape,
            pltpu.SemaphoreType.DMA((2,)),
            pltpu.VMEM((tokens_here, model_width), jnp.float32),
        ),
        opening=form_joint_grad,
        ending=share_gains,
    )
    my_units = jnp.take(slot_unit, my_owner, axis=0)
    my_filled = jnp.take(slot_filled, my_owner, axis=0)[:, None, None]
    bias_row = jnp.concatenate([bias_grad.reshape(-1), loss_local[None]])
    bias_row = jnp.pad(bias_row, (0, model_width - bias_row.shape[0]))[None]
    small = jnp.concatenate([gain_grads[:3], router_grad, bias_row], 0)
    small = jnp.pad(small, ((0, -small.shape[0] % 8), (0, 0)))
    slot_rates = unit_rates(my_units, table_units, query_units, value_units)[:, None, None]
    states = (master[0, 0], master_first[0, 0], master_second[0, 0])
    grad_rows = (
        slopes,
        head_low,
        local_ids[None, :],
        zero_grad_low,
        joint_grad,
        normed_one_low,
        attended,
        grad_one_low,
    )
    if on_square:
        mine, small = own_units(slot_unit.reshape(-1), most_units, unit_rows, *grad_rows, small, 10)
    else:
        outgoing = weight_grads(unit_slots, owners * most_units, unit_rows, *grad_rows)
        mine = lax.psum_scatter(
            outgoing.astype(jnp.float32), ("dp", "ctx"), scatter_dimension=0, tiled=True
        )
        small = lax.psum(small, ("dp", "ctx"))
    states = adam_update(*states, jnp.where(my_filled, mine, 0.0), slot_rates, decay_rate)
    gains_grad = small[:3]
    router_grad = small[3 : 3 + experts].T
    bias_grad = small[3 + experts, : rel_bias.size].reshape(rel_bias.shape)
    loss_totals = jnp.stack([small[3 + experts, rel_bias.size], weight_total])
    gains_new, gains_first_new, gains_second_new = adam_update(
        norm_gains, norm_gains_first, norm_gains_second, gains_grad, rate_gains, 0.0
    )
    router_new, router_first_new, router_second_new = adam_update(
        router, router_first, router_second, router_grad, rate_router, decay_rate
    )
    biases_new, biases_first_new, biases_second_new = adam_update(
        rel_bias, rel_bias_first, rel_bias_second, bias_grad, rate_biases, 0.0
    )
    return (
        loss_totals,
        *(state[None, None] for state in states),
        *(state[None] for state in expert_states),
        gains_new,
        gains_first_new,
        gains_second_new,
        router_new,
        router_first_new,
        router_second_new,
        biases_new,
        biases_first_new,
        biases_second_new,
    )


def solution(mesh):
    in_specs = (
        P("dp", "ctx"),
        P("dp", "ctx", None),
        P("dp", "ctx", None),
        P("dp", "ctx", None),
        P(("dp", "ctx"), None),
        P(),
        P("tensor", ("dp", "ctx"), None, None, None),
        P("tensor", ("dp", "ctx"), None, None, None),
        P("tensor", ("dp", "ctx"), None, None, None),
        P(("dp", "ctx"), None, "tensor"),
        P(("dp", "ctx"), None, "tensor"),
        P(("dp", "ctx"), None, "tensor"),
        P(("dp", "ctx"), "tensor", None),
        P(("dp", "ctx"), "tensor", None),
        P(("dp", "ctx"), "tensor", None),
        P(),
        P(),
        P(),
        P(),
        P(),
        P(),
        P("tensor", None),
        P("tensor", None),
        P("tensor", None),
    )
    out_specs = (
        P(),
        P("tensor", ("dp", "ctx"), None, None, None),
        P("tensor", ("dp", "ctx"), None, None, None),
        P("tensor", ("dp", "ctx"), None, None, None),
        P(("dp", "ctx"), None, "tensor"),
        P(("dp", "ctx"), None, "tensor"),
        P(("dp", "ctx"), None, "tensor"),
        P(("dp", "ctx"), "tensor", None),
        P(("dp", "ctx"), "tensor", None),
        P(("dp", "ctx"), "tensor", None),
        P(),
        P(),
        P(),
        P(),
        P(),
        P(),
        P("tensor", None),
        P("tensor", None),
        P("tensor", None),
    )
    return jax.shard_map(
        on_device, mesh=mesh, in_specs=in_specs, out_specs=out_specs, check_vma=False
    )
```

```python
import functools
import math

import jax
import jax.numpy as jnp
from jax import lax
from jax.experimental import pallas as pl
from jax.experimental.pallas import tpu as pltpu
from jax.sharding import PartitionSpec as P

VOCAB = 32000
BLOCK = 256
STEP = 10


highest_precision = lax.Precision.HIGHEST
beta_first = 0.9
beta_second = 0.95
adam_epsilon = 1e-08
norm_epsilon = 1e-06
ahead_weight = 0.3
masked_score = -1e30
rate_table = 0.1
rate_query = 0.05
rate_values = 0.05
rate_project = 0.5
rate_inner = 0.05
rate_outer = 0.03
rate_gains = 0.5
rate_router = 0.05
rate_biases = 0.5
decay_rate = 0.1


MESH_ID = pl.DeviceIdType.MESH
whole_vmem = pl.BlockSpec(memory_space=pltpu.VMEM)
whole_any = pl.BlockSpec(memory_space=pl.ANY)
line_lag = 2


def sum_line_kernel(
    rows, count, opening, with_core, prologue, epilogue, ending, n_extra, n_aux, n_scratch, *refs
):
    extras = refs[:n_extra]
    out_ref = refs[n_extra]
    aux = refs[n_extra + 1 : n_extra + 1 + n_aux]
    rest = refs[n_extra + 1 + n_aux :]
    scratch = rest[:n_scratch]
    part_ref = scratch[-1] if with_core else extras[0]
    extras = extras if with_core else extras[1:]
    stage, from_end, from_mid, send_sem, end_sem, mid_sem, back_sem, back_recv = rest[n_scratch:]
    rank = lax.axis_index("tensor")
    inner = (rank == 1) | (rank == 2)
    end_peer = jnp.where(rank < 2, 1 - rank, 5 - rank)
    mid_peer = 3 - rank
    barrier = pltpu.get_barrier_semaphore()
    if opening is None or with_core:
        pl.semaphore_signal(barrier, inc=1, device_id={"tensor": end_peer}, device_id_type=MESH_ID)
        if with_core:
            other_core = {"ctx": 1 - lax.axis_index("ctx")}
            pl.semaphore_signal(barrier, inc=1, device_id=other_core, device_id_type=MESH_ID)

        @pl.when(inner)
        def _():
            pl.semaphore_signal(
                barrier, inc=1, device_id={"tensor": mid_peer}, device_id_type=MESH_ID
            )
            pl.semaphore_wait(barrier, 2 + with_core)

        @pl.when(jnp.logical_not(inner))
        def _():
            pl.semaphore_wait(barrier, 1 + with_core)
    else:
        for step in (1, 2, 3):
            other = lax.rem(rank + step, 4)
            pl.semaphore_signal(barrier, inc=1, device_id={"tensor": other}, device_id_type=MESH_ID)
        pl.semaphore_wait(barrier, 3)

    def span(i):
        return pl.ds(pl.multiple_of(i * rows, rows), rows)

    def to_inner(i):
        return pltpu.make_async_remote_copy(
            src_ref=stage.at[i],
            dst_ref=from_end.at[i],
            send_sem=send_sem.at[i],
            recv_sem=end_sem.at[i],
            device_id={"tensor": end_peer},
            device_id_type=MESH_ID,
        )

    def to_middle(i):
        return pltpu.make_async_remote_copy(
            src_ref=stage.at[i],
            dst_ref=from_mid.at[i],
            send_sem=send_sem.at[i],
            recv_sem=mid_sem.at[i],
            device_id={"tensor": mid_peer},
            device_id_type=MESH_ID,
        )

    def to_end(i):
        return pltpu.make_async_remote_copy(
            src_ref=out_ref.at[span(i)],
            dst_ref=out_ref.at[span(i)],
            send_sem=back_sem.at[i],
            recv_sem=back_recv.at[i],
            device_id={"tensor": end_peer},
            device_id_type=MESH_ID,
        )

    if opening is not None:
        opening(rank, extras, aux, scratch)

    @pl.when(jnp.logical_not(inner))
    def _():
        def push(i, carry):
            stage[i] = part_ref[span(i)].astype(jnp.bfloat16)
            to_inner(i).start()
            return carry

        lax.fori_loop(0, count, push, 0)

    if prologue is not None:
        prologue(rank, inner, extras, aux, scratch)

    @pl.when(inner)
    def _():
        def step(i, carry):
            @pl.when(i < count)
            def _():
                to_inner(i).wait_recv()
                mine = part_ref[span(i)].astype(jnp.float32) + from_end[i].astype(jnp.float32)
                stage[i] = mine.astype(jnp.bfloat16)
                to_middle(i).start()

            @pl.when(i >= line_lag)
            def _():
                j = i - line_lag
                to_middle(j).wait_recv()
                total = stage[j].astype(jnp.float32) + from_mid[j].astype(jnp.float32)
                out_ref[span(j)] = epilogue(total, span(j), rank, extras, aux, scratch)
                to_end(j).start()

            return carry

        lax.fori_loop(0, count + line_lag, step, 0)

        def drain(i, carry):
            to_middle(i).wait_send()
            to_end(i).wait_send()
            return carry

        lax.fori_loop(0, count, drain, 0)

    @pl.when(jnp.logical_not(inner))
    def _():
        def finish(i, carry):
            to_end(i).wait_recv()
            to_inner(i).wait_send()
            return carry

        lax.fori_loop(0, count, finish, 0)

    if ending is not None:
        ending(inner, end_peer, extras, aux, scratch)


def sum_line(
    part,
    extras,
    aux_shapes,
    epilogue,
    collective_id,
    prologue=None,
    scratch=(),
    opening=None,
    ending=None,
    rows=64,
):
    tokens, width = scratch[-1].shape if part is None else part.shape
    inputs = list(extras) if part is None else [part, *extras]
    count = tokens // rows
    chunks = pltpu.VMEM((count, rows, width), jnp.bfloat16)
    return pl.pallas_call(
        functools.partial(
            sum_line_kernel,
            rows,
            count,
            opening,
            part is None,
            prologue,
            epilogue,
            ending,
            len(inputs),
            len(aux_shapes),
            len(scratch),
        ),
        out_shape=[jax.ShapeDtypeStruct((tokens, width), jnp.bfloat16)] + list(aux_shapes),
        in_specs=[whole_vmem] * len(inputs),
        out_specs=[whole_vmem] * (1 + len(aux_shapes)),
        scratch_shapes=list(scratch)
        + [chunks, chunks, chunks]
        + [pltpu.SemaphoreType.DMA((count,))] * 5,
        compiler_params=pltpu.CompilerParams(
            collective_id=collective_id, has_side_effects=True, vmem_limit_bytes=48 << 20
        ),
    )(*inputs)


def keep_total(total, span, rank, extras, aux, scratch):
    return total.astype(jnp.bfloat16)


def inverse_rms(values):
    return lax.rsqrt(jnp.mean(values * values, -1, keepdims=True) + norm_epsilon)


def norm_back_rows(values, gain, upstream):
    inverse = inverse_rms(values)
    normed = values * inverse
    scaled = upstream * gain
    gain_grad = jnp.sum(upstream * normed, 0, keepdims=True)
    inputs_grad = inverse * (scaled - normed * jnp.mean(scaled * normed, -1, keepdims=True))
    return (inputs_grad, gain_grad)


def clear_gain(rank, inner, extras, aux, scratch):
    @pl.when(inner)
    def _():
        aux[-1][...] = jnp.zeros_like(aux[-1])


def share_gains(inner, end_peer, extras, aux, scratch):
    gains = aux[-1]
    copy = pltpu.make_async_remote_copy(
        src_ref=gains,
        dst_ref=gains,
        send_sem=scratch[0],
        recv_sem=scratch[1],
        device_id={"tensor": end_peer},
        device_id_type=MESH_ID,
    )

    @pl.when(inner)
    def _():
        gains[1:2, :] = extras[3][...]
        gains[2:3, :] = extras[4][...]
        copy.start()
        copy.wait_send()

    @pl.when(jnp.logical_not(inner))
    def _():
        copy.wait_recv()


def gate_copies(rank, extras, scratch):
    gate_part = extras[3]
    landed, gate_send, gate_recv = scratch
    return [
        pltpu.make_async_remote_copy(
            src_ref=gate_part,
            dst_ref=landed.at[step - 1],
            send_sem=gate_send.at[step - 1],
            recv_sem=gate_recv.at[step - 1],
            device_id={"tensor": lax.rem(rank + step, 4)},
            device_id_type=MESH_ID,
        )
        for step in (1, 2, 3)
    ]


def send_gate_parts(rank, extras, aux, scratch):
    for copy in gate_copies(rank, extras, scratch):
        copy.start()


def start_router_grad(rank, inner, extras, aux, scratch):
    stream_one, gain, grad_two, gate_part, gates, routes, router_low = extras
    grad_one, logit_grad, target_total, gain_grad = aux
    landed = scratch[0]
    clear_gain(rank, inner, extras, aux, scratch)
    for copy in gate_copies(rank, extras, scratch):
        copy.wait()
    gate_grad = jnp.zeros(gate_part.shape, jnp.float32)
    for source in range(4):
        piece = jnp.zeros(gate_part.shape, jnp.float32)
        for step in (1, 2, 3):
            piece = jnp.where(lax.rem(source + step, 4) == rank, landed[step - 1], piece)
        gate_grad = gate_grad + jnp.where(rank == source, gate_part[...], piece)
    target_total[...] = gate_grad[2:3]
    gate_grad = gate_grad[0:2]
    weighted = gates[...] * gate_grad
    chosen = gates[...] * (gate_grad - (weighted[0:1] + weighted[1:2]))
    experts, tokens = logit_grad.shape
    row = lax.broadcasted_iota(jnp.int32, (experts, tokens), 0)
    placed = jnp.where(row == routes[0:1], chosen[0:1], 0.0) + jnp.where(
        row == routes[1:2], chosen[1:2], 0.0
    )
    logit_grad[...] = placed.astype(jnp.bfloat16)

    @pl.when(inner)
    def _():
        grad_one[...] = lax.dot_general(
            logit_grad[...],
            router_low[...],
            (((0,), (1,)), ((), ())),
            preferred_element_type=jnp.float32,
        )


def finish_expert_grad(total, span, rank, extras, aux, scratch):
    stream_one, gain, grad_two, gate_part, gates, routes, router_low = extras
    grad_one, logit_grad, target_total, gain_grad = aux
    part, gain_part = norm_back_rows(
        stream_one[span], gain[...], total + grad_one[span]
    )
    result = grad_two[span] + part
    grad_one[span] = result
    gain_grad[...] += gain_part
    return result.astype(jnp.bfloat16)


def form_joint_grad(rank, extras, aux, scratch):
    query_grad, pair_grad, before_grad, joint_weights = extras[5:]
    joint_grad = aux[0]
    landed, pair_sem, part = scratch[2:]
    hidden = query_grad.shape[0]
    later = lax.axis_index("ctx") > 0
    copy = pltpu.make_async_remote_copy(
        src_ref=before_grad,
        dst_ref=landed,
        send_sem=pair_sem.at[0],
        recv_sem=pair_sem.at[1],
        device_id={"ctx": 1 - lax.axis_index("ctx")},
        device_id_type=MESH_ID,
    )
    joint_grad[0:hidden, :] = query_grad[...]

    @pl.when(later)
    def _():
        copy.start()
        joint_grad[hidden:, :] = pair_grad[...].astype(jnp.bfloat16)

    @pl.when(jnp.logical_not(later))
    def _():
        copy.wait_recv()
        both = pair_grad[...] + landed[...].astype(jnp.float32)
        joint_grad[hidden:, :] = both.astype(jnp.bfloat16)

    part[...] = lax.dot_general(
        joint_grad[...], joint_weights[...], (((0,), (0,)), ((), ())), preferred_element_type=jnp.float32
    )

    @pl.when(later)
    def _():
        copy.wait_send()


def finish_input_grad(scale, total, span, rank, extras, aux, scratch):
    embedded, gain, grad_one = extras[:3]
    stream_zero = embedded[span].astype(jnp.float32) * scale
    part, gain_part = norm_back_rows(stream_zero, gain[...], total)
    aux[-1][0:1, :] += gain_part
    return ((grad_one[span] + part) * scale).astype(jnp.bfloat16)


def middle_kernel(
    attended_ref, embedded_ref, gain_ref, router_ref, routes_ref, *refs
):
    rolled, (stream_ref, normed_ref, rows_ref, columns_ref, project_ref) = refs[:4], refs[4:]

    @pl.when(pl.program_id(0) == 0)
    def _():
        for step in range(4):
            lines = rolled[step].shape[0]
            owner = lax.rem(lax.axis_index("tensor") + 4 - step, 4)
            project_ref[pl.ds(pl.multiple_of(owner * lines, lines), lines)] = rolled[step][...]

    scale = math.sqrt(embedded_ref.shape[1])
    stream = embedded_ref[...].astype(jnp.float32) * scale + lax.dot_general(
        attended_ref[...], project_ref[...], (((0,), (0,)), ((), ())), preferred_element_type=jnp.float32
    )
    stream_ref[...] = stream
    normed = (stream * inverse_rms(stream) * gain_ref[...]).astype(jnp.bfloat16)
    normed_ref[...] = normed
    scores = lax.dot_general(
        router_ref[...], normed, (((1,), (1,)), ((), ())), preferred_element_type=jnp.float32
    )
    expert = lax.broadcasted_iota(jnp.int32, scores.shape, 0)
    first, second = (
        jnp.sum(jnp.where(expert == routes_ref[k : k + 1, :], scores, 0.0), 0, keepdims=True)
        for k in range(2)
    )
    top = jnp.maximum(first, second)
    first, second = jnp.exp(first - top), jnp.exp(second - top)
    total = first + second
    gates = jnp.concatenate([first / total, second / total], 0)
    rows_ref[...] = gates
    columns_ref[...] = jnp.concatenate([gates, jnp.zeros((6, gates.shape[1]), jnp.float32)], 0).T


def middle(attended, rolled, embedded, gain, router, routes):
    tokens, width = embedded.shape
    tile = 256
    fixed = lambda k: (0, 0)
    whole = lambda x: pl.BlockSpec(x.shape, fixed)
    down = lambda n: pl.BlockSpec((tile, n), lambda k: (k, 0))
    along = lambda n: pl.BlockSpec((n, tile), lambda k: (0, k))
    return pl.pallas_call(
        middle_kernel,
        grid=(tokens // tile,),
        out_shape=[
            jax.ShapeDtypeStruct((tokens, width), jnp.float32),
            jax.ShapeDtypeStruct((tokens, width), jnp.bfloat16),
            jax.ShapeDtypeStruct((2, tokens), jnp.float32),
            jax.ShapeDtypeStruct((tokens, 8), jnp.float32),
        ],
        in_specs=[along(width), down(width), whole(gain), whole(router), along(2)]
        + [whole(x) for x in rolled],
        out_specs=[down(width), down(width), along(2), down(8)],
        scratch_shapes=[pltpu.VMEM((width, width), jnp.bfloat16)],
        compiler_params=pltpu.CompilerParams(vmem_limit_bytes=40 << 20),
    )(attended, embedded, gain, router, routes, *rolled)


def embed_kernel(
    chunks, first_unit, slots_ref, mine_ref, rows_ref, gain_ref, units_ref, embedded_ref, normed_ref, joint_ref,
    joint_weights, project_weights, *refs
):
    held, total, stage, from_end, from_mid, units, store_sem = refs[:7]
    send_x, recv_x, send_y, recv_y, send_z, recv_z, send_core, recv_core = refs[7:15]
    send_sem, end_sem, mid_sem, back_sem, back_recv = refs[15:]
    chip, core = lax.axis_index("dp"), lax.axis_index("ctx")
    beside = chip + 1 - 2 * lax.rem(chip, 2)
    across = lax.rem(chip + 2, 4)
    opposite = across + 1 - 2 * lax.rem(across, 2)
    places = (chip, beside, across, opposite)
    rank = lax.axis_index("tensor")
    inner = (rank == 1) | (rank == 2)
    end_peer = jnp.where(rank < 2, 1 - rank, 5 - rank)
    mid_peer = 3 - rank
    slots, unit_rows = mine_ref.shape[:2]
    width = total.shape[2]
    size = slots // chunks
    split = (chunks + 1) // 2
    tokens = rows_ref.shape[0]
    count, rows = stage.shape[1:3]

    def repeat(first, last, body):
        def step(i, carry):
            body(i)
            return carry

        lax.fori_loop(first, last, step, 0)

    def columns(h):
        return slice(h * width, (h + 1) * width)

    own = (chip * 2 + core) * slots
    for h in range(2):
        held[h, pl.ds(own, slots)] = mine_ref[:, :, columns(h)].astype(jnp.bfloat16)
    barrier = pltpu.get_barrier_semaphore()
    for place in ({"ctx": 1 - core}, {"dp": beside}, {"dp": across}, {"tensor": end_peer}):
        pl.semaphore_signal(barrier, inc=1, device_id=place, device_id_type=MESH_ID)

    @pl.when(inner)
    def _():
        pl.semaphore_signal(barrier, inc=1, device_id={"tensor": mid_peer}, device_id_type=MESH_ID)
        pl.semaphore_wait(barrier, 5)

    @pl.when(jnp.logical_not(inner))
    def _():
        pl.semaphore_wait(barrier, 4)

    def remote(source, target, send, recv, place):
        return pltpu.make_async_remote_copy(
            src_ref=source,
            dst_ref=target,
            send_sem=send,
            recv_sem=recv,
            device_id=place,
            device_id_type=MESH_ID,
        )

    def copy(h, place, q, send, recv, target):
        piece = held.at[h, pl.ds((place * 2 + core) * slots + q * size, size)]
        return remote(piece, piece, send, recv, target)

    def to_beside(h, q):
        return copy(h, chip, q, send_x.at[h, q], recv_x.at[h, q], {"dp": beside})

    def to_across(h, q):
        return copy(h, chip, q, send_y.at[h, q], recv_y.at[h, q], {"dp": across})

    def passed_on(h, q, source, target):
        return copy(h, source, q, send_z.at[h, q], recv_z.at[h, q], {"dp": target})

    def to_core(h, k, q):
        return copy(h, places[k], q, send_core.at[h, k, q], recv_core.at[h, k, q], {"ctx": 1 - core})

    def start(h):
        def both(i):
            to_beside(h, i).start()
            to_across(h, lax.rem(i + split, chunks)).start()

        repeat(0, chunks, both)
        repeat(0, chunks, lambda q: to_core(h, 0, q).start())

    def look(h, place, which):
        begin = (place * 2 + which) * slots
        lines = slots * unit_rows
        column = lax.broadcasted_iota(jnp.int32, (tokens, lines), 1) + begin * unit_rows
        hit = jnp.where(column == rows_ref[...], 1.0, 0.0).astype(jnp.bfloat16)
        block = held[h, pl.ds(begin, slots)].reshape(lines, width)
        total[h] += jnp.dot(hit, block, preferred_element_type=jnp.float32)

    def relay(h, i):
        to_beside(h, i).wait_recv()

        @pl.when(i < split)
        def _():
            passed_on(h, i, beside, across).start()

        to_core(h, 1, i).start()
        j = lax.rem(i + split, chunks)
        to_across(h, j).wait_recv()

        @pl.when(j >= split)
        def _():
            passed_on(h, j, across, beside).start()

        to_core(h, 2, j).start()

    def rest(h):
        repeat(0, chunks, lambda q: to_core(h, 0, q).wait_recv())
        look(h, chip, 1 - core)
        look(h, beside, core)
        look(h, across, core)

        def last(q):
            passed_on(h, q, opposite, opposite).wait_recv()
            to_core(h, 3, q).start()
            to_core(h, 1, q).wait_recv()
            to_core(h, 2, q).wait_recv()

        repeat(0, chunks, last)
        look(h, beside, 1 - core)
        look(h, across, 1 - core)
        look(h, opposite, core)
        repeat(0, chunks, lambda q: to_core(h, 3, q).wait_recv())
        look(h, opposite, 1 - core)

    def span(i):
        return pl.ds(pl.multiple_of(i * rows, rows), rows)

    def to_inner(h, i):
        return remote(
            stage.at[h, i], from_end.at[h, i], send_sem.at[h, i], end_sem.at[h, i], {"tensor": end_peer}
        )

    def to_middle(h, i):
        return remote(
            stage.at[h, i], from_mid.at[h, i], send_sem.at[h, i], mid_sem.at[h, i], {"tensor": mid_peer}
        )

    def to_end(h, i):
        piece = embedded_ref.at[span(i), columns(h)]
        return remote(piece, piece, back_sem.at[h, i], back_recv.at[h, i], {"tensor": end_peer})

    def push(h):
        @pl.when(jnp.logical_not(inner))
        def _():
            def one(i):
                stage[h, i] = total[h, span(i)].astype(jnp.bfloat16)
                to_inner(h, i).start()

            repeat(0, count, one)

    def exchange(h, i):
        @pl.when(inner & (i < count))
        def _():
            to_inner(h, i).wait_recv()
            stage[h, i] = (total[h, span(i)] + from_end[h, i].astype(jnp.float32)).astype(jnp.bfloat16)
            to_middle(h, i).start()

        @pl.when(inner & (i >= line_lag))
        def _():
            j = i - line_lag
            to_middle(h, j).wait_recv()
            both = stage[h, j].astype(jnp.float32) + from_mid[h, j].astype(jnp.float32)
            embedded_ref[span(j), columns(h)] = both.astype(jnp.bfloat16)
            to_end(h, j).start()

    total[...] = jnp.zeros_like(total)
    start(0)
    look(0, chip, core)
    repeat(0, chunks, lambda i: relay(0, i))
    start(1)
    rest(0)
    push(0)
    look(1, chip, core)

    def between(i):
        exchange(0, i)

        @pl.when(i < chunks)
        def _():
            relay(1, i)

    repeat(0, count + line_lag, between)
    rest(1)
    push(1)

    def place_unit(u):
        for h in range(2):
            units[u, :, columns(h)] = held[h, slots_ref[u]]

    turns = count + line_lag
    share = -(-units.shape[0] // turns)

    def exchange_and_place(i):
        exchange(1, i)
        repeat(i * share, jnp.minimum((i + 1) * share, units.shape[0]), place_unit)

    repeat(0, turns, exchange_and_place)
    store = pltpu.make_async_copy(units, units_ref, store_sem)
    store.start()

    def finish(q):
        for h in range(2):
            to_beside(h, q).wait_send()
            to_across(h, q).wait_send()
            for k in range(4):
                to_core(h, k, q).wait_send()
            passed_on(h, q, opposite, opposite).wait_send()

    repeat(0, chunks, finish)

    @pl.when(inner)
    def _():
        def drain(i):
            for h in range(2):
                to_middle(h, i).wait_send()
                to_end(h, i).wait_send()

        repeat(0, count, drain)

    @pl.when(jnp.logical_not(inner))
    def _():
        def drain(i):
            for h in range(2):
                to_end(h, i).wait_recv()
                to_inner(h, i).wait_send()

        repeat(0, count, drain)

    stream = embedded_ref[...].astype(jnp.float32) * math.sqrt(2 * width)
    normed = (stream * inverse_rms(stream) * gain_ref[...]).astype(jnp.bfloat16)
    normed_ref[...] = normed
    lines = joint_ref.shape[0]
    weights = units[first_unit : first_unit + lines // unit_rows].reshape(lines, 2 * width)
    joint_weights[...] = weights
    project_weights[...] = units[first_unit + lines // unit_rows :].reshape(
        project_weights.shape
    )
    joint_ref[...] = lax.dot_general(
        weights, normed, (((1,), (1,)), ((), ())), preferred_element_type=jnp.float32
    ).astype(jnp.bfloat16)
    store.wait()


def embed(unit_slots, mine, slot_rows, gain, first_unit, lines, collective_id):
    slots, unit_rows, width = mine.shape
    tokens = slot_rows.shape[0]
    chunks = max(k for k in range(1, 8) if slots % k == 0)
    rows = 128
    half = width // 2
    sems = pltpu.SemaphoreType.DMA((2, chunks))
    line = pltpu.VMEM((2, tokens // rows, rows, half), jnp.bfloat16)
    return pl.pallas_call(
        functools.partial(embed_kernel, chunks, first_unit),
        out_shape=[
            jax.ShapeDtypeStruct((unit_slots.shape[0], unit_rows, width), jnp.bfloat16),
            jax.ShapeDtypeStruct((tokens, width), jnp.bfloat16),
            jax.ShapeDtypeStruct((tokens, width), jnp.bfloat16),
            jax.ShapeDtypeStruct((lines, tokens), jnp.bfloat16),
            jax.ShapeDtypeStruct((lines, width), jnp.bfloat16),
            jax.ShapeDtypeStruct((lines // 3, width), jnp.bfloat16),
        ],
        in_specs=[pl.BlockSpec(memory_space=pltpu.SMEM)] + [whole_vmem] * 3,
        out_specs=[whole_any] + [whole_vmem] * 5,
        scratch_shapes=[
            pltpu.VMEM((2, 8 * slots, unit_rows, half), jnp.bfloat16),
            pltpu.VMEM((2, tokens, half), jnp.float32),
            line,
            line,
            line,
            pltpu.VMEM((unit_slots.shape[0], unit_rows, width), jnp.bfloat16),
            pltpu.SemaphoreType.DMA,
        ]
        + [sems] * 6
        + [pltpu.SemaphoreType.DMA((2, 4, chunks))] * 2
        + [pltpu.SemaphoreType.DMA((2, tokens // rows))] * 5,
        compiler_params=pltpu.CompilerParams(
            collective_id=collective_id, has_side_effects=True, vmem_limit_bytes=60 << 20
        ),
    )(unit_slots, mine, slot_rows, gain)


def pull_units_kernel(parts, slots_ref, *refs):
    sources, out_ref, sem = refs[:parts], refs[parts], refs[parts + 1]
    width = out_ref.shape[-1] // parts

    def push(u, carry):
        for part in range(parts):
            pltpu.make_async_copy(
                sources[part].at[slots_ref[u]],
                out_ref.at[u, :, part * width : (part + 1) * width],
                sem,
            ).start()
        return carry

    lax.fori_loop(0, out_ref.shape[0], push, 0)
    pltpu.make_async_copy(out_ref, out_ref, sem).wait()


def pull_units(sources, slots):
    count = slots.shape[0]
    rows, width = sources[0].shape[1:]
    return pl.pallas_call(
        functools.partial(pull_units_kernel, len(sources)),
        out_shape=jax.ShapeDtypeStruct((count, rows, width * len(sources)), sources[0].dtype),
        in_specs=[pl.BlockSpec(memory_space=pltpu.SMEM)] + [whole_any] * len(sources),
        out_specs=whole_vmem,
        scratch_shapes=[pltpu.SemaphoreType.DMA],
        compiler_params=pltpu.CompilerParams(vmem_limit_bytes=40 << 20),
    )(slots, *sources)


def attention_kernel(
    heads, size, bias_ref, own_ref, out_ref, logsum_ref, before_ref, mine_ref,
    queries, own_values, old_values, scores, peak, total, keys_sem, send_sem, recv_sem,
):
    tokens = own_ref.shape[1]
    blocks = tokens // BLOCK
    hidden = heads * size
    later = lax.axis_index("ctx") > 0
    rank = lax.axis_index("tensor")
    inner = (rank == 1) | (rank == 2)
    end_peer = jnp.where(rank < 2, 1 - rank, 5 - rank)
    mid_peer = 3 - rank
    mid_owner = jnp.where(inner, mid_peer, 3 - end_peer)
    far_owner = jnp.where(inner, 3 - end_peer, 3 - rank)
    other_core = {"ctx": 1 - lax.axis_index("ctx")}
    barrier = pltpu.get_barrier_semaphore()
    for place in (other_core, {"tensor": end_peer}):
        pl.semaphore_signal(barrier, inc=1, device_id=place, device_id_type=MESH_ID)

    @pl.when(inner)
    def _():
        pl.semaphore_signal(barrier, inc=1, device_id={"tensor": mid_peer}, device_id_type=MESH_ID)
        pl.semaphore_wait(barrier, 3)

    @pl.when(jnp.logical_not(inner))
    def _():
        pl.semaphore_wait(barrier, 2)

    pairs = pltpu.make_async_remote_copy(
        src_ref=own_ref.at[pl.ds(hidden, 2 * hidden)],
        dst_ref=before_ref,
        send_sem=keys_sem.at[0],
        recv_sem=keys_sem.at[1],
        device_id=other_core,
        device_id_type=MESH_ID,
    )

    @pl.when(jnp.logical_not(later))
    def _():
        pairs.start()
        before_ref[...] = jnp.zeros_like(before_ref)

    def flipped(rows):
        return rows.astype(jnp.float32).T.astype(jnp.bfloat16)

    for head in range(heads):
        span = slice(head * size, (head + 1) * size)
        queries[head] = flipped(own_ref[span, :]) * jnp.bfloat16(size**-0.5)
        own_values[head] = flipped(
            own_ref[2 * hidden + head * size : 2 * hidden + (head + 1) * size, :]
        )

    @pl.when(later)
    def _():
        pairs.wait_recv()
        for head in range(heads):
            old_values[head] = flipped(
                before_ref[hidden + head * size : hidden + (head + 1) * size, :]
            )

    def sent(owner, block, peer, send, recv):
        piece = out_ref.at[owner, :, pl.ds(block * BLOCK, BLOCK)]
        return pltpu.make_async_remote_copy(
            src_ref=piece,
            dst_ref=piece,
            send_sem=send_sem.at[block, send],
            recv_sem=recv_sem.at[block, recv],
            device_id={"tensor": peer},
            device_id_type=MESH_ID,
        )

    def own_to_end(block):
        return sent(rank, block, end_peer, 0, 0)

    def from_end(block):
        return sent(end_peer, block, end_peer, 0, 0)

    def own_to_middle(block):
        return sent(rank, block, mid_peer, 1, 1)

    def end_to_middle(block):
        return sent(end_peer, block, mid_peer, 2, 2)

    def middle_to_end(block):
        return sent(mid_owner, block, end_peer, 3, 1)

    def far_to_end(block):
        return sent(far_owner, block, end_peer, 4, 2)

    def hand_on(block, stages):
        @pl.when(inner)
        def _():
            if 0 in stages:
                from_end(block).wait_recv()
                end_to_middle(block).start()
                middle_to_end(block).wait_recv()
                middle_to_end(block).start()
            if 1 in stages:
                far_to_end(block).wait_recv()
                far_to_end(block).start()

    for block in range(blocks):
        for head in range(heads):
            span = slice(head * size, (head + 1) * size)
            rows = queries[head, block * BLOCK : (block + 1) * BLOCK]
            own_keys = own_ref[hidden + head * size : hidden + (head + 1) * size, :]
            width = (block + 1) * BLOCK
            mine = jnp.dot(rows, own_keys[:, :width], preferred_element_type=jnp.float32)
            top = None
            parts = []
            for k in range(block + 1):
                part = mine[:, k * BLOCK : (k + 1) * BLOCK] + bias_ref[head, block - k]
                parts.append(part)
                high = jnp.max(part, 1, keepdims=True)
                top = high if top is None else jnp.maximum(top, high)
            peak[...] = top

            @pl.when(later)
            def _():
                old = jnp.dot(rows, before_ref[span, :], preferred_element_type=jnp.float32)
                top_old = None
                for k in range(blocks):
                    part = old[:, k * BLOCK : (k + 1) * BLOCK] + bias_ref[head, block + blocks - k]
                    scores[:, k * BLOCK : (k + 1) * BLOCK] = part
                    high = jnp.max(part, 1, keepdims=True)
                    top_old = high if top_old is None else jnp.maximum(top_old, high)
                peak[...] = jnp.maximum(peak[...], top_old)

            top = peak[...]
            parts = [jnp.exp(part - top) for part in parts]
            own_sum = None
            for part in parts:
                part_sum = jnp.sum(part, 1, keepdims=True)
                own_sum = part_sum if own_sum is None else own_sum + part_sum
            total[...] = own_sum

            @pl.when(later)
            def _():
                old_exp = jnp.exp(scores[...] - top)
                scores[...] = old_exp
                total[...] += jnp.sum(old_exp, 1, keepdims=True)

            full = total[...]
            inverse = 1.0 / full
            low = jnp.concatenate([(part * inverse).astype(jnp.bfloat16) for part in parts], 1)
            result = jnp.dot(low, own_values[head, :width], preferred_element_type=jnp.float32)
            logsum_ref[head, block * BLOCK : (block + 1) * BLOCK, :] = top + jnp.log(full)
            place = (rank, span, slice(block * BLOCK, (block + 1) * BLOCK))

            @pl.when(later)
            def _():
                low_old = (scores[...] * inverse).astype(jnp.bfloat16)
                both = result + jnp.dot(low_old, old_values[head], preferred_element_type=jnp.float32)
                out_ref[place] = both.T.astype(jnp.bfloat16)
                mine_ref[place[1:]] = both.T.astype(jnp.bfloat16)

            @pl.when(jnp.logical_not(later))
            def _():
                out_ref[place] = result.T.astype(jnp.bfloat16)
                mine_ref[place[1:]] = result.T.astype(jnp.bfloat16)

        own_to_end(block).start()

        @pl.when(inner)
        def _():
            own_to_middle(block).start()

        if block >= 1:
            hand_on(block - 1, (0,))
        if block >= 2:
            hand_on(block - 2, (1,))

    hand_on(blocks - 1, (0,))
    hand_on(blocks - 2, (1,))
    hand_on(blocks - 1, (1,))
    for block in range(blocks):
        own_to_end(block).wait_send()

        @pl.when(inner)
        def _():
            for copy in (own_to_middle, end_to_middle, middle_to_end, far_to_end):
                copy(block).wait_send()

        @pl.when(jnp.logical_not(inner))
        def _():
            from_end(block).wait_recv()
            middle_to_end(block).wait_recv()
            far_to_end(block).wait_recv()

    @pl.when(jnp.logical_not(later))
    def _():
        pairs.wait_send()


def attention(biases, own, heads, size, collective_id):
    tokens = own.shape[1]
    blocks = tokens // BLOCK
    flat = pltpu.VMEM((heads, tokens, size), jnp.bfloat16)
    return pl.pallas_call(
        functools.partial(attention_kernel, heads, size),
        out_shape=[
            jax.ShapeDtypeStruct((4, heads * size, tokens), jnp.bfloat16),
            jax.ShapeDtypeStruct((heads, tokens, 1), jnp.float32),
            jax.ShapeDtypeStruct((2 * heads * size, tokens), jnp.bfloat16),
            jax.ShapeDtypeStruct((heads * size, tokens), jnp.bfloat16),
        ],
        in_specs=[pl.BlockSpec(memory_space=pltpu.SMEM), whole_vmem],
        out_specs=[whole_vmem] * 4,
        scratch_shapes=[
            flat,
            flat,
            flat,
            pltpu.VMEM((BLOCK, tokens), jnp.float32),
            pltpu.VMEM((BLOCK, 1), jnp.float32),
            pltpu.VMEM((BLOCK, 1), jnp.float32),
            pltpu.SemaphoreType.DMA((2,)),
            pltpu.SemaphoreType.DMA((blocks, 5)),
            pltpu.SemaphoreType.DMA((blocks, 3)),
        ],
        compiler_params=pltpu.CompilerParams(
            collective_id=collective_id, has_side_effects=True, vmem_limit_bytes=40 << 20
        ),
    )(biases, own)


def attention_back_kernel(
    heads, size, bias_ref, own_ref, before_ref, logsum_ref, grad_ref, project_ref,
    *refs
):
    states, (query_out, own_out, before_out, bias_out) = refs[:8], refs[8:12]
    updated, (probs, slopes, inner, query_sum, own_sum, before_sum) = refs[12:18], refs[18:24]
    held, load_sem, store_sem = refs[24:]
    loads = [pltpu.make_async_copy(states[k], held.at[k], load_sem.at[k]) for k in range(8)]
    stores = [
        pltpu.make_async_copy(held.at[4 * (k // 3) + k % 3], updated[k], store_sem.at[k])
        for k in range(6)
    ]
    for load in loads:
        load.start()

    def update(i, carry):
        lines = held.shape[1] // 16
        span = pl.ds(pl.multiple_of(i * lines, lines), lines)
        for k, rate in enumerate((rate_inner, rate_outer)):
            fresh = adam_update(*(held[4 * k + n, span] for n in range(4)), rate, decay_rate)
            for n in range(3):
                held[4 * k + n, span] = fresh[n]
        return carry

    tokens = own_ref.shape[1]
    blocks = tokens // BLOCK
    hidden = heads * size
    later = lax.axis_index("ctx") > 0
    bias_out[...] = jnp.zeros_like(bias_out)

    def flipped(rows):
        return rows.astype(jnp.float32).T.astype(jnp.bfloat16)

    for head in range(heads):
        span = slice(head * size, (head + 1) * size)
        value_span = slice(hidden + head * size, hidden + (head + 1) * size)
        query_rows = own_ref[span, :]
        query = flipped(query_rows) * jnp.bfloat16(size**-0.5)
        own_keys = own_ref[hidden + head * size : hidden + (head + 1) * size, :]
        own_values = own_ref[2 * hidden + head * size : 2 * hidden + (head + 1) * size, :]
        old_keys = before_ref[span, :]
        old_values = before_ref[value_span, :]
        own_keys_flip = flipped(own_keys)
        grad = lax.dot_general(
            grad_ref[...], project_ref[span, :], (((1,), (1,)), ((), ())), preferred_element_type=jnp.float32
        )
        grad_rows = grad.T.astype(jnp.bfloat16)
        grad = grad.astype(jnp.bfloat16)
        own_sum[...] = jnp.zeros_like(own_sum)

        @pl.when(later)
        def _():
            before_sum[...] = jnp.zeros_like(before_sum)

        for block in range(blocks):
            at = slice(block * BLOCK, (block + 1) * BLOCK)
            width = (block + 1) * BLOCK
            rows, up = query[at], grad[at]
            lse = logsum_ref[head, at, :]
            score = jnp.dot(rows, own_keys[:, :width], preferred_element_type=jnp.float32)
            prob = jnp.concatenate(
                [
                    jnp.exp(score[:, k * BLOCK : (k + 1) * BLOCK] + (bias_ref[head, block - k] - lse))
                    for k in range(block + 1)
                ],
                1,
            )
            slope = jnp.dot(up, own_values[:, :width], preferred_element_type=jnp.float32)
            inner[...] = jnp.sum(prob * slope, 1, keepdims=True)

            @pl.when(later)
            def _():
                score = jnp.dot(rows, old_keys, preferred_element_type=jnp.float32)
                old_slope = jnp.dot(up, old_values, preferred_element_type=jnp.float32)
                old_prob = jnp.concatenate(
                    [
                        jnp.exp(
                            score[:, k * BLOCK : (k + 1) * BLOCK]
                            + (bias_ref[head, block + blocks - k] - lse)
                        )
                        for k in range(blocks)
                    ],
                    1,
                )
                probs[...] = old_prob
                slopes[...] = old_slope
                inner[...] += jnp.sum(old_prob * old_slope, 1, keepdims=True)

            row_inner = inner[...]
            low_grad = (prob * (slope - row_inner)).astype(jnp.bfloat16)
            query_sum[...] = jnp.dot(
                low_grad, own_keys_flip[:width], preferred_element_type=jnp.float32
            )
            own_sum[:size, :width] += jnp.dot(
                query_rows[:, at], low_grad, preferred_element_type=jnp.float32
            )
            own_sum[size:, :width] += jnp.dot(
                grad_rows[:, at], prob.astype(jnp.bfloat16), preferred_element_type=jnp.float32
            )
            for k in range(block + 1):
                line = head * 2 * blocks + block - k
                bias_out[line : line + 1, :] += jnp.sum(
                    low_grad[:, k * BLOCK : (k + 1) * BLOCK].astype(jnp.float32), 0, keepdims=True
                )

            @pl.when(later)
            def _():
                old_prob = probs[...]
                low_old = (old_prob * (slopes[...] - row_inner)).astype(jnp.bfloat16)
                query_sum[...] += jnp.dot(
                    low_old, flipped(old_keys), preferred_element_type=jnp.float32
                )
                before_sum[:size, :] += jnp.dot(
                    query_rows[:, at], low_old, preferred_element_type=jnp.float32
                )
                before_sum[size:, :] += jnp.dot(
                    grad_rows[:, at], old_prob.astype(jnp.bfloat16), preferred_element_type=jnp.float32
                )
                for k in range(blocks):
                    line = head * 2 * blocks + block + blocks - k
                    bias_out[line : line + 1, :] += jnp.sum(
                        low_old[:, k * BLOCK : (k + 1) * BLOCK].astype(jnp.float32), 0, keepdims=True
                    )

            query_out[span, at] = (query_sum[...].T * size**-0.5).astype(jnp.bfloat16)

        own_out[span, :] = own_sum[:size, :] * size**-0.5
        own_out[value_span, :] = own_sum[size:, :]

        @pl.when(later)
        def _():
            before_out[span, :] = (before_sum[:size, :] * size**-0.5).astype(jnp.bfloat16)
            before_out[value_span, :] = before_sum[size:, :].astype(jnp.bfloat16)

        if head == 0:
            for load in loads:
                load.wait()
            lax.fori_loop(0, 16, update, 0)
            for store in stores:
                store.start()

    @pl.when(jnp.logical_not(later))
    def _():
        before_out[...] = jnp.zeros_like(before_out)

    for store in stores:
        store.wait()


def attention_back(biases, own, before, logsum, grad, project, states, heads, size):
    tokens = own.shape[1]
    hidden = heads * size
    return pl.pallas_call(
        functools.partial(attention_back_kernel, heads, size),
        out_shape=[
            jax.ShapeDtypeStruct((hidden, tokens), jnp.bfloat16),
            jax.ShapeDtypeStruct((2 * hidden, tokens), jnp.float32),
            jax.ShapeDtypeStruct((2 * hidden, tokens), jnp.bfloat16),
            jax.ShapeDtypeStruct((heads * 2 * (tokens // BLOCK), BLOCK), jnp.float32),
        ]
        + [jax.ShapeDtypeStruct(states[0].shape, jnp.float32)] * 6,
        in_specs=[pl.BlockSpec(memory_space=pltpu.SMEM)] + [whole_vmem] * 5 + [whole_any] * 8,
        out_specs=[whole_vmem] * 4 + [whole_any] * 6,
        scratch_shapes=[
            pltpu.VMEM((BLOCK, tokens), jnp.float32),
            pltpu.VMEM((BLOCK, tokens), jnp.float32),
            pltpu.VMEM((BLOCK, 1), jnp.float32),
            pltpu.VMEM((BLOCK, size), jnp.float32),
            pltpu.VMEM((2 * size, tokens), jnp.float32),
            pltpu.VMEM((2 * size, tokens), jnp.float32),
            pltpu.VMEM((8,) + states[0].shape, jnp.float32),
            pltpu.SemaphoreType.DMA((8,)),
            pltpu.SemaphoreType.DMA((6,)),
        ],
        compiler_params=pltpu.CompilerParams(vmem_limit_bytes=48 << 20),
    )(biases, own, before, logsum, grad, project, *states)


def vocab_tile(vocab):
    return max(k for k in range(16, 1601, 16) if vocab % k == 0)


def head_line_kernel(
    tile, part_ref, stream_ref, gain_ref, table_ref, wanted_ref, weight_ref,
    low_ref, grad_low_ref, grad_ref, gain_grad, logsum_ref, picked_ref, slopes_ref,
    logits, table, stage, from_end, from_mid, own, turned, stats, landed, slope_tiles, total,
    load_sem, send_sem, end_sem, mid_sem, back_sem, back_recv, stat_send, stat_recv, store_sem,
):
    rank = lax.axis_index("tensor")
    inner = (rank == 1) | (rank == 2)
    end_peer = jnp.where(rank < 2, 1 - rank, 5 - rank)
    mid_peer = 3 - rank
    count, rows = stage.shape[:2]
    columns = turned.shape[1]
    pieces = table.shape[0] // tile
    group = columns // rows
    tiles = count // group
    vocab = table.shape[0]
    load = pltpu.make_async_copy(table_ref.at[pl.ds(0, vocab)], table, load_sem)
    load.start()
    barrier = pltpu.get_barrier_semaphore()
    for step in (1, 2, 3):
        other = lax.rem(rank + step, 4)
        pl.semaphore_signal(barrier, inc=1, device_id={"tensor": other}, device_id_type=MESH_ID)
    pl.semaphore_wait(barrier, 3)

    def span(i):
        return pl.ds(pl.multiple_of(i * rows, rows), rows)

    def over(t):
        return pl.ds(pl.multiple_of(t * columns, columns), columns)

    def line_copy(source, target, send, recv, peer):
        return pltpu.make_async_remote_copy(
            src_ref=source,
            dst_ref=target,
            send_sem=send,
            recv_sem=recv,
            device_id={"tensor": peer},
            device_id_type=MESH_ID,
        )

    def to_inner(i):
        return line_copy(stage.at[i], from_end.at[i], send_sem.at[i], end_sem.at[i], end_peer)

    def to_middle(i):
        return line_copy(stage.at[i], from_mid.at[i], send_sem.at[i], mid_sem.at[i], mid_peer)

    def to_end(ref, i):
        rows_of = ref.at[span(i)]
        return line_copy(rows_of, rows_of, back_sem.at[i], back_recv.at[i], end_peer)

    def repeat(first, last, body):
        def step(i, carry):
            body(i)
            return carry

        lax.fori_loop(first, last, step, 0)

    def turn(t):
        turned[...] = low_ref[over(t)].astype(jnp.float32).T.astype(jnp.bfloat16)

    def table_rows(k):
        return table[k * tile : (k + 1) * tile]

    def first_logits(t):
        turn(t)
        logits[0] = jnp.dot(table_rows(0), turned[...], preferred_element_type=jnp.float32)

    def next_logits(k):
        if k + 1 < pieces:
            logits[(k + 1) % 2] = jnp.dot(
                table_rows(k + 1), turned[...], preferred_element_type=jnp.float32
            )

    def sums_unit(t, k):
        next_logits(k)
        before = stats[0:1, over(t)]
        top = jnp.maximum(before, jnp.max(logits[k % 2], 0, keepdims=True))
        stats[1:2, over(t)] = stats[1:2, over(t)] * jnp.exp(before - top) + jnp.sum(
            jnp.exp(logits[k % 2] - top), 0, keepdims=True
        )
        stats[0:1, over(t)] = top

    def sums_tile(t):
        first_logits(t)
        for k in range(pieces):
            sums_unit(t, k)

    stats[0:1, :] = jnp.full_like(stats[0:1, :], masked_score)
    stats[1:2, :] = jnp.zeros_like(stats[1:2, :])

    @pl.when(jnp.logical_not(inner))
    def _():
        def push(i):
            stage[i] = part_ref[span(i)].astype(jnp.bfloat16)
            to_inner(i).start()

        repeat(0, count, push)
        load.wait()

        def forward(t):
            repeat(0, group, lambda c: to_end(low_ref, t * group + c).wait_recv())
            sums_tile(t)

        repeat(0, tiles, forward)
        repeat(0, count, lambda i: to_inner(i).wait_send())

    @pl.when(inner)
    def _():
        gain_grad[...] = jnp.zeros_like(gain_grad)
        load.wait()

        def gather(i):
            to_inner(i).wait_recv()
            mine = part_ref[span(i)] + from_end[i].astype(jnp.float32)
            stage[i] = mine.astype(jnp.bfloat16)
            to_middle(i).start()

        def settle_rows(j):
            to_middle(j).wait_recv()
            stream_two = stream_ref[span(j)] + (
                stage[j].astype(jnp.float32) + from_mid[j].astype(jnp.float32)
            )
            grad_ref[span(j)] = stream_two
            low_ref[span(j)] = (stream_two * inverse_rms(stream_two) * gain_ref[...]).astype(
                jnp.bfloat16
            )
            to_end(low_ref, j).start()

        turns = [[k for k in range(pieces) if k * (group - 1) // pieces == c - 1] for c in range(group)]

        def advance(t):
            for c in range(group):
                i = t * group + c
                gather(i)

                @pl.when(i >= line_lag)
                def _():
                    settle_rows(i - line_lag)

                if turns[c]:

                    @pl.when(t >= 1)
                    def _():
                        if c == 1:
                            first_logits(t - 1)
                        for k in turns[c]:
                            sums_unit(t - 1, k)

        repeat(0, tiles, advance)
        repeat(count - line_lag, count, settle_rows)
        sums_tile(tiles - 1)

        def drain(i):
            to_middle(i).wait_send()
            to_end(low_ref, i).wait_send()

        repeat(0, count, drain)

    copies = [
        line_copy(
            stats, landed.at[step - 1], stat_send.at[step - 1], stat_recv.at[step - 1], lax.rem(rank + step, 4)
        )
        for step in (1, 2, 3)
    ]
    for copy in copies:
        copy.start()
    for copy in copies:
        copy.wait()
    tops, sums = [], []
    for source in range(4):
        piece = stats[...]
        for step in (1, 2, 3):
            piece = jnp.where(lax.rem(source + step, 4) == rank, landed[step - 1], piece)
        tops.append(piece[0:1])
        sums.append(piece[1:2])
    top = jnp.maximum(jnp.maximum(tops[0], tops[1]), jnp.maximum(tops[2], tops[3]))
    whole = sums[0] * jnp.exp(tops[0] - top)
    for source in (1, 2, 3):
        whole = whole + sums[source] * jnp.exp(tops[source] - top)
    logsum_ref[...] = top + jnp.log(whole)
    picked_ref[...] = jnp.zeros_like(picked_ref)

    def store(t):
        return pltpu.make_async_copy(
            slope_tiles.at[lax.rem(t, 2)], slopes_ref.at[:, over(t)], store_sem.at[lax.rem(t, 2)]
        )

    def slope_unit(t, k):
        values = logits[k % 2]
        row = lax.broadcasted_iota(jnp.int32, values.shape, 0)
        base = k * tile
        hits = jnp.where(row == wanted_ref[0:1, over(t)] - base, weight_ref[0:1, over(t)], 0.0)
        hits = hits + jnp.where(
            row == wanted_ref[1:2, over(t)] - base, weight_ref[1:2, over(t)], 0.0
        )
        picked_ref[:, over(t)] += jnp.sum(hits * values, 0, keepdims=True)
        softmax = jnp.exp(values - logsum_ref[:, over(t)])
        slope_tiles[lax.rem(t, 2), base : base + tile] = (
            (weight_ref[2:3, over(t)] * softmax - hits) * weight_ref[3:4, over(t)]
        ).astype(jnp.bfloat16)

    def add_rows(t, k):
        total[...] += lax.dot_general(
            slope_tiles[lax.rem(t, 2), k * tile : (k + 1) * tile],
            table_rows(k),
            (((0,), (0,)), ((), ())),
            preferred_element_type=jnp.float32,
        )

    def settle(j):
        to_middle(j).wait_recv()
        upstream = stage[j].astype(jnp.float32) + from_mid[j].astype(jnp.float32)
        grad_two, gain_part = norm_back_rows(grad_ref[span(j)], gain_ref[...], upstream)
        grad_ref[span(j)] = grad_two
        gain_grad[...] += gain_part
        grad_low_ref[span(j)] = grad_two.astype(jnp.bfloat16)
        to_end(grad_low_ref, j).start()

    def exchange(i):
        to_inner(i).wait_recv()
        stage[i] = (own[span(i)] + from_end[i].astype(jnp.float32)).astype(jnp.bfloat16)
        to_middle(i).start()

        @pl.when(i >= line_lag)
        def _():
            settle(i - line_lag)

    def back_tile(t):
        @pl.when(t >= 2)
        def _():
            store(t - 2).wait()

        total[...] = jnp.zeros_like(total)
        first_logits(t)
        for k in range(pieces):
            next_logits(k)
            slope_unit(t, k)
            if k >= 1:
                add_rows(t, k - 1)
            if k >= pieces - group:

                @pl.when(inner & (t >= 1))
                def _():
                    exchange((t - 1) * group + k - (pieces - group))

        add_rows(t, pieces - 1)
        store(t).start()

        @pl.when(inner)
        def _():
            own[over(t)] = total[...]

        @pl.when(jnp.logical_not(inner))
        def _():
            def push(c):
                stage[t * group + c] = total[span(c)].astype(jnp.bfloat16)
                to_inner(t * group + c).start()

            repeat(0, group, push)

    repeat(0, tiles, back_tile)

    @pl.when(jnp.logical_not(inner))
    def _():
        def finish(i):
            to_end(grad_low_ref, i).wait_recv()
            to_inner(i).wait_send()

        repeat(0, count, finish)

    @pl.when(inner)
    def _():
        repeat(count - group, count, exchange)
        repeat(count - line_lag, count, settle)

        def drain(i):
            to_middle(i).wait_send()
            to_end(grad_low_ref, i).wait_send()

        repeat(0, count, drain)

    store(tiles - 2).wait()
    store(tiles - 1).wait()


def head_line(part, stream, gain, weights, wanted, weight_rows, vocab, collective_id):
    tokens, width = part.shape
    rows, columns = 64, 256
    count = tokens // rows
    chunks = pltpu.VMEM((count, rows, width), jnp.bfloat16)
    rows_low = jax.ShapeDtypeStruct((tokens, width), jnp.bfloat16)
    along = jax.ShapeDtypeStruct((1, tokens), jnp.float32)
    line_sems = pltpu.SemaphoreType.DMA((count,))
    return pl.pallas_call(
        functools.partial(head_line_kernel, vocab_tile(vocab)),
        out_shape=[
            rows_low,
            rows_low,
            jax.ShapeDtypeStruct((tokens, width), jnp.float32),
            jax.ShapeDtypeStruct((1, width), jnp.float32),
            along,
            along,
            jax.ShapeDtypeStruct((vocab, tokens), jnp.bfloat16),
        ],
        in_specs=[whole_vmem] * 3 + [whole_any] + [whole_vmem] * 2,
        out_specs=[whole_vmem] * 6 + [whole_any],
        scratch_shapes=[
            pltpu.VMEM((2, vocab_tile(vocab), columns), jnp.float32),
            pltpu.VMEM((vocab, width), jnp.bfloat16),
            chunks,
            chunks,
            chunks,
            pltpu.VMEM((tokens, width), jnp.float32),
            pltpu.VMEM((width, columns), jnp.bfloat16),
            pltpu.VMEM((2, tokens), jnp.float32),
            pltpu.VMEM((3, 2, tokens), jnp.float32),
            pltpu.VMEM((2, vocab, columns), jnp.bfloat16),
            pltpu.VMEM((columns, width), jnp.float32),
            pltpu.SemaphoreType.DMA,
        ]
        + [line_sems] * 5
        + [pltpu.SemaphoreType.DMA((3,))] * 2
        + [pltpu.SemaphoreType.DMA((2,))],
        compiler_params=pltpu.CompilerParams(
            collective_id=collective_id, has_side_effects=True, vmem_limit_bytes=62 << 20
        ),
    )(part, stream, gain, weights, wanted, weight_rows)


def weight_grads_kernel(
    tile_units, tiles, place_ref, slope_ref, rows_ref, ids_ref, zero_ref, joint_ref, normed_ref,
    attended_ref, grad_ref, out_ref, made, sem,
):
    step = pl.program_id(0)
    unit_rows = out_ref.shape[1]
    buffer = lax.rem(step, 2)
    last_units = joint_ref.shape[0] // unit_rows + attended_ref.shape[0] // unit_rows

    def settle(which, count):
        pltpu.make_async_copy(
            made.at[which, pl.ds(0, count)], made.at[which, pl.ds(0, count)], sem.at[which]
        ).wait()

    def send(first, count):
        def push(u, carry):
            pltpu.make_async_copy(
                made.at[buffer, u], out_ref.at[place_ref[first + u]], sem.at[buffer]
            ).start()
            return carry

        lax.fori_loop(0, count, push, 0)

    @pl.when(step >= 2)
    def _():
        settle(buffer, tile_units)

    @pl.when(step < tiles)
    def _():
        row = lax.broadcasted_iota(jnp.int32, slope_ref.shape, 0)
        seen = jnp.where(row == ids_ref[...] - step * slope_ref.shape[0], 1.0, 0.0).astype(jnp.bfloat16)
        made[buffer] = (
            jnp.dot(slope_ref[...], rows_ref[...], preferred_element_type=jnp.float32)
            + jnp.dot(seen, zero_ref[...], preferred_element_type=jnp.float32)
        ).astype(jnp.bfloat16).reshape(tile_units, unit_rows, -1)
        send(step * tile_units, tile_units)

    @pl.when(step == tiles)
    def _():
        joint_units = joint_ref.shape[0] // unit_rows
        made[buffer, pl.ds(0, joint_units)] = jnp.dot(
            joint_ref[...], normed_ref[...], preferred_element_type=jnp.float32
        ).astype(jnp.bfloat16).reshape(joint_units, unit_rows, -1)
        made[buffer, pl.ds(joint_units, last_units - joint_units)] = jnp.dot(
            attended_ref[...], grad_ref[...], preferred_element_type=jnp.float32
        ).astype(jnp.bfloat16).reshape(last_units - joint_units, unit_rows, -1)
        send(tiles * tile_units, last_units)
        settle(1 - buffer, tile_units)
        settle(buffer, last_units)


def weight_grads(place, slots, unit_rows, slope, rows, ids, zero, joint, normed, attended, grad):
    vocab, tokens = slope.shape
    width = rows.shape[1]
    tile = vocab_tile(vocab)
    tiles = vocab // tile
    fixed = lambda k: (0, 0)
    whole = lambda x: pl.BlockSpec(x.shape, fixed)
    return pl.pallas_call(
        functools.partial(weight_grads_kernel, tile // unit_rows, tiles),
        grid=(tiles + 1,),
        out_shape=jax.ShapeDtypeStruct((slots, unit_rows, width), jnp.bfloat16),
        in_specs=[
            pl.BlockSpec(memory_space=pltpu.SMEM),
            pl.BlockSpec((tile, tokens), lambda k: (jnp.minimum(k, tiles - 1), 0)),
        ]
        + [whole(x) for x in (rows, ids, zero, joint, normed, attended, grad)],
        out_specs=whole_any,
        scratch_shapes=[
            pltpu.VMEM((2, tile // unit_rows, unit_rows, width), jnp.bfloat16),
            pltpu.SemaphoreType.DMA((2,)),
        ],
        compiler_params=pltpu.CompilerParams(vmem_limit_bytes=60 << 20),
    )(place, slope, rows, ids, zero, joint, normed, attended, grad)


def adam_update(weight, moment_one, moment_two, gradient, step_rate, decay_factor):
    moment_new = beta_first * moment_one + (1.0 - beta_first) * gradient
    square_new = beta_second * moment_two + (1.0 - beta_second) * gradient * gradient
    moment_hat = moment_new / (1.0 - beta_first**STEP)
    square_hat = square_new / (1.0 - beta_second**STEP)
    weight_new = weight - step_rate * (
        moment_hat / (jnp.sqrt(square_hat) + adam_epsilon) + decay_factor * weight
    )
    return (weight_new, moment_new, square_new)


def norm_forward(values, gain_row):
    return values * inverse_rms(values) * gain_row


def slot_tables(owner_ids, owners, most_units):
    unit_count = owner_ids.shape[0]
    unit_index = jnp.arange(unit_count, dtype=jnp.int32)
    earlier = (owner_ids[None, :] == owner_ids[:, None]) & (
        unit_index[None, :] < unit_index[:, None]
    )
    unit_rank = jnp.sum(earlier.astype(jnp.int32), 1)
    placed = (owner_ids[None, None, :] == jnp.arange(owners, dtype=jnp.int32)[:, None, None]) & (
        unit_rank[None, None, :] == jnp.arange(most_units, dtype=jnp.int32)[None, :, None]
    )
    slot_filled = jnp.any(placed, 2)
    slot_unit = jnp.sum(jnp.where(placed, unit_index[None, None, :], 0), 2)
    return (unit_rank, slot_unit, slot_filled)


def unit_rates(unit_ids, table_units, query_units, value_units):
    return jnp.where(
        unit_ids < table_units,
        rate_table,
        jnp.where(
            unit_ids < query_units,
            rate_query,
            jnp.where(unit_ids < value_units, rate_values, rate_project),
        ),
    )


def pair_slots(route_pairs, priorities, experts, capacity):
    tokens_here = priorities.shape[0]
    pair_expert = route_pairs.T.reshape(-1)
    pair_key = (
        jnp.arange(2, dtype=jnp.int32)[:, None] * tokens_here + priorities[None, :]
    ).reshape(-1)
    before = (pair_expert[None, :] == pair_expert[:, None]) & (
        pair_key[None, :] < pair_key[:, None]
    )
    pair_rank = jnp.sum(before.astype(jnp.int32), 1)
    pair_kept = pair_rank < capacity
    pair_dest = pair_expert * capacity + jnp.minimum(pair_rank, capacity - 1)
    return (pair_kept, pair_dest)


def gelu_tanh(values):
    return jax.nn.gelu(values, approximate=True)


def gelu_slope(values):
    root = math.sqrt(2.0 / math.pi)
    bent = jnp.tanh(root * (values + 0.044715 * values * values * values))
    return 0.5 * (1.0 + bent) + 0.5 * values * (1.0 - bent * bent) * root * (
        1.0 + 3.0 * 0.044715 * values * values
    )


def plane_peer(step):
    chip, core = lax.axis_index("dp"), lax.axis_index("ctx")
    row = lax.rem(chip // 2 + step // 4, 2)
    column = lax.rem(lax.rem(chip, 2) + lax.rem(step // 2, 2), 2)
    place = {"dp": row * 2 + column, "ctx": lax.rem(core + lax.rem(step, 2), 2)}
    return place, place["dp"] * 2 + place["ctx"]


def greet_plane():
    barrier = pltpu.get_barrier_semaphore()
    for step in range(1, 8):
        place, _ = plane_peer(step)
        pl.semaphore_signal(barrier, inc=1, device_id=place, device_id_type=MESH_ID)
    pl.semaphore_wait(barrier, 7)


def plane_copy(source, target, send_sem, recv_sem, step):
    place, _ = plane_peer(step)
    return pltpu.make_async_remote_copy(
        src_ref=source.at[step],
        dst_ref=target.at[step],
        send_sem=send_sem.at[step],
        recv_sem=recv_sem.at[step],
        device_id=place,
        device_id_type=MESH_ID,
    )


def slot_hits(dest_rows, expert, capacity, tokens):
    slot = lax.broadcasted_iota(jnp.int32, (capacity, tokens), 0) + expert * capacity
    return (slot == dest_rows[0:1, :]) | (slot == dest_rows[1:2, :])


def token_hits(dest_columns, expert, capacity, tokens):
    slot = lax.broadcasted_iota(jnp.int32, (tokens, capacity), 1) + expert * capacity
    hit = (slot == dest_columns[:, 0:1]) | (slot == dest_columns[:, 1:2])
    return jnp.where(hit, 1.0, 0.0).astype(jnp.bfloat16)


def gate_of(routes, gates, expert, axis):
    pick = (lambda a, k: a[k : k + 1, :]) if axis == 0 else (lambda a, k: a[:, k : k + 1])
    return jnp.where(pick(routes, 0) == expert, pick(gates, 0), 0.0) + jnp.where(
        pick(routes, 1) == expert, pick(gates, 1), 0.0
    )


def arrival(i):
    return jnp.where(i < 2, i, 9 - i)


def experts_kernel(
    rows_ref, dest_rows, dest_columns, gates, routes, inner_full, outer_full, counts_ref,
    mix_ref, arrived, returned, totals_ref,
    inner_ref, outer_ref, outgoing, results, counts, send_one, recv_one, send_two, recv_two, send_count, recv_count,
):
    capacity = arrived.shape[1]
    tokens = rows_ref.shape[0]
    greet_plane()
    counts[0] = counts_ref[...]

    def send_counts(step, carry):
        place, _ = plane_peer(step)
        pltpu.make_async_remote_copy(
            src_ref=counts_ref,
            dst_ref=counts.at[step],
            send_sem=send_count.at[step],
            recv_sem=recv_count.at[step],
            device_id=place,
            device_id_type=MESH_ID,
        ).start()
        return carry

    def dispatch(i, carry):
        step = 7 - i
        _, expert = plane_peer(step)
        hit = jnp.where(slot_hits(dest_rows, expert, capacity, tokens), 1.0, 0.0).astype(jnp.bfloat16)
        rows = jnp.dot(hit, rows_ref[...], preferred_element_type=jnp.float32).astype(jnp.bfloat16)

        @pl.when(step > 0)
        def _():
            outgoing[step] = rows
            plane_copy(outgoing, arrived, send_one, recv_one, step).start()

        @pl.when(step == 0)
        def _():
            arrived[0] = rows

        return carry

    def work(i, carry):
        step = arrival(i)

        @pl.when(step > 0)
        def _():
            plane_copy(outgoing, arrived, send_one, recv_one, step).wait_recv()

        before = jnp.dot(arrived[step], inner_ref[...], preferred_element_type=jnp.float32)
        active = gelu_tanh(before).astype(jnp.bfloat16)
        part = jnp.dot(active, outer_ref[...], preferred_element_type=jnp.float32).astype(jnp.bfloat16)

        @pl.when(step > 0)
        def _():
            results[step] = part
            plane_copy(results, returned, send_two, recv_two, step).start()

        @pl.when(step == 0)
        def _():
            returned[0] = part

        return carry

    def combine(i, carry):
        step = arrival(i)
        _, expert = plane_peer(step)
        hit = token_hits(dest_columns, expert, capacity, tokens)
        gate = gate_of(routes, gates, expert, 1)

        @pl.when(step > 0)
        def _():
            plane_copy(results, returned, send_two, recv_two, step).wait_recv()

        part = gate * jnp.dot(hit, returned[step], preferred_element_type=jnp.float32)

        @pl.when(i == 0)
        def _():
            mix_ref[...] = part

        @pl.when(i > 0)
        def _():
            mix_ref[...] += part

        return carry

    def finish(step, carry):
        plane_copy(outgoing, arrived, send_one, recv_one, step).wait_send()
        plane_copy(results, returned, send_two, recv_two, step).wait_send()
        place, _ = plane_peer(step)
        pltpu.make_async_remote_copy(
            src_ref=counts_ref,
            dst_ref=counts.at[step],
            send_sem=send_count.at[step],
            recv_sem=recv_count.at[step],
            device_id=place,
            device_id_type=MESH_ID,
        ).wait()
        return carry

    lax.fori_loop(0, 8, dispatch, 0)
    lax.fori_loop(1, 8, send_counts, 0)
    inner_ref[...] = inner_full[...].astype(jnp.bfloat16)
    outer_ref[...] = outer_full[...].astype(jnp.bfloat16)
    lax.fori_loop(0, 8, work, 0)
    lax.fori_loop(0, 8, combine, 0)
    lax.fori_loop(1, 8, finish, 0)
    totals_ref[...] = jnp.sum(counts[...], 0)


def experts_forward(rows, dest, gates, routes, inner, outer, counts, capacity, collective_id):
    tokens, width = rows.shape
    buffer = pltpu.VMEM((8, capacity, width), jnp.bfloat16)
    return pl.pallas_call(
        experts_kernel,
        out_shape=[
            jax.ShapeDtypeStruct((tokens, width), jnp.float32),
            jax.ShapeDtypeStruct((8, capacity, width), jnp.bfloat16),
            jax.ShapeDtypeStruct((8, capacity, width), jnp.bfloat16),
            jax.ShapeDtypeStruct(counts.shape, jnp.float32),
        ],
        in_specs=[whole_vmem] * 8,
        out_specs=[whole_vmem] * 4,
        scratch_shapes=[pltpu.VMEM(w.shape, jnp.bfloat16) for w in (inner, outer)]
        + [buffer, buffer, pltpu.VMEM((8,) + counts.shape, jnp.float32)]
        + [pltpu.SemaphoreType.DMA((8,))] * 6,
        compiler_params=pltpu.CompilerParams(
            collective_id=collective_id, has_side_effects=True, vmem_limit_bytes=60 << 20
        ),
    )(rows, dest, dest.T, gates, routes, inner, outer, counts)


def experts_back_kernel(
    rows_ref, dest_rows, dest_columns, gates, routes, returned, arrived, *refs
):
    inner_full, outer_full, grad_ref, gate_ref, inner_grad, outer_grad, inner_ref, outer_ref = refs[:8]
    outgoing, landed, results, landed_two, active, slopes = refs[8:14]
    send_one, recv_one, send_two, recv_two = refs[14:]
    capacity = arrived.shape[1]
    tokens = rows_ref.shape[0]
    greet_plane()
    gate_ref[...] = jnp.zeros_like(gate_ref)

    def dispatch(i, carry):
        step = 7 - i
        _, expert = plane_peer(step)
        hit = slot_hits(dest_rows, expert, capacity, tokens)
        rows = jnp.dot(
            jnp.where(hit, 1.0, 0.0).astype(jnp.bfloat16), rows_ref[...], preferred_element_type=jnp.float32
        )
        scale = jnp.sum(jnp.where(hit, gate_of(routes, gates, expert, 0), 0.0), 1, keepdims=True)
        sent = (rows * scale).astype(jnp.bfloat16)

        @pl.when(step > 0)
        def _():
            outgoing[step] = sent
            plane_copy(outgoing, landed, send_one, recv_one, step).start()

        @pl.when(step == 0)
        def _():
            landed[0] = sent

        dots = jnp.sum(rows * returned[step].astype(jnp.float32), 1, keepdims=True)
        part = jnp.sum(jnp.where(hit, dots, 0.0), 0, keepdims=True)
        for k in range(2):
            gate_ref[k : k + 1, :] += jnp.where(routes[k : k + 1, :] == expert, part, 0.0)
        return carry

    def work(i, carry):
        step = arrival(i)

        @pl.when(step > 0)
        def _():
            plane_copy(outgoing, landed, send_one, recv_one, step).wait_recv()

        grad_active = lax.dot_general(
            landed[step], outer_ref[...], (((1,), (1,)), ((), ())), preferred_element_type=jnp.float32
        )
        before = jnp.dot(arrived[step], inner_ref[...], preferred_element_type=jnp.float32)
        slope = (grad_active * gelu_slope(before)).astype(jnp.bfloat16)
        back = lax.dot_general(
            slope, inner_ref[...], (((1,), (1,)), ((), ())), preferred_element_type=jnp.float32
        ).astype(jnp.bfloat16)

        @pl.when(step > 0)
        def _():
            results[step] = back
            plane_copy(results, landed_two, send_two, recv_two, step).start()

        @pl.when(step == 0)
        def _():
            landed_two[0] = back

        slopes[step] = slope
        active[step] = gelu_tanh(before).astype(jnp.bfloat16)
        return carry

    def weigh(step, carry):
        outer_part = lax.dot_general(
            active[step], landed[step], (((0,), (0,)), ((), ())), preferred_element_type=jnp.float32
        )
        inner_part = lax.dot_general(
            arrived[step], slopes[step], (((0,), (0,)), ((), ())), preferred_element_type=jnp.float32
        )

        @pl.when(step == 0)
        def _():
            inner_grad[...] = inner_part
            outer_grad[...] = outer_part

        @pl.when(step > 0)
        def _():
            inner_grad[...] += inner_part
            outer_grad[...] += outer_part

        return carry

    def combine(i, carry):
        step = arrival(i)
        _, expert = plane_peer(step)
        hit = token_hits(dest_columns, expert, capacity, tokens)

        @pl.when(step > 0)
        def _():
            plane_copy(results, landed_two, send_two, recv_two, step).wait_recv()

        part = jnp.dot(hit, landed_two[step], preferred_element_type=jnp.float32)

        @pl.when(i == 0)
        def _():
            grad_ref[...] = part

        @pl.when(i > 0)
        def _():
            grad_ref[...] += part

        return carry

    def finish(step, carry):
        plane_copy(outgoing, landed, send_one, recv_one, step).wait_send()
        plane_copy(results, landed_two, send_two, recv_two, step).wait_send()
        return carry

    lax.fori_loop(0, 8, dispatch, 0)
    inner_ref[...] = inner_full[...].astype(jnp.bfloat16)
    outer_ref[...] = outer_full[...].astype(jnp.bfloat16)
    lax.fori_loop(0, 8, work, 0)
    lax.fori_loop(0, 8, weigh, 0)
    lax.fori_loop(0, 8, combine, 0)
    lax.fori_loop(1, 8, finish, 0)


def experts_backward(rows, dest, gates, routes, returned, arrived, inner, outer, collective_id):
    tokens, width = rows.shape
    capacity = arrived.shape[1]
    inside = inner.shape[1]
    buffer = pltpu.VMEM((8, capacity, width), jnp.bfloat16)
    inside_buffer = pltpu.VMEM((8, capacity, inside), jnp.bfloat16)
    return pl.pallas_call(
        experts_back_kernel,
        out_shape=[
            jax.ShapeDtypeStruct((tokens, width), jnp.float32),
            jax.ShapeDtypeStruct((2, tokens), jnp.float32),
            jax.ShapeDtypeStruct((width, inside), jnp.float32),
            jax.ShapeDtypeStruct((inside, width), jnp.float32),
        ],
        in_specs=[whole_vmem] * 9,
        out_specs=[whole_vmem] * 4,
        scratch_shapes=[pltpu.VMEM(w.shape, jnp.bfloat16) for w in (inner, outer)]
        + [buffer] * 4
        + [inside_buffer] * 2
        + [pltpu.SemaphoreType.DMA((8,))] * 4,
        compiler_params=pltpu.CompilerParams(
            collective_id=collective_id, has_side_effects=True, vmem_limit_bytes=60 << 20
        ),
    )(rows, dest, dest.T, gates, routes, returned, arrived, inner, outer)


def own_units_kernel(
    chunks, units_of, slopes_ref, rows_ref, ids_ref, zero_ref, joint_ref, normed_ref, attended_ref,
    grad_ref, small_ref, grads_ref, small_out, *refs
):
    slopes, late, mixed, made, passing, own, other, relay, landed, small_landed, ready = refs[:11]
    other_send, other_recv, relay_send, relay_recv, landed_send, landed_recv = refs[11:17]
    small_send, small_recv, load_sem, store_sem = refs[17:]
    chip, core = lax.axis_index("dp"), lax.axis_index("ctx")
    beside = chip + 1 - 2 * lax.rem(chip, 2)
    across = lax.rem(chip + 2, 4)
    opposite = across + 1 - 2 * lax.rem(across, 2)
    places = (opposite, beside, across, chip)
    slots, unit_rows = own.shape[1:3]
    table_units = slopes.shape[0]
    tokens = rows_ref.shape[0]
    size = slots // chunks
    split = (chunks + 1) // 2
    load = pltpu.make_async_copy(slopes_ref, slopes, load_sem)
    load.start()
    greet_plane()

    def repeat(first, last, body):
        def step(i, carry):
            body(i)
            return carry

        lax.fori_loop(first, last, step, 0)

    def span(q):
        return pl.ds(q * size, size)

    def remote(source, target, send, recv, place):
        return pltpu.make_async_remote_copy(
            src_ref=source,
            dst_ref=target,
            send_sem=send,
            recv_sem=recv,
            device_id=place,
            device_id_type=MESH_ID,
        )

    def pass_over(k, q):
        return remote(
            passing.at[k % 2, span(q)],
            other.at[k, span(q)],
            other_send.at[k, q],
            other_recv.at[k, q],
            {"ctx": 1 - core},
        )

    def to_relay(q, place):
        return remote(own.at[0, span(q)], relay.at[span(q)], relay_send.at[q], relay_recv.at[q], {"dp": place})

    def to_owner(k, q):
        return remote(
            own.at[k, span(q)],
            landed.at[k - 1, span(q)],
            landed_send.at[k - 1, q],
            landed_recv.at[k - 1, q],
            {"dp": places[k]},
        )

    def small_copy(step):
        place, _ = plane_peer(step)
        return remote(
            small_ref, small_landed.at[chip * 2 + core], small_send.at[step], small_recv.at[step], place
        )

    joint_units = joint_ref.shape[0] // unit_rows
    late[pl.ds(0, joint_units)] = jnp.dot(
        joint_ref[...], normed_ref[...], preferred_element_type=jnp.float32
    ).reshape(joint_units, unit_rows, -1)
    last_units = attended_ref.shape[0] // unit_rows
    late[pl.ds(joint_units, last_units)] = jnp.dot(
        attended_ref[...], grad_ref[...], preferred_element_type=jnp.float32
    ).reshape(last_units, unit_rows, -1)
    load.wait()
    group = made.shape[0] // unit_rows

    def form(owner, target, first_group=0, last_group=slots // group):
        def some(g):
            first = owner * slots + g * group

            def fill(s):
                unit = units_of[first + s]
                lines = pl.ds(pl.multiple_of(s * unit_rows, unit_rows), unit_rows)
                mixed[lines, :tokens] = slopes[jnp.minimum(unit, table_units - 1)]
                row = lax.broadcasted_iota(jnp.int32, (unit_rows, tokens), 0) + unit * unit_rows
                mixed[lines, tokens:] = jnp.where(row == ids_ref[...], 1.0, 0.0).astype(jnp.bfloat16)

            repeat(0, group, fill)
            made[...] = jnp.dot(
                mixed[:, :tokens], rows_ref[...], preferred_element_type=jnp.float32
            ) + jnp.dot(mixed[:, tokens:], zero_ref[...], preferred_element_type=jnp.float32)

            def put(s):
                unit = units_of[first + s]
                table_piece = made[pl.ds(pl.multiple_of(s * unit_rows, unit_rows), unit_rows)]
                late_piece = late[jnp.clip(unit - table_units, 0, late.shape[0] - 1)]
                marks = jnp.zeros(table_piece.shape, jnp.int32) + unit
                piece = jnp.where(marks < table_units, table_piece, late_piece)
                target[g * group + s] = piece.astype(jnp.bfloat16)

            repeat(0, group, put)

        repeat(first_group, last_group, some)

    def joined(k, q):
        pass_over(k, q).wait_recv()
        return own[k, span(q)].astype(jnp.float32) + other[k, span(q)].astype(jnp.float32)

    def first_leg(place):
        def leg(q):
            own[0, span(q)] = joined(0, q).astype(jnp.bfloat16)
            to_relay(q, place).start()

        return leg

    def direct(k):
        def leg(q):
            own[k, span(q)] = joined(k, q).astype(jnp.bfloat16)
            to_owner(k, q).start()

        return leg

    def relayed(k, place):
        def leg(q):
            to_relay(q, place).wait_recv()
            total = joined(k, q) + relay[span(q)].astype(jnp.float32)
            own[k, span(q)] = total.astype(jnp.bfloat16)
            to_owner(k, q).start()

        return leg

    def form_pair(k):
        if k >= 2:
            repeat(0, chunks, lambda q: pass_over(k - 2, q).wait_send())
        form(places[k] * 2 + 1 - core, passing.at[k % 2])
        repeat(0, chunks, lambda q: pass_over(k, q).start())
        form(places[k] * 2 + core, own.at[k])

    for g in range(slots // group):
        done = [q for q in range(chunks) if g * group < (q + 1) * size <= (g + 1) * group]
        form(places[0] * 2 + 1 - core, passing.at[0], g, g + 1)
        for q in done:
            pass_over(0, q).start()
        form(places[0] * 2 + core, own.at[0], g, g + 1)
        for q in done:
            first_leg(beside if q < split else across)(q)
    repeat(1, 8, lambda step: small_copy(step).start())
    small_landed[chip * 2 + core] = small_ref[...]
    form_pair(1)
    repeat(0, split, direct(1))
    form_pair(2)
    repeat(split, chunks, direct(2))
    repeat(0, split, relayed(2, beside))
    repeat(split, chunks, relayed(1, across))
    form_pair(3)

    def store(q):
        return pltpu.make_async_copy(
            ready.at[lax.rem(q, 2)], grads_ref.at[span(q)], store_sem.at[lax.rem(q, 2)]
        )

    def keep(q):
        total = joined(3, q)
        to_owner(1, q).wait_recv()
        to_owner(2, q).wait_recv()

        @pl.when(q >= 2)
        def _():
            store(q - 2).wait()

        ready[lax.rem(q, 2)] = (
            total + landed[0, span(q)].astype(jnp.float32) + landed[1, span(q)].astype(jnp.float32)
        )
        store(q).start()

    repeat(0, chunks, keep)

    def finish(q):
        for k in (2, 3):
            pass_over(k, q).wait_send()
        to_owner(1, q).wait_send()
        to_owner(2, q).wait_send()

    repeat(0, chunks, finish)
    repeat(0, split, lambda q: to_relay(q, beside).wait_send())
    repeat(split, chunks, lambda q: to_relay(q, across).wait_send())
    repeat(1, 8, lambda step: small_copy(step).wait())
    total = small_landed[0]
    for source in range(1, 8):
        total = total + small_landed[source]
    small_out[...] = total
    for q in range(max(0, chunks - 2), chunks):
        store(q).wait()


def own_units(units_of, slots, unit_rows, slopes, rows, ids, zero, joint, normed, attended, grad, small, collective_id):
    tokens, width = rows.shape
    unit = (unit_rows, width)
    chunks = max(k for k in range(1, 8) if slots % k == 0)
    group = max(k for k in range(1, 8) if slots % k == 0)
    late = (joint.shape[0] + attended.shape[0]) // unit_rows
    slopes = slopes.reshape(-1, unit_rows, tokens)
    return pl.pallas_call(
        functools.partial(own_units_kernel, chunks),
        out_shape=[
            jax.ShapeDtypeStruct((slots,) + unit, jnp.float32),
            jax.ShapeDtypeStruct(small.shape, jnp.float32),
        ],
        in_specs=[pl.BlockSpec(memory_space=pltpu.SMEM), whole_any] + [whole_vmem] * 8,
        out_specs=[whole_any, whole_vmem],
        scratch_shapes=[
            pltpu.VMEM(slopes.shape, jnp.bfloat16),
            pltpu.VMEM((late,) + unit, jnp.float32),
            pltpu.VMEM((group * unit_rows, 2 * tokens), jnp.bfloat16),
            pltpu.VMEM((group * unit_rows, width), jnp.float32),
            pltpu.VMEM((2, slots) + unit, jnp.bfloat16),
            pltpu.VMEM((4, slots) + unit, jnp.bfloat16),
            pltpu.VMEM((4, slots) + unit, jnp.bfloat16),
            pltpu.VMEM((slots,) + unit, jnp.bfloat16),
            pltpu.VMEM((2, slots) + unit, jnp.bfloat16),
            pltpu.VMEM((8,) + small.shape, jnp.float32),
            pltpu.VMEM((2, slots // chunks) + unit, jnp.float32),
            pltpu.SemaphoreType.DMA((4, chunks)),
            pltpu.SemaphoreType.DMA((4, chunks)),
            pltpu.SemaphoreType.DMA((chunks,)),
            pltpu.SemaphoreType.DMA((chunks,)),
            pltpu.SemaphoreType.DMA((2, chunks)),
            pltpu.SemaphoreType.DMA((2, chunks)),
            pltpu.SemaphoreType.DMA((8,)),
            pltpu.SemaphoreType.DMA((8,)),
            pltpu.SemaphoreType.DMA,
            pltpu.SemaphoreType.DMA((2,)),
        ],
        compiler_params=pltpu.CompilerParams(
            collective_id=collective_id, has_side_effects=True, vmem_limit_bytes=63 << 20
        ),
    )(units_of, slopes, rows, ids, zero, joint, normed, attended, grad, small)


def to_plane(buffer):
    return lax.all_to_all(buffer, ("dp", "ctx"), split_axis=0, concat_axis=0, tiled=True)


def plain_hits(dest, experts, capacity):
    slots = lax.broadcasted_iota(jnp.int32, (experts * capacity, dest.shape[1]), 0)
    return [slots == dest[k : k + 1] for k in range(2)]


def plain_forward(rows, dest, gates, inner, outer, owners, capacity):
    width = rows.shape[1]
    hits = plain_hits(dest, owners, capacity)
    both = (hits[0] | hits[1]).astype(jnp.bfloat16)
    sent = jnp.dot(both, rows, preferred_element_type=jnp.float32).astype(jnp.bfloat16)
    arrived = to_plane(sent.reshape(owners, capacity, width))
    hidden = jnp.einsum("ocd,df->ocf", arrived, inner, preferred_element_type=jnp.float32)
    active = gelu_tanh(hidden).astype(jnp.bfloat16)
    part = jnp.einsum("ocf,fd->ocd", active, outer, preferred_element_type=jnp.float32)
    returned = to_plane(part.astype(jnp.bfloat16))
    flat = returned.reshape(owners * capacity, width)
    mix = sum(
        gates[:, k : k + 1]
        * lax.dot_general(
            hits[k].astype(jnp.bfloat16),
            flat,
            (((0,), (0,)), ((), ())),
            preferred_element_type=jnp.float32,
        )
        for k in range(2)
    )
    return (mix, arrived, returned)


def plain_backward(rows, dest, gates, returned, arrived, inner, outer):
    owners, capacity, width = arrived.shape
    hits = plain_hits(dest, owners, capacity)
    both = (hits[0] | hits[1]).astype(jnp.bfloat16)
    slot_scale = jnp.sum(
        jnp.where(hits[0], gates[0:1], 0.0) + jnp.where(hits[1], gates[1:2], 0.0), 1, keepdims=True
    )
    slot_grads = jnp.dot(both, rows, preferred_element_type=jnp.float32)
    sent = (slot_grads * slot_scale).astype(jnp.bfloat16)
    flat = returned.reshape(owners * capacity, width)
    dots = jnp.sum(slot_grads * flat.astype(jnp.float32), 1, keepdims=True)
    gate_part = jnp.concatenate(
        [jnp.sum(jnp.where(hit, dots, 0.0), 0, keepdims=True) for hit in hits], 0
    )
    landed = to_plane(sent.reshape(owners, capacity, width))
    grad_active = jnp.einsum("ocd,fd->ocf", landed, outer, preferred_element_type=jnp.float32)
    hidden = jnp.einsum("ocd,df->ocf", arrived, inner, preferred_element_type=jnp.float32)
    active = gelu_tanh(hidden).astype(jnp.bfloat16)
    slope = (grad_active * gelu_slope(hidden)).astype(jnp.bfloat16)
    outer_grad = jnp.einsum("ocf,ocd->fd", active, landed, preferred_element_type=jnp.float32)
    inner_grad = jnp.einsum("ocd,ocf->df", arrived, slope, preferred_element_type=jnp.float32)
    back = jnp.einsum("ocf,df->ocd", slope, inner, preferred_element_type=jnp.float32)
    back = to_plane(back.astype(jnp.bfloat16)).reshape(owners * capacity, width)
    grad = lax.dot_general(
        both, back, (((0,), (0,)), ((), ())), preferred_element_type=jnp.float32
    )
    return (grad, gate_part, inner_grad, outer_grad)


def on_device(
    token_ids,
    targets,
    counted,
    routes,
    priority,
    owner_of,
    master,
    master_first,
    master_second,
    expert_in,
    expert_in_first,
    expert_in_second,
    expert_out,
    expert_out_first,
    expert_out_second,
    norm_gains,
    norm_gains_first,
    norm_gains_second,
    router,
    router_first,
    router_second,
    rel_bias,
    rel_bias_first,
    rel_bias_second,
):
    owners = lax.axis_size(("dp", "ctx"))
    tensor_ranks = lax.axis_size("tensor")
    my_owner = lax.axis_index(("dp", "ctx"))
    my_rank = lax.axis_index("tensor")
    my_context = lax.axis_index("ctx")
    sequences, half_length = token_ids.shape
    tokens_here = sequences * half_length
    most_units = master.shape[2]
    unit_rows = master.shape[3]
    model_width = master.shape[4]
    vocab_here = VOCAB // tensor_ranks
    heads_here = rel_bias.shape[0]
    head_size = model_width // (heads_here * tensor_ranks)
    hidden_here = heads_here * head_size
    experts = router.shape[1]
    capacity = (18 * tokens_here + 8 * experts - 1) // (8 * experts)
    table_units = vocab_here // unit_rows
    query_units = table_units + 2 * hidden_here // unit_rows
    value_units = table_units + 3 * hidden_here // unit_rows
    embed_scale = math.sqrt(model_width)
    owner_ids = owner_of[:, 0]
    on_square = lax.axis_size("dp") == 4 and lax.axis_size("ctx") == 2
    unit_rank, slot_unit, slot_filled = slot_tables(owner_ids, owners, most_units)
    counted_rows = counted.reshape(tokens_here, 2).T.astype(jnp.float32)
    loss_weights = counted_rows * jnp.array([[1.0], [ahead_weight]], jnp.float32)
    counts = jnp.zeros((8, 128), jnp.float32).at[0:2].set(jnp.sum(counted_rows, 1, keepdims=True))
    unit_slots = owner_ids * most_units + unit_rank
    route_pairs = routes.reshape(tokens_here, 2)
    pair_kept, pair_dest = pair_slots(route_pairs, priority[0], experts, capacity)
    dest = jnp.where(pair_kept, pair_dest, -1).reshape(2, tokens_here)
    unit_slots, dest = lax.optimization_barrier((unit_slots, dest))
    local_ids = token_ids.reshape(-1) - my_rank * vocab_here
    inside = (local_ids >= 0) & (local_ids < vocab_here)
    clipped_ids = jnp.clip(local_ids, 0, vocab_here - 1)
    unit_starts = jnp.sum(
        jnp.where(
            (clipped_ids // unit_rows)[None, :] == jnp.arange(unit_slots.shape[0])[:, None],
            unit_slots[:, None] * unit_rows,
            0,
        ),
        0,
    )
    slot_rows = unit_starts + clipped_ids % unit_rows
    if on_square:
        slot_rows = jnp.where(inside, slot_rows, -1)[:, None]
        weights_low, embedded, normed_one_low, joint, joint_low, project_low = embed(
            unit_slots,
            master[0, 0],
            slot_rows,
            norm_gains[0:1],
            table_units,
            3 * hidden_here,
            11,
        )
    else:
        master_low = master[0, 0].astype(jnp.bfloat16)
        gathered = lax.all_gather(master_low, ("dp", "ctx"), axis=0, tiled=True)
        looked = jnp.take(gathered.reshape(-1, model_width), slot_rows, axis=0)
        looked = jnp.where(inside[:, None], looked, 0)
        weights_low = pull_units([gathered], unit_slots)
        (embedded,) = sum_line(looked, [], [], keep_total, 1)
    weights_low = weights_low.reshape(-1, model_width)
    if not on_square:
        joint_low = weights_low[vocab_here : vocab_here + 3 * hidden_here]
        project_low = weights_low[vocab_here + 3 * hidden_here :]
    rolled = [project_low] + [
        lax.ppermute(project_low, "tensor", [(source, (source + step) % 4) for source in range(4)])
        for step in (1, 2, 3)
    ]
    gain_rows = [norm_gains[k : k + 1] for k in range(3)]
    stream_shape = jax.ShapeDtypeStruct((tokens_here, model_width), jnp.float32)
    gain_shape = jax.ShapeDtypeStruct((1, model_width), jnp.float32)
    if not on_square:
        stream_zero = embedded.astype(jnp.float32) * embed_scale
        normed_one_low = norm_forward(stream_zero, norm_gains[0]).astype(jnp.bfloat16)
        joint = lax.dot_general(
            joint_low, normed_one_low, (((1,), (1,)), ((), ())), preferred_element_type=jnp.float32
        ).astype(jnp.bfloat16)
    attended_all, logsum_rows, pairs_before, attended = attention(
        rel_bias, joint, heads_here, head_size, 2
    )
    router_low = router.astype(jnp.bfloat16)
    stream_one, normed_two_low, gate_rows, gate_columns = middle(
        attended_all.reshape(model_width, tokens_here),
        rolled,
        embedded,
        gain_rows[1],
        router_low.T,
        route_pairs.T,
    )
    if on_square:
        moe_partial, arrived, returned, counts = experts_forward(
            normed_two_low, dest, gate_columns, route_pairs, expert_in[0], expert_out[0], counts, capacity, 8
        )
    else:
        inner_low, outer_low = expert_in[0].astype(jnp.bfloat16), expert_out[0].astype(jnp.bfloat16)
        moe_partial, arrived, returned = plain_forward(
            normed_two_low, dest, gate_columns, inner_low, outer_low, owners, capacity
        )
        counts = lax.psum(counts, ("dp", "ctx"))
    weight_total = counts[0, 0] + ahead_weight * counts[1, 0]
    local_targets = targets.reshape(tokens_here, 2).T - my_rank * vocab_here
    weight_rows = jnp.concatenate(
        [
            loss_weights,
            loss_weights[0:1] + loss_weights[1:2],
            jnp.broadcast_to(1.0 / weight_total, (1, tokens_here)),
        ],
        0,
    )
    head_low, grad_two_low, grad_two, gain_grad_three, logsum_vocab, target_sums, slopes = head_line(
        moe_partial, stream_one, gain_rows[2], weights_low, local_targets, weight_rows, vocab_here, 3
    )
    if on_square:
        moe_grad_part, gate_part, inner_grad, outer_grad = experts_backward(
            grad_two_low,
            dest,
            gate_rows,
            route_pairs.T,
            returned,
            arrived,
            expert_in[0],
            expert_out[0],
            9,
        )
    else:
        moe_grad_part, gate_part, inner_grad, outer_grad = plain_backward(
            grad_two_low, dest, gate_rows, returned, arrived, inner_low, outer_low
        )
    gate_part = jnp.concatenate([gate_part, target_sums, jnp.zeros_like(target_sums)], 0)
    gate_block = pltpu.VMEM((3, 4, tokens_here), jnp.float32)
    grad_one_low, grad_one, logit_grad, target_total, gain_grad_two = sum_line(
        moe_grad_part,
        [
            stream_one,
            gain_rows[1],
            grad_two,
            gate_part,
            gate_rows,
            route_pairs.T,
            router_low,
        ],
        [
            stream_shape,
            jax.ShapeDtypeStruct((experts, tokens_here), jnp.bfloat16),
            jax.ShapeDtypeStruct((1, tokens_here), jnp.float32),
            gain_shape,
        ],
        finish_expert_grad,
        5,
        prologue=start_router_grad,
        scratch=(gate_block, pltpu.SemaphoreType.DMA((3,)), pltpu.SemaphoreType.DMA((3,))),
        opening=send_gate_parts,
    )
    router_grad = jnp.dot(logit_grad, normed_two_low, preferred_element_type=jnp.float32)
    loss_local = jnp.sum(weight_rows[2:3] * logsum_vocab) - jnp.sum(target_total)
    query_grad, pair_grad, before_grad, bias_lines, *expert_states = attention_back(
        rel_bias,
        joint,
        pairs_before,
        logsum_rows,
        grad_one_low,
        project_low,
        (
            expert_in[0],
            expert_in_first[0],
            expert_in_second[0],
            inner_grad,
            expert_out[0],
            expert_out_first[0],
            expert_out_second[0],
            outer_grad,
        ),
        heads_here,
        head_size,
    )
    distances = 2 * (half_length // BLOCK)
    bias_grad = jnp.sum(bias_lines, 1).reshape(heads_here, distances)
    pair_shape = pltpu.VMEM((2 * hidden_here, tokens_here), jnp.bfloat16)
    zero_grad_low, joint_grad, gain_grads = sum_line(
        None,
        [
            embedded,
            gain_rows[0],
            grad_one,
            gain_grad_two,
            gain_grad_three,
            query_grad,
            pair_grad,
            before_grad,
            joint_low,
        ],
        [
            jax.ShapeDtypeStruct((3 * hidden_here, tokens_here), jnp.bfloat16),
            jax.ShapeDtypeStruct((8, model_width), jnp.float32),
        ],
        functools.partial(finish_input_grad, embed_scale),
        6,
        prologue=clear_gain,
        scratch=(
            pltpu.SemaphoreType.DMA,
            pltpu.SemaphoreType.DMA,
            pair_shape,
            pltpu.SemaphoreType.DMA((2,)),
            pltpu.VMEM((tokens_here, model_width), jnp.float32),
        ),
        opening=form_joint_grad,
        ending=share_gains,
    )
    my_units = jnp.take(slot_unit, my_owner, axis=0)
    my_filled = jnp.take(slot_filled, my_owner, axis=0)[:, None, None]
    bias_row = jnp.concatenate([bias_grad.reshape(-1), loss_local[None]])
    bias_row = jnp.pad(bias_row, (0, model_width - bias_row.shape[0]))[None]
    small = jnp.concatenate([gain_grads[:3], router_grad, bias_row], 0)
    small = jnp.pad(small, ((0, -small.shape[0] % 8), (0, 0)))
    slot_rates = unit_rates(my_units, table_units, query_units, value_units)[:, None, None]
    states = (master[0, 0], master_first[0, 0], master_second[0, 0])
    grad_rows = (
        slopes,
        head_low,
        local_ids[None, :],
        zero_grad_low,
        joint_grad,
        normed_one_low,
        attended,
        grad_one_low,
    )
    if on_square:
        mine, small = own_units(slot_unit.reshape(-1), most_units, unit_rows, *grad_rows, small, 10)
    else:
        outgoing = weight_grads(unit_slots, owners * most_units, unit_rows, *grad_rows)
        mine = lax.psum_scatter(
            outgoing.astype(jnp.float32), ("dp", "ctx"), scatter_dimension=0, tiled=True
        )
        small = lax.psum(small, ("dp", "ctx"))
    states = adam_update(*states, jnp.where(my_filled, mine, 0.0), slot_rates, decay_rate)
    gains_grad = small[:3]
    router_grad = small[3 : 3 + experts].T
    bias_grad = small[3 + experts, : rel_bias.size].reshape(rel_bias.shape)
    loss_totals = jnp.stack([small[3 + experts, rel_bias.size], weight_total])
    gains_new, gains_first_new, gains_second_new = adam_update(
        norm_gains, norm_gains_first, norm_gains_second, gains_grad, rate_gains, 0.0
    )
    router_new, router_first_new, router_second_new = adam_update(
        router, router_first, router_second, router_grad, rate_router, decay_rate
    )
    biases_new, biases_first_new, biases_second_new = adam_update(
        rel_bias, rel_bias_first, rel_bias_second, bias_grad, rate_biases, 0.0
    )
    return (
        loss_totals,
        *(state[None, None] for state in states),
        *(state[None] for state in expert_states),
        gains_new,
        gains_first_new,
        gains_second_new,
        router_new,
        router_first_new,
        router_second_new,
        biases_new,
        biases_first_new,
        biases_second_new,
    )


def solution(mesh):
    in_specs = (
        P("dp", "ctx"),
        P("dp", "ctx", None),
        P("dp", "ctx", None),
        P("dp", "ctx", None),
        P(("dp", "ctx"), None),
        P(),
        P("tensor", ("dp", "ctx"), None, None, None),
        P("tensor", ("dp", "ctx"), None, None, None),
        P("tensor", ("dp", "ctx"), None, None, None),
        P(("dp", "ctx"), None, "tensor"),
        P(("dp", "ctx"), None, "tensor"),
        P(("dp", "ctx"), None, "tensor"),
        P(("dp", "ctx"), "tensor", None),
        P(("dp", "ctx"), "tensor", None),
        P(("dp", "ctx"), "tensor", None),
        P(),
        P(),
        P(),
        P(),
        P(),
        P(),
        P("tensor", None),
        P("tensor", None),
        P("tensor", None),
    )
    out_specs = (
        P(),
        P("tensor", ("dp", "ctx"), None, None, None),
        P("tensor", ("dp", "ctx"), None, None, None),
        P("tensor", ("dp", "ctx"), None, None, None),
        P(("dp", "ctx"), None, "tensor"),
        P(("dp", "ctx"), None, "tensor"),
        P(("dp", "ctx"), None, "tensor"),
        P(("dp", "ctx"), "tensor", None),
        P(("dp", "ctx"), "tensor", None),
        P(("dp", "ctx"), "tensor", None),
        P(),
        P(),
        P(),
        P(),
        P(),
        P(),
        P("tensor", None),
        P("tensor", None),
        P("tensor", None),
    )
    return jax.shard_map(
        on_device, mesh=mesh, in_specs=in_specs, out_specs=out_specs, check_vma=False
    )
```

```python
import functools
import math

import jax
import jax.numpy as jnp
from jax import lax
from jax.experimental import pallas as pl
from jax.experimental.pallas import tpu as pltpu
from jax.sharding import PartitionSpec as P

VOCAB = 32000
BLOCK = 256
STEP = 10


highest_precision = lax.Precision.HIGHEST
beta_first = 0.9
beta_second = 0.95
adam_epsilon = 1e-08
norm_epsilon = 1e-06
ahead_weight = 0.3
masked_score = -1e30
rate_table = 0.1
rate_query = 0.05
rate_values = 0.05
rate_project = 0.5
rate_inner = 0.05
rate_outer = 0.03
rate_gains = 0.5
rate_router = 0.05
rate_biases = 0.5
decay_rate = 0.1


MESH_ID = pl.DeviceIdType.MESH
whole_vmem = pl.BlockSpec(memory_space=pltpu.VMEM)
whole_any = pl.BlockSpec(memory_space=pl.ANY)
line_lag = 2


def sum_line_kernel(
    rows, count, opening, with_core, prologue, epilogue, ending, n_extra, n_aux, n_scratch, *refs
):
    extras = refs[:n_extra]
    out_ref = refs[n_extra]
    aux = refs[n_extra + 1 : n_extra + 1 + n_aux]
    rest = refs[n_extra + 1 + n_aux :]
    scratch = rest[:n_scratch]
    part_ref = scratch[-1] if with_core else extras[0]
    extras = extras if with_core else extras[1:]
    stage, from_end, from_mid, send_sem, end_sem, mid_sem, back_sem, back_recv = rest[n_scratch:]
    rank = lax.axis_index("tensor")
    inner = (rank == 1) | (rank == 2)
    end_peer = jnp.where(rank < 2, 1 - rank, 5 - rank)
    mid_peer = 3 - rank
    barrier = pltpu.get_barrier_semaphore()
    if opening is None or with_core:
        pl.semaphore_signal(barrier, inc=1, device_id={"tensor": end_peer}, device_id_type=MESH_ID)
        if with_core:
            other_core = {"ctx": 1 - lax.axis_index("ctx")}
            pl.semaphore_signal(barrier, inc=1, device_id=other_core, device_id_type=MESH_ID)

        @pl.when(inner)
        def _():
            pl.semaphore_signal(
                barrier, inc=1, device_id={"tensor": mid_peer}, device_id_type=MESH_ID
            )
            pl.semaphore_wait(barrier, 2 + with_core)

        @pl.when(jnp.logical_not(inner))
        def _():
            pl.semaphore_wait(barrier, 1 + with_core)
    else:
        for step in (1, 2, 3):
            other = lax.rem(rank + step, 4)
            pl.semaphore_signal(barrier, inc=1, device_id={"tensor": other}, device_id_type=MESH_ID)
        pl.semaphore_wait(barrier, 3)

    def span(i):
        return pl.ds(pl.multiple_of(i * rows, rows), rows)

    def to_inner(i):
        return pltpu.make_async_remote_copy(
            src_ref=stage.at[i],
            dst_ref=from_end.at[i],
            send_sem=send_sem.at[i],
            recv_sem=end_sem.at[i],
            device_id={"tensor": end_peer},
            device_id_type=MESH_ID,
        )

    def to_middle(i):
        return pltpu.make_async_remote_copy(
            src_ref=stage.at[i],
            dst_ref=from_mid.at[i],
            send_sem=send_sem.at[i],
            recv_sem=mid_sem.at[i],
            device_id={"tensor": mid_peer},
            device_id_type=MESH_ID,
        )

    def to_end(i):
        return pltpu.make_async_remote_copy(
            src_ref=out_ref.at[span(i)],
            dst_ref=out_ref.at[span(i)],
            send_sem=back_sem.at[i],
            recv_sem=back_recv.at[i],
            device_id={"tensor": end_peer},
            device_id_type=MESH_ID,
        )

    if opening is not None:
        opening(rank, extras, aux, scratch)

    @pl.when(jnp.logical_not(inner))
    def _():
        def push(i, carry):
            stage[i] = part_ref[span(i)].astype(jnp.bfloat16)
            to_inner(i).start()
            return carry

        lax.fori_loop(0, count, push, 0)

    if prologue is not None:
        prologue(rank, inner, extras, aux, scratch)

    @pl.when(inner)
    def _():
        def step(i, carry):
            @pl.when(i < count)
            def _():
                to_inner(i).wait_recv()
                mine = part_ref[span(i)].astype(jnp.float32) + from_end[i].astype(jnp.float32)
                stage[i] = mine.astype(jnp.bfloat16)
                to_middle(i).start()

            @pl.when(i >= line_lag)
            def _():
                j = i - line_lag
                to_middle(j).wait_recv()
                total = stage[j].astype(jnp.float32) + from_mid[j].astype(jnp.float32)
                out_ref[span(j)] = epilogue(total, span(j), rank, extras, aux, scratch)
                to_end(j).start()

            return carry

        lax.fori_loop(0, count + line_lag, step, 0)

        def drain(i, carry):
            to_middle(i).wait_send()
            to_end(i).wait_send()
            return carry

        lax.fori_loop(0, count, drain, 0)

    @pl.when(jnp.logical_not(inner))
    def _():
        def finish(i, carry):
            to_end(i).wait_recv()
            to_inner(i).wait_send()
            return carry

        lax.fori_loop(0, count, finish, 0)

    if ending is not None:
        ending(inner, end_peer, extras, aux, scratch)


def sum_line(
    part,
    extras,
    aux_shapes,
    epilogue,
    collective_id,
    prologue=None,
    scratch=(),
    opening=None,
    ending=None,
    rows=64,
):
    tokens, width = scratch[-1].shape if part is None else part.shape
    inputs = list(extras) if part is None else [part, *extras]
    count = tokens // rows
    chunks = pltpu.VMEM((count, rows, width), jnp.bfloat16)
    return pl.pallas_call(
        functools.partial(
            sum_line_kernel,
            rows,
            count,
            opening,
            part is None,
            prologue,
            epilogue,
            ending,
            len(inputs),
            len(aux_shapes),
            len(scratch),
        ),
        out_shape=[jax.ShapeDtypeStruct((tokens, width), jnp.bfloat16)] + list(aux_shapes),
        in_specs=[whole_vmem] * len(inputs),
        out_specs=[whole_vmem] * (1 + len(aux_shapes)),
        scratch_shapes=list(scratch)
        + [chunks, chunks, chunks]
        + [pltpu.SemaphoreType.DMA((count,))] * 5,
        compiler_params=pltpu.CompilerParams(
            collective_id=collective_id, has_side_effects=True, vmem_limit_bytes=48 << 20
        ),
    )(*inputs)


def keep_total(total, span, rank, extras, aux, scratch):
    return total.astype(jnp.bfloat16)


def inverse_rms(values):
    return lax.rsqrt(jnp.mean(values * values, -1, keepdims=True) + norm_epsilon)


def norm_back_rows(values, gain, upstream):
    inverse = inverse_rms(values)
    normed = values * inverse
    scaled = upstream * gain
    gain_grad = jnp.sum(upstream * normed, 0, keepdims=True)
    inputs_grad = inverse * (scaled - normed * jnp.mean(scaled * normed, -1, keepdims=True))
    return (inputs_grad, gain_grad)


def clear_gain(rank, inner, extras, aux, scratch):
    @pl.when(inner)
    def _():
        aux[-1][...] = jnp.zeros_like(aux[-1])


def share_gains(inner, end_peer, extras, aux, scratch):
    gains = aux[-1]
    copy = pltpu.make_async_remote_copy(
        src_ref=gains,
        dst_ref=gains,
        send_sem=scratch[0],
        recv_sem=scratch[1],
        device_id={"tensor": end_peer},
        device_id_type=MESH_ID,
    )

    @pl.when(inner)
    def _():
        gains[1:2, :] = extras[3][...]
        gains[2:3, :] = extras[4][...]
        copy.start()
        copy.wait_send()

    @pl.when(jnp.logical_not(inner))
    def _():
        copy.wait_recv()


def gate_copies(rank, extras, scratch):
    gate_part = extras[3]
    landed, gate_send, gate_recv = scratch
    return [
        pltpu.make_async_remote_copy(
            src_ref=gate_part,
            dst_ref=landed.at[step - 1],
            send_sem=gate_send.at[step - 1],
            recv_sem=gate_recv.at[step - 1],
            device_id={"tensor": lax.rem(rank + step, 4)},
            device_id_type=MESH_ID,
        )
        for step in (1, 2, 3)
    ]


def send_gate_parts(rank, extras, aux, scratch):
    for copy in gate_copies(rank, extras, scratch):
        copy.start()


def start_router_grad(rank, inner, extras, aux, scratch):
    stream_one, gain, grad_two, gate_part, gates, routes, router_low = extras
    grad_one, logit_grad, target_total, gain_grad = aux
    landed = scratch[0]
    clear_gain(rank, inner, extras, aux, scratch)
    for copy in gate_copies(rank, extras, scratch):
        copy.wait()
    gate_grad = jnp.zeros(gate_part.shape, jnp.float32)
    for source in range(4):
        piece = jnp.zeros(gate_part.shape, jnp.float32)
        for step in (1, 2, 3):
            piece = jnp.where(lax.rem(source + step, 4) == rank, landed[step - 1], piece)
        gate_grad = gate_grad + jnp.where(rank == source, gate_part[...], piece)
    target_total[...] = gate_grad[2:3]
    gate_grad = gate_grad[0:2]
    weighted = gates[...] * gate_grad
    chosen = gates[...] * (gate_grad - (weighted[0:1] + weighted[1:2]))
    experts, tokens = logit_grad.shape
    row = lax.broadcasted_iota(jnp.int32, (experts, tokens), 0)
    placed = jnp.where(row == routes[0:1], chosen[0:1], 0.0) + jnp.where(
        row == routes[1:2], chosen[1:2], 0.0
    )
    logit_grad[...] = placed.astype(jnp.bfloat16)

    @pl.when(inner)
    def _():
        grad_one[...] = lax.dot_general(
            logit_grad[...],
            router_low[...],
            (((0,), (1,)), ((), ())),
            preferred_element_type=jnp.float32,
        )


def finish_expert_grad(total, span, rank, extras, aux, scratch):
    stream_one, gain, grad_two, gate_part, gates, routes, router_low = extras
    grad_one, logit_grad, target_total, gain_grad = aux
    part, gain_part = norm_back_rows(
        stream_one[span], gain[...], total + grad_one[span]
    )
    result = grad_two[span] + part
    grad_one[span] = result
    gain_grad[...] += gain_part
    return result.astype(jnp.bfloat16)


def form_joint_grad(rank, extras, aux, scratch):
    query_grad, pair_grad, before_grad, joint_weights = extras[5:]
    joint_grad = aux[0]
    landed, pair_sem, part = scratch[2:]
    hidden = query_grad.shape[0]
    later = lax.axis_index("ctx") > 0
    copy = pltpu.make_async_remote_copy(
        src_ref=before_grad,
        dst_ref=landed,
        send_sem=pair_sem.at[0],
        recv_sem=pair_sem.at[1],
        device_id={"ctx": 1 - lax.axis_index("ctx")},
        device_id_type=MESH_ID,
    )
    joint_grad[0:hidden, :] = query_grad[...]

    @pl.when(later)
    def _():
        copy.start()
        joint_grad[hidden:, :] = pair_grad[...].astype(jnp.bfloat16)

    @pl.when(jnp.logical_not(later))
    def _():
        copy.wait_recv()
        both = pair_grad[...] + landed[...].astype(jnp.float32)
        joint_grad[hidden:, :] = both.astype(jnp.bfloat16)

    part[...] = lax.dot_general(
        joint_grad[...], joint_weights[...], (((0,), (0,)), ((), ())), preferred_element_type=jnp.float32
    )

    @pl.when(later)
    def _():
        copy.wait_send()


def finish_input_grad(scale, total, span, rank, extras, aux, scratch):
    embedded, gain, grad_one = extras[:3]
    stream_zero = embedded[span].astype(jnp.float32) * scale
    part, gain_part = norm_back_rows(stream_zero, gain[...], total)
    aux[-1][0:1, :] += gain_part
    return ((grad_one[span] + part) * scale).astype(jnp.bfloat16)


def middle_kernel(
    attended_ref, embedded_ref, gain_ref, router_ref, routes_ref, *refs
):
    rolled, (stream_ref, normed_ref, rows_ref, columns_ref, project_ref) = refs[:4], refs[4:]

    @pl.when(pl.program_id(0) == 0)
    def _():
        for step in range(4):
            lines = rolled[step].shape[0]
            owner = lax.rem(lax.axis_index("tensor") + 4 - step, 4)
            project_ref[pl.ds(pl.multiple_of(owner * lines, lines), lines)] = rolled[step][...]

    scale = math.sqrt(embedded_ref.shape[1])
    stream = embedded_ref[...].astype(jnp.float32) * scale + lax.dot_general(
        attended_ref[...], project_ref[...], (((0,), (0,)), ((), ())), preferred_element_type=jnp.float32
    )
    stream_ref[...] = stream
    normed = (stream * inverse_rms(stream) * gain_ref[...]).astype(jnp.bfloat16)
    normed_ref[...] = normed
    scores = lax.dot_general(
        router_ref[...], normed, (((1,), (1,)), ((), ())), preferred_element_type=jnp.float32
    )
    expert = lax.broadcasted_iota(jnp.int32, scores.shape, 0)
    first, second = (
        jnp.sum(jnp.where(expert == routes_ref[k : k + 1, :], scores, 0.0), 0, keepdims=True)
        for k in range(2)
    )
    top = jnp.maximum(first, second)
    first, second = jnp.exp(first - top), jnp.exp(second - top)
    total = first + second
    gates = jnp.concatenate([first / total, second / total], 0)
    rows_ref[...] = gates
    columns_ref[...] = jnp.concatenate([gates, jnp.zeros((6, gates.shape[1]), jnp.float32)], 0).T


def middle(attended, rolled, embedded, gain, router, routes):
    tokens, width = embedded.shape
    tile = 256
    fixed = lambda k: (0, 0)
    whole = lambda x: pl.BlockSpec(x.shape, fixed)
    down = lambda n: pl.BlockSpec((tile, n), lambda k: (k, 0))
    along = lambda n: pl.BlockSpec((n, tile), lambda k: (0, k))
    return pl.pallas_call(
        middle_kernel,
        grid=(tokens // tile,),
        out_shape=[
            jax.ShapeDtypeStruct((tokens, width), jnp.float32),
            jax.ShapeDtypeStruct((tokens, width), jnp.bfloat16),
            jax.ShapeDtypeStruct((2, tokens), jnp.float32),
            jax.ShapeDtypeStruct((tokens, 8), jnp.float32),
        ],
        in_specs=[along(width), down(width), whole(gain), whole(router), along(2)]
        + [whole(x) for x in rolled],
        out_specs=[down(width), down(width), along(2), down(8)],
        scratch_shapes=[pltpu.VMEM((width, width), jnp.bfloat16)],
        compiler_params=pltpu.CompilerParams(vmem_limit_bytes=40 << 20),
    )(attended, embedded, gain, router, routes, *rolled)


def embed_kernel(
    chunks, first_unit, slots_ref, mine_ref, rows_ref, gain_ref, units_ref, embedded_ref, normed_ref, joint_ref,
    joint_weights, project_weights, *refs
):
    held, total, stage, from_end, from_mid, units, store_sem = refs[:7]
    send_x, recv_x, send_y, recv_y, send_z, recv_z, send_core, recv_core = refs[7:15]
    send_sem, end_sem, mid_sem, back_sem, back_recv = refs[15:]
    chip, core = lax.axis_index("dp"), lax.axis_index("ctx")
    beside = chip + 1 - 2 * lax.rem(chip, 2)
    across = lax.rem(chip + 2, 4)
    opposite = across + 1 - 2 * lax.rem(across, 2)
    places = (chip, beside, across, opposite)
    rank = lax.axis_index("tensor")
    inner = (rank == 1) | (rank == 2)
    end_peer = jnp.where(rank < 2, 1 - rank, 5 - rank)
    mid_peer = 3 - rank
    slots, unit_rows = mine_ref.shape[:2]
    width = total.shape[2]
    size = slots // chunks
    split = (chunks + 1) // 2
    tokens = rows_ref.shape[0]
    count, rows = stage.shape[1:3]

    def repeat(first, last, body):
        def step(i, carry):
            body(i)
            return carry

        lax.fori_loop(first, last, step, 0)

    def columns(h):
        return slice(h * width, (h + 1) * width)

    own = (chip * 2 + core) * slots
    for h in range(2):
        held[h, pl.ds(own, slots)] = mine_ref[:, :, columns(h)].astype(jnp.bfloat16)
    barrier = pltpu.get_barrier_semaphore()
    for place in ({"ctx": 1 - core}, {"dp": beside}, {"dp": across}, {"tensor": end_peer}):
        pl.semaphore_signal(barrier, inc=1, device_id=place, device_id_type=MESH_ID)

    @pl.when(inner)
    def _():
        pl.semaphore_signal(barrier, inc=1, device_id={"tensor": mid_peer}, device_id_type=MESH_ID)
        pl.semaphore_wait(barrier, 5)

    @pl.when(jnp.logical_not(inner))
    def _():
        pl.semaphore_wait(barrier, 4)

    def remote(source, target, send, recv, place):
        return pltpu.make_async_remote_copy(
            src_ref=source,
            dst_ref=target,
            send_sem=send,
            recv_sem=recv,
            device_id=place,
            device_id_type=MESH_ID,
        )

    def copy(h, place, q, send, recv, target):
        piece = held.at[h, pl.ds((place * 2 + core) * slots + q * size, size)]
        return remote(piece, piece, send, recv, target)

    def to_beside(h, q):
        return copy(h, chip, q, send_x.at[h, q], recv_x.at[h, q], {"dp": beside})

    def to_across(h, q):
        return copy(h, chip, q, send_y.at[h, q], recv_y.at[h, q], {"dp": across})

    def passed_on(h, q, source, target):
        return copy(h, source, q, send_z.at[h, q], recv_z.at[h, q], {"dp": target})

    def to_core(h, k, q):
        return copy(h, places[k], q, send_core.at[h, k, q], recv_core.at[h, k, q], {"ctx": 1 - core})

    def start(h):
        def both(i):
            to_beside(h, i).start()
            to_across(h, lax.rem(i + split, chunks)).start()

        repeat(0, chunks, both)
        repeat(0, chunks, lambda q: to_core(h, 0, q).start())

    def look(h, place, which):
        begin = (place * 2 + which) * slots
        lines = slots * unit_rows
        column = lax.broadcasted_iota(jnp.int32, (tokens, lines), 1) + begin * unit_rows
        hit = jnp.where(column == rows_ref[...], 1.0, 0.0).astype(jnp.bfloat16)
        block = held[h, pl.ds(begin, slots)].reshape(lines, width)
        total[h] += jnp.dot(hit, block, preferred_element_type=jnp.float32)

    def relay(h, i):
        to_beside(h, i).wait_recv()

        @pl.when(i < split)
        def _():
            passed_on(h, i, beside, across).start()

        to_core(h, 1, i).start()
        j = lax.rem(i + split, chunks)
        to_across(h, j).wait_recv()

        @pl.when(j >= split)
        def _():
            passed_on(h, j, across, beside).start()

        to_core(h, 2, j).start()

    def rest(h):
        repeat(0, chunks, lambda q: to_core(h, 0, q).wait_recv())
        look(h, chip, 1 - core)
        look(h, beside, core)
        look(h, across, core)

        def last(q):
            passed_on(h, q, opposite, opposite).wait_recv()
            to_core(h, 3, q).start()
            to_core(h, 1, q).wait_recv()
            to_core(h, 2, q).wait_recv()

        repeat(0, chunks, last)
        look(h, beside, 1 - core)
        look(h, across, 1 - core)
        look(h, opposite, core)
        repeat(0, chunks, lambda q: to_core(h, 3, q).wait_recv())
        look(h, opposite, 1 - core)

    def span(i):
        return pl.ds(pl.multiple_of(i * rows, rows), rows)

    def to_inner(h, i):
        return remote(
            stage.at[h, i], from_end.at[h, i], send_sem.at[h, i], end_sem.at[h, i], {"tensor": end_peer}
        )

    def to_middle(h, i):
        return remote(
            stage.at[h, i], from_mid.at[h, i], send_sem.at[h, i], mid_sem.at[h, i], {"tensor": mid_peer}
        )

    def to_end(h, i):
        piece = embedded_ref.at[span(i), columns(h)]
        return remote(piece, piece, back_sem.at[h, i], back_recv.at[h, i], {"tensor": end_peer})

    def push(h):
        @pl.when(jnp.logical_not(inner))
        def _():
            def one(i):
                stage[h, i] = total[h, span(i)].astype(jnp.bfloat16)
                to_inner(h, i).start()

            repeat(0, count, one)

    def exchange(h, i):
        @pl.when(inner & (i < count))
        def _():
            to_inner(h, i).wait_recv()
            stage[h, i] = (total[h, span(i)] + from_end[h, i].astype(jnp.float32)).astype(jnp.bfloat16)
            to_middle(h, i).start()

        @pl.when(inner & (i >= line_lag))
        def _():
            j = i - line_lag
            to_middle(h, j).wait_recv()
            both = stage[h, j].astype(jnp.float32) + from_mid[h, j].astype(jnp.float32)
            embedded_ref[span(j), columns(h)] = both.astype(jnp.bfloat16)
            to_end(h, j).start()

    total[...] = jnp.zeros_like(total)
    start(0)
    look(0, chip, core)
    repeat(0, chunks, lambda i: relay(0, i))
    start(1)
    rest(0)
    push(0)
    look(1, chip, core)

    def between(i):
        exchange(0, i)

        @pl.when(i < chunks)
        def _():
            relay(1, i)

    repeat(0, count + line_lag, between)
    rest(1)
    push(1)

    def place_unit(u):
        for h in range(2):
            units[u, :, columns(h)] = held[h, slots_ref[u]]

    turns = count + line_lag
    share = -(-units.shape[0] // turns)

    def exchange_and_place(i):
        exchange(1, i)
        repeat(i * share, jnp.minimum((i + 1) * share, units.shape[0]), place_unit)

    repeat(0, turns, exchange_and_place)
    store = pltpu.make_async_copy(units, units_ref, store_sem)
    store.start()

    def finish(q):
        for h in range(2):
            to_beside(h, q).wait_send()
            to_across(h, q).wait_send()
            for k in range(4):
                to_core(h, k, q).wait_send()
            passed_on(h, q, opposite, opposite).wait_send()

    repeat(0, chunks, finish)

    @pl.when(inner)
    def _():
        def drain(i):
            for h in range(2):
                to_middle(h, i).wait_send()
                to_end(h, i).wait_send()

        repeat(0, count, drain)

    @pl.when(jnp.logical_not(inner))
    def _():
        def drain(i):
            for h in range(2):
                to_end(h, i).wait_recv()
                to_inner(h, i).wait_send()

        repeat(0, count, drain)

    stream = embedded_ref[...].astype(jnp.float32) * math.sqrt(2 * width)
    normed = (stream * inverse_rms(stream) * gain_ref[...]).astype(jnp.bfloat16)
    normed_ref[...] = normed
    lines = joint_ref.shape[0]
    weights = units[first_unit : first_unit + lines // unit_rows].reshape(lines, 2 * width)
    joint_weights[...] = weights
    project_weights[...] = units[first_unit + lines // unit_rows :].reshape(
        project_weights.shape
    )
    joint_ref[...] = lax.dot_general(
        weights, normed, (((1,), (1,)), ((), ())), preferred_element_type=jnp.float32
    ).astype(jnp.bfloat16)
    store.wait()


def embed(unit_slots, mine, slot_rows, gain, first_unit, lines, collective_id):
    slots, unit_rows, width = mine.shape
    tokens = slot_rows.shape[0]
    chunks = max(k for k in range(1, 8) if slots % k == 0)
    rows = 128
    half = width // 2
    sems = pltpu.SemaphoreType.DMA((2, chunks))
    line = pltpu.VMEM((2, tokens // rows, rows, half), jnp.bfloat16)
    return pl.pallas_call(
        functools.partial(embed_kernel, chunks, first_unit),
        out_shape=[
            jax.ShapeDtypeStruct((unit_slots.shape[0], unit_rows, width), jnp.bfloat16),
            jax.ShapeDtypeStruct((tokens, width), jnp.bfloat16),
            jax.ShapeDtypeStruct((tokens, width), jnp.bfloat16),
            jax.ShapeDtypeStruct((lines, tokens), jnp.bfloat16),
            jax.ShapeDtypeStruct((lines, width), jnp.bfloat16),
            jax.ShapeDtypeStruct((lines // 3, width), jnp.bfloat16),
        ],
        in_specs=[pl.BlockSpec(memory_space=pltpu.SMEM)] + [whole_vmem] * 3,
        out_specs=[whole_any] + [whole_vmem] * 5,
        scratch_shapes=[
            pltpu.VMEM((2, 8 * slots, unit_rows, half), jnp.bfloat16),
            pltpu.VMEM((2, tokens, half), jnp.float32),
            line,
            line,
            line,
            pltpu.VMEM((unit_slots.shape[0], unit_rows, width), jnp.bfloat16),
            pltpu.SemaphoreType.DMA,
        ]
        + [sems] * 6
        + [pltpu.SemaphoreType.DMA((2, 4, chunks))] * 2
        + [pltpu.SemaphoreType.DMA((2, tokens // rows))] * 5,
        compiler_params=pltpu.CompilerParams(
            collective_id=collective_id, has_side_effects=True, vmem_limit_bytes=60 << 20
        ),
    )(unit_slots, mine, slot_rows, gain)


def pull_units_kernel(parts, slots_ref, *refs):
    sources, out_ref, sem = refs[:parts], refs[parts], refs[parts + 1]
    width = out_ref.shape[-1] // parts

    def push(u, carry):
        for part in range(parts):
            pltpu.make_async_copy(
                sources[part].at[slots_ref[u]],
                out_ref.at[u, :, part * width : (part + 1) * width],
                sem,
            ).start()
        return carry

    lax.fori_loop(0, out_ref.shape[0], push, 0)
    pltpu.make_async_copy(out_ref, out_ref, sem).wait()


def pull_units(sources, slots):
    count = slots.shape[0]
    rows, width = sources[0].shape[1:]
    return pl.pallas_call(
        functools.partial(pull_units_kernel, len(sources)),
        out_shape=jax.ShapeDtypeStruct((count, rows, width * len(sources)), sources[0].dtype),
        in_specs=[pl.BlockSpec(memory_space=pltpu.SMEM)] + [whole_any] * len(sources),
        out_specs=whole_vmem,
        scratch_shapes=[pltpu.SemaphoreType.DMA],
        compiler_params=pltpu.CompilerParams(vmem_limit_bytes=40 << 20),
    )(slots, *sources)


def attention_kernel(
    heads, size, bias_ref, own_ref, out_ref, logsum_ref, before_ref, mine_ref,
    scores, peak, total, keys_sem, send_sem, recv_sem,
):
    tokens = own_ref.shape[1]
    blocks = tokens // BLOCK
    hidden = heads * size
    later = lax.axis_index("ctx") > 0
    rank = lax.axis_index("tensor")
    inner = (rank == 1) | (rank == 2)
    end_peer = jnp.where(rank < 2, 1 - rank, 5 - rank)
    mid_peer = 3 - rank
    mid_owner = jnp.where(inner, mid_peer, 3 - end_peer)
    far_owner = jnp.where(inner, 3 - end_peer, 3 - rank)
    other_core = {"ctx": 1 - lax.axis_index("ctx")}
    barrier = pltpu.get_barrier_semaphore()
    for place in (other_core, {"tensor": end_peer}):
        pl.semaphore_signal(barrier, inc=1, device_id=place, device_id_type=MESH_ID)

    @pl.when(inner)
    def _():
        pl.semaphore_signal(barrier, inc=1, device_id={"tensor": mid_peer}, device_id_type=MESH_ID)
        pl.semaphore_wait(barrier, 3)

    @pl.when(jnp.logical_not(inner))
    def _():
        pl.semaphore_wait(barrier, 2)

    pairs = pltpu.make_async_remote_copy(
        src_ref=own_ref.at[pl.ds(hidden, 2 * hidden)],
        dst_ref=before_ref,
        send_sem=keys_sem.at[0],
        recv_sem=keys_sem.at[1],
        device_id=other_core,
        device_id_type=MESH_ID,
    )

    @pl.when(jnp.logical_not(later))
    def _():
        pairs.start()
        before_ref[...] = jnp.zeros_like(before_ref)

    def flipped(rows):
        return rows.astype(jnp.float32).T.astype(jnp.bfloat16)

    @pl.when(later)
    def _():
        pairs.wait_recv()

    def sent(owner, block, peer, send, recv):
        piece = out_ref.at[owner, pl.ds(block * size, size), :]
        return pltpu.make_async_remote_copy(
            src_ref=piece,
            dst_ref=piece,
            send_sem=send_sem.at[block, send],
            recv_sem=recv_sem.at[block, recv],
            device_id={"tensor": peer},
            device_id_type=MESH_ID,
        )

    def own_to_end(block):
        return sent(rank, block, end_peer, 0, 0)

    def from_end(block):
        return sent(end_peer, block, end_peer, 0, 0)

    def own_to_middle(block):
        return sent(rank, block, mid_peer, 1, 1)

    def end_to_middle(block):
        return sent(end_peer, block, mid_peer, 2, 2)

    def middle_to_end(block):
        return sent(mid_owner, block, end_peer, 3, 1)

    def far_to_end(block):
        return sent(far_owner, block, end_peer, 4, 2)

    def hand_on(block, stages):
        @pl.when(inner)
        def _():
            if 0 in stages:
                from_end(block).wait_recv()
                end_to_middle(block).start()
                middle_to_end(block).wait_recv()
                middle_to_end(block).start()
            if 1 in stages:
                far_to_end(block).wait_recv()
                far_to_end(block).start()

    for head in range(heads):
        span = slice(head * size, (head + 1) * size)
        query = flipped(own_ref[span, :]) * jnp.bfloat16(size**-0.5)
        own_keys = own_ref[hidden + head * size : hidden + (head + 1) * size, :]
        own_values = flipped(
            own_ref[2 * hidden + head * size : 2 * hidden + (head + 1) * size, :]
        )
        old_values = flipped(before_ref[hidden + head * size : hidden + (head + 1) * size, :])
        for block in range(blocks):
            rows = query[block * BLOCK : (block + 1) * BLOCK]
            width = (block + 1) * BLOCK
            mine = jnp.dot(rows, own_keys[:, :width], preferred_element_type=jnp.float32)
            top = None
            parts = []
            for k in range(block + 1):
                part = mine[:, k * BLOCK : (k + 1) * BLOCK] + bias_ref[head, block - k]
                parts.append(part)
                high = jnp.max(part, 1, keepdims=True)
                top = high if top is None else jnp.maximum(top, high)
            peak[...] = top

            @pl.when(later)
            def _():
                old = jnp.dot(rows, before_ref[span, :], preferred_element_type=jnp.float32)
                top_old = None
                for k in range(blocks):
                    part = old[:, k * BLOCK : (k + 1) * BLOCK] + bias_ref[head, block + blocks - k]
                    scores[:, k * BLOCK : (k + 1) * BLOCK] = part
                    high = jnp.max(part, 1, keepdims=True)
                    top_old = high if top_old is None else jnp.maximum(top_old, high)
                peak[...] = jnp.maximum(peak[...], top_old)

            top = peak[...]
            parts = [jnp.exp(part - top) for part in parts]
            own_sum = None
            for part in parts:
                part_sum = jnp.sum(part, 1, keepdims=True)
                own_sum = part_sum if own_sum is None else own_sum + part_sum
            total[...] = own_sum

            @pl.when(later)
            def _():
                old_exp = jnp.exp(scores[...] - top)
                scores[...] = old_exp
                total[...] += jnp.sum(old_exp, 1, keepdims=True)

            full = total[...]
            inverse = 1.0 / full
            low = jnp.concatenate([(part * inverse).astype(jnp.bfloat16) for part in parts], 1)
            result = jnp.dot(low, own_values[:width], preferred_element_type=jnp.float32)
            logsum_ref[head, block * BLOCK : (block + 1) * BLOCK, :] = top + jnp.log(full)
            place = (rank, span, slice(block * BLOCK, (block + 1) * BLOCK))

            @pl.when(later)
            def _():
                low_old = (scores[...] * inverse).astype(jnp.bfloat16)
                both = result + jnp.dot(low_old, old_values, preferred_element_type=jnp.float32)
                out_ref[place] = both.T.astype(jnp.bfloat16)
                mine_ref[place[1:]] = both.T.astype(jnp.bfloat16)

            @pl.when(jnp.logical_not(later))
            def _():
                out_ref[place] = result.T.astype(jnp.bfloat16)
                mine_ref[place[1:]] = result.T.astype(jnp.bfloat16)

        own_to_end(head).start()

        @pl.when(inner)
        def _():
            own_to_middle(head).start()

        if head >= 1:
            hand_on(head - 1, (0,))
        if head >= 2:
            hand_on(head - 2, (1,))

    hand_on(heads - 1, (0,))
    hand_on(heads - 2, (1,))
    hand_on(heads - 1, (1,))
    for head in range(heads):
        own_to_end(head).wait_send()

        @pl.when(inner)
        def _():
            for copy in (own_to_middle, end_to_middle, middle_to_end, far_to_end):
                copy(head).wait_send()

        @pl.when(jnp.logical_not(inner))
        def _():
            from_end(head).wait_recv()
            middle_to_end(head).wait_recv()
            far_to_end(head).wait_recv()

    @pl.when(jnp.logical_not(later))
    def _():
        pairs.wait_send()


def attention(biases, own, heads, size, collective_id):
    tokens = own.shape[1]
    blocks = tokens // BLOCK
    return pl.pallas_call(
        functools.partial(attention_kernel, heads, size),
        out_shape=[
            jax.ShapeDtypeStruct((4, heads * size, tokens), jnp.bfloat16),
            jax.ShapeDtypeStruct((heads, tokens, 1), jnp.float32),
            jax.ShapeDtypeStruct((2 * heads * size, tokens), jnp.bfloat16),
            jax.ShapeDtypeStruct((heads * size, tokens), jnp.bfloat16),
        ],
        in_specs=[pl.BlockSpec(memory_space=pltpu.SMEM), whole_vmem],
        out_specs=[whole_vmem] * 4,
        scratch_shapes=[
            pltpu.VMEM((BLOCK, tokens), jnp.float32),
            pltpu.VMEM((BLOCK, 1), jnp.float32),
            pltpu.VMEM((BLOCK, 1), jnp.float32),
            pltpu.SemaphoreType.DMA((2,)),
            pltpu.SemaphoreType.DMA((heads, 5)),
            pltpu.SemaphoreType.DMA((heads, 3)),
        ],
        compiler_params=pltpu.CompilerParams(
            collective_id=collective_id, has_side_effects=True, vmem_limit_bytes=40 << 20
        ),
    )(biases, own)


def attention_back_kernel(
    heads, size, bias_ref, own_ref, before_ref, logsum_ref, grad_ref, project_ref,
    *refs
):
    states, (query_out, own_out, before_out, bias_out) = refs[:8], refs[8:12]
    updated, (probs, slopes, inner, query_sum, own_sum, before_sum) = refs[12:18], refs[18:24]
    held, load_sem, store_sem = refs[24:]
    loads = [pltpu.make_async_copy(states[k], held.at[k], load_sem.at[k]) for k in range(8)]
    stores = [
        pltpu.make_async_copy(held.at[4 * (k // 3) + k % 3], updated[k], store_sem.at[k])
        for k in range(6)
    ]
    for load in loads:
        load.start()

    def update(i, carry):
        lines = held.shape[1] // 16
        span = pl.ds(pl.multiple_of(i * lines, lines), lines)
        for k, rate in enumerate((rate_inner, rate_outer)):
            fresh = adam_update(*(held[4 * k + n, span] for n in range(4)), rate, decay_rate)
            for n in range(3):
                held[4 * k + n, span] = fresh[n]
        return carry

    tokens = own_ref.shape[1]
    blocks = tokens // BLOCK
    hidden = heads * size
    later = lax.axis_index("ctx") > 0
    bias_out[...] = jnp.zeros_like(bias_out)

    def flipped(rows):
        return rows.astype(jnp.float32).T.astype(jnp.bfloat16)

    for head in range(heads):
        span = slice(head * size, (head + 1) * size)
        value_span = slice(hidden + head * size, hidden + (head + 1) * size)
        query_rows = own_ref[span, :]
        query = flipped(query_rows) * jnp.bfloat16(size**-0.5)
        own_keys = own_ref[hidden + head * size : hidden + (head + 1) * size, :]
        own_values = own_ref[2 * hidden + head * size : 2 * hidden + (head + 1) * size, :]
        old_keys = before_ref[span, :]
        old_values = before_ref[value_span, :]
        own_keys_flip = flipped(own_keys)
        grad = lax.dot_general(
            grad_ref[...], project_ref[span, :], (((1,), (1,)), ((), ())), preferred_element_type=jnp.float32
        )
        grad_rows = grad.T.astype(jnp.bfloat16)
        grad = grad.astype(jnp.bfloat16)
        own_sum[...] = jnp.zeros_like(own_sum)

        @pl.when(later)
        def _():
            before_sum[...] = jnp.zeros_like(before_sum)

        for block in range(blocks):
            at = slice(block * BLOCK, (block + 1) * BLOCK)
            width = (block + 1) * BLOCK
            rows, up = query[at], grad[at]
            lse = logsum_ref[head, at, :]
            score = jnp.dot(rows, own_keys[:, :width], preferred_element_type=jnp.float32)
            prob = jnp.concatenate(
                [
                    jnp.exp(score[:, k * BLOCK : (k + 1) * BLOCK] + (bias_ref[head, block - k] - lse))
                    for k in range(block + 1)
                ],
                1,
            )
            slope = jnp.dot(up, own_values[:, :width], preferred_element_type=jnp.float32)
            inner[...] = jnp.sum(prob * slope, 1, keepdims=True)

            @pl.when(later)
            def _():
                score = jnp.dot(rows, old_keys, preferred_element_type=jnp.float32)
                old_slope = jnp.dot(up, old_values, preferred_element_type=jnp.float32)
                old_prob = jnp.concatenate(
                    [
                        jnp.exp(
                            score[:, k * BLOCK : (k + 1) * BLOCK]
                            + (bias_ref[head, block + blocks - k] - lse)
                        )
                        for k in range(blocks)
                    ],
                    1,
                )
                probs[...] = old_prob
                slopes[...] = old_slope
                inner[...] += jnp.sum(old_prob * old_slope, 1, keepdims=True)

            row_inner = inner[...]
            low_grad = (prob * (slope - row_inner)).astype(jnp.bfloat16)
            query_sum[...] = jnp.dot(
                low_grad, own_keys_flip[:width], preferred_element_type=jnp.float32
            )
            own_sum[:size, :width] += jnp.dot(
                query_rows[:, at], low_grad, preferred_element_type=jnp.float32
            )
            own_sum[size:, :width] += jnp.dot(
                grad_rows[:, at], prob.astype(jnp.bfloat16), preferred_element_type=jnp.float32
            )
            for k in range(block + 1):
                line = head * 2 * blocks + block - k
                bias_out[line : line + 1, :] += jnp.sum(
                    low_grad[:, k * BLOCK : (k + 1) * BLOCK].astype(jnp.float32), 0, keepdims=True
                )

            @pl.when(later)
            def _():
                old_prob = probs[...]
                low_old = (old_prob * (slopes[...] - row_inner)).astype(jnp.bfloat16)
                query_sum[...] += jnp.dot(
                    low_old, flipped(old_keys), preferred_element_type=jnp.float32
                )
                before_sum[:size, :] += jnp.dot(
                    query_rows[:, at], low_old, preferred_element_type=jnp.float32
                )
                before_sum[size:, :] += jnp.dot(
                    grad_rows[:, at], old_prob.astype(jnp.bfloat16), preferred_element_type=jnp.float32
                )
                for k in range(blocks):
                    line = head * 2 * blocks + block + blocks - k
                    bias_out[line : line + 1, :] += jnp.sum(
                        low_old[:, k * BLOCK : (k + 1) * BLOCK].astype(jnp.float32), 0, keepdims=True
                    )

            query_out[span, at] = (query_sum[...].T * size**-0.5).astype(jnp.bfloat16)

        own_out[span, :] = own_sum[:size, :] * size**-0.5
        own_out[value_span, :] = own_sum[size:, :]

        @pl.when(later)
        def _():
            before_out[span, :] = (before_sum[:size, :] * size**-0.5).astype(jnp.bfloat16)
            before_out[value_span, :] = before_sum[size:, :].astype(jnp.bfloat16)

        if head == 0:
            for load in loads:
                load.wait()
            lax.fori_loop(0, 16, update, 0)
            for store in stores:
                store.start()

    @pl.when(jnp.logical_not(later))
    def _():
        before_out[...] = jnp.zeros_like(before_out)

    for store in stores:
        store.wait()


def attention_back(biases, own, before, logsum, grad, project, states, heads, size):
    tokens = own.shape[1]
    hidden = heads * size
    return pl.pallas_call(
        functools.partial(attention_back_kernel, heads, size),
        out_shape=[
            jax.ShapeDtypeStruct((hidden, tokens), jnp.bfloat16),
            jax.ShapeDtypeStruct((2 * hidden, tokens), jnp.float32),
            jax.ShapeDtypeStruct((2 * hidden, tokens), jnp.bfloat16),
            jax.ShapeDtypeStruct((heads * 2 * (tokens // BLOCK), BLOCK), jnp.float32),
        ]
        + [jax.ShapeDtypeStruct(states[0].shape, jnp.float32)] * 6,
        in_specs=[pl.BlockSpec(memory_space=pltpu.SMEM)] + [whole_vmem] * 5 + [whole_any] * 8,
        out_specs=[whole_vmem] * 4 + [whole_any] * 6,
        scratch_shapes=[
            pltpu.VMEM((BLOCK, tokens), jnp.float32),
            pltpu.VMEM((BLOCK, tokens), jnp.float32),
            pltpu.VMEM((BLOCK, 1), jnp.float32),
            pltpu.VMEM((BLOCK, size), jnp.float32),
            pltpu.VMEM((2 * size, tokens), jnp.float32),
            pltpu.VMEM((2 * size, tokens), jnp.float32),
            pltpu.VMEM((8,) + states[0].shape, jnp.float32),
            pltpu.SemaphoreType.DMA((8,)),
            pltpu.SemaphoreType.DMA((6,)),
        ],
        compiler_params=pltpu.CompilerParams(vmem_limit_bytes=48 << 20),
    )(biases, own, before, logsum, grad, project, *states)


def vocab_tile(vocab):
    return max(k for k in range(16, 1601, 16) if vocab % k == 0)


def head_line_kernel(
    tile, part_ref, stream_ref, gain_ref, table_ref, wanted_ref, weight_ref,
    low_ref, grad_low_ref, grad_ref, gain_grad, logsum_ref, picked_ref, slopes_ref,
    logits, table, stage, from_end, from_mid, own, turned, stats, landed, slope_tiles, total,
    load_sem, send_sem, end_sem, mid_sem, back_sem, back_recv, stat_send, stat_recv, store_sem,
):
    rank = lax.axis_index("tensor")
    inner = (rank == 1) | (rank == 2)
    end_peer = jnp.where(rank < 2, 1 - rank, 5 - rank)
    mid_peer = 3 - rank
    count, rows = stage.shape[:2]
    columns = turned.shape[1]
    pieces = table.shape[0] // tile
    group = columns // rows
    tiles = count // group
    vocab = table.shape[0]
    load = pltpu.make_async_copy(table_ref.at[pl.ds(0, vocab)], table, load_sem)
    load.start()
    barrier = pltpu.get_barrier_semaphore()
    for step in (1, 2, 3):
        other = lax.rem(rank + step, 4)
        pl.semaphore_signal(barrier, inc=1, device_id={"tensor": other}, device_id_type=MESH_ID)
    pl.semaphore_wait(barrier, 3)

    def span(i):
        return pl.ds(pl.multiple_of(i * rows, rows), rows)

    def over(t):
        return pl.ds(pl.multiple_of(t * columns, columns), columns)

    def line_copy(source, target, send, recv, peer):
        return pltpu.make_async_remote_copy(
            src_ref=source,
            dst_ref=target,
            send_sem=send,
            recv_sem=recv,
            device_id={"tensor": peer},
            device_id_type=MESH_ID,
        )

    def to_inner(i):
        return line_copy(stage.at[i], from_end.at[i], send_sem.at[i], end_sem.at[i], end_peer)

    def to_middle(i):
        return line_copy(stage.at[i], from_mid.at[i], send_sem.at[i], mid_sem.at[i], mid_peer)

    def to_end(ref, i):
        rows_of = ref.at[span(i)]
        return line_copy(rows_of, rows_of, back_sem.at[i], back_recv.at[i], end_peer)

    def repeat(first, last, body):
        def step(i, carry):
            body(i)
            return carry

        lax.fori_loop(first, last, step, 0)

    def turn(t):
        turned[...] = low_ref[over(t)].astype(jnp.float32).T.astype(jnp.bfloat16)

    def table_rows(k):
        return table[k * tile : (k + 1) * tile]

    def first_logits(t):
        turn(t)
        logits[0] = jnp.dot(table_rows(0), turned[...], preferred_element_type=jnp.float32)

    def next_logits(k):
        if k + 1 < pieces:
            logits[(k + 1) % 2] = jnp.dot(
                table_rows(k + 1), turned[...], preferred_element_type=jnp.float32
            )

    def sums_unit(t, k):
        next_logits(k)
        before = stats[0:1, over(t)]
        top = jnp.maximum(before, jnp.max(logits[k % 2], 0, keepdims=True))
        stats[1:2, over(t)] = stats[1:2, over(t)] * jnp.exp(before - top) + jnp.sum(
            jnp.exp(logits[k % 2] - top), 0, keepdims=True
        )
        stats[0:1, over(t)] = top

    def sums_tile(t):
        first_logits(t)
        for k in range(pieces):
            sums_unit(t, k)

    stats[0:1, :] = jnp.full_like(stats[0:1, :], masked_score)
    stats[1:2, :] = jnp.zeros_like(stats[1:2, :])

    @pl.when(jnp.logical_not(inner))
    def _():
        def push(i):
            stage[i] = part_ref[span(i)].astype(jnp.bfloat16)
            to_inner(i).start()

        repeat(0, count, push)
        load.wait()

        def forward(t):
            repeat(0, group, lambda c: to_end(low_ref, t * group + c).wait_recv())
            sums_tile(t)

        repeat(0, tiles, forward)
        repeat(0, count, lambda i: to_inner(i).wait_send())

    @pl.when(inner)
    def _():
        gain_grad[...] = jnp.zeros_like(gain_grad)
        load.wait()

        def gather(i):
            to_inner(i).wait_recv()
            mine = part_ref[span(i)] + from_end[i].astype(jnp.float32)
            stage[i] = mine.astype(jnp.bfloat16)
            to_middle(i).start()

        def settle_rows(j):
            to_middle(j).wait_recv()
            stream_two = stream_ref[span(j)] + (
                stage[j].astype(jnp.float32) + from_mid[j].astype(jnp.float32)
            )
            grad_ref[span(j)] = stream_two
            low_ref[span(j)] = (stream_two * inverse_rms(stream_two) * gain_ref[...]).astype(
                jnp.bfloat16
            )
            to_end(low_ref, j).start()

        turns = [[k for k in range(pieces) if k * (group - 1) // pieces == c - 1] for c in range(group)]

        def advance(t):
            for c in range(group):
                i = t * group + c
                gather(i)

                @pl.when(i >= line_lag)
                def _():
                    settle_rows(i - line_lag)

                if turns[c]:

                    @pl.when(t >= 1)
                    def _():
                        if c == 1:
                            first_logits(t - 1)
                        for k in turns[c]:
                            sums_unit(t - 1, k)

        repeat(0, tiles, advance)
        repeat(count - line_lag, count, settle_rows)
        sums_tile(tiles - 1)

        def drain(i):
            to_middle(i).wait_send()
            to_end(low_ref, i).wait_send()

        repeat(0, count, drain)

    copies = [
        line_copy(
            stats, landed.at[step - 1], stat_send.at[step - 1], stat_recv.at[step - 1], lax.rem(rank + step, 4)
        )
        for step in (1, 2, 3)
    ]
    for copy in copies:
        copy.start()
    for copy in copies:
        copy.wait()
    tops, sums = [], []
    for source in range(4):
        piece = stats[...]
        for step in (1, 2, 3):
            piece = jnp.where(lax.rem(source + step, 4) == rank, landed[step - 1], piece)
        tops.append(piece[0:1])
        sums.append(piece[1:2])
    top = jnp.maximum(jnp.maximum(tops[0], tops[1]), jnp.maximum(tops[2], tops[3]))
    whole = sums[0] * jnp.exp(tops[0] - top)
    for source in (1, 2, 3):
        whole = whole + sums[source] * jnp.exp(tops[source] - top)
    logsum_ref[...] = top + jnp.log(whole)
    picked_ref[...] = jnp.zeros_like(picked_ref)

    def store(t):
        return pltpu.make_async_copy(
            slope_tiles.at[lax.rem(t, 2)], slopes_ref.at[:, over(t)], store_sem.at[lax.rem(t, 2)]
        )

    def slope_unit(t, k):
        values = logits[k % 2]
        row = lax.broadcasted_iota(jnp.int32, values.shape, 0)
        base = k * tile
        hits = jnp.where(row == wanted_ref[0:1, over(t)] - base, weight_ref[0:1, over(t)], 0.0)
        hits = hits + jnp.where(
            row == wanted_ref[1:2, over(t)] - base, weight_ref[1:2, over(t)], 0.0
        )
        picked_ref[:, over(t)] += jnp.sum(hits * values, 0, keepdims=True)
        softmax = jnp.exp(values - logsum_ref[:, over(t)])
        slope_tiles[lax.rem(t, 2), base : base + tile] = (
            (weight_ref[2:3, over(t)] * softmax - hits) * weight_ref[3:4, over(t)]
        ).astype(jnp.bfloat16)

    def add_rows(t, k):
        total[...] += lax.dot_general(
            slope_tiles[lax.rem(t, 2), k * tile : (k + 1) * tile],
            table_rows(k),
            (((0,), (0,)), ((), ())),
            preferred_element_type=jnp.float32,
        )

    def settle(j):
        to_middle(j).wait_recv()
        upstream = stage[j].astype(jnp.float32) + from_mid[j].astype(jnp.float32)
        grad_two, gain_part = norm_back_rows(grad_ref[span(j)], gain_ref[...], upstream)
        grad_ref[span(j)] = grad_two
        gain_grad[...] += gain_part
        grad_low_ref[span(j)] = grad_two.astype(jnp.bfloat16)
        to_end(grad_low_ref, j).start()

    def exchange(i):
        to_inner(i).wait_recv()
        stage[i] = (own[span(i)] + from_end[i].astype(jnp.float32)).astype(jnp.bfloat16)
        to_middle(i).start()

        @pl.when(i >= line_lag)
        def _():
            settle(i - line_lag)

    def back_tile(t):
        @pl.when(t >= 2)
        def _():
            store(t - 2).wait()

        total[...] = jnp.zeros_like(total)
        first_logits(t)
        for k in range(pieces):
            next_logits(k)
            slope_unit(t, k)
            if k >= 1:
                add_rows(t, k - 1)
            if k >= pieces - group:

                @pl.when(inner & (t >= 1))
                def _():
                    exchange((t - 1) * group + k - (pieces - group))

        add_rows(t, pieces - 1)
        store(t).start()

        @pl.when(inner)
        def _():
            own[over(t)] = total[...]

        @pl.when(jnp.logical_not(inner))
        def _():
            def push(c):
                stage[t * group + c] = total[span(c)].astype(jnp.bfloat16)
                to_inner(t * group + c).start()

            repeat(0, group, push)

    repeat(0, tiles, back_tile)

    @pl.when(jnp.logical_not(inner))
    def _():
        def finish(i):
            to_end(grad_low_ref, i).wait_recv()
            to_inner(i).wait_send()

        repeat(0, count, finish)

    @pl.when(inner)
    def _():
        repeat(count - group, count, exchange)
        repeat(count - line_lag, count, settle)

        def drain(i):
            to_middle(i).wait_send()
            to_end(grad_low_ref, i).wait_send()

        repeat(0, count, drain)

    store(tiles - 2).wait()
    store(tiles - 1).wait()


def head_line(part, stream, gain, weights, wanted, weight_rows, vocab, collective_id):
    tokens, width = part.shape
    rows, columns = 64, 256
    count = tokens // rows
    chunks = pltpu.VMEM((count, rows, width), jnp.bfloat16)
    rows_low = jax.ShapeDtypeStruct((tokens, width), jnp.bfloat16)
    along = jax.ShapeDtypeStruct((1, tokens), jnp.float32)
    line_sems = pltpu.SemaphoreType.DMA((count,))
    return pl.pallas_call(
        functools.partial(head_line_kernel, vocab_tile(vocab)),
        out_shape=[
            rows_low,
            rows_low,
            jax.ShapeDtypeStruct((tokens, width), jnp.float32),
            jax.ShapeDtypeStruct((1, width), jnp.float32),
            along,
            along,
            jax.ShapeDtypeStruct((vocab, tokens), jnp.bfloat16),
        ],
        in_specs=[whole_vmem] * 3 + [whole_any] + [whole_vmem] * 2,
        out_specs=[whole_vmem] * 6 + [whole_any],
        scratch_shapes=[
            pltpu.VMEM((2, vocab_tile(vocab), columns), jnp.float32),
            pltpu.VMEM((vocab, width), jnp.bfloat16),
            chunks,
            chunks,
            chunks,
            pltpu.VMEM((tokens, width), jnp.float32),
            pltpu.VMEM((width, columns), jnp.bfloat16),
            pltpu.VMEM((2, tokens), jnp.float32),
            pltpu.VMEM((3, 2, tokens), jnp.float32),
            pltpu.VMEM((2, vocab, columns), jnp.bfloat16),
            pltpu.VMEM((columns, width), jnp.float32),
            pltpu.SemaphoreType.DMA,
        ]
        + [line_sems] * 5
        + [pltpu.SemaphoreType.DMA((3,))] * 2
        + [pltpu.SemaphoreType.DMA((2,))],
        compiler_params=pltpu.CompilerParams(
            collective_id=collective_id, has_side_effects=True, vmem_limit_bytes=62 << 20
        ),
    )(part, stream, gain, weights, wanted, weight_rows)


def weight_grads_kernel(
    tile_units, tiles, place_ref, slope_ref, rows_ref, ids_ref, zero_ref, joint_ref, normed_ref,
    attended_ref, grad_ref, out_ref, made, sem,
):
    step = pl.program_id(0)
    unit_rows = out_ref.shape[1]
    buffer = lax.rem(step, 2)
    last_units = joint_ref.shape[0] // unit_rows + attended_ref.shape[0] // unit_rows

    def settle(which, count):
        pltpu.make_async_copy(
            made.at[which, pl.ds(0, count)], made.at[which, pl.ds(0, count)], sem.at[which]
        ).wait()

    def send(first, count):
        def push(u, carry):
            pltpu.make_async_copy(
                made.at[buffer, u], out_ref.at[place_ref[first + u]], sem.at[buffer]
            ).start()
            return carry

        lax.fori_loop(0, count, push, 0)

    @pl.when(step >= 2)
    def _():
        settle(buffer, tile_units)

    @pl.when(step < tiles)
    def _():
        row = lax.broadcasted_iota(jnp.int32, slope_ref.shape, 0)
        seen = jnp.where(row == ids_ref[...] - step * slope_ref.shape[0], 1.0, 0.0).astype(jnp.bfloat16)
        made[buffer] = (
            jnp.dot(slope_ref[...], rows_ref[...], preferred_element_type=jnp.float32)
            + jnp.dot(seen, zero_ref[...], preferred_element_type=jnp.float32)
        ).astype(jnp.bfloat16).reshape(tile_units, unit_rows, -1)
        send(step * tile_units, tile_units)

    @pl.when(step == tiles)
    def _():
        joint_units = joint_ref.shape[0] // unit_rows
        made[buffer, pl.ds(0, joint_units)] = jnp.dot(
            joint_ref[...], normed_ref[...], preferred_element_type=jnp.float32
        ).astype(jnp.bfloat16).reshape(joint_units, unit_rows, -1)
        made[buffer, pl.ds(joint_units, last_units - joint_units)] = jnp.dot(
            attended_ref[...], grad_ref[...], preferred_element_type=jnp.float32
        ).astype(jnp.bfloat16).reshape(last_units - joint_units, unit_rows, -1)
        send(tiles * tile_units, last_units)
        settle(1 - buffer, tile_units)
        settle(buffer, last_units)


def weight_grads(place, slots, unit_rows, slope, rows, ids, zero, joint, normed, attended, grad):
    vocab, tokens = slope.shape
    width = rows.shape[1]
    tile = vocab_tile(vocab)
    tiles = vocab // tile
    fixed = lambda k: (0, 0)
    whole = lambda x: pl.BlockSpec(x.shape, fixed)
    return pl.pallas_call(
        functools.partial(weight_grads_kernel, tile // unit_rows, tiles),
        grid=(tiles + 1,),
        out_shape=jax.ShapeDtypeStruct((slots, unit_rows, width), jnp.bfloat16),
        in_specs=[
            pl.BlockSpec(memory_space=pltpu.SMEM),
            pl.BlockSpec((tile, tokens), lambda k: (jnp.minimum(k, tiles - 1), 0)),
        ]
        + [whole(x) for x in (rows, ids, zero, joint, normed, attended, grad)],
        out_specs=whole_any,
        scratch_shapes=[
            pltpu.VMEM((2, tile // unit_rows, unit_rows, width), jnp.bfloat16),
            pltpu.SemaphoreType.DMA((2,)),
        ],
        compiler_params=pltpu.CompilerParams(vmem_limit_bytes=60 << 20),
    )(place, slope, rows, ids, zero, joint, normed, attended, grad)


def adam_update(weight, moment_one, moment_two, gradient, step_rate, decay_factor):
    moment_new = beta_first * moment_one + (1.0 - beta_first) * gradient
    square_new = beta_second * moment_two + (1.0 - beta_second) * gradient * gradient
    moment_hat = moment_new / (1.0 - beta_first**STEP)
    square_hat = square_new / (1.0 - beta_second**STEP)
    weight_new = weight - step_rate * (
        moment_hat / (jnp.sqrt(square_hat) + adam_epsilon) + decay_factor * weight
    )
    return (weight_new, moment_new, square_new)


def norm_forward(values, gain_row):
    return values * inverse_rms(values) * gain_row


def slot_tables(owner_ids, owners, most_units):
    unit_count = owner_ids.shape[0]
    unit_index = jnp.arange(unit_count, dtype=jnp.int32)
    earlier = (owner_ids[None, :] == owner_ids[:, None]) & (
        unit_index[None, :] < unit_index[:, None]
    )
    unit_rank = jnp.sum(earlier.astype(jnp.int32), 1)
    placed = (owner_ids[None, None, :] == jnp.arange(owners, dtype=jnp.int32)[:, None, None]) & (
        unit_rank[None, None, :] == jnp.arange(most_units, dtype=jnp.int32)[None, :, None]
    )
    slot_filled = jnp.any(placed, 2)
    slot_unit = jnp.sum(jnp.where(placed, unit_index[None, None, :], 0), 2)
    return (unit_rank, slot_unit, slot_filled)


def unit_rates(unit_ids, table_units, query_units, value_units):
    return jnp.where(
        unit_ids < table_units,
        rate_table,
        jnp.where(
            unit_ids < query_units,
            rate_query,
            jnp.where(unit_ids < value_units, rate_values, rate_project),
        ),
    )


def pair_slots(route_pairs, priorities, experts, capacity):
    tokens_here = priorities.shape[0]
    pair_expert = route_pairs.T.reshape(-1)
    pair_key = (
        jnp.arange(2, dtype=jnp.int32)[:, None] * tokens_here + priorities[None, :]
    ).reshape(-1)
    before = (pair_expert[None, :] == pair_expert[:, None]) & (
        pair_key[None, :] < pair_key[:, None]
    )
    pair_rank = jnp.sum(before.astype(jnp.int32), 1)
    pair_kept = pair_rank < capacity
    pair_dest = pair_expert * capacity + jnp.minimum(pair_rank, capacity - 1)
    return (pair_kept, pair_dest)


def gelu_tanh(values):
    return jax.nn.gelu(values, approximate=True)


def gelu_slope(values):
    root = math.sqrt(2.0 / math.pi)
    bent = jnp.tanh(root * (values + 0.044715 * values * values * values))
    return 0.5 * (1.0 + bent) + 0.5 * values * (1.0 - bent * bent) * root * (
        1.0 + 3.0 * 0.044715 * values * values
    )


def plane_peer(step):
    chip, core = lax.axis_index("dp"), lax.axis_index("ctx")
    row = lax.rem(chip // 2 + step // 4, 2)
    column = lax.rem(lax.rem(chip, 2) + lax.rem(step // 2, 2), 2)
    place = {"dp": row * 2 + column, "ctx": lax.rem(core + lax.rem(step, 2), 2)}
    return place, place["dp"] * 2 + place["ctx"]


def greet_plane():
    barrier = pltpu.get_barrier_semaphore()
    for step in range(1, 8):
        place, _ = plane_peer(step)
        pl.semaphore_signal(barrier, inc=1, device_id=place, device_id_type=MESH_ID)
    pl.semaphore_wait(barrier, 7)


def plane_copy(source, target, send_sem, recv_sem, step):
    place, _ = plane_peer(step)
    return pltpu.make_async_remote_copy(
        src_ref=source.at[step],
        dst_ref=target.at[step],
        send_sem=send_sem.at[step],
        recv_sem=recv_sem.at[step],
        device_id=place,
        device_id_type=MESH_ID,
    )


def slot_hits(dest_rows, expert, capacity, tokens):
    slot = lax.broadcasted_iota(jnp.int32, (capacity, tokens), 0) + expert * capacity
    return (slot == dest_rows[0:1, :]) | (slot == dest_rows[1:2, :])


def token_hits(dest_columns, expert, capacity, tokens):
    slot = lax.broadcasted_iota(jnp.int32, (tokens, capacity), 1) + expert * capacity
    hit = (slot == dest_columns[:, 0:1]) | (slot == dest_columns[:, 1:2])
    return jnp.where(hit, 1.0, 0.0).astype(jnp.bfloat16)


def gate_of(routes, gates, expert, axis):
    pick = (lambda a, k: a[k : k + 1, :]) if axis == 0 else (lambda a, k: a[:, k : k + 1])
    return jnp.where(pick(routes, 0) == expert, pick(gates, 0), 0.0) + jnp.where(
        pick(routes, 1) == expert, pick(gates, 1), 0.0
    )


def arrival(i):
    return jnp.where(i < 2, i, 9 - i)


def experts_kernel(
    rows_ref, dest_rows, dest_columns, gates, routes, inner_full, outer_full, counts_ref,
    mix_ref, arrived, returned, totals_ref,
    inner_ref, outer_ref, outgoing, results, counts, send_one, recv_one, send_two, recv_two, send_count, recv_count,
):
    capacity = arrived.shape[1]
    tokens = rows_ref.shape[0]
    greet_plane()
    counts[0] = counts_ref[...]

    def send_counts(step, carry):
        place, _ = plane_peer(step)
        pltpu.make_async_remote_copy(
            src_ref=counts_ref,
            dst_ref=counts.at[step],
            send_sem=send_count.at[step],
            recv_sem=recv_count.at[step],
            device_id=place,
            device_id_type=MESH_ID,
        ).start()
        return carry

    def dispatch(i, carry):
        step = 7 - i
        _, expert = plane_peer(step)
        hit = jnp.where(slot_hits(dest_rows, expert, capacity, tokens), 1.0, 0.0).astype(jnp.bfloat16)
        rows = jnp.dot(hit, rows_ref[...], preferred_element_type=jnp.float32).astype(jnp.bfloat16)

        @pl.when(step > 0)
        def _():
            outgoing[step] = rows
            plane_copy(outgoing, arrived, send_one, recv_one, step).start()

        @pl.when(step == 0)
        def _():
            arrived[0] = rows

        return carry

    def work(i, carry):
        step = arrival(i)

        @pl.when(step > 0)
        def _():
            plane_copy(outgoing, arrived, send_one, recv_one, step).wait_recv()

        before = jnp.dot(arrived[step], inner_ref[...], preferred_element_type=jnp.float32)
        active = gelu_tanh(before).astype(jnp.bfloat16)
        part = jnp.dot(active, outer_ref[...], preferred_element_type=jnp.float32).astype(jnp.bfloat16)

        @pl.when(step > 0)
        def _():
            results[step] = part
            plane_copy(results, returned, send_two, recv_two, step).start()

        @pl.when(step == 0)
        def _():
            returned[0] = part

        return carry

    def combine(i, carry):
        step = arrival(i)
        _, expert = plane_peer(step)
        hit = token_hits(dest_columns, expert, capacity, tokens)
        gate = gate_of(routes, gates, expert, 1)

        @pl.when(step > 0)
        def _():
            plane_copy(results, returned, send_two, recv_two, step).wait_recv()

        part = gate * jnp.dot(hit, returned[step], preferred_element_type=jnp.float32)

        @pl.when(i == 0)
        def _():
            mix_ref[...] = part

        @pl.when(i > 0)
        def _():
            mix_ref[...] += part

        return carry

    def finish(step, carry):
        plane_copy(outgoing, arrived, send_one, recv_one, step).wait_send()
        plane_copy(results, returned, send_two, recv_two, step).wait_send()
        place, _ = plane_peer(step)
        pltpu.make_async_remote_copy(
            src_ref=counts_ref,
            dst_ref=counts.at[step],
            send_sem=send_count.at[step],
            recv_sem=recv_count.at[step],
            device_id=place,
            device_id_type=MESH_ID,
        ).wait()
        return carry

    lax.fori_loop(0, 8, dispatch, 0)
    lax.fori_loop(1, 8, send_counts, 0)
    inner_ref[...] = inner_full[...].astype(jnp.bfloat16)
    outer_ref[...] = outer_full[...].astype(jnp.bfloat16)
    lax.fori_loop(0, 8, work, 0)
    lax.fori_loop(0, 8, combine, 0)
    lax.fori_loop(1, 8, finish, 0)
    totals_ref[...] = jnp.sum(counts[...], 0)


def experts_forward(rows, dest, gates, routes, inner, outer, counts, capacity, collective_id):
    tokens, width = rows.shape
    buffer = pltpu.VMEM((8, capacity, width), jnp.bfloat16)
    return pl.pallas_call(
        experts_kernel,
        out_shape=[
            jax.ShapeDtypeStruct((tokens, width), jnp.float32),
            jax.ShapeDtypeStruct((8, capacity, width), jnp.bfloat16),
            jax.ShapeDtypeStruct((8, capacity, width), jnp.bfloat16),
            jax.ShapeDtypeStruct(counts.shape, jnp.float32),
        ],
        in_specs=[whole_vmem] * 8,
        out_specs=[whole_vmem] * 4,
        scratch_shapes=[pltpu.VMEM(w.shape, jnp.bfloat16) for w in (inner, outer)]
        + [buffer, buffer, pltpu.VMEM((8,) + counts.shape, jnp.float32)]
        + [pltpu.SemaphoreType.DMA((8,))] * 6,
        compiler_params=pltpu.CompilerParams(
            collective_id=collective_id, has_side_effects=True, vmem_limit_bytes=60 << 20
        ),
    )(rows, dest, dest.T, gates, routes, inner, outer, counts)


def experts_back_kernel(
    rows_ref, dest_rows, dest_columns, gates, routes, returned, arrived, *refs
):
    inner_full, outer_full, grad_ref, gate_ref, inner_grad, outer_grad, inner_ref, outer_ref = refs[:8]
    outgoing, landed, results, landed_two, active, slopes = refs[8:14]
    send_one, recv_one, send_two, recv_two = refs[14:]
    capacity = arrived.shape[1]
    tokens = rows_ref.shape[0]
    greet_plane()
    gate_ref[...] = jnp.zeros_like(gate_ref)

    def dispatch(i, carry):
        step = 7 - i
        _, expert = plane_peer(step)
        hit = slot_hits(dest_rows, expert, capacity, tokens)
        rows = jnp.dot(
            jnp.where(hit, 1.0, 0.0).astype(jnp.bfloat16), rows_ref[...], preferred_element_type=jnp.float32
        )
        scale = jnp.sum(jnp.where(hit, gate_of(routes, gates, expert, 0), 0.0), 1, keepdims=True)
        sent = (rows * scale).astype(jnp.bfloat16)

        @pl.when(step > 0)
        def _():
            outgoing[step] = sent
            plane_copy(outgoing, landed, send_one, recv_one, step).start()

        @pl.when(step == 0)
        def _():
            landed[0] = sent

        dots = jnp.sum(rows * returned[step].astype(jnp.float32), 1, keepdims=True)
        part = jnp.sum(jnp.where(hit, dots, 0.0), 0, keepdims=True)
        for k in range(2):
            gate_ref[k : k + 1, :] += jnp.where(routes[k : k + 1, :] == expert, part, 0.0)
        return carry

    def work(i, carry):
        step = arrival(i)

        @pl.when(step > 0)
        def _():
            plane_copy(outgoing, landed, send_one, recv_one, step).wait_recv()

        grad_active = lax.dot_general(
            landed[step], outer_ref[...], (((1,), (1,)), ((), ())), preferred_element_type=jnp.float32
        )
        before = jnp.dot(arrived[step], inner_ref[...], preferred_element_type=jnp.float32)
        slope = (grad_active * gelu_slope(before)).astype(jnp.bfloat16)
        back = lax.dot_general(
            slope, inner_ref[...], (((1,), (1,)), ((), ())), preferred_element_type=jnp.float32
        ).astype(jnp.bfloat16)

        @pl.when(step > 0)
        def _():
            results[step] = back
            plane_copy(results, landed_two, send_two, recv_two, step).start()

        @pl.when(step == 0)
        def _():
            landed_two[0] = back

        slopes[step] = slope
        active[step] = gelu_tanh(before).astype(jnp.bfloat16)
        return carry

    def weigh(step, carry):
        outer_part = lax.dot_general(
            active[step], landed[step], (((0,), (0,)), ((), ())), preferred_element_type=jnp.float32
        )
        inner_part = lax.dot_general(
            arrived[step], slopes[step], (((0,), (0,)), ((), ())), preferred_element_type=jnp.float32
        )

        @pl.when(step == 0)
        def _():
            inner_grad[...] = inner_part
            outer_grad[...] = outer_part

        @pl.when(step > 0)
        def _():
            inner_grad[...] += inner_part
            outer_grad[...] += outer_part

        return carry

    def combine(i, carry):
        step = arrival(i)
        _, expert = plane_peer(step)
        hit = token_hits(dest_columns, expert, capacity, tokens)

        @pl.when(step > 0)
        def _():
            plane_copy(results, landed_two, send_two, recv_two, step).wait_recv()

        part = jnp.dot(hit, landed_two[step], preferred_element_type=jnp.float32)

        @pl.when(i == 0)
        def _():
            grad_ref[...] = part

        @pl.when(i > 0)
        def _():
            grad_ref[...] += part

        return carry

    def finish(step, carry):
        plane_copy(outgoing, landed, send_one, recv_one, step).wait_send()
        plane_copy(results, landed_two, send_two, recv_two, step).wait_send()
        return carry

    lax.fori_loop(0, 8, dispatch, 0)
    inner_ref[...] = inner_full[...].astype(jnp.bfloat16)
    outer_ref[...] = outer_full[...].astype(jnp.bfloat16)
    lax.fori_loop(0, 8, work, 0)
    lax.fori_loop(0, 8, weigh, 0)
    lax.fori_loop(0, 8, combine, 0)
    lax.fori_loop(1, 8, finish, 0)


def experts_backward(rows, dest, gates, routes, returned, arrived, inner, outer, collective_id):
    tokens, width = rows.shape
    capacity = arrived.shape[1]
    inside = inner.shape[1]
    buffer = pltpu.VMEM((8, capacity, width), jnp.bfloat16)
    inside_buffer = pltpu.VMEM((8, capacity, inside), jnp.bfloat16)
    return pl.pallas_call(
        experts_back_kernel,
        out_shape=[
            jax.ShapeDtypeStruct((tokens, width), jnp.float32),
            jax.ShapeDtypeStruct((2, tokens), jnp.float32),
            jax.ShapeDtypeStruct((width, inside), jnp.float32),
            jax.ShapeDtypeStruct((inside, width), jnp.float32),
        ],
        in_specs=[whole_vmem] * 9,
        out_specs=[whole_vmem] * 4,
        scratch_shapes=[pltpu.VMEM(w.shape, jnp.bfloat16) for w in (inner, outer)]
        + [buffer] * 4
        + [inside_buffer] * 2
        + [pltpu.SemaphoreType.DMA((8,))] * 4,
        compiler_params=pltpu.CompilerParams(
            collective_id=collective_id, has_side_effects=True, vmem_limit_bytes=60 << 20
        ),
    )(rows, dest, dest.T, gates, routes, returned, arrived, inner, outer)


def own_units_kernel(
    chunks, units_of, slopes_ref, rows_ref, ids_ref, zero_ref, joint_ref, normed_ref, attended_ref,
    grad_ref, small_ref, grads_ref, small_out, *refs
):
    slopes, late, mixed, made, passing, own, other, relay, landed, small_landed, ready = refs[:11]
    other_send, other_recv, relay_send, relay_recv, landed_send, landed_recv = refs[11:17]
    small_send, small_recv, load_sem, store_sem = refs[17:]
    chip, core = lax.axis_index("dp"), lax.axis_index("ctx")
    beside = chip + 1 - 2 * lax.rem(chip, 2)
    across = lax.rem(chip + 2, 4)
    opposite = across + 1 - 2 * lax.rem(across, 2)
    places = (opposite, beside, across, chip)
    slots, unit_rows = own.shape[1:3]
    table_units = slopes.shape[0]
    tokens = rows_ref.shape[0]
    size = slots // chunks
    split = (chunks + 1) // 2
    load = pltpu.make_async_copy(slopes_ref, slopes, load_sem)
    load.start()
    greet_plane()

    def repeat(first, last, body):
        def step(i, carry):
            body(i)
            return carry

        lax.fori_loop(first, last, step, 0)

    def span(q):
        return pl.ds(q * size, size)

    def remote(source, target, send, recv, place):
        return pltpu.make_async_remote_copy(
            src_ref=source,
            dst_ref=target,
            send_sem=send,
            recv_sem=recv,
            device_id=place,
            device_id_type=MESH_ID,
        )

    def pass_over(k, q):
        return remote(
            passing.at[k % 2, span(q)],
            other.at[k, span(q)],
            other_send.at[k, q],
            other_recv.at[k, q],
            {"ctx": 1 - core},
        )

    def to_relay(q, place):
        return remote(own.at[0, span(q)], relay.at[span(q)], relay_send.at[q], relay_recv.at[q], {"dp": place})

    def to_owner(k, q):
        return remote(
            own.at[k, span(q)],
            landed.at[k - 1, span(q)],
            landed_send.at[k - 1, q],
            landed_recv.at[k - 1, q],
            {"dp": places[k]},
        )

    def small_copy(step):
        place, _ = plane_peer(step)
        return remote(
            small_ref, small_landed.at[chip * 2 + core], small_send.at[step], small_recv.at[step], place
        )

    joint_units = joint_ref.shape[0] // unit_rows
    late[pl.ds(0, joint_units)] = jnp.dot(
        joint_ref[...], normed_ref[...], preferred_element_type=jnp.float32
    ).reshape(joint_units, unit_rows, -1)
    last_units = attended_ref.shape[0] // unit_rows
    late[pl.ds(joint_units, last_units)] = jnp.dot(
        attended_ref[...], grad_ref[...], preferred_element_type=jnp.float32
    ).reshape(last_units, unit_rows, -1)
    load.wait()
    group = made.shape[0] // unit_rows

    def form(owner, target, first_group=0, last_group=slots // group):
        def some(g):
            first = owner * slots + g * group

            def fill(s):
                unit = units_of[first + s]
                lines = pl.ds(pl.multiple_of(s * unit_rows, unit_rows), unit_rows)
                mixed[lines, :tokens] = slopes[jnp.minimum(unit, table_units - 1)]
                row = lax.broadcasted_iota(jnp.int32, (unit_rows, tokens), 0) + unit * unit_rows
                mixed[lines, tokens:] = jnp.where(row == ids_ref[...], 1.0, 0.0).astype(jnp.bfloat16)

            repeat(0, group, fill)
            made[...] = jnp.dot(
                mixed[:, :tokens], rows_ref[...], preferred_element_type=jnp.float32
            ) + jnp.dot(mixed[:, tokens:], zero_ref[...], preferred_element_type=jnp.float32)

            def put(s):
                unit = units_of[first + s]
                table_piece = made[pl.ds(pl.multiple_of(s * unit_rows, unit_rows), unit_rows)]
                late_piece = late[jnp.clip(unit - table_units, 0, late.shape[0] - 1)]
                marks = jnp.zeros(table_piece.shape, jnp.int32) + unit
                piece = jnp.where(marks < table_units, table_piece, late_piece)
                target[g * group + s] = piece.astype(jnp.bfloat16)

            repeat(0, group, put)

        repeat(first_group, last_group, some)

    def joined(k, q):
        pass_over(k, q).wait_recv()
        return own[k, span(q)].astype(jnp.float32) + other[k, span(q)].astype(jnp.float32)

    def first_leg(place):
        def leg(q):
            own[0, span(q)] = joined(0, q).astype(jnp.bfloat16)
            to_relay(q, place).start()

        return leg

    def direct(k):
        def leg(q):
            own[k, span(q)] = joined(k, q).astype(jnp.bfloat16)
            to_owner(k, q).start()

        return leg

    def relayed(k, place):
        def leg(q):
            to_relay(q, place).wait_recv()
            total = joined(k, q) + relay[span(q)].astype(jnp.float32)
            own[k, span(q)] = total.astype(jnp.bfloat16)
            to_owner(k, q).start()

        return leg

    def form_pair(k):
        if k >= 2:
            repeat(0, chunks, lambda q: pass_over(k - 2, q).wait_send())
        form(places[k] * 2 + 1 - core, passing.at[k % 2])
        repeat(0, chunks, lambda q: pass_over(k, q).start())
        form(places[k] * 2 + core, own.at[k])

    form_pair(0)
    repeat(0, split, first_leg(beside))
    repeat(split, chunks, first_leg(across))
    repeat(1, 8, lambda step: small_copy(step).start())
    small_landed[chip * 2 + core] = small_ref[...]
    form_pair(1)
    repeat(0, split, direct(1))
    form_pair(2)
    repeat(split, chunks, direct(2))
    repeat(0, split, relayed(2, beside))
    repeat(split, chunks, relayed(1, across))
    form_pair(3)

    def store(q):
        return pltpu.make_async_copy(
            ready.at[lax.rem(q, 2)], grads_ref.at[span(q)], store_sem.at[lax.rem(q, 2)]
        )

    def keep(q):
        total = joined(3, q)
        to_owner(1, q).wait_recv()
        to_owner(2, q).wait_recv()

        @pl.when(q >= 2)
        def _():
            store(q - 2).wait()

        ready[lax.rem(q, 2)] = (
            total + landed[0, span(q)].astype(jnp.float32) + landed[1, span(q)].astype(jnp.float32)
        )
        store(q).start()

    repeat(0, chunks, keep)

    def finish(q):
        for k in (2, 3):
            pass_over(k, q).wait_send()
        to_owner(1, q).wait_send()
        to_owner(2, q).wait_send()

    repeat(0, chunks, finish)
    repeat(0, split, lambda q: to_relay(q, beside).wait_send())
    repeat(split, chunks, lambda q: to_relay(q, across).wait_send())
    repeat(1, 8, lambda step: small_copy(step).wait())
    total = small_landed[0]
    for source in range(1, 8):
        total = total + small_landed[source]
    small_out[...] = total
    for q in range(max(0, chunks - 2), chunks):
        store(q).wait()


def own_units(units_of, slots, unit_rows, slopes, rows, ids, zero, joint, normed, attended, grad, small, collective_id):
    tokens, width = rows.shape
    unit = (unit_rows, width)
    chunks = max(k for k in range(1, 8) if slots % k == 0)
    group = max(k for k in range(1, 8) if slots % k == 0)
    late = (joint.shape[0] + attended.shape[0]) // unit_rows
    slopes = slopes.reshape(-1, unit_rows, tokens)
    return pl.pallas_call(
        functools.partial(own_units_kernel, chunks),
        out_shape=[
            jax.ShapeDtypeStruct((slots,) + unit, jnp.float32),
            jax.ShapeDtypeStruct(small.shape, jnp.float32),
        ],
        in_specs=[pl.BlockSpec(memory_space=pltpu.SMEM), whole_any] + [whole_vmem] * 8,
        out_specs=[whole_any, whole_vmem],
        scratch_shapes=[
            pltpu.VMEM(slopes.shape, jnp.bfloat16),
            pltpu.VMEM((late,) + unit, jnp.float32),
            pltpu.VMEM((group * unit_rows, 2 * tokens), jnp.bfloat16),
            pltpu.VMEM((group * unit_rows, width), jnp.float32),
            pltpu.VMEM((2, slots) + unit, jnp.bfloat16),
            pltpu.VMEM((4, slots) + unit, jnp.bfloat16),
            pltpu.VMEM((4, slots) + unit, jnp.bfloat16),
            pltpu.VMEM((slots,) + unit, jnp.bfloat16),
            pltpu.VMEM((2, slots) + unit, jnp.bfloat16),
            pltpu.VMEM((8,) + small.shape, jnp.float32),
            pltpu.VMEM((2, slots // chunks) + unit, jnp.float32),
            pltpu.SemaphoreType.DMA((4, chunks)),
            pltpu.SemaphoreType.DMA((4, chunks)),
            pltpu.SemaphoreType.DMA((chunks,)),
            pltpu.SemaphoreType.DMA((chunks,)),
            pltpu.SemaphoreType.DMA((2, chunks)),
            pltpu.SemaphoreType.DMA((2, chunks)),
            pltpu.SemaphoreType.DMA((8,)),
            pltpu.SemaphoreType.DMA((8,)),
            pltpu.SemaphoreType.DMA,
            pltpu.SemaphoreType.DMA((2,)),
        ],
        compiler_params=pltpu.CompilerParams(
            collective_id=collective_id, has_side_effects=True, vmem_limit_bytes=63 << 20
        ),
    )(units_of, slopes, rows, ids, zero, joint, normed, attended, grad, small)


def to_plane(buffer):
    return lax.all_to_all(buffer, ("dp", "ctx"), split_axis=0, concat_axis=0, tiled=True)


def plain_hits(dest, experts, capacity):
    slots = lax.broadcasted_iota(jnp.int32, (experts * capacity, dest.shape[1]), 0)
    return [slots == dest[k : k + 1] for k in range(2)]


def plain_forward(rows, dest, gates, inner, outer, owners, capacity):
    width = rows.shape[1]
    hits = plain_hits(dest, owners, capacity)
    both = (hits[0] | hits[1]).astype(jnp.bfloat16)
    sent = jnp.dot(both, rows, preferred_element_type=jnp.float32).astype(jnp.bfloat16)
    arrived = to_plane(sent.reshape(owners, capacity, width))
    hidden = jnp.einsum("ocd,df->ocf", arrived, inner, preferred_element_type=jnp.float32)
    active = gelu_tanh(hidden).astype(jnp.bfloat16)
    part = jnp.einsum("ocf,fd->ocd", active, outer, preferred_element_type=jnp.float32)
    returned = to_plane(part.astype(jnp.bfloat16))
    flat = returned.reshape(owners * capacity, width)
    mix = sum(
        gates[:, k : k + 1]
        * lax.dot_general(
            hits[k].astype(jnp.bfloat16),
            flat,
            (((0,), (0,)), ((), ())),
            preferred_element_type=jnp.float32,
        )
        for k in range(2)
    )
    return (mix, arrived, returned)


def plain_backward(rows, dest, gates, returned, arrived, inner, outer):
    owners, capacity, width = arrived.shape
    hits = plain_hits(dest, owners, capacity)
    both = (hits[0] | hits[1]).astype(jnp.bfloat16)
    slot_scale = jnp.sum(
        jnp.where(hits[0], gates[0:1], 0.0) + jnp.where(hits[1], gates[1:2], 0.0), 1, keepdims=True
    )
    slot_grads = jnp.dot(both, rows, preferred_element_type=jnp.float32)
    sent = (slot_grads * slot_scale).astype(jnp.bfloat16)
    flat = returned.reshape(owners * capacity, width)
    dots = jnp.sum(slot_grads * flat.astype(jnp.float32), 1, keepdims=True)
    gate_part = jnp.concatenate(
        [jnp.sum(jnp.where(hit, dots, 0.0), 0, keepdims=True) for hit in hits], 0
    )
    landed = to_plane(sent.reshape(owners, capacity, width))
    grad_active = jnp.einsum("ocd,fd->ocf", landed, outer, preferred_element_type=jnp.float32)
    hidden = jnp.einsum("ocd,df->ocf", arrived, inner, preferred_element_type=jnp.float32)
    active = gelu_tanh(hidden).astype(jnp.bfloat16)
    slope = (grad_active * gelu_slope(hidden)).astype(jnp.bfloat16)
    outer_grad = jnp.einsum("ocf,ocd->fd", active, landed, preferred_element_type=jnp.float32)
    inner_grad = jnp.einsum("ocd,ocf->df", arrived, slope, preferred_element_type=jnp.float32)
    back = jnp.einsum("ocf,df->ocd", slope, inner, preferred_element_type=jnp.float32)
    back = to_plane(back.astype(jnp.bfloat16)).reshape(owners * capacity, width)
    grad = lax.dot_general(
        both, back, (((0,), (0,)), ((), ())), preferred_element_type=jnp.float32
    )
    return (grad, gate_part, inner_grad, outer_grad)


def on_device(
    token_ids,
    targets,
    counted,
    routes,
    priority,
    owner_of,
    master,
    master_first,
    master_second,
    expert_in,
    expert_in_first,
    expert_in_second,
    expert_out,
    expert_out_first,
    expert_out_second,
    norm_gains,
    norm_gains_first,
    norm_gains_second,
    router,
    router_first,
    router_second,
    rel_bias,
    rel_bias_first,
    rel_bias_second,
):
    owners = lax.axis_size(("dp", "ctx"))
    tensor_ranks = lax.axis_size("tensor")
    my_owner = lax.axis_index(("dp", "ctx"))
    my_rank = lax.axis_index("tensor")
    my_context = lax.axis_index("ctx")
    sequences, half_length = token_ids.shape
    tokens_here = sequences * half_length
    most_units = master.shape[2]
    unit_rows = master.shape[3]
    model_width = master.shape[4]
    vocab_here = VOCAB // tensor_ranks
    heads_here = rel_bias.shape[0]
    head_size = model_width // (heads_here * tensor_ranks)
    hidden_here = heads_here * head_size
    experts = router.shape[1]
    capacity = (18 * tokens_here + 8 * experts - 1) // (8 * experts)
    table_units = vocab_here // unit_rows
    query_units = table_units + 2 * hidden_here // unit_rows
    value_units = table_units + 3 * hidden_here // unit_rows
    embed_scale = math.sqrt(model_width)
    owner_ids = owner_of[:, 0]
    on_square = lax.axis_size("dp") == 4 and lax.axis_size("ctx") == 2
    unit_rank, slot_unit, slot_filled = slot_tables(owner_ids, owners, most_units)
    counted_rows = counted.reshape(tokens_here, 2).T.astype(jnp.float32)
    loss_weights = counted_rows * jnp.array([[1.0], [ahead_weight]], jnp.float32)
    counts = jnp.zeros((8, 128), jnp.float32).at[0:2].set(jnp.sum(counted_rows, 1, keepdims=True))
    unit_slots = owner_ids * most_units + unit_rank
    route_pairs = routes.reshape(tokens_here, 2)
    pair_kept, pair_dest = pair_slots(route_pairs, priority[0], experts, capacity)
    dest = jnp.where(pair_kept, pair_dest, -1).reshape(2, tokens_here)
    unit_slots, dest = lax.optimization_barrier((unit_slots, dest))
    local_ids = token_ids.reshape(-1) - my_rank * vocab_here
    inside = (local_ids >= 0) & (local_ids < vocab_here)
    clipped_ids = jnp.clip(local_ids, 0, vocab_here - 1)
    unit_starts = jnp.sum(
        jnp.where(
            (clipped_ids // unit_rows)[None, :] == jnp.arange(unit_slots.shape[0])[:, None],
            unit_slots[:, None] * unit_rows,
            0,
        ),
        0,
    )
    slot_rows = unit_starts + clipped_ids % unit_rows
    if on_square:
        slot_rows = jnp.where(inside, slot_rows, -1)[:, None]
        weights_low, embedded, normed_one_low, joint, joint_low, project_low = embed(
            unit_slots,
            master[0, 0],
            slot_rows,
            norm_gains[0:1],
            table_units,
            3 * hidden_here,
            11,
        )
    else:
        master_low = master[0, 0].astype(jnp.bfloat16)
        gathered = lax.all_gather(master_low, ("dp", "ctx"), axis=0, tiled=True)
        looked = jnp.take(gathered.reshape(-1, model_width), slot_rows, axis=0)
        looked = jnp.where(inside[:, None], looked, 0)
        weights_low = pull_units([gathered], unit_slots)
        (embedded,) = sum_line(looked, [], [], keep_total, 1)
    weights_low = weights_low.reshape(-1, model_width)
    if not on_square:
        joint_low = weights_low[vocab_here : vocab_here + 3 * hidden_here]
        project_low = weights_low[vocab_here + 3 * hidden_here :]
    rolled = [project_low] + [
        lax.ppermute(project_low, "tensor", [(source, (source + step) % 4) for source in range(4)])
        for step in (1, 2, 3)
    ]
    gain_rows = [norm_gains[k : k + 1] for k in range(3)]
    stream_shape = jax.ShapeDtypeStruct((tokens_here, model_width), jnp.float32)
    gain_shape = jax.ShapeDtypeStruct((1, model_width), jnp.float32)
    if not on_square:
        stream_zero = embedded.astype(jnp.float32) * embed_scale
        normed_one_low = norm_forward(stream_zero, norm_gains[0]).astype(jnp.bfloat16)
        joint = lax.dot_general(
            joint_low, normed_one_low, (((1,), (1,)), ((), ())), preferred_element_type=jnp.float32
        ).astype(jnp.bfloat16)
    attended_all, logsum_rows, pairs_before, attended = attention(
        rel_bias, joint, heads_here, head_size, 2
    )
    router_low = router.astype(jnp.bfloat16)
    stream_one, normed_two_low, gate_rows, gate_columns = middle(
        attended_all.reshape(model_width, tokens_here),
        rolled,
        embedded,
        gain_rows[1],
        router_low.T,
        route_pairs.T,
    )
    if on_square:
        moe_partial, arrived, returned, counts = experts_forward(
            normed_two_low, dest, gate_columns, route_pairs, expert_in[0], expert_out[0], counts, capacity, 8
        )
    else:
        inner_low, outer_low = expert_in[0].astype(jnp.bfloat16), expert_out[0].astype(jnp.bfloat16)
        moe_partial, arrived, returned = plain_forward(
            normed_two_low, dest, gate_columns, inner_low, outer_low, owners, capacity
        )
        counts = lax.psum(counts, ("dp", "ctx"))
    weight_total = counts[0, 0] + ahead_weight * counts[1, 0]
    local_targets = targets.reshape(tokens_here, 2).T - my_rank * vocab_here
    weight_rows = jnp.concatenate(
        [
            loss_weights,
            loss_weights[0:1] + loss_weights[1:2],
            jnp.broadcast_to(1.0 / weight_total, (1, tokens_here)),
        ],
        0,
    )
    head_low, grad_two_low, grad_two, gain_grad_three, logsum_vocab, target_sums, slopes = head_line(
        moe_partial, stream_one, gain_rows[2], weights_low, local_targets, weight_rows, vocab_here, 3
    )
    if on_square:
        moe_grad_part, gate_part, inner_grad, outer_grad = experts_backward(
            grad_two_low,
            dest,
            gate_rows,
            route_pairs.T,
            returned,
            arrived,
            expert_in[0],
            expert_out[0],
            9,
        )
    else:
        moe_grad_part, gate_part, inner_grad, outer_grad = plain_backward(
            grad_two_low, dest, gate_rows, returned, arrived, inner_low, outer_low
        )
    gate_part = jnp.concatenate([gate_part, target_sums, jnp.zeros_like(target_sums)], 0)
    gate_block = pltpu.VMEM((3, 4, tokens_here), jnp.float32)
    grad_one_low, grad_one, logit_grad, target_total, gain_grad_two = sum_line(
        moe_grad_part,
        [
            stream_one,
            gain_rows[1],
            grad_two,
            gate_part,
            gate_rows,
            route_pairs.T,
            router_low,
        ],
        [
            stream_shape,
            jax.ShapeDtypeStruct((experts, tokens_here), jnp.bfloat16),
            jax.ShapeDtypeStruct((1, tokens_here), jnp.float32),
            gain_shape,
        ],
        finish_expert_grad,
        5,
        prologue=start_router_grad,
        scratch=(gate_block, pltpu.SemaphoreType.DMA((3,)), pltpu.SemaphoreType.DMA((3,))),
        opening=send_gate_parts,
    )
    router_grad = jnp.dot(logit_grad, normed_two_low, preferred_element_type=jnp.float32)
    loss_local = jnp.sum(weight_rows[2:3] * logsum_vocab) - jnp.sum(target_total)
    query_grad, pair_grad, before_grad, bias_lines, *expert_states = attention_back(
        rel_bias,
        joint,
        pairs_before,
        logsum_rows,
        grad_one_low,
        project_low,
        (
            expert_in[0],
            expert_in_first[0],
            expert_in_second[0],
            inner_grad,
            expert_out[0],
            expert_out_first[0],
            expert_out_second[0],
            outer_grad,
        ),
        heads_here,
        head_size,
    )
    distances = 2 * (half_length // BLOCK)
    bias_grad = jnp.sum(bias_lines, 1).reshape(heads_here, distances)
    pair_shape = pltpu.VMEM((2 * hidden_here, tokens_here), jnp.bfloat16)
    zero_grad_low, joint_grad, gain_grads = sum_line(
        None,
        [
            embedded,
            gain_rows[0],
            grad_one,
            gain_grad_two,
            gain_grad_three,
            query_grad,
            pair_grad,
            before_grad,
            joint_low,
        ],
        [
            jax.ShapeDtypeStruct((3 * hidden_here, tokens_here), jnp.bfloat16),
            jax.ShapeDtypeStruct((8, model_width), jnp.float32),
        ],
        functools.partial(finish_input_grad, embed_scale),
        6,
        prologue=clear_gain,
        scratch=(
            pltpu.SemaphoreType.DMA,
            pltpu.SemaphoreType.DMA,
            pair_shape,
            pltpu.SemaphoreType.DMA((2,)),
            pltpu.VMEM((tokens_here, model_width), jnp.float32),
        ),
        opening=form_joint_grad,
        ending=share_gains,
    )
    my_units = jnp.take(slot_unit, my_owner, axis=0)
    my_filled = jnp.take(slot_filled, my_owner, axis=0)[:, None, None]
    bias_row = jnp.concatenate([bias_grad.reshape(-1), loss_local[None]])
    bias_row = jnp.pad(bias_row, (0, model_width - bias_row.shape[0]))[None]
    small = jnp.concatenate([gain_grads[:3], router_grad, bias_row], 0)
    small = jnp.pad(small, ((0, -small.shape[0] % 8), (0, 0)))
    slot_rates = unit_rates(my_units, table_units, query_units, value_units)[:, None, None]
    states = (master[0, 0], master_first[0, 0], master_second[0, 0])
    grad_rows = (
        slopes,
        head_low,
        local_ids[None, :],
        zero_grad_low,
        joint_grad,
        normed_one_low,
        attended,
        grad_one_low,
    )
    if on_square:
        mine, small = own_units(slot_unit.reshape(-1), most_units, unit_rows, *grad_rows, small, 10)
    else:
        outgoing = weight_grads(unit_slots, owners * most_units, unit_rows, *grad_rows)
        mine = lax.psum_scatter(
            outgoing.astype(jnp.float32), ("dp", "ctx"), scatter_dimension=0, tiled=True
        )
        small = lax.psum(small, ("dp", "ctx"))
    states = adam_update(*states, jnp.where(my_filled, mine, 0.0), slot_rates, decay_rate)
    gains_grad = small[:3]
    router_grad = small[3 : 3 + experts].T
    bias_grad = small[3 + experts, : rel_bias.size].reshape(rel_bias.shape)
    loss_totals = jnp.stack([small[3 + experts, rel_bias.size], weight_total])
    gains_new, gains_first_new, gains_second_new = adam_update(
        norm_gains, norm_gains_first, norm_gains_second, gains_grad, rate_gains, 0.0
    )
    router_new, router_first_new, router_second_new = adam_update(
        router, router_first, router_second, router_grad, rate_router, decay_rate
    )
    biases_new, biases_first_new, biases_second_new = adam_update(
        rel_bias, rel_bias_first, rel_bias_second, bias_grad, rate_biases, 0.0
    )
    return (
        loss_totals,
        *(state[None, None] for state in states),
        *(state[None] for state in expert_states),
        gains_new,
        gains_first_new,
        gains_second_new,
        router_new,
        router_first_new,
        router_second_new,
        biases_new,
        biases_first_new,
        biases_second_new,
    )


def solution(mesh):
    in_specs = (
        P("dp", "ctx"),
        P("dp", "ctx", None),
        P("dp", "ctx", None),
        P("dp", "ctx", None),
        P(("dp", "ctx"), None),
        P(),
        P("tensor", ("dp", "ctx"), None, None, None),
        P("tensor", ("dp", "ctx"), None, None, None),
        P("tensor", ("dp", "ctx"), None, None, None),
        P(("dp", "ctx"), None, "tensor"),
        P(("dp", "ctx"), None, "tensor"),
        P(("dp", "ctx"), None, "tensor"),
        P(("dp", "ctx"), "tensor", None),
        P(("dp", "ctx"), "tensor", None),
        P(("dp", "ctx"), "tensor", None),
        P(),
        P(),
        P(),
        P(),
        P(),
        P(),
        P("tensor", None),
        P("tensor", None),
        P("tensor", None),
    )
    out_specs = (
        P(),
        P("tensor", ("dp", "ctx"), None, None, None),
        P("tensor", ("dp", "ctx"), None, None, None),
        P("tensor", ("dp", "ctx"), None, None, None),
        P(("dp", "ctx"), None, "tensor"),
        P(("dp", "ctx"), None, "tensor"),
        P(("dp", "ctx"), None, "tensor"),
        P(("dp", "ctx"), "tensor", None),
        P(("dp", "ctx"), "tensor", None),
        P(("dp", "ctx"), "tensor", None),
        P(),
        P(),
        P(),
        P(),
        P(),
        P(),
        P("tensor", None),
        P("tensor", None),
        P("tensor", None),
    )
    return jax.shard_map(
        on_device, mesh=mesh, in_specs=in_specs, out_specs=out_specs, check_vma=False
    )
```
